32 devices in a mesh: dp: 8 (over y, x, core), fsdp: 4 (over z).
Axes of the slice: x: 2, y: 2, z: 4, core: 2. Of those that a mesh axis runs over, the one named last changes fastest.
Arguments:
- hidden_in: bfloat16 [16, 1024, 1536], P('dp', 'fsdp'), may hold values from -6 to 6
- cotangent: bfloat16 [16, 1024, 1536], P('dp', 'fsdp'), may hold values from -6 to 6
- in_proj: bfloat16 [1536, 6448], P(('dp', 'fsdp')), may hold values from -0.15625 to 0.15625
- out_proj: bfloat16 [3072, 1536], P(('dp', 'fsdp')), may hold values from -0.109375 to 0.109375
- conv_params: bfloat16 [5, 3328], P(None, ('dp', 'fsdp')), may hold values from -0.5 to 0.5
- pre_gain: bfloat16 [1536], P(('dp', 'fsdp')), may hold values from 0.5 to 1.5
- gated_gain: bfloat16 [3072], P(('dp', 'fsdp')), may hold values from 0.5 to 1.5
- head_params: float32 [3, 48], replicated, may hold values from -6 to 2, as said below
Outputs:
- hidden_out: bfloat16 [16, 1024, 1536], P('dp', 'fsdp')
- grad_in: bfloat16 [16, 1024, 1536], P('dp', 'fsdp')
- in_proj_grad: float32 [1536, 6448], P(('dp', 'fsdp'))
- out_proj_grad: float32 [3072, 1536], P(('dp', 'fsdp'))
- conv_grad: float32 [5, 3328], P(None, ('dp', 'fsdp'))
- pre_gain_grad: float32 [1536], P(('dp', 'fsdp'))
- gated_gain_grad: float32 [3072], P(('dp', 'fsdp'))
- head_grad: float32 [3, 48], replicated
The draws below stay inside these ranges and needn't reach their ends.
Inputs may be any that keep to these rules, and one draw needn't show every extreme that they name: `head_params`: row 0 holds each head's log decay coefficient (the decay rate is minus its exponential), row 1 each head's step bias, row 2 each head's skip coefficient.
All inputs are finite; a program needn't handle non-finite values.
Results may differ from the reference program's by a relative error of at most 0.0063.
The reference program's roundings to bfloat16 on the way count: a program that leaves them out, or rounds other values in their place, can miss the bound.
Values may be sent and summed in bfloat16 or wider, within the bound.
No kernel may reach another device: no remote copies, remote signals or barrier semaphores. Data moves between devices by JAX's collectives and lax.ppermute only.
A program may use at most 160 MiB of HBM per device.

```python
import math
import jax
import jax.numpy as jnp
from jax import lax

D = 1536
HEADS = 48
HEADDIM = 64
STATE = 128
CONV = 4
GROUP = 256
INNER = 3072
XBC = 3328
PROJ = 6448
LENGTH = 1024
BATCH = 16
N_FSDP = 4


def draw_head_params(key, part):
    key = jax.random.fold_in(key, 7)
    keys = jax.random.split(key, 6)
    fast_share = 0.4
    skip_lower = 0.5
    skip_upper = 1.5
    fast = jax.random.uniform(keys[0], (HEADS,)) < fast_share
    slow_rate = jnp.exp(jax.random.uniform(keys[1], (HEADS,), minval=math.log(0.3), maxval=math.log(2.0))) / LENGTH
    fast_rate = 1.0 / jax.random.uniform(keys[2], (HEADS,), minval=30.0, maxval=50.0)
    slow_step = 1.0 / (math.sqrt(LENGTH) * jnp.exp(jax.random.uniform(keys[3], (HEADS,), minval=0.0, maxval=math.log(4.0))))
    fast_step = 0.05 * jnp.exp(jax.random.uniform(keys[4], (HEADS,), minval=math.log(0.5), maxval=math.log(2.0)))
    rate_value = jnp.where(fast, fast_rate, slow_rate)
    mean_step = jnp.where(fast, fast_step, slow_step)
    log_coeff = jnp.log(rate_value / mean_step)
    step_bias = jnp.log(mean_step) - 0.5
    skip_coeff = jax.random.uniform(keys[5], (HEADS,), minval=skip_lower, maxval=skip_upper)
    return jnp.stack([log_coeff, step_bias, skip_coeff]).astype(jnp.float32)


def strengthened(values, stream_key, source, target, blocks, factor):
    owner, partner = [(jnp.arange(values.shape[axis_at]) // (values.shape[axis_at] // blocks)).reshape([-1 if axis == axis_at else 1 for axis in range(values.ndim)]) for axis_at in (source, target)]
    chosen = jax.random.permutation(stream_key, blocks)[partner]
    strong = (owner == chosen) | (owner == (partner + blocks // 2) % blocks)
    return jnp.where(strong, factor * values, values)


def level_of(rng, extent, cuts, low, high):
    factor_of, own = 1.0, jax.random.fold_in(rng, 6)
    for axis_at, shards_of in cuts:
        heights = jnp.exp(jax.random.uniform(jax.random.fold_in(own, axis_at), (shards_of,), jnp.float32, low / len(cuts), high / len(cuts)))
        factor_of = factor_of * jnp.repeat(heights, extent[axis_at] // shards_of).reshape([-1 if axis == axis_at else 1 for axis in range(len(extent))])
    return factor_of


def scatter_about(stream_key, shape, width, reach, shards=(), held_as=jnp.bfloat16):
    factor_of = level_of(stream_key, shape, shards, -0.22, 0.18) if shards else 1.0
    drawn = jax.random.normal(stream_key, shape, jnp.float32) * width * factor_of
    return jnp.minimum(jnp.maximum(drawn, -reach), reach).astype(held_as)


def noise_with(key, extent, scale, reach, shards, heavy, dtype=jnp.bfloat16):
    values = scale * jax.random.normal(key, extent, jnp.float32)
    if shards:
        values = values * level_of(key, extent, shards, -0.22, 0.18)
    return jnp.clip(strengthened(values, jax.random.fold_in(key, 3), *heavy), -reach, reach).astype(dtype)


def setup_inputs(seed: int = 0) -> dict:
    streams_of = jax.random.split(jax.random.key(seed), 9)
    return {
        "hidden_in": noise_with(streams_of[0], (BATCH, LENGTH, D), 1.0, 6.0, ((0, 8), (1, 4)), (0, 2, 8, 2.0)),
        "cotangent": scatter_about(streams_of[1], (BATCH, LENGTH, D), 1.0, 6.0, ((0, 8), (1, 4))),
        "in_proj": scatter_about(streams_of[2], (D, PROJ), D ** -0.5, 0.15625, ((0, 32),)),
        "out_proj": scatter_about(streams_of[3], (INNER, D), INNER ** -0.5, 0.109375, ((0, 32),)),
        "conv_params": jnp.clip(jax.random.uniform(streams_of[4], (CONV + 1, XBC), jnp.float32, -0.5, 0.5) * level_of(streams_of[4], (CONV + 1, XBC), ((1, 32),), -0.4, 0.0), -0.5, 0.5).astype(jnp.bfloat16),
        "pre_gain": jnp.clip(1.0 + 0.1 * jax.random.normal(streams_of[5], (D,), jnp.float32), 0.5, 1.5).astype(jnp.bfloat16),
        "gated_gain": jnp.clip(1.0 + 0.1 * jax.random.normal(streams_of[6], (INNER,), jnp.float32), 0.5, 1.5).astype(jnp.bfloat16),
        "head_params": draw_head_params(jax.random.fold_in(streams_of[8], 71), 0),
    }


epsilon = 1e-05
highest = lax.Precision.HIGHEST

@jax.custom_vjp
def low(v):
    return lax.optimization_barrier(v.astype(jnp.bfloat16)).astype(jnp.float32)

@jax.custom_vjp
def low_back(v):
    return v

def low_keep(v):
    return (low(v), None)

def low_pass(kept, grad):
    return (grad,)

def back_keep(v):
    return (v, None)

def back_low(kept, grad):
    return (low(grad),)
low.defvjp(low_keep, low_pass)
low_back.defvjp(back_keep, back_low)

def segment_weights(scores, decay_sum, step_size):
    row_count = scores.shape[0]
    causal = lax.broadcasted_iota(jnp.int32, (row_count, row_count), 0) >= lax.broadcasted_iota(jnp.int32, (row_count, row_count), 1)
    sum_heads = decay_sum.T
    step_heads = step_size.T
    spread = jnp.exp(jnp.where(causal, sum_heads[:, :, None] - sum_heads[:, None, :], 0.0))
    return jnp.where(causal, scores[None] * spread * step_heads[:, None, :], 0.0)

def segment_pass(state, pieces):
    x_low, b_low, c_low, step_size, log_decay = pieces
    decay_sum = jnp.cumsum(log_decay, axis=0)
    scores = low_back(jnp.dot(c_low, b_low.T, precision=highest))
    weights = low(segment_weights(scores, decay_sum, step_size))
    intra = low_back(jnp.einsum('hts,shp->thp', weights, x_low, precision=highest))
    last_sum = decay_sum[-1]
    carry_scale = jnp.exp(last_sum[None, :] - decay_sum) * step_size
    scaled_x = low(carry_scale[:, :, None] * x_low)
    local_state = low_back(jnp.einsum('shp,sn->hpn', scaled_x, b_low, precision=highest))
    from_state = jnp.exp(decay_sum)[:, :, None] * jnp.einsum('tn,hpn->thp', c_low, state, precision=highest)
    new_state = jnp.exp(last_sum)[:, None, None] * state + local_state
    return (new_state, intra + from_state)

def mixer(hidden, in_matrix, out_matrix, conv_taps, pre_gain, gated_gain, head_params):
    row_scale = lax.rsqrt(lax.optimization_barrier(jnp.mean(hidden * hidden, axis=-1, keepdims=True)) + epsilon)
    normed = low(hidden * row_scale * pre_gain)
    projected = low_back(jnp.dot(normed, in_matrix, precision=highest))
    gate_input = projected[:, :INNER]
    conv_input = projected[:, INNER:INNER + XBC]
    step_raw = projected[:, INNER + XBC:]
    padded = jnp.concatenate([jnp.zeros((CONV - 1, XBC), jnp.float32), conv_input], axis=0)
    summed = conv_taps[CONV]
    for offset in range(CONV):
        summed = summed + conv_taps[offset] * padded[offset:offset + LENGTH]
    activated = jax.nn.silu(summed)
    x_values = activated[:, :INNER].reshape(LENGTH, HEADS, HEADDIM)
    x_low = low(x_values)
    b_low = low(activated[:, INNER:INNER + STATE])
    c_low = low(activated[:, INNER + STATE:])
    step_size = jax.nn.softplus(step_raw + head_params[1])
    log_decay = step_size * -jnp.exp(head_params[0])
    pieces = (x_low.reshape(N_FSDP, GROUP, HEADS, HEADDIM), b_low.reshape(N_FSDP, GROUP, STATE), c_low.reshape(N_FSDP, GROUP, STATE), step_size.reshape(N_FSDP, GROUP, HEADS), log_decay.reshape(N_FSDP, GROUP, HEADS))
    zero_state = jnp.zeros((HEADS, HEADDIM, STATE), jnp.float32)
    final_state, scanned = lax.scan(jax.checkpoint(segment_pass), zero_state, pieces)
    values = scanned.reshape(LENGTH, HEADS, HEADDIM) + head_params[2][:, None] * x_values
    gated = values.reshape(LENGTH, INNER) * jax.nn.silu(gate_input)
    gate_scale = lax.rsqrt(lax.optimization_barrier(jnp.mean(gated * gated, axis=-1, keepdims=True)) + epsilon)
    mixed = low(gated * gate_scale * gated_gain)
    return hidden + jnp.dot(mixed, out_matrix, precision=highest)

def reference(hidden_in, cotangent, in_proj, out_proj, conv_params, pre_gain, gated_gain, head_params):
    in_matrix = in_proj.astype(jnp.float32)
    out_matrix = out_proj.astype(jnp.float32)
    conv_taps = conv_params.astype(jnp.float32)
    pre_wide = pre_gain.astype(jnp.float32)
    gated_wide = gated_gain.astype(jnp.float32)

    def one_sequence(running, pieces):
        sequence, upstream = pieces
        result, pull_back = jax.vjp(mixer, sequence.astype(jnp.float32), in_matrix, out_matrix, conv_taps, pre_wide, gated_wide, head_params)
        gradients = pull_back(upstream.astype(jnp.float32))
        running = tuple((before + update for before, update in zip(running, gradients[1:])))
        return (running, (result.astype(jnp.bfloat16), gradients[0].astype(jnp.bfloat16)))
    initial = (jnp.zeros_like(in_matrix), jnp.zeros_like(out_matrix), jnp.zeros_like(conv_taps), jnp.zeros_like(pre_wide), jnp.zeros_like(gated_wide), jnp.zeros_like(head_params))
    totals, (hidden_out, grad_in) = lax.scan(one_sequence, initial, (hidden_in, cotangent))
    return (hidden_out, grad_in, totals[0], totals[1], totals[2], totals[3], totals[4], totals[5])
```

```python
import jax
import jax.numpy as jnp
from jax import lax
from jax.sharding import Mesh
from jax.sharding import PartitionSpec as P

HEADS = 48
HEADDIM = 64
STATE = 128
CONV = 4
INNER = 3072
XBC = 3328
HALF = INNER // 2
LANES = 128
SEGS = 4

epsilon = 1e-05
f32 = jnp.float32
bf16 = jnp.bfloat16


def own_columns(array, core):
    chips = lax.axis_size("chip")
    width = array.shape[-1] // (2 * chips)
    parted = array.reshape(array.shape[:-1] + (chips, 2, width))
    picked = lax.dynamic_index_in_dim(parted, core, axis=parted.ndim - 2, keepdims=False)
    return picked.reshape(array.shape[:-1] + (chips * width,))


def to_partner(array):
    return lax.ppermute(array, "core", [(0, 1), (1, 0)])


def in_core_order(mine, theirs, core, axis):
    first = jnp.where(core == 0, mine, theirs)
    second = jnp.where(core == 0, theirs, mine)
    return jnp.stack([first, second], axis=axis)


def line_perm(turn, back):
    line = lax.axis_size("seg")
    parts = line // SEGS
    pairs = []
    for core in range(2):
        for place in range(line):
            piece = (place % SEGS) ^ turn
            half, index = divmod(piece, 2)
            source = core * line + place
            target = half * line + (2 * core + index) * parts + place // SEGS
            pairs.append((target, source) if back else (source, target))
    return pairs


def whole_sequence(array, core, place):
    parts = lax.axis_size("seg") // SEGS
    half = array.shape[1] // 2
    pieces = array.reshape(2, 2, half, -1).transpose(1, 0, 2, 3).reshape(4, half, -1)
    mine = place % SEGS
    target = 2 * core + (place // parts) % 2
    got = []
    for turn in range(4):
        piece = lax.dynamic_index_in_dim(pieces, mine ^ turn, axis=0, keepdims=False)
        got.append(lax.ppermute(piece, ("core", "seg"), line_perm(turn, False)))
    got = jnp.stack(got)
    ordered = jnp.stack([lax.dynamic_index_in_dim(got, target ^ k, axis=0, keepdims=False) for k in range(4)])
    return ordered, in_core_order(ordered, to_partner(ordered), core, 1)


def back_to_owner(ordered, core, place):
    parts = lax.axis_size("seg") // SEGS
    half = ordered.shape[1]
    mine = place % SEGS
    target = 2 * core + (place // parts) % 2
    got = []
    for turn in range(4):
        piece = lax.dynamic_index_in_dim(ordered, target ^ turn, axis=0, keepdims=False)
        got.append(lax.ppermute(piece, ("core", "seg"), line_perm(turn, True)))
    got = jnp.stack(got)
    pieces = jnp.stack([lax.dynamic_index_in_dim(got, mine ^ k, axis=0, keepdims=False) for k in range(4)])
    return pieces.reshape(2, 2, half, -1).transpose(1, 0, 2, 3).reshape(2, 2 * half, -1)


def part_pairs(step):
    line = lax.axis_size("seg")
    parts = line // SEGS
    return [(i, i + step) for i in range(line) if 0 <= i + step < line and i // parts == (i + step) // parts]


def entering(decay, state, step):
    parts = lax.axis_size("seg") // SEGS
    total = jnp.zeros_like(state)
    for _ in range(parts - 1):
        total = lax.ppermute(decay[:, None, None] * total + state, "seg", part_pairs(step))
    return total


def borrowed(array, step):
    parts = lax.axis_size("seg") // SEGS
    if parts == 1:
        return jnp.zeros_like(array)
    return lax.ppermute(array, "seg", part_pairs(step))


def pre_norm(hidden, norm_gain):
    row_scale = lax.rsqrt(jnp.mean(hidden * hidden, axis=-1, keepdims=True) + epsilon)
    return hidden * row_scale * norm_gain


def conv_apply(padded, conv_taps):
    length = padded.shape[0] - CONV + 1
    summed = conv_taps[CONV]
    for offset in range(CONV):
        summed = summed + conv_taps[offset] * padded[offset : offset + length, :]
    return jax.nn.silu(summed)


def head_terms(step_raw, params):
    step_size = jax.nn.softplus(step_raw + params[1])
    decay_sum = jnp.cumsum(step_size * -jnp.exp(params[0]), axis=1)
    return (step_size, decay_sum)


def decay_terms(decay_sum, step_size):
    last_sum = decay_sum[:, -1:, :]
    carry_scale = jnp.exp(last_sum - decay_sum) * step_size
    return (carry_scale, jnp.exp(decay_sum[:, -1, :]), jnp.exp(decay_sum))


def dot(a, b, contract):
    return lax.dot_general(a, b, (contract, ((), ())), preferred_element_type=f32)


def per_device(hidden_in, cotangent, in_proj, out_proj, conv_params, pre_gain, gated_gain, head_params):
    chips, line = lax.axis_size("chip"), lax.axis_size("seg")
    core, place = lax.axis_index("core"), lax.axis_index("seg")
    rows, model_width = in_proj.shape[0], hidden_in.shape[2]
    heads = HEADS // 2
    group = ("chip", "seg")

    permuted = (
        hidden_in.reshape(hidden_in.shape[:2] + (chips, 2, line, rows))
        .transpose(0, 1, 2, 4, 3, 5)
        .reshape(hidden_in.shape)
    )
    hidden_half, hidden = whole_sequence(permuted, core, place)
    conv_width, gain_width = conv_params.shape[1], gated_gain.shape[0]
    used = HALF + 2 * STATE + heads
    spare = -used % LANES
    small = jnp.zeros((rows, spare), bf16)
    small = small.at[: CONV + 1, :conv_width].set(conv_params)
    small = small.at[CONV + 1, :rows].set(pre_gain)
    small = small.at[CONV + 2, :gain_width].set(gated_gain)

    def conv_side(which):
        return jnp.concatenate(
            [
                own_columns(in_proj[:, INNER : 2 * INNER], which),
                in_proj[:, 2 * INNER : INNER + XBC],
                own_columns(in_proj[:, INNER + XBC :], which),
                small,
            ],
            axis=1,
        )

    def gate_side(which):
        return own_columns(in_proj[:, :INNER], which)

    conv_block = in_core_order(conv_side(core), to_partner(conv_side(1 - core)), core, 0)
    gate_block = in_core_order(gate_side(core), to_partner(gate_side(1 - core)), core, 0)
    conv_all = lax.all_gather(conv_block.reshape(2 * rows, -1), group, axis=0, tiled=True)
    gate_matrix = lax.all_gather(gate_block.reshape(2 * rows, -1), group, axis=0, tiled=True)
    out_matrix = lax.all_gather(out_proj, group, axis=0, tiled=True)
    cot_half, cot = whole_sequence(cotangent, core, place)

    small_all = conv_all.reshape(chips, line, 2, rows, -1)[..., used:].astype(f32)
    taps_full = small_all[..., : CONV + 1, :conv_width].transpose(3, 0, 2, 1, 4).reshape(CONV + 1, XBC)
    taps = jnp.concatenate([own_columns(taps_full[:, :INNER], core), taps_full[:, INNER:]], axis=1)
    gain_pre = small_all[..., CONV + 1, :rows].reshape(model_width)
    gain_gate = lax.dynamic_index_in_dim(
        small_all[..., CONV + 2, :gain_width], core, axis=2, keepdims=False
    ).reshape(HALF)
    params = own_columns(head_params, core)

    seg_len = hidden.shape[1] * hidden.shape[2]
    tokens = SEGS * seg_len
    upstream = cot.reshape(tokens, model_width)
    normed = pre_norm(hidden.reshape(tokens, model_width).astype(f32), gain_pre).astype(bf16)
    projected = dot(normed, conv_all, ((1,), (0,)))
    gate_input = dot(normed, gate_matrix, ((1,), (0,)))
    grad_mixed = dot(upstream, out_matrix, ((1,), (1,)))

    conv_input = projected[:, : HALF + 2 * STATE]
    step_raw = projected[:, HALF + 2 * STATE : used].reshape(SEGS, seg_len, heads)
    rim = borrowed(conv_input[tokens - CONV + 1 :], 1)
    padded = jnp.concatenate([rim, conv_input], axis=0)
    activated, conv_pull = jax.vjp(conv_apply, padded, taps)
    activated = activated.reshape(SEGS, seg_len, -1)
    x_values = activated[:, :, :HALF].reshape(SEGS, seg_len, heads, HEADDIM)
    x_low = x_values.astype(bf16)
    x_wide = x_low.astype(f32)
    b_low = activated[:, :, HALF : HALF + STATE].astype(bf16)
    c_low = activated[:, :, HALF + STATE :].astype(bf16)
    (step_size, decay_sum), head_pull = jax.vjp(head_terms, step_raw, params)
    (carry_scale, decay_all, growth), decay_pull = jax.vjp(decay_terms, decay_sum, step_size)
    scores = jnp.einsum("btn,bsn->bts", c_low, b_low, preferred_element_type=f32)
    causal = lax.broadcasted_iota(jnp.int32, (seg_len, seg_len), 0) >= lax.broadcasted_iota(
        jnp.int32, (seg_len, seg_len), 1
    )
    sum_heads = jnp.transpose(decay_sum, (0, 2, 1))
    step_heads = jnp.transpose(step_size, (0, 2, 1))
    spread = jnp.exp(jnp.where(causal, sum_heads[:, :, :, None] - sum_heads[:, :, None, :], 0.0))
    weights = jnp.where(causal, scores[:, None] * spread * step_heads[:, :, None, :], 0.0).astype(bf16)
    intra = jnp.einsum("bhts,bshp->bthp", weights, x_low, preferred_element_type=f32)
    scaled_x = (carry_scale[:, :, :, None] * x_wide).astype(bf16)
    local_state = jnp.einsum("bshp,bsn->bhpn", scaled_x, b_low, preferred_element_type=f32)

    def scan_states(start, order):
        states, state = [None] * SEGS, start
        for index in order:
            states[index] = state
            part = local_state if order[0] == 0 else grad_prior
            state = decay_all[index][:, None, None] * state + part[index]
        return jnp.stack(states), state

    nothing = jnp.zeros_like(local_state[0])
    forward_order, backward_order = range(SEGS), range(SEGS - 1, -1, -1)
    if line > SEGS:
        start = entering(jnp.prod(decay_all, axis=0), scan_states(nothing, forward_order)[1], 1)
    else:
        start = nothing
    prior_state, _ = scan_states(start, forward_order)
    prior_low = prior_state.astype(bf16)
    c_state = jnp.einsum("btn,bhpn->bthp", c_low, prior_low, preferred_element_type=f32)
    skip_gain = params[2]
    values = intra + growth[:, :, :, None] * c_state + skip_gain[:, None] * x_values
    values = values.reshape(tokens, HALF)

    silu_gate = jax.nn.silu(gate_input)
    gated = values * silu_gate
    gain_grad = grad_mixed * gain_gate
    sums = jnp.stack([jnp.sum(gated * gated, axis=1), jnp.sum(gain_grad * gated, axis=1)])
    sums = (sums + to_partner(sums)) / INNER
    scale = lax.rsqrt(sums[0] + epsilon)[:, None]
    unit = gated * scale
    mixed = (unit * gain_gate).astype(bf16)
    gate_gain_grad = jnp.sum(grad_mixed * unit, axis=0)
    grad_gated = scale * (gain_grad - unit * (scale * sums[1][:, None]))
    grad_values = (grad_gated * silu_gate).reshape(SEGS, seg_len, heads, HEADDIM)
    sigmoid = jax.nn.sigmoid(gate_input)
    grad_gate = (grad_gated * values * (sigmoid * (1.0 + gate_input * (1.0 - sigmoid)))).astype(bf16)

    out_grad = dot(mixed, upstream, ((0,), (0,))).astype(bf16)
    out_share = lax.psum_scatter(out_grad, group, scatter_dimension=0, tiled=True).astype(f32)
    gate_grad = dot(normed, grad_gate, ((0,), (0,))).astype(bf16)
    gate_share = lax.psum_scatter(gate_grad, group, scatter_dimension=0, tiled=True)

    def halves(partial):
        parted = partial.reshape(SEGS, 2, seg_len // 2, model_width)
        mine = lax.dynamic_index_in_dim(parted, core, axis=1, keepdims=False)
        theirs = lax.dynamic_index_in_dim(parted, 1 - core, axis=1, keepdims=False)
        return mine + to_partner(theirs.astype(bf16)).astype(f32)

    branch = halves(dot(mixed, out_matrix, ((1,), (0,))))
    unpermute = lambda array: (
        array.reshape(array.shape[:2] + (chips, line, 2, rows)).transpose(0, 1, 2, 4, 3, 5).reshape(array.shape)
    )
    hidden_out = back_to_owner(
        (unpermute(hidden_half).astype(f32) + branch).astype(bf16), core, place
    )

    skip_grad = jnp.sum(grad_values * x_values, axis=(0, 1, 3))
    grad_x = skip_gain[:, None] * grad_values
    grad_growth = jnp.sum(grad_values * c_state, axis=3)
    grad_cstate = (grad_values * growth[:, :, :, None]).astype(bf16)
    grad_prior = jnp.einsum("bthp,btn->bhpn", grad_cstate, c_low, preferred_element_type=f32)
    grad_c = jnp.einsum("bthp,bhpn->btn", grad_cstate, prior_low, preferred_element_type=f32)
    grad_low = grad_values.astype(bf16)
    grad_weights = jnp.einsum("bthp,bshp->bhts", grad_low, x_low, preferred_element_type=f32)
    grad_x = grad_x + jnp.einsum("bhts,bthp->bshp", weights, grad_low, preferred_element_type=f32)
    if line > SEGS:
        end = entering(jnp.prod(decay_all, axis=0), scan_states(nothing, backward_order)[1], -1)
    else:
        end = nothing
    later_grad, _ = scan_states(end, backward_order)
    grad_decay = jnp.sum(later_grad * prior_state, axis=(2, 3))
    grad_local = later_grad.astype(bf16)
    grad_scaled = jnp.einsum("bhpn,bsn->bshp", grad_local, b_low, preferred_element_type=f32)
    grad_b = jnp.einsum("bshp,bhpn->bsn", scaled_x, grad_local, preferred_element_type=f32)
    grad_carry = jnp.sum(grad_scaled * x_wide, axis=3)
    grad_x = grad_x + carry_scale[:, :, :, None] * grad_scaled
    masked = jnp.where(causal, grad_weights * spread, 0.0)
    grad_scores = jnp.sum(masked * step_heads[:, :, None, :], axis=1)
    grad_step_heads = jnp.sum(masked * scores[:, None], axis=2)
    grad_diff = masked * scores[:, None] * step_heads[:, :, None, :]
    grad_sum_heads = jnp.sum(grad_diff, axis=3) - jnp.sum(grad_diff, axis=2)
    scores_low = grad_scores.astype(bf16)
    grad_c = grad_c + jnp.einsum("bts,bsn->btn", scores_low, b_low, preferred_element_type=f32)
    grad_b = grad_b + jnp.einsum("bts,btn->bsn", scores_low, c_low, preferred_element_type=f32)
    sum_part, step_part = decay_pull((grad_carry, grad_decay, grad_growth))
    grad_sum = sum_part + jnp.transpose(grad_sum_heads, (0, 2, 1))
    grad_step = step_part + jnp.transpose(grad_step_heads, (0, 2, 1))
    grad_raw, head_grad = head_pull((grad_step, grad_sum))
    head_grad = head_grad.at[2].add(skip_grad)

    kept = jnp.where(core == 0, grad_b, grad_c)
    kept = kept + to_partner(jnp.where(core == 0, grad_c, grad_b))
    zero = jnp.zeros_like(kept)
    grad_act = jnp.concatenate(
        [grad_x.reshape(SEGS, seg_len, HALF), jnp.where(core == 0, kept, zero), jnp.where(core == 0, zero, kept)],
        axis=2,
    )
    grad_padded, taps_grad = conv_pull(grad_act.reshape(tokens, -1))
    spill = borrowed(grad_padded[: CONV - 1], -1)
    grad_conv = grad_padded[CONV - 1 :].at[tokens - CONV + 1 :].add(spill)
    state_columns = lax.dynamic_slice_in_dim(grad_conv, HALF + core * STATE, STATE, axis=1)
    width = -(HALF + STATE + heads) % LANES
    grad_proj = jnp.concatenate(
        [grad_conv[:, :HALF], state_columns, grad_raw.reshape(tokens, heads), jnp.zeros((tokens, width), f32)],
        axis=1,
    ).astype(bf16)
    conv_grad = dot(normed, grad_proj, ((0,), (0,))).astype(bf16)
    conv_share = lax.psum_scatter(conv_grad, group, scatter_dimension=0, tiled=True)

    state_weights = lax.dynamic_slice_in_dim(conv_all, HALF + core * STATE, STATE, axis=1)
    conv_matrix = jnp.concatenate(
        [conv_all[:, :HALF], state_weights, conv_all[:, HALF + 2 * STATE : HALF + 2 * STATE + heads + width]], axis=1
    )
    grad_normed = halves(
        dot(grad_gate, gate_matrix, ((1,), (1,))) + dot(grad_proj, conv_matrix, ((1,), (1,)))
    )
    _, pre_pull = jax.vjp(pre_norm, hidden_half.astype(f32), gain_pre)
    grad_hidden, pre_gain_grad = pre_pull(grad_normed)
    grad_in = back_to_owner(
        (cot_half.astype(f32) + unpermute(grad_hidden)).astype(bf16), core, place
    )

    def spread_own(array):
        width = array.shape[-1] // chips
        parted = array.reshape(array.shape[:-1] + (chips, 1, width))
        none = jnp.zeros_like(parted)
        both = jnp.where(
            core == 0,
            jnp.concatenate([parted, none], axis=-2),
            jnp.concatenate([none, parted], axis=-2),
        )
        return both.reshape(array.shape[:-1] + (2 * array.shape[-1],))

    taps_all = jnp.concatenate([spread_own(taps_grad[:, :HALF]), taps_grad[:, HALF:]], axis=1)
    taps_all = taps_all.reshape(CONV + 1, chips, 2, line, conv_width).transpose(1, 3, 2, 0, 4)
    gate_all = spread_own(gate_gain_grad).reshape(chips, 2, line, gain_width).transpose(0, 2, 1, 3)
    head_all = jnp.broadcast_to(spread_own(head_grad).reshape(-1), (chips, line, 2, 3 * HEADS))
    small_grads = jnp.concatenate(
        [
            taps_all.reshape(chips, line, 2, -1),
            pre_gain_grad.reshape(chips, line, 2, rows),
            gate_all,
            head_all,
        ],
        axis=3,
    )
    count = small_grads.shape[3]
    small_share = lax.psum_scatter(
        small_grads.reshape(chips * line, 2 * count), group, scatter_dimension=0, tiled=True
    ).reshape(2, count)

    def mine_and_partner(share):
        keep = lax.dynamic_index_in_dim(share, core, axis=0, keepdims=False)
        give = lax.dynamic_index_in_dim(share, 1 - core, axis=0, keepdims=False)
        return keep, to_partner(give)

    keep, got = mine_and_partner(small_share)
    small_total = keep + got
    taps_end = (CONV + 1) * conv_width
    taps_share = small_total[:taps_end].reshape(CONV + 1, conv_width)
    pre_share = small_total[taps_end : taps_end + rows]
    gain_share = small_total[taps_end + rows : taps_end + rows + gain_width]
    head_total = small_total[taps_end + rows + gain_width :].reshape(3, HEADS)

    def interleave(mine, theirs):
        width = mine.shape[1] // chips
        both = in_core_order(mine.reshape(rows, chips, width), theirs.reshape(rows, chips, width), core, 2)
        return both.reshape(rows, -1)

    keep_gate, got_gate = mine_and_partner(gate_share.reshape(2, rows, -1))
    keep, got = mine_and_partner(conv_share.reshape(2, rows, -1))
    state_end = HALF + STATE
    in_share = jnp.concatenate(
        [
            interleave(keep_gate, got_gate),
            interleave(keep[:, :HALF], got[:, :HALF]),
            in_core_order(keep[:, HALF:state_end], got[:, HALF:state_end], core, 1).reshape(rows, -1),
            interleave(keep[:, state_end : state_end + heads], got[:, state_end : state_end + heads]),
        ],
        axis=1,
    ).astype(f32)
    return (hidden_out, grad_in, in_share, out_share, taps_share, pre_share, gain_share, head_total)


def solution(mesh):
    devices = mesh.devices
    cores = Mesh(devices.reshape(devices.shape[0] // 2, 2, devices.shape[1]), ("chip", "core", "seg"))
    dp, both = ("chip", "core"), ("chip", "core", "seg")
    tokens = P(dp, "seg", None)
    return jax.shard_map(
        per_device,
        mesh=cores,
        in_specs=(tokens, tokens, P(both, None), P(both, None), P(None, both), P(both), P(both), P()),
        out_specs=(tokens, tokens, P(both, None), P(both, None), P(None, both), P(both), P(both), P()),
        check_vma=False,
    )
```

```python
import jax
import jax.numpy as jnp
from jax import lax
from jax.experimental import pallas as pl
from jax.experimental.pallas import tpu as pltpu
from jax.sharding import Mesh
from jax.sharding import PartitionSpec as P

HEADS = 48
HEADDIM = 64
STATE = 128
CONV = 4
INNER = 3072
XBC = 3328
HALF = INNER // 2
LANES = 128
SEGS = 4

epsilon = 1e-05
f32 = jnp.float32
bf16 = jnp.bfloat16


def own_columns(array, core):
    chips = lax.axis_size("chip")
    width = array.shape[-1] // (2 * chips)
    parted = array.reshape(array.shape[:-1] + (chips, 2, width))
    picked = lax.dynamic_index_in_dim(parted, core, axis=parted.ndim - 2, keepdims=False)
    return picked.reshape(array.shape[:-1] + (chips * width,))


def to_partner(array):
    return lax.ppermute(array, "core", [(0, 1), (1, 0)])


def in_core_order(mine, theirs, core, axis):
    first = jnp.where(core == 0, mine, theirs)
    second = jnp.where(core == 0, theirs, mine)
    return jnp.stack([first, second], axis=axis)


def chip_dims():
    return (lax.axis_size("chip") // 2, 2, lax.axis_size("seg"))


def chip_place():
    chip = lax.axis_index("chip")
    return (chip // 2, chip % 2, lax.axis_index("seg"))


def moved(array, dim, by):
    sizes = chip_dims()
    index = lambda at: (at[0] * sizes[1] + at[1]) * sizes[2] + at[2]
    pairs = []
    for a in range(sizes[0]):
        for b in range(sizes[1]):
            for z in range(sizes[2]):
                to = [a, b, z]
                to[dim] = (to[dim] + by) % sizes[dim]
                pairs.append((index((a, b, z)), index(to)))
    return lax.ppermute(array, ("chip", "seg"), pairs)


def gathered(block, order):
    data = block
    for dim in order[:-1]:
        data = jnp.stack([data] + [moved(data, dim, by) for by in range(1, chip_dims()[dim])])
    return [data] + [moved(data, order[-1], by) for by in range(1, chip_dims()[order[-1]])]


def placed_kernel(plan, place_ref, *refs):
    sources, out_ref, sems = refs[:-2], refs[-2], refs[-1]
    copies = []
    for source, lead, at, columns, paired in plan:
        spot = [lax.rem(place_ref[dim] + (size - back), size) for dim, (back, size) in enumerate(at)]
        target = out_ref.at[spot[0], spot[1]]
        target = target.at[:, spot[2]] if paired else target.at[spot[2]]
        target = target.at[..., pl.ds(*columns)]
        copies.append(pltpu.make_async_copy(sources[source].at[lead], target, sems.at[len(copies)]))
    for copy in copies:
        copy.start()
    for copy in copies:
        copy.wait()


def whole_matrix(block, paired):
    width = block.shape[-1]
    cut = -(-(width // 2) // LANES) * LANES
    sizes = chip_dims()
    plan, sources = [], []
    for order, (begin, end) in (((2, 0, 1), (0, cut)), ((2, 1, 0), (cut, width))):
        parts = gathered(block[..., begin:end], order)
        for back_last, part in enumerate(parts):
            for back_mid in range(sizes[order[1]]):
                for back_first in range(sizes[order[0]]):
                    at = [None] * 3
                    at[order[2]] = (back_last, sizes[order[2]])
                    at[order[1]] = (back_mid, sizes[order[1]])
                    at[order[0]] = (back_first, sizes[order[0]])
                    plan.append((len(sources), (back_mid, back_first), at, (begin, end - begin), paired))
            sources.append(part)
    if paired:
        shape = sizes[:2] + (2, sizes[2]) + block.shape[1:]
    else:
        shape = sizes + block.shape
    anywhere = pl.BlockSpec(memory_space=pl.ANY)
    return pl.pallas_call(
        lambda *refs: placed_kernel(plan, *refs),
        out_shape=jax.ShapeDtypeStruct(shape, block.dtype),
        in_specs=[pl.BlockSpec(memory_space=pltpu.SMEM)] + [anywhere] * len(sources),
        out_specs=anywhere,
        scratch_shapes=[pltpu.SemaphoreType.DMA((len(plan),))],
        cost_estimate=pl.CostEstimate(flops=0, bytes_accessed=4 * block.size * sizes[0] * sizes[1] * sizes[2], transcendentals=0),
    )(jnp.stack(chip_place()).astype(jnp.int32), *sources)


def summed(partial, order, wire):
    place, sizes = chip_place(), chip_dims()
    data, left = partial, [0, 1, 2]
    for dim in order:
        axis = left.index(dim)
        left.remove(dim)
        pick = lambda at: lax.dynamic_index_in_dim(data, at, axis=axis, keepdims=False)
        sent = [
            moved(pick((place[dim] + by) % sizes[dim]).astype(wire), dim, by) for by in range(1, sizes[dim])
        ]
        data = pick(place[dim]).astype(f32)
        for part in sent:
            data = data + part.astype(f32)
    return data


def owner_share(partial):
    width = partial.shape[-1]
    cut = -(-(width // 2) // LANES) * LANES
    return jnp.concatenate(
        [summed(partial[..., :cut], (1, 0, 2), bf16), summed(partial[..., cut:], (0, 1, 2), bf16)], axis=-1
    )


def line_perm(turn, back):
    line = lax.axis_size("seg")
    parts = line // SEGS
    pairs = []
    for core in range(2):
        for place in range(line):
            piece = (place % SEGS) ^ turn
            half, index = divmod(piece, 2)
            source = core * line + place
            target = half * line + (2 * core + index) * parts + place // SEGS
            pairs.append((target, source) if back else (source, target))
    return pairs


def whole_sequence(array, core, place):
    parts = lax.axis_size("seg") // SEGS
    half = array.shape[1] // 2
    pieces = array.reshape(2, 2, half, -1).transpose(1, 0, 2, 3).reshape(4, half, -1)
    mine = place % SEGS
    target = 2 * core + (place // parts) % 2
    got = []
    for turn in range(4):
        piece = lax.dynamic_index_in_dim(pieces, mine ^ turn, axis=0, keepdims=False)
        got.append(lax.ppermute(piece, ("core", "seg"), line_perm(turn, False)))
    got = jnp.stack(got)
    ordered = jnp.stack([lax.dynamic_index_in_dim(got, target ^ k, axis=0, keepdims=False) for k in range(4)])
    return ordered, in_core_order(ordered, to_partner(ordered), core, 1)


def back_to_owner(ordered, core, place):
    parts = lax.axis_size("seg") // SEGS
    half = ordered.shape[1]
    mine = place % SEGS
    target = 2 * core + (place // parts) % 2
    got = []
    for turn in range(4):
        piece = lax.dynamic_index_in_dim(ordered, target ^ turn, axis=0, keepdims=False)
        got.append(lax.ppermute(piece, ("core", "seg"), line_perm(turn, True)))
    got = jnp.stack(got)
    pieces = jnp.stack([lax.dynamic_index_in_dim(got, mine ^ k, axis=0, keepdims=False) for k in range(4)])
    return pieces.reshape(2, 2, half, -1).transpose(1, 0, 2, 3).reshape(2, 2 * half, -1)


def part_pairs(step):
    line = lax.axis_size("seg")
    parts = line // SEGS
    return [(i, i + step) for i in range(line) if 0 <= i + step < line and i // parts == (i + step) // parts]


def entering(decay, state, step):
    parts = lax.axis_size("seg") // SEGS
    total = jnp.zeros_like(state)
    for _ in range(parts - 1):
        total = lax.ppermute(decay[:, None, None] * total + state, "seg", part_pairs(step))
    return total


def borrowed(array, step):
    parts = lax.axis_size("seg") // SEGS
    if parts == 1:
        return jnp.zeros_like(array)
    return lax.ppermute(array, "seg", part_pairs(step))


def pre_norm(hidden, norm_gain):
    row_scale = lax.rsqrt(jnp.mean(hidden * hidden, axis=-1, keepdims=True) + epsilon)
    return hidden * row_scale * norm_gain


def conv_apply(padded, conv_taps):
    length = padded.shape[0] - CONV + 1
    summed = conv_taps[CONV]
    for offset in range(CONV):
        summed = summed + conv_taps[offset] * padded[offset : offset + length, :]
    return jax.nn.silu(summed)


def head_terms(step_raw, params):
    step_size = jax.nn.softplus(step_raw + params[1])
    decay_sum = jnp.cumsum(step_size * -jnp.exp(params[0]), axis=1)
    return (step_size, decay_sum)


def decay_terms(decay_sum, step_size):
    last_sum = decay_sum[:, -1:, :]
    carry_scale = jnp.exp(last_sum - decay_sum) * step_size
    return (carry_scale, jnp.exp(decay_sum[:, -1, :]), jnp.exp(decay_sum))


def dot(a, b, contract):
    return lax.dot_general(a, b, (contract, ((), ())), preferred_element_type=f32)


def per_device(hidden_in, cotangent, in_proj, out_proj, conv_params, pre_gain, gated_gain, head_params):
    chips, line = lax.axis_size("chip"), lax.axis_size("seg")
    core, place = lax.axis_index("core"), lax.axis_index("seg")
    rows, model_width = in_proj.shape[0], hidden_in.shape[2]
    heads = HEADS // 2

    hidden_half, hidden = whole_sequence(hidden_in, core, place)
    conv_width, gain_width = conv_params.shape[1], gated_gain.shape[0]
    used = HALF + 2 * STATE + heads
    spare = -used % LANES
    small = jnp.zeros((rows, spare), bf16)
    small = small.at[: CONV + 1, :conv_width].set(conv_params)
    small = small.at[CONV + 1, :rows].set(pre_gain)
    small = small.at[CONV + 2, :gain_width].set(gated_gain)

    def conv_side(which):
        return jnp.concatenate(
            [
                own_columns(in_proj[:, INNER : 2 * INNER], which),
                in_proj[:, 2 * INNER : INNER + XBC],
                own_columns(in_proj[:, INNER + XBC :], which),
                small,
            ],
            axis=1,
        )

    def gate_side(which):
        return own_columns(in_proj[:, :INNER], which)

    conv_block = in_core_order(conv_side(core), to_partner(conv_side(1 - core)), core, 0)
    gate_block = in_core_order(gate_side(core), to_partner(gate_side(1 - core)), core, 0)
    conv_all = whole_matrix(conv_block, True).reshape(model_width, -1)
    gate_matrix = whole_matrix(gate_block, True).reshape(model_width, -1)
    out_matrix = whole_matrix(out_proj, False).reshape(HALF, model_width)
    cot_half, cot = whole_sequence(cotangent, core, place)

    small_all = conv_all.reshape(chips, 2, line, rows, -1)[..., used:].astype(f32)
    taps_full = small_all[..., : CONV + 1, :conv_width].transpose(3, 0, 1, 2, 4).reshape(CONV + 1, XBC)
    taps = jnp.concatenate([own_columns(taps_full[:, :INNER], core), taps_full[:, INNER:]], axis=1)
    gain_pre = small_all[..., CONV + 1, :rows].reshape(model_width)
    gain_gate = lax.dynamic_index_in_dim(
        small_all[..., CONV + 2, :gain_width], core, axis=1, keepdims=False
    ).reshape(HALF)
    params = own_columns(head_params, core)

    seg_len = hidden.shape[1] * hidden.shape[2]
    tokens = SEGS * seg_len
    upstream = cot.reshape(tokens, model_width)
    normed = pre_norm(hidden.reshape(tokens, model_width).astype(f32), gain_pre).astype(bf16)
    projected = dot(normed, conv_all, ((1,), (0,)))
    gate_input = dot(normed, gate_matrix, ((1,), (0,)))
    grad_mixed = dot(upstream, out_matrix, ((1,), (1,)))

    conv_input = projected[:, : HALF + 2 * STATE]
    step_raw = projected[:, HALF + 2 * STATE : used].reshape(SEGS, seg_len, heads)
    rim = borrowed(conv_input[tokens - CONV + 1 :], 1)
    padded = jnp.concatenate([rim, conv_input], axis=0)
    activated, conv_pull = jax.vjp(conv_apply, padded, taps)
    activated = activated.reshape(SEGS, seg_len, -1)
    x_values = activated[:, :, :HALF].reshape(SEGS, seg_len, heads, HEADDIM)
    x_low = x_values.astype(bf16)
    x_wide = x_low.astype(f32)
    b_low = activated[:, :, HALF : HALF + STATE].astype(bf16)
    c_low = activated[:, :, HALF + STATE :].astype(bf16)
    (step_size, decay_sum), head_pull = jax.vjp(head_terms, step_raw, params)
    (carry_scale, decay_all, growth), decay_pull = jax.vjp(decay_terms, decay_sum, step_size)
    scores = jnp.einsum("btn,bsn->bts", c_low, b_low, preferred_element_type=f32)
    causal = lax.broadcasted_iota(jnp.int32, (seg_len, seg_len), 0) >= lax.broadcasted_iota(
        jnp.int32, (seg_len, seg_len), 1
    )
    sum_heads = jnp.transpose(decay_sum, (0, 2, 1))
    step_heads = jnp.transpose(step_size, (0, 2, 1))
    spread = jnp.exp(jnp.where(causal, sum_heads[:, :, :, None] - sum_heads[:, :, None, :], 0.0))
    weights = jnp.where(causal, scores[:, None] * spread * step_heads[:, :, None, :], 0.0).astype(bf16)
    intra = jnp.einsum("bhts,bshp->bthp", weights, x_low, preferred_element_type=f32)
    scaled_x = (carry_scale[:, :, :, None] * x_wide).astype(bf16)
    local_state = jnp.einsum("bshp,bsn->bhpn", scaled_x, b_low, preferred_element_type=f32)

    def scan_states(start, order):
        states, state = [None] * SEGS, start
        for index in order:
            states[index] = state
            part = local_state if order[0] == 0 else grad_prior
            state = decay_all[index][:, None, None] * state + part[index]
        return jnp.stack(states), state

    nothing = jnp.zeros_like(local_state[0])
    forward_order, backward_order = range(SEGS), range(SEGS - 1, -1, -1)
    if line > SEGS:
        start = entering(jnp.prod(decay_all, axis=0), scan_states(nothing, forward_order)[1], 1)
    else:
        start = nothing
    prior_state, _ = scan_states(start, forward_order)
    prior_low = prior_state.astype(bf16)
    c_state = jnp.einsum("btn,bhpn->bthp", c_low, prior_low, preferred_element_type=f32)
    skip_gain = params[2]
    values = intra + growth[:, :, :, None] * c_state + skip_gain[:, None] * x_values
    values = values.reshape(tokens, HALF)

    silu_gate = jax.nn.silu(gate_input)
    gated = values * silu_gate
    gain_grad = grad_mixed * gain_gate
    sums = jnp.stack([jnp.sum(gated * gated, axis=1), jnp.sum(gain_grad * gated, axis=1)])
    sums = (sums + to_partner(sums)) / INNER
    scale = lax.rsqrt(sums[0] + epsilon)[:, None]
    unit = gated * scale
    mixed = (unit * gain_gate).astype(bf16)
    gate_gain_grad = jnp.sum(grad_mixed * unit, axis=0)
    grad_gated = scale * (gain_grad - unit * (scale * sums[1][:, None]))
    grad_values = (grad_gated * silu_gate).reshape(SEGS, seg_len, heads, HEADDIM)
    sigmoid = jax.nn.sigmoid(gate_input)
    grad_gate = (grad_gated * values * (sigmoid * (1.0 + gate_input * (1.0 - sigmoid)))).astype(bf16)

    out_grad = dot(mixed, upstream, ((0,), (0,)))
    out_share = owner_share(out_grad.reshape(chip_dims() + (-1, model_width)))

    def paired_share(grad):
        a, b, z = chip_dims()
        parted = grad.reshape(a, b, 2, z, rows, -1).transpose(0, 1, 3, 2, 4, 5)
        return owner_share(parted)

    gate_share = paired_share(dot(normed, grad_gate, ((0,), (0,)))).astype(bf16)

    def halves(partial):
        parted = partial.reshape(SEGS, 2, seg_len // 2, model_width)
        mine = lax.dynamic_index_in_dim(parted, core, axis=1, keepdims=False)
        theirs = lax.dynamic_index_in_dim(parted, 1 - core, axis=1, keepdims=False)
        return mine + to_partner(theirs.astype(bf16)).astype(f32)

    branch = halves(dot(mixed, out_matrix, ((1,), (0,))))
    hidden_out = back_to_owner(
        (hidden_half.astype(f32) + branch).astype(bf16), core, place
    )

    skip_grad = jnp.sum(grad_values * x_values, axis=(0, 1, 3))
    grad_x = skip_gain[:, None] * grad_values
    grad_growth = jnp.sum(grad_values * c_state, axis=3)
    grad_cstate = (grad_values * growth[:, :, :, None]).astype(bf16)
    grad_prior = jnp.einsum("bthp,btn->bhpn", grad_cstate, c_low, preferred_element_type=f32)
    grad_c = jnp.einsum("bthp,bhpn->btn", grad_cstate, prior_low, preferred_element_type=f32)
    grad_low = grad_values.astype(bf16)
    grad_weights = jnp.einsum("bthp,bshp->bhts", grad_low, x_low, preferred_element_type=f32)
    grad_x = grad_x + jnp.einsum("bhts,bthp->bshp", weights, grad_low, preferred_element_type=f32)
    if line > SEGS:
        end = entering(jnp.prod(decay_all, axis=0), scan_states(nothing, backward_order)[1], -1)
    else:
        end = nothing
    later_grad, _ = scan_states(end, backward_order)
    grad_decay = jnp.sum(later_grad * prior_state, axis=(2, 3))
    grad_local = later_grad.astype(bf16)
    grad_scaled = jnp.einsum("bhpn,bsn->bshp", grad_local, b_low, preferred_element_type=f32)
    grad_b = jnp.einsum("bshp,bhpn->bsn", scaled_x, grad_local, preferred_element_type=f32)
    grad_carry = jnp.sum(grad_scaled * x_wide, axis=3)
    grad_x = grad_x + carry_scale[:, :, :, None] * grad_scaled
    masked = jnp.where(causal, grad_weights * spread, 0.0)
    grad_scores = jnp.sum(masked * step_heads[:, :, None, :], axis=1)
    grad_step_heads = jnp.sum(masked * scores[:, None], axis=2)
    grad_diff = masked * scores[:, None] * step_heads[:, :, None, :]
    grad_sum_heads = jnp.sum(grad_diff, axis=3) - jnp.sum(grad_diff, axis=2)
    scores_low = grad_scores.astype(bf16)
    grad_c = grad_c + jnp.einsum("bts,bsn->btn", scores_low, b_low, preferred_element_type=f32)
    grad_b = grad_b + jnp.einsum("bts,btn->bsn", scores_low, c_low, preferred_element_type=f32)
    sum_part, step_part = decay_pull((grad_carry, grad_decay, grad_growth))
    grad_sum = sum_part + jnp.transpose(grad_sum_heads, (0, 2, 1))
    grad_step = step_part + jnp.transpose(grad_step_heads, (0, 2, 1))
    grad_raw, head_grad = head_pull((grad_step, grad_sum))
    head_grad = head_grad.at[2].add(skip_grad)

    kept = jnp.where(core == 0, grad_b, grad_c)
    kept = kept + to_partner(jnp.where(core == 0, grad_c, grad_b))
    zero = jnp.zeros_like(kept)
    grad_act = jnp.concatenate(
        [grad_x.reshape(SEGS, seg_len, HALF), jnp.where(core == 0, kept, zero), jnp.where(core == 0, zero, kept)],
        axis=2,
    )
    grad_padded, taps_grad = conv_pull(grad_act.reshape(tokens, -1))
    spill = borrowed(grad_padded[: CONV - 1], -1)
    grad_conv = grad_padded[CONV - 1 :].at[tokens - CONV + 1 :].add(spill)
    state_columns = lax.dynamic_slice_in_dim(grad_conv, HALF + core * STATE, STATE, axis=1)
    width = -(HALF + STATE + heads) % LANES
    grad_proj = jnp.concatenate(
        [grad_conv[:, :HALF], state_columns, grad_raw.reshape(tokens, heads), jnp.zeros((tokens, width), f32)],
        axis=1,
    ).astype(bf16)
    conv_share = paired_share(dot(normed, grad_proj, ((0,), (0,)))).astype(bf16)

    state_weights = lax.dynamic_slice_in_dim(conv_all, HALF + core * STATE, STATE, axis=1)
    conv_matrix = jnp.concatenate(
        [conv_all[:, :HALF], state_weights, conv_all[:, HALF + 2 * STATE : HALF + 2 * STATE + heads + width]], axis=1
    )
    grad_normed = halves(
        dot(grad_gate, gate_matrix, ((1,), (1,))) + dot(grad_proj, conv_matrix, ((1,), (1,)))
    )
    _, pre_pull = jax.vjp(pre_norm, hidden_half.astype(f32), gain_pre)
    grad_hidden, pre_gain_grad = pre_pull(grad_normed)
    grad_in = back_to_owner(
        (cot_half.astype(f32) + grad_hidden).astype(bf16), core, place
    )

    def spread_own(array):
        width = array.shape[-1] // chips
        parted = array.reshape(array.shape[:-1] + (chips, 1, width))
        none = jnp.zeros_like(parted)
        both = jnp.where(
            core == 0,
            jnp.concatenate([parted, none], axis=-2),
            jnp.concatenate([none, parted], axis=-2),
        )
        return both.reshape(array.shape[:-1] + (2 * array.shape[-1],))

    taps_all = jnp.concatenate([spread_own(taps_grad[:, :HALF]), taps_grad[:, HALF:]], axis=1)
    taps_all = taps_all.reshape(CONV + 1, chips, 2, line, conv_width).transpose(1, 3, 2, 0, 4)
    gate_all = spread_own(gate_gain_grad).reshape(chips, 2, line, gain_width).transpose(0, 2, 1, 3)
    head_all = jnp.broadcast_to(spread_own(head_grad).reshape(-1), (chips, line, 2, 3 * HEADS))
    small_grads = jnp.concatenate(
        [
            taps_all.reshape(chips, line, 2, -1),
            pre_gain_grad.reshape(chips, 2, line, rows).transpose(0, 2, 1, 3),
            gate_all,
            head_all,
        ],
        axis=3,
    )
    count = small_grads.shape[3]
    small_share = summed(small_grads.reshape(chip_dims() + (2, count)), (1, 0, 2), f32)

    def mine_and_partner(share):
        keep = lax.dynamic_index_in_dim(share, core, axis=0, keepdims=False)
        give = lax.dynamic_index_in_dim(share, 1 - core, axis=0, keepdims=False)
        return keep, to_partner(give)

    keep, got = mine_and_partner(small_share)
    small_total = keep + got
    taps_end = (CONV + 1) * conv_width
    taps_share = small_total[:taps_end].reshape(CONV + 1, conv_width)
    pre_share = small_total[taps_end : taps_end + rows]
    gain_share = small_total[taps_end + rows : taps_end + rows + gain_width]
    head_total = small_total[taps_end + rows + gain_width :].reshape(3, HEADS)

    def interleave(mine, theirs):
        width = mine.shape[1] // chips
        both = in_core_order(mine.reshape(rows, chips, width), theirs.reshape(rows, chips, width), core, 2)
        return both.reshape(rows, -1)

    keep_gate, got_gate = mine_and_partner(gate_share)
    keep, got = mine_and_partner(conv_share)
    state_end = HALF + STATE
    in_share = jnp.concatenate(
        [
            interleave(keep_gate, got_gate),
            interleave(keep[:, :HALF], got[:, :HALF]),
            in_core_order(keep[:, HALF:state_end], got[:, HALF:state_end], core, 1).reshape(rows, -1),
            interleave(keep[:, state_end : state_end + heads], got[:, state_end : state_end + heads]),
        ],
        axis=1,
    ).astype(f32)
    return (hidden_out, grad_in, in_share, out_share, taps_share, pre_share, gain_share, head_total)


def solution(mesh):
    devices = mesh.devices
    cores = Mesh(devices.reshape(devices.shape[0] // 2, 2, devices.shape[1]), ("chip", "core", "seg"))
    dp, both = ("chip", "core"), ("chip", "core", "seg")
    tokens = P(dp, "seg", None)
    return jax.shard_map(
        per_device,
        mesh=cores,
        in_specs=(tokens, tokens, P(both, None), P(both, None), P(None, both), P(both), P(both), P()),
        out_specs=(tokens, tokens, P(both, None), P(both, None), P(None, both), P(both), P(both), P()),
        check_vma=False,
    )
```

```python
import jax
import jax.numpy as jnp
from jax import lax
from jax.experimental import pallas as pl
from jax.experimental.pallas import tpu as pltpu
from jax.sharding import Mesh
from jax.sharding import PartitionSpec as P

HEADS = 48
HEADDIM = 64
STATE = 128
CONV = 4
INNER = 3072
XBC = 3328
HALF = INNER // 2
LANES = 128
SEGS = 4
VMEM_LIMIT = 48 * 1024 * 1024
LOG2E = 1.4426950408889634

epsilon = 1e-05
f32 = jnp.float32
bf16 = jnp.bfloat16


def own_columns(array, core):
    chips = lax.axis_size("chip")
    width = array.shape[-1] // (2 * chips)
    parted = array.reshape(array.shape[:-1] + (chips, 2, width))
    picked = lax.dynamic_index_in_dim(parted, core, axis=parted.ndim - 2, keepdims=False)
    return picked.reshape(array.shape[:-1] + (chips * width,))


def to_partner(array):
    return lax.ppermute(array, "core", [(0, 1), (1, 0)])


def in_core_order(mine, theirs, core, axis):
    first = jnp.where(core == 0, mine, theirs)
    second = jnp.where(core == 0, theirs, mine)
    return jnp.stack([first, second], axis=axis)


def chip_dims():
    return (lax.axis_size("chip") // 2, 2, lax.axis_size("seg"))


def chip_place():
    chip = lax.axis_index("chip")
    return (chip // 2, chip % 2, lax.axis_index("seg"))


def moved(array, dim, by):
    sizes = chip_dims()
    index = lambda at: (at[0] * sizes[1] + at[1]) * sizes[2] + at[2]
    pairs = []
    for a in range(sizes[0]):
        for b in range(sizes[1]):
            for z in range(sizes[2]):
                to = [a, b, z]
                to[dim] = (to[dim] + by) % sizes[dim]
                pairs.append((index((a, b, z)), index(to)))
    return lax.ppermute(array, ("chip", "seg"), pairs)


def gathered(block, order):
    data = block
    for dim in order[:-1]:
        data = jnp.stack([data] + [moved(data, dim, by) for by in range(1, chip_dims()[dim])])
    return [data] + [moved(data, order[-1], by) for by in range(1, chip_dims()[order[-1]])]


def placed_kernel(plan, place_ref, *refs):
    sources, out_ref, sems = refs[:-2], refs[-2], refs[-1]
    copies = []
    for source, lead, at, columns, paired in plan:
        spot = [lax.rem(place_ref[dim] + (size - back), size) for dim, (back, size) in enumerate(at)]
        target = out_ref.at[spot[0], spot[1]]
        target = target.at[:, spot[2]] if paired else target.at[spot[2]]
        target = target.at[..., pl.ds(*columns)]
        copies.append(pltpu.make_async_copy(sources[source].at[lead], target, sems.at[len(copies)]))
    for copy in copies:
        copy.start()
    for copy in copies:
        copy.wait()


def whole_matrix(block, paired):
    width = block.shape[-1]
    cut = -(-(width // 2) // LANES) * LANES
    sizes = chip_dims()
    plan, sources = [], []
    for order, (begin, end) in (((2, 0, 1), (0, cut)), ((2, 1, 0), (cut, width))):
        parts = gathered(block[..., begin:end], order)
        for back_last, part in enumerate(parts):
            for back_mid in range(sizes[order[1]]):
                for back_first in range(sizes[order[0]]):
                    at = [None] * 3
                    at[order[2]] = (back_last, sizes[order[2]])
                    at[order[1]] = (back_mid, sizes[order[1]])
                    at[order[0]] = (back_first, sizes[order[0]])
                    plan.append((len(sources), (back_mid, back_first), at, (begin, end - begin), paired))
            sources.append(part)
    if paired:
        shape = sizes[:2] + (2, sizes[2]) + block.shape[1:]
    else:
        shape = sizes + block.shape
    anywhere = pl.BlockSpec(memory_space=pl.ANY)
    return pl.pallas_call(
        lambda *refs: placed_kernel(plan, *refs),
        out_shape=jax.ShapeDtypeStruct(shape, block.dtype),
        in_specs=[pl.BlockSpec(memory_space=pltpu.SMEM)] + [anywhere] * len(sources),
        out_specs=pl.BlockSpec(memory_space=pltpu.VMEM),
        scratch_shapes=[pltpu.SemaphoreType.DMA((len(plan),))],
        compiler_params=pltpu.CompilerParams(vmem_limit_bytes=VMEM_LIMIT),
        cost_estimate=pl.CostEstimate(flops=0, bytes_accessed=4 * block.size * sizes[0] * sizes[1] * sizes[2], transcendentals=0),
    )(jnp.stack(chip_place()).astype(jnp.int32), *sources)


def summed(partial, order, wire):
    place, sizes = chip_place(), chip_dims()
    data, left = partial, [0, 1, 2]
    for dim in order:
        axis = left.index(dim)
        left.remove(dim)
        pick = lambda at: lax.dynamic_index_in_dim(data, at, axis=axis, keepdims=False)
        sent = [
            moved(pick((place[dim] + by) % sizes[dim]).astype(wire), dim, by) for by in range(1, sizes[dim])
        ]
        data = pick(place[dim]).astype(f32)
        for part in sent:
            data = data + part.astype(f32)
    return data


def owner_share(partial):
    width = partial.shape[-1]
    cut = -(-(width // 2) // LANES) * LANES
    return jnp.concatenate(
        [summed(partial[..., :cut], (1, 0, 2), bf16), summed(partial[..., cut:], (0, 1, 2), bf16)], axis=-1
    )


def line_perm(turn, back):
    line = lax.axis_size("seg")
    parts = line // SEGS
    pairs = []
    for core in range(2):
        for place in range(line):
            piece = (place % SEGS) ^ turn
            half, index = divmod(piece, 2)
            source = core * line + place
            target = half * line + (2 * core + index) * parts + place // SEGS
            pairs.append((target, source) if back else (source, target))
    return pairs


def whole_sequence(array, core, place):
    parts = lax.axis_size("seg") // SEGS
    half = array.shape[1] // 2
    pieces = array.reshape(2, 2, half, -1).transpose(1, 0, 2, 3).reshape(4, half, -1)
    mine = place % SEGS
    target = 2 * core + (place // parts) % 2
    got = []
    for turn in range(4):
        piece = lax.dynamic_index_in_dim(pieces, mine ^ turn, axis=0, keepdims=False)
        got.append(lax.ppermute(piece, ("core", "seg"), line_perm(turn, False)))
    got = jnp.stack(got)
    ordered = jnp.stack([lax.dynamic_index_in_dim(got, target ^ k, axis=0, keepdims=False) for k in range(4)])
    return ordered, in_core_order(ordered, to_partner(ordered), core, 1)


def back_to_owner(ordered, core, place):
    parts = lax.axis_size("seg") // SEGS
    half = ordered.shape[1]
    mine = place % SEGS
    target = 2 * core + (place // parts) % 2
    got = []
    for turn in range(4):
        piece = lax.dynamic_index_in_dim(ordered, target ^ turn, axis=0, keepdims=False)
        got.append(lax.ppermute(piece, ("core", "seg"), line_perm(turn, True)))
    got = jnp.stack(got)
    pieces = jnp.stack([lax.dynamic_index_in_dim(got, mine ^ k, axis=0, keepdims=False) for k in range(4)])
    return pieces.reshape(2, 2, half, -1).transpose(1, 0, 2, 3).reshape(2, 2 * half, -1)


def part_pairs(step):
    line = lax.axis_size("seg")
    parts = line // SEGS
    return [(i, i + step) for i in range(line) if 0 <= i + step < line and i // parts == (i + step) // parts]


def entering(decay, state, step):
    parts = lax.axis_size("seg") // SEGS
    total = jnp.zeros_like(state)
    for _ in range(parts - 1):
        total = lax.ppermute(decay * total + state, "seg", part_pairs(step))
    return total


def borrowed(array, step):
    parts = lax.axis_size("seg") // SEGS
    if parts == 1:
        return jnp.zeros_like(array)
    return lax.ppermute(array, "seg", part_pairs(step))


def pre_norm(hidden, norm_gain):
    row_scale = lax.rsqrt(jnp.mean(hidden * hidden, axis=-1, keepdims=True) + epsilon)
    return hidden * row_scale * norm_gain


def conv_apply(padded, conv_taps):
    length = padded.shape[0] - CONV + 1
    summed = conv_taps[CONV]
    for offset in range(CONV):
        summed = summed + conv_taps[offset] * padded[offset : offset + length, :]
    return jax.nn.silu(summed)


def head_terms(step_raw, params):
    step_size = jax.nn.softplus(step_raw + params[1])
    decay_sum = jnp.cumsum(step_size * -jnp.exp(params[0]), axis=1)
    return (step_size, decay_sum)


def decay_terms(decay_sum, step_size):
    last_sum = decay_sum[:, -1:, :]
    carry_scale = jnp.exp(last_sum - decay_sum) * step_size
    return (carry_scale, jnp.exp(decay_sum[:, -1, :]), jnp.exp(decay_sum))


def dot(a, b, contract):
    return lax.dot_general(a, b, (contract, ((), ())), preferred_element_type=f32)


def columns_of(pair):
    return pl.ds(pair * LANES, LANES)


def low_half(shape):
    return lax.broadcasted_iota(jnp.int32, shape, len(shape) - 1) < HEADDIM


def pair_columns(array, pair, low):
    rows = array.shape[0]
    first = jnp.broadcast_to(array[:, 2 * pair : 2 * pair + 1], (rows, LANES))
    second = jnp.broadcast_to(array[:, 2 * pair + 1 : 2 * pair + 2], (rows, LANES))
    return jnp.where(low, first, second)


def conv_parts(current, before, taps):
    rows = current.shape[0]
    padded = jnp.concatenate([before, current], axis=0)
    seen = [padded[8 - CONV + 1 + k : 8 - CONV + 1 + k + rows] for k in range(CONV - 1)] + [current]
    total = taps[CONV : CONV + 1]
    for k in range(CONV):
        total = total + taps[k : k + 1] * seen[k]
    return total, seen


def step_terms(raw, head, seg_len):
    shifted = raw + head[1:2]
    step = jnp.maximum(shifted, 0.0) + jnp.log1p(jnp.exp(-jnp.abs(shifted)))
    log_decay = step * head[0:1]
    at_or_before = lax.broadcasted_iota(jnp.int32, (seg_len, seg_len), 0) >= lax.broadcasted_iota(
        jnp.int32, (seg_len, seg_len), 1
    )
    sums = lax.dot_general(
        jnp.where(at_or_before, 1.0, 0.0), log_decay, (((1,), (0,)), ((), ())),
        precision=lax.Precision.HIGHEST, preferred_element_type=f32,
    )
    return shifted, step, log_decay, sums * LOG2E


def forward_kernel(
    proj_ref, taps_ref, head_ref, skip_ref, rim_ref, init_ref,
    values_ref, prior_ref, final_ref, last_ref, state_ref, tail_ref,
):
    seg_len = proj_ref.shape[0]
    half = seg_len // 2

    @pl.when(pl.program_id(0) == 0)
    def _():
        state_ref[...] = init_ref[...]
        tail_ref[...] = rim_ref[...]

    def activated(begin):
        at = pl.ds(begin, LANES)
        total, _ = conv_parts(proj_ref[:, at], tail_ref[:, at], taps_ref[:, at])
        return total * jax.nn.sigmoid(total)

    b_low = activated(HALF).astype(bf16)
    b_turned = activated(HALF).T.astype(bf16)
    c_low = activated(HALF + STATE).astype(bf16)
    _, step, _, sums = step_terms(proj_ref[:, HALF + 2 * STATE :], head_ref, seg_len)
    sums_turned, step_turned = sums.T, step.T
    scores = dot(c_low, b_low, ((1,), (1,)))
    kept = lax.broadcasted_iota(jnp.int32, (half, half), 0) >= lax.broadcasted_iota(jnp.int32, (half, half), 1)
    first_scores = jnp.where(kept, scores[:half, :half], 0.0)
    later_scores = scores[half:, :half]
    second_scores = jnp.where(kept, scores[half:, half:], 0.0)
    low = low_half((seg_len, LANES))
    last_ref[...] = jnp.broadcast_to(sums[seg_len - 1 :], last_ref.shape)

    for pair in range(HEADS // 4):
        at = columns_of(pair)
        x_values = activated(pair * LANES)
        x_low = x_values.astype(bf16)
        sums_pair = pair_columns(sums, pair, low)
        last_pair = sums_pair[seg_len - 1 :]
        carry = jnp.exp2(last_pair - sums_pair) * pair_columns(step, pair, low)
        scaled_x = (carry * x_low.astype(f32)).astype(bf16)
        prior = state_ref[:, at]
        prior_low = prior.astype(bf16)
        prior_ref[0, :, at] = prior_low
        from_state = jnp.exp2(sums_pair) * dot(c_low, prior_low, ((1,), (0,)))
        state_ref[:, at] = jnp.exp2(last_pair) * prior + dot(b_turned, scaled_x, ((1,), (0,)))
        early, late = 0.0, 0.0
        for side in range(2):
            head = 2 * pair + side
            x_side = jnp.where(low if side == 0 else ~low, x_values, 0.0).astype(bf16)
            at_token = jnp.broadcast_to(sums[:, head : head + 1], (seg_len, half))
            at_source, source_step = sums_turned[head : head + 1], step_turned[head : head + 1]
            first = jnp.exp2(jnp.minimum(at_token[:half] - at_source[:, :half], 0.0)) * first_scores
            first = (first * source_step[:, :half]).astype(bf16)
            later = jnp.exp2(at_token[half:] - at_source[:, :half]) * later_scores
            later = (later * source_step[:, :half]).astype(bf16)
            second = jnp.exp2(jnp.minimum(at_token[half:] - at_source[:, half:], 0.0)) * second_scores
            second = (second * source_step[:, half:]).astype(bf16)
            early = early + dot(first, x_side[:half], ((1,), (0,)))
            late = late + dot(jnp.concatenate([later, second], axis=1), x_side, ((1,), (0,)))
        intra = jnp.concatenate([early, late], axis=0)
        values_ref[:, at] = intra + from_state + skip_ref[:, at] * x_values

    tail_ref[...] = proj_ref[seg_len - 8 :, : HALF + 2 * STATE]
    final_ref[...] = state_ref[...]


def full_block(shape):
    return pl.BlockSpec(shape, lambda *_: (0,) * len(shape))


def scan_forward(proj, taps, head, skip, rim, init, seg_len):
    segs = proj.shape[0] // seg_len
    wide = HALF + 2 * STATE
    return pl.pallas_call(
        forward_kernel,
        grid=(segs,),
        out_shape=(
            jax.ShapeDtypeStruct((proj.shape[0], HALF), f32),
            jax.ShapeDtypeStruct((segs, STATE, HALF), bf16),
            jax.ShapeDtypeStruct((STATE, HALF), f32),
            jax.ShapeDtypeStruct((segs * 8, LANES), f32),
        ),
        in_specs=[
            pl.BlockSpec((seg_len, proj.shape[1]), lambda i: (i, 0)),
            full_block((8, wide)),
            full_block((8, LANES)),
            full_block((1, HALF)),
            full_block((8, wide)),
            full_block((STATE, HALF)),
        ],
        out_specs=(
            pl.BlockSpec((seg_len, HALF), lambda i: (i, 0)),
            pl.BlockSpec((1, STATE, HALF), lambda i: (i, 0, 0)),
            full_block((STATE, HALF)),
            pl.BlockSpec((8, LANES), lambda i: (i, 0)),
        ),
        scratch_shapes=[pltpu.VMEM((STATE, HALF), f32), pltpu.VMEM((8, wide), f32)],
        compiler_params=pltpu.CompilerParams(
            dimension_semantics=("arbitrary",), vmem_limit_bytes=VMEM_LIMIT
        ),
        cost_estimate=pl.CostEstimate(
            flops=4 * proj.shape[0] * seg_len * HALF,
            bytes_accessed=proj.size * 8,
            transcendentals=proj.shape[0] * seg_len * HEADS // 2,
        ),
    )(proj, taps, head, skip, rim, init)


def split_dot(array, other):
    high = array.astype(bf16)
    rest = (array - high.astype(f32)).astype(bf16)
    return dot(high, other, ((1,), (0,))) + dot(rest, other, ((1,), (0,)))


def backward_kernel(
    proj_ref, before_ref, taps_ref, head_ref, skip_ref, rim_ref, heads_ref, end_ref, prior_ref, values_ref, grad_ref,
    grad_x_ref, grad_b_ref, grad_c_ref, grad_raw_ref, taps_grad_ref, skip_grad_ref, head_grad_ref, edge_ref, start_ref,
    later_ref, local_ref, scaled_ref, grad_state_ref, inner_ref, source_ref, carry_ref, decay_ref,
):
    seg_len = proj_ref.shape[0]
    half = seg_len // 2
    turn = pl.program_id(0)

    @pl.when(turn == 0)
    def _():
        later_ref[...] = end_ref[...]
        edge_ref[...] = jnp.zeros_like(edge_ref)
        taps_grad_ref[...] = jnp.zeros_like(taps_grad_ref)
        skip_grad_ref[...] = jnp.zeros_like(skip_grad_ref)
        head_grad_ref[...] = jnp.zeros_like(head_grad_ref)

    first_segment = turn == pl.num_programs(0) - 1

    def conv_at(begin):
        at = pl.ds(begin, LANES)
        before = jnp.where(first_segment, rim_ref[:, at], before_ref[:, at])
        return conv_parts(proj_ref[:, at], before, taps_ref[:, at])

    def activated(begin):
        total, _ = conv_at(begin)
        return total * jax.nn.sigmoid(total)

    b_values = activated(HALF)
    c_values = activated(HALF + STATE)
    b_low, c_low, c_turned = b_values.astype(bf16), c_values.astype(bf16), c_values.T.astype(bf16)
    shifted, step, log_decay, sums = step_terms(proj_ref[:, HALF + 2 * STATE :], head_ref, seg_len)
    sums_turned = sums.T
    scores = dot(b_low, c_low, ((1,), (1,)))
    kept = lax.broadcasted_iota(jnp.int32, (half, half), 0) <= lax.broadcasted_iota(jnp.int32, (half, half), 1)
    first_scores = jnp.where(kept, scores[:half, :half], 0.0)
    later_scores = scores[:half, half:]
    second_scores = jnp.where(kept, scores[half:, half:], 0.0)
    low = low_half((seg_len, LANES))
    first_grad, later_grad, second_grad = 0.0, 0.0, 0.0

    for pair in range(HEADS // 4):
        at = columns_of(pair)
        total, seen = conv_at(pair * LANES)
        sigmoid = jax.nn.sigmoid(total)
        x_values = total * sigmoid
        x_low = x_values.astype(bf16)
        x_wide = x_low.astype(f32)
        sums_pair = pair_columns(sums, pair, low)
        step_pair = pair_columns(step, pair, low)
        last_pair = sums_pair[seg_len - 1 :]
        gap = jnp.exp2(last_pair - sums_pair)
        scaled_ref[:, at] = (gap * step_pair * x_wide).astype(bf16)
        grad_values = grad_ref[:, at]
        grad_state_ref[:, at] = (grad_values * jnp.exp2(sums_pair)).astype(bf16)
        later = later_ref[:, at]
        later_low = later.astype(bf16)
        local_ref[:, at] = later_low
        prior = prior_ref[0, :, at]
        decay_ref[:, at] = jnp.broadcast_to(
            jnp.sum(later * prior.astype(f32), axis=0, keepdims=True), (8, LANES)
        )
        grad_prior = dot(c_turned, grad_state_ref[:, at], ((1,), (0,)))
        later_ref[:, at] = jnp.exp2(last_pair) * later + grad_prior
        grad_scaled = dot(b_low, later_low, ((1,), (0,)))
        stepped = (step_pair * x_wide).astype(bf16)
        early, late = 0.0, 0.0
        for side in range(2):
            head = 2 * pair + side
            grad_low = jnp.where(low if side == 0 else ~low, grad_values, 0.0).astype(bf16)
            at_source = jnp.broadcast_to(sums[:, head : head + 1], (seg_len, half))
            at_token = sums_turned[head : head + 1]
            grad_weights = dot(stepped, grad_low, ((1,), (1,)))
            first = jnp.exp2(jnp.minimum(at_token[:, :half] - at_source[:half], 0.0))
            after = jnp.exp2(at_token[:, half:] - at_source[:half])
            second = jnp.exp2(jnp.minimum(at_token[:, half:] - at_source[half:], 0.0))
            first_grad = first_grad + first * grad_weights[:half, :half]
            later_grad = later_grad + after * grad_weights[:half, half:]
            second_grad = second_grad + second * grad_weights[half:, half:]
            upper = jnp.concatenate([first * first_scores, after * later_scores], axis=1).astype(bf16)
            early = early + dot(upper, grad_low, ((1,), (0,)))
            late = late + dot((second * second_scores).astype(bf16), grad_low[half:], ((1,), (0,)))
        inner = jnp.concatenate([early, late], axis=0)
        skip = skip_ref[:, at]
        skip_grad_ref[:, at] += jnp.sum(grad_values * x_values, axis=0, keepdims=True)
        inner_ref[:, at] = grad_values * (values_ref[:, at] - skip * x_values)
        source_ref[:, at] = x_wide * inner
        carry_ref[:, at] = x_wide * grad_scaled
        grad_x = skip * grad_values + step_pair * (inner + gap * grad_scaled)
        grad_total = grad_x * (sigmoid * (1.0 + total * (1.0 - sigmoid)))
        for k in range(CONV):
            taps_grad_ref[k : k + 1, at] += jnp.sum(grad_total * seen[k], axis=0, keepdims=True)
        taps_grad_ref[CONV : CONV + 1, at] += jnp.sum(grad_total, axis=0, keepdims=True)
        extended = jnp.concatenate([grad_total, edge_ref[:, at]], axis=0)
        edge_ref[:, at] = grad_total[:8]
        taps = taps_ref[:, at]
        grad_conv = taps[CONV - 1 : CONV] * grad_total
        for k in range(CONV - 1):
            grad_conv = grad_conv + taps[k : k + 1] * extended[CONV - 1 - k : CONV - 1 - k + seg_len]
        grad_x_ref[:, at] = grad_conv.astype(bf16)

    heads = heads_ref[...]
    tail = jnp.exp2(sums[seg_len - 1 :] - sums)
    source_grad = split_dot(source_ref[...], heads)
    step_grad = source_grad + tail * split_dot(carry_ref[...], heads)
    used = step * step_grad
    sum_grad = split_dot(inner_ref[...], heads) - used
    at_last = jnp.sum(used - step * source_grad, axis=0, keepdims=True)
    at_last = at_last + split_dot(decay_ref[...], heads)[:1] * jnp.exp2(sums[seg_len - 1 :])
    is_last = lax.broadcasted_iota(jnp.int32, (seg_len, LANES), 0) == seg_len - 1
    sum_grad = sum_grad + jnp.where(is_last, at_last, 0.0)
    at_or_after = lax.broadcasted_iota(jnp.int32, (seg_len, seg_len), 0) <= lax.broadcasted_iota(
        jnp.int32, (seg_len, seg_len), 1
    )
    log_grad = lax.dot_general(
        jnp.where(at_or_after, 1.0, 0.0), sum_grad, (((1,), (0,)), ((), ())),
        precision=lax.Precision.HIGHEST, preferred_element_type=f32,
    )
    grad_raw = (step_grad + head_ref[0:1] * log_grad) * jax.nn.sigmoid(shifted)
    grad_raw_ref[...] = grad_raw
    head_grad_ref[0:1] += jnp.sum(log_grad * log_decay, axis=0, keepdims=True)
    head_grad_ref[1:2] += jnp.sum(grad_raw, axis=0, keepdims=True)

    first_low = jnp.where(kept, first_grad, 0.0)
    second_low = jnp.where(kept, second_grad, 0.0)
    grad_scores = jnp.concatenate(
        [
            jnp.concatenate([first_low, later_grad], axis=1),
            jnp.concatenate([jnp.zeros_like(first_low), second_low], axis=1),
        ],
        axis=0,
    )
    start_ref[...] = later_ref[...]
    grad_b_ref[...] = dot(scaled_ref[...], local_ref[...], ((1,), (1,))) + dot(
        grad_scores.astype(bf16), c_low, ((1,), (0,))
    )
    grad_c_ref[...] = dot(grad_state_ref[...], prior_ref[0], ((1,), (1,))) + dot(
        grad_scores.T.astype(bf16), b_low, ((1,), (0,))
    )


def scan_backward(proj, taps, head, skip, rim, end, prior, values, grad_values, seg_len):
    length = proj.shape[0]
    segs = length // seg_len
    wide = HALF + 2 * STATE
    channel = lax.broadcasted_iota(jnp.int32, (HALF, LANES), 0) // HEADDIM
    heads = (channel == lax.broadcasted_iota(jnp.int32, (HALF, LANES), 1)).astype(bf16)
    back = lambda width: pl.BlockSpec((seg_len, width), lambda i: (segs - 1 - i, 0))
    ahead = lambda i: (jnp.maximum((segs - 1 - i) * (seg_len // 8) - 1, 0), 0)
    return pl.pallas_call(
        backward_kernel,
        grid=(segs,),
        out_shape=(
            jax.ShapeDtypeStruct((length, HALF), bf16),
            jax.ShapeDtypeStruct((length, STATE), f32),
            jax.ShapeDtypeStruct((length, STATE), f32),
            jax.ShapeDtypeStruct((length, LANES), f32),
            jax.ShapeDtypeStruct((8, HALF), f32),
            jax.ShapeDtypeStruct((1, HALF), f32),
            jax.ShapeDtypeStruct((8, LANES), f32),
            jax.ShapeDtypeStruct((8, HALF), f32),
            jax.ShapeDtypeStruct((STATE, HALF), f32),
        ),
        in_specs=[
            back(proj.shape[1]),
            pl.BlockSpec((8, proj.shape[1]), ahead),
            full_block((8, wide)),
            full_block((8, LANES)),
            full_block((1, HALF)),
            full_block((8, wide)),
            full_block((HALF, LANES)),
            full_block((STATE, HALF)),
            pl.BlockSpec((1, STATE, HALF), lambda i: (segs - 1 - i, 0, 0)),
            back(HALF),
            back(HALF),
        ],
        out_specs=(
            back(HALF),
            back(STATE),
            back(STATE),
            back(LANES),
            full_block((8, HALF)),
            full_block((1, HALF)),
            full_block((8, LANES)),
            full_block((8, HALF)),
            full_block((STATE, HALF)),
        ),
        scratch_shapes=[
            pltpu.VMEM((STATE, HALF), f32),
            pltpu.VMEM((STATE, HALF), bf16),
            pltpu.VMEM((seg_len, HALF), bf16),
            pltpu.VMEM((seg_len, HALF), bf16),
            pltpu.VMEM((seg_len, HALF), f32),
            pltpu.VMEM((seg_len, HALF), f32),
            pltpu.VMEM((seg_len, HALF), f32),
            pltpu.VMEM((8, HALF), f32),
        ],
        compiler_params=pltpu.CompilerParams(
            dimension_semantics=("arbitrary",), vmem_limit_bytes=VMEM_LIMIT
        ),
        cost_estimate=pl.CostEstimate(
            flops=10 * length * seg_len * HALF,
            bytes_accessed=proj.size * 16,
            transcendentals=length * seg_len * HEADS // 2,
        ),
    )(proj, proj, taps, head, skip, rim, heads, end, prior, values, grad_values)


def shared_kernel(core_ref, proj_ref, rim_ref, taps_ref, b_ref, c_ref, other_ref, grad_ref, taps_grad_ref, edge_ref):
    total, seen = conv_parts(proj_ref[...], rim_ref[...], taps_ref[...])
    sigmoid = jax.nn.sigmoid(total)
    grad_total = jnp.where(core_ref[0] == 0, b_ref[...], c_ref[...]) + other_ref[...]
    grad_total = grad_total * (sigmoid * (1.0 + total * (1.0 - sigmoid)))
    sums = [jnp.sum(grad_total * part, axis=0, keepdims=True) for part in seen]
    sums = sums + [jnp.sum(grad_total, axis=0, keepdims=True), jnp.zeros((8 - CONV - 1, LANES), f32)]
    taps_grad_ref[...] = jnp.concatenate(sums, axis=0)
    edge_ref[...] = grad_total[:8]
    taps = taps_ref[...]
    extended = jnp.concatenate([grad_total, jnp.zeros((8, LANES), f32)], axis=0)
    grad_conv = taps[CONV - 1 : CONV] * grad_total
    for k in range(CONV - 1):
        grad_conv = grad_conv + taps[k : k + 1] * extended[CONV - 1 - k : CONV - 1 - k + grad_total.shape[0]]
    grad_ref[...] = grad_conv.astype(bf16)


def shared_backward(core, proj, rim, taps, grad_b, grad_c, other):
    length = proj.shape[0]
    picked = lambda rows: pl.BlockSpec((rows, LANES), lambda i, core: (0, HALF // LANES + core[0]))
    whole = lambda rows: pl.BlockSpec((rows, LANES), lambda i, core: (0, 0))
    return pl.pallas_call(
        shared_kernel,
        grid_spec=pltpu.PrefetchScalarGridSpec(
            num_scalar_prefetch=1,
            grid=(1,),
            in_specs=[picked(length), picked(8), picked(8), whole(length), whole(length), whole(length)],
            out_specs=(whole(length), whole(8), whole(8)),
        ),
        out_shape=(
            jax.ShapeDtypeStruct((length, LANES), bf16),
            jax.ShapeDtypeStruct((8, LANES), f32),
            jax.ShapeDtypeStruct((8, LANES), f32),
        ),
        compiler_params=pltpu.CompilerParams(vmem_limit_bytes=VMEM_LIMIT),
        cost_estimate=pl.CostEstimate(flops=40 * length * LANES, bytes_accessed=24 * length * LANES, transcendentals=length * LANES),
    )(core.reshape(1).astype(jnp.int32), proj, rim, taps, grad_b, grad_c, other)


def per_device(hidden_in, cotangent, in_proj, out_proj, conv_params, pre_gain, gated_gain, head_params):
    chips, line = lax.axis_size("chip"), lax.axis_size("seg")
    core, place = lax.axis_index("core"), lax.axis_index("seg")
    rows, model_width = in_proj.shape[0], hidden_in.shape[2]
    heads = HEADS // 2

    hidden_half, hidden = whole_sequence(hidden_in, core, place)
    conv_width, gain_width = conv_params.shape[1], gated_gain.shape[0]
    used = HALF + 2 * STATE + heads
    spare = -used % LANES
    small = jnp.zeros((rows, spare), bf16)
    small = small.at[: CONV + 1, :conv_width].set(conv_params)
    small = small.at[CONV + 1, :rows].set(pre_gain)
    small = small.at[CONV + 2, :gain_width].set(gated_gain)

    def conv_side(which):
        return jnp.concatenate(
            [
                own_columns(in_proj[:, INNER : 2 * INNER], which),
                in_proj[:, 2 * INNER : INNER + XBC],
                own_columns(in_proj[:, INNER + XBC :], which),
                small,
            ],
            axis=1,
        )

    def gate_side(which):
        return own_columns(in_proj[:, :INNER], which)

    conv_block = in_core_order(conv_side(core), to_partner(conv_side(1 - core)), core, 0)
    gate_block = in_core_order(gate_side(core), to_partner(gate_side(1 - core)), core, 0)
    conv_all = whole_matrix(conv_block, True).reshape(model_width, -1)
    gate_matrix = whole_matrix(gate_block, True).reshape(model_width, -1)
    out_matrix = whole_matrix(out_proj, False).reshape(HALF, model_width)
    cot_half, cot = whole_sequence(cotangent, core, place)

    small_all = conv_all.reshape(chips, 2, line, rows, -1)[..., used:].astype(f32)
    taps_full = small_all[..., : CONV + 1, :conv_width].transpose(3, 0, 1, 2, 4).reshape(CONV + 1, XBC)
    taps = jnp.concatenate([own_columns(taps_full[:, :INNER], core), taps_full[:, INNER:]], axis=1)
    gain_pre = small_all[..., CONV + 1, :rows].reshape(model_width)
    gain_gate = lax.dynamic_index_in_dim(
        small_all[..., CONV + 2, :gain_width], core, axis=1, keepdims=False
    ).reshape(HALF)
    params = own_columns(head_params, core)

    seg_len = hidden.shape[1] * hidden.shape[2]
    tokens = SEGS * seg_len
    upstream = cot.reshape(tokens, model_width)
    normed = pre_norm(hidden.reshape(tokens, model_width).astype(f32), gain_pre).astype(bf16)
    projected = dot(normed, conv_all, ((1,), (0,)))
    gate_input = dot(normed, gate_matrix, ((1,), (0,)))
    grad_mixed = dot(upstream, out_matrix, ((1,), (1,)))

    taps = jnp.pad(taps, ((0, 8 - CONV - 1), (0, 0)))
    head = jnp.pad(jnp.stack([-jnp.exp(params[0]), params[1]]), ((0, 6), (0, LANES - heads)))
    skip = jnp.repeat(params[2], HEADDIM).reshape(1, HALF)
    wide = HALF + 2 * STATE
    rim = borrowed(projected[tokens - 8 :, :wide], 1)
    nothing = jnp.zeros((STATE, HALF), f32)
    values, prior, final, last = scan_forward(projected, taps, head, skip, rim, nothing, seg_len)
    if line > SEGS:
        last = jnp.sum(last.reshape(SEGS, 8, LANES)[:, 0, :heads], axis=0)
        decay = jnp.repeat(jnp.exp2(last), HEADDIM)
        begin = entering(decay, final, 1)
        values, prior, _, _ = scan_forward(projected, taps, head, skip, rim, begin, seg_len)

    silu_gate = jax.nn.silu(gate_input)
    gated = values * silu_gate
    gain_grad = grad_mixed * gain_gate
    sums = jnp.stack([jnp.sum(gated * gated, axis=1), jnp.sum(gain_grad * gated, axis=1)])
    sums = (sums + to_partner(sums)) / INNER
    scale = lax.rsqrt(sums[0] + epsilon)[:, None]
    unit = gated * scale
    mixed = (unit * gain_gate).astype(bf16)
    gate_gain_grad = jnp.sum(grad_mixed * unit, axis=0)
    grad_gated = scale * (gain_grad - unit * (scale * sums[1][:, None]))
    grad_values = grad_gated * silu_gate
    sigmoid = jax.nn.sigmoid(gate_input)
    grad_gate = (grad_gated * values * (sigmoid * (1.0 + gate_input * (1.0 - sigmoid)))).astype(bf16)

    out_grad = dot(mixed, upstream, ((0,), (0,)))
    out_share = owner_share(out_grad.reshape(chip_dims() + (-1, model_width)))

    def paired_share(grad):
        a, b, z = chip_dims()
        parted = grad.reshape(a, b, 2, z, rows, -1).transpose(0, 1, 3, 2, 4, 5)
        return owner_share(parted)

    gate_share = paired_share(dot(normed, grad_gate, ((0,), (0,)))).astype(bf16)

    def halves(partial):
        parted = partial.reshape(SEGS, 2, seg_len // 2, model_width)
        mine = lax.dynamic_index_in_dim(parted, core, axis=1, keepdims=False)
        theirs = lax.dynamic_index_in_dim(parted, 1 - core, axis=1, keepdims=False)
        return mine + to_partner(theirs.astype(bf16)).astype(f32)

    branch = halves(dot(mixed, out_matrix, ((1,), (0,))))
    hidden_out = back_to_owner(
        (hidden_half.astype(f32) + branch).astype(bf16), core, place
    )

    back = scan_backward(projected, taps, head, skip, rim, nothing, prior, values, grad_values, seg_len)
    if line > SEGS:
        end = entering(decay, back[-1], -1)
        back = scan_backward(projected, taps, head, skip, rim, end, prior, values, grad_values, seg_len)
    grad_x, grad_b, grad_c, grad_raw, x_taps_grad, skip_grad, head_sums, x_edge, _ = back
    head_grad = jnp.concatenate([head_sums[:2, :heads], skip_grad.reshape(1, heads, HEADDIM).sum(axis=2)])

    other = to_partner(jnp.where(core == 0, grad_c, grad_b))
    grad_state, state_taps_grad, state_edge = shared_backward(core, projected, rim, taps, grad_b, grad_c, other)
    if line > SEGS:
        edge = borrowed(jnp.concatenate([x_edge, state_edge], axis=1), -1)
        own_taps = jnp.concatenate(
            [taps[:, :HALF], lax.dynamic_slice_in_dim(taps, HALF + core * STATE, STATE, axis=1)], axis=1
        )
        spill = jnp.stack(
            [
                sum(own_taps[k] * edge[CONV - 1 - k - early] for k in range(CONV - early))
                for early in range(CONV - 1, 0, -1)
            ]
        )
        add = lambda array, part: array.at[tokens - CONV + 1 :].set(
            (array[tokens - CONV + 1 :].astype(f32) + part).astype(bf16)
        )
        grad_x, grad_state = add(grad_x, spill[:, :HALF]), add(grad_state, spill[:, HALF:])
    grad_proj = jnp.concatenate([grad_x, grad_state, grad_raw.astype(bf16)], axis=1)
    state_taps_grad = state_taps_grad[: CONV + 1]
    none = jnp.zeros_like(state_taps_grad)
    taps_grad = jnp.concatenate(
        [
            x_taps_grad[: CONV + 1],
            jnp.where(core == 0, state_taps_grad, none),
            jnp.where(core == 0, none, state_taps_grad),
        ],
        axis=1,
    )
    conv_share = paired_share(dot(normed, grad_proj, ((0,), (0,)))).astype(bf16)

    state_weights = lax.dynamic_slice_in_dim(conv_all, HALF + core * STATE, STATE, axis=1)
    conv_matrix = jnp.concatenate(
        [conv_all[:, :HALF], state_weights, conv_all[:, HALF + 2 * STATE :]], axis=1
    )
    grad_normed = halves(
        dot(grad_gate, gate_matrix, ((1,), (1,))) + dot(grad_proj, conv_matrix, ((1,), (1,)))
    )
    _, pre_pull = jax.vjp(pre_norm, hidden_half.astype(f32), gain_pre)
    grad_hidden, pre_gain_grad = pre_pull(grad_normed)
    grad_in = back_to_owner(
        (cot_half.astype(f32) + grad_hidden).astype(bf16), core, place
    )

    def spread_own(array):
        width = array.shape[-1] // chips
        parted = array.reshape(array.shape[:-1] + (chips, 1, width))
        none = jnp.zeros_like(parted)
        both = jnp.where(
            core == 0,
            jnp.concatenate([parted, none], axis=-2),
            jnp.concatenate([none, parted], axis=-2),
        )
        return both.reshape(array.shape[:-1] + (2 * array.shape[-1],))

    taps_all = jnp.concatenate([spread_own(taps_grad[:, :HALF]), taps_grad[:, HALF:]], axis=1)
    taps_all = taps_all.reshape(CONV + 1, chips, 2, line, conv_width).transpose(1, 3, 2, 0, 4)
    gate_all = spread_own(gate_gain_grad).reshape(chips, 2, line, gain_width).transpose(0, 2, 1, 3)
    head_all = jnp.broadcast_to(spread_own(head_grad).reshape(-1), (chips, line, 2, 3 * HEADS))
    small_grads = jnp.concatenate(
        [
            taps_all.reshape(chips, line, 2, -1),
            pre_gain_grad.reshape(chips, 2, line, rows).transpose(0, 2, 1, 3),
            gate_all,
            head_all,
        ],
        axis=3,
    )
    count = small_grads.shape[3]
    small_share = summed(small_grads.reshape(chip_dims() + (2, count)), (1, 0, 2), f32)

    def mine_and_partner(share):
        keep = lax.dynamic_index_in_dim(share, core, axis=0, keepdims=False)
        give = lax.dynamic_index_in_dim(share, 1 - core, axis=0, keepdims=False)
        return keep, to_partner(give)

    keep, got = mine_and_partner(small_share)
    small_total = keep + got
    taps_end = (CONV + 1) * conv_width
    taps_share = small_total[:taps_end].reshape(CONV + 1, conv_width)
    pre_share = small_total[taps_end : taps_end + rows]
    gain_share = small_total[taps_end + rows : taps_end + rows + gain_width]
    head_total = small_total[taps_end + rows + gain_width :].reshape(3, HEADS)

    def interleave(mine, theirs):
        width = mine.shape[1] // chips
        both = in_core_order(mine.reshape(rows, chips, width), theirs.reshape(rows, chips, width), core, 2)
        return both.reshape(rows, -1)

    keep_gate, got_gate = mine_and_partner(gate_share)
    keep, got = mine_and_partner(conv_share)
    state_end = HALF + STATE
    in_share = jnp.concatenate(
        [
            interleave(keep_gate, got_gate),
            interleave(keep[:, :HALF], got[:, :HALF]),
            in_core_order(keep[:, HALF:state_end], got[:, HALF:state_end], core, 1).reshape(rows, -1),
            interleave(keep[:, state_end : state_end + heads], got[:, state_end : state_end + heads]),
        ],
        axis=1,
    ).astype(f32)
    return (hidden_out, grad_in, in_share, out_share, taps_share, pre_share, gain_share, head_total)


def solution(mesh):
    devices = mesh.devices
    cores = Mesh(devices.reshape(devices.shape[0] // 2, 2, devices.shape[1]), ("chip", "core", "seg"))
    dp, both = ("chip", "core"), ("chip", "core", "seg")
    tokens = P(dp, "seg", None)
    return jax.shard_map(
        per_device,
        mesh=cores,
        in_specs=(tokens, tokens, P(both, None), P(both, None), P(None, both), P(both), P(both), P()),
        out_specs=(tokens, tokens, P(both, None), P(both, None), P(None, both), P(both), P(both), P()),
        check_vma=False,
    )
```

```python
import jax
import jax.numpy as jnp
from jax import lax
from jax.experimental import pallas as pl
from jax.experimental.pallas import tpu as pltpu
from jax.sharding import Mesh
from jax.sharding import PartitionSpec as P

HEADS = 48
HEADDIM = 64
STATE = 128
CONV = 4
INNER = 3072
XBC = 3328
HALF = INNER // 2
LANES = 128
SEGS = 4
VMEM_LIMIT = 48 * 1024 * 1024
LOG2E = 1.4426950408889634

epsilon = 1e-05
f32 = jnp.float32
bf16 = jnp.bfloat16


def own_columns(array, core):
    chips = lax.axis_size("chip")
    width = array.shape[-1] // (2 * chips)
    parted = array.reshape(array.shape[:-1] + (chips, 2, width))
    picked = lax.dynamic_index_in_dim(parted, core, axis=parted.ndim - 2, keepdims=False)
    return picked.reshape(array.shape[:-1] + (chips * width,))


def to_partner(array):
    return lax.ppermute(array, "core", [(0, 1), (1, 0)])


def in_core_order(mine, theirs, core, axis):
    first = jnp.where(core == 0, mine, theirs)
    second = jnp.where(core == 0, theirs, mine)
    return jnp.stack([first, second], axis=axis)


def chip_dims():
    return (lax.axis_size("chip") // 2, 2, lax.axis_size("seg"))


def chip_place():
    chip = lax.axis_index("chip")
    return (chip // 2, chip % 2, lax.axis_index("seg"))


def moved(array, dim, by):
    sizes = chip_dims()
    index = lambda at: (at[0] * sizes[1] + at[1]) * sizes[2] + at[2]
    pairs = []
    for a in range(sizes[0]):
        for b in range(sizes[1]):
            for z in range(sizes[2]):
                to = [a, b, z]
                to[dim] = (to[dim] + by) % sizes[dim]
                pairs.append((index((a, b, z)), index(to)))
    return lax.ppermute(array, ("chip", "seg"), pairs)


def after(value, *earlier):
    return lax.optimization_barrier((value, earlier))[0]


ORDERS = ((2, 0, 1), (2, 1, 0))


def column_parts(width):
    cut = -(-(width // 2) // LANES) * LANES
    return ((0, cut), (cut, width))


def gather_step(data, dim):
    return [data] + [moved(data, dim, by) for by in range(1, chip_dims()[dim])]


def gather_first(block):
    return [
        gather_step(block[..., begin:end], order[0])
        for order, (begin, end) in zip(ORDERS, column_parts(block.shape[-1]))
    ]


def gather_next(parts, step):
    return [gather_step(jnp.stack(part), order[step]) for order, part in zip(ORDERS, parts)]


def placed_kernel(plan, place_ref, *refs):
    sources, out_ref, sems = refs[:-2], refs[-2], refs[-1]
    copies = []
    for source, lead, at, columns, paired in plan:
        spot = [lax.rem(place_ref[dim] + (size - back), size) for dim, (back, size) in enumerate(at)]
        target = out_ref.at[spot[0], spot[1]]
        target = target.at[:, spot[2]] if paired else target.at[spot[2]]
        target = target.at[..., pl.ds(*columns)]
        copies.append(pltpu.make_async_copy(sources[source].at[lead], target, sems.at[len(copies)]))
    for copy in copies:
        copy.start()
    for copy in copies:
        copy.wait()


def whole_matrix(parts, block, paired):
    sizes = chip_dims()
    plan, sources = [], []
    for order, (begin, end), part in zip(ORDERS, column_parts(block.shape[-1]), parts):
        for back_last, piece in enumerate(part):
            for back_mid in range(sizes[order[1]]):
                for back_first in range(sizes[order[0]]):
                    at = [None] * 3
                    at[order[2]] = (back_last, sizes[order[2]])
                    at[order[1]] = (back_mid, sizes[order[1]])
                    at[order[0]] = (back_first, sizes[order[0]])
                    plan.append((len(sources), (back_mid, back_first), at, (begin, end - begin), paired))
            sources.append(piece)
    if paired:
        shape = sizes[:2] + (2, sizes[2]) + block.shape[1:]
    else:
        shape = sizes + block.shape
    anywhere = pl.BlockSpec(memory_space=pl.ANY)
    return pl.pallas_call(
        lambda *refs: placed_kernel(plan, *refs),
        out_shape=jax.ShapeDtypeStruct(shape, block.dtype),
        in_specs=[pl.BlockSpec(memory_space=pltpu.SMEM)] + [anywhere] * len(sources),
        out_specs=pl.BlockSpec(memory_space=pltpu.VMEM),
        scratch_shapes=[pltpu.SemaphoreType.DMA((len(plan),))],
        compiler_params=pltpu.CompilerParams(vmem_limit_bytes=VMEM_LIMIT),
        cost_estimate=pl.CostEstimate(flops=0, bytes_accessed=4 * block.size * sizes[0] * sizes[1] * sizes[2], transcendentals=0),
    )(jnp.stack(chip_place()).astype(jnp.int32), *sources)


def reduce_send(data, axis, dim, wire):
    place, size = chip_place()[dim], chip_dims()[dim]
    pick = lambda at: lax.dynamic_index_in_dim(data, at, axis=axis, keepdims=False)
    received = [moved(pick((place + by) % size).astype(wire), dim, by) for by in range(1, size)]
    return pick(place).astype(f32), received


def reduce_add(kept, received):
    for part in received:
        kept = kept + part.astype(f32)
    return kept


def reduce_first(partial, wire=bf16):
    (begin, cut), (_, end) = column_parts(partial.shape[-1])
    return [
        reduce_send(partial[..., begin:cut], 1, 1, wire),
        reduce_send(partial[..., cut:end], 0, 0, wire),
    ]


def reduce_second(first, wire=bf16):
    return [
        reduce_send(reduce_add(*first[0]), 0, 0, wire),
        reduce_send(reduce_add(*first[1]), 0, 1, wire),
    ]


def reduce_third(second, wire=bf16):
    return [reduce_send(reduce_add(*part), 0, 2, wire) for part in second]


def reduce_end(third):
    return jnp.concatenate([reduce_add(*part) for part in third], axis=-1)


def line_perm(turn, back):
    line = lax.axis_size("seg")
    parts = line // SEGS
    pairs = []
    for core in range(2):
        for place in range(line):
            piece = (place % SEGS) ^ turn
            half, index = divmod(piece, 2)
            source = core * line + place
            target = half * line + (2 * core + index) * parts + place // SEGS
            pairs.append((target, source) if back else (source, target))
    return pairs


def whole_sequence(array, core, place):
    parts = lax.axis_size("seg") // SEGS
    half = array.shape[1] // 2
    pieces = array.reshape(2, 2, half, -1).transpose(1, 0, 2, 3).reshape(4, half, -1)
    mine = place % SEGS
    target = 2 * core + (place // parts) % 2
    got = []
    for turn in range(4):
        piece = lax.dynamic_index_in_dim(pieces, mine ^ turn, axis=0, keepdims=False)
        got.append(lax.ppermute(piece, ("core", "seg"), line_perm(turn, False)))
    got = jnp.stack(got)
    return jnp.stack([lax.dynamic_index_in_dim(got, target ^ k, axis=0, keepdims=False) for k in range(4)])


def back_to_owner(ordered, core, place):
    parts = lax.axis_size("seg") // SEGS
    half = ordered.shape[1]
    mine = place % SEGS
    target = 2 * core + (place // parts) % 2
    got = []
    for turn in range(4):
        piece = lax.dynamic_index_in_dim(ordered, target ^ turn, axis=0, keepdims=False)
        got.append(lax.ppermute(piece, ("core", "seg"), line_perm(turn, True)))
    got = jnp.stack(got)
    pieces = jnp.stack([lax.dynamic_index_in_dim(got, mine ^ k, axis=0, keepdims=False) for k in range(4)])
    return pieces.reshape(2, 2, half, -1).transpose(1, 0, 2, 3).reshape(2, 2 * half, -1)


def part_pairs(step):
    line = lax.axis_size("seg")
    parts = line // SEGS
    return [(i, i + step) for i in range(line) if 0 <= i + step < line and i // parts == (i + step) // parts]


def entering(decay, state, step):
    parts = lax.axis_size("seg") // SEGS
    total = jnp.zeros_like(state)
    for _ in range(parts - 1):
        total = lax.ppermute(decay * total + state, "seg", part_pairs(step))
    return total


def borrowed(array, step):
    parts = lax.axis_size("seg") // SEGS
    if parts == 1:
        return jnp.zeros_like(array)
    return lax.ppermute(array, "seg", part_pairs(step))


def pre_norm(hidden, norm_gain):
    row_scale = lax.rsqrt(jnp.mean(hidden * hidden, axis=-1, keepdims=True) + epsilon)
    return hidden * row_scale * norm_gain


def conv_apply(padded, conv_taps):
    length = padded.shape[0] - CONV + 1
    summed = conv_taps[CONV]
    for offset in range(CONV):
        summed = summed + conv_taps[offset] * padded[offset : offset + length, :]
    return jax.nn.silu(summed)


def head_terms(step_raw, params):
    step_size = jax.nn.softplus(step_raw + params[1])
    decay_sum = jnp.cumsum(step_size * -jnp.exp(params[0]), axis=1)
    return (step_size, decay_sum)


def decay_terms(decay_sum, step_size):
    last_sum = decay_sum[:, -1:, :]
    carry_scale = jnp.exp(last_sum - decay_sum) * step_size
    return (carry_scale, jnp.exp(decay_sum[:, -1, :]), jnp.exp(decay_sum))


def dot(a, b, contract):
    return lax.dot_general(a, b, (contract, ((), ())), preferred_element_type=f32)


def columns_of(pair):
    return pl.ds(pair * LANES, LANES)


def low_half(shape):
    return lax.broadcasted_iota(jnp.int32, shape, len(shape) - 1) < HEADDIM


def pair_columns(array, pair, low):
    rows = array.shape[0]
    first = jnp.broadcast_to(array[:, 2 * pair : 2 * pair + 1], (rows, LANES))
    second = jnp.broadcast_to(array[:, 2 * pair + 1 : 2 * pair + 2], (rows, LANES))
    return jnp.where(low, first, second)


def conv_parts(current, before, taps):
    rows = current.shape[0]
    padded = jnp.concatenate([before, current], axis=0)
    seen = [padded[8 - CONV + 1 + k : 8 - CONV + 1 + k + rows] for k in range(CONV - 1)] + [current]
    total = taps[CONV : CONV + 1]
    for k in range(CONV):
        total = total + taps[k : k + 1] * seen[k]
    return total, seen


def step_terms(raw, head, seg_len):
    shifted = raw + head[1:2]
    step = jnp.maximum(shifted, 0.0) + jnp.log1p(jnp.exp(-jnp.abs(shifted)))
    log_decay = step * head[0:1]
    at_or_before = lax.broadcasted_iota(jnp.int32, (seg_len, seg_len), 0) >= lax.broadcasted_iota(
        jnp.int32, (seg_len, seg_len), 1
    )
    sums = lax.dot_general(
        jnp.where(at_or_before, 1.0, 0.0), log_decay, (((1,), (0,)), ((), ())),
        precision=lax.Precision.HIGHEST, preferred_element_type=f32,
    )
    return shifted, step, log_decay, sums * LOG2E


def forward_kernel(
    proj_ref, taps_ref, head_ref, skip_ref, rim_ref, init_ref,
    values_ref, prior_ref, final_ref, last_ref, state_ref, tail_ref,
):
    seg_len = proj_ref.shape[0]
    half = seg_len // 2

    @pl.when(pl.program_id(0) == 0)
    def _():
        state_ref[...] = init_ref[...]
        tail_ref[...] = rim_ref[...]

    def activated(begin):
        at = pl.ds(begin, LANES)
        total, _ = conv_parts(proj_ref[:, at], tail_ref[:, at], taps_ref[:, at])
        return total * jax.nn.sigmoid(total)

    b_low = activated(HALF).astype(bf16)
    b_turned = activated(HALF).T.astype(bf16)
    c_low = activated(HALF + STATE).astype(bf16)
    _, step, _, sums = step_terms(proj_ref[:, HALF + 2 * STATE :], head_ref, seg_len)
    sums_turned, step_turned = sums.T, step.T
    scores = dot(c_low, b_low, ((1,), (1,)))
    kept = lax.broadcasted_iota(jnp.int32, (half, half), 0) >= lax.broadcasted_iota(jnp.int32, (half, half), 1)
    first_scores = jnp.where(kept, scores[:half, :half], 0.0)
    later_scores = scores[half:, :half]
    second_scores = jnp.where(kept, scores[half:, half:], 0.0)
    low = low_half((seg_len, LANES))
    last_ref[...] = jnp.broadcast_to(sums[seg_len - 1 :], last_ref.shape)

    for pair in range(HEADS // 4):
        at = columns_of(pair)
        x_values = activated(pair * LANES)
        x_low = x_values.astype(bf16)
        sums_pair = pair_columns(sums, pair, low)
        last_pair = sums_pair[seg_len - 1 :]
        carry = jnp.exp2(last_pair - sums_pair) * pair_columns(step, pair, low)
        scaled_x = (carry * x_low.astype(f32)).astype(bf16)
        prior = state_ref[:, at]
        prior_low = prior.astype(bf16)
        prior_ref[0, :, at] = prior_low
        from_state = jnp.exp2(sums_pair) * dot(c_low, prior_low, ((1,), (0,)))
        state_ref[:, at] = jnp.exp2(last_pair) * prior + dot(b_turned, scaled_x, ((1,), (0,)))
        early, late = 0.0, 0.0
        for side in range(2):
            head = 2 * pair + side
            x_side = jnp.where(low if side == 0 else ~low, x_values, 0.0).astype(bf16)
            at_token = jnp.broadcast_to(sums[:, head : head + 1], (seg_len, half))
            at_source, source_step = sums_turned[head : head + 1], step_turned[head : head + 1]
            first = jnp.exp2(jnp.minimum(at_token[:half] - at_source[:, :half], 0.0)) * first_scores
            first = (first * source_step[:, :half]).astype(bf16)
            later = jnp.exp2(at_token[half:] - at_source[:, :half]) * later_scores
            later = (later * source_step[:, :half]).astype(bf16)
            second = jnp.exp2(jnp.minimum(at_token[half:] - at_source[:, half:], 0.0)) * second_scores
            second = (second * source_step[:, half:]).astype(bf16)
            early = early + dot(first, x_side[:half], ((1,), (0,)))
            late = late + dot(jnp.concatenate([later, second], axis=1), x_side, ((1,), (0,)))
        intra = jnp.concatenate([early, late], axis=0)
        values_ref[:, at] = intra + from_state + skip_ref[:, at] * x_values

    tail_ref[...] = proj_ref[seg_len - 8 :, : HALF + 2 * STATE]
    final_ref[...] = state_ref[...]


def full_block(shape):
    return pl.BlockSpec(shape, lambda *_: (0,) * len(shape))


def scan_forward(proj, taps, head, skip, rim, init, seg_len):
    segs = proj.shape[0] // seg_len
    wide = HALF + 2 * STATE
    return pl.pallas_call(
        forward_kernel,
        grid=(segs,),
        out_shape=(
            jax.ShapeDtypeStruct((proj.shape[0], HALF), f32),
            jax.ShapeDtypeStruct((segs, STATE, HALF), bf16),
            jax.ShapeDtypeStruct((STATE, HALF), f32),
            jax.ShapeDtypeStruct((segs * 8, LANES), f32),
        ),
        in_specs=[
            pl.BlockSpec((seg_len, proj.shape[1]), lambda i: (i, 0)),
            full_block((8, wide)),
            full_block((8, LANES)),
            full_block((1, HALF)),
            full_block((8, wide)),
            full_block((STATE, HALF)),
        ],
        out_specs=(
            pl.BlockSpec((seg_len, HALF), lambda i: (i, 0)),
            pl.BlockSpec((1, STATE, HALF), lambda i: (i, 0, 0)),
            full_block((STATE, HALF)),
            pl.BlockSpec((8, LANES), lambda i: (i, 0)),
        ),
        scratch_shapes=[pltpu.VMEM((STATE, HALF), f32), pltpu.VMEM((8, wide), f32)],
        compiler_params=pltpu.CompilerParams(
            dimension_semantics=("arbitrary",), vmem_limit_bytes=VMEM_LIMIT
        ),
        cost_estimate=pl.CostEstimate(
            flops=4 * proj.shape[0] * seg_len * HALF,
            bytes_accessed=proj.size * 8,
            transcendentals=proj.shape[0] * seg_len * HEADS // 2,
        ),
    )(proj, taps, head, skip, rim, init)


def split_dot(array, other):
    high = array.astype(bf16)
    rest = (array - high.astype(f32)).astype(bf16)
    return dot(high, other, ((1,), (0,))) + dot(rest, other, ((1,), (0,)))


def backward_kernel(
    proj_ref, before_ref, taps_ref, head_ref, skip_ref, rim_ref, heads_ref, end_ref, prior_ref, values_ref, grad_ref,
    grad_x_ref, grad_b_ref, grad_c_ref, grad_raw_ref, taps_grad_ref, skip_grad_ref, head_grad_ref, edge_ref, start_ref,
    later_ref, local_ref, scaled_ref, grad_state_ref, inner_ref, source_ref, carry_ref, decay_ref,
):
    seg_len = proj_ref.shape[0]
    half = seg_len // 2
    turn = pl.program_id(0)

    @pl.when(turn == 0)
    def _():
        later_ref[...] = end_ref[...]
        edge_ref[...] = jnp.zeros_like(edge_ref)
        taps_grad_ref[...] = jnp.zeros_like(taps_grad_ref)
        skip_grad_ref[...] = jnp.zeros_like(skip_grad_ref)
        head_grad_ref[...] = jnp.zeros_like(head_grad_ref)

    first_segment = turn == pl.num_programs(0) - 1

    def conv_at(begin):
        at = pl.ds(begin, LANES)
        before = jnp.where(first_segment, rim_ref[:, at], before_ref[:, at])
        return conv_parts(proj_ref[:, at], before, taps_ref[:, at])

    def activated(begin):
        total, _ = conv_at(begin)
        return total * jax.nn.sigmoid(total)

    b_values = activated(HALF)
    c_values = activated(HALF + STATE)
    b_low, c_low, c_turned = b_values.astype(bf16), c_values.astype(bf16), c_values.T.astype(bf16)
    shifted, step, log_decay, sums = step_terms(proj_ref[:, HALF + 2 * STATE :], head_ref, seg_len)
    sums_turned = sums.T
    scores = dot(b_low, c_low, ((1,), (1,)))
    kept = lax.broadcasted_iota(jnp.int32, (half, half), 0) <= lax.broadcasted_iota(jnp.int32, (half, half), 1)
    first_scores = jnp.where(kept, scores[:half, :half], 0.0)
    later_scores = scores[:half, half:]
    second_scores = jnp.where(kept, scores[half:, half:], 0.0)
    low = low_half((seg_len, LANES))
    first_grad, later_grad, second_grad = 0.0, 0.0, 0.0

    for pair in range(HEADS // 4):
        at = columns_of(pair)
        total, seen = conv_at(pair * LANES)
        sigmoid = jax.nn.sigmoid(total)
        x_values = total * sigmoid
        x_low = x_values.astype(bf16)
        x_wide = x_low.astype(f32)
        sums_pair = pair_columns(sums, pair, low)
        step_pair = pair_columns(step, pair, low)
        last_pair = sums_pair[seg_len - 1 :]
        gap = jnp.exp2(last_pair - sums_pair)
        scaled_ref[:, at] = (gap * step_pair * x_wide).astype(bf16)
        grad_values = grad_ref[:, at]
        grad_state_ref[:, at] = (grad_values * jnp.exp2(sums_pair)).astype(bf16)
        later = later_ref[:, at]
        later_low = later.astype(bf16)
        local_ref[:, at] = later_low
        prior = prior_ref[0, :, at]
        decay_ref[:, at] = jnp.broadcast_to(
            jnp.sum(later * prior.astype(f32), axis=0, keepdims=True), (8, LANES)
        )
        grad_prior = dot(c_turned, grad_state_ref[:, at], ((1,), (0,)))
        later_ref[:, at] = jnp.exp2(last_pair) * later + grad_prior
        grad_scaled = dot(b_low, later_low, ((1,), (0,)))
        stepped = (step_pair * x_wide).astype(bf16)
        early, late = 0.0, 0.0
        for side in range(2):
            head = 2 * pair + side
            grad_low = jnp.where(low if side == 0 else ~low, grad_values, 0.0).astype(bf16)
            at_source = jnp.broadcast_to(sums[:, head : head + 1], (seg_len, half))
            at_token = sums_turned[head : head + 1]
            grad_weights = dot(stepped, grad_low, ((1,), (1,)))
            first = jnp.exp2(jnp.minimum(at_token[:, :half] - at_source[:half], 0.0))
            after = jnp.exp2(at_token[:, half:] - at_source[:half])
            second = jnp.exp2(jnp.minimum(at_token[:, half:] - at_source[half:], 0.0))
            first_grad = first_grad + first * grad_weights[:half, :half]
            later_grad = later_grad + after * grad_weights[:half, half:]
            second_grad = second_grad + second * grad_weights[half:, half:]
            upper = jnp.concatenate([first * first_scores, after * later_scores], axis=1).astype(bf16)
            early = early + dot(upper, grad_low, ((1,), (0,)))
            late = late + dot((second * second_scores).astype(bf16), grad_low[half:], ((1,), (0,)))
        inner = jnp.concatenate([early, late], axis=0)
        skip = skip_ref[:, at]
        skip_grad_ref[:, at] += jnp.sum(grad_values * x_values, axis=0, keepdims=True)
        inner_ref[:, at] = grad_values * (values_ref[:, at] - skip * x_values)
        source_ref[:, at] = x_wide * inner
        carry_ref[:, at] = x_wide * grad_scaled
        grad_x = skip * grad_values + step_pair * (inner + gap * grad_scaled)
        grad_total = grad_x * (sigmoid * (1.0 + total * (1.0 - sigmoid)))
        for k in range(CONV):
            taps_grad_ref[k : k + 1, at] += jnp.sum(grad_total * seen[k], axis=0, keepdims=True)
        taps_grad_ref[CONV : CONV + 1, at] += jnp.sum(grad_total, axis=0, keepdims=True)
        extended = jnp.concatenate([grad_total, edge_ref[:, at]], axis=0)
        edge_ref[:, at] = grad_total[:8]
        taps = taps_ref[:, at]
        grad_conv = taps[CONV - 1 : CONV] * grad_total
        for k in range(CONV - 1):
            grad_conv = grad_conv + taps[k : k + 1] * extended[CONV - 1 - k : CONV - 1 - k + seg_len]
        grad_x_ref[:, at] = grad_conv.astype(bf16)

    heads = heads_ref[...]
    tail = jnp.exp2(sums[seg_len - 1 :] - sums)
    source_grad = split_dot(source_ref[...], heads)
    step_grad = source_grad + tail * split_dot(carry_ref[...], heads)
    used = step * step_grad
    sum_grad = split_dot(inner_ref[...], heads) - used
    at_last = jnp.sum(used - step * source_grad, axis=0, keepdims=True)
    at_last = at_last + split_dot(decay_ref[...], heads)[:1] * jnp.exp2(sums[seg_len - 1 :])
    is_last = lax.broadcasted_iota(jnp.int32, (seg_len, LANES), 0) == seg_len - 1
    sum_grad = sum_grad + jnp.where(is_last, at_last, 0.0)
    at_or_after = lax.broadcasted_iota(jnp.int32, (seg_len, seg_len), 0) <= lax.broadcasted_iota(
        jnp.int32, (seg_len, seg_len), 1
    )
    log_grad = lax.dot_general(
        jnp.where(at_or_after, 1.0, 0.0), sum_grad, (((1,), (0,)), ((), ())),
        precision=lax.Precision.HIGHEST, preferred_element_type=f32,
    )
    grad_raw = (step_grad + head_ref[0:1] * log_grad) * jax.nn.sigmoid(shifted)
    grad_raw_ref[...] = grad_raw
    head_grad_ref[0:1] += jnp.sum(log_grad * log_decay, axis=0, keepdims=True)
    head_grad_ref[1:2] += jnp.sum(grad_raw, axis=0, keepdims=True)

    first_low = jnp.where(kept, first_grad, 0.0)
    second_low = jnp.where(kept, second_grad, 0.0)
    grad_scores = jnp.concatenate(
        [
            jnp.concatenate([first_low, later_grad], axis=1),
            jnp.concatenate([jnp.zeros_like(first_low), second_low], axis=1),
        ],
        axis=0,
    )
    start_ref[...] = later_ref[...]
    grad_b_ref[...] = dot(scaled_ref[...], local_ref[...], ((1,), (1,))) + dot(
        grad_scores.astype(bf16), c_low, ((1,), (0,))
    )
    grad_c_ref[...] = dot(grad_state_ref[...], prior_ref[0], ((1,), (1,))) + dot(
        grad_scores.T.astype(bf16), b_low, ((1,), (0,))
    )


def scan_backward(proj, taps, head, skip, rim, end, prior, values, grad_values, seg_len):
    length = proj.shape[0]
    segs = length // seg_len
    wide = HALF + 2 * STATE
    channel = lax.broadcasted_iota(jnp.int32, (HALF, LANES), 0) // HEADDIM
    heads = (channel == lax.broadcasted_iota(jnp.int32, (HALF, LANES), 1)).astype(bf16)
    back = lambda width: pl.BlockSpec((seg_len, width), lambda i: (segs - 1 - i, 0))
    ahead = lambda i: (jnp.maximum((segs - 1 - i) * (seg_len // 8) - 1, 0), 0)
    return pl.pallas_call(
        backward_kernel,
        grid=(segs,),
        out_shape=(
            jax.ShapeDtypeStruct((length, HALF), bf16),
            jax.ShapeDtypeStruct((length, STATE), f32),
            jax.ShapeDtypeStruct((length, STATE), f32),
            jax.ShapeDtypeStruct((length, LANES), f32),
            jax.ShapeDtypeStruct((8, HALF), f32),
            jax.ShapeDtypeStruct((1, HALF), f32),
            jax.ShapeDtypeStruct((8, LANES), f32),
            jax.ShapeDtypeStruct((8, HALF), f32),
            jax.ShapeDtypeStruct((STATE, HALF), f32),
        ),
        in_specs=[
            back(proj.shape[1]),
            pl.BlockSpec((8, proj.shape[1]), ahead),
            full_block((8, wide)),
            full_block((8, LANES)),
            full_block((1, HALF)),
            full_block((8, wide)),
            full_block((HALF, LANES)),
            full_block((STATE, HALF)),
            pl.BlockSpec((1, STATE, HALF), lambda i: (segs - 1 - i, 0, 0)),
            back(HALF),
            back(HALF),
        ],
        out_specs=(
            back(HALF),
            back(STATE),
            back(STATE),
            back(LANES),
            full_block((8, HALF)),
            full_block((1, HALF)),
            full_block((8, LANES)),
            full_block((8, HALF)),
            full_block((STATE, HALF)),
        ),
        scratch_shapes=[
            pltpu.VMEM((STATE, HALF), f32),
            pltpu.VMEM((STATE, HALF), bf16),
            pltpu.VMEM((seg_len, HALF), bf16),
            pltpu.VMEM((seg_len, HALF), bf16),
            pltpu.VMEM((seg_len, HALF), f32),
            pltpu.VMEM((seg_len, HALF), f32),
            pltpu.VMEM((seg_len, HALF), f32),
            pltpu.VMEM((8, HALF), f32),
        ],
        compiler_params=pltpu.CompilerParams(
            dimension_semantics=("arbitrary",), vmem_limit_bytes=VMEM_LIMIT
        ),
        cost_estimate=pl.CostEstimate(
            flops=10 * length * seg_len * HALF,
            bytes_accessed=proj.size * 16,
            transcendentals=length * seg_len * HEADS // 2,
        ),
    )(proj, proj, taps, head, skip, rim, heads, end, prior, values, grad_values)


def shared_kernel(core_ref, proj_ref, rim_ref, taps_ref, b_ref, c_ref, other_ref, grad_ref, taps_grad_ref, edge_ref):
    total, seen = conv_parts(proj_ref[...], rim_ref[...], taps_ref[...])
    sigmoid = jax.nn.sigmoid(total)
    grad_total = jnp.where(core_ref[0] == 0, b_ref[...], c_ref[...]) + other_ref[...]
    grad_total = grad_total * (sigmoid * (1.0 + total * (1.0 - sigmoid)))
    sums = [jnp.sum(grad_total * part, axis=0, keepdims=True) for part in seen]
    sums = sums + [jnp.sum(grad_total, axis=0, keepdims=True), jnp.zeros((8 - CONV - 1, LANES), f32)]
    taps_grad_ref[...] = jnp.concatenate(sums, axis=0)
    edge_ref[...] = grad_total[:8]
    taps = taps_ref[...]
    extended = jnp.concatenate([grad_total, jnp.zeros((8, LANES), f32)], axis=0)
    grad_conv = taps[CONV - 1 : CONV] * grad_total
    for k in range(CONV - 1):
        grad_conv = grad_conv + taps[k : k + 1] * extended[CONV - 1 - k : CONV - 1 - k + grad_total.shape[0]]
    grad_ref[...] = grad_conv.astype(bf16)


def shared_backward(core, proj, rim, taps, grad_b, grad_c, other):
    length = proj.shape[0]
    picked = lambda rows: pl.BlockSpec((rows, LANES), lambda i, core: (0, HALF // LANES + core[0]))
    whole = lambda rows: pl.BlockSpec((rows, LANES), lambda i, core: (0, 0))
    return pl.pallas_call(
        shared_kernel,
        grid_spec=pltpu.PrefetchScalarGridSpec(
            num_scalar_prefetch=1,
            grid=(1,),
            in_specs=[picked(length), picked(8), picked(8), whole(length), whole(length), whole(length)],
            out_specs=(whole(length), whole(8), whole(8)),
        ),
        out_shape=(
            jax.ShapeDtypeStruct((length, LANES), bf16),
            jax.ShapeDtypeStruct((8, LANES), f32),
            jax.ShapeDtypeStruct((8, LANES), f32),
        ),
        compiler_params=pltpu.CompilerParams(vmem_limit_bytes=VMEM_LIMIT),
        cost_estimate=pl.CostEstimate(flops=40 * length * LANES, bytes_accessed=24 * length * LANES, transcendentals=length * LANES),
    )(core.reshape(1).astype(jnp.int32), proj, rim, taps, grad_b, grad_c, other)


def per_device(hidden_in, cotangent, in_proj, out_proj, conv_params, pre_gain, gated_gain, head_params):
    chips, line = lax.axis_size("chip"), lax.axis_size("seg")
    core, place = lax.axis_index("core"), lax.axis_index("seg")
    rows, model_width = in_proj.shape[0], hidden_in.shape[2]
    heads = HEADS // 2

    conv_width, gain_width = conv_params.shape[1], gated_gain.shape[0]
    used = HALF + 2 * STATE + heads
    spare = -used % LANES
    small = jnp.zeros((rows, spare), bf16)
    small = small.at[: CONV + 1, :conv_width].set(conv_params)
    small = small.at[CONV + 1, :rows].set(pre_gain)
    small = small.at[CONV + 2, :gain_width].set(gated_gain)

    def conv_side(which):
        return jnp.concatenate(
            [
                own_columns(in_proj[:, INNER : 2 * INNER], which),
                in_proj[:, 2 * INNER : INNER + XBC],
                own_columns(in_proj[:, INNER + XBC :], which),
                small,
            ],
            axis=1,
        )

    def gate_side(which):
        return own_columns(in_proj[:, :INNER], which)

    conv_swap = to_partner(conv_side(1 - core))
    conv_block = in_core_order(conv_side(core), conv_swap, core, 0)
    gate_swap = to_partner(after(gate_side(1 - core), conv_swap))
    gate_block = in_core_order(gate_side(core), gate_swap, core, 0)
    conv_parts_z = gather_first(conv_block)
    gate_parts_z = gather_first(after(gate_block, conv_parts_z))
    conv_parts_2 = gather_next(conv_parts_z, 1)
    hidden_half = whole_sequence(after(hidden_in, gate_parts_z), core, place)
    conv_all_parts = gather_next(conv_parts_2, 2)
    hidden = in_core_order(hidden_half, to_partner(hidden_half), core, 1)
    out_parts_z = gather_first(after(out_proj, hidden_half))
    conv_all = whole_matrix(conv_all_parts, conv_block, True).reshape(model_width, -1)
    gate_parts_2 = gather_next(after(gate_parts_z, conv_all_parts), 1)
    gate_all_parts = gather_next(gate_parts_2, 2)
    cot_half = whole_sequence(after(cotangent, out_parts_z), core, place)
    out_parts_2 = gather_next(after(out_parts_z, gate_all_parts), 1)
    out_all_parts = gather_next(out_parts_2, 2)
    cot = in_core_order(cot_half, to_partner(cot_half), core, 1)

    small_all = conv_all.reshape(chips, 2, line, rows, -1)[..., used:].astype(f32)
    taps_full = small_all[..., : CONV + 1, :conv_width].transpose(3, 0, 1, 2, 4).reshape(CONV + 1, XBC)
    taps = jnp.concatenate([own_columns(taps_full[:, :INNER], core), taps_full[:, INNER:]], axis=1)
    gain_pre = small_all[..., CONV + 1, :rows].reshape(model_width)
    gain_gate = lax.dynamic_index_in_dim(
        small_all[..., CONV + 2, :gain_width], core, axis=1, keepdims=False
    ).reshape(HALF)
    params = own_columns(head_params, core)

    seg_len = hidden.shape[1] * hidden.shape[2]
    tokens = SEGS * seg_len
    upstream = cot.reshape(tokens, model_width)
    normed = pre_norm(hidden.reshape(tokens, model_width).astype(f32), gain_pre).astype(bf16)
    projected = dot(normed, conv_all, ((1,), (0,)))

    taps = jnp.pad(taps, ((0, 8 - CONV - 1), (0, 0)))
    head = jnp.pad(jnp.stack([-jnp.exp(params[0]), params[1]]), ((0, 6), (0, LANES - heads)))
    skip = jnp.repeat(params[2], HEADDIM).reshape(1, HALF)
    wide = HALF + 2 * STATE
    rim = borrowed(projected[tokens - 8 :, :wide], 1)
    nothing = jnp.zeros((STATE, HALF), f32)
    values, prior, final, last = scan_forward(projected, taps, head, skip, rim, nothing, seg_len)
    if line > SEGS:
        last = jnp.sum(last.reshape(SEGS, 8, LANES)[:, 0, :heads], axis=0)
        decay = jnp.repeat(jnp.exp2(last), HEADDIM)
        begin = entering(decay, final, 1)
        values, prior, _, _ = scan_forward(projected, taps, head, skip, rim, begin, seg_len)

    values, gate_all_parts = lax.optimization_barrier((values, gate_all_parts))
    gate_matrix = whole_matrix(gate_all_parts, gate_block, True).reshape(model_width, -1)
    gate_input = dot(normed, gate_matrix, ((1,), (0,)))
    out_matrix = whole_matrix(after(out_all_parts, gate_input), out_proj, False).reshape(HALF, model_width)
    grad_mixed = dot(upstream, out_matrix, ((1,), (1,)))

    silu_gate = jax.nn.silu(gate_input)
    gated = values * silu_gate
    gain_grad = grad_mixed * gain_gate
    sums = jnp.stack([jnp.sum(gated * gated, axis=1), jnp.sum(gain_grad * gated, axis=1)])
    sums = (sums + to_partner(sums)) / INNER
    scale = lax.rsqrt(sums[0] + epsilon)[:, None]
    unit = gated * scale
    mixed = (unit * gain_gate).astype(bf16)
    gate_gain_grad = jnp.sum(grad_mixed * unit, axis=0)
    grad_gated = scale * (gain_grad - unit * (scale * sums[1][:, None]))
    grad_values = grad_gated * silu_gate
    sigmoid = jax.nn.sigmoid(gate_input)
    grad_gate = (grad_gated * values * (sigmoid * (1.0 + gate_input * (1.0 - sigmoid)))).astype(bf16)

    def by_owner(grad):
        a, b, z = chip_dims()
        return grad.reshape(a, b, 2, z, rows, -1).transpose(0, 1, 3, 2, 4, 5)

    out_grad = dot(mixed, upstream, ((0,), (0,))).reshape(chip_dims() + (-1, model_width))
    out_first = reduce_first(out_grad)
    gate_grad = by_owner(dot(normed, grad_gate, ((0,), (0,))))
    gate_first = reduce_first(after(gate_grad, out_first))

    def halves(partial):
        parted = partial.reshape(SEGS, 2, seg_len // 2, model_width)
        mine = lax.dynamic_index_in_dim(parted, core, axis=1, keepdims=False)
        theirs = lax.dynamic_index_in_dim(parted, 1 - core, axis=1, keepdims=False)
        return mine + to_partner(theirs.astype(bf16)).astype(f32)

    branch = halves(dot(mixed, out_matrix, ((1,), (0,))))
    hidden_out = back_to_owner(
        (hidden_half.astype(f32) + branch).astype(bf16), core, place
    )

    grad_values = after(grad_values, branch)
    back = scan_backward(projected, taps, head, skip, rim, nothing, prior, values, grad_values, seg_len)
    back, out_first, gate_first = lax.optimization_barrier((back, out_first, gate_first))
    if line > SEGS:
        end = entering(decay, back[-1], -1)
        back = scan_backward(projected, taps, head, skip, rim, end, prior, values, grad_values, seg_len)
    grad_x, grad_b, grad_c, grad_raw, x_taps_grad, skip_grad, head_sums, x_edge, _ = back
    head_grad = jnp.concatenate([head_sums[:2, :heads], skip_grad.reshape(1, heads, HEADDIM).sum(axis=2)])

    out_second = reduce_second(out_first)
    gate_second = reduce_second(after(gate_first, out_second))

    other = to_partner(jnp.where(core == 0, grad_c, grad_b))
    grad_state, state_taps_grad, state_edge = shared_backward(core, projected, rim, taps, grad_b, grad_c, other)
    if line > SEGS:
        edge = borrowed(jnp.concatenate([x_edge, state_edge], axis=1), -1)
        own_taps = jnp.concatenate(
            [taps[:, :HALF], lax.dynamic_slice_in_dim(taps, HALF + core * STATE, STATE, axis=1)], axis=1
        )
        spill = jnp.stack(
            [
                sum(own_taps[k] * edge[CONV - 1 - k - early] for k in range(CONV - early))
                for early in range(CONV - 1, 0, -1)
            ]
        )
        add = lambda array, part: array.at[tokens - CONV + 1 :].set(
            (array[tokens - CONV + 1 :].astype(f32) + part).astype(bf16)
        )
        grad_x, grad_state = add(grad_x, spill[:, :HALF]), add(grad_state, spill[:, HALF:])
    grad_proj = jnp.concatenate([grad_x, grad_state, grad_raw.astype(bf16)], axis=1)
    state_taps_grad = state_taps_grad[: CONV + 1]
    none = jnp.zeros_like(state_taps_grad)
    taps_grad = jnp.concatenate(
        [
            x_taps_grad[: CONV + 1],
            jnp.where(core == 0, state_taps_grad, none),
            jnp.where(core == 0, none, state_taps_grad),
        ],
        axis=1,
    )
    conv_grad = by_owner(dot(normed, grad_proj, ((0,), (0,))))
    conv_grad, out_second, gate_second = lax.optimization_barrier((conv_grad, out_second, gate_second))
    conv_first = reduce_first(conv_grad)
    out_third = reduce_third(out_second)
    gate_third = reduce_third(after(gate_second, out_third))

    state_weights = lax.dynamic_slice_in_dim(conv_all, HALF + core * STATE, STATE, axis=1)
    conv_matrix = jnp.concatenate(
        [conv_all[:, :HALF], state_weights, conv_all[:, HALF + 2 * STATE :]], axis=1
    )
    grad_normed = halves(
        dot(grad_gate, gate_matrix, ((1,), (1,))) + dot(grad_proj, conv_matrix, ((1,), (1,)))
    )
    grad_normed, conv_first = lax.optimization_barrier((grad_normed, conv_first))
    conv_second = reduce_second(conv_first)
    _, pre_pull = jax.vjp(pre_norm, hidden_half.astype(f32), gain_pre)
    grad_hidden, pre_gain_grad = pre_pull(grad_normed)
    grad_in = back_to_owner(
        (cot_half.astype(f32) + grad_hidden).astype(bf16), core, place
    )

    def spread_own(array):
        width = array.shape[-1] // chips
        parted = array.reshape(array.shape[:-1] + (chips, 1, width))
        none = jnp.zeros_like(parted)
        both = jnp.where(
            core == 0,
            jnp.concatenate([parted, none], axis=-2),
            jnp.concatenate([none, parted], axis=-2),
        )
        return both.reshape(array.shape[:-1] + (2 * array.shape[-1],))

    taps_all = jnp.concatenate([spread_own(taps_grad[:, :HALF]), taps_grad[:, HALF:]], axis=1)
    taps_all = taps_all.reshape(CONV + 1, chips, 2, line, conv_width).transpose(1, 3, 2, 0, 4)
    gate_all = spread_own(gate_gain_grad).reshape(chips, 2, line, gain_width).transpose(0, 2, 1, 3)
    head_all = jnp.broadcast_to(spread_own(head_grad).reshape(-1), (chips, line, 2, 3 * HEADS))
    small_grads = jnp.concatenate(
        [
            taps_all.reshape(chips, line, 2, -1),
            pre_gain_grad.reshape(chips, 2, line, rows).transpose(0, 2, 1, 3),
            gate_all,
            head_all,
        ],
        axis=3,
    )
    count = small_grads.shape[3]
    small_grads = small_grads.reshape(chip_dims() + (2, count))
    small_share = reduce_end(reduce_third(reduce_second(reduce_first(small_grads, f32), f32), f32))
    conv_second, out_third, gate_third = lax.optimization_barrier((conv_second, out_third, gate_third))
    conv_third = reduce_third(conv_second)
    out_share = reduce_end(out_third).reshape(-1, model_width)
    gate_share = reduce_end(gate_third).astype(bf16)
    conv_share = reduce_end(conv_third).astype(bf16)

    def mine_and_partner(share):
        keep = lax.dynamic_index_in_dim(share, core, axis=0, keepdims=False)
        give = lax.dynamic_index_in_dim(share, 1 - core, axis=0, keepdims=False)
        return keep, to_partner(give)

    keep, got = mine_and_partner(small_share)
    small_total = keep + got
    taps_end = (CONV + 1) * conv_width
    taps_share = small_total[:taps_end].reshape(CONV + 1, conv_width)
    pre_share = small_total[taps_end : taps_end + rows]
    gain_share = small_total[taps_end + rows : taps_end + rows + gain_width]
    head_total = small_total[taps_end + rows + gain_width :].reshape(3, HEADS)

    def interleave(mine, theirs):
        width = mine.shape[1] // chips
        both = in_core_order(mine.reshape(rows, chips, width), theirs.reshape(rows, chips, width), core, 2)
        return both.reshape(rows, -1)

    keep_gate, got_gate = mine_and_partner(gate_share)
    keep, got = mine_and_partner(conv_share)
    state_end = HALF + STATE
    in_share = jnp.concatenate(
        [
            interleave(keep_gate, got_gate),
            interleave(keep[:, :HALF], got[:, :HALF]),
            in_core_order(keep[:, HALF:state_end], got[:, HALF:state_end], core, 1).reshape(rows, -1),
            interleave(keep[:, state_end : state_end + heads], got[:, state_end : state_end + heads]),
        ],
        axis=1,
    ).astype(f32)
    return (hidden_out, grad_in, in_share, out_share, taps_share, pre_share, gain_share, head_total)


def solution(mesh):
    devices = mesh.devices
    cores = Mesh(devices.reshape(devices.shape[0] // 2, 2, devices.shape[1]), ("chip", "core", "seg"))
    dp, both = ("chip", "core"), ("chip", "core", "seg")
    tokens = P(dp, "seg", None)
    return jax.shard_map(
        per_device,
        mesh=cores,
        in_specs=(tokens, tokens, P(both, None), P(both, None), P(None, both), P(both), P(both), P()),
        out_specs=(tokens, tokens, P(both, None), P(both, None), P(None, both), P(both), P(both), P()),
        check_vma=False,
    )
```

```python
import jax
import jax.numpy as jnp
from jax import lax
from jax.experimental import pallas as pl
from jax.experimental.pallas import tpu as pltpu
from jax.sharding import Mesh
from jax.sharding import PartitionSpec as P

HEADS = 48
HEADDIM = 64
STATE = 128
CONV = 4
INNER = 3072
XBC = 3328
HALF = INNER // 2
LANES = 128
SEGS = 4
VMEM_LIMIT = 48 * 1024 * 1024
LOG2E = 1.4426950408889634

epsilon = 1e-05
f32 = jnp.float32
bf16 = jnp.bfloat16


def own_columns(array, core):
    chips = lax.axis_size("chip")
    width = array.shape[-1] // (2 * chips)
    parted = array.reshape(array.shape[:-1] + (chips, 2, width))
    picked = lax.dynamic_index_in_dim(parted, core, axis=parted.ndim - 2, keepdims=False)
    return picked.reshape(array.shape[:-1] + (chips * width,))


def to_partner(array):
    return lax.ppermute(array, "core", [(0, 1), (1, 0)])


def in_core_order(mine, theirs, core, axis):
    first = jnp.where(core == 0, mine, theirs)
    second = jnp.where(core == 0, theirs, mine)
    return jnp.stack([first, second], axis=axis)


def chip_dims():
    return (lax.axis_size("chip") // 2, 2, lax.axis_size("seg"))


def chip_place():
    chip = lax.axis_index("chip")
    return (chip // 2, chip % 2, lax.axis_index("seg"))


def moved(array, dim, by):
    sizes = chip_dims()
    index = lambda at: (at[0] * sizes[1] + at[1]) * sizes[2] + at[2]
    pairs = []
    for a in range(sizes[0]):
        for b in range(sizes[1]):
            for z in range(sizes[2]):
                to = [a, b, z]
                to[dim] = (to[dim] + by) % sizes[dim]
                pairs.append((index((a, b, z)), index(to)))
    return lax.ppermute(array, ("chip", "seg"), pairs)


def after(value, *earlier):
    return lax.optimization_barrier((value, earlier))[0]


ORDERS = ((2, 0, 1), (2, 1, 0))


def column_parts(width):
    cut = -(-(width // 2) // LANES) * LANES
    return ((0, cut), (cut, width))


def gather_step(data, dim):
    return [data] + [moved(data, dim, by) for by in range(1, chip_dims()[dim])]


def gather_first(block):
    pieces = gather_step(block, 2)
    return [[piece[..., begin:end] for piece in pieces] for begin, end in column_parts(block.shape[-1])]


def gather_next(parts, step):
    return [gather_step(jnp.stack(part), order[step]) for order, part in zip(ORDERS, parts)]


def placed_kernel(plan, place_ref, *refs):
    sources, out_ref, sems = refs[:-2], refs[-2], refs[-1]
    copies = []
    for source, lead, at, columns, paired in plan:
        spot = [lax.rem(place_ref[dim] + (size - back), size) for dim, (back, size) in enumerate(at)]
        target = out_ref.at[spot[0], spot[1]]
        target = target.at[:, spot[2]] if paired else target.at[spot[2]]
        target = target.at[..., pl.ds(*columns)]
        copies.append(pltpu.make_async_copy(sources[source].at[lead], target, sems.at[len(copies)]))
    for copy in copies:
        copy.start()
    for copy in copies:
        copy.wait()


def whole_matrix(parts, block, paired):
    sizes = chip_dims()
    plan, sources = [], []
    for order, (begin, end), part in zip(ORDERS, column_parts(block.shape[-1]), parts):
        for back_last, piece in enumerate(part):
            for back_mid in range(sizes[order[1]]):
                for back_first in range(sizes[order[0]]):
                    at = [None] * 3
                    at[order[2]] = (back_last, sizes[order[2]])
                    at[order[1]] = (back_mid, sizes[order[1]])
                    at[order[0]] = (back_first, sizes[order[0]])
                    plan.append((len(sources), (back_mid, back_first), at, (begin, end - begin), paired))
            sources.append(piece)
    if paired:
        shape = sizes[:2] + (2, sizes[2]) + block.shape[1:]
    else:
        shape = sizes + block.shape
    anywhere = pl.BlockSpec(memory_space=pl.ANY)
    return pl.pallas_call(
        lambda *refs: placed_kernel(plan, *refs),
        out_shape=jax.ShapeDtypeStruct(shape, block.dtype),
        in_specs=[pl.BlockSpec(memory_space=pltpu.SMEM)] + [anywhere] * len(sources),
        out_specs=pl.BlockSpec(memory_space=pltpu.VMEM),
        scratch_shapes=[pltpu.SemaphoreType.DMA((len(plan),))],
        compiler_params=pltpu.CompilerParams(vmem_limit_bytes=VMEM_LIMIT),
        cost_estimate=pl.CostEstimate(flops=0, bytes_accessed=4 * block.size * sizes[0] * sizes[1] * sizes[2], transcendentals=0),
    )(jnp.stack(chip_place()).astype(jnp.int32), *sources)


def reduce_send(data, axis, dim, wire):
    place, size = chip_place()[dim], chip_dims()[dim]
    pick = lambda at: lax.dynamic_index_in_dim(data, at, axis=axis, keepdims=False)
    received = [moved(pick((place + by) % size).astype(wire), dim, by) for by in range(1, size)]
    return pick(place).astype(f32), received


def reduce_add(kept, received):
    for part in received:
        kept = kept + part.astype(f32)
    return kept


def reduce_first(partial, wire=bf16):
    (begin, cut), (_, end) = column_parts(partial.shape[-1])
    return [
        reduce_send(partial[..., begin:cut], 1, 1, wire),
        reduce_send(partial[..., cut:end], 0, 0, wire),
    ]


def weight_grad_kernel(
    cut, slabs, place_ref, left_ref, right_ref, keep_b_ref, send_b_ref, keep_a_ref, send_a_ref
):
    turn, last = pl.program_id(0), pl.num_programs(0) - 1
    rows, width = left_ref.shape[1] // 2, right_ref.shape[1]
    left = left_ref[...]
    own_first = place_ref[1] == 0
    begin = 0
    while begin < width:
        end = min(begin + 2 * LANES, cut if begin < cut else width)
        grad = dot(left, right_ref[:, begin:end], ((0,), (0,)))
        if begin < cut:
            mine = jnp.where(own_first, grad[:rows], grad[rows:])
            theirs = jnp.where(own_first, grad[rows:], grad[:rows]).astype(bf16)
            for to, at, size in slabs:
                keep_b_ref[0, to : to + size, begin:end] = mine[at : at + size]
                send_b_ref[0, to : to + size, begin:end] = theirs[at : at + size]
        else:
            columns = slice(begin - cut, end - cut)

            @pl.when(turn == last)
            def _(grad=grad, columns=columns):
                for half in range(2):
                    for to, at, size in slabs:
                        keep_a_ref[half, to : to + size, columns] = grad[half * rows + at : half * rows + at + size]

            @pl.when(turn < last)
            def _(grad=grad, columns=columns):
                for half in range(2):
                    for to, at, size in slabs:
                        part = grad[half * rows + at : half * rows + at + size]
                        send_a_ref[0, half, to : to + size, columns] = part.astype(bf16)

        begin = end


def weight_grad(left, right, paired):
    a, b, z = chip_dims()
    length, width = right.shape
    rows = left.shape[1] // (a * b)
    (_, cut), _ = column_parts(width)
    size = rows // (2 * z)
    inside = paired and size % 16 == 0
    if inside:
        slabs = [((at * 2 + core) * size, (core * z + at) * size, size) for core in range(2) for at in range(z)]
    else:
        slabs = [(0, 0, rows)]
    rest = width - cut
    others = max(a - 1, 1)
    turned = lambda i, place: lax.rem(place[0] + 1 + i, a)
    keep_b, send_b, keep_a, send_a = pl.pallas_call(
        lambda *refs: weight_grad_kernel(cut, slabs, *refs),
        grid_spec=pltpu.PrefetchScalarGridSpec(
            num_scalar_prefetch=1,
            grid=(a,),
            in_specs=[
                pl.BlockSpec((length, 2 * rows), lambda i, place: (0, turned(i, place))),
                pl.BlockSpec((length, width), lambda i, place: (0, 0)),
            ],
            out_specs=(
                pl.BlockSpec((1, rows, cut), lambda i, place: (turned(i, place), 0, 0)),
                pl.BlockSpec((1, rows, cut), lambda i, place: (turned(i, place), 0, 0)),
                pl.BlockSpec((2, rows, rest), lambda i, place: (0, 0, 0)),
                pl.BlockSpec((1, 2, rows, rest), lambda i, place: (jnp.minimum(i, others - 1), 0, 0, 0)),
            ),
        ),
        out_shape=(
            jax.ShapeDtypeStruct((a, rows, cut), f32),
            jax.ShapeDtypeStruct((a, rows, cut), bf16),
            jax.ShapeDtypeStruct((2, rows, rest), f32),
            jax.ShapeDtypeStruct((others, 2, rows, rest), bf16),
        ),
        compiler_params=pltpu.CompilerParams(
            dimension_semantics=("arbitrary",), vmem_limit_bytes=VMEM_LIMIT
        ),
        cost_estimate=pl.CostEstimate(
            flops=2 * length * left.shape[1] * width,
            bytes_accessed=2 * left.size + 2 * right.size + 3 * left.shape[1] * width,
            transcendentals=0,
        ),
    )(jnp.stack(chip_place()[:2]).astype(jnp.int32), left, right)

    def shaped(array):
        lead = array.shape[:-2]
        if inside or not paired:
            return array.reshape(lead + (z, rows // z, array.shape[-1]))
        parted = array.reshape(lead + (2, z, size, array.shape[-1]))
        return jnp.swapaxes(parted, -4, -3).reshape(lead + (z, rows // z, array.shape[-1]))

    return shaped(keep_b), shaped(send_b), shaped(keep_a), shaped(send_a)


def send_first(grads, *earlier):
    keep_b, send_b, keep_a, send_a = grads
    send_b, send_a = after((send_b, send_a), *earlier)
    return [
        (keep_b, [moved(send_b, 1, 1)]),
        (keep_a, [moved(send_a[by - 1], 0, by) for by in range(1, chip_dims()[0])]),
    ]


def reduce_second(first, wire=bf16):
    return [
        reduce_send(reduce_add(*first[0]), 0, 0, wire),
        reduce_send(reduce_add(*first[1]), 0, 1, wire),
    ]


def reduce_third(second, wire=bf16):
    return reduce_send(jnp.concatenate([reduce_add(*part) for part in second], axis=-1), 0, 2, wire)


def reduce_end(third):
    return reduce_add(*third)


def line_perm(turn, back):
    line = lax.axis_size("seg")
    parts = line // SEGS
    pairs = []
    for core in range(2):
        for place in range(line):
            piece = (place % SEGS) ^ turn
            half, index = divmod(piece, 2)
            source = core * line + place
            target = half * line + (2 * core + index) * parts + place // SEGS
            pairs.append((target, source) if back else (source, target))
    return pairs


def whole_sequence(array, core, place):
    parts = lax.axis_size("seg") // SEGS
    half = array.shape[1] // 2
    pieces = array.reshape(2, 2, half, -1).transpose(1, 0, 2, 3).reshape(4, half, -1)
    mine = place % SEGS
    target = 2 * core + (place // parts) % 2
    got = []
    for turn in range(4):
        piece = lax.dynamic_index_in_dim(pieces, mine ^ turn, axis=0, keepdims=False)
        got.append(lax.ppermute(piece, ("core", "seg"), line_perm(turn, False)))
    got = jnp.stack(got)
    return jnp.stack([lax.dynamic_index_in_dim(got, target ^ k, axis=0, keepdims=False) for k in range(4)])


def back_to_owner(ordered, core, place):
    parts = lax.axis_size("seg") // SEGS
    half = ordered.shape[1]
    mine = place % SEGS
    target = 2 * core + (place // parts) % 2
    got = []
    for turn in range(4):
        piece = lax.dynamic_index_in_dim(ordered, target ^ turn, axis=0, keepdims=False)
        got.append(lax.ppermute(piece, ("core", "seg"), line_perm(turn, True)))
    got = jnp.stack(got)
    pieces = jnp.stack([lax.dynamic_index_in_dim(got, mine ^ k, axis=0, keepdims=False) for k in range(4)])
    return pieces.reshape(2, 2, half, -1).transpose(1, 0, 2, 3).reshape(2, 2 * half, -1)


def part_pairs(step):
    line = lax.axis_size("seg")
    parts = line // SEGS
    return [(i, i + step) for i in range(line) if 0 <= i + step < line and i // parts == (i + step) // parts]


def entering(decay, state, step):
    parts = lax.axis_size("seg") // SEGS
    total = jnp.zeros_like(state)
    for _ in range(parts - 1):
        total = lax.ppermute(decay * total + state, "seg", part_pairs(step))
    return total


def borrowed(array, step):
    parts = lax.axis_size("seg") // SEGS
    if parts == 1:
        return jnp.zeros_like(array)
    return lax.ppermute(array, "seg", part_pairs(step))


def pre_norm(hidden, norm_gain):
    row_scale = lax.rsqrt(jnp.mean(hidden * hidden, axis=-1, keepdims=True) + epsilon)
    return hidden * row_scale * norm_gain


def conv_apply(padded, conv_taps):
    length = padded.shape[0] - CONV + 1
    summed = conv_taps[CONV]
    for offset in range(CONV):
        summed = summed + conv_taps[offset] * padded[offset : offset + length, :]
    return jax.nn.silu(summed)


def head_terms(step_raw, params):
    step_size = jax.nn.softplus(step_raw + params[1])
    decay_sum = jnp.cumsum(step_size * -jnp.exp(params[0]), axis=1)
    return (step_size, decay_sum)


def decay_terms(decay_sum, step_size):
    last_sum = decay_sum[:, -1:, :]
    carry_scale = jnp.exp(last_sum - decay_sum) * step_size
    return (carry_scale, jnp.exp(decay_sum[:, -1, :]), jnp.exp(decay_sum))


def dot(a, b, contract):
    return lax.dot_general(a, b, (contract, ((), ())), preferred_element_type=f32)


def columns_of(pair):
    return pl.ds(pair * LANES, LANES)


def low_half(shape):
    return lax.broadcasted_iota(jnp.int32, shape, len(shape) - 1) < HEADDIM


def pair_columns(array, pair, low):
    rows = array.shape[0]
    first = jnp.broadcast_to(array[:, 2 * pair : 2 * pair + 1], (rows, LANES))
    second = jnp.broadcast_to(array[:, 2 * pair + 1 : 2 * pair + 2], (rows, LANES))
    return jnp.where(low, first, second)


def conv_parts(current, before, taps):
    rows = current.shape[0]
    padded = jnp.concatenate([before, current], axis=0)
    seen = [padded[8 - CONV + 1 + k : 8 - CONV + 1 + k + rows] for k in range(CONV - 1)] + [current]
    total = taps[CONV : CONV + 1]
    for k in range(CONV):
        total = total + taps[k : k + 1] * seen[k]
    return total, seen


def step_terms(raw, head, seg_len):
    shifted = raw + head[1:2]
    step = jnp.maximum(shifted, 0.0) + jnp.log1p(jnp.exp(-jnp.abs(shifted)))
    log_decay = step * head[0:1]
    at_or_before = lax.broadcasted_iota(jnp.int32, (seg_len, seg_len), 0) >= lax.broadcasted_iota(
        jnp.int32, (seg_len, seg_len), 1
    )
    sums = lax.dot_general(
        jnp.where(at_or_before, 1.0, 0.0), log_decay, (((1,), (0,)), ((), ())),
        precision=lax.Precision.HIGHEST, preferred_element_type=f32,
    )
    return shifted, step, log_decay, sums * LOG2E


def forward_kernel(
    proj_ref, taps_ref, head_ref, skip_ref, rim_ref, init_ref,
    values_ref, prior_ref, final_ref, last_ref, state_ref, tail_ref,
):
    seg_len = proj_ref.shape[0]
    half = seg_len // 2

    @pl.when(pl.program_id(0) == 0)
    def _():
        state_ref[...] = init_ref[...]
        tail_ref[...] = rim_ref[...]

    def activated(begin):
        at = pl.ds(begin, LANES)
        total, _ = conv_parts(proj_ref[:, at], tail_ref[:, at], taps_ref[:, at])
        return total * jax.nn.sigmoid(total)

    b_low = activated(HALF).astype(bf16)
    b_turned = activated(HALF).T.astype(bf16)
    c_low = activated(HALF + STATE).astype(bf16)
    _, step, _, sums = step_terms(proj_ref[:, HALF + 2 * STATE :], head_ref, seg_len)
    sums_turned, step_turned = sums.T, step.T
    scores = dot(c_low, b_low, ((1,), (1,)))
    kept = lax.broadcasted_iota(jnp.int32, (half, half), 0) >= lax.broadcasted_iota(jnp.int32, (half, half), 1)
    first_scores = jnp.where(kept, scores[:half, :half], 0.0)
    later_scores = scores[half:, :half]
    second_scores = jnp.where(kept, scores[half:, half:], 0.0)
    low = low_half((seg_len, LANES))
    last_ref[...] = jnp.broadcast_to(sums[seg_len - 1 :], last_ref.shape)

    for pair in range(HEADS // 4):
        at = columns_of(pair)
        x_values = activated(pair * LANES)
        x_low = x_values.astype(bf16)
        sums_pair = pair_columns(sums, pair, low)
        last_pair = sums_pair[seg_len - 1 :]
        carry = jnp.exp2(last_pair - sums_pair) * pair_columns(step, pair, low)
        scaled_x = (carry * x_low.astype(f32)).astype(bf16)
        prior = state_ref[:, at]
        prior_low = prior.astype(bf16)
        prior_ref[0, :, at] = prior_low
        from_state = jnp.exp2(sums_pair) * dot(c_low, prior_low, ((1,), (0,)))
        state_ref[:, at] = jnp.exp2(last_pair) * prior + dot(b_turned, scaled_x, ((1,), (0,)))
        early, late = 0.0, 0.0
        for side in range(2):
            head = 2 * pair + side
            x_side = jnp.where(low if side == 0 else ~low, x_values, 0.0).astype(bf16)
            at_token = jnp.broadcast_to(sums[:, head : head + 1], (seg_len, half))
            at_source, source_step = sums_turned[head : head + 1], step_turned[head : head + 1]
            first = jnp.exp2(jnp.minimum(at_token[:half] - at_source[:, :half], 0.0)) * first_scores
            first = (first * source_step[:, :half]).astype(bf16)
            later = jnp.exp2(at_token[half:] - at_source[:, :half]) * later_scores
            later = (later * source_step[:, :half]).astype(bf16)
            second = jnp.exp2(jnp.minimum(at_token[half:] - at_source[:, half:], 0.0)) * second_scores
            second = (second * source_step[:, half:]).astype(bf16)
            early = early + dot(first, x_side[:half], ((1,), (0,)))
            late = late + dot(jnp.concatenate([later, second], axis=1), x_side, ((1,), (0,)))
        intra = jnp.concatenate([early, late], axis=0)
        values_ref[:, at] = intra + from_state + skip_ref[:, at] * x_values

    tail_ref[...] = proj_ref[seg_len - 8 :, : HALF + 2 * STATE]
    final_ref[...] = state_ref[...]


def full_block(shape):
    return pl.BlockSpec(shape, lambda *_: (0,) * len(shape))


def scan_forward(proj, taps, head, skip, rim, init, seg_len):
    segs = proj.shape[0] // seg_len
    wide = HALF + 2 * STATE
    return pl.pallas_call(
        forward_kernel,
        grid=(segs,),
        out_shape=(
            jax.ShapeDtypeStruct((proj.shape[0], HALF), f32),
            jax.ShapeDtypeStruct((segs, STATE, HALF), bf16),
            jax.ShapeDtypeStruct((STATE, HALF), f32),
            jax.ShapeDtypeStruct((segs * 8, LANES), f32),
        ),
        in_specs=[
            pl.BlockSpec((seg_len, proj.shape[1]), lambda i: (i, 0)),
            full_block((8, wide)),
            full_block((8, LANES)),
            full_block((1, HALF)),
            full_block((8, wide)),
            full_block((STATE, HALF)),
        ],
        out_specs=(
            pl.BlockSpec((seg_len, HALF), lambda i: (i, 0)),
            pl.BlockSpec((1, STATE, HALF), lambda i: (i, 0, 0)),
            full_block((STATE, HALF)),
            pl.BlockSpec((8, LANES), lambda i: (i, 0)),
        ),
        scratch_shapes=[pltpu.VMEM((STATE, HALF), f32), pltpu.VMEM((8, wide), f32)],
        compiler_params=pltpu.CompilerParams(
            dimension_semantics=("arbitrary",), vmem_limit_bytes=VMEM_LIMIT
        ),
        cost_estimate=pl.CostEstimate(
            flops=4 * proj.shape[0] * seg_len * HALF,
            bytes_accessed=proj.size * 8,
            transcendentals=proj.shape[0] * seg_len * HEADS // 2,
        ),
    )(proj, taps, head, skip, rim, init)


def split_dot(array, other):
    high = array.astype(bf16)
    rest = (array - high.astype(f32)).astype(bf16)
    return dot(high, other, ((1,), (0,))) + dot(rest, other, ((1,), (0,)))


def backward_kernel(
    proj_ref, before_ref, taps_ref, head_ref, skip_ref, rim_ref, heads_ref, end_ref, prior_ref, values_ref, grad_ref,
    grad_x_ref, grad_b_ref, grad_c_ref, grad_raw_ref, taps_grad_ref, skip_grad_ref, head_grad_ref, edge_ref, start_ref,
    later_ref, local_ref, scaled_ref, grad_state_ref, inner_ref, source_ref, carry_ref, decay_ref,
):
    seg_len = proj_ref.shape[0]
    half = seg_len // 2
    turn = pl.program_id(0)

    @pl.when(turn == 0)
    def _():
        later_ref[...] = end_ref[...]
        edge_ref[...] = jnp.zeros_like(edge_ref)
        taps_grad_ref[...] = jnp.zeros_like(taps_grad_ref)
        skip_grad_ref[...] = jnp.zeros_like(skip_grad_ref)
        head_grad_ref[...] = jnp.zeros_like(head_grad_ref)

    first_segment = turn == pl.num_programs(0) - 1

    def conv_at(begin):
        at = pl.ds(begin, LANES)
        before = jnp.where(first_segment, rim_ref[:, at], before_ref[:, at])
        return conv_parts(proj_ref[:, at], before, taps_ref[:, at])

    def activated(begin):
        total, _ = conv_at(begin)
        return total * jax.nn.sigmoid(total)

    b_values = activated(HALF)
    c_values = activated(HALF + STATE)
    b_low, c_low, c_turned = b_values.astype(bf16), c_values.astype(bf16), c_values.T.astype(bf16)
    shifted, step, log_decay, sums = step_terms(proj_ref[:, HALF + 2 * STATE :], head_ref, seg_len)
    sums_turned = sums.T
    scores = dot(b_low, c_low, ((1,), (1,)))
    kept = lax.broadcasted_iota(jnp.int32, (half, half), 0) <= lax.broadcasted_iota(jnp.int32, (half, half), 1)
    first_scores = jnp.where(kept, scores[:half, :half], 0.0)
    later_scores = scores[:half, half:]
    second_scores = jnp.where(kept, scores[half:, half:], 0.0)
    low = low_half((seg_len, LANES))
    first_grad, later_grad, second_grad = 0.0, 0.0, 0.0

    for pair in range(HEADS // 4):
        at = columns_of(pair)
        total, seen = conv_at(pair * LANES)
        sigmoid = jax.nn.sigmoid(total)
        x_values = total * sigmoid
        x_low = x_values.astype(bf16)
        x_wide = x_low.astype(f32)
        sums_pair = pair_columns(sums, pair, low)
        step_pair = pair_columns(step, pair, low)
        last_pair = sums_pair[seg_len - 1 :]
        gap = jnp.exp2(last_pair - sums_pair)
        scaled_ref[:, at] = (gap * step_pair * x_wide).astype(bf16)
        grad_values = grad_ref[:, at]
        grad_state_ref[:, at] = (grad_values * jnp.exp2(sums_pair)).astype(bf16)
        later = later_ref[:, at]
        later_low = later.astype(bf16)
        local_ref[:, at] = later_low
        prior = prior_ref[0, :, at]
        decay_ref[:, at] = jnp.broadcast_to(
            jnp.sum(later * prior.astype(f32), axis=0, keepdims=True), (8, LANES)
        )
        grad_prior = dot(c_turned, grad_state_ref[:, at], ((1,), (0,)))
        later_ref[:, at] = jnp.exp2(last_pair) * later + grad_prior
        grad_scaled = dot(b_low, later_low, ((1,), (0,)))
        stepped = (step_pair * x_wide).astype(bf16)
        early, late = 0.0, 0.0
        for side in range(2):
            head = 2 * pair + side
            grad_low = jnp.where(low if side == 0 else ~low, grad_values, 0.0).astype(bf16)
            at_source = jnp.broadcast_to(sums[:, head : head + 1], (seg_len, half))
            at_token = sums_turned[head : head + 1]
            grad_weights = dot(stepped, grad_low, ((1,), (1,)))
            first = jnp.exp2(jnp.minimum(at_token[:, :half] - at_source[:half], 0.0))
            after = jnp.exp2(at_token[:, half:] - at_source[:half])
            second = jnp.exp2(jnp.minimum(at_token[:, half:] - at_source[half:], 0.0))
            first_grad = first_grad + first * grad_weights[:half, :half]
            later_grad = later_grad + after * grad_weights[:half, half:]
            second_grad = second_grad + second * grad_weights[half:, half:]
            upper = jnp.concatenate([first * first_scores, after * later_scores], axis=1).astype(bf16)
            early = early + dot(upper, grad_low, ((1,), (0,)))
            late = late + dot((second * second_scores).astype(bf16), grad_low[half:], ((1,), (0,)))
        inner = jnp.concatenate([early, late], axis=0)
        skip = skip_ref[:, at]
        skip_grad_ref[:, at] += jnp.sum(grad_values * x_values, axis=0, keepdims=True)
        inner_ref[:, at] = grad_values * (values_ref[:, at] - skip * x_values)
        source_ref[:, at] = x_wide * inner
        carry_ref[:, at] = x_wide * grad_scaled
        grad_x = skip * grad_values + step_pair * (inner + gap * grad_scaled)
        grad_total = grad_x * (sigmoid * (1.0 + total * (1.0 - sigmoid)))
        for k in range(CONV):
            taps_grad_ref[k : k + 1, at] += jnp.sum(grad_total * seen[k], axis=0, keepdims=True)
        taps_grad_ref[CONV : CONV + 1, at] += jnp.sum(grad_total, axis=0, keepdims=True)
        extended = jnp.concatenate([grad_total, edge_ref[:, at]], axis=0)
        edge_ref[:, at] = grad_total[:8]
        taps = taps_ref[:, at]
        grad_conv = taps[CONV - 1 : CONV] * grad_total
        for k in range(CONV - 1):
            grad_conv = grad_conv + taps[k : k + 1] * extended[CONV - 1 - k : CONV - 1 - k + seg_len]
        grad_x_ref[:, at] = grad_conv.astype(bf16)

    heads = heads_ref[...]
    tail = jnp.exp2(sums[seg_len - 1 :] - sums)
    source_grad = split_dot(source_ref[...], heads)
    step_grad = source_grad + tail * split_dot(carry_ref[...], heads)
    used = step * step_grad
    sum_grad = split_dot(inner_ref[...], heads) - used
    at_last = jnp.sum(used - step * source_grad, axis=0, keepdims=True)
    at_last = at_last + split_dot(decay_ref[...], heads)[:1] * jnp.exp2(sums[seg_len - 1 :])
    is_last = lax.broadcasted_iota(jnp.int32, (seg_len, LANES), 0) == seg_len - 1
    sum_grad = sum_grad + jnp.where(is_last, at_last, 0.0)
    at_or_after = lax.broadcasted_iota(jnp.int32, (seg_len, seg_len), 0) <= lax.broadcasted_iota(
        jnp.int32, (seg_len, seg_len), 1
    )
    log_grad = lax.dot_general(
        jnp.where(at_or_after, 1.0, 0.0), sum_grad, (((1,), (0,)), ((), ())),
        precision=lax.Precision.HIGHEST, preferred_element_type=f32,
    )
    grad_raw = (step_grad + head_ref[0:1] * log_grad) * jax.nn.sigmoid(shifted)
    grad_raw_ref[...] = grad_raw
    head_grad_ref[0:1] += jnp.sum(log_grad * log_decay, axis=0, keepdims=True)
    head_grad_ref[1:2] += jnp.sum(grad_raw, axis=0, keepdims=True)

    first_low = jnp.where(kept, first_grad, 0.0)
    second_low = jnp.where(kept, second_grad, 0.0)
    grad_scores = jnp.concatenate(
        [
            jnp.concatenate([first_low, later_grad], axis=1),
            jnp.concatenate([jnp.zeros_like(first_low), second_low], axis=1),
        ],
        axis=0,
    )
    start_ref[...] = later_ref[...]
    grad_b_ref[...] = dot(scaled_ref[...], local_ref[...], ((1,), (1,))) + dot(
        grad_scores.astype(bf16), c_low, ((1,), (0,))
    )
    grad_c_ref[...] = dot(grad_state_ref[...], prior_ref[0], ((1,), (1,))) + dot(
        grad_scores.T.astype(bf16), b_low, ((1,), (0,))
    )


def scan_backward(proj, taps, head, skip, rim, end, prior, values, grad_values, seg_len):
    length = proj.shape[0]
    segs = length // seg_len
    wide = HALF + 2 * STATE
    channel = lax.broadcasted_iota(jnp.int32, (HALF, LANES), 0) // HEADDIM
    heads = (channel == lax.broadcasted_iota(jnp.int32, (HALF, LANES), 1)).astype(bf16)
    back = lambda width: pl.BlockSpec((seg_len, width), lambda i: (segs - 1 - i, 0))
    ahead = lambda i: (jnp.maximum((segs - 1 - i) * (seg_len // 8) - 1, 0), 0)
    return pl.pallas_call(
        backward_kernel,
        grid=(segs,),
        out_shape=(
            jax.ShapeDtypeStruct((length, HALF), bf16),
            jax.ShapeDtypeStruct((length, STATE), f32),
            jax.ShapeDtypeStruct((length, STATE), f32),
            jax.ShapeDtypeStruct((length, LANES), f32),
            jax.ShapeDtypeStruct((8, HALF), f32),
            jax.ShapeDtypeStruct((1, HALF), f32),
            jax.ShapeDtypeStruct((8, LANES), f32),
            jax.ShapeDtypeStruct((8, HALF), f32),
            jax.ShapeDtypeStruct((STATE, HALF), f32),
        ),
        in_specs=[
            back(proj.shape[1]),
            pl.BlockSpec((8, proj.shape[1]), ahead),
            full_block((8, wide)),
            full_block((8, LANES)),
            full_block((1, HALF)),
            full_block((8, wide)),
            full_block((HALF, LANES)),
            full_block((STATE, HALF)),
            pl.BlockSpec((1, STATE, HALF), lambda i: (segs - 1 - i, 0, 0)),
            back(HALF),
            back(HALF),
        ],
        out_specs=(
            back(HALF),
            back(STATE),
            back(STATE),
            back(LANES),
            full_block((8, HALF)),
            full_block((1, HALF)),
            full_block((8, LANES)),
            full_block((8, HALF)),
            full_block((STATE, HALF)),
        ),
        scratch_shapes=[
            pltpu.VMEM((STATE, HALF), f32),
            pltpu.VMEM((STATE, HALF), bf16),
            pltpu.VMEM((seg_len, HALF), bf16),
            pltpu.VMEM((seg_len, HALF), bf16),
            pltpu.VMEM((seg_len, HALF), f32),
            pltpu.VMEM((seg_len, HALF), f32),
            pltpu.VMEM((seg_len, HALF), f32),
            pltpu.VMEM((8, HALF), f32),
        ],
        compiler_params=pltpu.CompilerParams(
            dimension_semantics=("arbitrary",), vmem_limit_bytes=VMEM_LIMIT
        ),
        cost_estimate=pl.CostEstimate(
            flops=10 * length * seg_len * HALF,
            bytes_accessed=proj.size * 16,
            transcendentals=length * seg_len * HEADS // 2,
        ),
    )(proj, proj, taps, head, skip, rim, heads, end, prior, values, grad_values)


def shared_kernel(core_ref, proj_ref, rim_ref, taps_ref, b_ref, c_ref, other_ref, grad_ref, taps_grad_ref, edge_ref):
    total, seen = conv_parts(proj_ref[...], rim_ref[...], taps_ref[...])
    sigmoid = jax.nn.sigmoid(total)
    grad_total = jnp.where(core_ref[0] == 0, b_ref[...], c_ref[...]) + other_ref[...]
    grad_total = grad_total * (sigmoid * (1.0 + total * (1.0 - sigmoid)))
    sums = [jnp.sum(grad_total * part, axis=0, keepdims=True) for part in seen]
    sums = sums + [jnp.sum(grad_total, axis=0, keepdims=True), jnp.zeros((8 - CONV - 1, LANES), f32)]
    taps_grad_ref[...] = jnp.concatenate(sums, axis=0)
    edge_ref[...] = grad_total[:8]
    taps = taps_ref[...]
    extended = jnp.concatenate([grad_total, jnp.zeros((8, LANES), f32)], axis=0)
    grad_conv = taps[CONV - 1 : CONV] * grad_total
    for k in range(CONV - 1):
        grad_conv = grad_conv + taps[k : k + 1] * extended[CONV - 1 - k : CONV - 1 - k + grad_total.shape[0]]
    grad_ref[...] = grad_conv.astype(bf16)


def shared_backward(core, proj, rim, taps, grad_b, grad_c, other):
    length = proj.shape[0]
    picked = lambda rows: pl.BlockSpec((rows, LANES), lambda i, core: (0, HALF // LANES + core[0]))
    whole = lambda rows: pl.BlockSpec((rows, LANES), lambda i, core: (0, 0))
    return pl.pallas_call(
        shared_kernel,
        grid_spec=pltpu.PrefetchScalarGridSpec(
            num_scalar_prefetch=1,
            grid=(1,),
            in_specs=[picked(length), picked(8), picked(8), whole(length), whole(length), whole(length)],
            out_specs=(whole(length), whole(8), whole(8)),
        ),
        out_shape=(
            jax.ShapeDtypeStruct((length, LANES), bf16),
            jax.ShapeDtypeStruct((8, LANES), f32),
            jax.ShapeDtypeStruct((8, LANES), f32),
        ),
        compiler_params=pltpu.CompilerParams(vmem_limit_bytes=VMEM_LIMIT),
        cost_estimate=pl.CostEstimate(flops=40 * length * LANES, bytes_accessed=24 * length * LANES, transcendentals=length * LANES),
    )(core.reshape(1).astype(jnp.int32), proj, rim, taps, grad_b, grad_c, other)


def per_device(hidden_in, cotangent, in_proj, out_proj, conv_params, pre_gain, gated_gain, head_params):
    chips, line = lax.axis_size("chip"), lax.axis_size("seg")
    core, place = lax.axis_index("core"), lax.axis_index("seg")
    rows, model_width = in_proj.shape[0], hidden_in.shape[2]
    heads = HEADS // 2

    conv_width, gain_width = conv_params.shape[1], gated_gain.shape[0]
    used = HALF + 2 * STATE + heads
    spare = -used % LANES
    small = jnp.zeros((rows, spare), bf16)
    small = small.at[: CONV + 1, :conv_width].set(conv_params)
    small = small.at[CONV + 1, :rows].set(pre_gain)
    small = small.at[CONV + 2, :gain_width].set(gated_gain)

    def conv_side(which):
        return jnp.concatenate(
            [
                own_columns(in_proj[:, INNER : 2 * INNER], which),
                in_proj[:, 2 * INNER : INNER + XBC],
                own_columns(in_proj[:, INNER + XBC :], which),
                small,
            ],
            axis=1,
        )

    def gate_side(which):
        return own_columns(in_proj[:, :INNER], which)

    conv_swap = to_partner(conv_side(1 - core))
    conv_block = in_core_order(conv_side(core), conv_swap, core, 0)
    conv_z = gather_first(conv_block)
    gate_swap = to_partner(after(gate_side(1 - core), conv_swap))
    gate_block = in_core_order(gate_side(core), gate_swap, core, 0)
    gate_z = gather_first(after(gate_block, conv_z))
    conv_2 = gather_next(conv_z, 1)
    conv_2, gate_z = lax.optimization_barrier((conv_2, gate_z))
    conv_all = gather_next(conv_2, 2)
    hidden_half = whole_sequence(after(hidden_in, gate_z), core, place)
    conv_all, hidden_half = lax.optimization_barrier((conv_all, hidden_half))
    hidden = in_core_order(hidden_half, to_partner(hidden_half), core, 1)
    gate_2 = gather_next(after(gate_z, conv_all), 1)
    out_z = gather_first(after(out_proj, hidden_half))
    conv_all = whole_matrix(conv_all, conv_block, True).reshape(model_width, -1)

    small_all = conv_all.reshape(chips, 2, line, rows, -1)[..., used:].astype(f32)
    taps_full = small_all[..., : CONV + 1, :conv_width].transpose(3, 0, 1, 2, 4).reshape(CONV + 1, XBC)
    taps = jnp.concatenate([own_columns(taps_full[:, :INNER], core), taps_full[:, INNER:]], axis=1)
    gain_pre = small_all[..., CONV + 1, :rows].reshape(model_width)
    gain_gate = lax.dynamic_index_in_dim(
        small_all[..., CONV + 2, :gain_width], core, axis=1, keepdims=False
    ).reshape(HALF)
    params = own_columns(head_params, core)

    seg_len = hidden.shape[1] * hidden.shape[2]
    tokens = SEGS * seg_len
    normed = pre_norm(hidden.reshape(tokens, model_width).astype(f32), gain_pre).astype(bf16)
    projected = dot(normed, conv_all, ((1,), (0,)))
    projected, gate_2, out_z = lax.optimization_barrier((projected, gate_2, out_z))
    gate_all = gather_next(gate_2, 2)
    cot_half = whole_sequence(after(cotangent, out_z), core, place)

    taps = jnp.pad(taps, ((0, 8 - CONV - 1), (0, 0)))
    head = jnp.pad(jnp.stack([-jnp.exp(params[0]), params[1]]), ((0, 6), (0, LANES - heads)))
    skip = jnp.repeat(params[2], HEADDIM).reshape(1, HALF)
    wide = HALF + 2 * STATE
    rim = borrowed(projected[tokens - 8 :, :wide], 1)
    nothing = jnp.zeros((STATE, HALF), f32)
    values, prior, final, last = scan_forward(projected, taps, head, skip, rim, nothing, seg_len)
    if line > SEGS:
        last = jnp.sum(last.reshape(SEGS, 8, LANES)[:, 0, :heads], axis=0)
        decay = jnp.repeat(jnp.exp2(last), HEADDIM)
        begin = entering(decay, final, 1)
        values, prior, _, _ = scan_forward(projected, taps, head, skip, rim, begin, seg_len)

    values, gate_all, cot_half = lax.optimization_barrier((values, gate_all, cot_half))
    out_2 = gather_next(after(out_z, gate_all), 1)
    cot = in_core_order(cot_half, to_partner(cot_half), core, 1)
    upstream = cot.reshape(tokens, model_width)
    gate_matrix = whole_matrix(gate_all, gate_block, True).reshape(model_width, -1)
    gate_input = dot(normed, gate_matrix, ((1,), (0,)))
    gate_input, out_2 = lax.optimization_barrier((gate_input, out_2))
    out_all = gather_next(out_2, 2)

    silu_gate = jax.nn.silu(gate_input)
    gated = values * silu_gate
    squares = jnp.sum(gated * gated, axis=1)
    scale = lax.rsqrt((squares + to_partner(squares)) / INNER + epsilon)[:, None]
    unit = gated * scale
    mixed = (unit * gain_gate).astype(bf16)
    out_grads = weight_grad(mixed, upstream, False)
    out_grads, out_all = lax.optimization_barrier((out_grads, out_all))
    out_first = send_first(out_grads)
    out_matrix = whole_matrix(out_all, out_proj, False).reshape(HALF, model_width)
    grad_mixed = dot(upstream, out_matrix, ((1,), (1,)))
    gain_grad = grad_mixed * gain_gate
    along = jnp.sum(gain_grad * unit, axis=1)
    along_other = to_partner(along)
    branch = dot(mixed, out_matrix, ((1,), (0,)))
    along_other, branch = lax.optimization_barrier((along_other, branch))
    along = ((along + along_other) / INNER)[:, None]
    gate_gain_grad = jnp.sum(grad_mixed * unit, axis=0)
    grad_gated = scale * (gain_grad - unit * along)
    grad_values = grad_gated * silu_gate
    sigmoid = jax.nn.sigmoid(gate_input)
    grad_gate = (grad_gated * values * (sigmoid * (1.0 + gate_input * (1.0 - sigmoid)))).astype(bf16)

    def halves(partial):
        parted = partial.reshape(SEGS, 2, seg_len // 2, model_width)
        mine = lax.dynamic_index_in_dim(parted, core, axis=1, keepdims=False)
        theirs = lax.dynamic_index_in_dim(parted, 1 - core, axis=1, keepdims=False)
        return mine + to_partner(theirs.astype(bf16)).astype(f32)

    branch = halves(branch)
    grad_gate, grad_values, out_first, branch = lax.optimization_barrier((grad_gate, grad_values, out_first, branch))
    out_second = reduce_second(out_first)
    hidden_out = back_to_owner((hidden_half.astype(f32) + branch).astype(bf16), core, place)
    gate_grads = weight_grad(normed, grad_gate, True)
    gate_grads, out_second = lax.optimization_barrier((gate_grads, out_second))
    gate_first = send_first(gate_grads)
    grad_values = after(grad_values, gate_grads)
    back = scan_backward(projected, taps, head, skip, rim, nothing, prior, values, grad_values, seg_len)
    back, gate_first, hidden_out = lax.optimization_barrier((back, gate_first, hidden_out))
    if line > SEGS:
        end = entering(decay, back[-1], -1)
        back = scan_backward(projected, taps, head, skip, rim, end, prior, values, grad_values, seg_len)
    grad_x, grad_b, grad_c, grad_raw, x_taps_grad, skip_grad, head_sums, x_edge, _ = back
    head_grad = jnp.concatenate([head_sums[:2, :heads], skip_grad.reshape(1, heads, HEADDIM).sum(axis=2)])
    gate_second = reduce_second(gate_first)
    out_third = reduce_third(out_second)

    other = to_partner(jnp.where(core == 0, grad_c, grad_b))
    grad_state, state_taps_grad, state_edge = shared_backward(core, projected, rim, taps, grad_b, grad_c, other)
    if line > SEGS:
        edge = borrowed(jnp.concatenate([x_edge, state_edge], axis=1), -1)
        own_taps = jnp.concatenate(
            [taps[:, :HALF], lax.dynamic_slice_in_dim(taps, HALF + core * STATE, STATE, axis=1)], axis=1
        )
        spill = jnp.stack(
            [
                sum(own_taps[k] * edge[CONV - 1 - k - early] for k in range(CONV - early))
                for early in range(CONV - 1, 0, -1)
            ]
        )
        add = lambda array, part: array.at[tokens - CONV + 1 :].set(
            (array[tokens - CONV + 1 :].astype(f32) + part).astype(bf16)
        )
        grad_x, grad_state = add(grad_x, spill[:, :HALF]), add(grad_state, spill[:, HALF:])
    grad_proj = jnp.concatenate([grad_x, grad_state, grad_raw.astype(bf16)], axis=1)
    state_taps_grad = state_taps_grad[: CONV + 1]
    none = jnp.zeros_like(state_taps_grad)
    taps_grad = jnp.concatenate(
        [
            x_taps_grad[: CONV + 1],
            jnp.where(core == 0, state_taps_grad, none),
            jnp.where(core == 0, none, state_taps_grad),
        ],
        axis=1,
    )
    conv_grads = weight_grad(normed, grad_proj, True)
    conv_grads, gate_second, out_third = lax.optimization_barrier((conv_grads, gate_second, out_third))
    conv_first = send_first(conv_grads)
    gate_third = reduce_third(gate_second)

    state_weights = lax.dynamic_slice_in_dim(conv_all, HALF + core * STATE, STATE, axis=1)
    conv_matrix = jnp.concatenate(
        [conv_all[:, :HALF], state_weights, conv_all[:, HALF + 2 * STATE :]], axis=1
    )
    gate_late, proj_late = after((grad_gate, grad_proj), conv_grads)
    grad_normed = halves(
        dot(gate_late, gate_matrix, ((1,), (1,))) + dot(proj_late, conv_matrix, ((1,), (1,)))
    )
    grad_normed, conv_first, gate_third = lax.optimization_barrier((grad_normed, conv_first, gate_third))
    conv_second = reduce_second(conv_first)
    _, pre_pull = jax.vjp(pre_norm, hidden_half.astype(f32), gain_pre)
    grad_hidden, pre_gain_grad = pre_pull(grad_normed)
    grad_in = back_to_owner(
        (cot_half.astype(f32) + grad_hidden).astype(bf16), core, place
    )

    def spread_own(array):
        width = array.shape[-1] // chips
        parted = array.reshape(array.shape[:-1] + (chips, 1, width))
        none = jnp.zeros_like(parted)
        both = jnp.where(
            core == 0,
            jnp.concatenate([parted, none], axis=-2),
            jnp.concatenate([none, parted], axis=-2),
        )
        return both.reshape(array.shape[:-1] + (2 * array.shape[-1],))

    taps_all = jnp.concatenate([spread_own(taps_grad[:, :HALF]), taps_grad[:, HALF:]], axis=1)
    taps_all = taps_all.reshape(CONV + 1, chips, 2, line, conv_width).transpose(1, 3, 2, 0, 4)
    gate_all = spread_own(gate_gain_grad).reshape(chips, 2, line, gain_width).transpose(0, 2, 1, 3)
    head_all = jnp.broadcast_to(spread_own(head_grad).reshape(-1), (chips, line, 2, 3 * HEADS))
    small_grads = jnp.concatenate(
        [
            taps_all.reshape(chips, line, 2, -1),
            pre_gain_grad.reshape(chips, 2, line, rows).transpose(0, 2, 1, 3),
            gate_all,
            head_all,
        ],
        axis=3,
    )
    count = small_grads.shape[3]
    small_grads = small_grads.reshape(chip_dims() + (2, count))
    small_second = reduce_second(reduce_first(small_grads, f32), f32)
    conv_second, small_second = lax.optimization_barrier((conv_second, small_second))
    small_share = reduce_end(reduce_third(small_second, f32))
    conv_third = reduce_third(conv_second)
    out_share = reduce_end(out_third).reshape(-1, model_width)
    gate_share = reduce_end(gate_third).astype(bf16).reshape(2, rows, -1)
    conv_share = reduce_end(conv_third).astype(bf16).reshape(2, rows, -1)

    def mine_and_partner(share):
        keep = lax.dynamic_index_in_dim(share, core, axis=0, keepdims=False)
        give = lax.dynamic_index_in_dim(share, 1 - core, axis=0, keepdims=False)
        return keep, to_partner(give)

    keep, got = mine_and_partner(small_share)
    small_total = keep + got
    taps_end = (CONV + 1) * conv_width
    taps_share = small_total[:taps_end].reshape(CONV + 1, conv_width)
    pre_share = small_total[taps_end : taps_end + rows]
    gain_share = small_total[taps_end + rows : taps_end + rows + gain_width]
    head_total = small_total[taps_end + rows + gain_width :].reshape(3, HEADS)

    def interleave(mine, theirs):
        width = mine.shape[1] // chips
        both = in_core_order(mine.reshape(rows, chips, width), theirs.reshape(rows, chips, width), core, 2)
        return both.reshape(rows, -1)

    keep_gate, got_gate = mine_and_partner(gate_share)
    keep, got = mine_and_partner(conv_share)
    state_end = HALF + STATE
    in_share = jnp.concatenate(
        [
            interleave(keep_gate, got_gate),
            interleave(keep[:, :HALF], got[:, :HALF]),
            in_core_order(keep[:, HALF:state_end], got[:, HALF:state_end], core, 1).reshape(rows, -1),
            interleave(keep[:, state_end : state_end + heads], got[:, state_end : state_end + heads]),
        ],
        axis=1,
    ).astype(f32)
    return (hidden_out, grad_in, in_share, out_share, taps_share, pre_share, gain_share, head_total)


def solution(mesh):
    devices = mesh.devices
    cores = Mesh(devices.reshape(devices.shape[0] // 2, 2, devices.shape[1]), ("chip", "core", "seg"))
    dp, both = ("chip", "core"), ("chip", "core", "seg")
    tokens = P(dp, "seg", None)
    return jax.shard_map(
        per_device,
        mesh=cores,
        in_specs=(tokens, tokens, P(both, None), P(both, None), P(None, both), P(both), P(both), P()),
        out_specs=(tokens, tokens, P(both, None), P(both, None), P(None, both), P(both), P(both), P()),
        check_vma=False,
    )
```

```python
import jax
import jax.numpy as jnp
from jax import lax
from jax.experimental import pallas as pl
from jax.experimental.pallas import tpu as pltpu
from jax.sharding import Mesh
from jax.sharding import PartitionSpec as P

HEADS = 48
HEADDIM = 64
STATE = 128
CONV = 4
INNER = 3072
XBC = 3328
HALF = INNER // 2
LANES = 128
SEGS = 4
VMEM_LIMIT = 48 * 1024 * 1024
LOG2E = 1.4426950408889634

epsilon = 1e-05
f32 = jnp.float32
bf16 = jnp.bfloat16


def own_columns(array, core):
    chips = lax.axis_size("chip")
    width = array.shape[-1] // (2 * chips)
    parted = array.reshape(array.shape[:-1] + (chips, 2, width))
    picked = lax.dynamic_index_in_dim(parted, core, axis=parted.ndim - 2, keepdims=False)
    return picked.reshape(array.shape[:-1] + (chips * width,))


def to_partner(array):
    return lax.ppermute(array, "core", [(0, 1), (1, 0)])


def in_core_order(mine, theirs, core, axis):
    first = jnp.where(core == 0, mine, theirs)
    second = jnp.where(core == 0, theirs, mine)
    return jnp.stack([first, second], axis=axis)


def chip_dims():
    return (lax.axis_size("chip") // 2, 2, lax.axis_size("seg"))


def chip_place():
    chip = lax.axis_index("chip")
    return (chip // 2, chip % 2, lax.axis_index("seg"))


def moved(array, dim, by):
    sizes = chip_dims()
    index = lambda at: (at[0] * sizes[1] + at[1]) * sizes[2] + at[2]
    pairs = []
    for a in range(sizes[0]):
        for b in range(sizes[1]):
            for z in range(sizes[2]):
                to = [a, b, z]
                to[dim] = (to[dim] + by) % sizes[dim]
                pairs.append((index((a, b, z)), index(to)))
    return lax.ppermute(array, ("chip", "seg"), pairs)


def tie(*values):
    return lax.optimization_barrier(values)


ORDERS = ((2, 0, 1), (2, 1, 0))


def column_parts(width):
    cut = -(-(width // 2) // LANES) * LANES
    return ((0, cut), (cut, width))


def gather_step(data, dim):
    return [data] + [moved(data, dim, by) for by in range(1, chip_dims()[dim])]


def gather_first(block):
    pieces = gather_step(block, 2)
    return [[piece[..., begin:end] for piece in pieces] for begin, end in column_parts(block.shape[-1])]


def gather_next(parts, step):
    return [gather_step(jnp.stack(part), order[step]) for order, part in zip(ORDERS, parts)]


def placed_kernel(plan, place_ref, *refs):
    sources, out_ref, sems = refs[:-2], refs[-2], refs[-1]
    copies = []
    for source, lead, at, columns, paired in plan:
        spot = [lax.rem(place_ref[dim] + (size - back), size) for dim, (back, size) in enumerate(at)]
        target = out_ref.at[spot[0], spot[1]]
        target = target.at[:, spot[2]] if paired else target.at[spot[2]]
        target = target.at[..., pl.ds(*columns)]
        copies.append(pltpu.make_async_copy(sources[source].at[lead], target, sems.at[len(copies)]))
    for copy in copies:
        copy.start()
    for copy in copies:
        copy.wait()


def whole_matrix(parts, block, paired):
    sizes = chip_dims()
    plan, sources = [], []
    for order, (begin, end), part in zip(ORDERS, column_parts(block.shape[-1]), parts):
        for back_last, piece in enumerate(part):
            for back_mid in range(sizes[order[1]]):
                for back_first in range(sizes[order[0]]):
                    at = [None] * 3
                    at[order[2]] = (back_last, sizes[order[2]])
                    at[order[1]] = (back_mid, sizes[order[1]])
                    at[order[0]] = (back_first, sizes[order[0]])
                    plan.append((len(sources), (back_mid, back_first), at, (begin, end - begin), paired))
            sources.append(piece)
    if paired:
        shape = sizes[:2] + (2, sizes[2]) + block.shape[1:]
    else:
        shape = sizes + block.shape
    anywhere = pl.BlockSpec(memory_space=pl.ANY)
    return pl.pallas_call(
        lambda *refs: placed_kernel(plan, *refs),
        out_shape=jax.ShapeDtypeStruct(shape, block.dtype),
        in_specs=[pl.BlockSpec(memory_space=pltpu.SMEM)] + [anywhere] * len(sources),
        out_specs=pl.BlockSpec(memory_space=pltpu.VMEM),
        scratch_shapes=[pltpu.SemaphoreType.DMA((len(plan),))],
        compiler_params=pltpu.CompilerParams(vmem_limit_bytes=VMEM_LIMIT),
        cost_estimate=pl.CostEstimate(flops=0, bytes_accessed=4 * block.size * sizes[0] * sizes[1] * sizes[2], transcendentals=0),
    )(jnp.stack(chip_place()).astype(jnp.int32), *sources)


def reduce_send(data, axis, dim, wire):
    place, size = chip_place()[dim], chip_dims()[dim]
    pick = lambda at: lax.dynamic_index_in_dim(data, at, axis=axis, keepdims=False)
    received = [moved(pick((place + by) % size).astype(wire), dim, by) for by in range(1, size)]
    return pick(place).astype(f32), received


def reduce_add(kept, received):
    for part in received:
        kept = kept + part.astype(f32)
    return kept


def reduce_first(partial, wire=bf16):
    (begin, cut), (_, end) = column_parts(partial.shape[-1])
    return [
        reduce_send(partial[..., begin:cut], 1, 1, wire),
        reduce_send(partial[..., cut:end], 0, 0, wire),
    ]


def weight_grad_kernel(
    cut, slabs, place_ref, left_ref, right_ref, keep_b_ref, send_b_ref, keep_a_ref, send_a_ref
):
    turn, last = pl.program_id(0), pl.num_programs(0) - 1
    rows, width = left_ref.shape[0] // 2, right_ref.shape[1]
    left = left_ref[...]
    own_first = place_ref[1] == 0
    begin = 0
    while begin < width:
        end = min(begin + 2 * LANES, cut if begin < cut else width)
        grad = dot(left, right_ref[:, begin:end], ((1,), (0,)))
        if begin < cut:
            mine = jnp.where(own_first, grad[:rows], grad[rows:])
            theirs = jnp.where(own_first, grad[rows:], grad[:rows]).astype(bf16)
            for to, at, size in slabs:
                keep_b_ref[0, to : to + size, begin:end] = mine[at : at + size]
                send_b_ref[0, to : to + size, begin:end] = theirs[at : at + size]
        else:
            columns = slice(begin - cut, end - cut)

            @pl.when(turn == last)
            def _(grad=grad, columns=columns):
                for half in range(2):
                    for to, at, size in slabs:
                        keep_a_ref[half, to : to + size, columns] = grad[half * rows + at : half * rows + at + size]

            @pl.when(turn < last)
            def _(grad=grad, columns=columns):
                for half in range(2):
                    for to, at, size in slabs:
                        part = grad[half * rows + at : half * rows + at + size]
                        send_a_ref[0, half, to : to + size, columns] = part.astype(bf16)

        begin = end


def weight_grad(left, right, paired):
    a, b, z = chip_dims()
    length, width = right.shape
    rows = left.shape[0] // (a * b)
    (_, cut), _ = column_parts(width)
    size = rows // (2 * z)
    inside = paired and size % 16 == 0
    if inside:
        slabs = [((at * 2 + core) * size, (core * z + at) * size, size) for core in range(2) for at in range(z)]
    else:
        slabs = [(0, 0, rows)]
    rest = width - cut
    others = max(a - 1, 1)
    turned = lambda i, place: lax.rem(place[0] + 1 + i, a)
    keep_b, send_b, keep_a, send_a = pl.pallas_call(
        lambda *refs: weight_grad_kernel(cut, slabs, *refs),
        grid_spec=pltpu.PrefetchScalarGridSpec(
            num_scalar_prefetch=1,
            grid=(a,),
            in_specs=[
                pl.BlockSpec((2 * rows, length), lambda i, place: (turned(i, place), 0)),
                pl.BlockSpec((length, width), lambda i, place: (0, 0)),
            ],
            out_specs=(
                pl.BlockSpec((1, rows, cut), lambda i, place: (turned(i, place), 0, 0)),
                pl.BlockSpec((1, rows, cut), lambda i, place: (turned(i, place), 0, 0)),
                pl.BlockSpec((2, rows, rest), lambda i, place: (0, 0, 0)),
                pl.BlockSpec((1, 2, rows, rest), lambda i, place: (jnp.minimum(i, others - 1), 0, 0, 0)),
            ),
        ),
        out_shape=(
            jax.ShapeDtypeStruct((a, rows, cut), f32),
            jax.ShapeDtypeStruct((a, rows, cut), bf16),
            jax.ShapeDtypeStruct((2, rows, rest), f32),
            jax.ShapeDtypeStruct((others, 2, rows, rest), bf16),
        ),
        compiler_params=pltpu.CompilerParams(
            dimension_semantics=("arbitrary",), vmem_limit_bytes=VMEM_LIMIT
        ),
        cost_estimate=pl.CostEstimate(
            flops=2 * left.size * width,
            bytes_accessed=2 * left.size + 2 * right.size + 3 * left.shape[0] * width,
            transcendentals=0,
        ),
    )(jnp.stack(chip_place()[:2]).astype(jnp.int32), left, right)

    def shaped(array):
        lead = array.shape[:-2]
        if inside or not paired:
            return array.reshape(lead + (z, rows // z, array.shape[-1]))
        parted = array.reshape(lead + (2, z, size, array.shape[-1]))
        return jnp.swapaxes(parted, -4, -3).reshape(lead + (z, rows // z, array.shape[-1]))

    return shaped(keep_b), shaped(send_b), shaped(keep_a), shaped(send_a)


def send_first(grads):
    keep_b, send_b, keep_a, send_a = grads
    return [
        (keep_b, [moved(send_b, 1, 1)]),
        (keep_a, [moved(send_a[by - 1], 0, by) for by in range(1, chip_dims()[0])]),
    ]


def reduce_second(first, wire=bf16):
    return [
        reduce_send(reduce_add(*first[0]), 0, 0, wire),
        reduce_send(reduce_add(*first[1]), 0, 1, wire),
    ]


def reduce_third(second, wire=bf16):
    return reduce_send(jnp.concatenate([reduce_add(*part) for part in second], axis=-1), 0, 2, wire)


def reduce_end(third):
    return reduce_add(*third)


def line_perm(turn, back):
    line = lax.axis_size("seg")
    parts = line // SEGS
    pairs = []
    for core in range(2):
        for place in range(line):
            piece = (place % SEGS) ^ turn
            half, index = divmod(piece, 2)
            source = core * line + place
            target = half * line + (2 * core + index) * parts + place // SEGS
            pairs.append((target, source) if back else (source, target))
    return pairs


def whole_sequence(array, core, place):
    parts = lax.axis_size("seg") // SEGS
    half = array.shape[1] // 2
    pieces = array.reshape(2, 2, half, -1).transpose(1, 0, 2, 3).reshape(4, half, -1)
    mine = place % SEGS
    target = 2 * core + (place // parts) % 2
    got = []
    for turn in range(4):
        piece = lax.dynamic_index_in_dim(pieces, mine ^ turn, axis=0, keepdims=False)
        got.append(lax.ppermute(piece, ("core", "seg"), line_perm(turn, False)))
    got = jnp.stack(got)
    return jnp.stack([lax.dynamic_index_in_dim(got, target ^ k, axis=0, keepdims=False) for k in range(4)])


def back_to_owner(ordered, core, place):
    parts = lax.axis_size("seg") // SEGS
    half = ordered.shape[1]
    mine = place % SEGS
    target = 2 * core + (place // parts) % 2
    got = []
    for turn in range(4):
        piece = lax.dynamic_index_in_dim(ordered, target ^ turn, axis=0, keepdims=False)
        got.append(lax.ppermute(piece, ("core", "seg"), line_perm(turn, True)))
    got = jnp.stack(got)
    pieces = jnp.stack([lax.dynamic_index_in_dim(got, mine ^ k, axis=0, keepdims=False) for k in range(4)])
    return pieces.reshape(2, 2, half, -1).transpose(1, 0, 2, 3).reshape(2, 2 * half, -1)


def part_pairs(step):
    line = lax.axis_size("seg")
    parts = line // SEGS
    return [(i, i + step) for i in range(line) if 0 <= i + step < line and i // parts == (i + step) // parts]


def entering(decay, state, step):
    parts = lax.axis_size("seg") // SEGS
    total = jnp.zeros_like(state)
    for _ in range(parts - 1):
        total = lax.ppermute(decay * total + state, "seg", part_pairs(step))
    return total


def borrowed(array, step):
    parts = lax.axis_size("seg") // SEGS
    if parts == 1:
        return jnp.zeros_like(array)
    return lax.ppermute(array, "seg", part_pairs(step))


def spilled(grad, edge, taps):
    if lax.axis_size("seg") == SEGS:
        return grad
    edge = borrowed(edge, -1)
    spill = jnp.stack(
        [
            sum(taps[k] * edge[CONV - 1 - k - early] for k in range(CONV - early))
            for early in range(CONV - 1, 0, -1)
        ]
    )
    at = grad.shape[0] - CONV + 1
    return grad.at[at:].set((grad[at:].astype(f32) + spill).astype(bf16))


def pre_norm(hidden, norm_gain):
    row_scale = lax.rsqrt(jnp.mean(hidden * hidden, axis=-1, keepdims=True) + epsilon)
    return hidden * row_scale * norm_gain


def conv_apply(padded, conv_taps):
    length = padded.shape[0] - CONV + 1
    summed = conv_taps[CONV]
    for offset in range(CONV):
        summed = summed + conv_taps[offset] * padded[offset : offset + length, :]
    return jax.nn.silu(summed)


def head_terms(step_raw, params):
    step_size = jax.nn.softplus(step_raw + params[1])
    decay_sum = jnp.cumsum(step_size * -jnp.exp(params[0]), axis=1)
    return (step_size, decay_sum)


def decay_terms(decay_sum, step_size):
    last_sum = decay_sum[:, -1:, :]
    carry_scale = jnp.exp(last_sum - decay_sum) * step_size
    return (carry_scale, jnp.exp(decay_sum[:, -1, :]), jnp.exp(decay_sum))


def dot(a, b, contract):
    return lax.dot_general(a, b, (contract, ((), ())), preferred_element_type=f32)


def columns_of(pair):
    return pl.ds(pair * LANES, LANES)


def low_half(shape):
    return lax.broadcasted_iota(jnp.int32, shape, len(shape) - 1) < HEADDIM


def pair_columns(array, pair, low):
    rows = array.shape[0]
    first = jnp.broadcast_to(array[:, 2 * pair : 2 * pair + 1], (rows, LANES))
    second = jnp.broadcast_to(array[:, 2 * pair + 1 : 2 * pair + 2], (rows, LANES))
    return jnp.where(low, first, second)


def conv_parts(current, before, taps):
    rows = current.shape[0]
    padded = jnp.concatenate([before, current], axis=0)
    seen = [padded[8 - CONV + 1 + k : 8 - CONV + 1 + k + rows] for k in range(CONV - 1)] + [current]
    total = taps[CONV : CONV + 1]
    for k in range(CONV):
        total = total + taps[k : k + 1] * seen[k]
    return total, seen


def step_terms(raw, head, seg_len):
    shifted = raw + head[1:2]
    step = jnp.maximum(shifted, 0.0) + jnp.log1p(jnp.exp(-jnp.abs(shifted)))
    log_decay = step * head[0:1]
    at_or_before = lax.broadcasted_iota(jnp.int32, (seg_len, seg_len), 0) >= lax.broadcasted_iota(
        jnp.int32, (seg_len, seg_len), 1
    )
    sums = lax.dot_general(
        jnp.where(at_or_before, 1.0, 0.0), log_decay, (((1,), (0,)), ((), ())),
        precision=lax.Precision.HIGHEST, preferred_element_type=f32,
    )
    return shifted, step, log_decay, sums * LOG2E


def forward_kernel(
    proj_ref, taps_ref, head_ref, skip_ref, rim_ref, init_ref,
    values_ref, prior_ref, final_ref, last_ref, state_ref, tail_ref,
):
    seg_len = proj_ref.shape[0]
    half = seg_len // 2

    @pl.when(pl.program_id(0) == 0)
    def _():
        state_ref[...] = init_ref[...]
        tail_ref[...] = rim_ref[...]

    def activated(begin):
        at = pl.ds(begin, LANES)
        total, _ = conv_parts(proj_ref[:, at], tail_ref[:, at], taps_ref[:, at])
        return total * jax.nn.sigmoid(total)

    b_low = activated(HALF).astype(bf16)
    b_turned = activated(HALF).T.astype(bf16)
    c_low = activated(HALF + STATE).astype(bf16)
    _, step, _, sums = step_terms(proj_ref[:, HALF + 2 * STATE :], head_ref, seg_len)
    sums_turned, step_turned = sums.T, step.T
    scores = dot(c_low, b_low, ((1,), (1,)))
    kept = lax.broadcasted_iota(jnp.int32, (half, half), 0) >= lax.broadcasted_iota(jnp.int32, (half, half), 1)
    first_scores = jnp.where(kept, scores[:half, :half], 0.0)
    later_scores = scores[half:, :half]
    second_scores = jnp.where(kept, scores[half:, half:], 0.0)
    low = low_half((seg_len, LANES))
    last_ref[...] = jnp.broadcast_to(sums[seg_len - 1 :], last_ref.shape)

    for pair in range(HEADS // 4):
        at = columns_of(pair)
        x_values = activated(pair * LANES)
        x_low = x_values.astype(bf16)
        sums_pair = pair_columns(sums, pair, low)
        last_pair = sums_pair[seg_len - 1 :]
        carry = jnp.exp2(last_pair - sums_pair) * pair_columns(step, pair, low)
        scaled_x = (carry * x_low.astype(f32)).astype(bf16)
        prior = state_ref[:, at]
        prior_low = prior.astype(bf16)
        prior_ref[0, :, at] = prior_low
        from_state = jnp.exp2(sums_pair) * dot(c_low, prior_low, ((1,), (0,)))
        state_ref[:, at] = jnp.exp2(last_pair) * prior + dot(b_turned, scaled_x, ((1,), (0,)))
        early, late = 0.0, 0.0
        for side in range(2):
            head = 2 * pair + side
            x_side = jnp.where(low if side == 0 else ~low, x_values, 0.0).astype(bf16)
            at_token = jnp.broadcast_to(sums[:, head : head + 1], (seg_len, half))
            at_source, source_step = sums_turned[head : head + 1], step_turned[head : head + 1]
            first = jnp.exp2(jnp.minimum(at_token[:half] - at_source[:, :half], 0.0)) * first_scores
            first = (first * source_step[:, :half]).astype(bf16)
            later = jnp.exp2(at_token[half:] - at_source[:, :half]) * later_scores
            later = (later * source_step[:, :half]).astype(bf16)
            second = jnp.exp2(jnp.minimum(at_token[half:] - at_source[:, half:], 0.0)) * second_scores
            second = (second * source_step[:, half:]).astype(bf16)
            early = early + dot(first, x_side[:half], ((1,), (0,)))
            late = late + dot(jnp.concatenate([later, second], axis=1), x_side, ((1,), (0,)))
        intra = jnp.concatenate([early, late], axis=0)
        values_ref[:, at] = intra + from_state + skip_ref[:, at] * x_values

    tail_ref[...] = proj_ref[seg_len - 8 :, : HALF + 2 * STATE]
    final_ref[...] = state_ref[...]


def full_block(shape):
    return pl.BlockSpec(shape, lambda *_: (0,) * len(shape))


def scan_forward(proj, taps, head, skip, rim, init, seg_len):
    segs = proj.shape[0] // seg_len
    wide = HALF + 2 * STATE
    return pl.pallas_call(
        forward_kernel,
        grid=(segs,),
        out_shape=(
            jax.ShapeDtypeStruct((proj.shape[0], HALF), f32),
            jax.ShapeDtypeStruct((segs, STATE, HALF), bf16),
            jax.ShapeDtypeStruct((STATE, HALF), f32),
            jax.ShapeDtypeStruct((segs * 8, LANES), f32),
        ),
        in_specs=[
            pl.BlockSpec((seg_len, proj.shape[1]), lambda i: (i, 0)),
            full_block((8, wide)),
            full_block((8, LANES)),
            full_block((1, HALF)),
            full_block((8, wide)),
            full_block((STATE, HALF)),
        ],
        out_specs=(
            pl.BlockSpec((seg_len, HALF), lambda i: (i, 0)),
            pl.BlockSpec((1, STATE, HALF), lambda i: (i, 0, 0)),
            full_block((STATE, HALF)),
            pl.BlockSpec((8, LANES), lambda i: (i, 0)),
        ),
        scratch_shapes=[pltpu.VMEM((STATE, HALF), f32), pltpu.VMEM((8, wide), f32)],
        compiler_params=pltpu.CompilerParams(
            dimension_semantics=("arbitrary",), vmem_limit_bytes=VMEM_LIMIT
        ),
        cost_estimate=pl.CostEstimate(
            flops=4 * proj.shape[0] * seg_len * HALF,
            bytes_accessed=proj.size * 8,
            transcendentals=proj.shape[0] * seg_len * HEADS // 2,
        ),
    )(proj, taps, head, skip, rim, init)


def split_dot(array, other):
    high = array.astype(bf16)
    rest = (array - high.astype(f32)).astype(bf16)
    return dot(high, other, ((1,), (0,))) + dot(rest, other, ((1,), (0,)))


def backward_kernel(
    group, proj_ref, before_ref, taps_ref, rim_ref, shared_ref, shared_before_ref, shared_taps_ref, shared_rim_ref,
    head_ref, skip_ref, heads_ref, end_ref, prior_ref, values_ref, grad_ref,
    grad_x_ref, grad_b_ref, grad_c_ref, grad_raw_ref, taps_grad_ref, skip_grad_ref, head_grad_ref, edge_ref, start_ref,
    later_ref, local_ref, scaled_ref, grad_state_ref, inner_ref, source_ref, carry_ref, decay_ref,
):
    seg_len = proj_ref.shape[0]
    half = seg_len // 2
    turn = pl.program_id(0)

    @pl.when(turn == 0)
    def _():
        later_ref[...] = end_ref[...]
        edge_ref[...] = jnp.zeros_like(edge_ref)
        taps_grad_ref[...] = jnp.zeros_like(taps_grad_ref)
        skip_grad_ref[...] = jnp.zeros_like(skip_grad_ref)
        head_grad_ref[...] = jnp.zeros_like(head_grad_ref)

    first_segment = turn == pl.num_programs(0) - 1

    def conv_at(at, current, ahead, taps, rim):
        before = jnp.where(first_segment, rim[:, at], ahead[:, at])
        return conv_parts(current[:, at], before, taps[:, at])

    def activated(begin):
        total, _ = conv_at(pl.ds(begin, LANES), shared_ref, shared_before_ref, shared_taps_ref, shared_rim_ref)
        return total * jax.nn.sigmoid(total)

    b_values = activated(0)
    c_values = activated(STATE)
    b_low, c_low, c_turned = b_values.astype(bf16), c_values.astype(bf16), c_values.T.astype(bf16)
    shifted, step, log_decay, sums = step_terms(shared_ref[:, 2 * STATE :], head_ref, seg_len)
    sums_turned = sums.T
    scores = dot(b_low, c_low, ((1,), (1,)))
    kept = lax.broadcasted_iota(jnp.int32, (half, half), 0) <= lax.broadcasted_iota(jnp.int32, (half, half), 1)
    first_scores = jnp.where(kept, scores[:half, :half], 0.0)
    later_scores = scores[:half, half:]
    second_scores = jnp.where(kept, scores[half:, half:], 0.0)
    low = low_half((seg_len, LANES))
    first_grad, later_grad, second_grad = 0.0, 0.0, 0.0

    pairs = grad_ref.shape[1] // LANES
    for pair in range(pairs):
        at = columns_of(pair)
        total, seen = conv_at(at, proj_ref, before_ref, taps_ref, rim_ref)
        sigmoid = jax.nn.sigmoid(total)
        x_values = total * sigmoid
        x_low = x_values.astype(bf16)
        x_wide = x_low.astype(f32)
        sums_pair = pair_columns(sums, group * pairs + pair, low)
        step_pair = pair_columns(step, group * pairs + pair, low)
        last_pair = sums_pair[seg_len - 1 :]
        gap = jnp.exp2(last_pair - sums_pair)
        scaled_ref[:, at] = (gap * step_pair * x_wide).astype(bf16)
        grad_values = grad_ref[:, at]
        grad_state_ref[:, at] = (grad_values * jnp.exp2(sums_pair)).astype(bf16)
        later = later_ref[:, at]
        later_low = later.astype(bf16)
        local_ref[:, at] = later_low
        prior = prior_ref[0, :, at]
        decay_ref[:, at] = jnp.broadcast_to(
            jnp.sum(later * prior.astype(f32), axis=0, keepdims=True), (8, LANES)
        )
        grad_prior = dot(c_turned, grad_state_ref[:, at], ((1,), (0,)))
        later_ref[:, at] = jnp.exp2(last_pair) * later + grad_prior
        grad_scaled = dot(b_low, later_low, ((1,), (0,)))
        stepped = (step_pair * x_wide).astype(bf16)
        early, late = 0.0, 0.0
        for side in range(2):
            head = 2 * (group * pairs + pair) + side
            grad_low = jnp.where(low if side == 0 else ~low, grad_values, 0.0).astype(bf16)
            at_source = jnp.broadcast_to(sums[:, head : head + 1], (seg_len, half))
            at_token = sums_turned[head : head + 1]
            grad_weights = dot(stepped, grad_low, ((1,), (1,)))
            first = jnp.exp2(jnp.minimum(at_token[:, :half] - at_source[:half], 0.0))
            after = jnp.exp2(at_token[:, half:] - at_source[:half])
            second = jnp.exp2(jnp.minimum(at_token[:, half:] - at_source[half:], 0.0))
            first_grad = first_grad + first * grad_weights[:half, :half]
            later_grad = later_grad + after * grad_weights[:half, half:]
            second_grad = second_grad + second * grad_weights[half:, half:]
            upper = jnp.concatenate([first * first_scores, after * later_scores], axis=1).astype(bf16)
            early = early + dot(upper, grad_low, ((1,), (0,)))
            late = late + dot((second * second_scores).astype(bf16), grad_low[half:], ((1,), (0,)))
        inner = jnp.concatenate([early, late], axis=0)
        skip = skip_ref[:, at]
        skip_grad_ref[:, at] += jnp.sum(grad_values * x_values, axis=0, keepdims=True)
        inner_ref[:, at] = grad_values * (values_ref[:, at] - skip * x_values)
        source_ref[:, at] = x_wide * inner
        carry_ref[:, at] = x_wide * grad_scaled
        grad_x = skip * grad_values + step_pair * (inner + gap * grad_scaled)
        grad_total = grad_x * (sigmoid * (1.0 + total * (1.0 - sigmoid)))
        for k in range(CONV):
            taps_grad_ref[k : k + 1, at] += jnp.sum(grad_total * seen[k], axis=0, keepdims=True)
        taps_grad_ref[CONV : CONV + 1, at] += jnp.sum(grad_total, axis=0, keepdims=True)
        extended = jnp.concatenate([grad_total, edge_ref[:, at]], axis=0)
        edge_ref[:, at] = grad_total[:8]
        taps = taps_ref[:, at]
        grad_conv = taps[CONV - 1 : CONV] * grad_total
        for k in range(CONV - 1):
            grad_conv = grad_conv + taps[k : k + 1] * extended[CONV - 1 - k : CONV - 1 - k + seg_len]
        grad_x_ref[:, at] = grad_conv.astype(bf16)

    heads = heads_ref[...]
    tail = jnp.exp2(sums[seg_len - 1 :] - sums)
    source_grad = split_dot(source_ref[...], heads)
    step_grad = source_grad + tail * split_dot(carry_ref[...], heads)
    used = step * step_grad
    sum_grad = split_dot(inner_ref[...], heads) - used
    at_last = jnp.sum(used - step * source_grad, axis=0, keepdims=True)
    at_last = at_last + split_dot(decay_ref[...], heads)[:1] * jnp.exp2(sums[seg_len - 1 :])
    is_last = lax.broadcasted_iota(jnp.int32, (seg_len, LANES), 0) == seg_len - 1
    sum_grad = sum_grad + jnp.where(is_last, at_last, 0.0)
    at_or_after = lax.broadcasted_iota(jnp.int32, (seg_len, seg_len), 0) <= lax.broadcasted_iota(
        jnp.int32, (seg_len, seg_len), 1
    )
    log_grad = lax.dot_general(
        jnp.where(at_or_after, 1.0, 0.0), sum_grad, (((1,), (0,)), ((), ())),
        precision=lax.Precision.HIGHEST, preferred_element_type=f32,
    )
    grad_raw = (step_grad + head_ref[0:1] * log_grad) * jax.nn.sigmoid(shifted)
    grad_raw_ref[...] = grad_raw
    head_grad_ref[0:1] += jnp.sum(log_grad * log_decay, axis=0, keepdims=True)
    head_grad_ref[1:2] += jnp.sum(grad_raw, axis=0, keepdims=True)

    first_low = jnp.where(kept, first_grad, 0.0)
    second_low = jnp.where(kept, second_grad, 0.0)
    grad_scores = jnp.concatenate(
        [
            jnp.concatenate([first_low, later_grad], axis=1),
            jnp.concatenate([jnp.zeros_like(first_low), second_low], axis=1),
        ],
        axis=0,
    )
    start_ref[...] = later_ref[...]
    grad_b_ref[...] = dot(scaled_ref[...], local_ref[...], ((1,), (1,))) + dot(
        grad_scores.astype(bf16), c_low, ((1,), (0,))
    )
    grad_c_ref[...] = dot(grad_state_ref[...], prior_ref[0], ((1,), (1,))) + dot(
        grad_scores.T.astype(bf16), b_low, ((1,), (0,))
    )


GROUPS = 2


def scan_backward(group, proj, taps, head, skip, rim, end, prior, values, grad_values, seg_len):
    length = proj.shape[0]
    segs = length // seg_len
    width, shared = HALF // GROUPS, proj.shape[1] - HALF
    channel = lax.broadcasted_iota(jnp.int32, (width, LANES), 0) // HEADDIM + group * width // HEADDIM
    heads = (channel == lax.broadcasted_iota(jnp.int32, (width, LANES), 1)).astype(bf16)
    back = lambda width, at=0: pl.BlockSpec((seg_len, width), lambda i: (segs - 1 - i, at))
    row_ahead = lambda i: jnp.maximum((segs - 1 - i) * (seg_len // 8) - 1, 0)
    ahead = lambda width, at: pl.BlockSpec((8, width), lambda i: (row_ahead(i), at))
    column = lambda rows, width, at: pl.BlockSpec((rows, width), lambda i: (0, at))
    both = HALF // shared
    taps, rim = jnp.pad(taps, ((0, 0), (0, shared - 2 * STATE))), jnp.pad(rim, ((0, 0), (0, shared - 2 * STATE)))
    return pl.pallas_call(
        lambda *refs: backward_kernel(group, *refs),
        grid=(segs,),
        out_shape=(
            jax.ShapeDtypeStruct((length, width), bf16),
            jax.ShapeDtypeStruct((length, STATE), f32),
            jax.ShapeDtypeStruct((length, STATE), f32),
            jax.ShapeDtypeStruct((length, LANES), f32),
            jax.ShapeDtypeStruct((8, width), f32),
            jax.ShapeDtypeStruct((1, width), f32),
            jax.ShapeDtypeStruct((8, LANES), f32),
            jax.ShapeDtypeStruct((8, width), f32),
            jax.ShapeDtypeStruct((STATE, width), f32),
        ),
        in_specs=[
            back(width, group),
            ahead(width, group),
            column(8, width, group),
            column(8, width, group),
            back(shared, both),
            ahead(shared, both),
            column(8, shared, both),
            column(8, shared, both),
            full_block((8, LANES)),
            column(1, width, group),
            full_block((width, LANES)),
            column(STATE, width, group),
            pl.BlockSpec((1, STATE, width), lambda i: (segs - 1 - i, 0, group)),
            back(width, group),
            back(width, group),
        ],
        out_specs=(
            back(width),
            back(STATE),
            back(STATE),
            back(LANES),
            full_block((8, width)),
            full_block((1, width)),
            full_block((8, LANES)),
            full_block((8, width)),
            full_block((STATE, width)),
        ),
        scratch_shapes=[
            pltpu.VMEM((STATE, width), f32),
            pltpu.VMEM((STATE, width), bf16),
            pltpu.VMEM((seg_len, width), bf16),
            pltpu.VMEM((seg_len, width), bf16),
            pltpu.VMEM((seg_len, width), f32),
            pltpu.VMEM((seg_len, width), f32),
            pltpu.VMEM((seg_len, width), f32),
            pltpu.VMEM((8, width), f32),
        ],
        compiler_params=pltpu.CompilerParams(
            dimension_semantics=("arbitrary",), vmem_limit_bytes=VMEM_LIMIT
        ),
        cost_estimate=pl.CostEstimate(
            flops=10 * length * seg_len * width,
            bytes_accessed=proj.size * 8,
            transcendentals=length * seg_len * HEADS // 4,
        ),
    )(proj, proj, taps, rim, proj, proj, taps, rim, head, skip, heads, end, prior, values, grad_values)


def half_kernel(transposed, count, core_ref, *refs):
    inputs, mine_ref, theirs_ref = refs[: 2 * count], refs[2 * count], refs[2 * count + 1]
    total = 0.0
    for left, right in zip(inputs[:count], inputs[count:]):
        total = total + dot(left[...], right[...], ((1,), (1 if transposed else 0,)))
    half = total.shape[0] // 2
    first = core_ref[0] == 0
    mine_ref[0] = jnp.where(first, total[:half], total[half:])
    theirs_ref[0] = jnp.where(first, total[half:], total[:half]).astype(bf16)


def half_products(core, terms, seg_len, width, transposed):
    length = terms[0][0].shape[0]
    left = [pl.BlockSpec((seg_len, array.shape[1]), lambda i, core: (i, 0)) for array, _, _ in terms]
    right = []
    for array, matrix, at in terms:
        if transposed:
            right.append(pl.BlockSpec((width, array.shape[1]), lambda i, core, at=at: (0, at(core[0]))))
        else:
            right.append(pl.BlockSpec(matrix.shape, lambda i, core: (0, 0)))
    depth = sum(array.shape[1] for array, _, _ in terms)
    mine, theirs = pl.pallas_call(
        lambda *refs: half_kernel(transposed, len(terms), *refs),
        grid_spec=pltpu.PrefetchScalarGridSpec(
            num_scalar_prefetch=1,
            grid=(length // seg_len,),
            in_specs=left + right,
            out_specs=[pl.BlockSpec((1, seg_len // 2, width), lambda i, core: (i, 0, 0))] * 2,
        ),
        out_shape=(
            jax.ShapeDtypeStruct((length // seg_len, seg_len // 2, width), f32),
            jax.ShapeDtypeStruct((length // seg_len, seg_len // 2, width), bf16),
        ),
        compiler_params=pltpu.CompilerParams(dimension_semantics=("arbitrary",), vmem_limit_bytes=VMEM_LIMIT),
        cost_estimate=pl.CostEstimate(
            flops=2 * length * depth * width, bytes_accessed=2 * depth * (length + width) + 3 * length * width, transcendentals=0
        ),
    )(core.reshape(1).astype(jnp.int32), *[array for array, _, _ in terms], *[matrix for _, matrix, _ in terms])
    return mine, to_partner(theirs)


def shared_kernel(core_ref, proj_ref, rim_ref, taps_ref, b_ref, c_ref, other_ref, grad_ref, taps_grad_ref, edge_ref):
    total, seen = conv_parts(proj_ref[...], rim_ref[...], taps_ref[...])
    sigmoid = jax.nn.sigmoid(total)
    grad_total = jnp.where(core_ref[0] == 0, b_ref[...], c_ref[...]) + other_ref[...]
    grad_total = grad_total * (sigmoid * (1.0 + total * (1.0 - sigmoid)))
    sums = [jnp.sum(grad_total * part, axis=0, keepdims=True) for part in seen]
    sums = sums + [jnp.sum(grad_total, axis=0, keepdims=True), jnp.zeros((8 - CONV - 1, LANES), f32)]
    taps_grad_ref[...] = jnp.concatenate(sums, axis=0)
    edge_ref[...] = grad_total[:8]
    taps = taps_ref[...]
    extended = jnp.concatenate([grad_total, jnp.zeros((8, LANES), f32)], axis=0)
    grad_conv = taps[CONV - 1 : CONV] * grad_total
    for k in range(CONV - 1):
        grad_conv = grad_conv + taps[k : k + 1] * extended[CONV - 1 - k : CONV - 1 - k + grad_total.shape[0]]
    grad_ref[...] = grad_conv.astype(bf16)


def shared_backward(core, proj, rim, taps, grad_b, grad_c, other):
    length = proj.shape[0]
    picked = lambda rows: pl.BlockSpec((rows, LANES), lambda i, core: (0, HALF // LANES + core[0]))
    whole = lambda rows: pl.BlockSpec((rows, LANES), lambda i, core: (0, 0))
    return pl.pallas_call(
        shared_kernel,
        grid_spec=pltpu.PrefetchScalarGridSpec(
            num_scalar_prefetch=1,
            grid=(1,),
            in_specs=[picked(length), picked(8), picked(8), whole(length), whole(length), whole(length)],
            out_specs=(whole(length), whole(8), whole(8)),
        ),
        out_shape=(
            jax.ShapeDtypeStruct((length, LANES), bf16),
            jax.ShapeDtypeStruct((8, LANES), f32),
            jax.ShapeDtypeStruct((8, LANES), f32),
        ),
        compiler_params=pltpu.CompilerParams(vmem_limit_bytes=VMEM_LIMIT),
        cost_estimate=pl.CostEstimate(flops=40 * length * LANES, bytes_accessed=24 * length * LANES, transcendentals=length * LANES),
    )(core.reshape(1).astype(jnp.int32), proj, rim, taps, grad_b, grad_c, other)


def per_device(hidden_in, cotangent, in_proj, out_proj, conv_params, pre_gain, gated_gain, head_params):
    chips, line = lax.axis_size("chip"), lax.axis_size("seg")
    core, place = lax.axis_index("core"), lax.axis_index("seg")
    rows, model_width = in_proj.shape[0], hidden_in.shape[2]
    heads = HEADS // 2

    conv_width, gain_width = conv_params.shape[1], gated_gain.shape[0]
    used = HALF + 2 * STATE + heads
    spare = -used % LANES
    small = jnp.zeros((rows, spare), bf16)
    small = small.at[: CONV + 1, :conv_width].set(conv_params)
    small = small.at[CONV + 1, :rows].set(pre_gain)
    small = small.at[CONV + 2, :gain_width].set(gated_gain)

    def conv_side(which):
        return jnp.concatenate(
            [
                own_columns(in_proj[:, INNER : 2 * INNER], which),
                in_proj[:, 2 * INNER : INNER + XBC],
                own_columns(in_proj[:, INNER + XBC :], which),
                small,
            ],
            axis=1,
        )

    def gate_side(which):
        return own_columns(in_proj[:, :INNER], which)

    conv_swap = to_partner(conv_side(1 - core))
    conv_block = in_core_order(conv_side(core), conv_swap, core, 0)
    conv_z = gather_first(conv_block)
    gate_swap = to_partner(gate_side(1 - core))
    gate_block = in_core_order(gate_side(core), gate_swap, core, 0)
    gate_block, conv_z = tie(gate_block, conv_z)
    gate_z = gather_first(gate_block)
    conv_2 = gather_next(conv_z, 1)
    conv_2, gate_z, hidden_in = tie(conv_2, gate_z, hidden_in)
    conv_all = gather_next(conv_2, 2)
    hidden_half = whole_sequence(hidden_in, core, place)
    conv_all, hidden_half, gate_z, out_proj = tie(conv_all, hidden_half, gate_z, out_proj)
    hidden = in_core_order(hidden_half, to_partner(hidden_half), core, 1)
    gate_2 = gather_next(gate_z, 1)
    out_z = gather_first(out_proj)
    conv_all = whole_matrix(conv_all, conv_block, True).reshape(model_width, -1)

    small_all = conv_all.reshape(chips, 2, line, rows, -1)[..., used:].astype(f32)
    taps_full = small_all[..., : CONV + 1, :conv_width].transpose(3, 0, 1, 2, 4).reshape(CONV + 1, XBC)
    taps = jnp.concatenate([own_columns(taps_full[:, :INNER], core), taps_full[:, INNER:]], axis=1)
    gain_pre = small_all[..., CONV + 1, :rows].reshape(model_width)
    gain_gate = lax.dynamic_index_in_dim(
        small_all[..., CONV + 2, :gain_width], core, axis=1, keepdims=False
    ).reshape(HALF)
    params = own_columns(head_params, core)

    seg_len = hidden.shape[1] * hidden.shape[2]
    tokens = SEGS * seg_len
    normed = pre_norm(hidden.reshape(tokens, model_width).astype(f32), gain_pre).astype(bf16)
    normed, gate_2 = tie(normed, gate_2)
    gate_all = gather_next(gate_2, 2)
    normed_turned = normed.T
    projected = dot(normed, conv_all, ((1,), (0,)))
    projected, out_z, cotangent = tie(projected, out_z, cotangent)
    out_2 = gather_next(out_z, 1)
    cot_half = whole_sequence(cotangent, core, place)

    taps = jnp.pad(taps, ((0, 8 - CONV - 1), (0, 0)))
    head = jnp.pad(jnp.stack([-jnp.exp(params[0]), params[1]]), ((0, 6), (0, LANES - heads)))
    skip = jnp.repeat(params[2], HEADDIM).reshape(1, HALF)
    wide = HALF + 2 * STATE
    rim = borrowed(projected[tokens - 8 :, :wide], 1)
    nothing = jnp.zeros((STATE, HALF), f32)
    values, prior, final, last = scan_forward(projected, taps, head, skip, rim, nothing, seg_len)
    if line > SEGS:
        last = jnp.sum(last.reshape(SEGS, 8, LANES)[:, 0, :heads], axis=0)
        decay = jnp.repeat(jnp.exp2(last), HEADDIM)
        begin = entering(decay, final, 1)
        values, prior, _, _ = scan_forward(projected, taps, head, skip, rim, begin, seg_len)

    values, gate_all, out_2 = tie(values, gate_all, out_2)
    out_all = gather_next(out_2, 2)
    cot = in_core_order(cot_half, to_partner(cot_half), core, 1)
    upstream = cot.reshape(tokens, model_width)
    gate_matrix = whole_matrix(gate_all, gate_block, True).reshape(model_width, -1)
    gate_input = dot(normed, gate_matrix, ((1,), (0,)))

    silu_gate = jax.nn.silu(gate_input)
    gated = values * silu_gate
    squares = jnp.sum(gated * gated, axis=1)
    scale = lax.rsqrt((squares + to_partner(squares)) / INNER + epsilon)[:, None]
    unit = gated * scale
    mixed = (unit * gain_gate).astype(bf16)
    out_grads = weight_grad(mixed.T, upstream, False)
    out_grads, out_all = tie(out_grads, out_all)
    out_first = send_first(out_grads)
    out_matrix = whole_matrix(out_all, out_proj, False).reshape(HALF, model_width)
    grad_mixed = dot(upstream, out_matrix, ((1,), (1,)))
    gain_grad = grad_mixed * gain_gate
    along = jnp.sum(gain_grad * unit, axis=1)
    along_other = to_partner(along)
    branch, branch_other = half_products(core, [(mixed, out_matrix, None)], seg_len, model_width, False)
    along_other, branch, mixed = tie(along_other, branch, mixed)
    along = ((along + along_other) / INNER)[:, None]
    gate_gain_grad = jnp.sum(grad_mixed * unit, axis=0)
    grad_gated = scale * (gain_grad - unit * along)
    grad_values = grad_gated * silu_gate
    sigmoid = jax.nn.sigmoid(gate_input)
    grad_gate = (grad_gated * values * (sigmoid * (1.0 + gate_input * (1.0 - sigmoid)))).astype(bf16)
    grad_gate, grad_values, out_first, branch_other = tie(grad_gate, grad_values, out_first, branch_other)
    out_second = reduce_second(out_first)
    hidden_out = back_to_owner(
        (hidden_half.astype(f32) + branch + branch_other.astype(f32)).astype(bf16), core, place
    )
    gate_grads = weight_grad(normed_turned, grad_gate, True)
    gate_grads, out_second, grad_values = tie(gate_grads, out_second, grad_values)
    gate_first = send_first(gate_grads)
    scan = lambda group, later: scan_backward(
        group, projected, taps, head, skip, rim, later, prior, values, grad_values, seg_len
    )
    if line > SEGS:
        later = jnp.concatenate([scan(group, nothing)[-1] for group in range(GROUPS)], axis=1)
        nothing = entering(decay, later, -1)
    back_a = scan(0, nothing)
    back_a, gate_first, hidden_out, grad_values = tie(back_a, gate_first, hidden_out, grad_values)
    gate_second = reduce_second(gate_first)
    out_third = reduce_third(out_second)
    grad_x_a = spilled(back_a[0], back_a[7], taps[:, : HALF // 2])
    x_grads_a = weight_grad(normed_turned, grad_x_a, True)
    x_first_a = send_first(x_grads_a)
    x_grads_a, grad_values = tie(x_grads_a, grad_values)
    back_b = scan(1, nothing)
    back_b, gate_second, out_third, x_first_a = tie(back_b, gate_second, out_third, x_first_a)
    grad_b, grad_c, grad_raw, head_sums = (one + two for one, two in zip(back_a[1:4] + back_a[6:7], back_b[1:4] + back_b[6:7]))
    x_taps_grad, skip_grad = (jnp.concatenate([back_a[at], back_b[at]], axis=1) for at in (4, 5))
    head_grad = jnp.concatenate([head_sums[:2, :heads], skip_grad.reshape(1, heads, HEADDIM).sum(axis=2)])
    x_second_a = reduce_second(x_first_a)
    gate_third = reduce_third(gate_second)

    other = to_partner(jnp.where(core == 0, grad_c, grad_b))
    grad_state, state_taps_grad, state_edge = shared_backward(core, projected, rim, taps, grad_b, grad_c, other)
    grad_state = spilled(grad_state, state_edge, lax.dynamic_slice_in_dim(taps, HALF + core * STATE, STATE, axis=1))
    grad_x_b = spilled(back_b[0], back_b[7], taps[:, HALF // 2 : HALF])
    x_grads_b = weight_grad(normed_turned, grad_x_b, True)
    x_first_b = send_first(x_grads_b)
    grad_raw = grad_raw.astype(bf16)
    grad_rest = jnp.concatenate([grad_state, grad_raw], axis=1)
    rest_grads = weight_grad(normed_turned, grad_rest, True)
    rest_first = send_first(rest_grads)
    state_taps_grad = state_taps_grad[: CONV + 1]
    none = jnp.zeros_like(state_taps_grad)
    taps_grad = jnp.concatenate(
        [
            x_taps_grad[: CONV + 1],
            jnp.where(core == 0, state_taps_grad, none),
            jnp.where(core == 0, none, state_taps_grad),
        ],
        axis=1,
    )
    rest_grads, x_grads_b, grad_gate, x_second_a = tie(rest_grads, x_grads_b, grad_gate, x_second_a)
    x_third_a = reduce_third(x_second_a)
    terms = [
        (grad_gate, gate_matrix, lambda core: 0),
        (grad_x_a, conv_all, lambda core: 0),
        (grad_x_b, conv_all, lambda core: 1),
        (grad_state, conv_all, lambda core: HALF // LANES + core),
        (grad_raw, conv_all, lambda core: (HALF + 2 * STATE) // LANES),
    ]
    grad_normed, other_normed = half_products(core, terms, seg_len, model_width, True)
    grad_normed, x_first_b, rest_first, gate_third = tie(grad_normed, x_first_b, rest_first, gate_third)
    x_second_b, rest_second = reduce_second(x_first_b), reduce_second(rest_first)
    _, pre_pull = jax.vjp(pre_norm, hidden_half.astype(f32), gain_pre)
    grad_hidden, pre_gain_grad = pre_pull(grad_normed + other_normed.astype(f32))
    grad_in = back_to_owner((cot_half.astype(f32) + grad_hidden).astype(bf16), core, place)

    def spread_own(array):
        width = array.shape[-1] // chips
        parted = array.reshape(array.shape[:-1] + (chips, 1, width))
        none = jnp.zeros_like(parted)
        both = jnp.where(
            core == 0,
            jnp.concatenate([parted, none], axis=-2),
            jnp.concatenate([none, parted], axis=-2),
        )
        return both.reshape(array.shape[:-1] + (2 * array.shape[-1],))

    taps_all = jnp.concatenate([spread_own(taps_grad[:, :HALF]), taps_grad[:, HALF:]], axis=1)
    taps_all = taps_all.reshape(CONV + 1, chips, 2, line, conv_width).transpose(1, 3, 2, 0, 4)
    gate_all = spread_own(gate_gain_grad).reshape(chips, 2, line, gain_width).transpose(0, 2, 1, 3)
    head_all = jnp.broadcast_to(spread_own(head_grad).reshape(-1), (chips, line, 2, 3 * HEADS))
    small_grads = jnp.concatenate(
        [
            taps_all.reshape(chips, line, 2, -1),
            pre_gain_grad.reshape(chips, 2, line, rows).transpose(0, 2, 1, 3),
            gate_all,
            head_all,
        ],
        axis=3,
    )
    count = small_grads.shape[3]
    small_grads = small_grads.reshape(chip_dims() + (2, count))
    small_second = reduce_second(reduce_first(small_grads, f32), f32)
    x_second_b, rest_second, small_second, x_third_a, grad_in = tie(
        x_second_b, rest_second, small_second, x_third_a, grad_in
    )
    small_share = reduce_end(reduce_third(small_second, f32))
    late_third = reduce_third(
        [(jnp.concatenate([reduce_add(*part) for part in x_second_b], axis=-1), []), (jnp.concatenate([reduce_add(*part) for part in rest_second], axis=-1), [])]
    )
    out_share = reduce_end(out_third).reshape(-1, model_width)
    paired = lambda third: reduce_end(third).astype(bf16).reshape(2, rows, -1)
    gate_share = paired(gate_third)
    x_share_a, late_share = paired(x_third_a), paired(late_third)

    def mine_and_partner(share):
        keep = lax.dynamic_index_in_dim(share, core, axis=0, keepdims=False)
        give = lax.dynamic_index_in_dim(share, 1 - core, axis=0, keepdims=False)
        return keep, to_partner(give)

    keep, got = mine_and_partner(small_share)
    small_total = keep + got
    taps_end = (CONV + 1) * conv_width
    taps_share = small_total[:taps_end].reshape(CONV + 1, conv_width)
    pre_share = small_total[taps_end : taps_end + rows]
    gain_share = small_total[taps_end + rows : taps_end + rows + gain_width]
    head_total = small_total[taps_end + rows + gain_width :].reshape(3, HEADS)

    def interleave(mine, theirs):
        width = mine.shape[1] // chips
        both = in_core_order(mine.reshape(rows, chips, width), theirs.reshape(rows, chips, width), core, 2)
        return both.reshape(rows, -1)

    keep_gate, got_gate = mine_and_partner(gate_share)
    keep_a, got_a = mine_and_partner(x_share_a)
    keep_b, got_b = mine_and_partner(late_share)
    keep, got = jnp.concatenate([keep_a, keep_b], axis=1), jnp.concatenate([got_a, got_b], axis=1)
    state_end = HALF + STATE
    in_share = jnp.concatenate(
        [
            interleave(keep_gate, got_gate),
            interleave(keep[:, :HALF], got[:, :HALF]),
            in_core_order(keep[:, HALF:state_end], got[:, HALF:state_end], core, 1).reshape(rows, -1),
            interleave(keep[:, state_end : state_end + heads], got[:, state_end : state_end + heads]),
        ],
        axis=1,
    ).astype(f32)
    return (hidden_out, grad_in, in_share, out_share, taps_share, pre_share, gain_share, head_total)


def solution(mesh):
    devices = mesh.devices
    cores = Mesh(devices.reshape(devices.shape[0] // 2, 2, devices.shape[1]), ("chip", "core", "seg"))
    dp, both = ("chip", "core"), ("chip", "core", "seg")
    tokens = P(dp, "seg", None)
    return jax.shard_map(
        per_device,
        mesh=cores,
        in_specs=(tokens, tokens, P(both, None), P(both, None), P(None, both), P(both), P(both), P()),
        out_specs=(tokens, tokens, P(both, None), P(both, None), P(None, both), P(both), P(both), P()),
        check_vma=False,
    )
```

```python
import jax
import jax.numpy as jnp
from jax import lax
from jax.experimental import pallas as pl
from jax.experimental.pallas import tpu as pltpu
from jax.sharding import Mesh
from jax.sharding import PartitionSpec as P

HEADS = 48
HEADDIM = 64
STATE = 128
CONV = 4
INNER = 3072
XBC = 3328
HALF = INNER // 2
LANES = 128
SEGS = 4
LIGHT = pl.CostEstimate(flops=1024, bytes_accessed=1024, transcendentals=0)
VMEM_LIMIT = 48 * 1024 * 1024
LOG2E = 1.4426950408889634

epsilon = 1e-05
f32 = jnp.float32
bf16 = jnp.bfloat16


def own_columns(array, core):
    chips = lax.axis_size("chip")
    width = array.shape[-1] // (2 * chips)
    parted = array.reshape(array.shape[:-1] + (chips, 2, width))
    picked = lax.dynamic_index_in_dim(parted, core, axis=parted.ndim - 2, keepdims=False)
    return picked.reshape(array.shape[:-1] + (chips * width,))


def to_partner(array):
    return lax.ppermute(array, "core", [(0, 1), (1, 0)])


def in_core_order(mine, theirs, core, axis):
    first = jnp.where(core == 0, mine, theirs)
    second = jnp.where(core == 0, theirs, mine)
    return jnp.stack([first, second], axis=axis)


def chip_dims():
    return (lax.axis_size("chip") // 2, 2, lax.axis_size("seg"))


def chip_place():
    chip = lax.axis_index("chip")
    return (chip // 2, chip % 2, lax.axis_index("seg"))


def moved(array, dim, by):
    sizes = chip_dims()
    index = lambda at: (at[0] * sizes[1] + at[1]) * sizes[2] + at[2]
    pairs = []
    for a in range(sizes[0]):
        for b in range(sizes[1]):
            for z in range(sizes[2]):
                to = [a, b, z]
                to[dim] = (to[dim] + by) % sizes[dim]
                pairs.append((index((a, b, z)), index(to)))
    return lax.ppermute(array, ("chip", "seg"), pairs)


def tie(*values):
    return lax.optimization_barrier(values)


ORDERS = ((2, 0, 1), (2, 1, 0))


def column_parts(width):
    cut = -(-(width // 2) // LANES) * LANES
    return ((0, cut), (cut, width))


def gather_step(data, dim):
    return [data] + [moved(data, dim, by) for by in range(1, chip_dims()[dim])]


def gather_first(block):
    pieces = gather_step(block, 2)
    return [[piece[..., begin:end] for piece in pieces] for begin, end in column_parts(block.shape[-1])]


def gather_next(parts, step):
    return [gather_step(jnp.stack(part), order[step]) for order, part in zip(ORDERS, parts)]


def placed_kernel(plan, outs, place_ref, *refs):
    sources, targets, sems = refs[: -outs - 1], refs[-outs - 1 : -1], refs[-1]
    copies = []
    for source, lead, at, columns, paired, out in plan:
        spot = [lax.rem(place_ref[dim] + (size - back), size) for dim, (back, size) in enumerate(at)]
        target = targets[out].at[spot[0], spot[1]]
        target = target.at[:, spot[2]] if paired else target.at[spot[2]]
        target = target.at[..., pl.ds(*columns)]
        copies.append(pltpu.make_async_copy(sources[source].at[lead], target, sems.at[len(copies)]))
    for copy in copies:
        copy.start()
    for copy in copies:
        copy.wait()


def whole_matrices(jobs):
    sizes = chip_dims()
    plan, sources, shapes = [], [], []
    for out, (shape, paired, parts) in enumerate(jobs):
        for order, (begin, end), part in parts:
            for back_last, piece in enumerate(part):
                for back_mid in range(sizes[order[1]]):
                    for back_first in range(sizes[order[0]]):
                        at = [None] * 3
                        at[order[2]] = (back_last, sizes[order[2]])
                        at[order[1]] = (back_mid, sizes[order[1]])
                        at[order[0]] = (back_first, sizes[order[0]])
                        plan.append((len(sources), (back_mid, back_first), at, (begin, end - begin), paired, out))
                sources.append(piece.reshape(piece.shape[:2] + shape[:-1] + piece.shape[-1:]))
        shapes.append(sizes[:2] + (2, sizes[2]) + shape[1:] if paired else sizes + shape)
    anywhere = pl.BlockSpec(memory_space=pl.ANY)
    total = sum(source.size for source in sources)
    return pl.pallas_call(
        lambda *refs: placed_kernel(plan, len(jobs), *refs),
        out_shape=[jax.ShapeDtypeStruct(shape, bf16) for shape in shapes],
        in_specs=[pl.BlockSpec(memory_space=pltpu.SMEM)] + [anywhere] * len(sources),
        out_specs=[pl.BlockSpec(memory_space=pltpu.VMEM)] * len(jobs),
        scratch_shapes=[pltpu.SemaphoreType.DMA((len(plan),))],
        compiler_params=pltpu.CompilerParams(vmem_limit_bytes=VMEM_LIMIT),
        cost_estimate=LIGHT,
    )(jnp.stack(chip_place()).astype(jnp.int32), *sources)


def total(terms):
    result = terms[0].astype(f32)
    for term in terms[1:]:
        result = result + term.astype(f32)
    return result


def reduce_send(terms, axis, dim, wire):
    place, size = chip_place()[dim], chip_dims()[dim]
    pick = lambda at: [lax.dynamic_index_in_dim(term, at, axis=axis, keepdims=False) for term in terms]
    received = [moved(total(pick((place + by) % size)).astype(wire), dim, by) for by in range(1, size)]
    return pick(place), received


def reduce_first(partial, wire=bf16):
    (begin, cut), (_, end) = column_parts(partial.shape[-1])
    return [
        reduce_send([partial[..., begin:cut]], 1, 1, wire),
        reduce_send([partial[..., cut:end]], 0, 0, wire),
    ]


def reduce_second(first, wire=bf16):
    return [
        reduce_send(first[0][0] + first[0][1], 0, 0, wire),
        reduce_send(first[1][0] + first[1][1], 0, 1, wire),
    ]


def reduce_third(second, wire=bf16):
    joined = jnp.concatenate([total(kept + received) for kept, received in second], axis=-1)
    return [reduce_send([joined], 0, 2, wire)]


def reduce_end(third):
    return total(third[0][0] + third[0][1])


def arrivals(parts):
    return [received for _, received in parts]


def arrived(parts, received):
    return [(kept, new) for (kept, _), new in zip(parts, received)]


def line_perm(turn, back):
    line = lax.axis_size("seg")
    parts = line // SEGS
    pairs = []
    for core in range(2):
        for place in range(line):
            piece = (place % SEGS) ^ turn
            half, index = divmod(piece, 2)
            source = core * line + place
            target = half * line + (2 * core + index) * parts + place // SEGS
            pairs.append((target, source) if back else (source, target))
    return pairs


def whole_sequence(array, core, place):
    parts = lax.axis_size("seg") // SEGS
    half = array.shape[1] // 2
    pieces = array.reshape(2, 2, half, -1).transpose(1, 0, 2, 3).reshape(4, half, -1)
    mine = place % SEGS
    target = 2 * core + (place // parts) % 2
    got = []
    for turn in range(4):
        piece = lax.dynamic_index_in_dim(pieces, mine ^ turn, axis=0, keepdims=False)
        got.append(lax.ppermute(piece, ("core", "seg"), line_perm(turn, False)))
    got = jnp.stack(got)
    return jnp.stack([lax.dynamic_index_in_dim(got, target ^ k, axis=0, keepdims=False) for k in range(4)])


def back_to_owner(ordered, core, place):
    parts = lax.axis_size("seg") // SEGS
    half = ordered.shape[1]
    mine = place % SEGS
    target = 2 * core + (place // parts) % 2
    got = []
    for turn in range(4):
        piece = lax.dynamic_index_in_dim(ordered, target ^ turn, axis=0, keepdims=False)
        got.append(lax.ppermute(piece, ("core", "seg"), line_perm(turn, True)))
    got = jnp.stack(got)
    pieces = jnp.stack([lax.dynamic_index_in_dim(got, mine ^ k, axis=0, keepdims=False) for k in range(4)])
    return pieces.reshape(2, 2, half, -1).transpose(1, 0, 2, 3).reshape(2, 2 * half, -1)


def part_pairs(step):
    line = lax.axis_size("seg")
    parts = line // SEGS
    return [(i, i + step) for i in range(line) if 0 <= i + step < line and i // parts == (i + step) // parts]


def entering(decay, state, step):
    parts = lax.axis_size("seg") // SEGS
    total = jnp.zeros_like(state)
    for _ in range(parts - 1):
        total = lax.ppermute(decay * total + state, "seg", part_pairs(step))
    return total


def borrowed(array, step):
    parts = lax.axis_size("seg") // SEGS
    if parts == 1:
        return jnp.zeros_like(array)
    return lax.ppermute(array, "seg", part_pairs(step))


def spilled(grad, edge, taps):
    if lax.axis_size("seg") == SEGS:
        return grad
    edge = borrowed(edge, -1)
    spill = jnp.stack(
        [
            sum(taps[k] * edge[CONV - 1 - k - early] for k in range(CONV - early))
            for early in range(CONV - 1, 0, -1)
        ]
    )
    at = grad.shape[0] - CONV + 1
    return grad.at[at:].set((grad[at:].astype(f32) + spill).astype(bf16))


def dot(a, b, contract):
    return lax.dot_general(a, b, (contract, ((), ())), preferred_element_type=f32)


def normed_kernel(slabs, core_ref, mine_ref, other_ref, gain_ref, normed_ref, turned_ref):
    mine, other = mine_ref[0], other_ref[0]
    first = core_ref[0] == 0
    hidden = jnp.concatenate([jnp.where(first, mine, other), jnp.where(first, other, mine)], axis=0).astype(f32)
    scale = lax.rsqrt(jnp.mean(hidden * hidden, axis=1, keepdims=True) + epsilon)
    normed = hidden * scale * gain_ref[...]
    normed_ref[...] = normed.astype(bf16)
    turned = normed.T.astype(bf16)
    for to, at, size in slabs:
        turned_ref[to : to + size] = turned[at : at + size]


def normed_tokens(core, mine, other, gain, rows):
    segs, half, width = mine.shape
    a, b, z = chip_dims()
    group = 2 * z * rows
    inside = rows % 16 == 0
    slabs = [(0, 0, width)]
    if inside:
        slabs = [
            (chip * group + (at * 2 + core_at) * rows, chip * group + (core_at * z + at) * rows, rows)
            for chip in range(a * b)
            for core_at in range(2)
            for at in range(z)
        ]
    normed, turned = pl.pallas_call(
        lambda *refs: normed_kernel(slabs, *refs),
        grid_spec=pltpu.PrefetchScalarGridSpec(
            num_scalar_prefetch=1,
            grid=(segs,),
            in_specs=[
                pl.BlockSpec((1, half, width), lambda i, core: (i, 0, 0)),
                pl.BlockSpec((1, half, width), lambda i, core: (i, 0, 0)),
                pl.BlockSpec((1, width), lambda i, core: (0, 0)),
            ],
            out_specs=(
                pl.BlockSpec((2 * half, width), lambda i, core: (i, 0)),
                pl.BlockSpec((width, 2 * half), lambda i, core: (0, i)),
            ),
        ),
        out_shape=(
            jax.ShapeDtypeStruct((segs * 2 * half, width), bf16),
            jax.ShapeDtypeStruct((width, segs * 2 * half), bf16),
        ),
        compiler_params=pltpu.CompilerParams(dimension_semantics=("arbitrary",), vmem_limit_bytes=VMEM_LIMIT),
        cost_estimate=LIGHT,
    )(core.reshape(1).astype(jnp.int32), mine, other, gain.reshape(1, width))
    if not inside:
        turned = turned.reshape(a, b, 2, z, rows, -1).transpose(0, 1, 3, 2, 4, 5).reshape(turned.shape)
    return normed, turned


def mixed_kernel(gated_ref, scale_ref, gain_ref, mixed_ref, turned_ref):
    mixed = gated_ref[...] * scale_ref[...] * gain_ref[...]
    mixed_ref[...] = mixed.astype(bf16)
    turned_ref[...] = mixed.T.astype(bf16)


def mixed_tokens(gated, scale, gain, seg_len):
    length, width = gated.shape
    return pl.pallas_call(
        mixed_kernel,
        grid=(length // seg_len,),
        in_specs=[
            pl.BlockSpec((seg_len, width), lambda i: (i, 0)),
            pl.BlockSpec((seg_len, 1), lambda i: (i, 0)),
            pl.BlockSpec((1, width), lambda i: (0, 0)),
        ],
        out_specs=(
            pl.BlockSpec((seg_len, width), lambda i: (i, 0)),
            pl.BlockSpec((width, seg_len), lambda i: (0, i)),
        ),
        out_shape=(
            jax.ShapeDtypeStruct((length, width), bf16),
            jax.ShapeDtypeStruct((width, length), bf16),
        ),
        compiler_params=pltpu.CompilerParams(dimension_semantics=("arbitrary",), vmem_limit_bytes=VMEM_LIMIT),
        cost_estimate=LIGHT,
    )(gated, scale, gain.reshape(1, width))


def columns_of(pair):
    return pl.ds(pair * LANES, LANES)


def low_half(shape):
    return lax.broadcasted_iota(jnp.int32, shape, len(shape) - 1) < HEADDIM


def pair_columns(array, pair, low):
    rows = array.shape[0]
    first = jnp.broadcast_to(array[:, 2 * pair : 2 * pair + 1], (rows, LANES))
    second = jnp.broadcast_to(array[:, 2 * pair + 1 : 2 * pair + 2], (rows, LANES))
    return jnp.where(low, first, second)


def conv_parts(current, before, taps):
    rows = current.shape[0]
    padded = jnp.concatenate([before, current], axis=0)
    seen = [padded[8 - CONV + 1 + k : 8 - CONV + 1 + k + rows] for k in range(CONV - 1)] + [current]
    total = taps[CONV : CONV + 1]
    for k in range(CONV):
        total = total + taps[k : k + 1] * seen[k]
    return total, seen


def step_terms(raw, head, seg_len):
    shifted = raw + head[1:2]
    step = jnp.maximum(shifted, 0.0) + jnp.log1p(jnp.exp(-jnp.abs(shifted)))
    log_decay = step * head[0:1]
    at_or_before = lax.broadcasted_iota(jnp.int32, (seg_len, seg_len), 0) >= lax.broadcasted_iota(
        jnp.int32, (seg_len, seg_len), 1
    )
    sums = lax.dot_general(
        jnp.where(at_or_before, 1.0, 0.0), log_decay, (((1,), (0,)), ((), ())),
        precision=lax.Precision.HIGHEST, preferred_element_type=f32,
    )
    return shifted, step, log_decay, sums * LOG2E


def forward_kernel(
    proj_ref, taps_ref, head_ref, skip_ref, rim_ref, init_ref,
    values_ref, prior_ref, final_ref, last_ref, state_ref, tail_ref,
):
    seg_len = proj_ref.shape[0]
    half = seg_len // 2

    @pl.when(pl.program_id(0) == 0)
    def _():
        state_ref[...] = init_ref[...]
        tail_ref[...] = rim_ref[...]

    def activated(begin):
        at = pl.ds(begin, LANES)
        total, _ = conv_parts(proj_ref[:, at], tail_ref[:, at], taps_ref[:, at])
        return total * jax.nn.sigmoid(total)

    b_low = activated(HALF).astype(bf16)
    b_turned = activated(HALF).T.astype(bf16)
    c_low = activated(HALF + STATE).astype(bf16)
    _, step, _, sums = step_terms(proj_ref[:, HALF + 2 * STATE :], head_ref, seg_len)
    sums_turned, step_turned = sums.T, step.T
    scores = dot(c_low, b_low, ((1,), (1,)))
    kept = lax.broadcasted_iota(jnp.int32, (half, half), 0) >= lax.broadcasted_iota(jnp.int32, (half, half), 1)
    first_scores = jnp.where(kept, scores[:half, :half], 0.0)
    later_scores = scores[half:, :half]
    second_scores = jnp.where(kept, scores[half:, half:], 0.0)
    low = low_half((seg_len, LANES))
    last_ref[...] = jnp.broadcast_to(sums[seg_len - 1 :], last_ref.shape)

    for pair in range(HEADS // 4):
        at = columns_of(pair)
        x_values = activated(pair * LANES)
        x_low = x_values.astype(bf16)
        sums_pair = pair_columns(sums, pair, low)
        last_pair = sums_pair[seg_len - 1 :]
        carry = jnp.exp2(last_pair - sums_pair) * pair_columns(step, pair, low)
        scaled_x = (carry * x_low.astype(f32)).astype(bf16)
        prior = state_ref[:, at]
        prior_low = prior.astype(bf16)
        prior_ref[0, :, at] = prior_low
        from_state = jnp.exp2(sums_pair) * dot(c_low, prior_low, ((1,), (0,)))
        state_ref[:, at] = jnp.exp2(last_pair) * prior + dot(b_turned, scaled_x, ((1,), (0,)))
        early, late = 0.0, 0.0
        for side in range(2):
            head = 2 * pair + side
            x_side = jnp.where(low if side == 0 else ~low, x_values, 0.0).astype(bf16)
            at_token = jnp.broadcast_to(sums[:, head : head + 1], (seg_len, half))
            at_source, source_step = sums_turned[head : head + 1], step_turned[head : head + 1]
            first = jnp.exp2(jnp.minimum(at_token[:half] - at_source[:, :half], 0.0)) * first_scores
            first = (first * source_step[:, :half]).astype(bf16)
            later = jnp.exp2(at_token[half:] - at_source[:, :half]) * later_scores
            later = (later * source_step[:, :half]).astype(bf16)
            second = jnp.exp2(jnp.minimum(at_token[half:] - at_source[:, half:], 0.0)) * second_scores
            second = (second * source_step[:, half:]).astype(bf16)
            early = early + dot(first, x_side[:half], ((1,), (0,)))
            late = late + dot(jnp.concatenate([later, second], axis=1), x_side, ((1,), (0,)))
        intra = jnp.concatenate([early, late], axis=0)
        values_ref[:, at] = intra + from_state + skip_ref[:, at] * x_values

    tail_ref[...] = proj_ref[seg_len - 8 :, : HALF + 2 * STATE]
    final_ref[...] = state_ref[...]


def full_block(shape):
    return pl.BlockSpec(shape, lambda *_: (0,) * len(shape))


def scan_forward(proj, taps, head, skip, rim, init, seg_len):
    segs = proj.shape[0] // seg_len
    wide = HALF + 2 * STATE
    return pl.pallas_call(
        forward_kernel,
        grid=(segs,),
        out_shape=(
            jax.ShapeDtypeStruct((proj.shape[0], HALF), f32),
            jax.ShapeDtypeStruct((segs, STATE, HALF), bf16),
            jax.ShapeDtypeStruct((STATE, HALF), f32),
            jax.ShapeDtypeStruct((segs * 8, LANES), f32),
        ),
        in_specs=[
            pl.BlockSpec((seg_len, proj.shape[1]), lambda i: (i, 0)),
            full_block((8, wide)),
            full_block((8, LANES)),
            full_block((1, HALF)),
            full_block((8, wide)),
            full_block((STATE, HALF)),
        ],
        out_specs=(
            pl.BlockSpec((seg_len, HALF), lambda i: (i, 0)),
            pl.BlockSpec((1, STATE, HALF), lambda i: (i, 0, 0)),
            full_block((STATE, HALF)),
            pl.BlockSpec((8, LANES), lambda i: (i, 0)),
        ),
        scratch_shapes=[pltpu.VMEM((STATE, HALF), f32), pltpu.VMEM((8, wide), f32)],
        compiler_params=pltpu.CompilerParams(
            dimension_semantics=("arbitrary",), vmem_limit_bytes=VMEM_LIMIT
        ),
        cost_estimate=LIGHT,
    )(proj, taps, head, skip, rim, init)


def split_dot(array, other):
    high = array.astype(bf16)
    rest = (array - high.astype(f32)).astype(bf16)
    return dot(high, other, ((1,), (0,))) + dot(rest, other, ((1,), (0,)))


def backward_kernel(
    group, proj_ref, before_ref, taps_ref, rim_ref, shared_ref, shared_before_ref, shared_taps_ref, shared_rim_ref,
    head_ref, skip_ref, heads_ref, end_ref, prior_ref, values_ref, grad_ref,
    grad_x_ref, grad_b_ref, grad_c_ref, grad_raw_ref, taps_grad_ref, skip_grad_ref, head_grad_ref, edge_ref, start_ref,
    later_ref, local_ref, scaled_ref, grad_state_ref, inner_ref, source_ref, carry_ref, decay_ref,
):
    seg_len = proj_ref.shape[0]
    half = seg_len // 2
    turn = pl.program_id(0)

    @pl.when(turn == 0)
    def _():
        later_ref[...] = end_ref[...]
        edge_ref[...] = jnp.zeros_like(edge_ref)
        taps_grad_ref[...] = jnp.zeros_like(taps_grad_ref)
        skip_grad_ref[...] = jnp.zeros_like(skip_grad_ref)
        head_grad_ref[...] = jnp.zeros_like(head_grad_ref)

    first_segment = turn == pl.num_programs(0) - 1

    def conv_at(at, current, ahead, taps, rim):
        before = jnp.where(first_segment, rim[:, at], ahead[:, at])
        return conv_parts(current[:, at], before, taps[:, at])

    def activated(begin):
        total, _ = conv_at(pl.ds(begin, LANES), shared_ref, shared_before_ref, shared_taps_ref, shared_rim_ref)
        return total * jax.nn.sigmoid(total)

    b_values = activated(0)
    c_values = activated(STATE)
    b_low, c_low, c_turned = b_values.astype(bf16), c_values.astype(bf16), c_values.T.astype(bf16)
    shifted, step, log_decay, sums = step_terms(shared_ref[:, 2 * STATE :], head_ref, seg_len)
    sums_turned = sums.T
    scores = dot(b_low, c_low, ((1,), (1,)))
    kept = lax.broadcasted_iota(jnp.int32, (half, half), 0) <= lax.broadcasted_iota(jnp.int32, (half, half), 1)
    first_scores = jnp.where(kept, scores[:half, :half], 0.0)
    later_scores = scores[:half, half:]
    second_scores = jnp.where(kept, scores[half:, half:], 0.0)
    low = low_half((seg_len, LANES))
    first_grad, later_grad, second_grad = 0.0, 0.0, 0.0

    pairs = grad_ref.shape[1] // LANES
    for pair in range(pairs):
        at = columns_of(pair)
        total, seen = conv_at(at, proj_ref, before_ref, taps_ref, rim_ref)
        sigmoid = jax.nn.sigmoid(total)
        x_values = total * sigmoid
        x_low = x_values.astype(bf16)
        x_wide = x_low.astype(f32)
        sums_pair = pair_columns(sums, group * pairs + pair, low)
        step_pair = pair_columns(step, group * pairs + pair, low)
        last_pair = sums_pair[seg_len - 1 :]
        gap = jnp.exp2(last_pair - sums_pair)
        scaled_ref[:, at] = (gap * step_pair * x_wide).astype(bf16)
        grad_values = grad_ref[:, at]
        grad_state_ref[:, at] = (grad_values * jnp.exp2(sums_pair)).astype(bf16)
        later = later_ref[:, at]
        later_low = later.astype(bf16)
        local_ref[:, at] = later_low
        prior = prior_ref[0, :, at]
        decay_ref[:, at] = jnp.broadcast_to(
            jnp.sum(later * prior.astype(f32), axis=0, keepdims=True), (8, LANES)
        )
        grad_prior = dot(c_turned, grad_state_ref[:, at], ((1,), (0,)))
        later_ref[:, at] = jnp.exp2(last_pair) * later + grad_prior
        grad_scaled = dot(b_low, later_low, ((1,), (0,)))
        stepped = (step_pair * x_wide).astype(bf16)
        early, late = 0.0, 0.0
        for side in range(2):
            head = 2 * (group * pairs + pair) + side
            grad_low = jnp.where(low if side == 0 else ~low, grad_values, 0.0).astype(bf16)
            at_source = jnp.broadcast_to(sums[:, head : head + 1], (seg_len, half))
            at_token = sums_turned[head : head + 1]
            grad_weights = dot(stepped, grad_low, ((1,), (1,)))
            first = jnp.exp2(jnp.minimum(at_token[:, :half] - at_source[:half], 0.0))
            after = jnp.exp2(at_token[:, half:] - at_source[:half])
            second = jnp.exp2(jnp.minimum(at_token[:, half:] - at_source[half:], 0.0))
            first_grad = first_grad + first * grad_weights[:half, :half]
            later_grad = later_grad + after * grad_weights[:half, half:]
            second_grad = second_grad + second * grad_weights[half:, half:]
            upper = jnp.concatenate([first * first_scores, after * later_scores], axis=1).astype(bf16)
            early = early + dot(upper, grad_low, ((1,), (0,)))
            late = late + dot((second * second_scores).astype(bf16), grad_low[half:], ((1,), (0,)))
        inner = jnp.concatenate([early, late], axis=0)
        skip = skip_ref[:, at]
        skip_grad_ref[:, at] += jnp.sum(grad_values * x_values, axis=0, keepdims=True)
        inner_ref[:, at] = grad_values * (values_ref[:, at] - skip * x_values)
        source_ref[:, at] = x_wide * inner
        carry_ref[:, at] = x_wide * grad_scaled
        grad_x = skip * grad_values + step_pair * (inner + gap * grad_scaled)
        grad_total = grad_x * (sigmoid * (1.0 + total * (1.0 - sigmoid)))
        for k in range(CONV):
            taps_grad_ref[k : k + 1, at] += jnp.sum(grad_total * seen[k], axis=0, keepdims=True)
        taps_grad_ref[CONV : CONV + 1, at] += jnp.sum(grad_total, axis=0, keepdims=True)
        extended = jnp.concatenate([grad_total, edge_ref[:, at]], axis=0)
        edge_ref[:, at] = grad_total[:8]
        taps = taps_ref[:, at]
        grad_conv = taps[CONV - 1 : CONV] * grad_total
        for k in range(CONV - 1):
            grad_conv = grad_conv + taps[k : k + 1] * extended[CONV - 1 - k : CONV - 1 - k + seg_len]
        grad_x_ref[:, at] = grad_conv.astype(bf16)

    heads = heads_ref[...]
    tail = jnp.exp2(sums[seg_len - 1 :] - sums)
    source_grad = split_dot(source_ref[...], heads)
    step_grad = source_grad + tail * split_dot(carry_ref[...], heads)
    used = step * step_grad
    sum_grad = split_dot(inner_ref[...], heads) - used
    at_last = jnp.sum(used - step * source_grad, axis=0, keepdims=True)
    at_last = at_last + split_dot(decay_ref[...], heads)[:1] * jnp.exp2(sums[seg_len - 1 :])
    is_last = lax.broadcasted_iota(jnp.int32, (seg_len, LANES), 0) == seg_len - 1
    sum_grad = sum_grad + jnp.where(is_last, at_last, 0.0)
    at_or_after = lax.broadcasted_iota(jnp.int32, (seg_len, seg_len), 0) <= lax.broadcasted_iota(
        jnp.int32, (seg_len, seg_len), 1
    )
    log_grad = lax.dot_general(
        jnp.where(at_or_after, 1.0, 0.0), sum_grad, (((1,), (0,)), ((), ())),
        precision=lax.Precision.HIGHEST, preferred_element_type=f32,
    )
    grad_raw = (step_grad + head_ref[0:1] * log_grad) * jax.nn.sigmoid(shifted)
    grad_raw_ref[...] = grad_raw
    head_grad_ref[0:1] += jnp.sum(log_grad * log_decay, axis=0, keepdims=True)
    head_grad_ref[1:2] += jnp.sum(grad_raw, axis=0, keepdims=True)

    first_low = jnp.where(kept, first_grad, 0.0)
    second_low = jnp.where(kept, second_grad, 0.0)
    grad_scores = jnp.concatenate(
        [
            jnp.concatenate([first_low, later_grad], axis=1),
            jnp.concatenate([jnp.zeros_like(first_low), second_low], axis=1),
        ],
        axis=0,
    )
    start_ref[...] = later_ref[...]
    grad_b_ref[...] = dot(scaled_ref[...], local_ref[...], ((1,), (1,))) + dot(
        grad_scores.astype(bf16), c_low, ((1,), (0,))
    )
    grad_c_ref[...] = dot(grad_state_ref[...], prior_ref[0], ((1,), (1,))) + dot(
        grad_scores.T.astype(bf16), b_low, ((1,), (0,))
    )


GROUPS = 1


def scan_backward(group, proj, taps, head, skip, rim, end, prior, values, grad_values, seg_len):
    length = proj.shape[0]
    segs = length // seg_len
    width, shared = HALF // GROUPS, proj.shape[1] - HALF
    channel = lax.broadcasted_iota(jnp.int32, (width, LANES), 0) // HEADDIM + group * width // HEADDIM
    heads = (channel == lax.broadcasted_iota(jnp.int32, (width, LANES), 1)).astype(bf16)
    back = lambda width, at=0: pl.BlockSpec((seg_len, width), lambda i: (segs - 1 - i, at))
    row_ahead = lambda i: jnp.maximum((segs - 1 - i) * (seg_len // 8) - 1, 0)
    ahead = lambda width, at: pl.BlockSpec((8, width), lambda i: (row_ahead(i), at))
    column = lambda rows, width, at: pl.BlockSpec((rows, width), lambda i: (0, at))
    both = HALF // shared
    taps, rim = jnp.pad(taps, ((0, 0), (0, shared - 2 * STATE))), jnp.pad(rim, ((0, 0), (0, shared - 2 * STATE)))
    return pl.pallas_call(
        lambda *refs: backward_kernel(group, *refs),
        grid=(segs,),
        out_shape=(
            jax.ShapeDtypeStruct((length, width), bf16),
            jax.ShapeDtypeStruct((length, STATE), f32),
            jax.ShapeDtypeStruct((length, STATE), f32),
            jax.ShapeDtypeStruct((length, LANES), f32),
            jax.ShapeDtypeStruct((8, width), f32),
            jax.ShapeDtypeStruct((1, width), f32),
            jax.ShapeDtypeStruct((8, LANES), f32),
            jax.ShapeDtypeStruct((8, width), f32),
            jax.ShapeDtypeStruct((STATE, width), f32),
        ),
        in_specs=[
            back(width, group),
            ahead(width, group),
            column(8, width, group),
            column(8, width, group),
            back(shared, both),
            ahead(shared, both),
            column(8, shared, both),
            column(8, shared, both),
            full_block((8, LANES)),
            column(1, width, group),
            full_block((width, LANES)),
            column(STATE, width, group),
            pl.BlockSpec((1, STATE, width), lambda i: (segs - 1 - i, 0, group)),
            back(width, group),
            back(width, group),
        ],
        out_specs=(
            back(width),
            back(STATE),
            back(STATE),
            back(LANES),
            full_block((8, width)),
            full_block((1, width)),
            full_block((8, LANES)),
            full_block((8, width)),
            full_block((STATE, width)),
        ),
        scratch_shapes=[
            pltpu.VMEM((STATE, width), f32),
            pltpu.VMEM((STATE, width), bf16),
            pltpu.VMEM((seg_len, width), bf16),
            pltpu.VMEM((seg_len, width), bf16),
            pltpu.VMEM((seg_len, width), f32),
            pltpu.VMEM((seg_len, width), f32),
            pltpu.VMEM((seg_len, width), f32),
            pltpu.VMEM((8, width), f32),
        ],
        compiler_params=pltpu.CompilerParams(
            dimension_semantics=("arbitrary",), vmem_limit_bytes=VMEM_LIMIT
        ),
        cost_estimate=LIGHT,
    )(proj, proj, taps, rim, proj, proj, taps, rim, head, skip, heads, end, prior, values, grad_values)


def half_kernel(transposed, count, core_ref, *refs):
    inputs, mine_ref, theirs_ref = refs[: 2 * count], refs[2 * count], refs[2 * count + 1]
    total = 0.0
    for left, right in zip(inputs[:count], inputs[count:]):
        total = total + dot(left[...], right[...], ((1,), (1 if transposed else 0,)))
    half = total.shape[0] // 2
    first = core_ref[0] == 0
    mine_ref[0] = jnp.where(first, total[:half], total[half:])
    theirs_ref[0] = jnp.where(first, total[half:], total[:half]).astype(bf16)


def half_products(core, terms, seg_len, width, transposed):
    length = terms[0][0].shape[0]
    left = [pl.BlockSpec((seg_len, array.shape[1]), lambda i, core: (i, 0)) for array, _, _ in terms]
    right = []
    for array, matrix, at in terms:
        if transposed:
            right.append(pl.BlockSpec((width, array.shape[1]), lambda i, core, at=at: (0, at(core[0]))))
        else:
            right.append(pl.BlockSpec(matrix.shape, lambda i, core: (0, 0)))
    depth = sum(array.shape[1] for array, _, _ in terms)
    mine, theirs = pl.pallas_call(
        lambda *refs: half_kernel(transposed, len(terms), *refs),
        grid_spec=pltpu.PrefetchScalarGridSpec(
            num_scalar_prefetch=1,
            grid=(length // seg_len,),
            in_specs=left + right,
            out_specs=[pl.BlockSpec((1, seg_len // 2, width), lambda i, core: (i, 0, 0))] * 2,
        ),
        out_shape=(
            jax.ShapeDtypeStruct((length // seg_len, seg_len // 2, width), f32),
            jax.ShapeDtypeStruct((length // seg_len, seg_len // 2, width), bf16),
        ),
        compiler_params=pltpu.CompilerParams(dimension_semantics=("arbitrary",), vmem_limit_bytes=VMEM_LIMIT),
        cost_estimate=LIGHT,
    )(core.reshape(1).astype(jnp.int32), *[array for array, _, _ in terms], *[matrix for _, matrix, _ in terms])
    return mine, theirs


def shared_kernel(core_ref, proj_ref, rim_ref, taps_ref, b_ref, c_ref, other_ref, grad_ref, taps_grad_ref, edge_ref):
    total, seen = conv_parts(proj_ref[...], rim_ref[...], taps_ref[...])
    sigmoid = jax.nn.sigmoid(total)
    grad_total = jnp.where(core_ref[0] == 0, b_ref[...], c_ref[...]) + other_ref[...]
    grad_total = grad_total * (sigmoid * (1.0 + total * (1.0 - sigmoid)))
    sums = [jnp.sum(grad_total * part, axis=0, keepdims=True) for part in seen]
    sums = sums + [jnp.sum(grad_total, axis=0, keepdims=True), jnp.zeros((8 - CONV - 1, LANES), f32)]
    taps_grad_ref[...] = jnp.concatenate(sums, axis=0)
    edge_ref[...] = grad_total[:8]
    taps = taps_ref[...]
    extended = jnp.concatenate([grad_total, jnp.zeros((8, LANES), f32)], axis=0)
    grad_conv = taps[CONV - 1 : CONV] * grad_total
    for k in range(CONV - 1):
        grad_conv = grad_conv + taps[k : k + 1] * extended[CONV - 1 - k : CONV - 1 - k + grad_total.shape[0]]
    grad_ref[...] = grad_conv.astype(bf16)


def shared_backward(core, proj, rim, taps, grad_b, grad_c, other):
    length = proj.shape[0]
    picked = lambda rows: pl.BlockSpec((rows, LANES), lambda i, core: (0, HALF // LANES + core[0]))
    whole = lambda rows: pl.BlockSpec((rows, LANES), lambda i, core: (0, 0))
    return pl.pallas_call(
        shared_kernel,
        grid_spec=pltpu.PrefetchScalarGridSpec(
            num_scalar_prefetch=1,
            grid=(1,),
            in_specs=[picked(length), picked(8), picked(8), whole(length), whole(length), whole(length)],
            out_specs=(whole(length), whole(8), whole(8)),
        ),
        out_shape=(
            jax.ShapeDtypeStruct((length, LANES), bf16),
            jax.ShapeDtypeStruct((8, LANES), f32),
            jax.ShapeDtypeStruct((8, LANES), f32),
        ),
        compiler_params=pltpu.CompilerParams(vmem_limit_bytes=VMEM_LIMIT),
        cost_estimate=LIGHT,
    )(core.reshape(1).astype(jnp.int32), proj, rim, taps, grad_b, grad_c, other)


def per_device(hidden_in, cotangent, in_proj, out_proj, conv_params, pre_gain, gated_gain, head_params):
    chips, line = lax.axis_size("chip"), lax.axis_size("seg")
    core, place = lax.axis_index("core"), lax.axis_index("seg")
    rows, model_width = in_proj.shape[0], hidden_in.shape[2]
    heads = HEADS // 2

    conv_width, gain_width = conv_params.shape[1], gated_gain.shape[0]
    used = HALF + 2 * STATE + heads
    spare = -used % LANES
    small = jnp.zeros((rows, spare), bf16)
    small = small.at[: CONV + 1, :conv_width].set(conv_params)
    small = small.at[CONV + 1, :rows].set(pre_gain)
    small = small.at[CONV + 2, :gain_width].set(gated_gain)

    def conv_side(which):
        return jnp.concatenate(
            [
                own_columns(in_proj[:, INNER : 2 * INNER], which),
                in_proj[:, 2 * INNER : INNER + XBC],
                own_columns(in_proj[:, INNER + XBC :], which),
                small,
            ],
            axis=1,
        )

    def gate_side(which):
        return own_columns(in_proj[:, :INNER], which)

    conv_swap = to_partner(conv_side(1 - core))
    conv_block = in_core_order(conv_side(core), conv_swap, core, 0)
    conv_z = gather_first(conv_block)
    gate_swap = to_partner(gate_side(1 - core))
    gate_block = in_core_order(gate_side(core), gate_swap, core, 0)
    rest_block = jnp.stack([gate_block.reshape(2 * rows, HALF), out_proj])
    rest_block, conv_z = tie(rest_block, conv_z)
    rest_z = gather_step(rest_block, 2)
    conv_2 = gather_next(conv_z, 1)
    conv_last = gather_next(conv_2, 2)
    conv_last, rest_z, hidden_in = tie(conv_last, rest_z, hidden_in)
    hidden_half = whole_sequence(hidden_in, core, place)
    rest_2 = gather_next([[piece[0] for piece in rest_z], [piece[1] for piece in rest_z]], 1)
    parts = list(zip(ORDERS, column_parts(conv_block.shape[-1]), conv_last))
    conv_all = whole_matrices([(conv_block.shape, True, parts)])[0].reshape(model_width, -1)

    small_all = conv_all.reshape(chips, 2, line, rows, -1)[..., used:].astype(f32)
    taps_full = small_all[..., : CONV + 1, :conv_width].transpose(3, 0, 1, 2, 4).reshape(CONV + 1, XBC)
    taps = jnp.concatenate([own_columns(taps_full[:, :INNER], core), taps_full[:, INNER:]], axis=1)
    gain_pre = small_all[..., CONV + 1, :rows].reshape(model_width)
    gain_gate = lax.dynamic_index_in_dim(
        small_all[..., CONV + 2, :gain_width], core, axis=1, keepdims=False
    ).reshape(HALF)
    params = own_columns(head_params, core)

    conv_all, hidden_half, rest_2, cotangent = tie(conv_all, hidden_half, rest_2, cotangent)
    hidden_other = to_partner(hidden_half)
    rest_last = gather_next(rest_2, 2)
    cot_half = whole_sequence(cotangent, core, place)
    seg_len = 2 * hidden_half.shape[1]
    tokens = SEGS * seg_len
    normed, normed_turned = normed_tokens(core, hidden_half, hidden_other, gain_pre, rows)
    projected = dot(normed, conv_all, ((1,), (0,)))

    taps = jnp.pad(taps, ((0, 8 - CONV - 1), (0, 0)))
    head = jnp.pad(jnp.stack([-jnp.exp(params[0]), params[1]]), ((0, 6), (0, LANES - heads)))
    skip = jnp.repeat(params[2], HEADDIM).reshape(1, HALF)
    wide = HALF + 2 * STATE
    rim = borrowed(projected[tokens - 8 :, :wide], 1)
    nothing = jnp.zeros((STATE, HALF), f32)
    values, prior, final, last = scan_forward(projected, taps, head, skip, rim, nothing, seg_len)
    if line > SEGS:
        last = jnp.sum(last.reshape(SEGS, 8, LANES)[:, 0, :heads], axis=0)
        decay = jnp.repeat(jnp.exp2(last), HEADDIM)
        begin = entering(decay, final, 1)
        values, prior, _, _ = scan_forward(projected, taps, head, skip, rim, begin, seg_len)

    values, rest_last, cot_half = tie(values, rest_last, cot_half)
    cot = in_core_order(cot_half, to_partner(cot_half), core, 1)
    upstream = cot.reshape(tokens, model_width)
    gate_matrix, out_matrix = whole_matrices(
        [
            (gate_block.shape, True, [(ORDERS[0], (0, HALF), rest_last[0])]),
            (out_proj.shape, False, [(ORDERS[1], (0, model_width), rest_last[1])]),
        ]
    )
    gate_matrix, out_matrix = gate_matrix.reshape(model_width, HALF), out_matrix.reshape(HALF, model_width)
    gate_input = dot(normed, gate_matrix, ((1,), (0,)))

    silu_gate = jax.nn.silu(gate_input)
    gated = values * silu_gate
    squares = jnp.sum(gated * gated, axis=1)
    squares_other = to_partner(squares)
    grad_mixed = dot(upstream, out_matrix, ((1,), (1,)))
    squares_other, grad_mixed = tie(squares_other, grad_mixed)
    scale = lax.rsqrt((squares + squares_other) / INNER + epsilon)[:, None]
    unit = gated * scale
    gain_grad = grad_mixed * gain_gate
    along = jnp.sum(gain_grad * unit, axis=1)
    along_other = to_partner(along)
    mixed, mixed_turned = mixed_tokens(gated, scale, gain_gate, seg_len)
    by_owner = lambda grad: grad.astype(bf16).reshape(chip_dims() + (-1, grad.shape[1]))
    out_first = reduce_first(by_owner(dot(mixed_turned, upstream, ((1,), (0,)))))
    along_other, mixed = tie(along_other, mixed)
    along = ((along + along_other) / INNER)[:, None]
    gate_gain_grad = jnp.sum(grad_mixed * unit, axis=0)
    grad_gated = scale * (gain_grad - unit * along)
    grad_values = grad_gated * silu_gate
    sigmoid = jax.nn.sigmoid(gate_input)
    grad_gate = (grad_gated * values * (sigmoid * (1.0 + gate_input * (1.0 - sigmoid)))).astype(bf16)
    branch, branch_sent = half_products(core, [(mixed, out_matrix, None)], seg_len, model_width, False)
    branch_other = to_partner(branch_sent)
    grad_gate, grad_values, out_got, branch_other = tie(grad_gate, grad_values, arrivals(out_first), branch_other)
    out_second = reduce_second(arrived(out_first, out_got))
    hidden_out = back_to_owner(
        (hidden_half.astype(f32) + branch + branch_other.astype(f32)).astype(bf16), core, place
    )
    gate_grad = by_owner(dot(normed_turned, grad_gate, ((1,), (0,))))
    gate_grad, out_got, grad_values = tie(gate_grad, arrivals(out_second), grad_values)
    out_second = arrived(out_second, out_got)
    gate_first = reduce_first(gate_grad)
    scan = lambda later: scan_backward(
        0, projected, taps, head, skip, rim, later, prior, values, grad_values, seg_len
    )
    if line > SEGS:
        nothing = entering(decay, scan(nothing)[-1], -1)
    back = scan(nothing)
    back, gate_got, hidden_out = tie(back, arrivals(gate_first), hidden_out)
    gate_second = reduce_second(arrived(gate_first, gate_got))
    out_third = reduce_third(out_second)
    grad_x, grad_b, grad_c, grad_raw, x_taps_grad, skip_grad, head_sums, x_edge, _ = back
    head_grad = jnp.concatenate([head_sums[:2, :heads], skip_grad.reshape(1, heads, HEADDIM).sum(axis=2)])

    other = to_partner(jnp.where(core == 0, grad_c, grad_b))
    grad_state, state_taps_grad, state_edge = shared_backward(core, projected, rim, taps, grad_b, grad_c, other)
    grad_state = spilled(grad_state, state_edge, lax.dynamic_slice_in_dim(taps, HALF + core * STATE, STATE, axis=1))
    grad_x = spilled(grad_x, x_edge, taps[:, :HALF])
    grad_raw = grad_raw.astype(bf16)
    grad_proj = jnp.concatenate([grad_x, grad_state, grad_raw], axis=1)
    conv_grad = by_owner(dot(normed_turned, grad_proj, ((1,), (0,))))
    state_taps_grad = state_taps_grad[: CONV + 1]
    none = jnp.zeros_like(state_taps_grad)
    taps_grad = jnp.concatenate(
        [
            x_taps_grad[: CONV + 1],
            jnp.where(core == 0, state_taps_grad, none),
            jnp.where(core == 0, none, state_taps_grad),
        ],
        axis=1,
    )
    conv_grad, gate_got, out_got, grad_gate = tie(conv_grad, arrivals(gate_second), arrivals(out_third), grad_gate)
    gate_second, out_third = arrived(gate_second, gate_got), arrived(out_third, out_got)
    conv_first = reduce_first(conv_grad)
    gate_third = reduce_third(gate_second)
    terms = [
        (grad_gate, gate_matrix, lambda core: 0),
        (grad_x, conv_all, lambda core: 0),
        (grad_state, conv_all, lambda core: HALF // LANES + core),
        (grad_raw, conv_all, lambda core: (HALF + 2 * STATE) // LANES),
    ]
    grad_normed, sent_normed = half_products(core, terms, seg_len, model_width, True)
    sent_normed, conv_got, gate_got = tie(sent_normed, arrivals(conv_first), arrivals(gate_third))
    other_normed = to_partner(sent_normed)
    conv_second = reduce_second(arrived(conv_first, conv_got))
    gate_third = arrived(gate_third, gate_got)
    wide_hidden = hidden_half.astype(f32)
    hidden_scale = lax.rsqrt(jnp.mean(wide_hidden * wide_hidden, axis=-1, keepdims=True) + epsilon)
    grad_normed = (grad_normed + other_normed.astype(f32)) * gain_pre
    hidden_unit = wide_hidden * hidden_scale
    along = jnp.mean(grad_normed * hidden_unit, axis=-1, keepdims=True)
    grad_hidden = hidden_scale * (grad_normed - hidden_unit * along)
    grad_in = back_to_owner((cot_half.astype(f32) + grad_hidden).astype(bf16), core, place)

    def spread_own(array):
        width = array.shape[-1] // chips
        parted = array.reshape(array.shape[:-1] + (chips, 1, width))
        none = jnp.zeros_like(parted)
        both = jnp.where(
            core == 0,
            jnp.concatenate([parted, none], axis=-2),
            jnp.concatenate([none, parted], axis=-2),
        )
        return both.reshape(array.shape[:-1] + (2 * array.shape[-1],))

    taps_all = jnp.concatenate([spread_own(taps_grad[:, :HALF]), taps_grad[:, HALF:]], axis=1)
    taps_all = taps_all.reshape(CONV + 1, chips, 2, line, conv_width).transpose(1, 3, 2, 0, 4)
    gate_all = spread_own(gate_gain_grad).reshape(chips, 2, line, gain_width).transpose(0, 2, 1, 3)
    head_all = jnp.broadcast_to(spread_own(head_grad).reshape(-1), (chips, line, 2, 3 * HEADS))
    small_grads = jnp.concatenate(
        [
            taps_all.reshape(chips, line, 2, -1),
            gate_all,
            head_all,
        ],
        axis=3,
    )
    count = small_grads.shape[3]
    small_grads = small_grads.reshape(chip_dims() + (2, count))
    small_second = reduce_second(reduce_first(small_grads, f32), f32)
    small_got, conv_got, grad_in = tie(arrivals(small_second), arrivals(conv_second), grad_in)
    small_share = reduce_end(reduce_third(arrived(small_second, small_got), f32))
    conv_third = reduce_third(arrived(conv_second, conv_got))
    out_share = reduce_end(out_third).reshape(-1, model_width)
    paired = lambda third: reduce_end(third).astype(bf16).reshape(2, rows, -1)
    gate_share, conv_share = paired(gate_third), paired(conv_third)

    def mine_and_partner(share):
        keep = lax.dynamic_index_in_dim(share, core, axis=0, keepdims=False)
        give = lax.dynamic_index_in_dim(share, 1 - core, axis=0, keepdims=False)
        return keep, to_partner(give)

    keep, got = mine_and_partner(small_share)
    small_total = keep + got
    taps_end = (CONV + 1) * conv_width
    taps_share = small_total[:taps_end].reshape(CONV + 1, conv_width)
    gain_share = small_total[taps_end : taps_end + gain_width]
    head_total = small_total[taps_end + gain_width :].reshape(3, HEADS)

    def interleave(mine, theirs):
        width = mine.shape[1] // chips
        both = in_core_order(mine.reshape(rows, chips, width), theirs.reshape(rows, chips, width), core, 2)
        return both.reshape(rows, -1)

    keep_gate, got_gate = mine_and_partner(gate_share)
    keep, got = mine_and_partner(conv_share)
    state_end = HALF + STATE
    in_share = jnp.concatenate(
        [
            interleave(keep_gate, got_gate),
            interleave(keep[:, :HALF], got[:, :HALF]),
            in_core_order(keep[:, HALF:state_end], got[:, HALF:state_end], core, 1).reshape(rows, -1),
            interleave(keep[:, state_end : state_end + heads], got[:, state_end : state_end + heads]),
        ],
        axis=1,
    ).astype(f32)
    pre_share = jnp.sum(in_proj.astype(f32) * in_share, axis=1) / pre_gain.astype(f32)
    return (hidden_out, grad_in, in_share, out_share, taps_share, pre_share, gain_share, head_total)


def solution(mesh):
    devices = mesh.devices
    cores = Mesh(devices.reshape(devices.shape[0] // 2, 2, devices.shape[1]), ("chip", "core", "seg"))
    dp, both = ("chip", "core"), ("chip", "core", "seg")
    tokens = P(dp, "seg", None)
    return jax.shard_map(
        per_device,
        mesh=cores,
        in_specs=(tokens, tokens, P(both, None), P(both, None), P(None, both), P(both), P(both), P()),
        out_specs=(tokens, tokens, P(both, None), P(both, None), P(None, both), P(both), P(both), P()),
        check_vma=False,
    )
```

```python
import jax
import jax.numpy as jnp
from jax import lax
from jax.experimental import pallas as pl
from jax.experimental.pallas import tpu as pltpu
from jax.sharding import Mesh
from jax.sharding import PartitionSpec as P

HEADS = 48
HEADDIM = 64
STATE = 128
CONV = 4
INNER = 3072
XBC = 3328
HALF = INNER // 2
LANES = 128
SEGS = 4
LIGHT = pl.CostEstimate(flops=1024, bytes_accessed=1024, transcendentals=0)
VMEM_LIMIT = 48 * 1024 * 1024
LOG2E = 1.4426950408889634

epsilon = 1e-05
f32 = jnp.float32
bf16 = jnp.bfloat16


def own_columns(array, core):
    chips = lax.axis_size("chip")
    width = array.shape[-1] // (2 * chips)
    parted = array.reshape(array.shape[:-1] + (chips, 2, width))
    picked = lax.dynamic_index_in_dim(parted, core, axis=parted.ndim - 2, keepdims=False)
    return picked.reshape(array.shape[:-1] + (chips * width,))


def to_partner(array):
    return lax.ppermute(array, "core", [(0, 1), (1, 0)])


def in_core_order(mine, theirs, core, axis):
    first = jnp.where(core == 0, mine, theirs)
    second = jnp.where(core == 0, theirs, mine)
    return jnp.stack([first, second], axis=axis)


def chip_dims():
    return (lax.axis_size("chip") // 2, 2, lax.axis_size("seg"))


def chip_place():
    chip = lax.axis_index("chip")
    return (chip // 2, chip % 2, lax.axis_index("seg"))


def moved(array, dim, by):
    sizes = chip_dims()
    index = lambda at: (at[0] * sizes[1] + at[1]) * sizes[2] + at[2]
    pairs = []
    for a in range(sizes[0]):
        for b in range(sizes[1]):
            for z in range(sizes[2]):
                to = [a, b, z]
                to[dim] = (to[dim] + by) % sizes[dim]
                pairs.append((index((a, b, z)), index(to)))
    return lax.ppermute(array, ("chip", "seg"), pairs)


def tie(*values):
    return lax.optimization_barrier(values)


ORDERS = ((2, 0, 1), (2, 1, 0))


def column_parts(width):
    cut = -(-(width // 2) // LANES) * LANES
    return ((0, cut), (cut, width))


def gather_step(data, dim):
    return [data] + [moved(data, dim, by) for by in range(1, chip_dims()[dim])]


def gather_first(block):
    pieces = gather_step(block, 2)
    return [[piece[..., begin:end] for piece in pieces] for begin, end in column_parts(block.shape[-1])]


def gather_next(parts, step):
    return [gather_step(jnp.stack(part), order[step]) for order, part in zip(ORDERS, parts)]


def placed_kernel(plan, outs, place_ref, *refs):
    sources, targets, sems = refs[: -outs - 1], refs[-outs - 1 : -1], refs[-1]
    copies = []
    for source, lead, at, columns, paired, out in plan:
        spot = [lax.rem(place_ref[dim] + (size - back), size) for dim, (back, size) in enumerate(at)]
        target = targets[out].at[spot[0], spot[1]]
        target = target.at[:, spot[2]] if paired else target.at[spot[2]]
        target = target.at[..., pl.ds(*columns)]
        copies.append(pltpu.make_async_copy(sources[source].at[lead], target, sems.at[len(copies)]))
    for copy in copies:
        copy.start()
    for copy in copies:
        copy.wait()


def whole_matrices(jobs):
    sizes = chip_dims()
    plan, sources, shapes = [], [], []
    for out, (shape, paired, parts) in enumerate(jobs):
        for order, (begin, end), part in parts:
            for back_last, piece in enumerate(part):
                for back_mid in range(sizes[order[1]]):
                    for back_first in range(sizes[order[0]]):
                        at = [None] * 3
                        at[order[2]] = (back_last, sizes[order[2]])
                        at[order[1]] = (back_mid, sizes[order[1]])
                        at[order[0]] = (back_first, sizes[order[0]])
                        plan.append((len(sources), (back_mid, back_first), at, (begin, end - begin), paired, out))
                sources.append(piece.reshape(piece.shape[:2] + shape[:-1] + piece.shape[-1:]))
        shapes.append(sizes[:2] + (2, sizes[2]) + shape[1:] if paired else sizes + shape)
    anywhere = pl.BlockSpec(memory_space=pl.ANY)
    total = sum(source.size for source in sources)
    return pl.pallas_call(
        lambda *refs: placed_kernel(plan, len(jobs), *refs),
        out_shape=[jax.ShapeDtypeStruct(shape, bf16) for shape in shapes],
        in_specs=[pl.BlockSpec(memory_space=pltpu.SMEM)] + [anywhere] * len(sources),
        out_specs=[pl.BlockSpec(memory_space=pltpu.VMEM)] * len(jobs),
        scratch_shapes=[pltpu.SemaphoreType.DMA((len(plan),))],
        compiler_params=pltpu.CompilerParams(vmem_limit_bytes=VMEM_LIMIT),
        cost_estimate=LIGHT,
    )(jnp.stack(chip_place()).astype(jnp.int32), *sources)


def total(terms):
    result = terms[0].astype(f32)
    for term in terms[1:]:
        result = result + term.astype(f32)
    return result


def reduce_send(terms, axis, dim, wire):
    place, size = chip_place()[dim], chip_dims()[dim]
    pick = lambda at: [lax.dynamic_index_in_dim(term, at, axis=axis, keepdims=False) for term in terms]
    received = [moved(total(pick((place + by) % size)).astype(wire), dim, by) for by in range(1, size)]
    return pick(place), received


def reduce_first(partial, wire=bf16):
    (begin, cut), (_, end) = column_parts(partial.shape[-1])
    return [
        reduce_send([partial[..., begin:cut]], 1, 1, wire),
        reduce_send([partial[..., cut:end]], 0, 0, wire),
    ]


def reduce_second(first, wire=bf16):
    return [
        reduce_send(first[0][0] + first[0][1], 0, 0, wire),
        reduce_send(first[1][0] + first[1][1], 0, 1, wire),
    ]


def reduce_third(second, wire=bf16):
    joined = jnp.concatenate([total(kept + received) for kept, received in second], axis=-1)
    return [reduce_send([joined], 0, 2, wire)]


def reduce_end(third):
    return total(third[0][0] + third[0][1])


def arrivals(parts):
    return [received for _, received in parts]


def arrived(parts, received):
    return [(kept, new) for (kept, _), new in zip(parts, received)]


def line_perm(turn, back):
    line = lax.axis_size("seg")
    parts = line // SEGS
    pairs = []
    for core in range(2):
        for place in range(line):
            piece = (place % SEGS) ^ turn
            half, index = divmod(piece, 2)
            source = core * line + place
            target = half * line + (2 * core + index) * parts + place // SEGS
            pairs.append((target, source) if back else (source, target))
    return pairs


def whole_sequence(array, core, place):
    parts = lax.axis_size("seg") // SEGS
    half = array.shape[1] // 2
    pieces = array.reshape(2, 2, half, -1).transpose(1, 0, 2, 3).reshape(4, half, -1)
    mine = place % SEGS
    target = 2 * core + (place // parts) % 2
    got = []
    for turn in range(4):
        piece = lax.dynamic_index_in_dim(pieces, mine ^ turn, axis=0, keepdims=False)
        got.append(lax.ppermute(piece, ("core", "seg"), line_perm(turn, False)))
    got = jnp.stack(got)
    return jnp.stack([lax.dynamic_index_in_dim(got, target ^ k, axis=0, keepdims=False) for k in range(4)])


def back_to_owner(ordered, core, place):
    parts = lax.axis_size("seg") // SEGS
    half = ordered.shape[1]
    mine = place % SEGS
    target = 2 * core + (place // parts) % 2
    got = []
    for turn in range(4):
        piece = lax.dynamic_index_in_dim(ordered, target ^ turn, axis=0, keepdims=False)
        got.append(lax.ppermute(piece, ("core", "seg"), line_perm(turn, True)))
    got = jnp.stack(got)
    pieces = jnp.stack([lax.dynamic_index_in_dim(got, mine ^ k, axis=0, keepdims=False) for k in range(4)])
    return pieces.reshape(2, 2, half, -1).transpose(1, 0, 2, 3).reshape(2, 2 * half, -1)


def part_pairs(step):
    line = lax.axis_size("seg")
    parts = line // SEGS
    return [(i, i + step) for i in range(line) if 0 <= i + step < line and i // parts == (i + step) // parts]


def entering(decay, state, step):
    parts = lax.axis_size("seg") // SEGS
    total = jnp.zeros_like(state)
    for _ in range(parts - 1):
        total = lax.ppermute(decay * total + state, "seg", part_pairs(step))
    return total


def borrowed(array, step):
    parts = lax.axis_size("seg") // SEGS
    if parts == 1:
        return jnp.zeros_like(array)
    return lax.ppermute(array, "seg", part_pairs(step))


def spilled(grad, edge, taps):
    if lax.axis_size("seg") == SEGS:
        return grad
    edge = borrowed(edge, -1)
    spill = jnp.stack(
        [
            sum(taps[k] * edge[CONV - 1 - k - early] for k in range(CONV - early))
            for early in range(CONV - 1, 0, -1)
        ]
    )
    at = grad.shape[0] - CONV + 1
    return grad.at[at:].set((grad[at:].astype(f32) + spill).astype(bf16))


def dot(a, b, contract):
    return lax.dot_general(a, b, (contract, ((), ())), preferred_element_type=f32)


def normed_kernel(slabs, core_ref, mine_ref, other_ref, gain_ref, normed_ref, turned_ref):
    mine, other = mine_ref[0], other_ref[0]
    first = core_ref[0] == 0
    hidden = jnp.concatenate([jnp.where(first, mine, other), jnp.where(first, other, mine)], axis=0).astype(f32)
    scale = lax.rsqrt(jnp.mean(hidden * hidden, axis=1, keepdims=True) + epsilon)
    normed = hidden * scale * gain_ref[...]
    normed_ref[...] = normed.astype(bf16)
    turned = normed.T.astype(bf16)
    for to, at, size in slabs:
        turned_ref[to : to + size] = turned[at : at + size]


def normed_tokens(core, mine, other, gain, rows):
    segs, half, width = mine.shape
    a, b, z = chip_dims()
    group = 2 * z * rows
    inside = rows % 16 == 0
    slabs = [(0, 0, width)]
    if inside:
        slabs = [
            (chip * group + (at * 2 + core_at) * rows, chip * group + (core_at * z + at) * rows, rows)
            for chip in range(a * b)
            for core_at in range(2)
            for at in range(z)
        ]
    normed, turned = pl.pallas_call(
        lambda *refs: normed_kernel(slabs, *refs),
        grid_spec=pltpu.PrefetchScalarGridSpec(
            num_scalar_prefetch=1,
            grid=(segs,),
            in_specs=[
                pl.BlockSpec((1, half, width), lambda i, core: (i, 0, 0)),
                pl.BlockSpec((1, half, width), lambda i, core: (i, 0, 0)),
                pl.BlockSpec((1, width), lambda i, core: (0, 0)),
            ],
            out_specs=(
                pl.BlockSpec((2 * half, width), lambda i, core: (i, 0)),
                pl.BlockSpec((width, 2 * half), lambda i, core: (0, i)),
            ),
        ),
        out_shape=(
            jax.ShapeDtypeStruct((segs * 2 * half, width), bf16),
            jax.ShapeDtypeStruct((width, segs * 2 * half), bf16),
        ),
        compiler_params=pltpu.CompilerParams(dimension_semantics=("arbitrary",), vmem_limit_bytes=VMEM_LIMIT),
        cost_estimate=LIGHT,
    )(core.reshape(1).astype(jnp.int32), mine, other, gain.reshape(1, width))
    if not inside:
        turned = turned.reshape(a, b, 2, z, rows, -1).transpose(0, 1, 3, 2, 4, 5).reshape(turned.shape)
    return normed, turned


def mixed_kernel(gated_ref, scale_ref, gain_ref, mixed_ref, turned_ref):
    mixed = gated_ref[...] * scale_ref[...] * gain_ref[...]
    mixed_ref[...] = mixed.astype(bf16)
    turned_ref[...] = mixed.T.astype(bf16)


def mixed_tokens(gated, scale, gain, seg_len):
    length, width = gated.shape
    return pl.pallas_call(
        mixed_kernel,
        grid=(length // seg_len,),
        in_specs=[
            pl.BlockSpec((seg_len, width), lambda i: (i, 0)),
            pl.BlockSpec((seg_len, 1), lambda i: (i, 0)),
            pl.BlockSpec((1, width), lambda i: (0, 0)),
        ],
        out_specs=(
            pl.BlockSpec((seg_len, width), lambda i: (i, 0)),
            pl.BlockSpec((width, seg_len), lambda i: (0, i)),
        ),
        out_shape=(
            jax.ShapeDtypeStruct((length, width), bf16),
            jax.ShapeDtypeStruct((width, length), bf16),
        ),
        compiler_params=pltpu.CompilerParams(dimension_semantics=("arbitrary",), vmem_limit_bytes=VMEM_LIMIT),
        cost_estimate=LIGHT,
    )(gated, scale, gain.reshape(1, width))


def columns_of(pair):
    return pl.ds(pair * LANES, LANES)


def low_half(shape):
    return lax.broadcasted_iota(jnp.int32, shape, len(shape) - 1) < HEADDIM


def pair_columns(array, pair, low):
    rows = array.shape[0]
    first = jnp.broadcast_to(array[:, 2 * pair : 2 * pair + 1], (rows, LANES))
    second = jnp.broadcast_to(array[:, 2 * pair + 1 : 2 * pair + 2], (rows, LANES))
    return jnp.where(low, first, second)


def conv_parts(current, before, taps):
    rows = current.shape[0]
    padded = jnp.concatenate([before, current], axis=0)
    seen = [padded[8 - CONV + 1 + k : 8 - CONV + 1 + k + rows] for k in range(CONV - 1)] + [current]
    total = taps[CONV : CONV + 1]
    for k in range(CONV):
        total = total + taps[k : k + 1] * seen[k]
    return total, seen


def step_terms(raw, head, seg_len):
    shifted = raw + head[1:2]
    step = jnp.maximum(shifted, 0.0) + jnp.log1p(jnp.exp(-jnp.abs(shifted)))
    log_decay = step * head[0:1]
    at_or_before = lax.broadcasted_iota(jnp.int32, (seg_len, seg_len), 0) >= lax.broadcasted_iota(
        jnp.int32, (seg_len, seg_len), 1
    )
    sums = lax.dot_general(
        jnp.where(at_or_before, 1.0, 0.0), log_decay, (((1,), (0,)), ((), ())),
        precision=lax.Precision.HIGHEST, preferred_element_type=f32,
    )
    return shifted, step, log_decay, sums * LOG2E


def forward_kernel(
    proj_ref, taps_ref, head_ref, skip_ref, rim_ref, init_ref,
    values_ref, prior_ref, final_ref, last_ref, state_ref, tail_ref,
):
    seg_len = proj_ref.shape[0]
    half = seg_len // 2

    @pl.when(pl.program_id(0) == 0)
    def _():
        state_ref[...] = init_ref[...]
        tail_ref[...] = rim_ref[...]

    def activated(begin):
        at = pl.ds(begin, LANES)
        total, _ = conv_parts(proj_ref[:, at], tail_ref[:, at], taps_ref[:, at])
        return total * jax.nn.sigmoid(total)

    b_low = activated(HALF).astype(bf16)
    b_turned = activated(HALF).T.astype(bf16)
    c_low = activated(HALF + STATE).astype(bf16)
    _, step, _, sums = step_terms(proj_ref[:, HALF + 2 * STATE :], head_ref, seg_len)
    sums_turned, step_turned = sums.T, step.T
    scores = dot(c_low, b_low, ((1,), (1,)))
    kept = lax.broadcasted_iota(jnp.int32, (half, half), 0) >= lax.broadcasted_iota(jnp.int32, (half, half), 1)
    first_scores = jnp.where(kept, scores[:half, :half], 0.0)
    later_scores = scores[half:, :half]
    second_scores = jnp.where(kept, scores[half:, half:], 0.0)
    low = low_half((seg_len, LANES))
    last_ref[...] = jnp.broadcast_to(sums[seg_len - 1 :], last_ref.shape)

    for pair in range(HEADS // 4):
        at = columns_of(pair)
        x_values = activated(pair * LANES)
        x_low = x_values.astype(bf16)
        sums_pair = pair_columns(sums, pair, low)
        last_pair = sums_pair[seg_len - 1 :]
        carry = jnp.exp2(last_pair - sums_pair) * pair_columns(step, pair, low)
        scaled_x = (carry * x_low.astype(f32)).astype(bf16)
        prior = state_ref[:, at]
        prior_low = prior.astype(bf16)
        prior_ref[0, :, at] = prior_low
        from_state = jnp.exp2(sums_pair) * dot(c_low, prior_low, ((1,), (0,)))
        state_ref[:, at] = jnp.exp2(last_pair) * prior + dot(b_turned, scaled_x, ((1,), (0,)))
        early, late = 0.0, 0.0
        for side in range(2):
            head = 2 * pair + side
            x_side = jnp.where(low if side == 0 else ~low, x_values, 0.0).astype(bf16)
            at_token = jnp.broadcast_to(sums[:, head : head + 1], (seg_len, half))
            at_source, source_step = sums_turned[head : head + 1], step_turned[head : head + 1]
            first = jnp.exp2(jnp.minimum(at_token[:half] - at_source[:, :half], 0.0)) * first_scores
            first = (first * source_step[:, :half]).astype(bf16)
            later = jnp.exp2(at_token[half:] - at_source[:, :half]) * later_scores
            later = (later * source_step[:, :half]).astype(bf16)
            second = jnp.exp2(jnp.minimum(at_token[half:] - at_source[:, half:], 0.0)) * second_scores
            second = (second * source_step[:, half:]).astype(bf16)
            early = early + dot(first, x_side[:half], ((1,), (0,)))
            late = late + dot(jnp.concatenate([later, second], axis=1), x_side, ((1,), (0,)))
        intra = jnp.concatenate([early, late], axis=0)
        values_ref[:, at] = intra + from_state + skip_ref[:, at] * x_values

    tail_ref[...] = proj_ref[seg_len - 8 :, : HALF + 2 * STATE]
    final_ref[...] = state_ref[...]


def full_block(shape):
    return pl.BlockSpec(shape, lambda *_: (0,) * len(shape))


def scan_forward(proj, taps, head, skip, rim, init, seg_len):
    segs = proj.shape[0] // seg_len
    wide = HALF + 2 * STATE
    return pl.pallas_call(
        forward_kernel,
        grid=(segs,),
        out_shape=(
            jax.ShapeDtypeStruct((proj.shape[0], HALF), f32),
            jax.ShapeDtypeStruct((segs, STATE, HALF), bf16),
            jax.ShapeDtypeStruct((STATE, HALF), f32),
            jax.ShapeDtypeStruct((segs * 8, LANES), f32),
        ),
        in_specs=[
            pl.BlockSpec((seg_len, proj.shape[1]), lambda i: (i, 0)),
            full_block((8, wide)),
            full_block((8, LANES)),
            full_block((1, HALF)),
            full_block((8, wide)),
            full_block((STATE, HALF)),
        ],
        out_specs=(
            pl.BlockSpec((seg_len, HALF), lambda i: (i, 0)),
            pl.BlockSpec((1, STATE, HALF), lambda i: (i, 0, 0)),
            full_block((STATE, HALF)),
            pl.BlockSpec((8, LANES), lambda i: (i, 0)),
        ),
        scratch_shapes=[pltpu.VMEM((STATE, HALF), f32), pltpu.VMEM((8, wide), f32)],
        compiler_params=pltpu.CompilerParams(
            dimension_semantics=("arbitrary",), vmem_limit_bytes=VMEM_LIMIT
        ),
        cost_estimate=LIGHT,
    )(proj, taps, head, skip, rim, init)


def split_dot(array, other):
    high = array.astype(bf16)
    rest = (array - high.astype(f32)).astype(bf16)
    return dot(high, other, ((1,), (0,))) + dot(rest, other, ((1,), (0,)))


def backward_kernel(
    group, proj_ref, before_ref, taps_ref, rim_ref, shared_ref, shared_before_ref, shared_taps_ref, shared_rim_ref,
    head_ref, skip_ref, heads_ref, end_ref, prior_ref, values_ref, grad_ref,
    grad_x_ref, grad_b_ref, grad_c_ref, grad_raw_ref, taps_grad_ref, skip_grad_ref, head_grad_ref, edge_ref, start_ref,
    later_ref, local_ref, scaled_ref, grad_state_ref, inner_ref, source_ref, carry_ref, decay_ref,
):
    seg_len = proj_ref.shape[0]
    half = seg_len // 2
    turn = pl.program_id(0)

    @pl.when(turn == 0)
    def _():
        later_ref[...] = end_ref[...]
        edge_ref[...] = jnp.zeros_like(edge_ref)
        taps_grad_ref[...] = jnp.zeros_like(taps_grad_ref)
        skip_grad_ref[...] = jnp.zeros_like(skip_grad_ref)
        head_grad_ref[...] = jnp.zeros_like(head_grad_ref)

    first_segment = turn == pl.num_programs(0) - 1

    def conv_at(at, current, ahead, taps, rim):
        before = jnp.where(first_segment, rim[:, at], ahead[:, at])
        return conv_parts(current[:, at], before, taps[:, at])

    def activated(begin):
        total, _ = conv_at(pl.ds(begin, LANES), shared_ref, shared_before_ref, shared_taps_ref, shared_rim_ref)
        return total * jax.nn.sigmoid(total)

    b_values = activated(0)
    c_values = activated(STATE)
    b_low, c_low, c_turned = b_values.astype(bf16), c_values.astype(bf16), c_values.T.astype(bf16)
    shifted, step, log_decay, sums = step_terms(shared_ref[:, 2 * STATE :], head_ref, seg_len)
    sums_turned = sums.T
    scores = dot(b_low, c_low, ((1,), (1,)))
    kept = lax.broadcasted_iota(jnp.int32, (half, half), 0) <= lax.broadcasted_iota(jnp.int32, (half, half), 1)
    first_scores = jnp.where(kept, scores[:half, :half], 0.0)
    later_scores = scores[:half, half:]
    second_scores = jnp.where(kept, scores[half:, half:], 0.0)
    low = low_half((seg_len, LANES))
    first_grad, later_grad, second_grad = 0.0, 0.0, 0.0

    pairs = grad_ref.shape[1] // LANES
    for pair in range(pairs):
        at = columns_of(pair)
        total, seen = conv_at(at, proj_ref, before_ref, taps_ref, rim_ref)
        sigmoid = jax.nn.sigmoid(total)
        x_values = total * sigmoid
        x_low = x_values.astype(bf16)
        x_wide = x_low.astype(f32)
        sums_pair = pair_columns(sums, group * pairs + pair, low)
        step_pair = pair_columns(step, group * pairs + pair, low)
        last_pair = sums_pair[seg_len - 1 :]
        gap = jnp.exp2(last_pair - sums_pair)
        scaled_ref[:, at] = (gap * step_pair * x_wide).astype(bf16)
        grad_values = grad_ref[:, at]
        grad_state_ref[:, at] = (grad_values * jnp.exp2(sums_pair)).astype(bf16)
        later = later_ref[:, at]
        later_low = later.astype(bf16)
        local_ref[:, at] = later_low
        prior = prior_ref[0, :, at]
        decay_ref[:, at] = jnp.broadcast_to(
            jnp.sum(later * prior.astype(f32), axis=0, keepdims=True), (8, LANES)
        )
        grad_prior = dot(c_turned, grad_state_ref[:, at], ((1,), (0,)))
        later_ref[:, at] = jnp.exp2(last_pair) * later + grad_prior
        grad_scaled = dot(b_low, later_low, ((1,), (0,)))
        stepped = (step_pair * x_wide).astype(bf16)
        early, late = 0.0, 0.0
        for side in range(2):
            head = 2 * (group * pairs + pair) + side
            grad_low = jnp.where(low if side == 0 else ~low, grad_values, 0.0).astype(bf16)
            at_source = jnp.broadcast_to(sums[:, head : head + 1], (seg_len, half))
            at_token = sums_turned[head : head + 1]
            grad_weights = dot(stepped, grad_low, ((1,), (1,)))
            first = jnp.exp2(jnp.minimum(at_token[:, :half] - at_source[:half], 0.0))
            after = jnp.exp2(at_token[:, half:] - at_source[:half])
            second = jnp.exp2(jnp.minimum(at_token[:, half:] - at_source[half:], 0.0))
            first_grad = first_grad + first * grad_weights[:half, :half]
            later_grad = later_grad + after * grad_weights[:half, half:]
            second_grad = second_grad + second * grad_weights[half:, half:]
            upper = jnp.concatenate([first * first_scores, after * later_scores], axis=1).astype(bf16)
            early = early + dot(upper, grad_low, ((1,), (0,)))
            late = late + dot((second * second_scores).astype(bf16), grad_low[half:], ((1,), (0,)))
        inner = jnp.concatenate([early, late], axis=0)
        skip = skip_ref[:, at]
        skip_grad_ref[:, at] += jnp.sum(grad_values * x_values, axis=0, keepdims=True)
        inner_ref[:, at] = grad_values * (values_ref[:, at] - skip * x_values)
        source_ref[:, at] = x_wide * inner
        carry_ref[:, at] = x_wide * grad_scaled
        grad_x = skip * grad_values + step_pair * (inner + gap * grad_scaled)
        grad_total = grad_x * (sigmoid * (1.0 + total * (1.0 - sigmoid)))
        for k in range(CONV):
            taps_grad_ref[k : k + 1, at] += jnp.sum(grad_total * seen[k], axis=0, keepdims=True)
        taps_grad_ref[CONV : CONV + 1, at] += jnp.sum(grad_total, axis=0, keepdims=True)
        extended = jnp.concatenate([grad_total, edge_ref[:, at]], axis=0)
        edge_ref[:, at] = grad_total[:8]
        taps = taps_ref[:, at]
        grad_conv = taps[CONV - 1 : CONV] * grad_total
        for k in range(CONV - 1):
            grad_conv = grad_conv + taps[k : k + 1] * extended[CONV - 1 - k : CONV - 1 - k + seg_len]
        grad_x_ref[:, at] = grad_conv.astype(bf16)

    heads = heads_ref[...]
    tail = jnp.exp2(sums[seg_len - 1 :] - sums)
    source_grad = split_dot(source_ref[...], heads)
    step_grad = source_grad + tail * split_dot(carry_ref[...], heads)
    used = step * step_grad
    sum_grad = split_dot(inner_ref[...], heads) - used
    at_last = jnp.sum(used - step * source_grad, axis=0, keepdims=True)
    at_last = at_last + split_dot(decay_ref[...], heads)[:1] * jnp.exp2(sums[seg_len - 1 :])
    is_last = lax.broadcasted_iota(jnp.int32, (seg_len, LANES), 0) == seg_len - 1
    sum_grad = sum_grad + jnp.where(is_last, at_last, 0.0)
    at_or_after = lax.broadcasted_iota(jnp.int32, (seg_len, seg_len), 0) <= lax.broadcasted_iota(
        jnp.int32, (seg_len, seg_len), 1
    )
    log_grad = lax.dot_general(
        jnp.where(at_or_after, 1.0, 0.0), sum_grad, (((1,), (0,)), ((), ())),
        precision=lax.Precision.HIGHEST, preferred_element_type=f32,
    )
    grad_raw = (step_grad + head_ref[0:1] * log_grad) * jax.nn.sigmoid(shifted)
    grad_raw_ref[...] = grad_raw
    head_grad_ref[0:1] += jnp.sum(log_grad * log_decay, axis=0, keepdims=True)
    head_grad_ref[1:2] += jnp.sum(grad_raw, axis=0, keepdims=True)

    first_low = jnp.where(kept, first_grad, 0.0)
    second_low = jnp.where(kept, second_grad, 0.0)
    grad_scores = jnp.concatenate(
        [
            jnp.concatenate([first_low, later_grad], axis=1),
            jnp.concatenate([jnp.zeros_like(first_low), second_low], axis=1),
        ],
        axis=0,
    )
    start_ref[...] = later_ref[...]
    grad_b_ref[...] = dot(scaled_ref[...], local_ref[...], ((1,), (1,))) + dot(
        grad_scores.astype(bf16), c_low, ((1,), (0,))
    )
    grad_c_ref[...] = dot(grad_state_ref[...], prior_ref[0], ((1,), (1,))) + dot(
        grad_scores.T.astype(bf16), b_low, ((1,), (0,))
    )


GROUPS = 1


def scan_backward(group, proj, taps, head, skip, rim, end, prior, values, grad_values, seg_len):
    length = proj.shape[0]
    segs = length // seg_len
    width, shared = HALF // GROUPS, proj.shape[1] - HALF
    channel = lax.broadcasted_iota(jnp.int32, (width, LANES), 0) // HEADDIM + group * width // HEADDIM
    heads = (channel == lax.broadcasted_iota(jnp.int32, (width, LANES), 1)).astype(bf16)
    back = lambda width, at=0: pl.BlockSpec((seg_len, width), lambda i: (segs - 1 - i, at))
    row_ahead = lambda i: jnp.maximum((segs - 1 - i) * (seg_len // 8) - 1, 0)
    ahead = lambda width, at: pl.BlockSpec((8, width), lambda i: (row_ahead(i), at))
    column = lambda rows, width, at: pl.BlockSpec((rows, width), lambda i: (0, at))
    both = HALF // shared
    taps, rim = jnp.pad(taps, ((0, 0), (0, shared - 2 * STATE))), jnp.pad(rim, ((0, 0), (0, shared - 2 * STATE)))
    return pl.pallas_call(
        lambda *refs: backward_kernel(group, *refs),
        grid=(segs,),
        out_shape=(
            jax.ShapeDtypeStruct((length, width), bf16),
            jax.ShapeDtypeStruct((length, STATE), f32),
            jax.ShapeDtypeStruct((length, STATE), f32),
            jax.ShapeDtypeStruct((length, LANES), f32),
            jax.ShapeDtypeStruct((8, width), f32),
            jax.ShapeDtypeStruct((1, width), f32),
            jax.ShapeDtypeStruct((8, LANES), f32),
            jax.ShapeDtypeStruct((8, width), f32),
            jax.ShapeDtypeStruct((STATE, width), f32),
        ),
        in_specs=[
            back(width, group),
            ahead(width, group),
            column(8, width, group),
            column(8, width, group),
            back(shared, both),
            ahead(shared, both),
            column(8, shared, both),
            column(8, shared, both),
            full_block((8, LANES)),
            column(1, width, group),
            full_block((width, LANES)),
            column(STATE, width, group),
            pl.BlockSpec((1, STATE, width), lambda i: (segs - 1 - i, 0, group)),
            back(width, group),
            back(width, group),
        ],
        out_specs=(
            back(width),
            back(STATE),
            back(STATE),
            back(LANES),
            full_block((8, width)),
            full_block((1, width)),
            full_block((8, LANES)),
            full_block((8, width)),
            full_block((STATE, width)),
        ),
        scratch_shapes=[
            pltpu.VMEM((STATE, width), f32),
            pltpu.VMEM((STATE, width), bf16),
            pltpu.VMEM((seg_len, width), bf16),
            pltpu.VMEM((seg_len, width), bf16),
            pltpu.VMEM((seg_len, width), f32),
            pltpu.VMEM((seg_len, width), f32),
            pltpu.VMEM((seg_len, width), f32),
            pltpu.VMEM((8, width), f32),
        ],
        compiler_params=pltpu.CompilerParams(
            dimension_semantics=("arbitrary",), vmem_limit_bytes=VMEM_LIMIT
        ),
        cost_estimate=LIGHT,
    )(proj, proj, taps, rim, proj, proj, taps, rim, head, skip, heads, end, prior, values, grad_values)


def half_kernel(transposed, count, core_ref, *refs):
    inputs, mine_ref, theirs_ref = refs[: 2 * count], refs[-2], refs[-1]
    total = refs[2 * count][...] if len(refs) > 2 * count + 2 else 0.0
    for left, right in zip(inputs[:count], inputs[count:]):
        total = total + dot(left[...], right[...], ((1,), (1 if transposed else 0,)))
    half = total.shape[0] // 2
    first = core_ref[0] == 0
    mine_ref[0] = jnp.where(first, total[:half], total[half:])
    theirs_ref[0] = jnp.where(first, total[half:], total[:half]).astype(bf16)


def half_products(core, terms, seg_len, width, transposed, base=()):
    length = terms[0][0].shape[0]
    left = [pl.BlockSpec((seg_len, array.shape[1]), lambda i, core: (i, 0)) for array, _, _ in terms]
    right = []
    for array, matrix, at in terms:
        if transposed:
            right.append(pl.BlockSpec((width, array.shape[1]), lambda i, core, at=at: (0, at(core[0]))))
        else:
            right.append(pl.BlockSpec(matrix.shape, lambda i, core: (0, 0)))
    depth = sum(array.shape[1] for array, _, _ in terms)
    mine, theirs = pl.pallas_call(
        lambda *refs: half_kernel(transposed, len(terms), *refs),
        grid_spec=pltpu.PrefetchScalarGridSpec(
            num_scalar_prefetch=1,
            grid=(length // seg_len,),
            in_specs=left + right + [pl.BlockSpec((seg_len, width), lambda i, core: (i, 0)) for _ in base],
            out_specs=[pl.BlockSpec((1, seg_len // 2, width), lambda i, core: (i, 0, 0))] * 2,
        ),
        out_shape=(
            jax.ShapeDtypeStruct((length // seg_len, seg_len // 2, width), f32),
            jax.ShapeDtypeStruct((length // seg_len, seg_len // 2, width), bf16),
        ),
        compiler_params=pltpu.CompilerParams(dimension_semantics=("arbitrary",), vmem_limit_bytes=VMEM_LIMIT),
        cost_estimate=LIGHT,
    )(core.reshape(1).astype(jnp.int32), *[array for array, _, _ in terms], *[matrix for _, matrix, _ in terms], *base)
    return mine, theirs


def shared_kernel(core_ref, proj_ref, rim_ref, taps_ref, b_ref, c_ref, other_ref, grad_ref, taps_grad_ref, edge_ref):
    total, seen = conv_parts(proj_ref[...], rim_ref[...], taps_ref[...])
    sigmoid = jax.nn.sigmoid(total)
    grad_total = jnp.where(core_ref[0] == 0, b_ref[...], c_ref[...]) + other_ref[...]
    grad_total = grad_total * (sigmoid * (1.0 + total * (1.0 - sigmoid)))
    sums = [jnp.sum(grad_total * part, axis=0, keepdims=True) for part in seen]
    sums = sums + [jnp.sum(grad_total, axis=0, keepdims=True), jnp.zeros((8 - CONV - 1, LANES), f32)]
    taps_grad_ref[...] = jnp.concatenate(sums, axis=0)
    edge_ref[...] = grad_total[:8]
    taps = taps_ref[...]
    extended = jnp.concatenate([grad_total, jnp.zeros((8, LANES), f32)], axis=0)
    grad_conv = taps[CONV - 1 : CONV] * grad_total
    for k in range(CONV - 1):
        grad_conv = grad_conv + taps[k : k + 1] * extended[CONV - 1 - k : CONV - 1 - k + grad_total.shape[0]]
    grad_ref[...] = grad_conv.astype(bf16)


def shared_backward(core, proj, rim, taps, grad_b, grad_c, other):
    length = proj.shape[0]
    picked = lambda rows: pl.BlockSpec((rows, LANES), lambda i, core: (0, HALF // LANES + core[0]))
    whole = lambda rows: pl.BlockSpec((rows, LANES), lambda i, core: (0, 0))
    return pl.pallas_call(
        shared_kernel,
        grid_spec=pltpu.PrefetchScalarGridSpec(
            num_scalar_prefetch=1,
            grid=(1,),
            in_specs=[picked(length), picked(8), picked(8), whole(length), whole(length), whole(length)],
            out_specs=(whole(length), whole(8), whole(8)),
        ),
        out_shape=(
            jax.ShapeDtypeStruct((length, LANES), bf16),
            jax.ShapeDtypeStruct((8, LANES), f32),
            jax.ShapeDtypeStruct((8, LANES), f32),
        ),
        compiler_params=pltpu.CompilerParams(vmem_limit_bytes=VMEM_LIMIT),
        cost_estimate=LIGHT,
    )(core.reshape(1).astype(jnp.int32), proj, rim, taps, grad_b, grad_c, other)


def per_device(hidden_in, cotangent, in_proj, out_proj, conv_params, pre_gain, gated_gain, head_params):
    chips, line = lax.axis_size("chip"), lax.axis_size("seg")
    core, place = lax.axis_index("core"), lax.axis_index("seg")
    rows, model_width = in_proj.shape[0], hidden_in.shape[2]
    heads = HEADS // 2

    conv_width, gain_width = conv_params.shape[1], gated_gain.shape[0]
    used = HALF + 2 * STATE + heads
    spare = -used % LANES
    small = jnp.zeros((rows, spare), bf16)
    small = small.at[: CONV + 1, :conv_width].set(conv_params)
    small = small.at[CONV + 1, :rows].set(pre_gain)
    small = small.at[CONV + 2, :gain_width].set(gated_gain)

    def conv_side(which):
        return jnp.concatenate(
            [
                own_columns(in_proj[:, INNER : 2 * INNER], which),
                in_proj[:, 2 * INNER : INNER + XBC],
                own_columns(in_proj[:, INNER + XBC :], which),
                small,
            ],
            axis=1,
        )

    def gate_side(which):
        return own_columns(in_proj[:, :INNER], which)

    conv_swap = to_partner(conv_side(1 - core))
    conv_block = in_core_order(conv_side(core), conv_swap, core, 0)
    conv_z = gather_first(conv_block)
    gate_swap = to_partner(gate_side(1 - core))
    gate_block = in_core_order(gate_side(core), gate_swap, core, 0)
    rest_block = jnp.stack([gate_block.reshape(2 * rows, HALF), out_proj])
    conv_z, hidden_in, rest_block = tie(conv_z, hidden_in, rest_block)
    conv_2 = gather_next(conv_z, 1)
    hidden_half = whole_sequence(hidden_in, core, place)
    conv_2, hidden_half, rest_block = tie(conv_2, hidden_half, rest_block)
    conv_last = gather_next(conv_2, 2)
    rest_z = gather_step(rest_block, 2)
    hidden_other = to_partner(hidden_half)
    conv_last, hidden_other = tie(conv_last, hidden_other)
    parts = list(zip(ORDERS, column_parts(conv_block.shape[-1]), conv_last))
    conv_all = whole_matrices([(conv_block.shape, True, parts)])[0].reshape(model_width, -1)

    small_all = conv_all.reshape(chips, 2, line, rows, -1)[..., used:].astype(f32)
    taps_full = small_all[..., : CONV + 1, :conv_width].transpose(3, 0, 1, 2, 4).reshape(CONV + 1, XBC)
    taps = jnp.concatenate([own_columns(taps_full[:, :INNER], core), taps_full[:, INNER:]], axis=1)
    gain_pre = small_all[..., CONV + 1, :rows].reshape(model_width)
    gain_gate = lax.dynamic_index_in_dim(
        small_all[..., CONV + 2, :gain_width], core, axis=1, keepdims=False
    ).reshape(HALF)
    params = own_columns(head_params, core)

    seg_len = 2 * hidden_half.shape[1]
    tokens = SEGS * seg_len
    normed, normed_turned = normed_tokens(core, hidden_half, hidden_other, gain_pre, rows)
    projected = dot(normed, conv_all, ((1,), (0,)))
    projected, rest_z = tie(projected, rest_z)
    cut = column_parts(HALF)
    gate_2, out_2 = (gather_next([[piece[at][..., begin:end] for piece in rest_z] for begin, end in cut], 1) for at in range(2))

    taps = jnp.pad(taps, ((0, 8 - CONV - 1), (0, 0)))
    head = jnp.pad(jnp.stack([-jnp.exp(params[0]), params[1]]), ((0, 6), (0, LANES - heads)))
    skip = jnp.repeat(params[2], HEADDIM).reshape(1, HALF)
    wide = HALF + 2 * STATE
    rim = borrowed(projected[tokens - 8 :, :wide], 1)
    nothing = jnp.zeros((STATE, HALF), f32)
    values, prior, final, last = scan_forward(projected, taps, head, skip, rim, nothing, seg_len)
    if line > SEGS:
        last = jnp.sum(last.reshape(SEGS, 8, LANES)[:, 0, :heads], axis=0)
        decay = jnp.repeat(jnp.exp2(last), HEADDIM)
        begin = entering(decay, final, 1)
        values, prior, _, _ = scan_forward(projected, taps, head, skip, rim, begin, seg_len)

    values, gate_2, out_2, cotangent = tie(values, gate_2, out_2, cotangent)
    gate_last = gather_next(gate_2, 2)
    cot_half = whole_sequence(cotangent, core, place)
    gate_last, out_2 = tie(gate_last, out_2)
    out_last = gather_next(out_2, 2)
    cot = in_core_order(cot_half, to_partner(cot_half), core, 1)
    upstream = cot.reshape(tokens, model_width)
    gate_matrix = whole_matrices([(gate_block.shape, True, list(zip(ORDERS, cut, gate_last)))])[0].reshape(model_width, HALF)
    gate_input = dot(normed, gate_matrix, ((1,), (0,)))

    silu_gate = jax.nn.silu(gate_input)
    gated = values * silu_gate
    squares = jnp.sum(gated * gated, axis=1)
    squares_other = to_partner(squares)
    scale = lax.rsqrt((squares + squares_other) / INNER + epsilon)[:, None]
    mixed, mixed_turned = mixed_tokens(gated, scale, gain_gate, seg_len)
    by_owner = lambda grad: grad.astype(bf16).reshape(chip_dims() + (-1, grad.shape[1]))
    out_grad = by_owner(dot(mixed_turned, upstream, ((1,), (0,))))
    out_grad, out_last = tie(out_grad, out_last)
    out_first = reduce_first(out_grad)
    out_matrix = whole_matrices([(out_proj.shape, False, list(zip(ORDERS, cut, out_last)))])[0].reshape(HALF, model_width)
    grad_mixed = dot(upstream, out_matrix, ((1,), (1,)))
    unit = gated * scale
    gain_grad = grad_mixed * gain_gate
    along = jnp.sum(gain_grad * unit, axis=1)
    along_other = to_partner(along)
    along_other, mixed = tie(along_other, mixed)
    along = ((along + along_other) / INNER)[:, None]
    gate_gain_grad = jnp.sum(grad_mixed * unit, axis=0)
    grad_gated = scale * (gain_grad - unit * along)
    grad_values = grad_gated * silu_gate
    sigmoid = jax.nn.sigmoid(gate_input)
    grad_gate = (grad_gated * values * (sigmoid * (1.0 + gate_input * (1.0 - sigmoid)))).astype(bf16)
    branch, branch_sent = half_products(core, [(mixed, out_matrix, None)], seg_len, model_width, False)
    branch_other = to_partner(branch_sent)
    grad_gate, grad_values, out_got, branch_other = tie(grad_gate, grad_values, arrivals(out_first), branch_other)
    out_second = reduce_second(arrived(out_first, out_got))
    hidden_out = back_to_owner(
        (hidden_half.astype(f32) + branch + branch_other.astype(f32)).astype(bf16), core, place
    )
    gate_grad = by_owner(dot(normed_turned, grad_gate, ((1,), (0,))))
    gate_grad, out_got, grad_values = tie(gate_grad, arrivals(out_second), grad_values)
    out_second = arrived(out_second, out_got)
    gate_first = reduce_first(gate_grad)
    out_third = reduce_third(out_second)
    scan = lambda later: scan_backward(
        0, projected, taps, head, skip, rim, later, prior, values, grad_values, seg_len
    )
    if line > SEGS:
        nothing = entering(decay, scan(nothing)[-1], -1)
    back = scan(nothing)
    back, gate_got, out_got, hidden_out, grad_gate = tie(
        back, arrivals(gate_first), arrivals(out_third), hidden_out, grad_gate
    )
    out_third = arrived(out_third, out_got)
    gate_second = reduce_second(arrived(gate_first, gate_got))
    grad_x, grad_b, grad_c, grad_raw, x_taps_grad, skip_grad, head_sums, x_edge, _ = back
    grad_x = spilled(grad_x, x_edge, taps[:, :HALF])
    x_first = reduce_first(by_owner(dot(normed_turned, grad_x, ((1,), (0,)))))
    head_grad = jnp.concatenate([head_sums[:2, :heads], skip_grad.reshape(1, heads, HEADDIM).sum(axis=2)])

    other = to_partner(jnp.where(core == 0, grad_c, grad_b))
    grad_state, state_taps_grad, state_edge = shared_backward(core, projected, rim, taps, grad_b, grad_c, other)
    grad_state = spilled(grad_state, state_edge, lax.dynamic_slice_in_dim(taps, HALF + core * STATE, STATE, axis=1))
    grad_raw = grad_raw.astype(bf16)
    grad_rest = jnp.concatenate([grad_state, grad_raw], axis=1)
    rest_grad = by_owner(dot(normed_turned, grad_rest, ((1,), (0,))))
    rest_first = reduce_first(rest_grad)
    state_taps_grad = state_taps_grad[: CONV + 1]
    none = jnp.zeros_like(state_taps_grad)
    taps_grad = jnp.concatenate(
        [
            x_taps_grad[: CONV + 1],
            jnp.where(core == 0, state_taps_grad, none),
            jnp.where(core == 0, none, state_taps_grad),
        ],
        axis=1,
    )
    def spread_own(array):
        width = array.shape[-1] // chips
        parted = array.reshape(array.shape[:-1] + (chips, 1, width))
        none = jnp.zeros_like(parted)
        both = jnp.where(
            core == 0,
            jnp.concatenate([parted, none], axis=-2),
            jnp.concatenate([none, parted], axis=-2),
        )
        return both.reshape(array.shape[:-1] + (2 * array.shape[-1],))

    taps_all = jnp.concatenate([spread_own(taps_grad[:, :HALF]), taps_grad[:, HALF:]], axis=1)
    taps_all = taps_all.reshape(CONV + 1, chips, 2, line, conv_width).transpose(1, 3, 2, 0, 4)
    gate_all = spread_own(gate_gain_grad).reshape(chips, 2, line, gain_width).transpose(0, 2, 1, 3)
    head_all = jnp.broadcast_to(spread_own(head_grad).reshape(-1), (chips, line, 2, 3 * HEADS))
    small_grads = jnp.concatenate(
        [
            taps_all.reshape(chips, line, 2, -1),
            gate_all,
            head_all,
        ],
        axis=3,
    )
    count = small_grads.shape[3]
    small_grads = small_grads.reshape(chip_dims() + (2, count))
    base = dot(grad_gate, gate_matrix, ((1,), (1,)))
    base, x_got, rest_got, gate_got = tie(base, arrivals(x_first), arrivals(rest_first), arrivals(gate_second))
    conv_first = [
        ([jnp.concatenate([total(x_kept + x_new), total(rest_kept + rest_new)], axis=-1)], [])
        for (x_kept, x_new), (rest_kept, rest_new) in zip(arrived(x_first, x_got), arrived(rest_first, rest_got))
    ]
    conv_second = reduce_second(conv_first)
    gate_third = reduce_third(arrived(gate_second, gate_got))
    terms = [
        (grad_x, conv_all, lambda core: 0),
        (grad_state, conv_all, lambda core: HALF // LANES + core),
        (grad_raw, conv_all, lambda core: (HALF + 2 * STATE) // LANES),
    ]
    grad_normed, sent_normed = half_products(core, terms, seg_len, model_width, True, (base,))
    sent_normed, conv_got, small_grads = tie(sent_normed, arrivals(conv_second), small_grads)
    other_normed = to_partner(sent_normed)
    conv_third = reduce_third(arrived(conv_second, conv_got))
    wide_hidden = hidden_half.astype(f32)
    hidden_scale = lax.rsqrt(jnp.mean(wide_hidden * wide_hidden, axis=-1, keepdims=True) + epsilon)
    grad_normed = (grad_normed + other_normed.astype(f32)) * gain_pre
    hidden_unit = wide_hidden * hidden_scale
    along = jnp.mean(grad_normed * hidden_unit, axis=-1, keepdims=True)
    grad_hidden = hidden_scale * (grad_normed - hidden_unit * along)
    grad_in = (cot_half.astype(f32) + grad_hidden).astype(bf16)
    grad_in = back_to_owner(grad_in, core, place)

    small_third = reduce_third(reduce_second(reduce_first(small_grads, f32), f32), f32)
    grad_in, conv_got, small_got, gate_got = tie(
        grad_in, arrivals(conv_third), arrivals(small_third), arrivals(gate_third)
    )
    gate_third = arrived(gate_third, gate_got)
    small_share = reduce_end(arrived(small_third, small_got))
    conv_third = arrived(conv_third, conv_got)
    out_share = reduce_end(out_third).reshape(-1, model_width)
    paired = lambda third: reduce_end(third).astype(bf16).reshape(2, rows, -1)
    gate_share, conv_share = paired(gate_third), paired(conv_third)

    def mine_and_partner(share):
        keep = lax.dynamic_index_in_dim(share, core, axis=0, keepdims=False)
        give = lax.dynamic_index_in_dim(share, 1 - core, axis=0, keepdims=False)
        return keep, to_partner(give)

    keep, got = mine_and_partner(small_share)
    small_total = keep + got
    taps_end = (CONV + 1) * conv_width
    taps_share = small_total[:taps_end].reshape(CONV + 1, conv_width)
    gain_share = small_total[taps_end : taps_end + gain_width]
    head_total = small_total[taps_end + gain_width :].reshape(3, HEADS)

    def interleave(mine, theirs):
        width = mine.shape[1] // chips
        both = in_core_order(mine.reshape(rows, chips, width), theirs.reshape(rows, chips, width), core, 2)
        return both.reshape(rows, -1)

    keep_gate, got_gate = mine_and_partner(gate_share)
    (_, x_cut), _ = column_parts(HALF)
    (_, state_cut), _ = column_parts(STATE + LANES)
    both = x_cut + state_cut
    conv_share = jnp.concatenate(
        [conv_share[..., :x_cut], conv_share[..., both : both + HALF - x_cut], conv_share[..., x_cut:both], conv_share[..., both + HALF - x_cut :]],
        axis=-1,
    )
    keep, got = mine_and_partner(conv_share)
    state_end = HALF + STATE
    in_share = jnp.concatenate(
        [
            interleave(keep_gate, got_gate),
            interleave(keep[:, :HALF], got[:, :HALF]),
            in_core_order(keep[:, HALF:state_end], got[:, HALF:state_end], core, 1).reshape(rows, -1),
            interleave(keep[:, state_end : state_end + heads], got[:, state_end : state_end + heads]),
        ],
        axis=1,
    ).astype(f32)
    pre_share = jnp.sum(in_proj.astype(f32) * in_share, axis=1) / pre_gain.astype(f32)
    return (hidden_out, grad_in, in_share, out_share, taps_share, pre_share, gain_share, head_total)


def solution(mesh):
    devices = mesh.devices
    cores = Mesh(devices.reshape(devices.shape[0] // 2, 2, devices.shape[1]), ("chip", "core", "seg"))
    dp, both = ("chip", "core"), ("chip", "core", "seg")
    tokens = P(dp, "seg", None)
    return jax.shard_map(
        per_device,
        mesh=cores,
        in_specs=(tokens, tokens, P(both, None), P(both, None), P(None, both), P(both), P(both), P()),
        out_specs=(tokens, tokens, P(both, None), P(both, None), P(None, both), P(both), P(both), P()),
        check_vma=False,
    )
```

```python
import jax
import jax.numpy as jnp
from jax import lax
from jax.experimental import pallas as pl
from jax.experimental.pallas import tpu as pltpu
from jax.sharding import Mesh
from jax.sharding import PartitionSpec as P

HEADS = 48
HEADDIM = 64
STATE = 128
CONV = 4
INNER = 3072
XBC = 3328
HALF = INNER // 2
LANES = 128
SEGS = 4
LIGHT = pl.CostEstimate(flops=1024, bytes_accessed=1024, transcendentals=0)
VMEM_LIMIT = 48 * 1024 * 1024
LOG2E = 1.4426950408889634

epsilon = 1e-05
f32 = jnp.float32
bf16 = jnp.bfloat16


def own_columns(array, core):
    chips = lax.axis_size("chip")
    width = array.shape[-1] // (2 * chips)
    parted = array.reshape(array.shape[:-1] + (chips, 2, width))
    picked = lax.dynamic_index_in_dim(parted, core, axis=parted.ndim - 2, keepdims=False)
    return picked.reshape(array.shape[:-1] + (chips * width,))


def to_partner(array):
    return lax.ppermute(array, "core", [(0, 1), (1, 0)])


def in_core_order(mine, theirs, core, axis):
    first = jnp.where(core == 0, mine, theirs)
    second = jnp.where(core == 0, theirs, mine)
    return jnp.stack([first, second], axis=axis)


def chip_dims():
    return (lax.axis_size("chip") // 2, 2, lax.axis_size("seg"))


def chip_place():
    chip = lax.axis_index("chip")
    return (chip // 2, chip % 2, lax.axis_index("seg"))


def moved(array, dim, by):
    sizes = chip_dims()
    index = lambda at: (at[0] * sizes[1] + at[1]) * sizes[2] + at[2]
    pairs = []
    for a in range(sizes[0]):
        for b in range(sizes[1]):
            for z in range(sizes[2]):
                to = [a, b, z]
                to[dim] = (to[dim] + by) % sizes[dim]
                pairs.append((index((a, b, z)), index(to)))
    return lax.ppermute(array, ("chip", "seg"), pairs)


def tie(*values):
    return lax.optimization_barrier(values)


ORDERS = ((2, 0, 1), (2, 1, 0))


def column_parts(width):
    cut = -(-(width // 2) // LANES) * LANES
    return ((0, cut), (cut, width))


def gather_step(data, dim):
    return [data] + [moved(data, dim, by) for by in range(1, chip_dims()[dim])]


def gather_first(block):
    pieces = gather_step(block, 2)
    return [[piece[..., begin:end] for piece in pieces] for begin, end in column_parts(block.shape[-1])]


def gather_next(parts, step):
    return [gather_step(jnp.stack(part), order[step]) for order, part in zip(ORDERS, parts)]


def placed_kernel(plan, outs, place_ref, *refs):
    sources, targets, sems = refs[: -outs - 1], refs[-outs - 1 : -1], refs[-1]
    copies = []
    for source, lead, at, columns, paired, out in plan:
        spot = [lax.rem(place_ref[dim] + (size - back), size) for dim, (back, size) in enumerate(at)]
        target = targets[out].at[spot[0], spot[1]]
        target = target.at[:, spot[2]] if paired else target.at[spot[2]]
        target = target.at[..., pl.ds(*columns)]
        copies.append(pltpu.make_async_copy(sources[source].at[lead], target, sems.at[len(copies)]))
    for copy in copies:
        copy.start()
    for copy in copies:
        copy.wait()


def whole_matrices(jobs):
    sizes = chip_dims()
    plan, sources, shapes = [], [], []
    for out, (shape, paired, parts) in enumerate(jobs):
        for order, (begin, end), part in parts:
            for back_last, piece in enumerate(part):
                for back_mid in range(sizes[order[1]]):
                    for back_first in range(sizes[order[0]]):
                        at = [None] * 3
                        at[order[2]] = (back_last, sizes[order[2]])
                        at[order[1]] = (back_mid, sizes[order[1]])
                        at[order[0]] = (back_first, sizes[order[0]])
                        plan.append((len(sources), (back_mid, back_first), at, (begin, end - begin), paired, out))
                sources.append(piece.reshape(piece.shape[:2] + shape[:-1] + piece.shape[-1:]))
        shapes.append(sizes[:2] + (2, sizes[2]) + shape[1:] if paired else sizes + shape)
    anywhere = pl.BlockSpec(memory_space=pl.ANY)
    total = sum(source.size for source in sources)
    return pl.pallas_call(
        lambda *refs: placed_kernel(plan, len(jobs), *refs),
        out_shape=[jax.ShapeDtypeStruct(shape, bf16) for shape in shapes],
        in_specs=[pl.BlockSpec(memory_space=pltpu.SMEM)] + [anywhere] * len(sources),
        out_specs=[pl.BlockSpec(memory_space=pltpu.VMEM)] * len(jobs),
        scratch_shapes=[pltpu.SemaphoreType.DMA((len(plan),))],
        compiler_params=pltpu.CompilerParams(vmem_limit_bytes=VMEM_LIMIT),
        cost_estimate=LIGHT,
    )(jnp.stack(chip_place()).astype(jnp.int32), *sources)


def total(terms):
    result = terms[0].astype(f32)
    for term in terms[1:]:
        result = result + term.astype(f32)
    return result


def reduce_send(terms, axis, dim, wire):
    place, size = chip_place()[dim], chip_dims()[dim]
    pick = lambda at: [lax.dynamic_index_in_dim(term, at, axis=axis, keepdims=False) for term in terms]
    received = [moved(total(pick((place + by) % size)).astype(wire), dim, by) for by in range(1, size)]
    return pick(place), received


def reduce_first(partial, wire=bf16):
    (begin, cut), (_, end) = column_parts(partial.shape[-1])
    return [
        reduce_send([partial[..., begin:cut]], 1, 1, wire),
        reduce_send([partial[..., cut:end]], 0, 0, wire),
    ]


def reduce_second(first, wire=bf16):
    return [
        reduce_send(first[0][0] + first[0][1], 0, 0, wire),
        reduce_send(first[1][0] + first[1][1], 0, 1, wire),
    ]


def reduce_third(second, wire=bf16):
    joined = jnp.concatenate([total(kept + received) for kept, received in second], axis=-1)
    return [reduce_send([joined], 0, 2, wire)]


def reduce_end(third):
    return total(third[0][0] + third[0][1])


def arrivals(parts):
    return [received for _, received in parts]


def arrived(parts, received):
    return [(kept, new) for (kept, _), new in zip(parts, received)]


def line_perm(turn, back):
    line = lax.axis_size("seg")
    parts = line // SEGS
    pairs = []
    for core in range(2):
        for place in range(line):
            piece = (place % SEGS) ^ turn
            half, index = divmod(piece, 2)
            source = core * line + place
            target = half * line + (2 * core + index) * parts + place // SEGS
            pairs.append((target, source) if back else (source, target))
    return pairs


def whole_sequence(array, core, place):
    parts = lax.axis_size("seg") // SEGS
    half = array.shape[1] // 2
    pieces = array.reshape(2, 2, half, -1).transpose(1, 0, 2, 3).reshape(4, half, -1)
    mine = place % SEGS
    target = 2 * core + (place // parts) % 2
    got = []
    for turn in range(4):
        piece = lax.dynamic_index_in_dim(pieces, mine ^ turn, axis=0, keepdims=False)
        got.append(lax.ppermute(piece, ("core", "seg"), line_perm(turn, False)))
    got = jnp.stack(got)
    return jnp.stack([lax.dynamic_index_in_dim(got, target ^ k, axis=0, keepdims=False) for k in range(4)])


def back_to_owner(ordered, core, place):
    parts = lax.axis_size("seg") // SEGS
    half = ordered.shape[1]
    mine = place % SEGS
    target = 2 * core + (place // parts) % 2
    got = []
    for turn in range(4):
        piece = lax.dynamic_index_in_dim(ordered, target ^ turn, axis=0, keepdims=False)
        got.append(lax.ppermute(piece, ("core", "seg"), line_perm(turn, True)))
    got = jnp.stack(got)
    pieces = jnp.stack([lax.dynamic_index_in_dim(got, mine ^ k, axis=0, keepdims=False) for k in range(4)])
    return pieces.reshape(2, 2, half, -1).transpose(1, 0, 2, 3).reshape(2, 2 * half, -1)


def part_pairs(step):
    line = lax.axis_size("seg")
    parts = line // SEGS
    return [(i, i + step) for i in range(line) if 0 <= i + step < line and i // parts == (i + step) // parts]


def entering(decay, state, step):
    parts = lax.axis_size("seg") // SEGS
    total = jnp.zeros_like(state)
    for _ in range(parts - 1):
        total = lax.ppermute(decay * total + state, "seg", part_pairs(step))
    return total


def borrowed(array, step):
    parts = lax.axis_size("seg") // SEGS
    if parts == 1:
        return jnp.zeros_like(array)
    return lax.ppermute(array, "seg", part_pairs(step))


def spilled(grad, edge, taps):
    if lax.axis_size("seg") == SEGS:
        return grad
    edge = borrowed(edge, -1)
    spill = jnp.stack(
        [
            sum(taps[k] * edge[CONV - 1 - k - early] for k in range(CONV - early))
            for early in range(CONV - 1, 0, -1)
        ]
    )
    at = grad.shape[0] - CONV + 1
    return grad.at[at:].set((grad[at:].astype(f32) + spill).astype(bf16))


def dot(a, b, contract):
    return lax.dot_general(a, b, (contract, ((), ())), preferred_element_type=f32)


def normed_kernel(slabs, core_ref, mine_ref, other_ref, gain_ref, normed_ref, turned_ref):
    mine, other = mine_ref[0], other_ref[0]
    first = core_ref[0] == 0
    hidden = jnp.concatenate([jnp.where(first, mine, other), jnp.where(first, other, mine)], axis=0).astype(f32)
    scale = lax.rsqrt(jnp.mean(hidden * hidden, axis=1, keepdims=True) + epsilon)
    normed = hidden * scale * gain_ref[...]
    normed_ref[...] = normed.astype(bf16)
    turned = normed.T.astype(bf16)
    for to, at, size in slabs:
        turned_ref[to : to + size] = turned[at : at + size]


def normed_tokens(core, mine, other, gain, rows):
    segs, half, width = mine.shape
    a, b, z = chip_dims()
    group = 2 * z * rows
    inside = rows % 16 == 0
    slabs = [(0, 0, width)]
    if inside:
        slabs = [
            (chip * group + (at * 2 + core_at) * rows, chip * group + (core_at * z + at) * rows, rows)
            for chip in range(a * b)
            for core_at in range(2)
            for at in range(z)
        ]
    normed, turned = pl.pallas_call(
        lambda *refs: normed_kernel(slabs, *refs),
        grid_spec=pltpu.PrefetchScalarGridSpec(
            num_scalar_prefetch=1,
            grid=(segs,),
            in_specs=[
                pl.BlockSpec((1, half, width), lambda i, core: (i, 0, 0)),
                pl.BlockSpec((1, half, width), lambda i, core: (i, 0, 0)),
                pl.BlockSpec((1, width), lambda i, core: (0, 0)),
            ],
            out_specs=(
                pl.BlockSpec((2 * half, width), lambda i, core: (i, 0)),
                pl.BlockSpec((width, 2 * half), lambda i, core: (0, i)),
            ),
        ),
        out_shape=(
            jax.ShapeDtypeStruct((segs * 2 * half, width), bf16),
            jax.ShapeDtypeStruct((width, segs * 2 * half), bf16),
        ),
        compiler_params=pltpu.CompilerParams(dimension_semantics=("arbitrary",), vmem_limit_bytes=VMEM_LIMIT),
        cost_estimate=LIGHT,
    )(core.reshape(1).astype(jnp.int32), mine, other, gain.reshape(1, width))
    if not inside:
        turned = turned.reshape(a, b, 2, z, rows, -1).transpose(0, 1, 3, 2, 4, 5).reshape(turned.shape)
    return normed, turned


def mixed_kernel(gated_ref, scale_ref, gain_ref, mixed_ref, turned_ref):
    mixed = gated_ref[...] * scale_ref[...] * gain_ref[...]
    mixed_ref[...] = mixed.astype(bf16)
    turned_ref[...] = mixed.T.astype(bf16)


def mixed_tokens(gated, scale, gain, seg_len):
    length, width = gated.shape
    return pl.pallas_call(
        mixed_kernel,
        grid=(length // seg_len,),
        in_specs=[
            pl.BlockSpec((seg_len, width), lambda i: (i, 0)),
            pl.BlockSpec((seg_len, 1), lambda i: (i, 0)),
            pl.BlockSpec((1, width), lambda i: (0, 0)),
        ],
        out_specs=(
            pl.BlockSpec((seg_len, width), lambda i: (i, 0)),
            pl.BlockSpec((width, seg_len), lambda i: (0, i)),
        ),
        out_shape=(
            jax.ShapeDtypeStruct((length, width), bf16),
            jax.ShapeDtypeStruct((width, length), bf16),
        ),
        compiler_params=pltpu.CompilerParams(dimension_semantics=("arbitrary",), vmem_limit_bytes=VMEM_LIMIT),
        cost_estimate=LIGHT,
    )(gated, scale, gain.reshape(1, width))


def columns_of(pair):
    return pl.ds(pair * LANES, LANES)


def low_half(shape):
    return lax.broadcasted_iota(jnp.int32, shape, len(shape) - 1) < HEADDIM


def pair_columns(array, pair, low):
    rows = array.shape[0]
    first = jnp.broadcast_to(array[:, 2 * pair : 2 * pair + 1], (rows, LANES))
    second = jnp.broadcast_to(array[:, 2 * pair + 1 : 2 * pair + 2], (rows, LANES))
    return jnp.where(low, first, second)


def conv_parts(current, before, taps):
    rows = current.shape[0]
    padded = jnp.concatenate([before, current], axis=0)
    seen = [padded[8 - CONV + 1 + k : 8 - CONV + 1 + k + rows] for k in range(CONV - 1)] + [current]
    total = taps[CONV : CONV + 1]
    for k in range(CONV):
        total = total + taps[k : k + 1] * seen[k]
    return total, seen


def step_terms(raw, head, seg_len):
    shifted = raw + head[1:2]
    step = jnp.maximum(shifted, 0.0) + jnp.log1p(jnp.exp(-jnp.abs(shifted)))
    log_decay = step * head[0:1]
    at_or_before = lax.broadcasted_iota(jnp.int32, (seg_len, seg_len), 0) >= lax.broadcasted_iota(
        jnp.int32, (seg_len, seg_len), 1
    )
    sums = lax.dot_general(
        jnp.where(at_or_before, 1.0, 0.0), log_decay, (((1,), (0,)), ((), ())),
        precision=lax.Precision.HIGHEST, preferred_element_type=f32,
    )
    return shifted, step, log_decay, sums * LOG2E


def forward_kernel(
    proj_ref, taps_ref, head_ref, skip_ref, rim_ref, init_ref,
    values_ref, prior_ref, final_ref, last_ref, state_ref, tail_ref,
):
    seg_len = proj_ref.shape[0]
    half = seg_len // 2

    @pl.when(pl.program_id(0) == 0)
    def _():
        state_ref[...] = init_ref[...]
        tail_ref[...] = rim_ref[...]

    def activated(begin):
        at = pl.ds(begin, LANES)
        total, _ = conv_parts(proj_ref[:, at], tail_ref[:, at], taps_ref[:, at])
        return total * jax.nn.sigmoid(total)

    b_low = activated(HALF).astype(bf16)
    b_turned = activated(HALF).T.astype(bf16)
    c_low = activated(HALF + STATE).astype(bf16)
    _, step, _, sums = step_terms(proj_ref[:, HALF + 2 * STATE :], head_ref, seg_len)
    sums_turned, step_turned = sums.T, step.T
    scores = dot(c_low, b_low, ((1,), (1,)))
    kept = lax.broadcasted_iota(jnp.int32, (half, half), 0) >= lax.broadcasted_iota(jnp.int32, (half, half), 1)
    first_scores = jnp.where(kept, scores[:half, :half], 0.0)
    later_scores = scores[half:, :half]
    second_scores = jnp.where(kept, scores[half:, half:], 0.0)
    low = low_half((seg_len, LANES))
    last_ref[...] = jnp.broadcast_to(sums[seg_len - 1 :], last_ref.shape)

    for pair in range(HEADS // 4):
        at = columns_of(pair)
        x_values = activated(pair * LANES)
        x_low = x_values.astype(bf16)
        sums_pair = pair_columns(sums, pair, low)
        last_pair = sums_pair[seg_len - 1 :]
        carry = jnp.exp2(last_pair - sums_pair) * pair_columns(step, pair, low)
        scaled_x = (carry * x_low.astype(f32)).astype(bf16)
        prior = state_ref[:, at]
        prior_low = prior.astype(bf16)
        prior_ref[0, :, at] = prior_low
        from_state = jnp.exp2(sums_pair) * dot(c_low, prior_low, ((1,), (0,)))
        state_ref[:, at] = jnp.exp2(last_pair) * prior + dot(b_turned, scaled_x, ((1,), (0,)))
        early, late = 0.0, 0.0
        for side in range(2):
            head = 2 * pair + side
            x_side = jnp.where(low if side == 0 else ~low, x_values, 0.0).astype(bf16)
            at_token = jnp.broadcast_to(sums[:, head : head + 1], (seg_len, half))
            at_source, source_step = sums_turned[head : head + 1], step_turned[head : head + 1]
            first = jnp.exp2(jnp.minimum(at_token[:half] - at_source[:, :half], 0.0)) * first_scores
            first = (first * source_step[:, :half]).astype(bf16)
            later = jnp.exp2(at_token[half:] - at_source[:, :half]) * later_scores
            later = (later * source_step[:, :half]).astype(bf16)
            second = jnp.exp2(jnp.minimum(at_token[half:] - at_source[:, half:], 0.0)) * second_scores
            second = (second * source_step[:, half:]).astype(bf16)
            early = early + dot(first, x_side[:half], ((1,), (0,)))
            late = late + dot(jnp.concatenate([later, second], axis=1), x_side, ((1,), (0,)))
        intra = jnp.concatenate([early, late], axis=0)
        values_ref[:, at] = intra + from_state + skip_ref[:, at] * x_values

    tail_ref[...] = proj_ref[seg_len - 8 :, : HALF + 2 * STATE]
    final_ref[...] = state_ref[...]


def full_block(shape):
    return pl.BlockSpec(shape, lambda *_: (0,) * len(shape))


def scan_forward(proj, taps, head, skip, rim, init, seg_len):
    segs = proj.shape[0] // seg_len
    wide = HALF + 2 * STATE
    return pl.pallas_call(
        forward_kernel,
        grid=(segs,),
        out_shape=(
            jax.ShapeDtypeStruct((proj.shape[0], HALF), f32),
            jax.ShapeDtypeStruct((segs, STATE, HALF), bf16),
            jax.ShapeDtypeStruct((STATE, HALF), f32),
            jax.ShapeDtypeStruct((segs * 8, LANES), f32),
        ),
        in_specs=[
            pl.BlockSpec((seg_len, proj.shape[1]), lambda i: (i, 0)),
            full_block((8, wide)),
            full_block((8, LANES)),
            full_block((1, HALF)),
            full_block((8, wide)),
            full_block((STATE, HALF)),
        ],
        out_specs=(
            pl.BlockSpec((seg_len, HALF), lambda i: (i, 0)),
            pl.BlockSpec((1, STATE, HALF), lambda i: (i, 0, 0)),
            full_block((STATE, HALF)),
            pl.BlockSpec((8, LANES), lambda i: (i, 0)),
        ),
        scratch_shapes=[pltpu.VMEM((STATE, HALF), f32), pltpu.VMEM((8, wide), f32)],
        compiler_params=pltpu.CompilerParams(
            dimension_semantics=("arbitrary",), vmem_limit_bytes=VMEM_LIMIT
        ),
        cost_estimate=LIGHT,
    )(proj, taps, head, skip, rim, init)


def split_dot(array, other):
    high = array.astype(bf16)
    rest = (array - high.astype(f32)).astype(bf16)
    return dot(high, other, ((1,), (0,))) + dot(rest, other, ((1,), (0,)))


def backward_kernel(
    group, proj_ref, before_ref, taps_ref, rim_ref, shared_ref, shared_before_ref, shared_taps_ref, shared_rim_ref,
    head_ref, skip_ref, heads_ref, end_ref, prior_ref, values_ref, grad_ref,
    grad_x_ref, grad_b_ref, grad_c_ref, grad_raw_ref, taps_grad_ref, skip_grad_ref, head_grad_ref, edge_ref, start_ref,
    later_ref, local_ref, scaled_ref, grad_state_ref, inner_ref, source_ref, carry_ref, decay_ref,
):
    seg_len = proj_ref.shape[0]
    half = seg_len // 2
    turn = pl.program_id(0)

    @pl.when(turn == 0)
    def _():
        later_ref[...] = end_ref[...]
        edge_ref[...] = jnp.zeros_like(edge_ref)
        taps_grad_ref[...] = jnp.zeros_like(taps_grad_ref)
        skip_grad_ref[...] = jnp.zeros_like(skip_grad_ref)
        head_grad_ref[...] = jnp.zeros_like(head_grad_ref)

    first_segment = turn == pl.num_programs(0) - 1

    def conv_at(at, current, ahead, taps, rim):
        before = jnp.where(first_segment, rim[:, at], ahead[:, at])
        return conv_parts(current[:, at], before, taps[:, at])

    def activated(begin):
        total, _ = conv_at(pl.ds(begin, LANES), shared_ref, shared_before_ref, shared_taps_ref, shared_rim_ref)
        return total * jax.nn.sigmoid(total)

    b_values = activated(0)
    c_values = activated(STATE)
    b_low, c_low, c_turned = b_values.astype(bf16), c_values.astype(bf16), c_values.T.astype(bf16)
    shifted, step, log_decay, sums = step_terms(shared_ref[:, 2 * STATE :], head_ref, seg_len)
    sums_turned = sums.T
    scores = dot(b_low, c_low, ((1,), (1,)))
    kept = lax.broadcasted_iota(jnp.int32, (half, half), 0) <= lax.broadcasted_iota(jnp.int32, (half, half), 1)
    first_scores = jnp.where(kept, scores[:half, :half], 0.0)
    later_scores = scores[:half, half:]
    second_scores = jnp.where(kept, scores[half:, half:], 0.0)
    low = low_half((seg_len, LANES))
    first_grad, later_grad, second_grad = 0.0, 0.0, 0.0

    pairs = grad_ref.shape[1] // LANES
    for pair in range(pairs):
        at = columns_of(pair)
        total, seen = conv_at(at, proj_ref, before_ref, taps_ref, rim_ref)
        sigmoid = jax.nn.sigmoid(total)
        x_values = total * sigmoid
        x_low = x_values.astype(bf16)
        x_wide = x_low.astype(f32)
        sums_pair = pair_columns(sums, group * pairs + pair, low)
        step_pair = pair_columns(step, group * pairs + pair, low)
        last_pair = sums_pair[seg_len - 1 :]
        gap = jnp.exp2(last_pair - sums_pair)
        scaled_ref[:, at] = (gap * step_pair * x_wide).astype(bf16)
        grad_values = grad_ref[:, at]
        grad_state_ref[:, at] = (grad_values * jnp.exp2(sums_pair)).astype(bf16)
        later = later_ref[:, at]
        later_low = later.astype(bf16)
        local_ref[:, at] = later_low
        prior = prior_ref[0, :, at]
        decay_ref[:, at] = jnp.broadcast_to(
            jnp.sum(later * prior.astype(f32), axis=0, keepdims=True), (8, LANES)
        )
        grad_prior = dot(c_turned, grad_state_ref[:, at], ((1,), (0,)))
        later_ref[:, at] = jnp.exp2(last_pair) * later + grad_prior
        grad_scaled = dot(b_low, later_low, ((1,), (0,)))
        stepped = (step_pair * x_wide).astype(bf16)
        early, late = 0.0, 0.0
        for side in range(2):
            head = 2 * (group * pairs + pair) + side
            grad_low = jnp.where(low if side == 0 else ~low, grad_values, 0.0).astype(bf16)
            at_source = jnp.broadcast_to(sums[:, head : head + 1], (seg_len, half))
            at_token = sums_turned[head : head + 1]
            grad_weights = dot(stepped, grad_low, ((1,), (1,)))
            first = jnp.exp2(jnp.minimum(at_token[:, :half] - at_source[:half], 0.0))
            after = jnp.exp2(at_token[:, half:] - at_source[:half])
            second = jnp.exp2(jnp.minimum(at_token[:, half:] - at_source[half:], 0.0))
            first_grad = first_grad + first * grad_weights[:half, :half]
            later_grad = later_grad + after * grad_weights[:half, half:]
            second_grad = second_grad + second * grad_weights[half:, half:]
            upper = jnp.concatenate([first * first_scores, after * later_scores], axis=1).astype(bf16)
            early = early + dot(upper, grad_low, ((1,), (0,)))
            late = late + dot((second * second_scores).astype(bf16), grad_low[half:], ((1,), (0,)))
        inner = jnp.concatenate([early, late], axis=0)
        skip = skip_ref[:, at]
        skip_grad_ref[:, at] += jnp.sum(grad_values * x_values, axis=0, keepdims=True)
        inner_ref[:, at] = grad_values * (values_ref[:, at] - skip * x_values)
        source_ref[:, at] = x_wide * inner
        carry_ref[:, at] = x_wide * grad_scaled
        grad_x = skip * grad_values + step_pair * (inner + gap * grad_scaled)
        grad_total = grad_x * (sigmoid * (1.0 + total * (1.0 - sigmoid)))
        for k in range(CONV):
            taps_grad_ref[k : k + 1, at] += jnp.sum(grad_total * seen[k], axis=0, keepdims=True)
        taps_grad_ref[CONV : CONV + 1, at] += jnp.sum(grad_total, axis=0, keepdims=True)
        extended = jnp.concatenate([grad_total, edge_ref[:, at]], axis=0)
        edge_ref[:, at] = grad_total[:8]
        taps = taps_ref[:, at]
        grad_conv = taps[CONV - 1 : CONV] * grad_total
        for k in range(CONV - 1):
            grad_conv = grad_conv + taps[k : k + 1] * extended[CONV - 1 - k : CONV - 1 - k + seg_len]
        grad_x_ref[:, at] = grad_conv.astype(bf16)

    heads = heads_ref[...]
    tail = jnp.exp2(sums[seg_len - 1 :] - sums)
    source_grad = split_dot(source_ref[...], heads)
    step_grad = source_grad + tail * split_dot(carry_ref[...], heads)
    used = step * step_grad
    sum_grad = split_dot(inner_ref[...], heads) - used
    at_last = jnp.sum(used - step * source_grad, axis=0, keepdims=True)
    at_last = at_last + split_dot(decay_ref[...], heads)[:1] * jnp.exp2(sums[seg_len - 1 :])
    is_last = lax.broadcasted_iota(jnp.int32, (seg_len, LANES), 0) == seg_len - 1
    sum_grad = sum_grad + jnp.where(is_last, at_last, 0.0)
    at_or_after = lax.broadcasted_iota(jnp.int32, (seg_len, seg_len), 0) <= lax.broadcasted_iota(
        jnp.int32, (seg_len, seg_len), 1
    )
    log_grad = lax.dot_general(
        jnp.where(at_or_after, 1.0, 0.0), sum_grad, (((1,), (0,)), ((), ())),
        precision=lax.Precision.HIGHEST, preferred_element_type=f32,
    )
    grad_raw = (step_grad + head_ref[0:1] * log_grad) * jax.nn.sigmoid(shifted)
    grad_raw_ref[...] = grad_raw
    head_grad_ref[0:1] += jnp.sum(log_grad * log_decay, axis=0, keepdims=True)
    head_grad_ref[1:2] += jnp.sum(grad_raw, axis=0, keepdims=True)

    first_low = jnp.where(kept, first_grad, 0.0)
    second_low = jnp.where(kept, second_grad, 0.0)
    grad_scores = jnp.concatenate(
        [
            jnp.concatenate([first_low, later_grad], axis=1),
            jnp.concatenate([jnp.zeros_like(first_low), second_low], axis=1),
        ],
        axis=0,
    )
    start_ref[...] = later_ref[...]
    grad_b_ref[...] = dot(scaled_ref[...], local_ref[...], ((1,), (1,))) + dot(
        grad_scores.astype(bf16), c_low, ((1,), (0,))
    )
    grad_c_ref[...] = dot(grad_state_ref[...], prior_ref[0], ((1,), (1,))) + dot(
        grad_scores.T.astype(bf16), b_low, ((1,), (0,))
    )


GROUPS = 1


def scan_backward(group, proj, taps, head, skip, rim, end, prior, values, grad_values, seg_len):
    length = proj.shape[0]
    segs = length // seg_len
    width, shared = HALF // GROUPS, proj.shape[1] - HALF
    channel = lax.broadcasted_iota(jnp.int32, (width, LANES), 0) // HEADDIM + group * width // HEADDIM
    heads = (channel == lax.broadcasted_iota(jnp.int32, (width, LANES), 1)).astype(bf16)
    back = lambda width, at=0: pl.BlockSpec((seg_len, width), lambda i: (segs - 1 - i, at))
    row_ahead = lambda i: jnp.maximum((segs - 1 - i) * (seg_len // 8) - 1, 0)
    ahead = lambda width, at: pl.BlockSpec((8, width), lambda i: (row_ahead(i), at))
    column = lambda rows, width, at: pl.BlockSpec((rows, width), lambda i: (0, at))
    both = HALF // shared
    taps, rim = jnp.pad(taps, ((0, 0), (0, shared - 2 * STATE))), jnp.pad(rim, ((0, 0), (0, shared - 2 * STATE)))
    return pl.pallas_call(
        lambda *refs: backward_kernel(group, *refs),
        grid=(segs,),
        out_shape=(
            jax.ShapeDtypeStruct((length, width), bf16),
            jax.ShapeDtypeStruct((length, STATE), f32),
            jax.ShapeDtypeStruct((length, STATE), f32),
            jax.ShapeDtypeStruct((length, LANES), f32),
            jax.ShapeDtypeStruct((8, width), f32),
            jax.ShapeDtypeStruct((1, width), f32),
            jax.ShapeDtypeStruct((8, LANES), f32),
            jax.ShapeDtypeStruct((8, width), f32),
            jax.ShapeDtypeStruct((STATE, width), f32),
        ),
        in_specs=[
            back(width, group),
            ahead(width, group),
            column(8, width, group),
            column(8, width, group),
            back(shared, both),
            ahead(shared, both),
            column(8, shared, both),
            column(8, shared, both),
            full_block((8, LANES)),
            column(1, width, group),
            full_block((width, LANES)),
            column(STATE, width, group),
            pl.BlockSpec((1, STATE, width), lambda i: (segs - 1 - i, 0, group)),
            back(width, group),
            back(width, group),
        ],
        out_specs=(
            back(width),
            back(STATE),
            back(STATE),
            back(LANES),
            full_block((8, width)),
            full_block((1, width)),
            full_block((8, LANES)),
            full_block((8, width)),
            full_block((STATE, width)),
        ),
        scratch_shapes=[
            pltpu.VMEM((STATE, width), f32),
            pltpu.VMEM((STATE, width), bf16),
            pltpu.VMEM((seg_len, width), bf16),
            pltpu.VMEM((seg_len, width), bf16),
            pltpu.VMEM((seg_len, width), f32),
            pltpu.VMEM((seg_len, width), f32),
            pltpu.VMEM((seg_len, width), f32),
            pltpu.VMEM((8, width), f32),
        ],
        compiler_params=pltpu.CompilerParams(
            dimension_semantics=("arbitrary",), vmem_limit_bytes=VMEM_LIMIT
        ),
        cost_estimate=LIGHT,
    )(proj, proj, taps, rim, proj, proj, taps, rim, head, skip, heads, end, prior, values, grad_values)


def half_kernel(transposed, count, core_ref, *refs):
    inputs, mine_ref, theirs_ref = refs[: 2 * count], refs[-2], refs[-1]
    total = refs[2 * count][...] if len(refs) > 2 * count + 2 else 0.0
    for left, right in zip(inputs[:count], inputs[count:]):
        total = total + dot(left[...], right[...], ((1,), (1 if transposed else 0,)))
    half = total.shape[0] // 2
    first = core_ref[0] == 0
    mine_ref[0] = jnp.where(first, total[:half], total[half:])
    theirs_ref[0] = jnp.where(first, total[half:], total[:half]).astype(bf16)


def half_products(core, terms, seg_len, width, transposed, base=()):
    length = terms[0][0].shape[0]
    left = [pl.BlockSpec((seg_len, array.shape[1]), lambda i, core: (i, 0)) for array, _, _ in terms]
    right = []
    for array, matrix, at in terms:
        if transposed:
            right.append(pl.BlockSpec((width, array.shape[1]), lambda i, core, at=at: (0, at(core[0]))))
        else:
            right.append(pl.BlockSpec(matrix.shape, lambda i, core: (0, 0)))
    depth = sum(array.shape[1] for array, _, _ in terms)
    mine, theirs = pl.pallas_call(
        lambda *refs: half_kernel(transposed, len(terms), *refs),
        grid_spec=pltpu.PrefetchScalarGridSpec(
            num_scalar_prefetch=1,
            grid=(length // seg_len,),
            in_specs=left + right + [pl.BlockSpec((seg_len, width), lambda i, core: (i, 0)) for _ in base],
            out_specs=[pl.BlockSpec((1, seg_len // 2, width), lambda i, core: (i, 0, 0))] * 2,
        ),
        out_shape=(
            jax.ShapeDtypeStruct((length // seg_len, seg_len // 2, width), f32),
            jax.ShapeDtypeStruct((length // seg_len, seg_len // 2, width), bf16),
        ),
        compiler_params=pltpu.CompilerParams(dimension_semantics=("arbitrary",), vmem_limit_bytes=VMEM_LIMIT),
        cost_estimate=LIGHT,
    )(core.reshape(1).astype(jnp.int32), *[array for array, _, _ in terms], *[matrix for _, matrix, _ in terms], *base)
    return mine, theirs


def shared_kernel(core_ref, proj_ref, rim_ref, taps_ref, b_ref, c_ref, other_ref, grad_ref, taps_grad_ref, edge_ref):
    total, seen = conv_parts(proj_ref[...], rim_ref[...], taps_ref[...])
    sigmoid = jax.nn.sigmoid(total)
    grad_total = jnp.where(core_ref[0] == 0, b_ref[...], c_ref[...]) + other_ref[...]
    grad_total = grad_total * (sigmoid * (1.0 + total * (1.0 - sigmoid)))
    sums = [jnp.sum(grad_total * part, axis=0, keepdims=True) for part in seen]
    sums = sums + [jnp.sum(grad_total, axis=0, keepdims=True), jnp.zeros((8 - CONV - 1, LANES), f32)]
    taps_grad_ref[...] = jnp.concatenate(sums, axis=0)
    edge_ref[...] = grad_total[:8]
    taps = taps_ref[...]
    extended = jnp.concatenate([grad_total, jnp.zeros((8, LANES), f32)], axis=0)
    grad_conv = taps[CONV - 1 : CONV] * grad_total
    for k in range(CONV - 1):
        grad_conv = grad_conv + taps[k : k + 1] * extended[CONV - 1 - k : CONV - 1 - k + grad_total.shape[0]]
    grad_ref[...] = grad_conv.astype(bf16)


def shared_backward(core, proj, rim, taps, grad_b, grad_c, other):
    length = proj.shape[0]
    picked = lambda rows: pl.BlockSpec((rows, LANES), lambda i, core: (0, HALF // LANES + core[0]))
    whole = lambda rows: pl.BlockSpec((rows, LANES), lambda i, core: (0, 0))
    return pl.pallas_call(
        shared_kernel,
        grid_spec=pltpu.PrefetchScalarGridSpec(
            num_scalar_prefetch=1,
            grid=(1,),
            in_specs=[picked(length), picked(8), picked(8), whole(length), whole(length), whole(length)],
            out_specs=(whole(length), whole(8), whole(8)),
        ),
        out_shape=(
            jax.ShapeDtypeStruct((length, LANES), bf16),
            jax.ShapeDtypeStruct((8, LANES), f32),
            jax.ShapeDtypeStruct((8, LANES), f32),
        ),
        compiler_params=pltpu.CompilerParams(vmem_limit_bytes=VMEM_LIMIT),
        cost_estimate=LIGHT,
    )(core.reshape(1).astype(jnp.int32), proj, rim, taps, grad_b, grad_c, other)


def per_device(hidden_in, cotangent, in_proj, out_proj, conv_params, pre_gain, gated_gain, head_params):
    chips, line = lax.axis_size("chip"), lax.axis_size("seg")
    core, place = lax.axis_index("core"), lax.axis_index("seg")
    rows, model_width = in_proj.shape[0], hidden_in.shape[2]
    heads = HEADS // 2

    conv_width, gain_width = conv_params.shape[1], gated_gain.shape[0]
    used = HALF + 2 * STATE + heads
    spare = -used % LANES
    small = jnp.zeros((rows, spare), bf16)
    small = small.at[: CONV + 1, :conv_width].set(conv_params)
    small = small.at[CONV + 1, :rows].set(pre_gain)
    small = small.at[CONV + 2, :gain_width].set(gated_gain)

    def conv_side(which):
        return jnp.concatenate(
            [
                own_columns(in_proj[:, INNER : 2 * INNER], which),
                in_proj[:, 2 * INNER : INNER + XBC],
                own_columns(in_proj[:, INNER + XBC :], which),
                small,
            ],
            axis=1,
        )

    def gate_side(which):
        return own_columns(in_proj[:, :INNER], which)

    conv_swap = to_partner(conv_side(1 - core))
    conv_block = in_core_order(conv_side(core), conv_swap, core, 0)
    conv_z = gather_first(conv_block)
    gate_swap = to_partner(gate_side(1 - core))
    gate_block = in_core_order(gate_side(core), gate_swap, core, 0)
    conv_z, hidden_in, gate_block = tie(conv_z, hidden_in, gate_block)
    conv_2 = gather_next(conv_z, 1)
    hidden_half = whole_sequence(hidden_in, core, place)
    conv_2, hidden_half, gate_block = tie(conv_2, hidden_half, gate_block)
    conv_last = gather_next(conv_2, 2)
    gate_z = gather_first(gate_block)
    hidden_other = to_partner(hidden_half)
    conv_last, hidden_other, gate_z, cotangent = tie(conv_last, hidden_other, gate_z, cotangent)
    gate_2 = gather_next(gate_z, 1)
    cot_half = whole_sequence(cotangent, core, place)
    parts = list(zip(ORDERS, column_parts(conv_block.shape[-1]), conv_last))
    conv_all = whole_matrices([(conv_block.shape, True, parts)])[0].reshape(model_width, -1)

    small_all = conv_all.reshape(chips, 2, line, rows, -1)[..., used:].astype(f32)
    taps_full = small_all[..., : CONV + 1, :conv_width].transpose(3, 0, 1, 2, 4).reshape(CONV + 1, XBC)
    taps = jnp.concatenate([own_columns(taps_full[:, :INNER], core), taps_full[:, INNER:]], axis=1)
    gain_pre = small_all[..., CONV + 1, :rows].reshape(model_width)
    gain_gate = lax.dynamic_index_in_dim(
        small_all[..., CONV + 2, :gain_width], core, axis=1, keepdims=False
    ).reshape(HALF)
    params = own_columns(head_params, core)

    seg_len = 2 * hidden_half.shape[1]
    tokens = SEGS * seg_len
    normed, normed_turned = normed_tokens(core, hidden_half, hidden_other, gain_pre, rows)
    projected = dot(normed, conv_all, ((1,), (0,)))
    projected, gate_2, cot_half, out_proj = tie(projected, gate_2, cot_half, out_proj)
    gate_last = gather_next(gate_2, 2)
    out_z = gather_first(out_proj)
    cot_other = to_partner(cot_half)

    taps = jnp.pad(taps, ((0, 8 - CONV - 1), (0, 0)))
    head = jnp.pad(jnp.stack([-jnp.exp(params[0]), params[1]]), ((0, 6), (0, LANES - heads)))
    skip = jnp.repeat(params[2], HEADDIM).reshape(1, HALF)
    wide = HALF + 2 * STATE
    rim = borrowed(projected[tokens - 8 :, :wide], 1)
    nothing = jnp.zeros((STATE, HALF), f32)
    values, prior, final, last = scan_forward(projected, taps, head, skip, rim, nothing, seg_len)
    if line > SEGS:
        last = jnp.sum(last.reshape(SEGS, 8, LANES)[:, 0, :heads], axis=0)
        decay = jnp.repeat(jnp.exp2(last), HEADDIM)
        begin = entering(decay, final, 1)
        values, prior, _, _ = scan_forward(projected, taps, head, skip, rim, begin, seg_len)

    values, gate_last, out_z, cot_other = tie(values, gate_last, out_z, cot_other)
    out_2 = gather_next(out_z, 1)
    cot = in_core_order(cot_half, cot_other, core, 1)
    upstream = cot.reshape(tokens, model_width)
    cut = column_parts(HALF)
    gate_matrix = whole_matrices([(gate_block.shape, True, list(zip(ORDERS, cut, gate_last)))])[0].reshape(model_width, HALF)
    gate_input = dot(normed, gate_matrix, ((1,), (0,)))

    silu_gate = jax.nn.silu(gate_input)
    gated = values * silu_gate
    squares = jnp.sum(gated * gated, axis=1)
    squares_other = to_partner(squares)
    scale = lax.rsqrt((squares + squares_other) / INNER + epsilon)[:, None]
    scale, out_2 = tie(scale, out_2)
    out_last = gather_next(out_2, 2)
    mixed, mixed_turned = mixed_tokens(gated, scale, gain_gate, seg_len)
    by_owner = lambda grad: grad.astype(bf16).reshape(chip_dims() + (-1, grad.shape[1]))
    out_grad = by_owner(dot(mixed_turned, upstream, ((1,), (0,))))
    out_grad, out_last = tie(out_grad, out_last)
    out_first = reduce_first(out_grad)
    out_matrix = whole_matrices([(out_proj.shape, False, list(zip(ORDERS, cut, out_last)))])[0].reshape(HALF, model_width)
    branch, branch_sent = half_products(core, [(mixed, out_matrix, None)], seg_len, model_width, False)
    branch_sent, upstream = tie(branch_sent, upstream)
    branch_other = to_partner(branch_sent)
    grad_mixed = dot(upstream, out_matrix, ((1,), (1,)))
    unit = gated * scale
    gain_grad = grad_mixed * gain_gate
    along = jnp.sum(gain_grad * unit, axis=1)
    along_other = to_partner(along)
    along_other, branch_other = tie(along_other, branch_other)
    hidden_out = back_to_owner(
        (hidden_half.astype(f32) + branch + branch_other.astype(f32)).astype(bf16), core, place
    )
    along = ((along + along_other) / INNER)[:, None]
    gate_gain_grad = jnp.sum(grad_mixed * unit, axis=0)
    grad_gated = scale * (gain_grad - unit * along)
    grad_values = grad_gated * silu_gate
    sigmoid = jax.nn.sigmoid(gate_input)
    grad_gate = (grad_gated * values * (sigmoid * (1.0 + gate_input * (1.0 - sigmoid)))).astype(bf16)
    grad_gate, grad_values, out_got = tie(grad_gate, grad_values, arrivals(out_first))
    out_second = reduce_second(arrived(out_first, out_got))
    gate_grad = by_owner(dot(normed_turned, grad_gate, ((1,), (0,))))
    gate_grad, out_got, grad_values, hidden_out = tie(gate_grad, arrivals(out_second), grad_values, hidden_out)
    out_second = arrived(out_second, out_got)
    gate_first = reduce_first(gate_grad)
    out_third = reduce_third(out_second)
    scan = lambda later: scan_backward(
        0, projected, taps, head, skip, rim, later, prior, values, grad_values, seg_len
    )
    if line > SEGS:
        nothing = entering(decay, scan(nothing)[-1], -1)
    back = scan(nothing)
    back, gate_got, out_got, grad_gate = tie(back, arrivals(gate_first), arrivals(out_third), grad_gate)
    out_third = arrived(out_third, out_got)
    gate_second = reduce_second(arrived(gate_first, gate_got))
    grad_x, grad_b, grad_c, grad_raw, x_taps_grad, skip_grad, head_sums, x_edge, _ = back
    grad_x = spilled(grad_x, x_edge, taps[:, :HALF])
    head_grad = jnp.concatenate([head_sums[:2, :heads], skip_grad.reshape(1, heads, HEADDIM).sum(axis=2)])

    other = to_partner(jnp.where(core == 0, grad_c, grad_b))
    grad_state, state_taps_grad, state_edge = shared_backward(core, projected, rim, taps, grad_b, grad_c, other)
    grad_state = spilled(grad_state, state_edge, lax.dynamic_slice_in_dim(taps, HALF + core * STATE, STATE, axis=1))
    grad_raw = grad_raw.astype(bf16)
    grad_proj = jnp.concatenate([grad_x, grad_state, grad_raw], axis=1)
    conv_grad = by_owner(dot(normed_turned, grad_proj, ((1,), (0,))))
    state_taps_grad = state_taps_grad[: CONV + 1]
    none = jnp.zeros_like(state_taps_grad)
    taps_grad = jnp.concatenate(
        [
            x_taps_grad[: CONV + 1],
            jnp.where(core == 0, state_taps_grad, none),
            jnp.where(core == 0, none, state_taps_grad),
        ],
        axis=1,
    )
    base = dot(grad_gate, gate_matrix, ((1,), (1,)))
    conv_grad, base, gate_got = tie(conv_grad, base, arrivals(gate_second))
    conv_first = reduce_first(conv_grad)
    gate_third = reduce_third(arrived(gate_second, gate_got))
    terms = [
        (grad_x, conv_all, lambda core: 0),
        (grad_state, conv_all, lambda core: HALF // LANES + core),
        (grad_raw, conv_all, lambda core: (HALF + 2 * STATE) // LANES),
    ]
    grad_normed, sent_normed = half_products(core, terms, seg_len, model_width, True, (base,))
    sent_normed, gate_got, taps_grad, gate_gain_grad, head_grad = tie(
        sent_normed, arrivals(gate_third), taps_grad, gate_gain_grad, head_grad
    )
    gate_third = arrived(gate_third, gate_got)
    other_normed = to_partner(sent_normed)
    wide_hidden = hidden_half.astype(f32)
    hidden_scale = lax.rsqrt(jnp.mean(wide_hidden * wide_hidden, axis=-1, keepdims=True) + epsilon)
    grad_normed = (grad_normed + other_normed.astype(f32)) * gain_pre
    hidden_unit = wide_hidden * hidden_scale
    along = jnp.mean(grad_normed * hidden_unit, axis=-1, keepdims=True)
    grad_hidden = hidden_scale * (grad_normed - hidden_unit * along)
    grad_in = (cot_half.astype(f32) + grad_hidden).astype(bf16)
    grad_in, conv_got = tie(grad_in, arrivals(conv_first))
    conv_second = reduce_second(arrived(conv_first, conv_got))
    grad_in = back_to_owner(grad_in, core, place)

    def spread_own(array):
        width = array.shape[-1] // chips
        parted = array.reshape(array.shape[:-1] + (chips, 1, width))
        none = jnp.zeros_like(parted)
        both = jnp.where(
            core == 0,
            jnp.concatenate([parted, none], axis=-2),
            jnp.concatenate([none, parted], axis=-2),
        )
        return both.reshape(array.shape[:-1] + (2 * array.shape[-1],))

    taps_all = jnp.concatenate([spread_own(taps_grad[:, :HALF]), taps_grad[:, HALF:]], axis=1)
    taps_all = taps_all.reshape(CONV + 1, chips, 2, line, conv_width).transpose(1, 3, 2, 0, 4)
    gate_all = spread_own(gate_gain_grad).reshape(chips, 2, line, gain_width).transpose(0, 2, 1, 3)
    head_all = jnp.broadcast_to(spread_own(head_grad).reshape(-1), (chips, line, 2, 3 * HEADS))
    small_grads = jnp.concatenate(
        [
            taps_all.reshape(chips, line, 2, -1),
            gate_all,
            head_all,
        ],
        axis=3,
    )
    count = small_grads.shape[3]
    small_grads = small_grads.reshape(chip_dims() + (2, count))
    small_second = reduce_second(reduce_first(small_grads, f32), f32)
    grad_in, conv_got, small_got = tie(grad_in, arrivals(conv_second), arrivals(small_second))
    conv_third = reduce_third(arrived(conv_second, conv_got))
    small_third = reduce_third(arrived(small_second, small_got), f32)
    small_share = reduce_end(small_third)
    out_share = reduce_end(out_third).reshape(-1, model_width)
    paired = lambda third: reduce_end(third).astype(bf16).reshape(2, rows, -1)
    gate_share, conv_share = paired(gate_third), paired(conv_third)

    def mine_and_partner(share):
        keep = lax.dynamic_index_in_dim(share, core, axis=0, keepdims=False)
        give = lax.dynamic_index_in_dim(share, 1 - core, axis=0, keepdims=False)
        return keep, to_partner(give)

    keep, got = mine_and_partner(small_share)
    small_total = keep + got
    taps_end = (CONV + 1) * conv_width
    taps_share = small_total[:taps_end].reshape(CONV + 1, conv_width)
    gain_share = small_total[taps_end : taps_end + gain_width]
    head_total = small_total[taps_end + gain_width :].reshape(3, HEADS)

    def interleave(mine, theirs):
        width = mine.shape[1] // chips
        both = in_core_order(mine.reshape(rows, chips, width), theirs.reshape(rows, chips, width), core, 2)
        return both.reshape(rows, -1)

    keep_gate, got_gate = mine_and_partner(gate_share)
    keep, got = mine_and_partner(conv_share)
    state_end = HALF + STATE
    in_share = jnp.concatenate(
        [
            interleave(keep_gate, got_gate),
            interleave(keep[:, :HALF], got[:, :HALF]),
            in_core_order(keep[:, HALF:state_end], got[:, HALF:state_end], core, 1).reshape(rows, -1),
            interleave(keep[:, state_end : state_end + heads], got[:, state_end : state_end + heads]),
        ],
        axis=1,
    ).astype(f32)
    pre_share = jnp.sum(in_proj.astype(f32) * in_share, axis=1) / pre_gain.astype(f32)
    return (hidden_out, grad_in, in_share, out_share, taps_share, pre_share, gain_share, head_total)


def solution(mesh):
    devices = mesh.devices
    cores = Mesh(devices.reshape(devices.shape[0] // 2, 2, devices.shape[1]), ("chip", "core", "seg"))
    dp, both = ("chip", "core"), ("chip", "core", "seg")
    tokens = P(dp, "seg", None)
    return jax.shard_map(
        per_device,
        mesh=cores,
        in_specs=(tokens, tokens, P(both, None), P(both, None), P(None, both), P(both), P(both), P()),
        out_specs=(tokens, tokens, P(both, None), P(both, None), P(None, both), P(both), P(both), P()),
        check_vma=False,
    )
```

```python
import jax
import jax.numpy as jnp
from jax import lax
from jax.experimental import pallas as pl
from jax.experimental.pallas import tpu as pltpu
from jax.sharding import Mesh
from jax.sharding import PartitionSpec as P

HEADS = 48
HEADDIM = 64
STATE = 128
CONV = 4
INNER = 3072
XBC = 3328
HALF = INNER // 2
LANES = 128
SEGS = 4
LIGHT = pl.CostEstimate(flops=1024, bytes_accessed=1024, transcendentals=0)
VMEM_LIMIT = 48 * 1024 * 1024
LOG2E = 1.4426950408889634

epsilon = 1e-05
f32 = jnp.float32
bf16 = jnp.bfloat16


def own_columns(array, core):
    chips = lax.axis_size("chip")
    width = array.shape[-1] // (2 * chips)
    parted = array.reshape(array.shape[:-1] + (chips, 2, width))
    picked = lax.dynamic_index_in_dim(parted, core, axis=parted.ndim - 2, keepdims=False)
    return picked.reshape(array.shape[:-1] + (chips * width,))


def to_partner(array):
    return lax.ppermute(array, "core", [(0, 1), (1, 0)])


def in_core_order(mine, theirs, core, axis):
    first = jnp.where(core == 0, mine, theirs)
    second = jnp.where(core == 0, theirs, mine)
    return jnp.stack([first, second], axis=axis)


def chip_dims():
    return (lax.axis_size("chip") // 2, 2, lax.axis_size("seg"))


def chip_place():
    chip = lax.axis_index("chip")
    return (chip // 2, chip % 2, lax.axis_index("seg"))


def moved(array, dim, by):
    sizes = chip_dims()
    index = lambda at: (at[0] * sizes[1] + at[1]) * sizes[2] + at[2]
    pairs = []
    for a in range(sizes[0]):
        for b in range(sizes[1]):
            for z in range(sizes[2]):
                to = [a, b, z]
                to[dim] = (to[dim] + by) % sizes[dim]
                pairs.append((index((a, b, z)), index(to)))
    return lax.ppermute(array, ("chip", "seg"), pairs)


def tie(*values):
    return lax.optimization_barrier(values)


ORDERS = ((2, 0, 1), (2, 1, 0))


def column_parts(width):
    cut = -(-(width // 2) // LANES) * LANES
    return ((0, cut), (cut, width))


def gather_step(data, dim):
    return [data] + [moved(data, dim, by) for by in range(1, chip_dims()[dim])]


def gather_first(block):
    pieces = gather_step(block, 2)
    return [[piece[..., begin:end] for piece in pieces] for begin, end in column_parts(block.shape[-1])]


def gather_next(parts, step):
    return [gather_step(jnp.stack(part), order[step]) for order, part in zip(ORDERS, parts)]


def placed_kernel(plan, outs, place_ref, *refs):
    sources, targets, sems = refs[: -outs - 1], refs[-outs - 1 : -1], refs[-1]
    copies = []
    for source, lead, at, columns, paired, out in plan:
        spot = [lax.rem(place_ref[dim] + (size - back), size) for dim, (back, size) in enumerate(at)]
        target = targets[out].at[spot[0], spot[1]]
        target = target.at[:, spot[2]] if paired else target.at[spot[2]]
        target = target.at[..., pl.ds(*columns)]
        copies.append(pltpu.make_async_copy(sources[source].at[lead], target, sems.at[len(copies)]))
    for copy in copies:
        copy.start()
    for copy in copies:
        copy.wait()


def whole_matrices(jobs):
    sizes = chip_dims()
    plan, sources, shapes = [], [], []
    for out, (shape, paired, parts) in enumerate(jobs):
        for order, (begin, end), part in parts:
            for back_last, piece in enumerate(part):
                for back_mid in range(sizes[order[1]]):
                    for back_first in range(sizes[order[0]]):
                        at = [None] * 3
                        at[order[2]] = (back_last, sizes[order[2]])
                        at[order[1]] = (back_mid, sizes[order[1]])
                        at[order[0]] = (back_first, sizes[order[0]])
                        plan.append((len(sources), (back_mid, back_first), at, (begin, end - begin), paired, out))
                sources.append(piece.reshape(piece.shape[:2] + shape[:-1] + piece.shape[-1:]))
        shapes.append(sizes[:2] + (2, sizes[2]) + shape[1:] if paired else sizes + shape)
    anywhere = pl.BlockSpec(memory_space=pl.ANY)
    total = sum(source.size for source in sources)
    return pl.pallas_call(
        lambda *refs: placed_kernel(plan, len(jobs), *refs),
        out_shape=[jax.ShapeDtypeStruct(shape, bf16) for shape in shapes],
        in_specs=[pl.BlockSpec(memory_space=pltpu.SMEM)] + [anywhere] * len(sources),
        out_specs=[pl.BlockSpec(memory_space=pltpu.VMEM)] * len(jobs),
        scratch_shapes=[pltpu.SemaphoreType.DMA((len(plan),))],
        compiler_params=pltpu.CompilerParams(vmem_limit_bytes=VMEM_LIMIT),
        cost_estimate=LIGHT,
    )(jnp.stack(chip_place()).astype(jnp.int32), *sources)


def total(terms):
    result = terms[0].astype(f32)
    for term in terms[1:]:
        result = result + term.astype(f32)
    return result


def reduce_send(terms, axis, dim, wire):
    place, size = chip_place()[dim], chip_dims()[dim]
    pick = lambda at: [lax.dynamic_index_in_dim(term, at, axis=axis, keepdims=False) for term in terms]
    received = [moved(total(pick((place + by) % size)).astype(wire), dim, by) for by in range(1, size)]
    return pick(place), received


def reduce_first(partial, wire=bf16):
    (begin, cut), (_, end) = column_parts(partial.shape[-1])
    return [
        reduce_send([partial[..., begin:cut]], 1, 1, wire),
        reduce_send([partial[..., cut:end]], 0, 0, wire),
    ]


def reduce_second(first, wire=bf16):
    return [
        reduce_send(first[0][0] + first[0][1], 0, 0, wire),
        reduce_send(first[1][0] + first[1][1], 0, 1, wire),
    ]


def reduce_third(second, wire=bf16):
    joined = jnp.concatenate([total(kept + received) for kept, received in second], axis=-1)
    return [reduce_send([joined], 0, 2, wire)]


def reduce_end(third):
    return total(third[0][0] + third[0][1])


def arrivals(parts):
    return [received for _, received in parts]


def arrived(parts, received):
    return [(kept, new) for (kept, _), new in zip(parts, received)]


def line_perm(turn, back):
    line = lax.axis_size("seg")
    parts = line // SEGS
    pairs = []
    for core in range(2):
        for place in range(line):
            piece = (place % SEGS) ^ turn
            half, index = divmod(piece, 2)
            source = core * line + place
            target = half * line + (2 * core + index) * parts + place // SEGS
            pairs.append((target, source) if back else (source, target))
    return pairs


def whole_sequence(array, core, place):
    parts = lax.axis_size("seg") // SEGS
    half = array.shape[1] // 2
    pieces = array.reshape(2, 2, half, -1).transpose(1, 0, 2, 3).reshape(4, half, -1)
    mine = place % SEGS
    target = 2 * core + (place // parts) % 2
    got = []
    for turn in range(4):
        piece = lax.dynamic_index_in_dim(pieces, mine ^ turn, axis=0, keepdims=False)
        got.append(lax.ppermute(piece, ("core", "seg"), line_perm(turn, False)))
    got = jnp.stack(got)
    return jnp.stack([lax.dynamic_index_in_dim(got, target ^ k, axis=0, keepdims=False) for k in range(4)])


def back_to_owner(ordered, core, place):
    parts = lax.axis_size("seg") // SEGS
    half = ordered.shape[1]
    mine = place % SEGS
    target = 2 * core + (place // parts) % 2
    got = []
    for turn in range(4):
        piece = lax.dynamic_index_in_dim(ordered, target ^ turn, axis=0, keepdims=False)
        got.append(lax.ppermute(piece, ("core", "seg"), line_perm(turn, True)))
    got = jnp.stack(got)
    pieces = jnp.stack([lax.dynamic_index_in_dim(got, mine ^ k, axis=0, keepdims=False) for k in range(4)])
    return pieces.reshape(2, 2, half, -1).transpose(1, 0, 2, 3).reshape(2, 2 * half, -1)


def part_pairs(step):
    line = lax.axis_size("seg")
    parts = line // SEGS
    return [(i, i + step) for i in range(line) if 0 <= i + step < line and i // parts == (i + step) // parts]


def entering(decay, state, step):
    parts = lax.axis_size("seg") // SEGS
    total = jnp.zeros_like(state)
    for _ in range(parts - 1):
        total = lax.ppermute(decay * total + state, "seg", part_pairs(step))
    return total


def borrowed(array, step):
    parts = lax.axis_size("seg") // SEGS
    if parts == 1:
        return jnp.zeros_like(array)
    return lax.ppermute(array, "seg", part_pairs(step))


def spilled(grad, edge, taps):
    if lax.axis_size("seg") == SEGS:
        return grad
    edge = borrowed(edge, -1)
    spill = jnp.stack(
        [
            sum(taps[k] * edge[CONV - 1 - k - early] for k in range(CONV - early))
            for early in range(CONV - 1, 0, -1)
        ]
    )
    at = grad.shape[0] - CONV + 1
    return grad.at[at:].set((grad[at:].astype(f32) + spill).astype(bf16))


def dot(a, b, contract):
    return lax.dot_general(a, b, (contract, ((), ())), preferred_element_type=f32)


def normed_kernel(slabs, core_ref, mine_ref, other_ref, gain_ref, normed_ref, turned_ref):
    mine, other = mine_ref[0], other_ref[0]
    first = core_ref[0] == 0
    hidden = jnp.concatenate([jnp.where(first, mine, other), jnp.where(first, other, mine)], axis=0).astype(f32)
    scale = lax.rsqrt(jnp.mean(hidden * hidden, axis=1, keepdims=True) + epsilon)
    normed = hidden * scale * gain_ref[...]
    normed_ref[...] = normed.astype(bf16)
    turned = normed.T.astype(bf16)
    for to, at, size in slabs:
        turned_ref[to : to + size] = turned[at : at + size]


def normed_tokens(core, mine, other, gain, rows):
    segs, half, width = mine.shape
    a, b, z = chip_dims()
    group = 2 * z * rows
    inside = rows % 16 == 0
    slabs = [(0, 0, width)]
    if inside:
        slabs = [
            (chip * group + (at * 2 + core_at) * rows, chip * group + (core_at * z + at) * rows, rows)
            for chip in range(a * b)
            for core_at in range(2)
            for at in range(z)
        ]
    normed, turned = pl.pallas_call(
        lambda *refs: normed_kernel(slabs, *refs),
        grid_spec=pltpu.PrefetchScalarGridSpec(
            num_scalar_prefetch=1,
            grid=(segs,),
            in_specs=[
                pl.BlockSpec((1, half, width), lambda i, core: (i, 0, 0)),
                pl.BlockSpec((1, half, width), lambda i, core: (i, 0, 0)),
                pl.BlockSpec((1, width), lambda i, core: (0, 0)),
            ],
            out_specs=(
                pl.BlockSpec((2 * half, width), lambda i, core: (i, 0)),
                pl.BlockSpec((width, 2 * half), lambda i, core: (0, i)),
            ),
        ),
        out_shape=(
            jax.ShapeDtypeStruct((segs * 2 * half, width), bf16),
            jax.ShapeDtypeStruct((width, segs * 2 * half), bf16),
        ),
        compiler_params=pltpu.CompilerParams(dimension_semantics=("arbitrary",), vmem_limit_bytes=VMEM_LIMIT),
        cost_estimate=LIGHT,
    )(core.reshape(1).astype(jnp.int32), mine, other, gain.reshape(1, width))
    if not inside:
        turned = turned.reshape(a, b, 2, z, rows, -1).transpose(0, 1, 3, 2, 4, 5).reshape(turned.shape)
    return normed, turned


def mixed_kernel(gated_ref, scale_ref, gain_ref, mixed_ref, turned_ref):
    mixed = gated_ref[...] * scale_ref[...] * gain_ref[...]
    mixed_ref[...] = mixed.astype(bf16)
    turned_ref[...] = mixed.T.astype(bf16)


def mixed_tokens(gated, scale, gain, seg_len):
    length, width = gated.shape
    return pl.pallas_call(
        mixed_kernel,
        grid=(length // seg_len,),
        in_specs=[
            pl.BlockSpec((seg_len, width), lambda i: (i, 0)),
            pl.BlockSpec((seg_len, 1), lambda i: (i, 0)),
            pl.BlockSpec((1, width), lambda i: (0, 0)),
        ],
        out_specs=(
            pl.BlockSpec((seg_len, width), lambda i: (i, 0)),
            pl.BlockSpec((width, seg_len), lambda i: (0, i)),
        ),
        out_shape=(
            jax.ShapeDtypeStruct((length, width), bf16),
            jax.ShapeDtypeStruct((width, length), bf16),
        ),
        compiler_params=pltpu.CompilerParams(dimension_semantics=("arbitrary",), vmem_limit_bytes=VMEM_LIMIT),
        cost_estimate=LIGHT,
    )(gated, scale, gain.reshape(1, width))


def columns_of(pair):
    return pl.ds(pair * LANES, LANES)


def low_half(shape):
    return lax.broadcasted_iota(jnp.int32, shape, len(shape) - 1) < HEADDIM


def pair_columns(array, pair, low):
    rows = array.shape[0]
    first = jnp.broadcast_to(array[:, 2 * pair : 2 * pair + 1], (rows, LANES))
    second = jnp.broadcast_to(array[:, 2 * pair + 1 : 2 * pair + 2], (rows, LANES))
    return jnp.where(low, first, second)


def conv_parts(current, before, taps):
    rows = current.shape[0]
    padded = jnp.concatenate([before, current], axis=0)
    seen = [padded[8 - CONV + 1 + k : 8 - CONV + 1 + k + rows] for k in range(CONV - 1)] + [current]
    total = taps[CONV : CONV + 1]
    for k in range(CONV):
        total = total + taps[k : k + 1] * seen[k]
    return total, seen


def step_terms(raw, head, seg_len):
    shifted = raw + head[1:2]
    step = jnp.maximum(shifted, 0.0) + jnp.log1p(jnp.exp(-jnp.abs(shifted)))
    log_decay = step * head[0:1]
    at_or_before = lax.broadcasted_iota(jnp.int32, (seg_len, seg_len), 0) >= lax.broadcasted_iota(
        jnp.int32, (seg_len, seg_len), 1
    )
    sums = lax.dot_general(
        jnp.where(at_or_before, 1.0, 0.0), log_decay, (((1,), (0,)), ((), ())),
        precision=lax.Precision.HIGHEST, preferred_element_type=f32,
    )
    return shifted, step, log_decay, sums * LOG2E


def forward_kernel(
    proj_ref, taps_ref, head_ref, skip_ref, rim_ref, init_ref,
    values_ref, prior_ref, final_ref, last_ref, state_ref, tail_ref,
):
    seg_len = proj_ref.shape[0]
    half = seg_len // 2

    @pl.when(pl.program_id(0) == 0)
    def _():
        state_ref[...] = init_ref[...]
        tail_ref[...] = rim_ref[...]

    def activated(begin):
        at = pl.ds(begin, LANES)
        total, _ = conv_parts(proj_ref[:, at], tail_ref[:, at], taps_ref[:, at])
        return total * jax.nn.sigmoid(total)

    b_low = activated(HALF).astype(bf16)
    b_turned = activated(HALF).T.astype(bf16)
    c_low = activated(HALF + STATE).astype(bf16)
    _, step, _, sums = step_terms(proj_ref[:, HALF + 2 * STATE :], head_ref, seg_len)
    sums_turned, step_turned = sums.T, step.T
    scores = dot(c_low, b_low, ((1,), (1,)))
    kept = lax.broadcasted_iota(jnp.int32, (half, half), 0) >= lax.broadcasted_iota(jnp.int32, (half, half), 1)
    first_scores = jnp.where(kept, scores[:half, :half], 0.0)
    later_scores = scores[half:, :half]
    second_scores = jnp.where(kept, scores[half:, half:], 0.0)
    low = low_half((seg_len, LANES))
    last_ref[...] = jnp.broadcast_to(sums[seg_len - 1 :], last_ref.shape)

    for pair in range(HEADS // 4):
        at = columns_of(pair)
        x_values = activated(pair * LANES)
        x_low = x_values.astype(bf16)
        sums_pair = pair_columns(sums, pair, low)
        last_pair = sums_pair[seg_len - 1 :]
        carry = jnp.exp2(last_pair - sums_pair) * pair_columns(step, pair, low)
        scaled_x = (carry * x_low.astype(f32)).astype(bf16)
        prior = state_ref[:, at]
        prior_low = prior.astype(bf16)
        prior_ref[0, :, at] = prior_low
        from_state = jnp.exp2(sums_pair) * dot(c_low, prior_low, ((1,), (0,)))
        state_ref[:, at] = jnp.exp2(last_pair) * prior + dot(b_turned, scaled_x, ((1,), (0,)))
        early, late = 0.0, 0.0
        for side in range(2):
            head = 2 * pair + side
            x_side = jnp.where(low if side == 0 else ~low, x_values, 0.0).astype(bf16)
            at_token = jnp.broadcast_to(sums[:, head : head + 1], (seg_len, half))
            at_source, source_step = sums_turned[head : head + 1], step_turned[head : head + 1]
            first = jnp.exp2(jnp.minimum(at_token[:half] - at_source[:, :half], 0.0)) * first_scores
            first = (first * source_step[:, :half]).astype(bf16)
            later = jnp.exp2(at_token[half:] - at_source[:, :half]) * later_scores
            later = (later * source_step[:, :half]).astype(bf16)
            second = jnp.exp2(jnp.minimum(at_token[half:] - at_source[:, half:], 0.0)) * second_scores
            second = (second * source_step[:, half:]).astype(bf16)
            early = early + dot(first, x_side[:half], ((1,), (0,)))
            late = late + dot(jnp.concatenate([later, second], axis=1), x_side, ((1,), (0,)))
        intra = jnp.concatenate([early, late], axis=0)
        values_ref[:, at] = intra + from_state + skip_ref[:, at] * x_values

    tail_ref[...] = proj_ref[seg_len - 8 :, : HALF + 2 * STATE]
    final_ref[...] = state_ref[...]


def full_block(shape):
    return pl.BlockSpec(shape, lambda *_: (0,) * len(shape))


def scan_forward(proj, taps, head, skip, rim, init, seg_len):
    segs = proj.shape[0] // seg_len
    wide = HALF + 2 * STATE
    return pl.pallas_call(
        forward_kernel,
        grid=(segs,),
        out_shape=(
            jax.ShapeDtypeStruct((proj.shape[0], HALF), f32),
            jax.ShapeDtypeStruct((segs, STATE, HALF), bf16),
            jax.ShapeDtypeStruct((STATE, HALF), f32),
            jax.ShapeDtypeStruct((segs * 8, LANES), f32),
        ),
        in_specs=[
            pl.BlockSpec((seg_len, proj.shape[1]), lambda i: (i, 0)),
            full_block((8, wide)),
            full_block((8, LANES)),
            full_block((1, HALF)),
            full_block((8, wide)),
            full_block((STATE, HALF)),
        ],
        out_specs=(
            pl.BlockSpec((seg_len, HALF), lambda i: (i, 0)),
            pl.BlockSpec((1, STATE, HALF), lambda i: (i, 0, 0)),
            full_block((STATE, HALF)),
            pl.BlockSpec((8, LANES), lambda i: (i, 0)),
        ),
        scratch_shapes=[pltpu.VMEM((STATE, HALF), f32), pltpu.VMEM((8, wide), f32)],
        compiler_params=pltpu.CompilerParams(
            dimension_semantics=("arbitrary",), vmem_limit_bytes=VMEM_LIMIT
        ),
        cost_estimate=LIGHT,
    )(proj, taps, head, skip, rim, init)


def split_dot(array, other):
    high = array.astype(bf16)
    rest = (array - high.astype(f32)).astype(bf16)
    return dot(high, other, ((1,), (0,))) + dot(rest, other, ((1,), (0,)))


def backward_kernel(
    group, proj_ref, before_ref, taps_ref, rim_ref, shared_ref, shared_before_ref, shared_taps_ref, shared_rim_ref,
    head_ref, skip_ref, heads_ref, end_ref, prior_ref, values_ref, grad_ref,
    grad_x_ref, grad_b_ref, grad_c_ref, grad_raw_ref, taps_grad_ref, skip_grad_ref, head_grad_ref, edge_ref, start_ref,
    later_ref, local_ref, scaled_ref, grad_state_ref, inner_ref, source_ref, carry_ref, decay_ref,
):
    seg_len = proj_ref.shape[0]
    half = seg_len // 2
    turn = pl.program_id(0)

    @pl.when(turn == 0)
    def _():
        later_ref[...] = end_ref[...]
        edge_ref[...] = jnp.zeros_like(edge_ref)
        taps_grad_ref[...] = jnp.zeros_like(taps_grad_ref)
        skip_grad_ref[...] = jnp.zeros_like(skip_grad_ref)
        head_grad_ref[...] = jnp.zeros_like(head_grad_ref)

    first_segment = turn == pl.num_programs(0) - 1

    def conv_at(at, current, ahead, taps, rim):
        before = jnp.where(first_segment, rim[:, at], ahead[:, at])
        return conv_parts(current[:, at], before, taps[:, at])

    def activated(begin):
        total, _ = conv_at(pl.ds(begin, LANES), shared_ref, shared_before_ref, shared_taps_ref, shared_rim_ref)
        return total * jax.nn.sigmoid(total)

    b_values = activated(0)
    c_values = activated(STATE)
    b_low, c_low, c_turned = b_values.astype(bf16), c_values.astype(bf16), c_values.T.astype(bf16)
    shifted, step, log_decay, sums = step_terms(shared_ref[:, 2 * STATE :], head_ref, seg_len)
    sums_turned = sums.T
    scores = dot(b_low, c_low, ((1,), (1,)))
    kept = lax.broadcasted_iota(jnp.int32, (half, half), 0) <= lax.broadcasted_iota(jnp.int32, (half, half), 1)
    first_scores = jnp.where(kept, scores[:half, :half], 0.0)
    later_scores = scores[:half, half:]
    second_scores = jnp.where(kept, scores[half:, half:], 0.0)
    low = low_half((seg_len, LANES))
    first_grad, later_grad, second_grad = 0.0, 0.0, 0.0

    pairs = grad_ref.shape[1] // LANES
    for pair in range(pairs):
        at = columns_of(pair)
        total, seen = conv_at(at, proj_ref, before_ref, taps_ref, rim_ref)
        sigmoid = jax.nn.sigmoid(total)
        x_values = total * sigmoid
        x_low = x_values.astype(bf16)
        x_wide = x_low.astype(f32)
        sums_pair = pair_columns(sums, group * pairs + pair, low)
        step_pair = pair_columns(step, group * pairs + pair, low)
        last_pair = sums_pair[seg_len - 1 :]
        gap = jnp.exp2(last_pair - sums_pair)
        scaled_ref[:, at] = (gap * step_pair * x_wide).astype(bf16)
        grad_values = grad_ref[:, at]
        grad_state_ref[:, at] = (grad_values * jnp.exp2(sums_pair)).astype(bf16)
        later = later_ref[:, at]
        later_low = later.astype(bf16)
        local_ref[:, at] = later_low
        prior = prior_ref[0, :, at]
        decay_ref[:, at] = jnp.broadcast_to(
            jnp.sum(later * prior.astype(f32), axis=0, keepdims=True), (8, LANES)
        )
        grad_prior = dot(c_turned, grad_state_ref[:, at], ((1,), (0,)))
        later_ref[:, at] = jnp.exp2(last_pair) * later + grad_prior
        grad_scaled = dot(b_low, later_low, ((1,), (0,)))
        stepped = (step_pair * x_wide).astype(bf16)
        early, late = 0.0, 0.0
        for side in range(2):
            head = 2 * (group * pairs + pair) + side
            grad_low = jnp.where(low if side == 0 else ~low, grad_values, 0.0).astype(bf16)
            at_source = jnp.broadcast_to(sums[:, head : head + 1], (seg_len, half))
            at_token = sums_turned[head : head + 1]
            grad_weights = dot(stepped, grad_low, ((1,), (1,)))
            first = jnp.exp2(jnp.minimum(at_token[:, :half] - at_source[:half], 0.0))
            after = jnp.exp2(at_token[:, half:] - at_source[:half])
            second = jnp.exp2(jnp.minimum(at_token[:, half:] - at_source[half:], 0.0))
            first_grad = first_grad + first * grad_weights[:half, :half]
            later_grad = later_grad + after * grad_weights[:half, half:]
            second_grad = second_grad + second * grad_weights[half:, half:]
            upper = jnp.concatenate([first * first_scores, after * later_scores], axis=1).astype(bf16)
            early = early + dot(upper, grad_low, ((1,), (0,)))
            late = late + dot((second * second_scores).astype(bf16), grad_low[half:], ((1,), (0,)))
        inner = jnp.concatenate([early, late], axis=0)
        skip = skip_ref[:, at]
        skip_grad_ref[:, at] += jnp.sum(grad_values * x_values, axis=0, keepdims=True)
        inner_ref[:, at] = grad_values * (values_ref[:, at] - skip * x_values)
        source_ref[:, at] = x_wide * inner
        carry_ref[:, at] = x_wide * grad_scaled
        grad_x = skip * grad_values + step_pair * (inner + gap * grad_scaled)
        grad_total = grad_x * (sigmoid * (1.0 + total * (1.0 - sigmoid)))
        for k in range(CONV):
            taps_grad_ref[k : k + 1, at] += jnp.sum(grad_total * seen[k], axis=0, keepdims=True)
        taps_grad_ref[CONV : CONV + 1, at] += jnp.sum(grad_total, axis=0, keepdims=True)
        extended = jnp.concatenate([grad_total, edge_ref[:, at]], axis=0)
        edge_ref[:, at] = grad_total[:8]
        taps = taps_ref[:, at]
        grad_conv = taps[CONV - 1 : CONV] * grad_total
        for k in range(CONV - 1):
            grad_conv = grad_conv + taps[k : k + 1] * extended[CONV - 1 - k : CONV - 1 - k + seg_len]
        grad_x_ref[:, at] = grad_conv.astype(bf16)

    heads = heads_ref[...]
    tail = jnp.exp2(sums[seg_len - 1 :] - sums)
    source_grad = split_dot(source_ref[...], heads)
    step_grad = source_grad + tail * split_dot(carry_ref[...], heads)
    used = step * step_grad
    sum_grad = split_dot(inner_ref[...], heads) - used
    at_last = jnp.sum(used - step * source_grad, axis=0, keepdims=True)
    at_last = at_last + split_dot(decay_ref[...], heads)[:1] * jnp.exp2(sums[seg_len - 1 :])
    is_last = lax.broadcasted_iota(jnp.int32, (seg_len, LANES), 0) == seg_len - 1
    sum_grad = sum_grad + jnp.where(is_last, at_last, 0.0)
    at_or_after = lax.broadcasted_iota(jnp.int32, (seg_len, seg_len), 0) <= lax.broadcasted_iota(
        jnp.int32, (seg_len, seg_len), 1
    )
    log_grad = lax.dot_general(
        jnp.where(at_or_after, 1.0, 0.0), sum_grad, (((1,), (0,)), ((), ())),
        precision=lax.Precision.HIGHEST, preferred_element_type=f32,
    )
    grad_raw = (step_grad + head_ref[0:1] * log_grad) * jax.nn.sigmoid(shifted)
    grad_raw_ref[...] = grad_raw
    head_grad_ref[0:1] += jnp.sum(log_grad * log_decay, axis=0, keepdims=True)
    head_grad_ref[1:2] += jnp.sum(grad_raw, axis=0, keepdims=True)

    first_low = jnp.where(kept, first_grad, 0.0)
    second_low = jnp.where(kept, second_grad, 0.0)
    grad_scores = jnp.concatenate(
        [
            jnp.concatenate([first_low, later_grad], axis=1),
            jnp.concatenate([jnp.zeros_like(first_low), second_low], axis=1),
        ],
        axis=0,
    )
    start_ref[...] = later_ref[...]
    grad_b_ref[...] = dot(scaled_ref[...], local_ref[...], ((1,), (1,))) + dot(
        grad_scores.astype(bf16), c_low, ((1,), (0,))
    )
    grad_c_ref[...] = dot(grad_state_ref[...], prior_ref[0], ((1,), (1,))) + dot(
        grad_scores.T.astype(bf16), b_low, ((1,), (0,))
    )


GROUPS = 1


def scan_backward(group, proj, taps, head, skip, rim, end, prior, values, grad_values, seg_len):
    length = proj.shape[0]
    segs = length // seg_len
    width, shared = HALF // GROUPS, proj.shape[1] - HALF
    channel = lax.broadcasted_iota(jnp.int32, (width, LANES), 0) // HEADDIM + group * width // HEADDIM
    heads = (channel == lax.broadcasted_iota(jnp.int32, (width, LANES), 1)).astype(bf16)
    back = lambda width, at=0: pl.BlockSpec((seg_len, width), lambda i: (segs - 1 - i, at))
    row_ahead = lambda i: jnp.maximum((segs - 1 - i) * (seg_len // 8) - 1, 0)
    ahead = lambda width, at: pl.BlockSpec((8, width), lambda i: (row_ahead(i), at))
    column = lambda rows, width, at: pl.BlockSpec((rows, width), lambda i: (0, at))
    both = HALF // shared
    taps, rim = jnp.pad(taps, ((0, 0), (0, shared - 2 * STATE))), jnp.pad(rim, ((0, 0), (0, shared - 2 * STATE)))
    return pl.pallas_call(
        lambda *refs: backward_kernel(group, *refs),
        grid=(segs,),
        out_shape=(
            jax.ShapeDtypeStruct((length, width), bf16),
            jax.ShapeDtypeStruct((length, STATE), f32),
            jax.ShapeDtypeStruct((length, STATE), f32),
            jax.ShapeDtypeStruct((length, LANES), f32),
            jax.ShapeDtypeStruct((8, width), f32),
            jax.ShapeDtypeStruct((1, width), f32),
            jax.ShapeDtypeStruct((8, LANES), f32),
            jax.ShapeDtypeStruct((8, width), f32),
            jax.ShapeDtypeStruct((STATE, width), f32),
        ),
        in_specs=[
            back(width, group),
            ahead(width, group),
            column(8, width, group),
            column(8, width, group),
            back(shared, both),
            ahead(shared, both),
            column(8, shared, both),
            column(8, shared, both),
            full_block((8, LANES)),
            column(1, width, group),
            full_block((width, LANES)),
            column(STATE, width, group),
            pl.BlockSpec((1, STATE, width), lambda i: (segs - 1 - i, 0, group)),
            back(width, group),
            back(width, group),
        ],
        out_specs=(
            back(width),
            back(STATE),
            back(STATE),
            back(LANES),
            full_block((8, width)),
            full_block((1, width)),
            full_block((8, LANES)),
            full_block((8, width)),
            full_block((STATE, width)),
        ),
        scratch_shapes=[
            pltpu.VMEM((STATE, width), f32),
            pltpu.VMEM((STATE, width), bf16),
            pltpu.VMEM((seg_len, width), bf16),
            pltpu.VMEM((seg_len, width), bf16),
            pltpu.VMEM((seg_len, width), f32),
            pltpu.VMEM((seg_len, width), f32),
            pltpu.VMEM((seg_len, width), f32),
            pltpu.VMEM((8, width), f32),
        ],
        compiler_params=pltpu.CompilerParams(
            dimension_semantics=("arbitrary",), vmem_limit_bytes=VMEM_LIMIT
        ),
        cost_estimate=LIGHT,
    )(proj, proj, taps, rim, proj, proj, taps, rim, head, skip, heads, end, prior, values, grad_values)


def half_kernel(transposed, count, core_ref, *refs):
    inputs, mine_ref, theirs_ref = refs[: 2 * count], refs[-2], refs[-1]
    total = refs[2 * count][...] if len(refs) > 2 * count + 2 else 0.0
    for left, right in zip(inputs[:count], inputs[count:]):
        total = total + dot(left[...], right[...], ((1,), (1 if transposed else 0,)))
    half = total.shape[0] // 2
    first = core_ref[0] == 0
    mine_ref[0] = jnp.where(first, total[:half], total[half:])
    theirs_ref[0] = jnp.where(first, total[half:], total[:half]).astype(bf16)


def half_products(core, terms, seg_len, width, transposed, base=()):
    length = terms[0][0].shape[0]
    left = [pl.BlockSpec((seg_len, array.shape[1]), lambda i, core: (i, 0)) for array, _, _ in terms]
    right = []
    for array, matrix, at in terms:
        if transposed:
            right.append(pl.BlockSpec((width, array.shape[1]), lambda i, core, at=at: (0, at(core[0]))))
        else:
            right.append(pl.BlockSpec(matrix.shape, lambda i, core: (0, 0)))
    depth = sum(array.shape[1] for array, _, _ in terms)
    mine, theirs = pl.pallas_call(
        lambda *refs: half_kernel(transposed, len(terms), *refs),
        grid_spec=pltpu.PrefetchScalarGridSpec(
            num_scalar_prefetch=1,
            grid=(length // seg_len,),
            in_specs=left + right + [pl.BlockSpec((seg_len, width), lambda i, core: (i, 0)) for _ in base],
            out_specs=[pl.BlockSpec((1, seg_len // 2, width), lambda i, core: (i, 0, 0))] * 2,
        ),
        out_shape=(
            jax.ShapeDtypeStruct((length // seg_len, seg_len // 2, width), f32),
            jax.ShapeDtypeStruct((length // seg_len, seg_len // 2, width), bf16),
        ),
        compiler_params=pltpu.CompilerParams(dimension_semantics=("arbitrary",), vmem_limit_bytes=VMEM_LIMIT),
        cost_estimate=LIGHT,
    )(core.reshape(1).astype(jnp.int32), *[array for array, _, _ in terms], *[matrix for _, matrix, _ in terms], *base)
    return mine, theirs


def shared_kernel(core_ref, proj_ref, rim_ref, taps_ref, b_ref, c_ref, other_ref, grad_ref, taps_grad_ref, edge_ref):
    total, seen = conv_parts(proj_ref[...], rim_ref[...], taps_ref[...])
    sigmoid = jax.nn.sigmoid(total)
    grad_total = jnp.where(core_ref[0] == 0, b_ref[...], c_ref[...]) + other_ref[...]
    grad_total = grad_total * (sigmoid * (1.0 + total * (1.0 - sigmoid)))
    sums = [jnp.sum(grad_total * part, axis=0, keepdims=True) for part in seen]
    sums = sums + [jnp.sum(grad_total, axis=0, keepdims=True), jnp.zeros((8 - CONV - 1, LANES), f32)]
    taps_grad_ref[...] = jnp.concatenate(sums, axis=0)
    edge_ref[...] = grad_total[:8]
    taps = taps_ref[...]
    extended = jnp.concatenate([grad_total, jnp.zeros((8, LANES), f32)], axis=0)
    grad_conv = taps[CONV - 1 : CONV] * grad_total
    for k in range(CONV - 1):
        grad_conv = grad_conv + taps[k : k + 1] * extended[CONV - 1 - k : CONV - 1 - k + grad_total.shape[0]]
    grad_ref[...] = grad_conv.astype(bf16)


def shared_backward(core, proj, rim, taps, grad_b, grad_c, other):
    length = proj.shape[0]
    picked = lambda rows: pl.BlockSpec((rows, LANES), lambda i, core: (0, HALF // LANES + core[0]))
    whole = lambda rows: pl.BlockSpec((rows, LANES), lambda i, core: (0, 0))
    return pl.pallas_call(
        shared_kernel,
        grid_spec=pltpu.PrefetchScalarGridSpec(
            num_scalar_prefetch=1,
            grid=(1,),
            in_specs=[picked(length), picked(8), picked(8), whole(length), whole(length), whole(length)],
            out_specs=(whole(length), whole(8), whole(8)),
        ),
        out_shape=(
            jax.ShapeDtypeStruct((length, LANES), bf16),
            jax.ShapeDtypeStruct((8, LANES), f32),
            jax.ShapeDtypeStruct((8, LANES), f32),
        ),
        compiler_params=pltpu.CompilerParams(vmem_limit_bytes=VMEM_LIMIT),
        cost_estimate=LIGHT,
    )(core.reshape(1).astype(jnp.int32), proj, rim, taps, grad_b, grad_c, other)


def per_device(hidden_in, cotangent, in_proj, out_proj, conv_params, pre_gain, gated_gain, head_params):
    chips, line = lax.axis_size("chip"), lax.axis_size("seg")
    core, place = lax.axis_index("core"), lax.axis_index("seg")
    rows, model_width = in_proj.shape[0], hidden_in.shape[2]
    heads = HEADS // 2

    conv_width, gain_width = conv_params.shape[1], gated_gain.shape[0]
    used = HALF + 2 * STATE + heads
    spare = -used % LANES
    small = jnp.zeros((rows, spare), bf16)
    small = small.at[: CONV + 1, :conv_width].set(conv_params)
    small = small.at[CONV + 1, :rows].set(pre_gain)
    small = small.at[CONV + 2, :gain_width].set(gated_gain)

    def conv_side(which):
        return jnp.concatenate(
            [
                own_columns(in_proj[:, INNER : 2 * INNER], which),
                in_proj[:, 2 * INNER : INNER + XBC],
                own_columns(in_proj[:, INNER + XBC :], which),
                small,
            ],
            axis=1,
        )

    def gate_side(which):
        return own_columns(in_proj[:, :INNER], which)

    conv_swap = to_partner(conv_side(1 - core))
    conv_block = in_core_order(conv_side(core), conv_swap, core, 0)
    conv_z = gather_first(conv_block)
    gate_swap = to_partner(gate_side(1 - core))
    gate_block = in_core_order(gate_side(core), gate_swap, core, 0)
    conv_z, gate_block = tie(conv_z, gate_block)
    conv_2 = gather_next(conv_z, 1)
    gate_z = gather_first(gate_block)
    conv_2, gate_z, hidden_in = tie(conv_2, gate_z, hidden_in)
    conv_last = gather_next(conv_2, 2)
    hidden_half = whole_sequence(hidden_in, core, place)
    conv_last, hidden_half, gate_z, out_proj = tie(conv_last, hidden_half, gate_z, out_proj)
    hidden_other = to_partner(hidden_half)
    gate_2 = gather_next(gate_z, 1)
    out_z = gather_first(out_proj)
    parts = list(zip(ORDERS, column_parts(conv_block.shape[-1]), conv_last))
    conv_all = whole_matrices([(conv_block.shape, True, parts)])[0].reshape(model_width, -1)

    small_all = conv_all.reshape(chips, 2, line, rows, -1)[..., used:].astype(f32)
    taps_full = small_all[..., : CONV + 1, :conv_width].transpose(3, 0, 1, 2, 4).reshape(CONV + 1, XBC)
    taps = jnp.concatenate([own_columns(taps_full[:, :INNER], core), taps_full[:, INNER:]], axis=1)
    gain_pre = small_all[..., CONV + 1, :rows].reshape(model_width)
    gain_gate = lax.dynamic_index_in_dim(
        small_all[..., CONV + 2, :gain_width], core, axis=1, keepdims=False
    ).reshape(HALF)
    params = own_columns(head_params, core)

    seg_len = 2 * hidden_half.shape[1]
    tokens = SEGS * seg_len
    normed, normed_turned = normed_tokens(core, hidden_half, hidden_other, gain_pre, rows)
    projected = dot(normed, conv_all, ((1,), (0,)))
    projected, gate_2, out_z, cotangent = tie(projected, gate_2, out_z, cotangent)
    gate_last = gather_next(gate_2, 2)
    cot_half = whole_sequence(cotangent, core, place)

    taps = jnp.pad(taps, ((0, 8 - CONV - 1), (0, 0)))
    head = jnp.pad(jnp.stack([-jnp.exp(params[0]), params[1]]), ((0, 6), (0, LANES - heads)))
    skip = jnp.repeat(params[2], HEADDIM).reshape(1, HALF)
    wide = HALF + 2 * STATE
    rim = borrowed(projected[tokens - 8 :, :wide], 1)
    nothing = jnp.zeros((STATE, HALF), f32)
    values, prior, final, last = scan_forward(projected, taps, head, skip, rim, nothing, seg_len)
    if line > SEGS:
        last = jnp.sum(last.reshape(SEGS, 8, LANES)[:, 0, :heads], axis=0)
        decay = jnp.repeat(jnp.exp2(last), HEADDIM)
        begin = entering(decay, final, 1)
        values, prior, _, _ = scan_forward(projected, taps, head, skip, rim, begin, seg_len)

    values, gate_last, out_z, cot_half = tie(values, gate_last, out_z, cot_half)
    out_2 = gather_next(out_z, 1)
    cot_other = to_partner(cot_half)
    cot = in_core_order(cot_half, cot_other, core, 1)
    upstream = cot.reshape(tokens, model_width)
    cut = column_parts(HALF)
    gate_matrix = whole_matrices([(gate_block.shape, True, list(zip(ORDERS, cut, gate_last)))])[0].reshape(model_width, HALF)
    gate_input = dot(normed, gate_matrix, ((1,), (0,)))

    silu_gate = jax.nn.silu(gate_input)
    gated = values * silu_gate
    squares = jnp.sum(gated * gated, axis=1)
    squares_other = to_partner(squares)
    scale = lax.rsqrt((squares + squares_other) / INNER + epsilon)[:, None]
    scale, out_2 = tie(scale, out_2)
    out_last = gather_next(out_2, 2)
    mixed, mixed_turned = mixed_tokens(gated, scale, gain_gate, seg_len)
    by_owner = lambda grad: grad.astype(bf16).reshape(chip_dims() + (-1, grad.shape[1]))
    out_grad = by_owner(dot(mixed_turned, upstream, ((1,), (0,))))
    out_grad, out_last = tie(out_grad, out_last)
    out_first = reduce_first(out_grad)
    out_matrix = whole_matrices([(out_proj.shape, False, list(zip(ORDERS, cut, out_last)))])[0].reshape(HALF, model_width)
    branch, branch_sent = half_products(core, [(mixed, out_matrix, None)], seg_len, model_width, False)
    branch_sent, upstream = tie(branch_sent, upstream)
    branch_other = to_partner(branch_sent)
    grad_mixed = dot(upstream, out_matrix, ((1,), (1,)))
    grad_mixed, out_got = tie(grad_mixed, arrivals(out_first))
    out_second = reduce_second(arrived(out_first, out_got))
    unit = gated * scale
    gain_grad = grad_mixed * gain_gate
    along = jnp.sum(gain_grad * unit, axis=1)
    along_other = to_partner(along)
    along_other, branch_other = tie(along_other, branch_other)
    hidden_out = back_to_owner(
        (hidden_half.astype(f32) + branch + branch_other.astype(f32)).astype(bf16), core, place
    )
    along = ((along + along_other) / INNER)[:, None]
    gate_gain_grad = jnp.sum(grad_mixed * unit, axis=0)
    grad_gated = scale * (gain_grad - unit * along)
    grad_values = grad_gated * silu_gate
    sigmoid = jax.nn.sigmoid(gate_input)
    grad_gate = (grad_gated * values * (sigmoid * (1.0 + gate_input * (1.0 - sigmoid)))).astype(bf16)
    gate_grad = by_owner(dot(normed_turned, grad_gate, ((1,), (0,))))
    gate_grad, grad_values, out_got = tie(gate_grad, grad_values, arrivals(out_second))
    out_second = arrived(out_second, out_got)
    gate_first = reduce_first(gate_grad)
    scan = lambda later: scan_backward(
        0, projected, taps, head, skip, rim, later, prior, values, grad_values, seg_len
    )
    if line > SEGS:
        nothing = entering(decay, scan(nothing)[-1], -1)
    back = scan(nothing)
    back, gate_got, hidden_out, grad_gate = tie(back, arrivals(gate_first), hidden_out, grad_gate)
    out_third = reduce_third(out_second)
    gate_second = reduce_second(arrived(gate_first, gate_got))
    grad_x, grad_b, grad_c, grad_raw, x_taps_grad, skip_grad, head_sums, x_edge, _ = back
    grad_x = spilled(grad_x, x_edge, taps[:, :HALF])
    head_grad = jnp.concatenate([head_sums[:2, :heads], skip_grad.reshape(1, heads, HEADDIM).sum(axis=2)])

    other = to_partner(jnp.where(core == 0, grad_c, grad_b))
    grad_state, state_taps_grad, state_edge = shared_backward(core, projected, rim, taps, grad_b, grad_c, other)
    grad_state = spilled(grad_state, state_edge, lax.dynamic_slice_in_dim(taps, HALF + core * STATE, STATE, axis=1))
    grad_raw = grad_raw.astype(bf16)
    grad_proj = jnp.concatenate([grad_x, grad_state, grad_raw], axis=1)
    conv_grad = by_owner(dot(normed_turned, grad_proj, ((1,), (0,))))
    state_taps_grad = state_taps_grad[: CONV + 1]
    none = jnp.zeros_like(state_taps_grad)
    taps_grad = jnp.concatenate(
        [
            x_taps_grad[: CONV + 1],
            jnp.where(core == 0, state_taps_grad, none),
            jnp.where(core == 0, none, state_taps_grad),
        ],
        axis=1,
    )
    conv_grad, gate_got, out_got, grad_gate = tie(conv_grad, arrivals(gate_second), arrivals(out_third), grad_gate)
    out_third = arrived(out_third, out_got)
    base = dot(grad_gate, gate_matrix, ((1,), (1,)))
    conv_first = reduce_first(conv_grad)
    gate_third = reduce_third(arrived(gate_second, gate_got))
    terms = [
        (grad_x, conv_all, lambda core: 0),
        (grad_state, conv_all, lambda core: HALF // LANES + core),
        (grad_raw, conv_all, lambda core: (HALF + 2 * STATE) // LANES),
    ]
    grad_normed, sent_normed = half_products(core, terms, seg_len, model_width, True, (base,))
    sent_normed, gate_got, conv_got, taps_grad, gate_gain_grad, head_grad = tie(
        sent_normed, arrivals(gate_third), arrivals(conv_first), taps_grad, gate_gain_grad, head_grad
    )
    gate_third = arrived(gate_third, gate_got)
    conv_second = reduce_second(arrived(conv_first, conv_got))
    other_normed = to_partner(sent_normed)
    wide_hidden = hidden_half.astype(f32)
    hidden_scale = lax.rsqrt(jnp.mean(wide_hidden * wide_hidden, axis=-1, keepdims=True) + epsilon)
    grad_normed = (grad_normed + other_normed.astype(f32)) * gain_pre
    hidden_unit = wide_hidden * hidden_scale
    along = jnp.mean(grad_normed * hidden_unit, axis=-1, keepdims=True)
    grad_hidden = hidden_scale * (grad_normed - hidden_unit * along)
    grad_in = (cot_half.astype(f32) + grad_hidden).astype(bf16)
    grad_in = back_to_owner(grad_in, core, place)

    def spread_own(array):
        width = array.shape[-1] // chips
        parted = array.reshape(array.shape[:-1] + (chips, 1, width))
        none = jnp.zeros_like(parted)
        both = jnp.where(
            core == 0,
            jnp.concatenate([parted, none], axis=-2),
            jnp.concatenate([none, parted], axis=-2),
        )
        return both.reshape(array.shape[:-1] + (2 * array.shape[-1],))

    taps_all = jnp.concatenate([spread_own(taps_grad[:, :HALF]), taps_grad[:, HALF:]], axis=1)
    taps_all = taps_all.reshape(CONV + 1, chips, 2, line, conv_width).transpose(1, 3, 2, 0, 4)
    gate_all = spread_own(gate_gain_grad).reshape(chips, 2, line, gain_width).transpose(0, 2, 1, 3)
    head_all = jnp.broadcast_to(spread_own(head_grad).reshape(-1), (chips, line, 2, 3 * HEADS))
    small_grads = jnp.concatenate(
        [
            taps_all.reshape(chips, line, 2, -1),
            gate_all,
            head_all,
        ],
        axis=3,
    )
    count = small_grads.shape[3]
    small_grads = small_grads.reshape(chip_dims() + (2, count))
    small_second = reduce_second(reduce_first(small_grads, f32), f32)
    grad_in, conv_got, small_got = tie(grad_in, arrivals(conv_second), arrivals(small_second))
    conv_third = reduce_third(arrived(conv_second, conv_got))
    small_third = reduce_third(arrived(small_second, small_got), f32)
    small_share = reduce_end(small_third)
    out_share = reduce_end(out_third).reshape(-1, model_width)
    paired = lambda third: reduce_end(third).astype(bf16).reshape(2, rows, -1)
    gate_share, conv_share = paired(gate_third), paired(conv_third)

    def mine_and_partner(share):
        keep = lax.dynamic_index_in_dim(share, core, axis=0, keepdims=False)
        give = lax.dynamic_index_in_dim(share, 1 - core, axis=0, keepdims=False)
        return keep, to_partner(give)

    keep, got = mine_and_partner(small_share)
    small_total = keep + got
    taps_end = (CONV + 1) * conv_width
    taps_share = small_total[:taps_end].reshape(CONV + 1, conv_width)
    gain_share = small_total[taps_end : taps_end + gain_width]
    head_total = small_total[taps_end + gain_width :].reshape(3, HEADS)

    def interleave(mine, theirs):
        width = mine.shape[1] // chips
        both = in_core_order(mine.reshape(rows, chips, width), theirs.reshape(rows, chips, width), core, 2)
        return both.reshape(rows, -1)

    keep_gate, got_gate = mine_and_partner(gate_share)
    keep, got = mine_and_partner(conv_share)
    state_end = HALF + STATE
    in_share = jnp.concatenate(
        [
            interleave(keep_gate, got_gate),
            interleave(keep[:, :HALF], got[:, :HALF]),
            in_core_order(keep[:, HALF:state_end], got[:, HALF:state_end], core, 1).reshape(rows, -1),
            interleave(keep[:, state_end : state_end + heads], got[:, state_end : state_end + heads]),
        ],
        axis=1,
    ).astype(f32)
    pre_share = jnp.sum(in_proj.astype(f32) * in_share, axis=1) / pre_gain.astype(f32)
    return (hidden_out, grad_in, in_share, out_share, taps_share, pre_share, gain_share, head_total)


def solution(mesh):
    devices = mesh.devices
    cores = Mesh(devices.reshape(devices.shape[0] // 2, 2, devices.shape[1]), ("chip", "core", "seg"))
    dp, both = ("chip", "core"), ("chip", "core", "seg")
    tokens = P(dp, "seg", None)
    return jax.shard_map(
        per_device,
        mesh=cores,
        in_specs=(tokens, tokens, P(both, None), P(both, None), P(None, both), P(both), P(both), P()),
        out_specs=(tokens, tokens, P(both, None), P(both, None), P(None, both), P(both), P(both), P()),
        check_vma=False,
    )
```

```python
import jax
import jax.numpy as jnp
from jax import lax
from jax.experimental import pallas as pl
from jax.experimental.pallas import tpu as pltpu
from jax.sharding import Mesh
from jax.sharding import PartitionSpec as P

HEADS = 48
HEADDIM = 64
STATE = 128
CONV = 4
INNER = 3072
XBC = 3328
HALF = INNER // 2
LANES = 128
SEGS = 4
LIGHT = pl.CostEstimate(flops=1024, bytes_accessed=1024, transcendentals=0)
VMEM_LIMIT = 48 * 1024 * 1024
LOG2E = 1.4426950408889634

epsilon = 1e-05
f32 = jnp.float32
bf16 = jnp.bfloat16


def own_columns(array, core):
    chips = lax.axis_size("chip")
    width = array.shape[-1] // (2 * chips)
    parted = array.reshape(array.shape[:-1] + (chips, 2, width))
    picked = lax.dynamic_index_in_dim(parted, core, axis=parted.ndim - 2, keepdims=False)
    return picked.reshape(array.shape[:-1] + (chips * width,))


def to_partner(array):
    return lax.ppermute(array, "core", [(0, 1), (1, 0)])


def in_core_order(mine, theirs, core, axis):
    first = jnp.where(core == 0, mine, theirs)
    second = jnp.where(core == 0, theirs, mine)
    return jnp.stack([first, second], axis=axis)


def chip_dims():
    return (lax.axis_size("chip") // 2, 2, lax.axis_size("seg"))


def chip_place():
    chip = lax.axis_index("chip")
    return (chip // 2, chip % 2, lax.axis_index("seg"))


def moved(array, dim, by):
    sizes = chip_dims()
    index = lambda at: (at[0] * sizes[1] + at[1]) * sizes[2] + at[2]
    pairs = []
    for a in range(sizes[0]):
        for b in range(sizes[1]):
            for z in range(sizes[2]):
                to = [a, b, z]
                to[dim] = (to[dim] + by) % sizes[dim]
                pairs.append((index((a, b, z)), index(to)))
    return lax.ppermute(array, ("chip", "seg"), pairs)


def tie(*values):
    return lax.optimization_barrier(values)


ORDERS = ((2, 0, 1), (2, 1, 0))


def column_parts(width):
    cut = -(-(width // 2) // LANES) * LANES
    return ((0, cut), (cut, width))


def gather_step(data, dim):
    return [data] + [moved(data, dim, by) for by in range(1, chip_dims()[dim])]


def gather_first(block):
    pieces = gather_step(block, 2)
    return [[piece[half] for piece in pieces] for half in range(2)]


def gather_next(parts, step):
    return [gather_step(jnp.stack(part), order[step]) for order, part in zip(ORDERS, parts)]


def placed_kernel(plan, outs, place_ref, *refs):
    sources, targets, sems = refs[: -outs - 1], refs[-outs - 1 : -1], refs[-1]
    copies = []
    for source, lead, at, half, paired, out in plan:
        spot = [lax.rem(place_ref[dim] + (size - back), size) for dim, (back, size) in enumerate(at)]
        target = targets[out].at[spot[0], spot[1]]
        target = target.at[half, spot[2]] if paired else target.at[spot[2], half]
        copies.append(pltpu.make_async_copy(sources[source].at[lead], target, sems.at[len(copies)]))
    for copy in copies:
        copy.start()
    for copy in copies:
        copy.wait()


def whole_matrices(jobs):
    sizes = chip_dims()
    plan, sources, shapes = [], [], []
    for out, (paired, halves) in enumerate(jobs):
        for half, (order, part) in enumerate(zip(ORDERS, halves)):
            for back_last, piece in enumerate(part):
                for back_mid in range(sizes[order[1]]):
                    for back_first in range(sizes[order[0]]):
                        at = [None] * 3
                        at[order[2]] = (back_last, sizes[order[2]])
                        at[order[1]] = (back_mid, sizes[order[1]])
                        at[order[0]] = (back_first, sizes[order[0]])
                        plan.append((len(sources), (back_mid, back_first), at, half, paired, out))
                sources.append(piece)
        block = halves[0][0].shape[-2:]
        shapes.append(sizes[:2] + ((2, sizes[2]) if paired else (sizes[2], 2)) + block)
    anywhere = pl.BlockSpec(memory_space=pl.ANY)
    return pl.pallas_call(
        lambda *refs: placed_kernel(plan, len(jobs), *refs),
        out_shape=[jax.ShapeDtypeStruct(shape, bf16) for shape in shapes],
        in_specs=[pl.BlockSpec(memory_space=pltpu.SMEM)] + [anywhere] * len(sources),
        out_specs=[pl.BlockSpec(memory_space=pltpu.VMEM)] * len(jobs),
        scratch_shapes=[pltpu.SemaphoreType.DMA((len(plan),))],
        compiler_params=pltpu.CompilerParams(vmem_limit_bytes=VMEM_LIMIT),
        cost_estimate=LIGHT,
    )(jnp.stack(chip_place()).astype(jnp.int32), *sources)


def total(terms):
    result = terms[0].astype(f32)
    for term in terms[1:]:
        result = result + term.astype(f32)
    return result


def reduce_send(terms, axis, dim, wire):
    place, size = chip_place()[dim], chip_dims()[dim]
    pick = lambda at: [lax.dynamic_index_in_dim(term, at, axis=axis, keepdims=False) for term in terms]
    received = [moved(total(pick((place + by) % size)).astype(wire), dim, by) for by in range(1, size)]
    return pick(place), received


def reduce_first(partials, wire=bf16):
    parts = []
    for half, (axis, dim) in enumerate(((1, 1), (0, 0))):
        place, size = chip_place()[dim], chip_dims()[dim]
        cuts = [(partial, *column_parts(partial.shape[-1])[half]) for partial in partials]
        pick = lambda at: jnp.concatenate(
            [
                lax.dynamic_index_in_dim(partial[..., begin:end], at, axis=axis, keepdims=False)
                for partial, begin, end in cuts
            ],
            axis=-1,
        )
        received = [moved(pick((place + by) % size).astype(wire), dim, by) for by in range(1, size)]
        parts.append(([pick(place)], received))
    return parts


def reduce_second(first, wire=bf16):
    return [
        reduce_send(first[0][0] + first[0][1], 0, 0, wire),
        reduce_send(first[1][0] + first[1][1], 0, 1, wire),
    ]


def reduce_third(second, wire=bf16):
    joined = jnp.concatenate([total(kept + received) for kept, received in second], axis=-1)
    return [reduce_send([joined], 0, 2, wire)]


def reduce_end(third):
    return total(third[0][0] + third[0][1])


def arrivals(parts):
    return [received for _, received in parts]


def arrived(parts, received):
    return [(kept, new) for (kept, _), new in zip(parts, received)]


def line_perm(turn, back):
    line = lax.axis_size("seg")
    parts = line // SEGS
    pairs = []
    for core in range(2):
        for place in range(line):
            piece = (place % SEGS) ^ turn
            half, index = divmod(piece, 2)
            source = core * line + place
            target = half * line + (2 * core + index) * parts + place // SEGS
            pairs.append((target, source) if back else (source, target))
    return pairs


def whole_sequence(array, core, place):
    parts = lax.axis_size("seg") // SEGS
    half = array.shape[1] // 2
    pieces = array.reshape(2, 2, half, -1).transpose(1, 0, 2, 3).reshape(4, half, -1)
    mine = place % SEGS
    target = 2 * core + (place // parts) % 2
    got = []
    for turn in range(4):
        piece = lax.dynamic_index_in_dim(pieces, mine ^ turn, axis=0, keepdims=False)
        got.append(lax.ppermute(piece, ("core", "seg"), line_perm(turn, False)))
    got = jnp.stack(got)
    return jnp.stack([lax.dynamic_index_in_dim(got, target ^ k, axis=0, keepdims=False) for k in range(4)])


def back_to_owner(ordered, core, place):
    parts = lax.axis_size("seg") // SEGS
    half = ordered.shape[1]
    mine = place % SEGS
    target = 2 * core + (place // parts) % 2
    got = []
    for turn in range(4):
        piece = lax.dynamic_index_in_dim(ordered, target ^ turn, axis=0, keepdims=False)
        got.append(lax.ppermute(piece, ("core", "seg"), line_perm(turn, True)))
    got = jnp.stack(got)
    pieces = jnp.stack([lax.dynamic_index_in_dim(got, mine ^ k, axis=0, keepdims=False) for k in range(4)])
    return pieces.reshape(2, 2, half, -1).transpose(1, 0, 2, 3).reshape(2, 2 * half, -1)


def part_pairs(step):
    line = lax.axis_size("seg")
    parts = line // SEGS
    return [(i, i + step) for i in range(line) if 0 <= i + step < line and i // parts == (i + step) // parts]


def entering(decay, state, step):
    parts = lax.axis_size("seg") // SEGS
    total = jnp.zeros_like(state)
    for _ in range(parts - 1):
        total = lax.ppermute(decay * total + state, "seg", part_pairs(step))
    return total


def borrowed(array, step):
    parts = lax.axis_size("seg") // SEGS
    if parts == 1:
        return jnp.zeros_like(array)
    return lax.ppermute(array, "seg", part_pairs(step))


def spilled(grad, edge, taps):
    if lax.axis_size("seg") == SEGS:
        return grad
    edge = borrowed(edge, -1)
    spill = jnp.stack(
        [
            sum(taps[k] * edge[CONV - 1 - k - early] for k in range(CONV - early))
            for early in range(CONV - 1, 0, -1)
        ]
    )
    at = grad.shape[0] - CONV + 1
    return grad.at[at:].set((grad[at:].astype(f32) + spill).astype(bf16))


def dot(a, b, contract):
    return lax.dot_general(a, b, (contract, ((), ())), preferred_element_type=f32)


def normed_kernel(slabs, core_ref, mine_ref, other_ref, gain_ref, normed_ref, turned_ref):
    mine, other = mine_ref[0], other_ref[0]
    first = core_ref[0] == 0
    hidden = jnp.concatenate([jnp.where(first, mine, other), jnp.where(first, other, mine)], axis=0).astype(f32)
    scale = lax.rsqrt(jnp.mean(hidden * hidden, axis=1, keepdims=True) + epsilon)
    normed = hidden * scale * gain_ref[...]
    normed_ref[...] = normed.astype(bf16)
    turned = normed.T.astype(bf16)
    for to, at, size in slabs:
        turned_ref[to : to + size] = turned[at : at + size]


def normed_tokens(core, mine, other, gain, rows):
    segs, half, width = mine.shape
    a, b, z = chip_dims()
    group = 2 * z * rows
    inside = rows % 16 == 0
    slabs = [(0, 0, width)]
    if inside:
        slabs = [
            (chip * group + (at * 2 + core_at) * rows, chip * group + (core_at * z + at) * rows, rows)
            for chip in range(a * b)
            for core_at in range(2)
            for at in range(z)
        ]
    normed, turned = pl.pallas_call(
        lambda *refs: normed_kernel(slabs, *refs),
        grid_spec=pltpu.PrefetchScalarGridSpec(
            num_scalar_prefetch=1,
            grid=(segs,),
            in_specs=[
                pl.BlockSpec((1, half, width), lambda i, core: (i, 0, 0)),
                pl.BlockSpec((1, half, width), lambda i, core: (i, 0, 0)),
                pl.BlockSpec((1, width), lambda i, core: (0, 0)),
            ],
            out_specs=(
                pl.BlockSpec((2 * half, width), lambda i, core: (i, 0)),
                pl.BlockSpec((width, 2 * half), lambda i, core: (0, i)),
            ),
        ),
        out_shape=(
            jax.ShapeDtypeStruct((segs * 2 * half, width), bf16),
            jax.ShapeDtypeStruct((width, segs * 2 * half), bf16),
        ),
        compiler_params=pltpu.CompilerParams(dimension_semantics=("arbitrary",), vmem_limit_bytes=VMEM_LIMIT),
        cost_estimate=LIGHT,
    )(core.reshape(1).astype(jnp.int32), mine, other, gain.reshape(1, width))
    if not inside:
        turned = turned.reshape(a, b, 2, z, rows, -1).transpose(0, 1, 3, 2, 4, 5).reshape(turned.shape)
    return normed, turned


def mixed_kernel(gated_ref, scale_ref, gain_ref, mixed_ref, turned_ref):
    mixed = gated_ref[...] * scale_ref[...] * gain_ref[...]
    mixed_ref[...] = mixed.astype(bf16)
    turned_ref[...] = mixed.T.astype(bf16)


def mixed_tokens(gated, scale, gain, seg_len):
    length, width = gated.shape
    return pl.pallas_call(
        mixed_kernel,
        grid=(length // seg_len,),
        in_specs=[
            pl.BlockSpec((seg_len, width), lambda i: (i, 0)),
            pl.BlockSpec((seg_len, 1), lambda i: (i, 0)),
            pl.BlockSpec((1, width), lambda i: (0, 0)),
        ],
        out_specs=(
            pl.BlockSpec((seg_len, width), lambda i: (i, 0)),
            pl.BlockSpec((width, seg_len), lambda i: (0, i)),
        ),
        out_shape=(
            jax.ShapeDtypeStruct((length, width), bf16),
            jax.ShapeDtypeStruct((width, length), bf16),
        ),
        compiler_params=pltpu.CompilerParams(dimension_semantics=("arbitrary",), vmem_limit_bytes=VMEM_LIMIT),
        cost_estimate=LIGHT,
    )(gated, scale, gain.reshape(1, width))


def columns_of(pair):
    return pl.ds(pair * LANES, LANES)


def low_half(shape):
    return lax.broadcasted_iota(jnp.int32, shape, len(shape) - 1) < HEADDIM


def pair_columns(array, pair, low):
    rows = array.shape[0]
    first = jnp.broadcast_to(array[:, 2 * pair : 2 * pair + 1], (rows, LANES))
    second = jnp.broadcast_to(array[:, 2 * pair + 1 : 2 * pair + 2], (rows, LANES))
    return jnp.where(low, first, second)


def conv_parts(current, before, taps):
    rows = current.shape[0]
    padded = jnp.concatenate([before, current], axis=0)
    seen = [padded[8 - CONV + 1 + k : 8 - CONV + 1 + k + rows] for k in range(CONV - 1)] + [current]
    total = taps[CONV : CONV + 1]
    for k in range(CONV):
        total = total + taps[k : k + 1] * seen[k]
    return total, seen


def step_terms(raw, head, seg_len):
    shifted = raw + head[1:2]
    step = jnp.maximum(shifted, 0.0) + jnp.log1p(jnp.exp(-jnp.abs(shifted)))
    log_decay = step * head[0:1]
    at_or_before = lax.broadcasted_iota(jnp.int32, (seg_len, seg_len), 0) >= lax.broadcasted_iota(
        jnp.int32, (seg_len, seg_len), 1
    )
    sums = lax.dot_general(
        jnp.where(at_or_before, 1.0, 0.0), log_decay, (((1,), (0,)), ((), ())),
        precision=lax.Precision.HIGHEST, preferred_element_type=f32,
    )
    return shifted, step, log_decay, sums * LOG2E


def forward_kernel(
    proj_ref, taps_ref, head_ref, skip_ref, rim_ref, init_ref,
    values_ref, prior_ref, final_ref, last_ref, state_ref, tail_ref,
):
    seg_len = proj_ref.shape[0]
    half = seg_len // 2

    @pl.when(pl.program_id(0) == 0)
    def _():
        state_ref[...] = init_ref[...]
        tail_ref[...] = rim_ref[...]

    def activated(begin):
        at = pl.ds(begin, LANES)
        total, _ = conv_parts(proj_ref[:, at], tail_ref[:, at], taps_ref[:, at])
        return total * jax.nn.sigmoid(total)

    b_low = activated(HALF).astype(bf16)
    b_turned = activated(HALF).T.astype(bf16)
    c_low = activated(HALF + STATE).astype(bf16)
    _, step, _, sums = step_terms(proj_ref[:, HALF + 2 * STATE :], head_ref, seg_len)
    sums_turned, step_turned = sums.T, step.T
    scores = dot(c_low, b_low, ((1,), (1,)))
    kept = lax.broadcasted_iota(jnp.int32, (half, half), 0) >= lax.broadcasted_iota(jnp.int32, (half, half), 1)
    first_scores = jnp.where(kept, scores[:half, :half], 0.0)
    later_scores = scores[half:, :half]
    second_scores = jnp.where(kept, scores[half:, half:], 0.0)
    low = low_half((seg_len, LANES))
    last_ref[...] = jnp.broadcast_to(sums[seg_len - 1 :], last_ref.shape)

    for pair in range(HEADS // 4):
        at = columns_of(pair)
        x_values = activated(pair * LANES)
        x_low = x_values.astype(bf16)
        sums_pair = pair_columns(sums, pair, low)
        last_pair = sums_pair[seg_len - 1 :]
        carry = jnp.exp2(last_pair - sums_pair) * pair_columns(step, pair, low)
        scaled_x = (carry * x_low.astype(f32)).astype(bf16)
        prior = state_ref[:, at]
        prior_low = prior.astype(bf16)
        prior_ref[0, :, at] = prior_low
        from_state = jnp.exp2(sums_pair) * dot(c_low, prior_low, ((1,), (0,)))
        state_ref[:, at] = jnp.exp2(last_pair) * prior + dot(b_turned, scaled_x, ((1,), (0,)))
        early, late = 0.0, 0.0
        for side in range(2):
            head = 2 * pair + side
            x_side = jnp.where(low if side == 0 else ~low, x_values, 0.0).astype(bf16)
            at_token = jnp.broadcast_to(sums[:, head : head + 1], (seg_len, half))
            at_source, source_step = sums_turned[head : head + 1], step_turned[head : head + 1]
            first = jnp.exp2(jnp.minimum(at_token[:half] - at_source[:, :half], 0.0)) * first_scores
            first = (first * source_step[:, :half]).astype(bf16)
            later = jnp.exp2(at_token[half:] - at_source[:, :half]) * later_scores
            later = (later * source_step[:, :half]).astype(bf16)
            second = jnp.exp2(jnp.minimum(at_token[half:] - at_source[:, half:], 0.0)) * second_scores
            second = (second * source_step[:, half:]).astype(bf16)
            early = early + dot(first, x_side[:half], ((1,), (0,)))
            late = late + dot(jnp.concatenate([later, second], axis=1), x_side, ((1,), (0,)))
        intra = jnp.concatenate([early, late], axis=0)
        values_ref[:, at] = intra + from_state + skip_ref[:, at] * x_values

    tail_ref[...] = proj_ref[seg_len - 8 :, : HALF + 2 * STATE]
    final_ref[...] = state_ref[...]


def full_block(shape):
    return pl.BlockSpec(shape, lambda *_: (0,) * len(shape))


def scan_forward(proj, taps, head, skip, rim, init, seg_len):
    segs = proj.shape[0] // seg_len
    wide = HALF + 2 * STATE
    return pl.pallas_call(
        forward_kernel,
        grid=(segs,),
        out_shape=(
            jax.ShapeDtypeStruct((proj.shape[0], HALF), f32),
            jax.ShapeDtypeStruct((segs, STATE, HALF), bf16),
            jax.ShapeDtypeStruct((STATE, HALF), f32),
            jax.ShapeDtypeStruct((segs * 8, LANES), f32),
        ),
        in_specs=[
            pl.BlockSpec((seg_len, proj.shape[1]), lambda i: (i, 0)),
            full_block((8, wide)),
            full_block((8, LANES)),
            full_block((1, HALF)),
            full_block((8, wide)),
            full_block((STATE, HALF)),
        ],
        out_specs=(
            pl.BlockSpec((seg_len, HALF), lambda i: (i, 0)),
            pl.BlockSpec((1, STATE, HALF), lambda i: (i, 0, 0)),
            full_block((STATE, HALF)),
            pl.BlockSpec((8, LANES), lambda i: (i, 0)),
        ),
        scratch_shapes=[pltpu.VMEM((STATE, HALF), f32), pltpu.VMEM((8, wide), f32)],
        compiler_params=pltpu.CompilerParams(
            dimension_semantics=("arbitrary",), vmem_limit_bytes=VMEM_LIMIT
        ),
        cost_estimate=LIGHT,
    )(proj, taps, head, skip, rim, init)


def split_dot(array, other):
    high = array.astype(bf16)
    rest = (array - high.astype(f32)).astype(bf16)
    return dot(high, other, ((1,), (0,))) + dot(rest, other, ((1,), (0,)))


def backward_kernel(
    group, proj_ref, before_ref, taps_ref, rim_ref, shared_ref, shared_before_ref, shared_taps_ref, shared_rim_ref,
    head_ref, skip_ref, heads_ref, end_ref, prior_ref, values_ref, grad_ref, core_ref,
    grad_x_ref, mine_ref, theirs_ref, grad_raw_ref, taps_grad_ref, skip_grad_ref, head_grad_ref, edge_ref, start_ref,
    later_ref, local_ref, scaled_ref, grad_state_ref, inner_ref, source_ref, carry_ref, decay_ref,
):
    seg_len = proj_ref.shape[0]
    half = seg_len // 2
    turn = pl.program_id(0)

    @pl.when(turn == 0)
    def _():
        later_ref[...] = end_ref[...]
        edge_ref[...] = jnp.zeros_like(edge_ref)
        taps_grad_ref[...] = jnp.zeros_like(taps_grad_ref)
        skip_grad_ref[...] = jnp.zeros_like(skip_grad_ref)
        head_grad_ref[...] = jnp.zeros_like(head_grad_ref)

    first_segment = turn == pl.num_programs(0) - 1

    def conv_at(at, current, ahead, taps, rim):
        before = jnp.where(first_segment, rim[:, at], ahead[:, at])
        return conv_parts(current[:, at], before, taps[:, at])

    def activated(begin):
        total, _ = conv_at(pl.ds(begin, LANES), shared_ref, shared_before_ref, shared_taps_ref, shared_rim_ref)
        return total * jax.nn.sigmoid(total)

    b_values = activated(0)
    c_values = activated(STATE)
    b_low, c_low, c_turned = b_values.astype(bf16), c_values.astype(bf16), c_values.T.astype(bf16)
    shifted, step, log_decay, sums = step_terms(shared_ref[:, 2 * STATE :], head_ref, seg_len)
    sums_turned = sums.T
    scores = dot(b_low, c_low, ((1,), (1,)))
    kept = lax.broadcasted_iota(jnp.int32, (half, half), 0) <= lax.broadcasted_iota(jnp.int32, (half, half), 1)
    first_scores = jnp.where(kept, scores[:half, :half], 0.0)
    later_scores = scores[:half, half:]
    second_scores = jnp.where(kept, scores[half:, half:], 0.0)
    low = low_half((seg_len, LANES))
    first_grad, later_grad, second_grad = 0.0, 0.0, 0.0

    pairs = grad_ref.shape[1] // LANES
    for pair in range(pairs):
        at = columns_of(pair)
        total, seen = conv_at(at, proj_ref, before_ref, taps_ref, rim_ref)
        sigmoid = jax.nn.sigmoid(total)
        x_values = total * sigmoid
        x_low = x_values.astype(bf16)
        x_wide = x_low.astype(f32)
        sums_pair = pair_columns(sums, group * pairs + pair, low)
        step_pair = pair_columns(step, group * pairs + pair, low)
        last_pair = sums_pair[seg_len - 1 :]
        gap = jnp.exp2(last_pair - sums_pair)
        scaled_ref[:, at] = (gap * step_pair * x_wide).astype(bf16)
        grad_values = grad_ref[:, at]
        grad_state_ref[:, at] = (grad_values * jnp.exp2(sums_pair)).astype(bf16)
        later = later_ref[:, at]
        later_low = later.astype(bf16)
        local_ref[:, at] = later_low
        prior = prior_ref[0, :, at]
        decay_ref[:, at] = jnp.broadcast_to(
            jnp.sum(later * prior.astype(f32), axis=0, keepdims=True), (8, LANES)
        )
        grad_prior = dot(c_turned, grad_state_ref[:, at], ((1,), (0,)))
        later_ref[:, at] = jnp.exp2(last_pair) * later + grad_prior
        grad_scaled = dot(b_low, later_low, ((1,), (0,)))
        stepped = (step_pair * x_wide).astype(bf16)
        early, late = 0.0, 0.0
        for side in range(2):
            head = 2 * (group * pairs + pair) + side
            grad_low = jnp.where(low if side == 0 else ~low, grad_values, 0.0).astype(bf16)
            at_source = jnp.broadcast_to(sums[:, head : head + 1], (seg_len, half))
            at_token = sums_turned[head : head + 1]
            grad_weights = dot(stepped, grad_low, ((1,), (1,)))
            first = jnp.exp2(jnp.minimum(at_token[:, :half] - at_source[:half], 0.0))
            after = jnp.exp2(at_token[:, half:] - at_source[:half])
            second = jnp.exp2(jnp.minimum(at_token[:, half:] - at_source[half:], 0.0))
            first_grad = first_grad + first * grad_weights[:half, :half]
            later_grad = later_grad + after * grad_weights[:half, half:]
            second_grad = second_grad + second * grad_weights[half:, half:]
            upper = jnp.concatenate([first * first_scores, after * later_scores], axis=1).astype(bf16)
            early = early + dot(upper, grad_low, ((1,), (0,)))
            late = late + dot((second * second_scores).astype(bf16), grad_low[half:], ((1,), (0,)))
        inner = jnp.concatenate([early, late], axis=0)
        skip = skip_ref[:, at]
        skip_grad_ref[:, at] += jnp.sum(grad_values * x_values, axis=0, keepdims=True)
        inner_ref[:, at] = grad_values * (values_ref[:, at] - skip * x_values)
        source_ref[:, at] = x_wide * inner
        carry_ref[:, at] = x_wide * grad_scaled
        grad_x = skip * grad_values + step_pair * (inner + gap * grad_scaled)
        grad_total = grad_x * (sigmoid * (1.0 + total * (1.0 - sigmoid)))
        for k in range(CONV):
            taps_grad_ref[k : k + 1, at] += jnp.sum(grad_total * seen[k], axis=0, keepdims=True)
        taps_grad_ref[CONV : CONV + 1, at] += jnp.sum(grad_total, axis=0, keepdims=True)
        extended = jnp.concatenate([grad_total, edge_ref[:, at]], axis=0)
        edge_ref[:, at] = grad_total[:8]
        taps = taps_ref[:, at]
        grad_conv = taps[CONV - 1 : CONV] * grad_total
        for k in range(CONV - 1):
            grad_conv = grad_conv + taps[k : k + 1] * extended[CONV - 1 - k : CONV - 1 - k + seg_len]
        grad_x_ref[:, at] = grad_conv.astype(bf16)

    heads = heads_ref[...]
    tail = jnp.exp2(sums[seg_len - 1 :] - sums)
    source_grad = split_dot(source_ref[...], heads)
    step_grad = source_grad + tail * split_dot(carry_ref[...], heads)
    used = step * step_grad
    sum_grad = split_dot(inner_ref[...], heads) - used
    at_last = jnp.sum(used - step * source_grad, axis=0, keepdims=True)
    at_last = at_last + split_dot(decay_ref[...], heads)[:1] * jnp.exp2(sums[seg_len - 1 :])
    is_last = lax.broadcasted_iota(jnp.int32, (seg_len, LANES), 0) == seg_len - 1
    sum_grad = sum_grad + jnp.where(is_last, at_last, 0.0)
    at_or_after = lax.broadcasted_iota(jnp.int32, (seg_len, seg_len), 0) <= lax.broadcasted_iota(
        jnp.int32, (seg_len, seg_len), 1
    )
    log_grad = lax.dot_general(
        jnp.where(at_or_after, 1.0, 0.0), sum_grad, (((1,), (0,)), ((), ())),
        precision=lax.Precision.HIGHEST, preferred_element_type=f32,
    )
    grad_raw = (step_grad + head_ref[0:1] * log_grad) * jax.nn.sigmoid(shifted)
    grad_raw_ref[...] = grad_raw
    head_grad_ref[0:1] += jnp.sum(log_grad * log_decay, axis=0, keepdims=True)
    head_grad_ref[1:2] += jnp.sum(grad_raw, axis=0, keepdims=True)

    first_low = jnp.where(kept, first_grad, 0.0)
    second_low = jnp.where(kept, second_grad, 0.0)
    grad_scores = jnp.concatenate(
        [
            jnp.concatenate([first_low, later_grad], axis=1),
            jnp.concatenate([jnp.zeros_like(first_low), second_low], axis=1),
        ],
        axis=0,
    )
    start_ref[...] = later_ref[...]
    grad_b = dot(scaled_ref[...], local_ref[...], ((1,), (1,))) + dot(
        grad_scores.astype(bf16), c_low, ((1,), (0,))
    )
    grad_c = dot(grad_state_ref[...], prior_ref[0], ((1,), (1,))) + dot(
        grad_scores.T.astype(bf16), b_low, ((1,), (0,))
    )
    first = core_ref[0] == 0
    mine_ref[...] = jnp.where(first, grad_b, grad_c)
    theirs_ref[...] = jnp.where(first, grad_c, grad_b)


GROUPS = 1


def scan_backward(group, core, proj, taps, head, skip, rim, end, prior, values, grad_values, seg_len):
    length = proj.shape[0]
    segs = length // seg_len
    width, shared = HALF // GROUPS, proj.shape[1] - HALF
    channel = lax.broadcasted_iota(jnp.int32, (width, LANES), 0) // HEADDIM + group * width // HEADDIM
    heads = (channel == lax.broadcasted_iota(jnp.int32, (width, LANES), 1)).astype(bf16)
    back = lambda width, at=0: pl.BlockSpec((seg_len, width), lambda i: (segs - 1 - i, at))
    row_ahead = lambda i: jnp.maximum((segs - 1 - i) * (seg_len // 8) - 1, 0)
    ahead = lambda width, at: pl.BlockSpec((8, width), lambda i: (row_ahead(i), at))
    column = lambda rows, width, at: pl.BlockSpec((rows, width), lambda i: (0, at))
    both = HALF // shared
    taps, rim = jnp.pad(taps, ((0, 0), (0, shared - 2 * STATE))), jnp.pad(rim, ((0, 0), (0, shared - 2 * STATE)))
    return pl.pallas_call(
        lambda *refs: backward_kernel(group, *refs),
        grid=(segs,),
        out_shape=(
            jax.ShapeDtypeStruct((length, width), bf16),
            jax.ShapeDtypeStruct((length, STATE), f32),
            jax.ShapeDtypeStruct((length, STATE), f32),
            jax.ShapeDtypeStruct((length, LANES), f32),
            jax.ShapeDtypeStruct((8, width), f32),
            jax.ShapeDtypeStruct((1, width), f32),
            jax.ShapeDtypeStruct((8, LANES), f32),
            jax.ShapeDtypeStruct((8, width), f32),
            jax.ShapeDtypeStruct((STATE, width), f32),
        ),
        in_specs=[
            back(width, group),
            ahead(width, group),
            column(8, width, group),
            column(8, width, group),
            back(shared, both),
            ahead(shared, both),
            column(8, shared, both),
            column(8, shared, both),
            full_block((8, LANES)),
            column(1, width, group),
            full_block((width, LANES)),
            column(STATE, width, group),
            pl.BlockSpec((1, STATE, width), lambda i: (segs - 1 - i, 0, group)),
            back(width, group),
            back(width, group),
            pl.BlockSpec(memory_space=pltpu.SMEM),
        ],
        out_specs=(
            back(width),
            back(STATE),
            back(STATE),
            back(LANES),
            full_block((8, width)),
            full_block((1, width)),
            full_block((8, LANES)),
            full_block((8, width)),
            full_block((STATE, width)),
        ),
        scratch_shapes=[
            pltpu.VMEM((STATE, width), f32),
            pltpu.VMEM((STATE, width), bf16),
            pltpu.VMEM((seg_len, width), bf16),
            pltpu.VMEM((seg_len, width), bf16),
            pltpu.VMEM((seg_len, width), f32),
            pltpu.VMEM((seg_len, width), f32),
            pltpu.VMEM((seg_len, width), f32),
            pltpu.VMEM((8, width), f32),
        ],
        compiler_params=pltpu.CompilerParams(
            dimension_semantics=("arbitrary",), vmem_limit_bytes=VMEM_LIMIT
        ),
        cost_estimate=LIGHT,
    )(
        proj, proj, taps, rim, proj, proj, taps, rim, head, skip, heads, end, prior, values, grad_values,
        core.reshape(1).astype(jnp.int32),
    )


def half_kernel(transposed, count, core_ref, *refs):
    inputs, mine_ref, theirs_ref = refs[: 2 * count], refs[-2], refs[-1]
    total = refs[2 * count][...] if len(refs) > 2 * count + 2 else 0.0
    for left, right in zip(inputs[:count], inputs[count:]):
        total = total + dot(left[...], right[...], ((1,), (1 if transposed else 0,)))
    half = total.shape[0] // 2
    first = core_ref[0] == 0
    mine_ref[0] = jnp.where(first, total[:half], total[half:])
    theirs_ref[0] = jnp.where(first, total[half:], total[:half]).astype(bf16)


def half_products(core, terms, seg_len, width, transposed, base=()):
    length = terms[0][0].shape[0]
    left = [pl.BlockSpec((seg_len, array.shape[1]), lambda i, core: (i, 0)) for array, _, _ in terms]
    right = []
    for array, matrix, at in terms:
        if transposed:
            right.append(pl.BlockSpec((width, array.shape[1]), lambda i, core, at=at: (0, at(core[0]))))
        else:
            right.append(pl.BlockSpec(matrix.shape, lambda i, core: (0, 0)))
    depth = sum(array.shape[1] for array, _, _ in terms)
    mine, theirs = pl.pallas_call(
        lambda *refs: half_kernel(transposed, len(terms), *refs),
        grid_spec=pltpu.PrefetchScalarGridSpec(
            num_scalar_prefetch=1,
            grid=(length // seg_len,),
            in_specs=left + right + [pl.BlockSpec((seg_len, width), lambda i, core: (i, 0)) for _ in base],
            out_specs=[pl.BlockSpec((1, seg_len // 2, width), lambda i, core: (i, 0, 0))] * 2,
        ),
        out_shape=(
            jax.ShapeDtypeStruct((length // seg_len, seg_len // 2, width), f32),
            jax.ShapeDtypeStruct((length // seg_len, seg_len // 2, width), bf16),
        ),
        compiler_params=pltpu.CompilerParams(dimension_semantics=("arbitrary",), vmem_limit_bytes=VMEM_LIMIT),
        cost_estimate=LIGHT,
    )(core.reshape(1).astype(jnp.int32), *[array for array, _, _ in terms], *[matrix for _, matrix, _ in terms], *base)
    return mine, theirs


def shared_kernel(core_ref, proj_ref, rim_ref, taps_ref, mine_ref, other_ref, grad_ref, taps_grad_ref, edge_ref):
    total, seen = conv_parts(proj_ref[...], rim_ref[...], taps_ref[...])
    sigmoid = jax.nn.sigmoid(total)
    grad_total = mine_ref[...] + other_ref[...]
    grad_total = grad_total * (sigmoid * (1.0 + total * (1.0 - sigmoid)))
    sums = [jnp.sum(grad_total * part, axis=0, keepdims=True) for part in seen]
    sums = sums + [jnp.sum(grad_total, axis=0, keepdims=True), jnp.zeros((8 - CONV - 1, LANES), f32)]
    taps_grad_ref[...] = jnp.concatenate(sums, axis=0)
    edge_ref[...] = grad_total[:8]
    taps = taps_ref[...]
    extended = jnp.concatenate([grad_total, jnp.zeros((8, LANES), f32)], axis=0)
    grad_conv = taps[CONV - 1 : CONV] * grad_total
    for k in range(CONV - 1):
        grad_conv = grad_conv + taps[k : k + 1] * extended[CONV - 1 - k : CONV - 1 - k + grad_total.shape[0]]
    grad_ref[...] = grad_conv.astype(bf16)


def shared_backward(core, proj, rim, taps, mine, other):
    length = proj.shape[0]
    picked = lambda rows: pl.BlockSpec((rows, LANES), lambda i, core: (0, HALF // LANES + core[0]))
    whole = lambda rows: pl.BlockSpec((rows, LANES), lambda i, core: (0, 0))
    return pl.pallas_call(
        shared_kernel,
        grid_spec=pltpu.PrefetchScalarGridSpec(
            num_scalar_prefetch=1,
            grid=(1,),
            in_specs=[picked(length), picked(8), picked(8), whole(length), whole(length)],
            out_specs=(whole(length), whole(8), whole(8)),
        ),
        out_shape=(
            jax.ShapeDtypeStruct((length, LANES), bf16),
            jax.ShapeDtypeStruct((8, LANES), f32),
            jax.ShapeDtypeStruct((8, LANES), f32),
        ),
        compiler_params=pltpu.CompilerParams(vmem_limit_bytes=VMEM_LIMIT),
        cost_estimate=LIGHT,
    )(core.reshape(1).astype(jnp.int32), proj, rim, taps, mine, other)


def per_device(hidden_in, cotangent, in_proj, out_proj, conv_params, pre_gain, gated_gain, head_params):
    chips, line = lax.axis_size("chip"), lax.axis_size("seg")
    core, place = lax.axis_index("core"), lax.axis_index("seg")
    rows, model_width = in_proj.shape[0], hidden_in.shape[2]
    heads = HEADS // 2

    conv_width, gain_width = conv_params.shape[1], gated_gain.shape[0]
    used = HALF + 2 * STATE + heads
    spare = -used % LANES
    small = jnp.zeros((rows, spare), bf16)
    small = small.at[: CONV + 1, :conv_width].set(conv_params)
    small = small.at[CONV + 1, :rows].set(pre_gain)
    small = small.at[CONV + 2, :gain_width].set(gated_gain)

    def conv_side(which):
        return jnp.concatenate(
            [
                own_columns(in_proj[:, INNER : 2 * INNER], which),
                in_proj[:, 2 * INNER : INNER + XBC],
                own_columns(in_proj[:, INNER + XBC :], which),
                small,
            ],
            axis=1,
        )

    def gate_side(which):
        return own_columns(in_proj[:, :INNER], which)

    conv_swap = to_partner(conv_side(1 - core))
    conv_block = in_core_order(conv_side(core), conv_swap, core, 0)
    conv_z = gather_first(conv_block)
    gate_swap = to_partner(gate_side(1 - core))
    gate_block = in_core_order(gate_side(core), gate_swap, core, 0)
    conv_z, gate_block = tie(conv_z, gate_block)
    conv_2 = gather_next(conv_z, 1)
    gate_z = gather_first(gate_block)
    conv_2, gate_z, hidden_in = tie(conv_2, gate_z, hidden_in)
    conv_last = gather_next(conv_2, 2)
    hidden_half = whole_sequence(hidden_in, core, place)
    conv_last, hidden_half, gate_z = tie(conv_last, hidden_half, gate_z)
    hidden_other = to_partner(hidden_half)
    gate_2 = gather_next(gate_z, 1)
    conv_all = whole_matrices([(True, conv_last)])[0].reshape(model_width, -1)

    small_all = conv_all.reshape(chips, 2, line, rows, -1)[..., used:].astype(f32)
    taps_full = small_all[..., : CONV + 1, :conv_width].transpose(3, 0, 1, 2, 4).reshape(CONV + 1, XBC)
    taps = jnp.concatenate([own_columns(taps_full[:, :INNER], core), taps_full[:, INNER:]], axis=1)
    gain_pre = small_all[..., CONV + 1, :rows].reshape(model_width)
    gain_gate = lax.dynamic_index_in_dim(
        small_all[..., CONV + 2, :gain_width], core, axis=1, keepdims=False
    ).reshape(HALF)
    params = own_columns(head_params, core)

    seg_len = 2 * hidden_half.shape[1]
    tokens = SEGS * seg_len
    normed, normed_turned = normed_tokens(core, hidden_half, hidden_other, gain_pre, rows)
    projected = dot(normed, conv_all, ((1,), (0,)))
    projected, gate_2, out_proj = tie(projected, gate_2, out_proj)
    gate_last = gather_next(gate_2, 2)
    out_z = gather_first(out_proj.reshape(2, -1, model_width))

    taps = jnp.pad(taps, ((0, 8 - CONV - 1), (0, 0)))
    head = jnp.pad(jnp.stack([-jnp.exp(params[0]), params[1]]), ((0, 6), (0, LANES - heads)))
    skip = jnp.repeat(params[2], HEADDIM).reshape(1, HALF)
    wide = HALF + 2 * STATE
    rim = borrowed(projected[tokens - 8 :, :wide], 1)
    nothing = jnp.zeros((STATE, HALF), f32)
    values, prior, final, last = scan_forward(projected, taps, head, skip, rim, nothing, seg_len)
    if line > SEGS:
        last = jnp.sum(last.reshape(SEGS, 8, LANES)[:, 0, :heads], axis=0)
        decay = jnp.repeat(jnp.exp2(last), HEADDIM)
        begin = entering(decay, final, 1)
        values, prior, _, _ = scan_forward(projected, taps, head, skip, rim, begin, seg_len)

    values, gate_last, out_z, cotangent = tie(values, gate_last, out_z, cotangent)
    out_2 = gather_next(out_z, 1)
    cot_half = whole_sequence(cotangent, core, place)
    cot_other = to_partner(cot_half)
    cot = in_core_order(cot_half, cot_other, core, 1)
    upstream = cot.reshape(tokens, model_width)
    gate_matrix = whole_matrices([(True, gate_last)])[0].reshape(model_width, HALF)
    gate_input = dot(normed, gate_matrix, ((1,), (0,)))

    silu_gate = jax.nn.silu(gate_input)
    gated = values * silu_gate
    squares = jnp.sum(gated * gated, axis=1)
    squares_other = to_partner(squares)
    scale = lax.rsqrt((squares + squares_other) / INNER + epsilon)[:, None]
    scale, out_2 = tie(scale, out_2)
    out_last = gather_next(out_2, 2)
    mixed, mixed_turned = mixed_tokens(gated, scale, gain_gate, seg_len)
    by_owner = lambda grad: grad.astype(bf16).reshape(chip_dims() + (-1, grad.shape[1]))
    out_grad = by_owner(dot(mixed_turned, upstream, ((1,), (0,))))
    out_grad, out_last = tie(out_grad, out_last)
    out_first = reduce_first([out_grad])
    out_matrix = whole_matrices([(False, out_last)])[0].reshape(HALF, model_width)
    branch, branch_sent = half_products(core, [(mixed, out_matrix, None)], seg_len, model_width, False)
    branch_sent, upstream = tie(branch_sent, upstream)
    branch_other = to_partner(branch_sent)
    grad_mixed = dot(upstream, out_matrix, ((1,), (1,)))
    grad_mixed, out_got = tie(grad_mixed, arrivals(out_first))
    out_second = reduce_second(arrived(out_first, out_got))
    unit = gated * scale
    gain_grad = grad_mixed * gain_gate
    along = jnp.sum(gain_grad * unit, axis=1)
    along_other = to_partner(along)
    along_other, branch_other = tie(along_other, branch_other)
    hidden_out = back_to_owner(
        (hidden_half.astype(f32) + branch + branch_other.astype(f32)).astype(bf16), core, place
    )
    along = ((along + along_other) / INNER)[:, None]
    gate_gain_grad = jnp.sum(grad_mixed * unit, axis=0)
    grad_gated = scale * (gain_grad - unit * along)
    grad_values = grad_gated * silu_gate
    sigmoid = jax.nn.sigmoid(gate_input)
    grad_gate = (grad_gated * values * (sigmoid * (1.0 + gate_input * (1.0 - sigmoid)))).astype(bf16)
    gate_grad = by_owner(dot(normed_turned, grad_gate, ((1,), (0,))))
    gate_grad, grad_values, out_got = tie(gate_grad, grad_values, arrivals(out_second))
    out_second = arrived(out_second, out_got)
    gate_first = reduce_first([gate_grad])
    scan = lambda later: scan_backward(
        0, core, projected, taps, head, skip, rim, later, prior, values, grad_values, seg_len
    )
    if line > SEGS:
        nothing = entering(decay, scan(nothing)[-1], -1)
    back = scan(nothing)
    back, gate_got, hidden_out, grad_gate = tie(back, arrivals(gate_first), hidden_out, grad_gate)
    grad_x, mine, theirs, grad_raw, x_taps_grad, skip_grad, head_sums, x_edge, _ = back
    grad_x = spilled(grad_x, x_edge, taps[:, :HALF])
    other = to_partner(theirs)
    x_grad = by_owner(dot(normed_turned, grad_x, ((1,), (0,))))
    other, x_grad, gate_got = tie(other, x_grad, gate_got)
    gate_second = reduce_second(arrived(gate_first, gate_got))
    out_third = reduce_third(out_second)
    grad_state, state_taps_grad, state_edge = shared_backward(core, projected, rim, taps, mine, other)
    grad_state = spilled(grad_state, state_edge, lax.dynamic_slice_in_dim(taps, HALF + core * STATE, STATE, axis=1))
    grad_raw = grad_raw.astype(bf16)
    rest_grad = by_owner(dot(normed_turned, jnp.concatenate([grad_state, grad_raw], axis=1), ((1,), (0,))))
    head_grad = jnp.concatenate([head_sums[:2, :heads], skip_grad.reshape(1, heads, HEADDIM).sum(axis=2)])
    state_taps_grad = state_taps_grad[: CONV + 1]
    none = jnp.zeros_like(state_taps_grad)
    taps_grad = jnp.concatenate(
        [
            x_taps_grad[: CONV + 1],
            jnp.where(core == 0, state_taps_grad, none),
            jnp.where(core == 0, none, state_taps_grad),
        ],
        axis=1,
    )
    rest_grad, gate_got, grad_gate, grad_state = tie(rest_grad, arrivals(gate_second), grad_gate, grad_state)
    base = dot(grad_gate, gate_matrix, ((1,), (1,)))
    conv_first = reduce_first([x_grad, rest_grad])
    gate_third = reduce_third(arrived(gate_second, gate_got))
    terms = [
        (grad_x, conv_all, lambda core: 0),
        (grad_state, conv_all, lambda core: HALF // LANES + core),
        (grad_raw, conv_all, lambda core: (HALF + 2 * STATE) // LANES),
    ]
    grad_normed, sent_normed = half_products(core, terms, seg_len, model_width, True, (base,))
    sent_normed, out_got, conv_got, taps_grad, gate_gain_grad, head_grad = tie(
        sent_normed, arrivals(out_third), arrivals(conv_first), taps_grad, gate_gain_grad, head_grad
    )
    out_third = arrived(out_third, out_got)
    conv_second = reduce_second(arrived(conv_first, conv_got))
    other_normed = to_partner(sent_normed)
    wide_hidden = hidden_half.astype(f32)
    hidden_scale = lax.rsqrt(jnp.mean(wide_hidden * wide_hidden, axis=-1, keepdims=True) + epsilon)
    grad_normed = (grad_normed + other_normed.astype(f32)) * gain_pre
    hidden_unit = wide_hidden * hidden_scale
    along = jnp.mean(grad_normed * hidden_unit, axis=-1, keepdims=True)
    grad_hidden = hidden_scale * (grad_normed - hidden_unit * along)
    grad_in = (cot_half.astype(f32) + grad_hidden).astype(bf16)
    grad_in, gate_got = tie(grad_in, arrivals(gate_third))
    gate_third = arrived(gate_third, gate_got)
    grad_in = back_to_owner(grad_in, core, place)

    def spread_own(array):
        width = array.shape[-1] // chips
        parted = array.reshape(array.shape[:-1] + (chips, 1, width))
        none = jnp.zeros_like(parted)
        both = jnp.where(
            core == 0,
            jnp.concatenate([parted, none], axis=-2),
            jnp.concatenate([none, parted], axis=-2),
        )
        return both.reshape(array.shape[:-1] + (2 * array.shape[-1],))

    taps_all = jnp.concatenate([spread_own(taps_grad[:, :HALF]), taps_grad[:, HALF:]], axis=1)
    taps_all = taps_all.reshape(CONV + 1, chips, 2, line, conv_width).transpose(1, 3, 2, 0, 4)
    gate_all = spread_own(gate_gain_grad).reshape(chips, 2, line, gain_width).transpose(0, 2, 1, 3)
    head_all = jnp.broadcast_to(spread_own(head_grad).reshape(-1), (chips, line, 2, 3 * HEADS))
    small_grads = jnp.concatenate(
        [
            taps_all.reshape(chips, line, 2, -1),
            gate_all,
            head_all,
        ],
        axis=3,
    )
    count = small_grads.shape[3]
    small_grads = small_grads.reshape(chip_dims() + (2, count))
    small_second = reduce_second(reduce_first([small_grads], f32), f32)
    conv_got, small_got = tie(arrivals(conv_second), arrivals(small_second))
    conv_third = reduce_third(arrived(conv_second, conv_got))
    small_third = reduce_third(arrived(small_second, small_got), f32)
    grad_in, conv_got, small_got = tie(grad_in, arrivals(conv_third), arrivals(small_third))
    conv_third = arrived(conv_third, conv_got)
    small_share = reduce_end(arrived(small_third, small_got))
    out_share = reduce_end(out_third).reshape(-1, model_width)
    paired = lambda third: reduce_end(third).astype(bf16).reshape(2, rows, -1)
    gate_share, conv_share = paired(gate_third), paired(conv_third)

    def mine_and_partner(share):
        keep = lax.dynamic_index_in_dim(share, core, axis=0, keepdims=False)
        give = lax.dynamic_index_in_dim(share, 1 - core, axis=0, keepdims=False)
        return keep, to_partner(give)

    keep, got = mine_and_partner(small_share)
    small_total = keep + got
    taps_end = (CONV + 1) * conv_width
    taps_share = small_total[:taps_end].reshape(CONV + 1, conv_width)
    gain_share = small_total[taps_end : taps_end + gain_width]
    head_total = small_total[taps_end + gain_width :].reshape(3, HEADS)

    def interleave(mine, theirs):
        width = mine.shape[1] // chips
        both = in_core_order(mine.reshape(rows, chips, width), theirs.reshape(rows, chips, width), core, 2)
        return both.reshape(rows, -1)

    keep_gate, got_gate = mine_and_partner(gate_share)
    (_, x_cut), _ = column_parts(HALF)
    (_, state_cut), _ = column_parts(STATE + LANES)
    both = x_cut + state_cut
    conv_share = jnp.concatenate(
        [conv_share[..., :x_cut], conv_share[..., both : both + HALF - x_cut], conv_share[..., x_cut:both], conv_share[..., both + HALF - x_cut :]],
        axis=-1,
    )
    keep, got = mine_and_partner(conv_share)
    state_end = HALF + STATE
    in_share = jnp.concatenate(
        [
            interleave(keep_gate, got_gate),
            interleave(keep[:, :HALF], got[:, :HALF]),
            in_core_order(keep[:, HALF:state_end], got[:, HALF:state_end], core, 1).reshape(rows, -1),
            interleave(keep[:, state_end : state_end + heads], got[:, state_end : state_end + heads]),
        ],
        axis=1,
    ).astype(f32)
    pre_share = jnp.sum(in_proj.astype(f32) * in_share, axis=1) / pre_gain.astype(f32)
    return (hidden_out, grad_in, in_share, out_share, taps_share, pre_share, gain_share, head_total)


def solution(mesh):
    devices = mesh.devices
    cores = Mesh(devices.reshape(devices.shape[0] // 2, 2, devices.shape[1]), ("chip", "core", "seg"))
    dp, both = ("chip", "core"), ("chip", "core", "seg")
    tokens = P(dp, "seg", None)
    return jax.shard_map(
        per_device,
        mesh=cores,
        in_specs=(tokens, tokens, P(both, None), P(both, None), P(None, both), P(both), P(both), P()),
        out_specs=(tokens, tokens, P(both, None), P(both, None), P(None, both), P(both), P(both), P()),
        check_vma=False,
    )
```

```python
import jax
import jax.numpy as jnp
from jax import lax
from jax.experimental import pallas as pl
from jax.experimental.pallas import tpu as pltpu
from jax.sharding import Mesh
from jax.sharding import PartitionSpec as P

HEADS = 48
HEADDIM = 64
STATE = 128
CONV = 4
INNER = 3072
XBC = 3328
HALF = INNER // 2
LANES = 128
SEGS = 4
LIGHT = pl.CostEstimate(flops=1024, bytes_accessed=1024, transcendentals=0)
VMEM_LIMIT = 48 * 1024 * 1024
LOG2E = 1.4426950408889634

epsilon = 1e-05
f32 = jnp.float32
bf16 = jnp.bfloat16


def own_columns(array, core):
    chips = lax.axis_size("chip")
    width = array.shape[-1] // (2 * chips)
    parted = array.reshape(array.shape[:-1] + (chips, 2, width))
    picked = lax.dynamic_index_in_dim(parted, core, axis=parted.ndim - 2, keepdims=False)
    return picked.reshape(array.shape[:-1] + (chips * width,))


def to_partner(array):
    return lax.ppermute(array, "core", [(0, 1), (1, 0)])


def in_core_order(mine, theirs, core, axis):
    first = jnp.where(core == 0, mine, theirs)
    second = jnp.where(core == 0, theirs, mine)
    return jnp.stack([first, second], axis=axis)


def chip_dims():
    return (lax.axis_size("chip") // 2, 2, lax.axis_size("seg"))


def chip_place():
    chip = lax.axis_index("chip")
    return (chip // 2, chip % 2, lax.axis_index("seg"))


def moved(array, dim, by):
    sizes = chip_dims()
    index = lambda at: (at[0] * sizes[1] + at[1]) * sizes[2] + at[2]
    pairs = []
    for a in range(sizes[0]):
        for b in range(sizes[1]):
            for z in range(sizes[2]):
                to = [a, b, z]
                to[dim] = (to[dim] + by) % sizes[dim]
                pairs.append((index((a, b, z)), index(to)))
    return lax.ppermute(array, ("chip", "seg"), pairs)


def tie(*values):
    return lax.optimization_barrier(values)


ORDERS = ((2, 0, 1), (2, 1, 0))


def column_parts(width):
    cut = -(-(width // 2) // LANES) * LANES
    return ((0, cut), (cut, width))


def gather_step(data, dim):
    return [data] + [moved(data, dim, by) for by in range(1, chip_dims()[dim])]


def gather_first(block):
    pieces = gather_step(block, 2)
    return [[piece[half] for piece in pieces] for half in range(2)]


def gather_next(parts, step):
    return [gather_step(jnp.stack(part), order[step]) for order, part in zip(ORDERS, parts)]


def placed_kernel(plan, outs, place_ref, *refs):
    sources, targets, sems = refs[: -outs - 1], refs[-outs - 1 : -1], refs[-1]
    copies = []
    for source, lead, at, half, paired, out in plan:
        spot = [lax.rem(place_ref[dim] + (size - back), size) for dim, (back, size) in enumerate(at)]
        target = targets[out].at[spot[0], spot[1]]
        target = target.at[half, spot[2]] if paired else target.at[spot[2], half]
        copies.append(pltpu.make_async_copy(sources[source].at[lead], target, sems.at[len(copies)]))
    for copy in copies:
        copy.start()
    for copy in copies:
        copy.wait()


def whole_matrices(jobs):
    sizes = chip_dims()
    plan, sources, shapes = [], [], []
    for out, (paired, halves) in enumerate(jobs):
        for half, (order, part) in enumerate(zip(ORDERS, halves)):
            for back_last, piece in enumerate(part):
                for back_mid in range(sizes[order[1]]):
                    for back_first in range(sizes[order[0]]):
                        at = [None] * 3
                        at[order[2]] = (back_last, sizes[order[2]])
                        at[order[1]] = (back_mid, sizes[order[1]])
                        at[order[0]] = (back_first, sizes[order[0]])
                        plan.append((len(sources), (back_mid, back_first), at, half, paired, out))
                sources.append(piece)
        block = halves[0][0].shape[-2:]
        shapes.append(sizes[:2] + ((2, sizes[2]) if paired else (sizes[2], 2)) + block)
    anywhere = pl.BlockSpec(memory_space=pl.ANY)
    return pl.pallas_call(
        lambda *refs: placed_kernel(plan, len(jobs), *refs),
        out_shape=[jax.ShapeDtypeStruct(shape, bf16) for shape in shapes],
        in_specs=[pl.BlockSpec(memory_space=pltpu.SMEM)] + [anywhere] * len(sources),
        out_specs=[pl.BlockSpec(memory_space=pltpu.VMEM)] * len(jobs),
        scratch_shapes=[pltpu.SemaphoreType.DMA((len(plan),))],
        compiler_params=pltpu.CompilerParams(vmem_limit_bytes=VMEM_LIMIT),
        cost_estimate=LIGHT,
    )(jnp.stack(chip_place()).astype(jnp.int32), *sources)


def total(terms):
    result = terms[0].astype(f32)
    for term in terms[1:]:
        result = result + term.astype(f32)
    return result


def reduce_send(terms, axis, dim, wire):
    place, size = chip_place()[dim], chip_dims()[dim]
    pick = lambda at: [lax.dynamic_index_in_dim(term, at, axis=axis, keepdims=False) for term in terms]
    received = [moved(total(pick((place + by) % size)).astype(wire), dim, by) for by in range(1, size)]
    return pick(place), received


def reduce_first(partials, wire=bf16):
    parts = []
    for half, (axis, dim) in enumerate(((1, 1), (0, 0))):
        place, size = chip_place()[dim], chip_dims()[dim]
        cuts = [(partial, *column_parts(partial.shape[-1])[half]) for partial in partials]
        pick = lambda at: jnp.concatenate(
            [
                lax.dynamic_index_in_dim(partial[..., begin:end], at, axis=axis, keepdims=False)
                for partial, begin, end in cuts
            ],
            axis=-1,
        )
        received = [moved(pick((place + by) % size).astype(wire), dim, by) for by in range(1, size)]
        parts.append(([pick(place)], received))
    return parts


def reduce_second(first, wire=bf16):
    return [
        reduce_send(first[0][0] + first[0][1], 0, 0, wire),
        reduce_send(first[1][0] + first[1][1], 0, 1, wire),
    ]


def reduce_third(second, wire=bf16):
    joined = jnp.concatenate([total(kept + received) for kept, received in second], axis=-1)
    return [reduce_send([joined], 0, 2, wire)]


def reduce_end(third):
    return total(third[0][0] + third[0][1])


def arrivals(parts):
    return [received for _, received in parts]


def arrived(parts, received):
    return [(kept, new) for (kept, _), new in zip(parts, received)]


def line_perm(turn, back):
    line = lax.axis_size("seg")
    parts = line // SEGS
    pairs = []
    for core in range(2):
        for place in range(line):
            piece = (place % SEGS) ^ turn
            half, index = divmod(piece, 2)
            source = core * line + place
            target = half * line + (2 * core + index) * parts + place // SEGS
            pairs.append((target, source) if back else (source, target))
    return pairs


def whole_sequence(array, core, place):
    parts = lax.axis_size("seg") // SEGS
    half = array.shape[1] // 2
    pieces = array.reshape(2, 2, half, -1).transpose(1, 0, 2, 3).reshape(4, half, -1)
    mine = place % SEGS
    target = 2 * core + (place // parts) % 2
    got = []
    for turn in range(4):
        piece = lax.dynamic_index_in_dim(pieces, mine ^ turn, axis=0, keepdims=False)
        got.append(lax.ppermute(piece, ("core", "seg"), line_perm(turn, False)))
    got = jnp.stack(got)
    return jnp.stack([lax.dynamic_index_in_dim(got, target ^ k, axis=0, keepdims=False) for k in range(4)])


def back_to_owner(ordered, core, place):
    parts = lax.axis_size("seg") // SEGS
    half = ordered.shape[1]
    mine = place % SEGS
    target = 2 * core + (place // parts) % 2
    got = []
    for turn in range(4):
        piece = lax.dynamic_index_in_dim(ordered, target ^ turn, axis=0, keepdims=False)
        got.append(lax.ppermute(piece, ("core", "seg"), line_perm(turn, True)))
    got = jnp.stack(got)
    pieces = jnp.stack([lax.dynamic_index_in_dim(got, mine ^ k, axis=0, keepdims=False) for k in range(4)])
    return pieces.reshape(2, 2, half, -1).transpose(1, 0, 2, 3).reshape(2, 2 * half, -1)


def part_pairs(step):
    line = lax.axis_size("seg")
    parts = line // SEGS
    return [(i, i + step) for i in range(line) if 0 <= i + step < line and i // parts == (i + step) // parts]


def entering(decay, state, step):
    parts = lax.axis_size("seg") // SEGS
    total = jnp.zeros_like(state)
    for _ in range(parts - 1):
        total = lax.ppermute(decay * total + state, "seg", part_pairs(step))
    return total


def borrowed(array, step):
    parts = lax.axis_size("seg") // SEGS
    if parts == 1:
        return jnp.zeros_like(array)
    return lax.ppermute(array, "seg", part_pairs(step))


def spilled(grad, edge, taps):
    if lax.axis_size("seg") == SEGS:
        return grad
    edge = borrowed(edge, -1)
    spill = jnp.stack(
        [
            sum(taps[k] * edge[CONV - 1 - k - early] for k in range(CONV - early))
            for early in range(CONV - 1, 0, -1)
        ]
    )
    at = grad.shape[0] - CONV + 1
    return grad.at[at:].set((grad[at:].astype(f32) + spill).astype(bf16))


def dot(a, b, contract):
    return lax.dot_general(a, b, (contract, ((), ())), preferred_element_type=f32)


def normed_kernel(slabs, core_ref, mine_ref, other_ref, gain_ref, normed_ref, turned_ref):
    mine, other = mine_ref[0], other_ref[0]
    first = core_ref[0] == 0
    hidden = jnp.concatenate([jnp.where(first, mine, other), jnp.where(first, other, mine)], axis=0).astype(f32)
    scale = lax.rsqrt(jnp.mean(hidden * hidden, axis=1, keepdims=True) + epsilon)
    normed = hidden * scale * gain_ref[...]
    normed_ref[...] = normed.astype(bf16)
    turned = normed.T.astype(bf16)
    for to, at, size in slabs:
        turned_ref[to : to + size] = turned[at : at + size]


def normed_tokens(core, mine, other, gain, rows):
    segs, half, width = mine.shape
    a, b, z = chip_dims()
    group = 2 * z * rows
    inside = rows % 16 == 0
    slabs = [(0, 0, width)]
    if inside:
        slabs = [
            (chip * group + (at * 2 + core_at) * rows, chip * group + (core_at * z + at) * rows, rows)
            for chip in range(a * b)
            for core_at in range(2)
            for at in range(z)
        ]
    normed, turned = pl.pallas_call(
        lambda *refs: normed_kernel(slabs, *refs),
        grid_spec=pltpu.PrefetchScalarGridSpec(
            num_scalar_prefetch=1,
            grid=(segs,),
            in_specs=[
                pl.BlockSpec((1, half, width), lambda i, core: (i, 0, 0)),
                pl.BlockSpec((1, half, width), lambda i, core: (i, 0, 0)),
                pl.BlockSpec((1, width), lambda i, core: (0, 0)),
            ],
            out_specs=(
                pl.BlockSpec((2 * half, width), lambda i, core: (i, 0)),
                pl.BlockSpec((width, 2 * half), lambda i, core: (0, i)),
            ),
        ),
        out_shape=(
            jax.ShapeDtypeStruct((segs * 2 * half, width), bf16),
            jax.ShapeDtypeStruct((width, segs * 2 * half), bf16),
        ),
        compiler_params=pltpu.CompilerParams(dimension_semantics=("arbitrary",), vmem_limit_bytes=VMEM_LIMIT),
        cost_estimate=LIGHT,
    )(core.reshape(1).astype(jnp.int32), mine, other, gain.reshape(1, width))
    if not inside:
        turned = turned.reshape(a, b, 2, z, rows, -1).transpose(0, 1, 3, 2, 4, 5).reshape(turned.shape)
    return normed, turned


def mixed_kernel(gated_ref, scale_ref, gain_ref, mixed_ref, turned_ref):
    mixed = gated_ref[...] * scale_ref[...] * gain_ref[...]
    mixed_ref[...] = mixed.astype(bf16)
    turned_ref[...] = mixed.T.astype(bf16)


def mixed_tokens(gated, scale, gain, seg_len):
    length, width = gated.shape
    return pl.pallas_call(
        mixed_kernel,
        grid=(length // seg_len,),
        in_specs=[
            pl.BlockSpec((seg_len, width), lambda i: (i, 0)),
            pl.BlockSpec((seg_len, 1), lambda i: (i, 0)),
            pl.BlockSpec((1, width), lambda i: (0, 0)),
        ],
        out_specs=(
            pl.BlockSpec((seg_len, width), lambda i: (i, 0)),
            pl.BlockSpec((width, seg_len), lambda i: (0, i)),
        ),
        out_shape=(
            jax.ShapeDtypeStruct((length, width), bf16),
            jax.ShapeDtypeStruct((width, length), bf16),
        ),
        compiler_params=pltpu.CompilerParams(dimension_semantics=("arbitrary",), vmem_limit_bytes=VMEM_LIMIT),
        cost_estimate=LIGHT,
    )(gated, scale, gain.reshape(1, width))


def columns_of(pair):
    return pl.ds(pair * LANES, LANES)


def low_half(shape):
    return lax.broadcasted_iota(jnp.int32, shape, len(shape) - 1) < HEADDIM


def pair_columns(array, pair, low):
    rows = array.shape[0]
    first = jnp.broadcast_to(array[:, 2 * pair : 2 * pair + 1], (rows, LANES))
    second = jnp.broadcast_to(array[:, 2 * pair + 1 : 2 * pair + 2], (rows, LANES))
    return jnp.where(low, first, second)


def conv_parts(current, before, taps):
    rows = current.shape[0]
    padded = jnp.concatenate([before, current], axis=0)
    seen = [padded[8 - CONV + 1 + k : 8 - CONV + 1 + k + rows] for k in range(CONV - 1)] + [current]
    total = taps[CONV : CONV + 1]
    for k in range(CONV):
        total = total + taps[k : k + 1] * seen[k]
    return total, seen


def step_terms(raw, head, seg_len):
    shifted = raw + head[1:2]
    step = jnp.maximum(shifted, 0.0) + jnp.log1p(jnp.exp(-jnp.abs(shifted)))
    log_decay = step * head[0:1]
    at_or_before = lax.broadcasted_iota(jnp.int32, (seg_len, seg_len), 0) >= lax.broadcasted_iota(
        jnp.int32, (seg_len, seg_len), 1
    )
    sums = lax.dot_general(
        jnp.where(at_or_before, 1.0, 0.0), log_decay, (((1,), (0,)), ((), ())),
        precision=lax.Precision.HIGHEST, preferred_element_type=f32,
    )
    return shifted, step, log_decay, sums * LOG2E


def forward_kernel(
    proj_ref, taps_ref, head_ref, skip_ref, rim_ref, init_ref,
    values_ref, prior_ref, final_ref, last_ref, state_ref, tail_ref,
):
    seg_len = proj_ref.shape[0]
    half = seg_len // 2

    @pl.when(pl.program_id(0) == 0)
    def _():
        state_ref[...] = init_ref[...]
        tail_ref[...] = rim_ref[...]

    def activated(begin):
        at = pl.ds(begin, LANES)
        total, _ = conv_parts(proj_ref[:, at], tail_ref[:, at], taps_ref[:, at])
        return total * jax.nn.sigmoid(total)

    b_low = activated(HALF).astype(bf16)
    b_turned = activated(HALF).T.astype(bf16)
    c_low = activated(HALF + STATE).astype(bf16)
    _, step, _, sums = step_terms(proj_ref[:, HALF + 2 * STATE :], head_ref, seg_len)
    sums_turned, step_turned = sums.T, step.T
    scores = dot(c_low, b_low, ((1,), (1,)))
    kept = lax.broadcasted_iota(jnp.int32, (half, half), 0) >= lax.broadcasted_iota(jnp.int32, (half, half), 1)
    first_scores = jnp.where(kept, scores[:half, :half], 0.0)
    later_scores = scores[half:, :half]
    second_scores = jnp.where(kept, scores[half:, half:], 0.0)
    low = low_half((seg_len, LANES))
    last_ref[...] = jnp.broadcast_to(sums[seg_len - 1 :], last_ref.shape)

    for pair in range(HEADS // 4):
        at = columns_of(pair)
        x_values = activated(pair * LANES)
        x_low = x_values.astype(bf16)
        sums_pair = pair_columns(sums, pair, low)
        last_pair = sums_pair[seg_len - 1 :]
        carry = jnp.exp2(last_pair - sums_pair) * pair_columns(step, pair, low)
        scaled_x = (carry * x_low.astype(f32)).astype(bf16)
        prior = state_ref[:, at]
        prior_low = prior.astype(bf16)
        prior_ref[0, :, at] = prior_low
        from_state = jnp.exp2(sums_pair) * dot(c_low, prior_low, ((1,), (0,)))
        state_ref[:, at] = jnp.exp2(last_pair) * prior + dot(b_turned, scaled_x, ((1,), (0,)))
        early, late = 0.0, 0.0
        for side in range(2):
            head = 2 * pair + side
            x_side = jnp.where(low if side == 0 else ~low, x_values, 0.0).astype(bf16)
            at_token = jnp.broadcast_to(sums[:, head : head + 1], (seg_len, half))
            at_source, source_step = sums_turned[head : head + 1], step_turned[head : head + 1]
            first = jnp.exp2(jnp.minimum(at_token[:half] - at_source[:, :half], 0.0)) * first_scores
            first = (first * source_step[:, :half]).astype(bf16)
            later = jnp.exp2(at_token[half:] - at_source[:, :half]) * later_scores
            later = (later * source_step[:, :half]).astype(bf16)
            second = jnp.exp2(jnp.minimum(at_token[half:] - at_source[:, half:], 0.0)) * second_scores
            second = (second * source_step[:, half:]).astype(bf16)
            early = early + dot(first, x_side[:half], ((1,), (0,)))
            late = late + dot(jnp.concatenate([later, second], axis=1), x_side, ((1,), (0,)))
        intra = jnp.concatenate([early, late], axis=0)
        values_ref[:, at] = intra + from_state + skip_ref[:, at] * x_values

    tail_ref[...] = proj_ref[seg_len - 8 :, : HALF + 2 * STATE]
    final_ref[...] = state_ref[...]


def full_block(shape):
    return pl.BlockSpec(shape, lambda *_: (0,) * len(shape))


def scan_forward(proj, taps, head, skip, rim, init, seg_len):
    segs = proj.shape[0] // seg_len
    wide = HALF + 2 * STATE
    return pl.pallas_call(
        forward_kernel,
        grid=(segs,),
        out_shape=(
            jax.ShapeDtypeStruct((proj.shape[0], HALF), f32),
            jax.ShapeDtypeStruct((segs, STATE, HALF), bf16),
            jax.ShapeDtypeStruct((STATE, HALF), f32),
            jax.ShapeDtypeStruct((segs * 8, LANES), f32),
        ),
        in_specs=[
            pl.BlockSpec((seg_len, proj.shape[1]), lambda i: (i, 0)),
            full_block((8, wide)),
            full_block((8, LANES)),
            full_block((1, HALF)),
            full_block((8, wide)),
            full_block((STATE, HALF)),
        ],
        out_specs=(
            pl.BlockSpec((seg_len, HALF), lambda i: (i, 0)),
            pl.BlockSpec((1, STATE, HALF), lambda i: (i, 0, 0)),
            full_block((STATE, HALF)),
            pl.BlockSpec((8, LANES), lambda i: (i, 0)),
        ),
        scratch_shapes=[pltpu.VMEM((STATE, HALF), f32), pltpu.VMEM((8, wide), f32)],
        compiler_params=pltpu.CompilerParams(
            dimension_semantics=("arbitrary",), vmem_limit_bytes=VMEM_LIMIT
        ),
        cost_estimate=LIGHT,
    )(proj, taps, head, skip, rim, init)


def split_dot(array, other):
    high = array.astype(bf16)
    rest = (array - high.astype(f32)).astype(bf16)
    return dot(high, other, ((1,), (0,))) + dot(rest, other, ((1,), (0,)))


def backward_kernel(
    group, proj_ref, before_ref, taps_ref, rim_ref, shared_ref, shared_before_ref, shared_taps_ref, shared_rim_ref,
    head_ref, skip_ref, end_ref, prior_ref, values_ref, grad_ref, core_ref,
    grad_x_ref, mine_ref, theirs_ref, grad_raw_ref, taps_grad_ref, skip_grad_ref, head_grad_ref, edge_ref, start_ref,
    later_ref, local_ref, scaled_ref, grad_state_ref, inner_ref, source_ref, carry_ref, decay_ref,
):
    seg_len = proj_ref.shape[0]
    half = seg_len // 2
    turn = pl.program_id(0)

    @pl.when(turn == 0)
    def _():
        later_ref[...] = end_ref[...]
        edge_ref[...] = jnp.zeros_like(edge_ref)
        taps_grad_ref[...] = jnp.zeros_like(taps_grad_ref)
        skip_grad_ref[...] = jnp.zeros_like(skip_grad_ref)
        head_grad_ref[...] = jnp.zeros_like(head_grad_ref)

    first_segment = turn == pl.num_programs(0) - 1

    def conv_at(at, current, ahead, taps, rim):
        before = jnp.where(first_segment, rim[:, at], ahead[:, at])
        return conv_parts(current[:, at], before, taps[:, at])

    def activated(begin):
        total, _ = conv_at(pl.ds(begin, LANES), shared_ref, shared_before_ref, shared_taps_ref, shared_rim_ref)
        return total * jax.nn.sigmoid(total)

    b_values = activated(0)
    c_values = activated(STATE)
    b_low, c_low, c_turned = b_values.astype(bf16), c_values.astype(bf16), c_values.T.astype(bf16)
    shifted, step, log_decay, sums = step_terms(shared_ref[:, 2 * STATE :], head_ref, seg_len)
    sums_turned = sums.T
    scores = dot(b_low, c_low, ((1,), (1,)))
    kept = lax.broadcasted_iota(jnp.int32, (half, half), 0) <= lax.broadcasted_iota(jnp.int32, (half, half), 1)
    first_scores = jnp.where(kept, scores[:half, :half], 0.0)
    later_scores = scores[:half, half:]
    second_scores = jnp.where(kept, scores[half:, half:], 0.0)
    low = low_half((seg_len, LANES))
    first_grad, later_grad, second_grad = 0.0, 0.0, 0.0

    pairs = grad_ref.shape[1] // LANES
    for pair in range(pairs):
        at = columns_of(pair)
        total, seen = conv_at(at, proj_ref, before_ref, taps_ref, rim_ref)
        sigmoid = jax.nn.sigmoid(total)
        x_values = total * sigmoid
        x_low = x_values.astype(bf16)
        x_wide = x_low.astype(f32)
        sums_pair = pair_columns(sums, group * pairs + pair, low)
        step_pair = pair_columns(step, group * pairs + pair, low)
        last_pair = sums_pair[seg_len - 1 :]
        gap = jnp.exp2(last_pair - sums_pair)
        scaled_ref[:, at] = (gap * step_pair * x_wide).astype(bf16)
        grad_values = grad_ref[:, at]
        grad_state_ref[:, at] = (grad_values * jnp.exp2(sums_pair)).astype(bf16)
        later = later_ref[:, at]
        later_low = later.astype(bf16)
        local_ref[:, at] = later_low
        prior = prior_ref[0, :, at]
        decay_ref[:, at] = jnp.broadcast_to(
            jnp.sum(later * prior.astype(f32), axis=0, keepdims=True), (8, LANES)
        )
        grad_prior = dot(c_turned, grad_state_ref[:, at], ((1,), (0,)))
        later_ref[:, at] = jnp.exp2(last_pair) * later + grad_prior
        grad_scaled = dot(b_low, later_low, ((1,), (0,)))
        stepped = (step_pair * x_wide).astype(bf16)
        early, late = 0.0, 0.0
        for side in range(2):
            head = 2 * (group * pairs + pair) + side
            grad_low = jnp.where(low if side == 0 else ~low, grad_values, 0.0).astype(bf16)
            at_source = jnp.broadcast_to(sums[:, head : head + 1], (seg_len, half))
            at_token = sums_turned[head : head + 1]
            grad_weights = dot(stepped, grad_low, ((1,), (1,)))
            first = jnp.exp2(jnp.minimum(at_token[:, :half] - at_source[:half], 0.0))
            after = jnp.exp2(at_token[:, half:] - at_source[:half])
            second = jnp.exp2(jnp.minimum(at_token[:, half:] - at_source[half:], 0.0))
            first_grad = first_grad + first * grad_weights[:half, :half]
            later_grad = later_grad + after * grad_weights[:half, half:]
            second_grad = second_grad + second * grad_weights[half:, half:]
            upper = jnp.concatenate([first * first_scores, after * later_scores], axis=1).astype(bf16)
            early = early + dot(upper, grad_low, ((1,), (0,)))
            late = late + dot((second * second_scores).astype(bf16), grad_low[half:], ((1,), (0,)))
        inner = jnp.concatenate([early, late], axis=0)
        skip = skip_ref[:, at]
        skip_grad_ref[:, at] += jnp.sum(grad_values * x_values, axis=0, keepdims=True)
        inner_ref[:, at] = grad_values * (values_ref[:, at] - skip * x_values)
        source_ref[:, at] = x_wide * inner
        carry_ref[:, at] = x_wide * grad_scaled
        grad_x = skip * grad_values + step_pair * (inner + gap * grad_scaled)
        grad_total = grad_x * (sigmoid * (1.0 + total * (1.0 - sigmoid)))
        for k in range(CONV):
            taps_grad_ref[k : k + 1, at] += jnp.sum(grad_total * seen[k], axis=0, keepdims=True)
        taps_grad_ref[CONV : CONV + 1, at] += jnp.sum(grad_total, axis=0, keepdims=True)
        extended = jnp.concatenate([grad_total, edge_ref[:, at]], axis=0)
        edge_ref[:, at] = grad_total[:8]
        taps = taps_ref[:, at]
        grad_conv = taps[CONV - 1 : CONV] * grad_total
        for k in range(CONV - 1):
            grad_conv = grad_conv + taps[k : k + 1] * extended[CONV - 1 - k : CONV - 1 - k + seg_len]
        grad_x_ref[:, at] = grad_conv.astype(bf16)

    width = grad_ref.shape[1]
    channel = lax.broadcasted_iota(jnp.int32, (width, LANES), 0) // HEADDIM + group * width // HEADDIM
    heads = jnp.where(channel == lax.broadcasted_iota(jnp.int32, (width, LANES), 1), 1.0, 0.0).astype(bf16)
    tail = jnp.exp2(sums[seg_len - 1 :] - sums)
    source_grad = split_dot(source_ref[...], heads)
    step_grad = source_grad + tail * split_dot(carry_ref[...], heads)
    used = step * step_grad
    sum_grad = split_dot(inner_ref[...], heads) - used
    at_last = jnp.sum(used - step * source_grad, axis=0, keepdims=True)
    at_last = at_last + split_dot(decay_ref[...], heads)[:1] * jnp.exp2(sums[seg_len - 1 :])
    is_last = lax.broadcasted_iota(jnp.int32, (seg_len, LANES), 0) == seg_len - 1
    sum_grad = sum_grad + jnp.where(is_last, at_last, 0.0)
    at_or_after = lax.broadcasted_iota(jnp.int32, (seg_len, seg_len), 0) <= lax.broadcasted_iota(
        jnp.int32, (seg_len, seg_len), 1
    )
    log_grad = lax.dot_general(
        jnp.where(at_or_after, 1.0, 0.0), sum_grad, (((1,), (0,)), ((), ())),
        precision=lax.Precision.HIGHEST, preferred_element_type=f32,
    )
    grad_raw = (step_grad + head_ref[0:1] * log_grad) * jax.nn.sigmoid(shifted)
    grad_raw_ref[...] = grad_raw
    head_grad_ref[CONV + 1 : CONV + 2] += jnp.sum(log_grad * log_decay, axis=0, keepdims=True)
    head_grad_ref[CONV + 2 : CONV + 3] += jnp.sum(grad_raw, axis=0, keepdims=True)

    first_low = jnp.where(kept, first_grad, 0.0)
    second_low = jnp.where(kept, second_grad, 0.0)
    grad_scores = jnp.concatenate(
        [
            jnp.concatenate([first_low, later_grad], axis=1),
            jnp.concatenate([jnp.zeros_like(first_low), second_low], axis=1),
        ],
        axis=0,
    )
    start_ref[...] = later_ref[...]
    grad_b = dot(scaled_ref[...], local_ref[...], ((1,), (1,))) + dot(
        grad_scores.astype(bf16), c_low, ((1,), (0,))
    )
    grad_c = dot(grad_state_ref[...], prior_ref[0], ((1,), (1,))) + dot(
        grad_scores.T.astype(bf16), b_low, ((1,), (0,))
    )
    first = core_ref[0] == 0
    mine_ref[...] = jnp.where(first, grad_b, grad_c)
    theirs_ref[...] = jnp.where(first, grad_c, grad_b)


GROUPS = 1


def scan_backward(group, core, proj, taps, head, skip, rim, end, prior, values, grad_values, seg_len):
    length = proj.shape[0]
    segs = length // seg_len
    width, shared = HALF // GROUPS, proj.shape[1] - HALF
    back = lambda width, at=0: pl.BlockSpec((seg_len, width), lambda i: (segs - 1 - i, at))
    row_ahead = lambda i: jnp.maximum((segs - 1 - i) * (seg_len // 8) - 1, 0)
    ahead = lambda width, at: pl.BlockSpec((8, width), lambda i: (row_ahead(i), at))
    column = lambda rows, width, at: pl.BlockSpec((rows, width), lambda i: (0, at))
    both = HALF // shared
    return pl.pallas_call(
        lambda *refs: backward_kernel(group, *refs),
        grid=(segs,),
        out_shape=(
            jax.ShapeDtypeStruct((length, width), bf16),
            jax.ShapeDtypeStruct((length, STATE), f32),
            jax.ShapeDtypeStruct((length, STATE), f32),
            jax.ShapeDtypeStruct((length, LANES), f32),
            jax.ShapeDtypeStruct((8, width), f32),
            jax.ShapeDtypeStruct((1, width), f32),
            jax.ShapeDtypeStruct((8, LANES), f32),
            jax.ShapeDtypeStruct((8, width), f32),
            jax.ShapeDtypeStruct((STATE, width), f32),
        ),
        in_specs=[
            back(width, group),
            ahead(width, group),
            column(8, width, group),
            column(8, width, group),
            back(shared, both),
            ahead(shared, both),
            column(8, shared, both),
            column(8, shared, both),
            full_block((8, LANES)),
            column(1, width, group),
            column(STATE, width, group),
            pl.BlockSpec((1, STATE, width), lambda i: (segs - 1 - i, 0, group)),
            back(width, group),
            back(width, group),
            pl.BlockSpec(memory_space=pltpu.SMEM),
        ],
        out_specs=(
            back(width),
            back(STATE),
            back(STATE),
            back(LANES),
            full_block((8, width)),
            full_block((1, width)),
            full_block((8, LANES)),
            full_block((8, width)),
            full_block((STATE, width)),
        ),
        scratch_shapes=[
            pltpu.VMEM((STATE, width), f32),
            pltpu.VMEM((STATE, width), bf16),
            pltpu.VMEM((seg_len, width), bf16),
            pltpu.VMEM((seg_len, width), bf16),
            pltpu.VMEM((seg_len, width), f32),
            pltpu.VMEM((seg_len, width), f32),
            pltpu.VMEM((seg_len, width), f32),
            pltpu.VMEM((8, width), f32),
        ],
        compiler_params=pltpu.CompilerParams(
            dimension_semantics=("arbitrary",), vmem_limit_bytes=VMEM_LIMIT
        ),
        cost_estimate=LIGHT,
    )(
        proj, proj, taps, rim, proj, proj, taps, rim, head, skip, end, prior, values, grad_values,
        core.reshape(1).astype(jnp.int32),
    )


def half_kernel(transposed, count, core_ref, *refs):
    inputs, mine_ref, theirs_ref = refs[: 2 * count], refs[-2], refs[-1]
    total = refs[2 * count][...] if len(refs) > 2 * count + 2 else 0.0
    for left, right in zip(inputs[:count], inputs[count:]):
        total = total + dot(left[...], right[...], ((1,), (1 if transposed else 0,)))
    half = total.shape[0] // 2
    first = core_ref[0] == 0
    mine_ref[0] = jnp.where(first, total[:half], total[half:])
    theirs_ref[0] = jnp.where(first, total[half:], total[:half]).astype(bf16)


def half_products(core, terms, seg_len, width, transposed, base=()):
    length = terms[0][0].shape[0]
    left = [pl.BlockSpec((seg_len, array.shape[1]), lambda i, core: (i, 0)) for array, _, _ in terms]
    right = []
    for array, matrix, at in terms:
        if transposed:
            right.append(pl.BlockSpec((width, array.shape[1]), lambda i, core, at=at: (0, at(core[0]))))
        else:
            right.append(pl.BlockSpec(matrix.shape, lambda i, core: (0, 0)))
    depth = sum(array.shape[1] for array, _, _ in terms)
    mine, theirs = pl.pallas_call(
        lambda *refs: half_kernel(transposed, len(terms), *refs),
        grid_spec=pltpu.PrefetchScalarGridSpec(
            num_scalar_prefetch=1,
            grid=(length // seg_len,),
            in_specs=left + right + [pl.BlockSpec((seg_len, width), lambda i, core: (i, 0)) for _ in base],
            out_specs=[pl.BlockSpec((1, seg_len // 2, width), lambda i, core: (i, 0, 0))] * 2,
        ),
        out_shape=(
            jax.ShapeDtypeStruct((length // seg_len, seg_len // 2, width), f32),
            jax.ShapeDtypeStruct((length // seg_len, seg_len // 2, width), bf16),
        ),
        compiler_params=pltpu.CompilerParams(dimension_semantics=("arbitrary",), vmem_limit_bytes=VMEM_LIMIT),
        cost_estimate=LIGHT,
    )(core.reshape(1).astype(jnp.int32), *[array for array, _, _ in terms], *[matrix for _, matrix, _ in terms], *base)
    return mine, theirs


def shared_kernel(core_ref, proj_ref, rim_ref, taps_ref, mine_ref, other_ref, grad_ref, taps_grad_ref, edge_ref):
    total, seen = conv_parts(proj_ref[...], rim_ref[...], taps_ref[...])
    sigmoid = jax.nn.sigmoid(total)
    grad_total = mine_ref[...] + other_ref[...]
    grad_total = grad_total * (sigmoid * (1.0 + total * (1.0 - sigmoid)))
    sums = [jnp.sum(grad_total * part, axis=0, keepdims=True) for part in seen]
    sums = sums + [jnp.sum(grad_total, axis=0, keepdims=True), jnp.zeros((8 - CONV - 1, LANES), f32)]
    taps_grad_ref[...] = jnp.concatenate(sums, axis=0)
    edge_ref[...] = grad_total[:8]
    taps = taps_ref[...]
    extended = jnp.concatenate([grad_total, jnp.zeros((8, LANES), f32)], axis=0)
    grad_conv = taps[CONV - 1 : CONV] * grad_total
    for k in range(CONV - 1):
        grad_conv = grad_conv + taps[k : k + 1] * extended[CONV - 1 - k : CONV - 1 - k + grad_total.shape[0]]
    grad_ref[...] = grad_conv.astype(bf16)


def shared_backward(core, proj, rim, taps, mine, other):
    length = proj.shape[0]
    picked = lambda rows: pl.BlockSpec((rows, LANES), lambda i, core: (0, HALF // LANES + core[0]))
    whole = lambda rows: pl.BlockSpec((rows, LANES), lambda i, core: (0, 0))
    return pl.pallas_call(
        shared_kernel,
        grid_spec=pltpu.PrefetchScalarGridSpec(
            num_scalar_prefetch=1,
            grid=(1,),
            in_specs=[picked(length), picked(8), picked(8), whole(length), whole(length)],
            out_specs=(whole(length), whole(8), whole(8)),
        ),
        out_shape=(
            jax.ShapeDtypeStruct((length, LANES), bf16),
            jax.ShapeDtypeStruct((8, LANES), f32),
            jax.ShapeDtypeStruct((8, LANES), f32),
        ),
        compiler_params=pltpu.CompilerParams(vmem_limit_bytes=VMEM_LIMIT),
        cost_estimate=LIGHT,
    )(core.reshape(1).astype(jnp.int32), proj, rim, taps, mine, other)


def per_device(hidden_in, cotangent, in_proj, out_proj, conv_params, pre_gain, gated_gain, head_params):
    chips, line = lax.axis_size("chip"), lax.axis_size("seg")
    core, place = lax.axis_index("core"), lax.axis_index("seg")
    rows, model_width = in_proj.shape[0], hidden_in.shape[2]
    heads = HEADS // 2

    conv_width, gain_width = conv_params.shape[1], gated_gain.shape[0]
    used = HALF + 2 * STATE + heads
    spare = -used % LANES
    small = jnp.zeros((rows, spare), bf16)
    small = small.at[: CONV + 1, :conv_width].set(conv_params)
    small = small.at[CONV + 1, :rows].set(pre_gain)
    small = small.at[CONV + 2, :gain_width].set(gated_gain)

    def conv_side(which):
        return jnp.concatenate(
            [
                own_columns(in_proj[:, INNER : 2 * INNER], which),
                in_proj[:, 2 * INNER : INNER + XBC],
                own_columns(in_proj[:, INNER + XBC :], which),
                small,
            ],
            axis=1,
        )

    def gate_side(which):
        return own_columns(in_proj[:, :INNER], which)

    conv_swap = to_partner(conv_side(1 - core))
    conv_block = in_core_order(conv_side(core), conv_swap, core, 0)
    conv_z = gather_first(conv_block)
    gate_swap = to_partner(gate_side(1 - core))
    gate_block = in_core_order(gate_side(core), gate_swap, core, 0)
    conv_z, gate_block = tie(conv_z, gate_block)
    conv_2 = gather_next(conv_z, 1)
    gate_z = gather_first(gate_block)
    conv_2, gate_z, hidden_in = tie(conv_2, gate_z, hidden_in)
    conv_last = gather_next(conv_2, 2)
    hidden_half = whole_sequence(hidden_in, core, place)
    conv_last, hidden_half, gate_z = tie(conv_last, hidden_half, gate_z)
    hidden_other = to_partner(hidden_half)
    gate_2 = gather_next(gate_z, 1)
    conv_all = whole_matrices([(True, conv_last)])[0].reshape(model_width, -1)

    small_all = conv_all.reshape(chips, 2, line, rows, -1)[..., used:].astype(f32)
    taps_full = small_all[..., : CONV + 1, :conv_width].transpose(3, 0, 1, 2, 4).reshape(CONV + 1, XBC)
    taps = jnp.concatenate([own_columns(taps_full[:, :INNER], core), taps_full[:, INNER:]], axis=1)
    gain_pre = small_all[..., CONV + 1, :rows].reshape(model_width)
    gain_gate = lax.dynamic_index_in_dim(
        small_all[..., CONV + 2, :gain_width], core, axis=1, keepdims=False
    ).reshape(HALF)
    params = own_columns(head_params, core)

    seg_len = 2 * hidden_half.shape[1]
    tokens = SEGS * seg_len
    normed, normed_turned = normed_tokens(core, hidden_half, hidden_other, gain_pre, rows)
    projected = dot(normed, conv_all, ((1,), (0,)))
    projected, gate_2, out_proj = tie(projected, gate_2, out_proj)
    gate_last = gather_next(gate_2, 2)
    out_z = gather_first(out_proj.reshape(2, -1, model_width))

    taps = jnp.pad(taps, ((0, 8 - CONV - 1), (0, projected.shape[1] - taps.shape[1])))
    head = jnp.pad(jnp.stack([-jnp.exp(params[0]), params[1]]), ((0, 6), (0, LANES - heads)))
    skip = jnp.repeat(params[2], HEADDIM).reshape(1, HALF)
    wide = HALF + 2 * STATE
    rim = borrowed(projected[tokens - 8 :], 1)
    nothing = jnp.zeros((STATE, HALF), f32)
    values, prior, final, last = scan_forward(projected, taps, head, skip, rim, nothing, seg_len)
    if line > SEGS:
        last = jnp.sum(last.reshape(SEGS, 8, LANES)[:, 0, :heads], axis=0)
        decay = jnp.repeat(jnp.exp2(last), HEADDIM)
        begin = entering(decay, final, 1)
        values, prior, _, _ = scan_forward(projected, taps, head, skip, rim, begin, seg_len)

    values, gate_last, out_z, cotangent = tie(values, gate_last, out_z, cotangent)
    out_2 = gather_next(out_z, 1)
    cot_half = whole_sequence(cotangent, core, place)
    gate_matrix = whole_matrices([(True, gate_last)])[0].reshape(model_width, HALF)
    gate_matrix, out_2 = tie(gate_matrix, out_2)
    out_last = gather_next(out_2, 2)
    gate_input = dot(normed, gate_matrix, ((1,), (0,)))
    gate_input, cot_half = tie(gate_input, cot_half)
    cot_other = to_partner(cot_half)

    silu_gate = jax.nn.silu(gate_input)
    gated = values * silu_gate
    squares = jnp.sum(gated * gated, axis=1)
    squares_other = to_partner(squares)
    scale = lax.rsqrt((squares + squares_other) / INNER + epsilon)[:, None]
    cot = in_core_order(cot_half, cot_other, core, 1)
    upstream = cot.reshape(tokens, model_width)
    mixed, mixed_turned = mixed_tokens(gated, scale, gain_gate, seg_len)
    by_owner = lambda grad: grad.astype(bf16).reshape(chip_dims() + (-1, grad.shape[1]))
    out_grad = by_owner(dot(mixed_turned, upstream, ((1,), (0,))))
    out_grad, out_last = tie(out_grad, out_last)
    out_first = reduce_first([out_grad])
    out_matrix = whole_matrices([(False, out_last)])[0].reshape(HALF, model_width)
    branch, branch_sent = half_products(core, [(mixed, out_matrix, None)], seg_len, model_width, False)
    branch_sent, upstream = tie(branch_sent, upstream)
    branch_other = to_partner(branch_sent)
    grad_mixed = dot(upstream, out_matrix, ((1,), (1,)))
    grad_mixed, out_got = tie(grad_mixed, arrivals(out_first))
    out_second = reduce_second(arrived(out_first, out_got))
    unit = gated * scale
    gain_grad = grad_mixed * gain_gate
    along = jnp.sum(gain_grad * unit, axis=1)
    along_other = to_partner(along)
    along_other, branch_other = tie(along_other, branch_other)
    hidden_out = back_to_owner(
        (hidden_half.astype(f32) + branch + branch_other.astype(f32)).astype(bf16), core, place
    )
    along = ((along + along_other) / INNER)[:, None]
    gate_gain_grad = jnp.sum(grad_mixed * unit, axis=0)
    grad_gated = scale * (gain_grad - unit * along)
    grad_values = grad_gated * silu_gate
    sigmoid = jax.nn.sigmoid(gate_input)
    grad_gate = (grad_gated * values * (sigmoid * (1.0 + gate_input * (1.0 - sigmoid)))).astype(bf16)
    gate_grad = by_owner(dot(normed_turned, grad_gate, ((1,), (0,))))
    gate_grad, grad_values, out_got, hidden_out = tie(gate_grad, grad_values, arrivals(out_second), hidden_out)
    out_third = reduce_third(arrived(out_second, out_got))
    gate_first = reduce_first([gate_grad])
    scan = lambda later: scan_backward(
        0, core, projected, taps, head, skip, rim, later, prior, values, grad_values, seg_len
    )
    if line > SEGS:
        nothing = entering(decay, scan(nothing)[-1], -1)
    back = scan(nothing)
    back, gate_got, out_got, grad_gate = tie(back, arrivals(gate_first), arrivals(out_third), grad_gate)
    out_third = arrived(out_third, out_got)
    grad_x, mine, theirs, grad_raw, x_taps_grad, skip_grad, head_sums, x_edge, _ = back
    grad_x = spilled(grad_x, x_edge, taps[:, :HALF])
    other = to_partner(theirs)
    x_grad = by_owner(dot(normed_turned, grad_x, ((1,), (0,))))
    gate_second = reduce_second(arrived(gate_first, gate_got))
    other, x_grad = tie(other, x_grad)
    grad_state, state_taps_grad, state_edge = shared_backward(core, projected, rim, taps, mine, other)
    grad_state = spilled(grad_state, state_edge, lax.dynamic_slice_in_dim(taps, HALF + core * STATE, STATE, axis=1))
    grad_raw = grad_raw.astype(bf16)
    rest_grad = by_owner(dot(normed_turned, jnp.concatenate([grad_state, grad_raw], axis=1), ((1,), (0,))))
    rest_grad, x_grad, grad_gate, grad_state = tie(rest_grad, x_grad, grad_gate, grad_state)
    conv_first = reduce_first([x_grad, rest_grad])
    base = dot(grad_gate, gate_matrix, ((1,), (1,)))
    base, gate_got = tie(base, arrivals(gate_second))
    gate_third = reduce_third(arrived(gate_second, gate_got))
    terms = [
        (grad_x, conv_all, lambda core: 0),
        (grad_state, conv_all, lambda core: HALF // LANES + core),
        (grad_raw, conv_all, lambda core: (HALF + 2 * STATE) // LANES),
    ]
    grad_normed, sent_normed = half_products(core, terms, seg_len, model_width, True, (base,))
    other_normed, gate_got = tie(to_partner(sent_normed), arrivals(gate_third))
    gate_third = arrived(gate_third, gate_got)
    wide_hidden = hidden_half.astype(f32)
    hidden_scale = lax.rsqrt(jnp.mean(wide_hidden * wide_hidden, axis=-1, keepdims=True) + epsilon)
    grad_normed = (grad_normed + other_normed.astype(f32)) * gain_pre
    hidden_unit = wide_hidden * hidden_scale
    along = jnp.mean(grad_normed * hidden_unit, axis=-1, keepdims=True)
    grad_hidden = hidden_scale * (grad_normed - hidden_unit * along)
    grad_in = (cot_half.astype(f32) + grad_hidden).astype(bf16)
    row = lax.broadcasted_iota(jnp.int32, (8, 1), 0)
    small = x_taps_grad + jnp.where(row == CONV + 1, gate_gain_grad, 0.0) + jnp.where(row == CONV + 2, skip_grad, 0.0)
    small = jnp.concatenate([small, state_taps_grad + head_sums], axis=1)
    grad_in, conv_got, small = tie(grad_in, arrivals(conv_first), small)
    conv_second = reduce_second(arrived(conv_first, conv_got))
    grad_in = back_to_owner(grad_in, core, place)
    for dim in (1, 0):
        small = small + sum(moved(small, dim, by) for by in range(1, chip_dims()[dim]))
    conv_got, small = tie(arrivals(conv_second), small)
    conv_third = reduce_third(arrived(conv_second, conv_got))
    small = small + sum(moved(small, 2, by) for by in range(1, line))
    small_other = to_partner(small)
    grad_in, conv_got, small_other = tie(grad_in, arrivals(conv_third), small_other)
    conv_third = arrived(conv_third, conv_got)
    out_share = reduce_end(out_third).reshape(-1, model_width)
    paired = lambda third: reduce_end(third).astype(bf16).reshape(2, rows, -1)
    gate_share, conv_share = paired(gate_third), paired(conv_third)

    def mine_and_partner(share):
        keep = lax.dynamic_index_in_dim(share, core, axis=0, keepdims=False)
        give = lax.dynamic_index_in_dim(share, 1 - core, axis=0, keepdims=False)
        return keep, to_partner(give)

    both = in_core_order(small, small_other, core, 0)
    natural = lambda array, width: array.reshape(2, -1, chips, width).transpose(1, 2, 0, 3).reshape(-1, 2 * chips * width)
    device = (lax.axis_index("chip") * 2 + core) * line + place
    columns = natural(both[:, :, :HALF], HALF // chips)
    taps_all = jnp.concatenate([columns, both[0, :, HALF:], both[1, :, HALF:]], axis=1)[: CONV + 1]
    taps_share = lax.dynamic_slice_in_dim(taps_all, device * conv_width, conv_width, axis=1)
    gain_share = lax.dynamic_slice_in_dim(columns[CONV + 1], device * gain_width, gain_width, axis=0)
    head_total = jnp.concatenate(
        [
            natural(both[:, CONV + 1 : CONV + 3, HALF : HALF + heads], heads // chips),
            jnp.sum(columns[CONV + 2].reshape(1, HEADS, HEADDIM), axis=2),
        ]
    )

    def interleave(mine, theirs):
        width = mine.shape[1] // chips
        both = in_core_order(mine.reshape(rows, chips, width), theirs.reshape(rows, chips, width), core, 2)
        return both.reshape(rows, -1)

    keep_gate, got_gate = mine_and_partner(gate_share)
    (_, x_cut), _ = column_parts(HALF)
    (_, state_cut), _ = column_parts(STATE + LANES)
    both = x_cut + state_cut
    conv_share = jnp.concatenate(
        [conv_share[..., :x_cut], conv_share[..., both : both + HALF - x_cut], conv_share[..., x_cut:both], conv_share[..., both + HALF - x_cut :]],
        axis=-1,
    )
    keep, got = mine_and_partner(conv_share)
    state_end = HALF + STATE
    in_share = jnp.concatenate(
        [
            interleave(keep_gate, got_gate),
            interleave(keep[:, :HALF], got[:, :HALF]),
            in_core_order(keep[:, HALF:state_end], got[:, HALF:state_end], core, 1).reshape(rows, -1),
            interleave(keep[:, state_end : state_end + heads], got[:, state_end : state_end + heads]),
        ],
        axis=1,
    ).astype(f32)
    pre_share = jnp.sum(in_proj.astype(f32) * in_share, axis=1) / pre_gain.astype(f32)
    return (hidden_out, grad_in, in_share, out_share, taps_share, pre_share, gain_share, head_total)


def solution(mesh):
    devices = mesh.devices
    cores = Mesh(devices.reshape(devices.shape[0] // 2, 2, devices.shape[1]), ("chip", "core", "seg"))
    dp, both = ("chip", "core"), ("chip", "core", "seg")
    tokens = P(dp, "seg", None)
    return jax.shard_map(
        per_device,
        mesh=cores,
        in_specs=(tokens, tokens, P(both, None), P(both, None), P(None, both), P(both), P(both), P()),
        out_specs=(tokens, tokens, P(both, None), P(both, None), P(None, both), P(both), P(both), P()),
        check_vma=False,
    )
```

```python
import jax
import jax.numpy as jnp
from jax import lax
from jax.experimental import pallas as pl
from jax.experimental.pallas import tpu as pltpu
from jax.sharding import Mesh
from jax.sharding import PartitionSpec as P

HEADS = 48
HEADDIM = 64
STATE = 128
CONV = 4
INNER = 3072
XBC = 3328
HALF = INNER // 2
LANES = 128
SEGS = 4
LIGHT = pl.CostEstimate(flops=1024, bytes_accessed=1024, transcendentals=0)
VMEM_LIMIT = 48 * 1024 * 1024
LOG2E = 1.4426950408889634

epsilon = 1e-05
f32 = jnp.float32
bf16 = jnp.bfloat16


def own_columns(array, core):
    chips = lax.axis_size("chip")
    width = array.shape[-1] // (2 * chips)
    parted = array.reshape(array.shape[:-1] + (chips, 2, width))
    picked = lax.dynamic_index_in_dim(parted, core, axis=parted.ndim - 2, keepdims=False)
    return picked.reshape(array.shape[:-1] + (chips * width,))


def to_partner(array):
    return lax.ppermute(array, "core", [(0, 1), (1, 0)])


def in_core_order(mine, theirs, core, axis):
    first = jnp.where(core == 0, mine, theirs)
    second = jnp.where(core == 0, theirs, mine)
    return jnp.stack([first, second], axis=axis)


def chip_dims():
    return (lax.axis_size("chip") // 2, 2, lax.axis_size("seg"))


def chip_place():
    chip = lax.axis_index("chip")
    return (chip // 2, chip % 2, lax.axis_index("seg"))


def moved(array, dim, by):
    sizes = chip_dims()
    index = lambda at: (at[0] * sizes[1] + at[1]) * sizes[2] + at[2]
    pairs = []
    for a in range(sizes[0]):
        for b in range(sizes[1]):
            for z in range(sizes[2]):
                to = [a, b, z]
                to[dim] = (to[dim] + by) % sizes[dim]
                pairs.append((index((a, b, z)), index(to)))
    return lax.ppermute(array, ("chip", "seg"), pairs)


def tie(*values):
    return lax.optimization_barrier(values)


def gather_step(data, dim):
    return [data] + [moved(data, dim, by) for by in range(1, chip_dims()[dim])]


def plane_steps():
    a, b, _ = chip_dims()
    steps = [(at // b, at % b) for at in range(1, a * b)]
    return sorted(steps, key=lambda by: bool(by[0] and by[1]))


def near_count():
    a, b, _ = chip_dims()
    return a + b - 2


def moved_plane(array, by_a, by_b):
    a, b, z = chip_dims()
    pairs = [
        ((at_a * b + at_b) * z + at_z, ((at_a + by_a) % a * b + (at_b + by_b) % b) * z + at_z)
        for at_a in range(a)
        for at_b in range(b)
        for at_z in range(z)
    ]
    return lax.ppermute(array, ("chip", "seg"), pairs)


def gather_plane(pieces):
    data = jnp.stack(pieces)
    moves = [moved_plane(data, *by) for by in plane_steps()]
    return data, moves[: near_count()], moves[near_count() :]


def placed_kernel(plan, place_ref, *refs):
    sources, target, sems = refs[:-2], refs[-2], refs[-1]
    copies = []
    for source, lead, at, paired in plan:
        spot = [lax.rem(place_ref[dim] + (size - back), size) for dim, (back, size) in enumerate(at)]
        to = target.at[spot[0], spot[1], :, spot[2]] if paired else target.at[spot[0], spot[1], spot[2]]
        copies.append(pltpu.make_async_copy(sources[source].at[lead], to, sems.at[len(copies)]))
    for copy in copies:
        copy.start()
    for copy in copies:
        copy.wait()


def whole_matrix(gathered, paired):
    a, b, z = chip_dims()
    plan = [
        (source, back, ((by[0], a), (by[1], b), (back, z)), paired)
        for source, by in enumerate([(0, 0)] + plane_steps())
        for back in range(z)
    ]
    block = gathered[0].shape[1:]
    shape = (a, b, 2, z) + block[1:] if paired else (a, b, z) + block
    anywhere = pl.BlockSpec(memory_space=pl.ANY)
    whole = pl.pallas_call(
        lambda *refs: placed_kernel(plan, *refs),
        out_shape=jax.ShapeDtypeStruct(shape, bf16),
        in_specs=[pl.BlockSpec(memory_space=pltpu.SMEM)] + [anywhere] * len(gathered),
        out_specs=pl.BlockSpec(memory_space=pltpu.VMEM),
        scratch_shapes=[pltpu.SemaphoreType.DMA((len(plan),))],
        compiler_params=pltpu.CompilerParams(vmem_limit_bytes=VMEM_LIMIT),
        cost_estimate=LIGHT,
    )(jnp.stack(chip_place()).astype(jnp.int32), *gathered)
    return whole.reshape(-1, shape[-1])


def total(terms):
    result = terms[0].astype(f32)
    for term in terms[1:]:
        result = result + term.astype(f32)
    return result


def reduce_send(terms, axis, dim, wire):
    place, size = chip_place()[dim], chip_dims()[dim]
    pick = lambda at: [lax.dynamic_index_in_dim(term, at, axis=axis, keepdims=False) for term in terms]
    received = [moved(total(pick((place + by) % size)).astype(wire), dim, by) for by in range(1, size)]
    return pick(place), received


def reduce_plane(partials):
    (at_a, at_b, _), (a, b, _) = chip_place(), chip_dims()

    def pick(by_a, by_b):
        chip = (at_a + by_a) % a * b + (at_b + by_b) % b
        flat = [partial.reshape((a * b,) + partial.shape[2:]) for partial in partials]
        return jnp.concatenate(
            [lax.dynamic_index_in_dim(array, chip, axis=0, keepdims=False) for array in flat], axis=-1
        )

    return [([pick(0, 0)], [moved_plane(pick(*by), *by) for by in plane_steps()])]


def reduce_z(firsts):
    joined = jnp.concatenate([total(kept + received) for kept, received in firsts], axis=-1)
    return [reduce_send([joined], 0, 2, bf16)]


def reduce_end(third):
    return total(third[0][0] + third[0][1])


def arrivals(parts):
    return [received for _, received in parts]


def arrived(parts, received):
    return [(kept, new) for (kept, _), new in zip(parts, received)]


def line_perm(turn, back):
    line = lax.axis_size("seg")
    parts = line // SEGS
    pairs = []
    for core in range(2):
        for place in range(line):
            half, odd = divmod(place % SEGS, 2)
            source = core * line + place
            target = odd * line + (2 * core + (half ^ turn)) * parts + place // SEGS
            pairs.append((target, source) if back else (source, target))
    return pairs


def swapped(pair, turn):
    return [jnp.where(turn == 0, pair[0], pair[1]), jnp.where(turn == 0, pair[1], pair[0])]


def whole_sequence(array, core, place):
    parts = lax.axis_size("seg") // SEGS
    pieces = swapped([array[0], array[1]], (place % SEGS) // 2)
    got = [lax.ppermute(piece, ("core", "seg"), line_perm(turn, False)) for turn, piece in enumerate(pieces)]
    return jnp.stack(swapped(got, (place // parts) % 2))


def back_to_owner(ordered, core, place):
    parts = lax.axis_size("seg") // SEGS
    pieces = swapped([ordered[0], ordered[1]], (place // parts) % 2)
    got = [lax.ppermute(piece, ("core", "seg"), line_perm(turn, True)) for turn, piece in enumerate(pieces)]
    return jnp.stack(swapped(got, (place % SEGS) // 2))


def part_pairs(step):
    line = lax.axis_size("seg")
    parts = line // SEGS
    return [(i, i + step) for i in range(line) if 0 <= i + step < line and i // parts == (i + step) // parts]


def entering(decay, state, step):
    parts = lax.axis_size("seg") // SEGS
    total = jnp.zeros_like(state)
    for _ in range(parts - 1):
        total = lax.ppermute(decay * total + state, "seg", part_pairs(step))
    return total


def borrowed(array, step):
    parts = lax.axis_size("seg") // SEGS
    if parts == 1:
        return jnp.zeros_like(array)
    return lax.ppermute(array, "seg", part_pairs(step))


def spilled(grad, edge, taps):
    if lax.axis_size("seg") == SEGS:
        return grad
    edge = borrowed(edge, -1)
    spill = jnp.stack(
        [
            sum(taps[k] * edge[CONV - 1 - k - early] for k in range(CONV - early))
            for early in range(CONV - 1, 0, -1)
        ]
    )
    at = grad.shape[0] - CONV + 1
    return grad.at[at:].set((grad[at:].astype(f32) + spill).astype(bf16))


def dot(a, b, contract):
    return lax.dot_general(a, b, (contract, ((), ())), preferred_element_type=f32)


def normed_kernel(slabs, core_ref, mine_ref, other_ref, gain_ref, normed_ref, turned_ref):
    own = lax.rem(pl.program_id(0), 2) == core_ref[0]
    hidden = jnp.where(own, mine_ref[0], other_ref[0]).astype(f32)
    scale = lax.rsqrt(jnp.mean(hidden * hidden, axis=1, keepdims=True) + epsilon)
    normed = hidden * scale * gain_ref[...]
    normed_ref[...] = normed.astype(bf16)
    turned = normed.T.astype(bf16)
    for to, at, size in slabs:
        turned_ref[to : to + size] = turned[at : at + size]


def normed_tokens(core, mine, other, gain, rows):
    segs, seg_len, width = 2 * mine.shape[0], mine.shape[1], mine.shape[2]
    a, b, z = chip_dims()
    group = 2 * z * rows
    inside = rows % 16 == 0
    slabs = [(0, 0, width)]
    if inside:
        slabs = [
            (chip * group + (at * 2 + core_at) * rows, chip * group + (core_at * z + at) * rows, rows)
            for chip in range(a * b)
            for core_at in range(2)
            for at in range(z)
        ]
    normed, turned = pl.pallas_call(
        lambda *refs: normed_kernel(slabs, *refs),
        grid_spec=pltpu.PrefetchScalarGridSpec(
            num_scalar_prefetch=1,
            grid=(segs,),
            in_specs=[
                pl.BlockSpec((1, seg_len, width), lambda i, core: (i // 2, 0, 0)),
                pl.BlockSpec((1, seg_len, width), lambda i, core: (i // 2, 0, 0)),
                pl.BlockSpec((1, width), lambda i, core: (0, 0)),
            ],
            out_specs=(
                pl.BlockSpec((seg_len, width), lambda i, core: (i, 0)),
                pl.BlockSpec((width, seg_len), lambda i, core: (0, i)),
            ),
        ),
        out_shape=(
            jax.ShapeDtypeStruct((segs * seg_len, width), bf16),
            jax.ShapeDtypeStruct((width, segs * seg_len), bf16),
        ),
        compiler_params=pltpu.CompilerParams(dimension_semantics=("arbitrary",), vmem_limit_bytes=VMEM_LIMIT),
        cost_estimate=LIGHT,
    )(core.reshape(1).astype(jnp.int32), mine, other, gain.reshape(1, width))
    if not inside:
        turned = turned.reshape(a, b, 2, z, rows, -1).transpose(0, 1, 3, 2, 4, 5).reshape(turned.shape)
    return normed, turned


def mixed_kernel(gated_ref, scale_ref, gain_ref, mixed_ref, turned_ref):
    mixed = gated_ref[...] * scale_ref[...] * gain_ref[...]
    mixed_ref[...] = mixed.astype(bf16)
    turned_ref[...] = mixed.T.astype(bf16)


def mixed_tokens(gated, scale, gain, seg_len):
    length, width = gated.shape
    return pl.pallas_call(
        mixed_kernel,
        grid=(length // seg_len,),
        in_specs=[
            pl.BlockSpec((seg_len, width), lambda i: (i, 0)),
            pl.BlockSpec((seg_len, 1), lambda i: (i, 0)),
            pl.BlockSpec((1, width), lambda i: (0, 0)),
        ],
        out_specs=(
            pl.BlockSpec((seg_len, width), lambda i: (i, 0)),
            pl.BlockSpec((width, seg_len), lambda i: (0, i)),
        ),
        out_shape=(
            jax.ShapeDtypeStruct((length, width), bf16),
            jax.ShapeDtypeStruct((width, length), bf16),
        ),
        compiler_params=pltpu.CompilerParams(dimension_semantics=("arbitrary",), vmem_limit_bytes=VMEM_LIMIT),
        cost_estimate=LIGHT,
    )(gated, scale, gain.reshape(1, width))


def columns_of(pair):
    return pl.ds(pair * LANES, LANES)


def low_half(shape):
    return lax.broadcasted_iota(jnp.int32, shape, len(shape) - 1) < HEADDIM


def pair_columns(array, pair, low):
    rows = array.shape[0]
    first = jnp.broadcast_to(array[:, 2 * pair : 2 * pair + 1], (rows, LANES))
    second = jnp.broadcast_to(array[:, 2 * pair + 1 : 2 * pair + 2], (rows, LANES))
    return jnp.where(low, first, second)


def conv_parts(current, before, taps):
    rows = current.shape[0]
    padded = jnp.concatenate([before, current], axis=0)
    seen = [padded[8 - CONV + 1 + k : 8 - CONV + 1 + k + rows] for k in range(CONV - 1)] + [current]
    total = taps[CONV : CONV + 1]
    for k in range(CONV):
        total = total + taps[k : k + 1] * seen[k]
    return total, seen


def step_terms(raw, head, seg_len):
    shifted = raw + head[1:2]
    step = jnp.maximum(shifted, 0.0) + jnp.log1p(jnp.exp(-jnp.abs(shifted)))
    log_decay = step * head[0:1]
    at_or_before = lax.broadcasted_iota(jnp.int32, (seg_len, seg_len), 0) >= lax.broadcasted_iota(
        jnp.int32, (seg_len, seg_len), 1
    )
    sums = lax.dot_general(
        jnp.where(at_or_before, 1.0, 0.0), log_decay, (((1,), (0,)), ((), ())),
        precision=lax.Precision.HIGHEST, preferred_element_type=f32,
    )
    return shifted, step, log_decay, sums * LOG2E


def forward_kernel(
    proj_ref, taps_ref, head_ref, skip_ref, rim_ref, init_ref,
    values_ref, prior_ref, final_ref, last_ref, state_ref, tail_ref,
):
    seg_len = proj_ref.shape[0]
    half = seg_len // 2

    @pl.when(pl.program_id(0) == 0)
    def _():
        state_ref[...] = init_ref[...]
        tail_ref[...] = rim_ref[...]

    def activated(begin):
        at = pl.ds(begin, LANES)
        total, _ = conv_parts(proj_ref[:, at], tail_ref[:, at], taps_ref[:, at])
        return total * jax.nn.sigmoid(total)

    b_low = activated(HALF).astype(bf16)
    b_turned = activated(HALF).T.astype(bf16)
    c_low = activated(HALF + STATE).astype(bf16)
    _, step, _, sums = step_terms(proj_ref[:, HALF + 2 * STATE :], head_ref, seg_len)
    sums_turned, step_turned = sums.T, step.T
    scores = dot(c_low, b_low, ((1,), (1,)))
    kept = lax.broadcasted_iota(jnp.int32, (half, half), 0) >= lax.broadcasted_iota(jnp.int32, (half, half), 1)
    first_scores = jnp.where(kept, scores[:half, :half], 0.0)
    later_scores = scores[half:, :half]
    second_scores = jnp.where(kept, scores[half:, half:], 0.0)
    low = low_half((seg_len, LANES))
    last_ref[...] = jnp.broadcast_to(sums[seg_len - 1 :], last_ref.shape)

    for pair in range(HEADS // 4):
        at = columns_of(pair)
        x_values = activated(pair * LANES)
        x_low = x_values.astype(bf16)
        sums_pair = pair_columns(sums, pair, low)
        last_pair = sums_pair[seg_len - 1 :]
        carry = jnp.exp2(last_pair - sums_pair) * pair_columns(step, pair, low)
        scaled_x = (carry * x_low.astype(f32)).astype(bf16)
        prior = state_ref[:, at]
        prior_low = prior.astype(bf16)
        prior_ref[0, :, at] = prior_low
        from_state = jnp.exp2(sums_pair) * dot(c_low, prior_low, ((1,), (0,)))
        state_ref[:, at] = jnp.exp2(last_pair) * prior + dot(b_turned, scaled_x, ((1,), (0,)))
        early, late = 0.0, 0.0
        for side in range(2):
            head = 2 * pair + side
            x_side = jnp.where(low if side == 0 else ~low, x_values, 0.0).astype(bf16)
            at_token = jnp.broadcast_to(sums[:, head : head + 1], (seg_len, half))
            at_source, source_step = sums_turned[head : head + 1], step_turned[head : head + 1]
            first = jnp.exp2(jnp.minimum(at_token[:half] - at_source[:, :half], 0.0)) * first_scores
            first = (first * source_step[:, :half]).astype(bf16)
            later = jnp.exp2(at_token[half:] - at_source[:, :half]) * later_scores
            later = (later * source_step[:, :half]).astype(bf16)
            second = jnp.exp2(jnp.minimum(at_token[half:] - at_source[:, half:], 0.0)) * second_scores
            second = (second * source_step[:, half:]).astype(bf16)
            early = early + dot(first, x_side[:half], ((1,), (0,)))
            late = late + dot(jnp.concatenate([later, second], axis=1), x_side, ((1,), (0,)))
        intra = jnp.concatenate([early, late], axis=0)
        values_ref[:, at] = intra + from_state + skip_ref[:, at] * x_values

    tail_ref[...] = proj_ref[seg_len - 8 :, : HALF + 2 * STATE]
    final_ref[...] = state_ref[...]


def full_block(shape):
    return pl.BlockSpec(shape, lambda *_: (0,) * len(shape))


def scan_forward(proj, taps, head, skip, rim, init, seg_len):
    segs = proj.shape[0] // seg_len
    wide = HALF + 2 * STATE
    return pl.pallas_call(
        forward_kernel,
        grid=(segs,),
        out_shape=(
            jax.ShapeDtypeStruct((proj.shape[0], HALF), f32),
            jax.ShapeDtypeStruct((segs, STATE, HALF), bf16),
            jax.ShapeDtypeStruct((STATE, HALF), f32),
            jax.ShapeDtypeStruct((segs * 8, LANES), f32),
        ),
        in_specs=[
            pl.BlockSpec((seg_len, proj.shape[1]), lambda i: (i, 0)),
            full_block((8, wide)),
            full_block((8, LANES)),
            full_block((1, HALF)),
            full_block((8, wide)),
            full_block((STATE, HALF)),
        ],
        out_specs=(
            pl.BlockSpec((seg_len, HALF), lambda i: (i, 0)),
            pl.BlockSpec((1, STATE, HALF), lambda i: (i, 0, 0)),
            full_block((STATE, HALF)),
            pl.BlockSpec((8, LANES), lambda i: (i, 0)),
        ),
        scratch_shapes=[pltpu.VMEM((STATE, HALF), f32), pltpu.VMEM((8, wide), f32)],
        compiler_params=pltpu.CompilerParams(
            dimension_semantics=("arbitrary",), vmem_limit_bytes=VMEM_LIMIT
        ),
        cost_estimate=LIGHT,
    )(proj, taps, head, skip, rim, init)


def split_dot(array, other):
    high = array.astype(bf16)
    rest = (array - high.astype(f32)).astype(bf16)
    return dot(high, other, ((1,), (0,))) + dot(rest, other, ((1,), (0,)))


def backward_kernel(
    group, proj_ref, before_ref, taps_ref, rim_ref, shared_ref, shared_before_ref, shared_taps_ref, shared_rim_ref,
    head_ref, skip_ref, end_ref, prior_ref, values_ref, grad_ref, core_ref,
    grad_x_ref, mine_ref, theirs_ref, grad_raw_ref, taps_grad_ref, skip_grad_ref, head_grad_ref, edge_ref, start_ref,
    later_ref, local_ref, scaled_ref, grad_state_ref, inner_ref, source_ref, carry_ref, decay_ref,
):
    seg_len = proj_ref.shape[0]
    half = seg_len // 2
    turn = pl.program_id(0)

    @pl.when(turn == 0)
    def _():
        later_ref[...] = end_ref[...]
        edge_ref[...] = jnp.zeros_like(edge_ref)
        taps_grad_ref[...] = jnp.zeros_like(taps_grad_ref)
        skip_grad_ref[...] = jnp.zeros_like(skip_grad_ref)
        head_grad_ref[...] = jnp.zeros_like(head_grad_ref)

    first_segment = turn == pl.num_programs(0) - 1

    def conv_at(at, current, ahead, taps, rim):
        before = jnp.where(first_segment, rim[:, at], ahead[:, at])
        return conv_parts(current[:, at], before, taps[:, at])

    def activated(begin):
        total, _ = conv_at(pl.ds(begin, LANES), shared_ref, shared_before_ref, shared_taps_ref, shared_rim_ref)
        return total * jax.nn.sigmoid(total)

    b_values = activated(0)
    c_values = activated(STATE)
    b_low, c_low, c_turned = b_values.astype(bf16), c_values.astype(bf16), c_values.T.astype(bf16)
    shifted, step, log_decay, sums = step_terms(shared_ref[:, 2 * STATE :], head_ref, seg_len)
    sums_turned = sums.T
    scores = dot(b_low, c_low, ((1,), (1,)))
    kept = lax.broadcasted_iota(jnp.int32, (half, half), 0) <= lax.broadcasted_iota(jnp.int32, (half, half), 1)
    first_scores = jnp.where(kept, scores[:half, :half], 0.0)
    later_scores = scores[:half, half:]
    second_scores = jnp.where(kept, scores[half:, half:], 0.0)
    low = low_half((seg_len, LANES))
    first_grad, later_grad, second_grad = 0.0, 0.0, 0.0

    pairs = grad_ref.shape[1] // LANES
    for pair in range(pairs):
        at = columns_of(pair)
        total, seen = conv_at(at, proj_ref, before_ref, taps_ref, rim_ref)
        sigmoid = jax.nn.sigmoid(total)
        x_values = total * sigmoid
        x_low = x_values.astype(bf16)
        x_wide = x_low.astype(f32)
        sums_pair = pair_columns(sums, group * pairs + pair, low)
        step_pair = pair_columns(step, group * pairs + pair, low)
        last_pair = sums_pair[seg_len - 1 :]
        gap = jnp.exp2(last_pair - sums_pair)
        scaled_ref[:, at] = (gap * step_pair * x_wide).astype(bf16)
        grad_values = grad_ref[:, at]
        grad_state_ref[:, at] = (grad_values * jnp.exp2(sums_pair)).astype(bf16)
        later = later_ref[:, at]
        later_low = later.astype(bf16)
        local_ref[:, at] = later_low
        prior = prior_ref[0, :, at]
        decay_ref[:, at] = jnp.broadcast_to(
            jnp.sum(later * prior.astype(f32), axis=0, keepdims=True), (8, LANES)
        )
        grad_prior = dot(c_turned, grad_state_ref[:, at], ((1,), (0,)))
        later_ref[:, at] = jnp.exp2(last_pair) * later + grad_prior
        grad_scaled = dot(b_low, later_low, ((1,), (0,)))
        stepped = (step_pair * x_wide).astype(bf16)
        early, late = 0.0, 0.0
        for side in range(2):
            head = 2 * (group * pairs + pair) + side
            grad_low = jnp.where(low if side == 0 else ~low, grad_values, 0.0).astype(bf16)
            at_source = jnp.broadcast_to(sums[:, head : head + 1], (seg_len, half))
            at_token = sums_turned[head : head + 1]
            grad_weights = dot(stepped, grad_low, ((1,), (1,)))
            first = jnp.exp2(jnp.minimum(at_token[:, :half] - at_source[:half], 0.0))
            after = jnp.exp2(at_token[:, half:] - at_source[:half])
            second = jnp.exp2(jnp.minimum(at_token[:, half:] - at_source[half:], 0.0))
            first_grad = first_grad + first * grad_weights[:half, :half]
            later_grad = later_grad + after * grad_weights[:half, half:]
            second_grad = second_grad + second * grad_weights[half:, half:]
            upper = jnp.concatenate([first * first_scores, after * later_scores], axis=1).astype(bf16)
            early = early + dot(upper, grad_low, ((1,), (0,)))
            late = late + dot((second * second_scores).astype(bf16), grad_low[half:], ((1,), (0,)))
        inner = jnp.concatenate([early, late], axis=0)
        skip = skip_ref[:, at]
        skip_grad_ref[:, at] += jnp.sum(grad_values * x_values, axis=0, keepdims=True)
        inner_ref[:, at] = grad_values * (values_ref[:, at] - skip * x_values)
        source_ref[:, at] = x_wide * inner
        carry_ref[:, at] = x_wide * grad_scaled
        grad_x = skip * grad_values + step_pair * (inner + gap * grad_scaled)
        grad_total = grad_x * (sigmoid * (1.0 + total * (1.0 - sigmoid)))
        for k in range(CONV):
            taps_grad_ref[k : k + 1, at] += jnp.sum(grad_total * seen[k], axis=0, keepdims=True)
        taps_grad_ref[CONV : CONV + 1, at] += jnp.sum(grad_total, axis=0, keepdims=True)
        extended = jnp.concatenate([grad_total, edge_ref[:, at]], axis=0)
        edge_ref[:, at] = grad_total[:8]
        taps = taps_ref[:, at]
        grad_conv = taps[CONV - 1 : CONV] * grad_total
        for k in range(CONV - 1):
            grad_conv = grad_conv + taps[k : k + 1] * extended[CONV - 1 - k : CONV - 1 - k + seg_len]
        grad_x_ref[:, at] = grad_conv.astype(bf16)

    width = grad_ref.shape[1]
    channel = lax.broadcasted_iota(jnp.int32, (width, LANES), 0) // HEADDIM + group * width // HEADDIM
    heads = jnp.where(channel == lax.broadcasted_iota(jnp.int32, (width, LANES), 1), 1.0, 0.0).astype(bf16)
    tail = jnp.exp2(sums[seg_len - 1 :] - sums)
    source_grad = split_dot(source_ref[...], heads)
    step_grad = source_grad + tail * split_dot(carry_ref[...], heads)
    used = step * step_grad
    sum_grad = split_dot(inner_ref[...], heads) - used
    at_last = jnp.sum(used - step * source_grad, axis=0, keepdims=True)
    at_last = at_last + split_dot(decay_ref[...], heads)[:1] * jnp.exp2(sums[seg_len - 1 :])
    is_last = lax.broadcasted_iota(jnp.int32, (seg_len, LANES), 0) == seg_len - 1
    sum_grad = sum_grad + jnp.where(is_last, at_last, 0.0)
    at_or_after = lax.broadcasted_iota(jnp.int32, (seg_len, seg_len), 0) <= lax.broadcasted_iota(
        jnp.int32, (seg_len, seg_len), 1
    )
    log_grad = lax.dot_general(
        jnp.where(at_or_after, 1.0, 0.0), sum_grad, (((1,), (0,)), ((), ())),
        precision=lax.Precision.HIGHEST, preferred_element_type=f32,
    )
    grad_raw = (step_grad + head_ref[0:1] * log_grad) * jax.nn.sigmoid(shifted)
    grad_raw_ref[...] = grad_raw
    head_grad_ref[CONV + 1 : CONV + 2] += jnp.sum(log_grad * log_decay, axis=0, keepdims=True)
    head_grad_ref[CONV + 2 : CONV + 3] += jnp.sum(grad_raw, axis=0, keepdims=True)

    first_low = jnp.where(kept, first_grad, 0.0)
    second_low = jnp.where(kept, second_grad, 0.0)
    grad_scores = jnp.concatenate(
        [
            jnp.concatenate([first_low, later_grad], axis=1),
            jnp.concatenate([jnp.zeros_like(first_low), second_low], axis=1),
        ],
        axis=0,
    )
    start_ref[...] = later_ref[...]
    grad_b = dot(scaled_ref[...], local_ref[...], ((1,), (1,))) + dot(
        grad_scores.astype(bf16), c_low, ((1,), (0,))
    )
    grad_c = dot(grad_state_ref[...], prior_ref[0], ((1,), (1,))) + dot(
        grad_scores.T.astype(bf16), b_low, ((1,), (0,))
    )
    first = core_ref[0] == 0
    mine_ref[...] = jnp.where(first, grad_b, grad_c)
    theirs_ref[...] = jnp.where(first, grad_c, grad_b)


GROUPS = 1


def scan_backward(group, core, proj, taps, head, skip, rim, end, prior, values, grad_values, seg_len):
    length = proj.shape[0]
    segs = length // seg_len
    width, shared = HALF // GROUPS, proj.shape[1] - HALF
    back = lambda width, at=0: pl.BlockSpec((seg_len, width), lambda i: (segs - 1 - i, at))
    row_ahead = lambda i: jnp.maximum((segs - 1 - i) * (seg_len // 8) - 1, 0)
    ahead = lambda width, at: pl.BlockSpec((8, width), lambda i: (row_ahead(i), at))
    column = lambda rows, width, at: pl.BlockSpec((rows, width), lambda i: (0, at))
    both = HALF // shared
    return pl.pallas_call(
        lambda *refs: backward_kernel(group, *refs),
        grid=(segs,),
        out_shape=(
            jax.ShapeDtypeStruct((length, width), bf16),
            jax.ShapeDtypeStruct((length, STATE), f32),
            jax.ShapeDtypeStruct((length, STATE), f32),
            jax.ShapeDtypeStruct((length, LANES), f32),
            jax.ShapeDtypeStruct((8, width), f32),
            jax.ShapeDtypeStruct((1, width), f32),
            jax.ShapeDtypeStruct((8, LANES), f32),
            jax.ShapeDtypeStruct((8, width), f32),
            jax.ShapeDtypeStruct((STATE, width), f32),
        ),
        in_specs=[
            back(width, group),
            ahead(width, group),
            column(8, width, group),
            column(8, width, group),
            back(shared, both),
            ahead(shared, both),
            column(8, shared, both),
            column(8, shared, both),
            full_block((8, LANES)),
            column(1, width, group),
            column(STATE, width, group),
            pl.BlockSpec((1, STATE, width), lambda i: (segs - 1 - i, 0, group)),
            back(width, group),
            back(width, group),
            pl.BlockSpec(memory_space=pltpu.SMEM),
        ],
        out_specs=(
            back(width),
            back(STATE),
            back(STATE),
            back(LANES),
            full_block((8, width)),
            full_block((1, width)),
            full_block((8, LANES)),
            full_block((8, width)),
            full_block((STATE, width)),
        ),
        scratch_shapes=[
            pltpu.VMEM((STATE, width), f32),
            pltpu.VMEM((STATE, width), bf16),
            pltpu.VMEM((seg_len, width), bf16),
            pltpu.VMEM((seg_len, width), bf16),
            pltpu.VMEM((seg_len, width), f32),
            pltpu.VMEM((seg_len, width), f32),
            pltpu.VMEM((seg_len, width), f32),
            pltpu.VMEM((8, width), f32),
        ],
        compiler_params=pltpu.CompilerParams(
            dimension_semantics=("arbitrary",), vmem_limit_bytes=VMEM_LIMIT
        ),
        cost_estimate=LIGHT,
    )(
        proj, proj, taps, rim, proj, proj, taps, rim, head, skip, end, prior, values, grad_values,
        core.reshape(1).astype(jnp.int32),
    )


def half_kernel(transposed, count, core_ref, *refs):
    inputs, mine_ref, theirs_ref = refs[: 2 * count], refs[-2], refs[-1]
    total = refs[2 * count][...] if len(refs) > 2 * count + 2 else 0.0
    for left, right in zip(inputs[:count], inputs[count:]):
        total = total + dot(left[...], right[...], ((1,), (1 if transposed else 0,)))
    own = lax.rem(pl.program_id(0), 2) == core_ref[0]

    @pl.when(own)
    def _():
        mine_ref[0] = total

    @pl.when(jnp.logical_not(own))
    def _():
        theirs_ref[0] = total.astype(bf16)


def half_products(core, terms, seg_len, width, transposed, base=()):
    length = terms[0][0].shape[0]
    left = [pl.BlockSpec((seg_len, array.shape[1]), lambda i, core: (i, 0)) for array, _, _ in terms]
    right = []
    for array, matrix, at in terms:
        if transposed:
            right.append(pl.BlockSpec((width, array.shape[1]), lambda i, core, at=at: (0, at(core[0]))))
        else:
            right.append(pl.BlockSpec(matrix.shape, lambda i, core: (0, 0)))
    depth = sum(array.shape[1] for array, _, _ in terms)
    mine, theirs = pl.pallas_call(
        lambda *refs: half_kernel(transposed, len(terms), *refs),
        grid_spec=pltpu.PrefetchScalarGridSpec(
            num_scalar_prefetch=1,
            grid=(length // seg_len,),
            in_specs=left + right + [pl.BlockSpec((seg_len, width), lambda i, core: (i, 0)) for _ in base],
            out_specs=[pl.BlockSpec((1, seg_len, width), lambda i, core: (i // 2, 0, 0))] * 2,
        ),
        out_shape=(
            jax.ShapeDtypeStruct((length // seg_len // 2, seg_len, width), f32),
            jax.ShapeDtypeStruct((length // seg_len // 2, seg_len, width), bf16),
        ),
        compiler_params=pltpu.CompilerParams(dimension_semantics=("arbitrary",), vmem_limit_bytes=VMEM_LIMIT),
        cost_estimate=LIGHT,
    )(core.reshape(1).astype(jnp.int32), *[array for array, _, _ in terms], *[matrix for _, matrix, _ in terms], *base)
    return mine, theirs


def shared_kernel(core_ref, proj_ref, rim_ref, taps_ref, mine_ref, other_ref, grad_ref, taps_grad_ref, edge_ref):
    total, seen = conv_parts(proj_ref[...], rim_ref[...], taps_ref[...])
    sigmoid = jax.nn.sigmoid(total)
    grad_total = mine_ref[...] + other_ref[...]
    grad_total = grad_total * (sigmoid * (1.0 + total * (1.0 - sigmoid)))
    sums = [jnp.sum(grad_total * part, axis=0, keepdims=True) for part in seen]
    sums = sums + [jnp.sum(grad_total, axis=0, keepdims=True), jnp.zeros((8 - CONV - 1, LANES), f32)]
    taps_grad_ref[...] = jnp.concatenate(sums, axis=0)
    edge_ref[...] = grad_total[:8]
    taps = taps_ref[...]
    extended = jnp.concatenate([grad_total, jnp.zeros((8, LANES), f32)], axis=0)
    grad_conv = taps[CONV - 1 : CONV] * grad_total
    for k in range(CONV - 1):
        grad_conv = grad_conv + taps[k : k + 1] * extended[CONV - 1 - k : CONV - 1 - k + grad_total.shape[0]]
    grad_ref[...] = grad_conv.astype(bf16)


def shared_backward(core, proj, rim, taps, mine, other):
    length = proj.shape[0]
    picked = lambda rows: pl.BlockSpec((rows, LANES), lambda i, core: (0, HALF // LANES + core[0]))
    whole = lambda rows: pl.BlockSpec((rows, LANES), lambda i, core: (0, 0))
    return pl.pallas_call(
        shared_kernel,
        grid_spec=pltpu.PrefetchScalarGridSpec(
            num_scalar_prefetch=1,
            grid=(1,),
            in_specs=[picked(length), picked(8), picked(8), whole(length), whole(length)],
            out_specs=(whole(length), whole(8), whole(8)),
        ),
        out_shape=(
            jax.ShapeDtypeStruct((length, LANES), bf16),
            jax.ShapeDtypeStruct((8, LANES), f32),
            jax.ShapeDtypeStruct((8, LANES), f32),
        ),
        compiler_params=pltpu.CompilerParams(vmem_limit_bytes=VMEM_LIMIT),
        cost_estimate=LIGHT,
    )(core.reshape(1).astype(jnp.int32), proj, rim, taps, mine, other)


def per_device(hidden_in, cotangent, in_proj, out_proj, conv_params, pre_gain, gated_gain, head_params):
    chips, line = lax.axis_size("chip"), lax.axis_size("seg")
    core, place = lax.axis_index("core"), lax.axis_index("seg")
    rows, model_width = in_proj.shape[0], hidden_in.shape[2]
    heads = HEADS // 2

    conv_width, gain_width = conv_params.shape[1], gated_gain.shape[0]
    used = HALF + 2 * STATE + heads
    spare = -used % LANES
    small = jnp.zeros((rows, spare), bf16)
    small = small.at[: CONV + 1, :conv_width].set(conv_params)
    small = small.at[CONV + 1, :rows].set(pre_gain)
    small = small.at[CONV + 2, :gain_width].set(gated_gain)

    def conv_side(which):
        return jnp.concatenate(
            [
                own_columns(in_proj[:, INNER : 2 * INNER], which),
                in_proj[:, 2 * INNER : INNER + XBC],
                own_columns(in_proj[:, INNER + XBC :], which),
                small,
            ],
            axis=1,
        )

    def gate_side(which):
        return own_columns(in_proj[:, :INNER], which)

    conv_swap = to_partner(conv_side(1 - core))
    conv_block = in_core_order(conv_side(core), conv_swap, core, 0)
    conv_z = gather_step(conv_block, 2)
    gate_swap = to_partner(gate_side(1 - core))
    gate_block = in_core_order(gate_side(core), gate_swap, core, 0)
    conv_z, hidden_in, gate_block = tie(conv_z, hidden_in, gate_block)
    conv_own, conv_near, conv_far = gather_plane(conv_z)
    hidden_half = whole_sequence(hidden_in, core, place)
    conv_own, conv_near, hidden_half, gate_block = tie(conv_own, conv_near, hidden_half, gate_block)
    gate_z = gather_step(gate_block, 2)
    hidden_other = to_partner(hidden_half)
    conv_far, gate_z, hidden_other, cotangent = tie(conv_far, gate_z, hidden_other, cotangent)
    gate_own, gate_near, gate_far = gather_plane(gate_z)
    cot_half = whole_sequence(cotangent, core, place)
    conv_all = whole_matrix([conv_own, *conv_near, *conv_far], True)

    small_all = conv_all.reshape(chips, 2, line, rows, -1)[..., used:].astype(f32)
    taps_full = small_all[..., : CONV + 1, :conv_width].transpose(3, 0, 1, 2, 4).reshape(CONV + 1, XBC)
    taps = jnp.concatenate([own_columns(taps_full[:, :INNER], core), taps_full[:, INNER:]], axis=1)
    gain_pre = small_all[..., CONV + 1, :rows].reshape(model_width)
    gain_gate = lax.dynamic_index_in_dim(
        small_all[..., CONV + 2, :gain_width], core, axis=1, keepdims=False
    ).reshape(HALF)
    params = own_columns(head_params, core)

    seg_len = hidden_half.shape[1]
    tokens = SEGS * seg_len
    normed, normed_turned = normed_tokens(core, hidden_half, hidden_other, gain_pre, rows)
    projected = dot(normed, conv_all, ((1,), (0,)))
    projected, cot_half, gate_near, out_proj = tie(projected, cot_half, gate_near, out_proj)
    out_z = gather_step(out_proj, 2)

    taps = jnp.pad(taps, ((0, 8 - CONV - 1), (0, projected.shape[1] - taps.shape[1])))
    head = jnp.pad(jnp.stack([-jnp.exp(params[0]), params[1]]), ((0, 6), (0, LANES - heads)))
    skip = jnp.repeat(params[2], HEADDIM).reshape(1, HALF)
    wide = HALF + 2 * STATE
    rim = borrowed(projected[tokens - 8 :], 1)
    nothing = jnp.zeros((STATE, HALF), f32)
    values, prior, final, last = scan_forward(projected, taps, head, skip, rim, nothing, seg_len)
    if line > SEGS:
        last = jnp.sum(last.reshape(SEGS, 8, LANES)[:, 0, :heads], axis=0)
        decay = jnp.repeat(jnp.exp2(last), HEADDIM)
        begin = entering(decay, final, 1)
        values, prior, _, _ = scan_forward(projected, taps, head, skip, rim, begin, seg_len)

    values, gate_far, out_z = tie(values, gate_far, out_z)
    out_own, out_near, out_far = gather_plane(out_z)
    gate_matrix = whole_matrix([gate_own, *gate_near, *gate_far], True)
    gate_input = dot(normed, gate_matrix, ((1,), (0,)))
    cot_other = to_partner(cot_half)

    silu_gate = jax.nn.silu(gate_input)
    gated = values * silu_gate
    squares = jnp.sum(gated * gated, axis=1)
    squares_other = to_partner(squares)
    scale = lax.rsqrt((squares + squares_other) / INNER + epsilon)[:, None]
    cot = in_core_order(cot_half, cot_other, core, 1)
    upstream = cot.reshape(tokens, model_width)
    scale, out_near = tie(scale, out_near)
    mixed, mixed_turned = mixed_tokens(gated, scale, gain_gate, seg_len)
    by_owner = lambda grad: grad.astype(bf16).reshape(chip_dims() + (-1, grad.shape[1]))
    out_grad = by_owner(dot(mixed_turned, upstream, ((1,), (0,))))
    out_grad, out_far = tie(out_grad, out_far)
    ((out_kept, out_got),) = reduce_plane([out_grad])
    out_matrix = whole_matrix([out_own, *out_near, *out_far], False)
    branch, branch_sent = half_products(core, [(mixed, out_matrix, None)], seg_len, model_width, False)
    branch_sent, upstream = tie(branch_sent, upstream)
    branch_other = to_partner(branch_sent)
    grad_mixed = dot(upstream, out_matrix, ((1,), (1,)))
    grad_mixed, out_got_near = tie(grad_mixed, out_got[: near_count()])
    unit = gated * scale
    gain_grad = grad_mixed * gain_gate
    along = jnp.sum(gain_grad * unit, axis=1)
    along_other = to_partner(along)
    along_other, branch_other = tie(along_other, branch_other)
    hidden_out = back_to_owner(
        (hidden_half.astype(f32) + branch + branch_other.astype(f32)).astype(bf16), core, place
    )
    along = ((along + along_other) / INNER)[:, None]
    gate_gain_grad = jnp.sum(grad_mixed * unit, axis=0)
    grad_gated = scale * (gain_grad - unit * along)
    grad_values = grad_gated * silu_gate
    sigmoid = jax.nn.sigmoid(gate_input)
    grad_gate = (grad_gated * values * (sigmoid * (1.0 + gate_input * (1.0 - sigmoid)))).astype(bf16)
    gate_grad = by_owner(dot(normed_turned, grad_gate, ((1,), (0,))))
    gate_grad, grad_values, out_got_far, hidden_out = tie(gate_grad, grad_values, out_got[near_count() :], hidden_out)
    out_first = [(out_kept, [*out_got_near, *out_got_far])]
    gate_first = reduce_plane([gate_grad])
    scan = lambda later: scan_backward(
        0, core, projected, taps, head, skip, rim, later, prior, values, grad_values, seg_len
    )
    if line > SEGS:
        nothing = entering(decay, scan(nothing)[-1], -1)
    back = scan(nothing)
    back, gate_got, grad_gate = tie(back, arrivals(gate_first), grad_gate)
    early = reduce_z(out_first + arrived(gate_first, gate_got))
    grad_x, mine, theirs, grad_raw, x_taps_grad, skip_grad, head_sums, x_edge, _ = back
    grad_x = spilled(grad_x, x_edge, taps[:, :HALF])
    other = to_partner(theirs)
    x_grad = by_owner(dot(normed_turned, grad_x, ((1,), (0,))))
    other, x_grad = tie(other, x_grad)
    grad_state, state_taps_grad, state_edge = shared_backward(core, projected, rim, taps, mine, other)
    grad_state = spilled(grad_state, state_edge, lax.dynamic_slice_in_dim(taps, HALF + core * STATE, STATE, axis=1))
    grad_raw = grad_raw.astype(bf16)
    rest_grad = by_owner(dot(normed_turned, jnp.concatenate([grad_state, grad_raw], axis=1), ((1,), (0,))))
    (early_kept, (nearest, *others)), = early
    rest_grad, x_grad, grad_gate, grad_state, nearest = tie(rest_grad, x_grad, grad_gate, grad_state, nearest)
    early = [(early_kept, [nearest, *others])]
    ((conv_kept, conv_got),) = reduce_plane([x_grad, rest_grad])
    base = dot(grad_gate, gate_matrix, ((1,), (1,)))
    terms = [
        (grad_x, conv_all, lambda core: 0),
        (grad_state, conv_all, lambda core: HALF // LANES + core),
        (grad_raw, conv_all, lambda core: (HALF + 2 * STATE) // LANES),
    ]
    grad_normed, sent_normed = half_products(core, terms, seg_len, model_width, True, (base,))
    (early_kept, early_got), = early
    row = lax.broadcasted_iota(jnp.int32, (8, 1), 0)
    small = x_taps_grad + jnp.where(row == CONV + 1, gate_gain_grad, 0.0) + jnp.where(row == CONV + 2, skip_grad, 0.0)
    small = jnp.concatenate([small, state_taps_grad + head_sums], axis=1)
    other_normed, early_got, conv_near, small = tie(to_partner(sent_normed), early_got, conv_got[: near_count()], small)
    early = [(early_kept, early_got)]
    wide_hidden = hidden_half.astype(f32)
    hidden_scale = lax.rsqrt(jnp.mean(wide_hidden * wide_hidden, axis=-1, keepdims=True) + epsilon)
    grad_normed = (grad_normed + other_normed.astype(f32)) * gain_pre
    hidden_unit = wide_hidden * hidden_scale
    along = jnp.mean(grad_normed * hidden_unit, axis=-1, keepdims=True)
    grad_hidden = hidden_scale * (grad_normed - hidden_unit * along)
    grad_in = (cot_half.astype(f32) + grad_hidden).astype(bf16)
    grad_in = back_to_owner(grad_in, core, place)
    grad_in, conv_far = tie(grad_in, conv_got[near_count() :])
    late = reduce_z([(conv_kept, [*conv_near, *conv_far])])
    for dim in range(3):
        small = small + sum(moved(small, dim, by) for by in range(1, chip_dims()[dim]))
    small_other = to_partner(small)
    late_got, small_other = tie(arrivals(late), small_other)
    early_share = reduce_end(early)
    out_share = early_share[:, :model_width]
    paired = lambda share: share.astype(bf16).reshape(2, rows, -1)
    gate_share, conv_share = paired(early_share[:, model_width:]), paired(reduce_end(arrived(late, late_got)))

    def mine_and_partner(share):
        keep = lax.dynamic_index_in_dim(share, core, axis=0, keepdims=False)
        give = lax.dynamic_index_in_dim(share, 1 - core, axis=0, keepdims=False)
        return keep, to_partner(give)

    both = in_core_order(small, small_other, core, 0)
    natural = lambda array, width: array.reshape(2, -1, chips, width).transpose(1, 2, 0, 3).reshape(-1, 2 * chips * width)
    device = (lax.axis_index("chip") * 2 + core) * line + place
    columns = natural(both[:, :, :HALF], HALF // chips)
    taps_all = jnp.concatenate([columns, both[0, :, HALF:], both[1, :, HALF:]], axis=1)[: CONV + 1]
    taps_share = lax.dynamic_slice_in_dim(taps_all, device * conv_width, conv_width, axis=1)
    gain_share = lax.dynamic_slice_in_dim(columns[CONV + 1], device * gain_width, gain_width, axis=0)
    head_total = jnp.concatenate(
        [
            natural(both[:, CONV + 1 : CONV + 3, HALF : HALF + heads], heads // chips),
            jnp.sum(columns[CONV + 2].reshape(1, HEADS, HEADDIM), axis=2),
        ]
    )

    def interleave(mine, theirs):
        width = mine.shape[1] // chips
        both = in_core_order(mine.reshape(rows, chips, width), theirs.reshape(rows, chips, width), core, 2)
        return both.reshape(rows, -1)

    keep_gate, got_gate = mine_and_partner(gate_share)
    keep, got = mine_and_partner(conv_share)
    state_end = HALF + STATE
    in_share = jnp.concatenate(
        [
            interleave(keep_gate, got_gate),
            interleave(keep[:, :HALF], got[:, :HALF]),
            in_core_order(keep[:, HALF:state_end], got[:, HALF:state_end], core, 1).reshape(rows, -1),
            interleave(keep[:, state_end : state_end + heads], got[:, state_end : state_end + heads]),
        ],
        axis=1,
    ).astype(f32)
    pre_share = jnp.sum(in_proj.astype(f32) * in_share, axis=1) / pre_gain.astype(f32)
    return (hidden_out, grad_in, in_share, out_share, taps_share, pre_share, gain_share, head_total)


def solution(mesh):
    devices = mesh.devices
    cores = Mesh(devices.reshape(devices.shape[0] // 2, 2, devices.shape[1]), ("chip", "core", "seg"))
    dp, both = ("chip", "core"), ("chip", "core", "seg")
    tokens = P(dp, "seg", None)
    return jax.shard_map(
        per_device,
        mesh=cores,
        in_specs=(tokens, tokens, P(both, None), P(both, None), P(None, both), P(both), P(both), P()),
        out_specs=(tokens, tokens, P(both, None), P(both, None), P(None, both), P(both), P(both), P()),
        check_vma=False,
    )
```

```python
import jax
import jax.numpy as jnp
from jax import lax
from jax.experimental import pallas as pl
from jax.experimental.pallas import tpu as pltpu
from jax.sharding import Mesh
from jax.sharding import PartitionSpec as P

HEADS = 48
HEADDIM = 64
STATE = 128
CONV = 4
INNER = 3072
XBC = 3328
HALF = INNER // 2
LANES = 128
SEGS = 4
LIGHT = pl.CostEstimate(flops=1024, bytes_accessed=1024, transcendentals=0)
VMEM_LIMIT = 48 * 1024 * 1024
LOG2E = 1.4426950408889634

epsilon = 1e-05
f32 = jnp.float32
bf16 = jnp.bfloat16


def own_columns(array, core):
    chips = lax.axis_size("chip")
    width = array.shape[-1] // (2 * chips)
    parted = array.reshape(array.shape[:-1] + (chips, 2, width))
    picked = lax.dynamic_index_in_dim(parted, core, axis=parted.ndim - 2, keepdims=False)
    return picked.reshape(array.shape[:-1] + (chips * width,))


def to_partner(array):
    return lax.ppermute(array, "core", [(0, 1), (1, 0)])


def in_core_order(mine, theirs, core, axis):
    first = jnp.where(core == 0, mine, theirs)
    second = jnp.where(core == 0, theirs, mine)
    return jnp.stack([first, second], axis=axis)


def chip_dims():
    return (lax.axis_size("chip") // 2, 2, lax.axis_size("seg"))


def chip_place():
    chip = lax.axis_index("chip")
    return (chip // 2, chip % 2, lax.axis_index("seg"))


def moved(array, dim, by):
    sizes = chip_dims()
    index = lambda at: (at[0] * sizes[1] + at[1]) * sizes[2] + at[2]
    pairs = []
    for a in range(sizes[0]):
        for b in range(sizes[1]):
            for z in range(sizes[2]):
                to = [a, b, z]
                to[dim] = (to[dim] + by) % sizes[dim]
                pairs.append((index((a, b, z)), index(to)))
    return lax.ppermute(array, ("chip", "seg"), pairs)


def tie(*values):
    return lax.optimization_barrier(values)


def gather_step(data, dim):
    return [data] + [moved(data, dim, by) for by in range(1, chip_dims()[dim])]


def plane_steps():
    a, b, _ = chip_dims()
    steps = [(at // b, at % b) for at in range(1, a * b)]
    return sorted(steps, key=lambda by: bool(by[0] and by[1]))


def near_count():
    a, b, _ = chip_dims()
    return a + b - 2


def moved_plane(array, by_a, by_b):
    a, b, z = chip_dims()
    pairs = [
        ((at_a * b + at_b) * z + at_z, ((at_a + by_a) % a * b + (at_b + by_b) % b) * z + at_z)
        for at_a in range(a)
        for at_b in range(b)
        for at_z in range(z)
    ]
    return lax.ppermute(array, ("chip", "seg"), pairs)


def gather_plane(pieces):
    data = jnp.stack(pieces)
    moves = [moved_plane(data, *by) for by in plane_steps()]
    return data, moves[: near_count()], moves[near_count() :]


def placed_kernel(plan, place_ref, *refs):
    sources, target, sems = refs[:-2], refs[-2], refs[-1]
    copies = []
    for source, lead, at, paired in plan:
        spot = [lax.rem(place_ref[dim] + (size - back), size) for dim, (back, size) in enumerate(at)]
        to = target.at[spot[0], spot[1], :, spot[2]] if paired else target.at[spot[0], spot[1], spot[2]]
        copies.append(pltpu.make_async_copy(sources[source].at[lead], to, sems.at[len(copies)]))
    for copy in copies:
        copy.start()
    for copy in copies:
        copy.wait()


def whole_matrix(gathered, paired):
    a, b, z = chip_dims()
    plan = [
        (source, back, ((by[0], a), (by[1], b), (back, z)), paired)
        for source, by in enumerate([(0, 0)] + plane_steps())
        for back in range(z)
    ]
    block = gathered[0].shape[1:]
    shape = (a, b, 2, z) + block[1:] if paired else (a, b, z) + block
    anywhere = pl.BlockSpec(memory_space=pl.ANY)
    whole = pl.pallas_call(
        lambda *refs: placed_kernel(plan, *refs),
        out_shape=jax.ShapeDtypeStruct(shape, bf16),
        in_specs=[pl.BlockSpec(memory_space=pltpu.SMEM)] + [anywhere] * len(gathered),
        out_specs=pl.BlockSpec(memory_space=pltpu.VMEM),
        scratch_shapes=[pltpu.SemaphoreType.DMA((len(plan),))],
        compiler_params=pltpu.CompilerParams(vmem_limit_bytes=VMEM_LIMIT),
        cost_estimate=LIGHT,
    )(jnp.stack(chip_place()).astype(jnp.int32), *gathered)
    return whole.reshape(-1, shape[-1])


def total(terms):
    result = terms[0].astype(f32)
    for term in terms[1:]:
        result = result + term.astype(f32)
    return result


def reduce_send(terms, axis, dim, wire):
    place, size = chip_place()[dim], chip_dims()[dim]
    pick = lambda at: [lax.dynamic_index_in_dim(term, at, axis=axis, keepdims=False) for term in terms]
    received = [moved(total(pick((place + by) % size)).astype(wire), dim, by) for by in range(1, size)]
    return pick(place), received


def reduce_plane(partials):
    (at_a, at_b, _), (a, b, _) = chip_place(), chip_dims()

    def pick(by_a, by_b):
        chip = (at_a + by_a) % a * b + (at_b + by_b) % b
        flat = [partial.reshape((a * b,) + partial.shape[2:]) for partial in partials]
        return jnp.concatenate(
            [lax.dynamic_index_in_dim(array, chip, axis=0, keepdims=False) for array in flat], axis=-1
        )

    return [([pick(0, 0)], [moved_plane(pick(*by), *by) for by in plane_steps()])]


def reduce_z(firsts):
    joined = jnp.concatenate([total(kept + received) for kept, received in firsts], axis=-1)
    return [reduce_send([joined], 0, 2, bf16)]


def reduce_end(third):
    return total(third[0][0] + third[0][1])


def arrivals(parts):
    return [received for _, received in parts]


def arrived(parts, received):
    return [(kept, new) for (kept, _), new in zip(parts, received)]


def line_perm(turn, back):
    line = lax.axis_size("seg")
    parts = line // SEGS
    pairs = []
    for core in range(2):
        for place in range(line):
            half, odd = divmod(place % SEGS, 2)
            source = core * line + place
            target = odd * line + (2 * core + (half ^ turn)) * parts + place // SEGS
            pairs.append((target, source) if back else (source, target))
    return pairs


def swapped(pair, turn):
    return [jnp.where(turn == 0, pair[0], pair[1]), jnp.where(turn == 0, pair[1], pair[0])]


def whole_sequence(array, core, place):
    parts = lax.axis_size("seg") // SEGS
    pieces = swapped([array[0], array[1]], (place % SEGS) // 2)
    got = [lax.ppermute(piece, ("core", "seg"), line_perm(turn, False)) for turn, piece in enumerate(pieces)]
    return jnp.stack(swapped(got, (place // parts) % 2))


def back_to_owner(ordered, core, place):
    parts = lax.axis_size("seg") // SEGS
    pieces = swapped([ordered[0], ordered[1]], (place // parts) % 2)
    got = [lax.ppermute(piece, ("core", "seg"), line_perm(turn, True)) for turn, piece in enumerate(pieces)]
    return jnp.stack(swapped(got, (place % SEGS) // 2))


def part_pairs(step):
    line = lax.axis_size("seg")
    parts = line // SEGS
    return [(i, i + step) for i in range(line) if 0 <= i + step < line and i // parts == (i + step) // parts]


def entering(decay, state, step):
    parts = lax.axis_size("seg") // SEGS
    total = jnp.zeros_like(state)
    for _ in range(parts - 1):
        total = lax.ppermute(decay * total + state, "seg", part_pairs(step))
    return total


def borrowed(array, step):
    parts = lax.axis_size("seg") // SEGS
    if parts == 1:
        return jnp.zeros_like(array)
    return lax.ppermute(array, "seg", part_pairs(step))


def spilled(grad, edge, taps):
    if lax.axis_size("seg") == SEGS:
        return grad
    edge = borrowed(edge, -1)
    spill = jnp.stack(
        [
            sum(taps[k] * edge[CONV - 1 - k - early] for k in range(CONV - early))
            for early in range(CONV - 1, 0, -1)
        ]
    )
    at = grad.shape[0] - CONV + 1
    return grad.at[at:].set((grad[at:].astype(f32) + spill).astype(bf16))


def dot(a, b, contract):
    return lax.dot_general(a, b, (contract, ((), ())), preferred_element_type=f32)


def normed_kernel(slabs, core_ref, mine_ref, other_ref, gain_ref, normed_ref, turned_ref):
    own = lax.rem(pl.program_id(0), 2) == core_ref[0]
    hidden = jnp.where(own, mine_ref[0], other_ref[0]).astype(f32)
    scale = lax.rsqrt(jnp.mean(hidden * hidden, axis=1, keepdims=True) + epsilon)
    normed = hidden * scale * gain_ref[...]
    normed_ref[...] = normed.astype(bf16)
    turned = normed.T.astype(bf16)
    for to, at, size in slabs:
        turned_ref[to : to + size] = turned[at : at + size]


def normed_tokens(core, mine, other, gain, rows):
    segs, seg_len, width = 2 * mine.shape[0], mine.shape[1], mine.shape[2]
    a, b, z = chip_dims()
    group = 2 * z * rows
    inside = rows % 16 == 0
    slabs = [(0, 0, width)]
    if inside:
        slabs = [
            (chip * group + (at * 2 + core_at) * rows, chip * group + (core_at * z + at) * rows, rows)
            for chip in range(a * b)
            for core_at in range(2)
            for at in range(z)
        ]
    normed, turned = pl.pallas_call(
        lambda *refs: normed_kernel(slabs, *refs),
        grid_spec=pltpu.PrefetchScalarGridSpec(
            num_scalar_prefetch=1,
            grid=(segs,),
            in_specs=[
                pl.BlockSpec((1, seg_len, width), lambda i, core: (i // 2, 0, 0)),
                pl.BlockSpec((1, seg_len, width), lambda i, core: (i // 2, 0, 0)),
                pl.BlockSpec((1, width), lambda i, core: (0, 0)),
            ],
            out_specs=(
                pl.BlockSpec((seg_len, width), lambda i, core: (i, 0)),
                pl.BlockSpec((width, seg_len), lambda i, core: (0, i)),
            ),
        ),
        out_shape=(
            jax.ShapeDtypeStruct((segs * seg_len, width), bf16),
            jax.ShapeDtypeStruct((width, segs * seg_len), bf16),
        ),
        compiler_params=pltpu.CompilerParams(dimension_semantics=("arbitrary",), vmem_limit_bytes=VMEM_LIMIT),
        cost_estimate=LIGHT,
    )(core.reshape(1).astype(jnp.int32), mine, other, gain.reshape(1, width))
    if not inside:
        turned = turned.reshape(a, b, 2, z, rows, -1).transpose(0, 1, 3, 2, 4, 5).reshape(turned.shape)
    return normed, turned


def mixed_kernel(gated_ref, scale_ref, gain_ref, mixed_ref, turned_ref):
    mixed = gated_ref[...] * scale_ref[...] * gain_ref[...]
    mixed_ref[...] = mixed.astype(bf16)
    turned_ref[...] = mixed.T.astype(bf16)


def mixed_tokens(gated, scale, gain, seg_len):
    length, width = gated.shape
    return pl.pallas_call(
        mixed_kernel,
        grid=(length // seg_len,),
        in_specs=[
            pl.BlockSpec((seg_len, width), lambda i: (i, 0)),
            pl.BlockSpec((seg_len, 1), lambda i: (i, 0)),
            pl.BlockSpec((1, width), lambda i: (0, 0)),
        ],
        out_specs=(
            pl.BlockSpec((seg_len, width), lambda i: (i, 0)),
            pl.BlockSpec((width, seg_len), lambda i: (0, i)),
        ),
        out_shape=(
            jax.ShapeDtypeStruct((length, width), bf16),
            jax.ShapeDtypeStruct((width, length), bf16),
        ),
        compiler_params=pltpu.CompilerParams(dimension_semantics=("arbitrary",), vmem_limit_bytes=VMEM_LIMIT),
        cost_estimate=LIGHT,
    )(gated, scale, gain.reshape(1, width))


def columns_of(pair):
    return pl.ds(pair * LANES, LANES)


def low_half(shape):
    return lax.broadcasted_iota(jnp.int32, shape, len(shape) - 1) < HEADDIM


def pair_columns(array, pair, low):
    rows = array.shape[0]
    first = jnp.broadcast_to(array[:, 2 * pair : 2 * pair + 1], (rows, LANES))
    second = jnp.broadcast_to(array[:, 2 * pair + 1 : 2 * pair + 2], (rows, LANES))
    return jnp.where(low, first, second)


def conv_parts(current, before, taps):
    rows = current.shape[0]
    padded = jnp.concatenate([before, current], axis=0)
    seen = [padded[8 - CONV + 1 + k : 8 - CONV + 1 + k + rows] for k in range(CONV - 1)] + [current]
    total = taps[CONV : CONV + 1]
    for k in range(CONV):
        total = total + taps[k : k + 1] * seen[k]
    return total, seen


def step_terms(raw, head, seg_len):
    shifted = raw + head[1:2]
    step = jnp.maximum(shifted, 0.0) + jnp.log1p(jnp.exp(-jnp.abs(shifted)))
    log_decay = step * head[0:1]
    at_or_before = lax.broadcasted_iota(jnp.int32, (seg_len, seg_len), 0) >= lax.broadcasted_iota(
        jnp.int32, (seg_len, seg_len), 1
    )
    sums = lax.dot_general(
        jnp.where(at_or_before, 1.0, 0.0), log_decay, (((1,), (0,)), ((), ())),
        precision=lax.Precision.HIGHEST, preferred_element_type=f32,
    )
    return shifted, step, log_decay, sums * LOG2E


def forward_kernel(
    proj_ref, taps_ref, head_ref, skip_ref, rim_ref, init_ref,
    values_ref, prior_ref, final_ref, last_ref, state_ref, tail_ref,
):
    seg_len = proj_ref.shape[0]
    half = seg_len // 2

    @pl.when(pl.program_id(0) == 0)
    def _():
        state_ref[...] = init_ref[...]
        tail_ref[...] = rim_ref[...]

    def activated(begin):
        at = pl.ds(begin, LANES)
        total, _ = conv_parts(proj_ref[:, at], tail_ref[:, at], taps_ref[:, at])
        return total * jax.nn.sigmoid(total)

    b_low = activated(HALF).astype(bf16)
    b_turned = activated(HALF).T.astype(bf16)
    c_low = activated(HALF + STATE).astype(bf16)
    _, step, _, sums = step_terms(proj_ref[:, HALF + 2 * STATE :], head_ref, seg_len)
    sums_turned, step_turned = sums.T, step.T
    scores = dot(c_low, b_low, ((1,), (1,)))
    kept = lax.broadcasted_iota(jnp.int32, (half, half), 0) >= lax.broadcasted_iota(jnp.int32, (half, half), 1)
    first_scores = jnp.where(kept, scores[:half, :half], 0.0)
    later_scores = scores[half:, :half]
    second_scores = jnp.where(kept, scores[half:, half:], 0.0)
    low = low_half((seg_len, LANES))
    last_ref[...] = jnp.broadcast_to(sums[seg_len - 1 :], last_ref.shape)

    for pair in range(HEADS // 4):
        at = columns_of(pair)
        x_values = activated(pair * LANES)
        x_low = x_values.astype(bf16)
        sums_pair = pair_columns(sums, pair, low)
        last_pair = sums_pair[seg_len - 1 :]
        carry = jnp.exp2(last_pair - sums_pair) * pair_columns(step, pair, low)
        scaled_x = (carry * x_low.astype(f32)).astype(bf16)
        prior = state_ref[:, at]
        prior_low = prior.astype(bf16)
        prior_ref[0, :, at] = prior_low
        from_state = jnp.exp2(sums_pair) * dot(c_low, prior_low, ((1,), (0,)))
        state_ref[:, at] = jnp.exp2(last_pair) * prior + dot(b_turned, scaled_x, ((1,), (0,)))
        early, late = 0.0, 0.0
        for side in range(2):
            head = 2 * pair + side
            x_side = jnp.where(low if side == 0 else ~low, x_values, 0.0).astype(bf16)
            at_token = jnp.broadcast_to(sums[:, head : head + 1], (seg_len, half))
            at_source, source_step = sums_turned[head : head + 1], step_turned[head : head + 1]
            first = jnp.exp2(jnp.minimum(at_token[:half] - at_source[:, :half], 0.0)) * first_scores
            first = (first * source_step[:, :half]).astype(bf16)
            later = jnp.exp2(at_token[half:] - at_source[:, :half]) * later_scores
            later = (later * source_step[:, :half]).astype(bf16)
            second = jnp.exp2(jnp.minimum(at_token[half:] - at_source[:, half:], 0.0)) * second_scores
            second = (second * source_step[:, half:]).astype(bf16)
            early = early + dot(first, x_side[:half], ((1,), (0,)))
            late = late + dot(jnp.concatenate([later, second], axis=1), x_side, ((1,), (0,)))
        intra = jnp.concatenate([early, late], axis=0)
        values_ref[:, at] = intra + from_state + skip_ref[:, at] * x_values

    tail_ref[...] = proj_ref[seg_len - 8 :, : HALF + 2 * STATE]
    final_ref[...] = state_ref[...]


def full_block(shape):
    return pl.BlockSpec(shape, lambda *_: (0,) * len(shape))


def scan_forward(proj, taps, head, skip, rim, init, seg_len):
    segs = proj.shape[0] // seg_len
    wide = HALF + 2 * STATE
    return pl.pallas_call(
        forward_kernel,
        grid=(segs,),
        out_shape=(
            jax.ShapeDtypeStruct((proj.shape[0], HALF), f32),
            jax.ShapeDtypeStruct((segs, STATE, HALF), bf16),
            jax.ShapeDtypeStruct((STATE, HALF), f32),
            jax.ShapeDtypeStruct((segs * 8, LANES), f32),
        ),
        in_specs=[
            pl.BlockSpec((seg_len, proj.shape[1]), lambda i: (i, 0)),
            full_block((8, wide)),
            full_block((8, LANES)),
            full_block((1, HALF)),
            full_block((8, wide)),
            full_block((STATE, HALF)),
        ],
        out_specs=(
            pl.BlockSpec((seg_len, HALF), lambda i: (i, 0)),
            pl.BlockSpec((1, STATE, HALF), lambda i: (i, 0, 0)),
            full_block((STATE, HALF)),
            pl.BlockSpec((8, LANES), lambda i: (i, 0)),
        ),
        scratch_shapes=[pltpu.VMEM((STATE, HALF), f32), pltpu.VMEM((8, wide), f32)],
        compiler_params=pltpu.CompilerParams(
            dimension_semantics=("arbitrary",), vmem_limit_bytes=VMEM_LIMIT
        ),
        cost_estimate=LIGHT,
    )(proj, taps, head, skip, rim, init)


def split_dot(array, other):
    high = array.astype(bf16)
    rest = (array - high.astype(f32)).astype(bf16)
    return dot(high, other, ((1,), (0,))) + dot(rest, other, ((1,), (0,)))


def backward_kernel(
    group, proj_ref, before_ref, taps_ref, rim_ref, shared_ref, shared_before_ref, shared_taps_ref, shared_rim_ref,
    head_ref, skip_ref, end_ref, prior_ref, values_ref, grad_ref, core_ref,
    grad_x_ref, mine_ref, theirs_ref, grad_raw_ref, taps_grad_ref, skip_grad_ref, head_grad_ref, edge_ref, start_ref,
    later_ref, local_ref, scaled_ref, grad_state_ref, inner_ref, source_ref, carry_ref, decay_ref,
):
    seg_len = proj_ref.shape[0]
    half = seg_len // 2
    turn = pl.program_id(0)

    @pl.when(turn == 0)
    def _():
        later_ref[...] = end_ref[...]
        edge_ref[...] = jnp.zeros_like(edge_ref)
        taps_grad_ref[...] = jnp.zeros_like(taps_grad_ref)
        skip_grad_ref[...] = jnp.zeros_like(skip_grad_ref)
        head_grad_ref[...] = jnp.zeros_like(head_grad_ref)

    first_segment = turn == pl.num_programs(0) - 1

    def conv_at(at, current, ahead, taps, rim):
        before = jnp.where(first_segment, rim[:, at], ahead[:, at])
        return conv_parts(current[:, at], before, taps[:, at])

    def activated(begin):
        total, _ = conv_at(pl.ds(begin, LANES), shared_ref, shared_before_ref, shared_taps_ref, shared_rim_ref)
        return total * jax.nn.sigmoid(total)

    b_values = activated(0)
    c_values = activated(STATE)
    b_low, c_low, c_turned = b_values.astype(bf16), c_values.astype(bf16), c_values.T.astype(bf16)
    shifted, step, log_decay, sums = step_terms(shared_ref[:, 2 * STATE :], head_ref, seg_len)
    sums_turned = sums.T
    scores = dot(b_low, c_low, ((1,), (1,)))
    kept = lax.broadcasted_iota(jnp.int32, (half, half), 0) <= lax.broadcasted_iota(jnp.int32, (half, half), 1)
    first_scores = jnp.where(kept, scores[:half, :half], 0.0)
    later_scores = scores[:half, half:]
    second_scores = jnp.where(kept, scores[half:, half:], 0.0)
    low = low_half((seg_len, LANES))
    first_grad, later_grad, second_grad = 0.0, 0.0, 0.0

    pairs = grad_ref.shape[1] // LANES
    for pair in range(pairs):
        at = columns_of(pair)
        total, seen = conv_at(at, proj_ref, before_ref, taps_ref, rim_ref)
        sigmoid = jax.nn.sigmoid(total)
        x_values = total * sigmoid
        x_low = x_values.astype(bf16)
        x_wide = x_low.astype(f32)
        sums_pair = pair_columns(sums, group * pairs + pair, low)
        step_pair = pair_columns(step, group * pairs + pair, low)
        last_pair = sums_pair[seg_len - 1 :]
        gap = jnp.exp2(last_pair - sums_pair)
        scaled_ref[:, at] = (gap * step_pair * x_wide).astype(bf16)
        grad_values = grad_ref[:, at]
        grad_state_ref[:, at] = (grad_values * jnp.exp2(sums_pair)).astype(bf16)
        later = later_ref[:, at]
        later_low = later.astype(bf16)
        local_ref[:, at] = later_low
        prior = prior_ref[0, :, at]
        decay_ref[:, at] = jnp.broadcast_to(
            jnp.sum(later * prior.astype(f32), axis=0, keepdims=True), (8, LANES)
        )
        grad_prior = dot(c_turned, grad_state_ref[:, at], ((1,), (0,)))
        later_ref[:, at] = jnp.exp2(last_pair) * later + grad_prior
        grad_scaled = dot(b_low, later_low, ((1,), (0,)))
        stepped = (step_pair * x_wide).astype(bf16)
        early, late = 0.0, 0.0
        for side in range(2):
            head = 2 * (group * pairs + pair) + side
            grad_low = jnp.where(low if side == 0 else ~low, grad_values, 0.0).astype(bf16)
            at_source = jnp.broadcast_to(sums[:, head : head + 1], (seg_len, half))
            at_token = sums_turned[head : head + 1]
            grad_weights = dot(stepped, grad_low, ((1,), (1,)))
            first = jnp.exp2(jnp.minimum(at_token[:, :half] - at_source[:half], 0.0))
            after = jnp.exp2(at_token[:, half:] - at_source[:half])
            second = jnp.exp2(jnp.minimum(at_token[:, half:] - at_source[half:], 0.0))
            first_grad = first_grad + first * grad_weights[:half, :half]
            later_grad = later_grad + after * grad_weights[:half, half:]
            second_grad = second_grad + second * grad_weights[half:, half:]
            upper = jnp.concatenate([first * first_scores, after * later_scores], axis=1).astype(bf16)
            early = early + dot(upper, grad_low, ((1,), (0,)))
            late = late + dot((second * second_scores).astype(bf16), grad_low[half:], ((1,), (0,)))
        inner = jnp.concatenate([early, late], axis=0)
        skip = skip_ref[:, at]
        skip_grad_ref[:, at] += jnp.sum(grad_values * x_values, axis=0, keepdims=True)
        inner_ref[:, at] = grad_values * (values_ref[:, at] - skip * x_values)
        source_ref[:, at] = x_wide * inner
        carry_ref[:, at] = x_wide * grad_scaled
        grad_x = skip * grad_values + step_pair * (inner + gap * grad_scaled)
        grad_total = grad_x * (sigmoid * (1.0 + total * (1.0 - sigmoid)))
        for k in range(CONV):
            taps_grad_ref[k : k + 1, at] += jnp.sum(grad_total * seen[k], axis=0, keepdims=True)
        taps_grad_ref[CONV : CONV + 1, at] += jnp.sum(grad_total, axis=0, keepdims=True)
        extended = jnp.concatenate([grad_total, edge_ref[:, at]], axis=0)
        edge_ref[:, at] = grad_total[:8]
        taps = taps_ref[:, at]
        grad_conv = taps[CONV - 1 : CONV] * grad_total
        for k in range(CONV - 1):
            grad_conv = grad_conv + taps[k : k + 1] * extended[CONV - 1 - k : CONV - 1 - k + seg_len]
        grad_x_ref[:, at] = grad_conv.astype(bf16)

    width = grad_ref.shape[1]
    channel = lax.broadcasted_iota(jnp.int32, (width, LANES), 0) // HEADDIM + group * width // HEADDIM
    heads = jnp.where(channel == lax.broadcasted_iota(jnp.int32, (width, LANES), 1), 1.0, 0.0).astype(bf16)
    tail = jnp.exp2(sums[seg_len - 1 :] - sums)
    source_grad = split_dot(source_ref[...], heads)
    step_grad = source_grad + tail * split_dot(carry_ref[...], heads)
    used = step * step_grad
    sum_grad = split_dot(inner_ref[...], heads) - used
    at_last = jnp.sum(used - step * source_grad, axis=0, keepdims=True)
    at_last = at_last + split_dot(decay_ref[...], heads)[:1] * jnp.exp2(sums[seg_len - 1 :])
    is_last = lax.broadcasted_iota(jnp.int32, (seg_len, LANES), 0) == seg_len - 1
    sum_grad = sum_grad + jnp.where(is_last, at_last, 0.0)
    at_or_after = lax.broadcasted_iota(jnp.int32, (seg_len, seg_len), 0) <= lax.broadcasted_iota(
        jnp.int32, (seg_len, seg_len), 1
    )
    log_grad = lax.dot_general(
        jnp.where(at_or_after, 1.0, 0.0), sum_grad, (((1,), (0,)), ((), ())),
        precision=lax.Precision.HIGHEST, preferred_element_type=f32,
    )
    grad_raw = (step_grad + head_ref[0:1] * log_grad) * jax.nn.sigmoid(shifted)
    grad_raw_ref[...] = grad_raw
    head_grad_ref[CONV + 1 : CONV + 2] += jnp.sum(log_grad * log_decay, axis=0, keepdims=True)
    head_grad_ref[CONV + 2 : CONV + 3] += jnp.sum(grad_raw, axis=0, keepdims=True)

    first_low = jnp.where(kept, first_grad, 0.0)
    second_low = jnp.where(kept, second_grad, 0.0)
    grad_scores = jnp.concatenate(
        [
            jnp.concatenate([first_low, later_grad], axis=1),
            jnp.concatenate([jnp.zeros_like(first_low), second_low], axis=1),
        ],
        axis=0,
    )
    start_ref[...] = later_ref[...]
    grad_b = dot(scaled_ref[...], local_ref[...], ((1,), (1,))) + dot(
        grad_scores.astype(bf16), c_low, ((1,), (0,))
    )
    grad_c = dot(grad_state_ref[...], prior_ref[0], ((1,), (1,))) + dot(
        grad_scores.T.astype(bf16), b_low, ((1,), (0,))
    )
    first = core_ref[0] == 0
    mine_ref[...] = jnp.where(first, grad_b, grad_c)
    theirs_ref[...] = jnp.where(first, grad_c, grad_b)


GROUPS = 1


def scan_backward(group, core, proj, taps, head, skip, rim, end, prior, values, grad_values, seg_len):
    length = proj.shape[0]
    segs = length // seg_len
    width, shared = HALF // GROUPS, proj.shape[1] - HALF
    back = lambda width, at=0: pl.BlockSpec((seg_len, width), lambda i: (segs - 1 - i, at))
    row_ahead = lambda i: jnp.maximum((segs - 1 - i) * (seg_len // 8) - 1, 0)
    ahead = lambda width, at: pl.BlockSpec((8, width), lambda i: (row_ahead(i), at))
    column = lambda rows, width, at: pl.BlockSpec((rows, width), lambda i: (0, at))
    both = HALF // shared
    return pl.pallas_call(
        lambda *refs: backward_kernel(group, *refs),
        grid=(segs,),
        out_shape=(
            jax.ShapeDtypeStruct((length, width), bf16),
            jax.ShapeDtypeStruct((length, STATE), f32),
            jax.ShapeDtypeStruct((length, STATE), f32),
            jax.ShapeDtypeStruct((length, LANES), f32),
            jax.ShapeDtypeStruct((8, width), f32),
            jax.ShapeDtypeStruct((1, width), f32),
            jax.ShapeDtypeStruct((8, LANES), f32),
            jax.ShapeDtypeStruct((8, width), f32),
            jax.ShapeDtypeStruct((STATE, width), f32),
        ),
        in_specs=[
            back(width, group),
            ahead(width, group),
            column(8, width, group),
            column(8, width, group),
            back(shared, both),
            ahead(shared, both),
            column(8, shared, both),
            column(8, shared, both),
            full_block((8, LANES)),
            column(1, width, group),
            column(STATE, width, group),
            pl.BlockSpec((1, STATE, width), lambda i: (segs - 1 - i, 0, group)),
            back(width, group),
            back(width, group),
            pl.BlockSpec(memory_space=pltpu.SMEM),
        ],
        out_specs=(
            back(width),
            back(STATE),
            back(STATE),
            back(LANES),
            full_block((8, width)),
            full_block((1, width)),
            full_block((8, LANES)),
            full_block((8, width)),
            full_block((STATE, width)),
        ),
        scratch_shapes=[
            pltpu.VMEM((STATE, width), f32),
            pltpu.VMEM((STATE, width), bf16),
            pltpu.VMEM((seg_len, width), bf16),
            pltpu.VMEM((seg_len, width), bf16),
            pltpu.VMEM((seg_len, width), f32),
            pltpu.VMEM((seg_len, width), f32),
            pltpu.VMEM((seg_len, width), f32),
            pltpu.VMEM((8, width), f32),
        ],
        compiler_params=pltpu.CompilerParams(
            dimension_semantics=("arbitrary",), vmem_limit_bytes=VMEM_LIMIT
        ),
        cost_estimate=LIGHT,
    )(
        proj, proj, taps, rim, proj, proj, taps, rim, head, skip, end, prior, values, grad_values,
        core.reshape(1).astype(jnp.int32),
    )


def half_kernel(transposed, count, core_ref, *refs):
    inputs, mine_ref, theirs_ref = refs[: 2 * count], refs[-2], refs[-1]
    total = refs[2 * count][...] if len(refs) > 2 * count + 2 else 0.0
    for left, right in zip(inputs[:count], inputs[count:]):
        total = total + dot(left[...], right[...], ((1,), (1 if transposed else 0,)))
    own = lax.rem(pl.program_id(0), 2) == core_ref[0]

    @pl.when(own)
    def _():
        mine_ref[0] = total

    @pl.when(jnp.logical_not(own))
    def _():
        theirs_ref[0] = total.astype(bf16)


def half_products(core, terms, seg_len, width, transposed, base=()):
    length = terms[0][0].shape[0]
    left = [pl.BlockSpec((seg_len, array.shape[1]), lambda i, core: (i, 0)) for array, _, _ in terms]
    right = []
    for array, matrix, at in terms:
        if transposed:
            right.append(pl.BlockSpec((width, array.shape[1]), lambda i, core, at=at: (0, at(core[0]))))
        else:
            right.append(pl.BlockSpec(matrix.shape, lambda i, core: (0, 0)))
    depth = sum(array.shape[1] for array, _, _ in terms)
    mine, theirs = pl.pallas_call(
        lambda *refs: half_kernel(transposed, len(terms), *refs),
        grid_spec=pltpu.PrefetchScalarGridSpec(
            num_scalar_prefetch=1,
            grid=(length // seg_len,),
            in_specs=left + right + [pl.BlockSpec((seg_len, width), lambda i, core: (i, 0)) for _ in base],
            out_specs=[pl.BlockSpec((1, seg_len, width), lambda i, core: (i // 2, 0, 0))] * 2,
        ),
        out_shape=(
            jax.ShapeDtypeStruct((length // seg_len // 2, seg_len, width), f32),
            jax.ShapeDtypeStruct((length // seg_len // 2, seg_len, width), bf16),
        ),
        compiler_params=pltpu.CompilerParams(dimension_semantics=("arbitrary",), vmem_limit_bytes=VMEM_LIMIT),
        cost_estimate=LIGHT,
    )(core.reshape(1).astype(jnp.int32), *[array for array, _, _ in terms], *[matrix for _, matrix, _ in terms], *base)
    return mine, theirs


def shared_kernel(core_ref, proj_ref, rim_ref, taps_ref, mine_ref, other_ref, grad_ref, taps_grad_ref, edge_ref):
    total, seen = conv_parts(proj_ref[...], rim_ref[...], taps_ref[...])
    sigmoid = jax.nn.sigmoid(total)
    grad_total = mine_ref[...] + other_ref[...]
    grad_total = grad_total * (sigmoid * (1.0 + total * (1.0 - sigmoid)))
    sums = [jnp.sum(grad_total * part, axis=0, keepdims=True) for part in seen]
    sums = sums + [jnp.sum(grad_total, axis=0, keepdims=True), jnp.zeros((8 - CONV - 1, LANES), f32)]
    taps_grad_ref[...] = jnp.concatenate(sums, axis=0)
    edge_ref[...] = grad_total[:8]
    taps = taps_ref[...]
    extended = jnp.concatenate([grad_total, jnp.zeros((8, LANES), f32)], axis=0)
    grad_conv = taps[CONV - 1 : CONV] * grad_total
    for k in range(CONV - 1):
        grad_conv = grad_conv + taps[k : k + 1] * extended[CONV - 1 - k : CONV - 1 - k + grad_total.shape[0]]
    grad_ref[...] = grad_conv.astype(bf16)


def shared_backward(core, proj, rim, taps, mine, other):
    length = proj.shape[0]
    picked = lambda rows: pl.BlockSpec((rows, LANES), lambda i, core: (0, HALF // LANES + core[0]))
    whole = lambda rows: pl.BlockSpec((rows, LANES), lambda i, core: (0, 0))
    return pl.pallas_call(
        shared_kernel,
        grid_spec=pltpu.PrefetchScalarGridSpec(
            num_scalar_prefetch=1,
            grid=(1,),
            in_specs=[picked(length), picked(8), picked(8), whole(length), whole(length)],
            out_specs=(whole(length), whole(8), whole(8)),
        ),
        out_shape=(
            jax.ShapeDtypeStruct((length, LANES), bf16),
            jax.ShapeDtypeStruct((8, LANES), f32),
            jax.ShapeDtypeStruct((8, LANES), f32),
        ),
        compiler_params=pltpu.CompilerParams(vmem_limit_bytes=VMEM_LIMIT),
        cost_estimate=LIGHT,
    )(core.reshape(1).astype(jnp.int32), proj, rim, taps, mine, other)


def per_device(hidden_in, cotangent, in_proj, out_proj, conv_params, pre_gain, gated_gain, head_params):
    chips, line = lax.axis_size("chip"), lax.axis_size("seg")
    core, place = lax.axis_index("core"), lax.axis_index("seg")
    rows, model_width = in_proj.shape[0], hidden_in.shape[2]
    heads = HEADS // 2

    conv_width, gain_width = conv_params.shape[1], gated_gain.shape[0]
    used = HALF + 2 * STATE + heads
    spare = -used % LANES
    small = jnp.zeros((rows, spare), bf16)
    small = small.at[: CONV + 1, :conv_width].set(conv_params)
    small = small.at[CONV + 1, :rows].set(pre_gain)
    small = small.at[CONV + 2, :gain_width].set(gated_gain)

    def conv_side(which):
        return jnp.concatenate(
            [
                own_columns(in_proj[:, INNER : 2 * INNER], which),
                in_proj[:, 2 * INNER : INNER + XBC],
                own_columns(in_proj[:, INNER + XBC :], which),
                small,
            ],
            axis=1,
        )

    def gate_side(which):
        return own_columns(in_proj[:, :INNER], which)

    conv_swap = to_partner(conv_side(1 - core))
    conv_block = in_core_order(conv_side(core), conv_swap, core, 0)
    conv_z = gather_step(conv_block, 2)
    gate_swap = to_partner(gate_side(1 - core))
    gate_block = in_core_order(gate_side(core), gate_swap, core, 0)
    conv_z, hidden_in, gate_block = tie(conv_z, hidden_in, gate_block)
    conv_own, conv_near, conv_far = gather_plane(conv_z)
    hidden_half = whole_sequence(hidden_in, core, place)
    conv_own, conv_near, hidden_half, gate_block = tie(conv_own, conv_near, hidden_half, gate_block)
    gate_z = gather_step(gate_block, 2)
    hidden_other = to_partner(hidden_half)
    conv_far, gate_z, hidden_other = tie(conv_far, gate_z, hidden_other)
    gate_own, gate_near, gate_far = gather_plane(gate_z)
    conv_all = whole_matrix([conv_own, *conv_near, *conv_far], True)

    small_all = conv_all.reshape(chips, 2, line, rows, -1)[..., used:].astype(f32)
    taps_full = small_all[..., : CONV + 1, :conv_width].transpose(3, 0, 1, 2, 4).reshape(CONV + 1, XBC)
    taps = jnp.concatenate([own_columns(taps_full[:, :INNER], core), taps_full[:, INNER:]], axis=1)
    gain_pre = small_all[..., CONV + 1, :rows].reshape(model_width)
    gain_gate = lax.dynamic_index_in_dim(
        small_all[..., CONV + 2, :gain_width], core, axis=1, keepdims=False
    ).reshape(HALF)
    params = own_columns(head_params, core)

    seg_len = hidden_half.shape[1]
    tokens = SEGS * seg_len
    normed, normed_turned = normed_tokens(core, hidden_half, hidden_other, gain_pre, rows)
    projected = dot(normed, conv_all, ((1,), (0,)))
    projected, gate_near, out_proj = tie(projected, gate_near, out_proj)
    out_z = gather_step(out_proj, 2)

    taps = jnp.pad(taps, ((0, 8 - CONV - 1), (0, projected.shape[1] - taps.shape[1])))
    head = jnp.pad(jnp.stack([-jnp.exp(params[0]), params[1]]), ((0, 6), (0, LANES - heads)))
    skip = jnp.repeat(params[2], HEADDIM).reshape(1, HALF)
    wide = HALF + 2 * STATE
    rim = borrowed(projected[tokens - 8 :], 1)
    nothing = jnp.zeros((STATE, HALF), f32)
    values, prior, final, last = scan_forward(projected, taps, head, skip, rim, nothing, seg_len)
    if line > SEGS:
        last = jnp.sum(last.reshape(SEGS, 8, LANES)[:, 0, :heads], axis=0)
        decay = jnp.repeat(jnp.exp2(last), HEADDIM)
        begin = entering(decay, final, 1)
        values, prior, _, _ = scan_forward(projected, taps, head, skip, rim, begin, seg_len)

    values, gate_far, out_z, cotangent = tie(values, gate_far, out_z, cotangent)
    out_own, out_near, out_far = gather_plane(out_z)
    cot_half = whole_sequence(cotangent, core, place)
    gate_matrix = whole_matrix([gate_own, *gate_near, *gate_far], True)
    gate_input = dot(normed, gate_matrix, ((1,), (0,)))

    silu_gate = jax.nn.silu(gate_input)
    gated = values * silu_gate
    squares = jnp.sum(gated * gated, axis=1)
    squares_other = to_partner(squares)
    scale = lax.rsqrt((squares + squares_other) / INNER + epsilon)[:, None]
    scale, out_near = tie(scale, out_near)
    mixed, mixed_turned = mixed_tokens(gated, scale, gain_gate, seg_len)
    mixed_turned, cot_half = tie(mixed_turned, cot_half)
    cot_other = to_partner(cot_half)
    cot = in_core_order(cot_half, cot_other, core, 1)
    upstream = cot.reshape(tokens, model_width)
    by_owner = lambda grad: grad.astype(bf16).reshape(chip_dims() + (-1, grad.shape[1]))
    out_grad = by_owner(dot(mixed_turned, upstream, ((1,), (0,))))
    out_grad, out_far = tie(out_grad, out_far)
    ((out_kept, out_got),) = reduce_plane([out_grad])
    out_matrix = whole_matrix([out_own, *out_near, *out_far], False)
    branch, branch_sent = half_products(core, [(mixed, out_matrix, None)], seg_len, model_width, False)
    branch_sent, upstream = tie(branch_sent, upstream)
    branch_other = to_partner(branch_sent)
    grad_mixed = dot(upstream, out_matrix, ((1,), (1,)))
    grad_mixed, out_got_near = tie(grad_mixed, out_got[: near_count()])
    unit = gated * scale
    gain_grad = grad_mixed * gain_gate
    along = jnp.sum(gain_grad * unit, axis=1)
    along_other = to_partner(along)
    along_other, branch_other = tie(along_other, branch_other)
    hidden_out = back_to_owner(
        (hidden_half.astype(f32) + branch + branch_other.astype(f32)).astype(bf16), core, place
    )
    along = ((along + along_other) / INNER)[:, None]
    gate_gain_grad = jnp.sum(grad_mixed * unit, axis=0)
    grad_gated = scale * (gain_grad - unit * along)
    grad_values = grad_gated * silu_gate
    sigmoid = jax.nn.sigmoid(gate_input)
    grad_gate = (grad_gated * values * (sigmoid * (1.0 + gate_input * (1.0 - sigmoid)))).astype(bf16)
    gate_grad = by_owner(dot(normed_turned, grad_gate, ((1,), (0,))))
    gate_grad, grad_values, out_got_far, hidden_out = tie(gate_grad, grad_values, out_got[near_count() :], hidden_out)
    out_third = reduce_z([(out_kept, [*out_got_near, *out_got_far])])
    ((gate_kept, gate_got),) = reduce_plane([gate_grad])
    scan = lambda later: scan_backward(
        0, core, projected, taps, head, skip, rim, later, prior, values, grad_values, seg_len
    )
    if line > SEGS:
        nothing = entering(decay, scan(nothing)[-1], -1)
    back = scan(nothing)
    back, gate_got_near, out_got, grad_gate = tie(back, gate_got[: near_count()], arrivals(out_third), grad_gate)
    out_third = arrived(out_third, out_got)
    grad_x, mine, theirs, grad_raw, x_taps_grad, skip_grad, head_sums, x_edge, _ = back
    grad_x = spilled(grad_x, x_edge, taps[:, :HALF])
    other = to_partner(theirs)
    x_grad = by_owner(dot(normed_turned, grad_x, ((1,), (0,))))
    other, x_grad = tie(other, x_grad)
    grad_state, state_taps_grad, state_edge = shared_backward(core, projected, rim, taps, mine, other)
    grad_state = spilled(grad_state, state_edge, lax.dynamic_slice_in_dim(taps, HALF + core * STATE, STATE, axis=1))
    grad_raw = grad_raw.astype(bf16)
    rest_grad = by_owner(dot(normed_turned, jnp.concatenate([grad_state, grad_raw], axis=1), ((1,), (0,))))
    rest_grad, x_grad, grad_gate, grad_state, gate_got_far = tie(
        rest_grad, x_grad, grad_gate, grad_state, gate_got[near_count() :]
    )
    gate_third = reduce_z([(gate_kept, [*gate_got_near, *gate_got_far])])
    ((conv_kept, conv_got),) = reduce_plane([x_grad, rest_grad])
    base = dot(grad_gate, gate_matrix, ((1,), (1,)))
    terms = [
        (grad_x, conv_all, lambda core: 0),
        (grad_state, conv_all, lambda core: HALF // LANES + core),
        (grad_raw, conv_all, lambda core: (HALF + 2 * STATE) // LANES),
    ]
    grad_normed, sent_normed = half_products(core, terms, seg_len, model_width, True, (base,))
    row = lax.broadcasted_iota(jnp.int32, (8, 1), 0)
    small = x_taps_grad + jnp.where(row == CONV + 1, gate_gain_grad, 0.0) + jnp.where(row == CONV + 2, skip_grad, 0.0)
    small = jnp.concatenate([small, state_taps_grad + head_sums], axis=1)
    sent_normed, gate_got, conv_near, small = tie(sent_normed, arrivals(gate_third), conv_got[: near_count()], small)
    other_normed = to_partner(sent_normed)
    wide_hidden = hidden_half.astype(f32)
    hidden_scale = lax.rsqrt(jnp.mean(wide_hidden * wide_hidden, axis=-1, keepdims=True) + epsilon)
    grad_normed = (grad_normed + other_normed.astype(f32)) * gain_pre
    hidden_unit = wide_hidden * hidden_scale
    along = jnp.mean(grad_normed * hidden_unit, axis=-1, keepdims=True)
    grad_hidden = hidden_scale * (grad_normed - hidden_unit * along)
    grad_in = (cot_half.astype(f32) + grad_hidden).astype(bf16)
    grad_in = back_to_owner(grad_in, core, place)
    grad_in, conv_far = tie(grad_in, conv_got[near_count() :])
    late = reduce_z([(conv_kept, [*conv_near, *conv_far])])
    for dim in range(3):
        small = small + sum(moved(small, dim, by) for by in range(1, chip_dims()[dim]))
    small_other = to_partner(small)
    late_got, small_other = tie(arrivals(late), small_other)
    out_share = reduce_end(out_third)
    paired = lambda share: share.astype(bf16).reshape(2, rows, -1)
    gate_share, conv_share = paired(reduce_end(arrived(gate_third, gate_got))), paired(reduce_end(arrived(late, late_got)))

    def mine_and_partner(share):
        keep = lax.dynamic_index_in_dim(share, core, axis=0, keepdims=False)
        give = lax.dynamic_index_in_dim(share, 1 - core, axis=0, keepdims=False)
        return keep, to_partner(give)

    both = in_core_order(small, small_other, core, 0)
    natural = lambda array, width: array.reshape(2, -1, chips, width).transpose(1, 2, 0, 3).reshape(-1, 2 * chips * width)
    device = (lax.axis_index("chip") * 2 + core) * line + place
    columns = natural(both[:, :, :HALF], HALF // chips)
    taps_all = jnp.concatenate([columns, both[0, :, HALF:], both[1, :, HALF:]], axis=1)[: CONV + 1]
    taps_share = lax.dynamic_slice_in_dim(taps_all, device * conv_width, conv_width, axis=1)
    gain_share = lax.dynamic_slice_in_dim(columns[CONV + 1], device * gain_width, gain_width, axis=0)
    head_total = jnp.concatenate(
        [
            natural(both[:, CONV + 1 : CONV + 3, HALF : HALF + heads], heads // chips),
            jnp.sum(columns[CONV + 2].reshape(1, HEADS, HEADDIM), axis=2),
        ]
    )

    def interleave(mine, theirs):
        width = mine.shape[1] // chips
        both = in_core_order(mine.reshape(rows, chips, width), theirs.reshape(rows, chips, width), core, 2)
        return both.reshape(rows, -1)

    keep_gate, got_gate = mine_and_partner(gate_share)
    keep, got = mine_and_partner(conv_share)
    state_end = HALF + STATE
    in_share = jnp.concatenate(
        [
            interleave(keep_gate, got_gate),
            interleave(keep[:, :HALF], got[:, :HALF]),
            in_core_order(keep[:, HALF:state_end], got[:, HALF:state_end], core, 1).reshape(rows, -1),
            interleave(keep[:, state_end : state_end + heads], got[:, state_end : state_end + heads]),
        ],
        axis=1,
    ).astype(f32)
    pre_share = jnp.sum(in_proj.astype(f32) * in_share, axis=1) / pre_gain.astype(f32)
    return (hidden_out, grad_in, in_share, out_share, taps_share, pre_share, gain_share, head_total)


def solution(mesh):
    devices = mesh.devices
    cores = Mesh(devices.reshape(devices.shape[0] // 2, 2, devices.shape[1]), ("chip", "core", "seg"))
    dp, both = ("chip", "core"), ("chip", "core", "seg")
    tokens = P(dp, "seg", None)
    return jax.shard_map(
        per_device,
        mesh=cores,
        in_specs=(tokens, tokens, P(both, None), P(both, None), P(None, both), P(both), P(both), P()),
        out_specs=(tokens, tokens, P(both, None), P(both, None), P(None, both), P(both), P(both), P()),
        check_vma=False,
    )
```

```python
import jax
import jax.numpy as jnp
from jax import lax
from jax.experimental import pallas as pl
from jax.experimental.pallas import tpu as pltpu
from jax.sharding import Mesh
from jax.sharding import PartitionSpec as P

HEADS = 48
HEADDIM = 64
STATE = 128
CONV = 4
INNER = 3072
XBC = 3328
HALF = INNER // 2
LANES = 128
SEGS = 4
LIGHT = pl.CostEstimate(flops=1024, bytes_accessed=1024, transcendentals=0)
VMEM_LIMIT = 48 * 1024 * 1024
LOG2E = 1.4426950408889634

epsilon = 1e-05
f32 = jnp.float32
bf16 = jnp.bfloat16


def own_columns(array, core):
    chips = lax.axis_size("chip")
    width = array.shape[-1] // (2 * chips)
    parted = array.reshape(array.shape[:-1] + (chips, 2, width))
    picked = lax.dynamic_index_in_dim(parted, core, axis=parted.ndim - 2, keepdims=False)
    return picked.reshape(array.shape[:-1] + (chips * width,))


def to_partner(array):
    return lax.ppermute(array, "core", [(0, 1), (1, 0)])


def in_core_order(mine, theirs, core, axis):
    first = jnp.where(core == 0, mine, theirs)
    second = jnp.where(core == 0, theirs, mine)
    return jnp.stack([first, second], axis=axis)


def chip_dims():
    return (lax.axis_size("chip") // 2, 2, lax.axis_size("seg"))


def chip_place():
    chip = lax.axis_index("chip")
    return (chip // 2, chip % 2, lax.axis_index("seg"))


def moved(array, dim, by):
    sizes = chip_dims()
    index = lambda at: (at[0] * sizes[1] + at[1]) * sizes[2] + at[2]
    pairs = []
    for a in range(sizes[0]):
        for b in range(sizes[1]):
            for z in range(sizes[2]):
                to = [a, b, z]
                to[dim] = (to[dim] + by) % sizes[dim]
                pairs.append((index((a, b, z)), index(to)))
    return lax.ppermute(array, ("chip", "seg"), pairs)


def tie(*values):
    return lax.optimization_barrier(values)


def gather_step(data, dim):
    return [data] + [moved(data, dim, by) for by in range(1, chip_dims()[dim])]


def plane_steps():
    a, b, _ = chip_dims()
    steps = [(at // b, at % b) for at in range(1, a * b)]
    return sorted(steps, key=lambda by: bool(by[0] and by[1]))


def near_steps():
    a, b, _ = chip_dims()
    return plane_steps()[: a + b - 2]


def far_steps():
    a, b, _ = chip_dims()
    return plane_steps()[a + b - 2 :]


def moved_plane(array, by_a, by_b):
    a, b, z = chip_dims()
    pairs = [
        ((at_a * b + at_b) * z + at_z, ((at_a + by_a) % a * b + (at_b + by_b) % b) * z + at_z)
        for at_a in range(a)
        for at_b in range(b)
        for at_z in range(z)
    ]
    return lax.ppermute(array, ("chip", "seg"), pairs)


def gather_plane(data, steps):
    return [moved_plane(data, *by) for by in steps]


def placed_kernel(plan, place_ref, *refs):
    sources, target, sems = refs[:-2], refs[-2], refs[-1]
    copies = []
    for source, lead, at, paired in plan:
        spot = [lax.rem(place_ref[dim] + (size - back), size) for dim, (back, size) in enumerate(at)]
        to = target.at[spot[0], spot[1], :, spot[2]] if paired else target.at[spot[0], spot[1], spot[2]]
        copies.append(pltpu.make_async_copy(sources[source].at[lead], to, sems.at[len(copies)]))
    for copy in copies:
        copy.start()
    for copy in copies:
        copy.wait()


def whole_matrix(gathered, paired):
    a, b, z = chip_dims()
    plan = [
        (source, back, ((by[0], a), (by[1], b), (back, z)), paired)
        for source, by in enumerate([(0, 0)] + plane_steps())
        for back in range(z)
    ]
    block = gathered[0].shape[1:]
    shape = (a, b, 2, z) + block[1:] if paired else (a, b, z) + block
    anywhere = pl.BlockSpec(memory_space=pl.ANY)
    whole = pl.pallas_call(
        lambda *refs: placed_kernel(plan, *refs),
        out_shape=jax.ShapeDtypeStruct(shape, bf16),
        in_specs=[pl.BlockSpec(memory_space=pltpu.SMEM)] + [anywhere] * len(gathered),
        out_specs=pl.BlockSpec(memory_space=pltpu.VMEM),
        scratch_shapes=[pltpu.SemaphoreType.DMA((len(plan),))],
        compiler_params=pltpu.CompilerParams(vmem_limit_bytes=VMEM_LIMIT),
        cost_estimate=LIGHT,
    )(jnp.stack(chip_place()).astype(jnp.int32), *gathered)
    return whole.reshape(-1, shape[-1])


def total(terms):
    result = terms[0].astype(f32)
    for term in terms[1:]:
        result = result + term.astype(f32)
    return result


def reduce_send(terms, axis, dim, wire):
    place, size = chip_place()[dim], chip_dims()[dim]
    pick = lambda at: [lax.dynamic_index_in_dim(term, at, axis=axis, keepdims=False) for term in terms]
    received = [moved(total(pick((place + by) % size)).astype(wire), dim, by) for by in range(1, size)]
    return pick(place), received


def plane_part(partials, by_a, by_b):
    (at_a, at_b, _), (a, b, _) = chip_place(), chip_dims()
    chip = (at_a + by_a) % a * b + (at_b + by_b) % b
    flat = [partial.reshape((a * b,) + partial.shape[2:]) for partial in partials]
    return jnp.concatenate([lax.dynamic_index_in_dim(array, chip, axis=0, keepdims=False) for array in flat], axis=-1)


def reduce_plane(partials, steps):
    return [moved_plane(plane_part(partials, *by), *by) for by in steps]


def reduce_z(firsts):
    joined = jnp.concatenate([total(kept + received) for kept, received in firsts], axis=-1)
    return [reduce_send([joined], 0, 2, bf16)]


def reduce_end(third):
    return total(third[0][0] + third[0][1])


def arrivals(parts):
    return [received for _, received in parts]


def arrived(parts, received):
    return [(kept, new) for (kept, _), new in zip(parts, received)]


def line_perm(turn, back):
    line = lax.axis_size("seg")
    parts = line // SEGS
    pairs = []
    for core in range(2):
        for place in range(line):
            half, odd = divmod(place % SEGS, 2)
            source = core * line + place
            target = odd * line + (2 * core + (half ^ turn)) * parts + place // SEGS
            pairs.append((target, source) if back else (source, target))
    return pairs


def swapped(pair, turn):
    return [jnp.where(turn == 0, pair[0], pair[1]), jnp.where(turn == 0, pair[1], pair[0])]


def whole_sequence(array, core, place):
    parts = lax.axis_size("seg") // SEGS
    pieces = swapped([array[0], array[1]], (place % SEGS) // 2)
    got = [lax.ppermute(piece, ("core", "seg"), line_perm(turn, False)) for turn, piece in enumerate(pieces)]
    return jnp.stack(swapped(got, (place // parts) % 2))


def back_to_owner(ordered, core, place):
    parts = lax.axis_size("seg") // SEGS
    pieces = swapped([ordered[0], ordered[1]], (place // parts) % 2)
    got = [lax.ppermute(piece, ("core", "seg"), line_perm(turn, True)) for turn, piece in enumerate(pieces)]
    return jnp.stack(swapped(got, (place % SEGS) // 2))


def part_pairs(step):
    line = lax.axis_size("seg")
    parts = line // SEGS
    return [(i, i + step) for i in range(line) if 0 <= i + step < line and i // parts == (i + step) // parts]


def entering(decay, state, step):
    parts = lax.axis_size("seg") // SEGS
    total = jnp.zeros_like(state)
    for _ in range(parts - 1):
        total = lax.ppermute(decay * total + state, "seg", part_pairs(step))
    return total


def borrowed(array, step):
    parts = lax.axis_size("seg") // SEGS
    if parts == 1:
        return jnp.zeros_like(array)
    return lax.ppermute(array, "seg", part_pairs(step))


def spilled(grad, edge, taps):
    if lax.axis_size("seg") == SEGS:
        return grad
    edge = borrowed(edge, -1)
    spill = jnp.stack(
        [
            sum(taps[k] * edge[CONV - 1 - k - early] for k in range(CONV - early))
            for early in range(CONV - 1, 0, -1)
        ]
    )
    at = grad.shape[0] - CONV + 1
    return grad.at[at:].set((grad[at:].astype(f32) + spill).astype(bf16))


def dot(a, b, contract):
    return lax.dot_general(a, b, (contract, ((), ())), preferred_element_type=f32)


def normed_kernel(slabs, core_ref, mine_ref, other_ref, gain_ref, normed_ref, turned_ref):
    own = lax.rem(pl.program_id(0), 2) == core_ref[0]
    hidden = jnp.where(own, mine_ref[0], other_ref[0]).astype(f32)
    scale = lax.rsqrt(jnp.mean(hidden * hidden, axis=1, keepdims=True) + epsilon)
    normed = hidden * scale * gain_ref[...]
    normed_ref[...] = normed.astype(bf16)
    turned = normed.T.astype(bf16)
    for to, at, size in slabs:
        turned_ref[to : to + size] = turned[at : at + size]


def normed_tokens(core, mine, other, gain, rows):
    segs, seg_len, width = 2 * mine.shape[0], mine.shape[1], mine.shape[2]
    a, b, z = chip_dims()
    group = 2 * z * rows
    inside = rows % 16 == 0
    slabs = [(0, 0, width)]
    if inside:
        slabs = [
            (chip * group + (at * 2 + core_at) * rows, chip * group + (core_at * z + at) * rows, rows)
            for chip in range(a * b)
            for core_at in range(2)
            for at in range(z)
        ]
    normed, turned = pl.pallas_call(
        lambda *refs: normed_kernel(slabs, *refs),
        grid_spec=pltpu.PrefetchScalarGridSpec(
            num_scalar_prefetch=1,
            grid=(segs,),
            in_specs=[
                pl.BlockSpec((1, seg_len, width), lambda i, core: (i // 2, 0, 0)),
                pl.BlockSpec((1, seg_len, width), lambda i, core: (i // 2, 0, 0)),
                pl.BlockSpec((1, width), lambda i, core: (0, 0)),
            ],
            out_specs=(
                pl.BlockSpec((seg_len, width), lambda i, core: (i, 0)),
                pl.BlockSpec((width, seg_len), lambda i, core: (0, i)),
            ),
        ),
        out_shape=(
            jax.ShapeDtypeStruct((segs * seg_len, width), bf16),
            jax.ShapeDtypeStruct((width, segs * seg_len), bf16),
        ),
        compiler_params=pltpu.CompilerParams(dimension_semantics=("arbitrary",), vmem_limit_bytes=VMEM_LIMIT),
        cost_estimate=LIGHT,
    )(core.reshape(1).astype(jnp.int32), mine, other, gain.reshape(1, width))
    if not inside:
        turned = turned.reshape(a, b, 2, z, rows, -1).transpose(0, 1, 3, 2, 4, 5).reshape(turned.shape)
    return normed, turned


def mixed_kernel(gated_ref, scale_ref, gain_ref, mixed_ref, turned_ref):
    mixed = gated_ref[...] * scale_ref[...] * gain_ref[...]
    mixed_ref[...] = mixed.astype(bf16)
    turned_ref[...] = mixed.T.astype(bf16)


def mixed_tokens(gated, scale, gain, seg_len):
    length, width = gated.shape
    return pl.pallas_call(
        mixed_kernel,
        grid=(length // seg_len,),
        in_specs=[
            pl.BlockSpec((seg_len, width), lambda i: (i, 0)),
            pl.BlockSpec((seg_len, 1), lambda i: (i, 0)),
            pl.BlockSpec((1, width), lambda i: (0, 0)),
        ],
        out_specs=(
            pl.BlockSpec((seg_len, width), lambda i: (i, 0)),
            pl.BlockSpec((width, seg_len), lambda i: (0, i)),
        ),
        out_shape=(
            jax.ShapeDtypeStruct((length, width), bf16),
            jax.ShapeDtypeStruct((width, length), bf16),
        ),
        compiler_params=pltpu.CompilerParams(dimension_semantics=("arbitrary",), vmem_limit_bytes=VMEM_LIMIT),
        cost_estimate=LIGHT,
    )(gated, scale, gain.reshape(1, width))


def columns_of(pair):
    return pl.ds(pair * LANES, LANES)


def low_half(shape):
    return lax.broadcasted_iota(jnp.int32, shape, len(shape) - 1) < HEADDIM


def pair_columns(array, pair, low):
    rows = array.shape[0]
    first = jnp.broadcast_to(array[:, 2 * pair : 2 * pair + 1], (rows, LANES))
    second = jnp.broadcast_to(array[:, 2 * pair + 1 : 2 * pair + 2], (rows, LANES))
    return jnp.where(low, first, second)


def conv_parts(current, before, taps):
    rows = current.shape[0]
    padded = jnp.concatenate([before, current], axis=0)
    seen = [padded[8 - CONV + 1 + k : 8 - CONV + 1 + k + rows] for k in range(CONV - 1)] + [current]
    total = taps[CONV : CONV + 1]
    for k in range(CONV):
        total = total + taps[k : k + 1] * seen[k]
    return total, seen


def step_terms(raw, head, seg_len):
    shifted = raw + head[1:2]
    step = jnp.maximum(shifted, 0.0) + jnp.log1p(jnp.exp(-jnp.abs(shifted)))
    log_decay = step * head[0:1]
    at_or_before = lax.broadcasted_iota(jnp.int32, (seg_len, seg_len), 0) >= lax.broadcasted_iota(
        jnp.int32, (seg_len, seg_len), 1
    )
    sums = lax.dot_general(
        jnp.where(at_or_before, 1.0, 0.0), log_decay, (((1,), (0,)), ((), ())),
        precision=lax.Precision.HIGHEST, preferred_element_type=f32,
    )
    return shifted, step, log_decay, sums * LOG2E


def forward_kernel(
    proj_ref, taps_ref, head_ref, skip_ref, rim_ref, init_ref,
    values_ref, prior_ref, final_ref, last_ref, state_ref, tail_ref,
):
    seg_len = proj_ref.shape[0]
    half = seg_len // 2

    @pl.when(pl.program_id(0) == 0)
    def _():
        state_ref[...] = init_ref[...]
        tail_ref[...] = rim_ref[...]

    def activated(begin):
        at = pl.ds(begin, LANES)
        total, _ = conv_parts(proj_ref[:, at], tail_ref[:, at], taps_ref[:, at])
        return total * jax.nn.sigmoid(total)

    b_low = activated(HALF).astype(bf16)
    b_turned = activated(HALF).T.astype(bf16)
    c_low = activated(HALF + STATE).astype(bf16)
    _, step, _, sums = step_terms(proj_ref[:, HALF + 2 * STATE :], head_ref, seg_len)
    sums_turned, step_turned = sums.T, step.T
    scores = dot(c_low, b_low, ((1,), (1,)))
    kept = lax.broadcasted_iota(jnp.int32, (half, half), 0) >= lax.broadcasted_iota(jnp.int32, (half, half), 1)
    first_scores = jnp.where(kept, scores[:half, :half], 0.0)
    later_scores = scores[half:, :half]
    second_scores = jnp.where(kept, scores[half:, half:], 0.0)
    low = low_half((seg_len, LANES))
    last_ref[...] = jnp.broadcast_to(sums[seg_len - 1 :], last_ref.shape)

    for pair in range(HEADS // 4):
        at = columns_of(pair)
        x_values = activated(pair * LANES)
        x_low = x_values.astype(bf16)
        sums_pair = pair_columns(sums, pair, low)
        last_pair = sums_pair[seg_len - 1 :]
        carry = jnp.exp2(last_pair - sums_pair) * pair_columns(step, pair, low)
        scaled_x = (carry * x_low.astype(f32)).astype(bf16)
        prior = state_ref[:, at]
        prior_low = prior.astype(bf16)
        prior_ref[0, :, at] = prior_low
        from_state = jnp.exp2(sums_pair) * dot(c_low, prior_low, ((1,), (0,)))
        state_ref[:, at] = jnp.exp2(last_pair) * prior + dot(b_turned, scaled_x, ((1,), (0,)))
        early, late = 0.0, 0.0
        for side in range(2):
            head = 2 * pair + side
            x_side = jnp.where(low if side == 0 else ~low, x_values, 0.0).astype(bf16)
            at_token = jnp.broadcast_to(sums[:, head : head + 1], (seg_len, half))
            at_source, source_step = sums_turned[head : head + 1], step_turned[head : head + 1]
            first = jnp.exp2(jnp.minimum(at_token[:half] - at_source[:, :half], 0.0)) * first_scores
            first = (first * source_step[:, :half]).astype(bf16)
            later = jnp.exp2(at_token[half:] - at_source[:, :half]) * later_scores
            later = (later * source_step[:, :half]).astype(bf16)
            second = jnp.exp2(jnp.minimum(at_token[half:] - at_source[:, half:], 0.0)) * second_scores
            second = (second * source_step[:, half:]).astype(bf16)
            early = early + dot(first, x_side[:half], ((1,), (0,)))
            late = late + dot(jnp.concatenate([later, second], axis=1), x_side, ((1,), (0,)))
        intra = jnp.concatenate([early, late], axis=0)
        values_ref[:, at] = intra + from_state + skip_ref[:, at] * x_values

    tail_ref[...] = proj_ref[seg_len - 8 :, : HALF + 2 * STATE]
    final_ref[...] = state_ref[...]


def full_block(shape):
    return pl.BlockSpec(shape, lambda *_: (0,) * len(shape))


def scan_forward(proj, taps, head, skip, rim, init, seg_len):
    segs = proj.shape[0] // seg_len
    wide = HALF + 2 * STATE
    return pl.pallas_call(
        forward_kernel,
        grid=(segs,),
        out_shape=(
            jax.ShapeDtypeStruct((proj.shape[0], HALF), f32),
            jax.ShapeDtypeStruct((segs, STATE, HALF), bf16),
            jax.ShapeDtypeStruct((STATE, HALF), f32),
            jax.ShapeDtypeStruct((segs * 8, LANES), f32),
        ),
        in_specs=[
            pl.BlockSpec((seg_len, proj.shape[1]), lambda i: (i, 0)),
            full_block((8, wide)),
            full_block((8, LANES)),
            full_block((1, HALF)),
            full_block((8, wide)),
            full_block((STATE, HALF)),
        ],
        out_specs=(
            pl.BlockSpec((seg_len, HALF), lambda i: (i, 0)),
            pl.BlockSpec((1, STATE, HALF), lambda i: (i, 0, 0)),
            full_block((STATE, HALF)),
            pl.BlockSpec((8, LANES), lambda i: (i, 0)),
        ),
        scratch_shapes=[pltpu.VMEM((STATE, HALF), f32), pltpu.VMEM((8, wide), f32)],
        compiler_params=pltpu.CompilerParams(
            dimension_semantics=("arbitrary",), vmem_limit_bytes=VMEM_LIMIT
        ),
        cost_estimate=LIGHT,
    )(proj, taps, head, skip, rim, init)


def split_dot(array, other):
    high = array.astype(bf16)
    rest = (array - high.astype(f32)).astype(bf16)
    return dot(high, other, ((1,), (0,))) + dot(rest, other, ((1,), (0,)))


def backward_kernel(
    group, proj_ref, before_ref, taps_ref, rim_ref, shared_ref, shared_before_ref, shared_taps_ref, shared_rim_ref,
    head_ref, skip_ref, end_ref, prior_ref, values_ref, grad_ref, core_ref,
    grad_x_ref, mine_ref, theirs_ref, grad_raw_ref, taps_grad_ref, skip_grad_ref, head_grad_ref, edge_ref, start_ref,
    later_ref, local_ref, scaled_ref, grad_state_ref, inner_ref, source_ref, carry_ref, decay_ref,
):
    seg_len = proj_ref.shape[0]
    half = seg_len // 2
    turn = pl.program_id(0)

    @pl.when(turn == 0)
    def _():
        later_ref[...] = end_ref[...]
        edge_ref[...] = jnp.zeros_like(edge_ref)
        taps_grad_ref[...] = jnp.zeros_like(taps_grad_ref)
        skip_grad_ref[...] = jnp.zeros_like(skip_grad_ref)
        head_grad_ref[...] = jnp.zeros_like(head_grad_ref)

    first_segment = turn == pl.num_programs(0) - 1

    def conv_at(at, current, ahead, taps, rim):
        before = jnp.where(first_segment, rim[:, at], ahead[:, at])
        return conv_parts(current[:, at], before, taps[:, at])

    def activated(begin):
        total, _ = conv_at(pl.ds(begin, LANES), shared_ref, shared_before_ref, shared_taps_ref, shared_rim_ref)
        return total * jax.nn.sigmoid(total)

    b_values = activated(0)
    c_values = activated(STATE)
    b_low, c_low, c_turned = b_values.astype(bf16), c_values.astype(bf16), c_values.T.astype(bf16)
    shifted, step, log_decay, sums = step_terms(shared_ref[:, 2 * STATE :], head_ref, seg_len)
    sums_turned = sums.T
    scores = dot(b_low, c_low, ((1,), (1,)))
    kept = lax.broadcasted_iota(jnp.int32, (half, half), 0) <= lax.broadcasted_iota(jnp.int32, (half, half), 1)
    first_scores = jnp.where(kept, scores[:half, :half], 0.0)
    later_scores = scores[:half, half:]
    second_scores = jnp.where(kept, scores[half:, half:], 0.0)
    low = low_half((seg_len, LANES))
    first_grad, later_grad, second_grad = 0.0, 0.0, 0.0

    pairs = grad_ref.shape[1] // LANES
    for pair in range(pairs):
        at = columns_of(pair)
        total, seen = conv_at(at, proj_ref, before_ref, taps_ref, rim_ref)
        sigmoid = jax.nn.sigmoid(total)
        x_values = total * sigmoid
        x_low = x_values.astype(bf16)
        x_wide = x_low.astype(f32)
        sums_pair = pair_columns(sums, group * pairs + pair, low)
        step_pair = pair_columns(step, group * pairs + pair, low)
        last_pair = sums_pair[seg_len - 1 :]
        gap = jnp.exp2(last_pair - sums_pair)
        scaled_ref[:, at] = (gap * step_pair * x_wide).astype(bf16)
        grad_values = grad_ref[:, at]
        grad_state_ref[:, at] = (grad_values * jnp.exp2(sums_pair)).astype(bf16)
        later = later_ref[:, at]
        later_low = later.astype(bf16)
        local_ref[:, at] = later_low
        prior = prior_ref[0, :, at]
        decay_ref[:, at] = jnp.broadcast_to(
            jnp.sum(later * prior.astype(f32), axis=0, keepdims=True), (8, LANES)
        )
        grad_prior = dot(c_turned, grad_state_ref[:, at], ((1,), (0,)))
        later_ref[:, at] = jnp.exp2(last_pair) * later + grad_prior
        grad_scaled = dot(b_low, later_low, ((1,), (0,)))
        stepped = (step_pair * x_wide).astype(bf16)
        early, late = 0.0, 0.0
        for side in range(2):
            head = 2 * (group * pairs + pair) + side
            grad_low = jnp.where(low if side == 0 else ~low, grad_values, 0.0).astype(bf16)
            at_source = jnp.broadcast_to(sums[:, head : head + 1], (seg_len, half))
            at_token = sums_turned[head : head + 1]
            grad_weights = dot(stepped, grad_low, ((1,), (1,)))
            first = jnp.exp2(jnp.minimum(at_token[:, :half] - at_source[:half], 0.0))
            after = jnp.exp2(at_token[:, half:] - at_source[:half])
            second = jnp.exp2(jnp.minimum(at_token[:, half:] - at_source[half:], 0.0))
            first_grad = first_grad + first * grad_weights[:half, :half]
            later_grad = later_grad + after * grad_weights[:half, half:]
            second_grad = second_grad + second * grad_weights[half:, half:]
            upper = jnp.concatenate([first * first_scores, after * later_scores], axis=1).astype(bf16)
            early = early + dot(upper, grad_low, ((1,), (0,)))
            late = late + dot((second * second_scores).astype(bf16), grad_low[half:], ((1,), (0,)))
        inner = jnp.concatenate([early, late], axis=0)
        skip = skip_ref[:, at]
        skip_grad_ref[:, at] += jnp.sum(grad_values * x_values, axis=0, keepdims=True)
        inner_ref[:, at] = grad_values * (values_ref[:, at] - skip * x_values)
        source_ref[:, at] = x_wide * inner
        carry_ref[:, at] = x_wide * grad_scaled
        grad_x = skip * grad_values + step_pair * (inner + gap * grad_scaled)
        grad_total = grad_x * (sigmoid * (1.0 + total * (1.0 - sigmoid)))
        for k in range(CONV):
            taps_grad_ref[k : k + 1, at] += jnp.sum(grad_total * seen[k], axis=0, keepdims=True)
        taps_grad_ref[CONV : CONV + 1, at] += jnp.sum(grad_total, axis=0, keepdims=True)
        extended = jnp.concatenate([grad_total, edge_ref[:, at]], axis=0)
        edge_ref[:, at] = grad_total[:8]
        taps = taps_ref[:, at]
        grad_conv = taps[CONV - 1 : CONV] * grad_total
        for k in range(CONV - 1):
            grad_conv = grad_conv + taps[k : k + 1] * extended[CONV - 1 - k : CONV - 1 - k + seg_len]
        grad_x_ref[:, at] = grad_conv.astype(bf16)

    width = grad_ref.shape[1]
    channel = lax.broadcasted_iota(jnp.int32, (width, LANES), 0) // HEADDIM + group * width // HEADDIM
    heads = jnp.where(channel == lax.broadcasted_iota(jnp.int32, (width, LANES), 1), 1.0, 0.0).astype(bf16)
    tail = jnp.exp2(sums[seg_len - 1 :] - sums)
    source_grad = split_dot(source_ref[...], heads)
    step_grad = source_grad + tail * split_dot(carry_ref[...], heads)
    used = step * step_grad
    sum_grad = split_dot(inner_ref[...], heads) - used
    at_last = jnp.sum(used - step * source_grad, axis=0, keepdims=True)
    at_last = at_last + split_dot(decay_ref[...], heads)[:1] * jnp.exp2(sums[seg_len - 1 :])
    is_last = lax.broadcasted_iota(jnp.int32, (seg_len, LANES), 0) == seg_len - 1
    sum_grad = sum_grad + jnp.where(is_last, at_last, 0.0)
    at_or_after = lax.broadcasted_iota(jnp.int32, (seg_len, seg_len), 0) <= lax.broadcasted_iota(
        jnp.int32, (seg_len, seg_len), 1
    )
    log_grad = lax.dot_general(
        jnp.where(at_or_after, 1.0, 0.0), sum_grad, (((1,), (0,)), ((), ())),
        precision=lax.Precision.HIGHEST, preferred_element_type=f32,
    )
    grad_raw = (step_grad + head_ref[0:1] * log_grad) * jax.nn.sigmoid(shifted)
    grad_raw_ref[...] = grad_raw
    head_grad_ref[CONV + 1 : CONV + 2] += jnp.sum(log_grad * log_decay, axis=0, keepdims=True)
    head_grad_ref[CONV + 2 : CONV + 3] += jnp.sum(grad_raw, axis=0, keepdims=True)

    first_low = jnp.where(kept, first_grad, 0.0)
    second_low = jnp.where(kept, second_grad, 0.0)
    grad_scores = jnp.concatenate(
        [
            jnp.concatenate([first_low, later_grad], axis=1),
            jnp.concatenate([jnp.zeros_like(first_low), second_low], axis=1),
        ],
        axis=0,
    )
    start_ref[...] = later_ref[...]
    grad_b = dot(scaled_ref[...], local_ref[...], ((1,), (1,))) + dot(
        grad_scores.astype(bf16), c_low, ((1,), (0,))
    )
    grad_c = dot(grad_state_ref[...], prior_ref[0], ((1,), (1,))) + dot(
        grad_scores.T.astype(bf16), b_low, ((1,), (0,))
    )
    first = core_ref[0] == 0
    mine_ref[...] = jnp.where(first, grad_b, grad_c)
    theirs_ref[...] = jnp.where(first, grad_c, grad_b)


GROUPS = 1


def scan_backward(group, core, proj, taps, head, skip, rim, end, prior, values, grad_values, seg_len):
    length = proj.shape[0]
    segs = length // seg_len
    width, shared = HALF // GROUPS, proj.shape[1] - HALF
    back = lambda width, at=0: pl.BlockSpec((seg_len, width), lambda i: (segs - 1 - i, at))
    row_ahead = lambda i: jnp.maximum((segs - 1 - i) * (seg_len // 8) - 1, 0)
    ahead = lambda width, at: pl.BlockSpec((8, width), lambda i: (row_ahead(i), at))
    column = lambda rows, width, at: pl.BlockSpec((rows, width), lambda i: (0, at))
    both = HALF // shared
    return pl.pallas_call(
        lambda *refs: backward_kernel(group, *refs),
        grid=(segs,),
        out_shape=(
            jax.ShapeDtypeStruct((length, width), bf16),
            jax.ShapeDtypeStruct((length, STATE), f32),
            jax.ShapeDtypeStruct((length, STATE), f32),
            jax.ShapeDtypeStruct((length, LANES), f32),
            jax.ShapeDtypeStruct((8, width), f32),
            jax.ShapeDtypeStruct((1, width), f32),
            jax.ShapeDtypeStruct((8, LANES), f32),
            jax.ShapeDtypeStruct((8, width), f32),
            jax.ShapeDtypeStruct((STATE, width), f32),
        ),
        in_specs=[
            back(width, group),
            ahead(width, group),
            column(8, width, group),
            column(8, width, group),
            back(shared, both),
            ahead(shared, both),
            column(8, shared, both),
            column(8, shared, both),
            full_block((8, LANES)),
            column(1, width, group),
            column(STATE, width, group),
            pl.BlockSpec((1, STATE, width), lambda i: (segs - 1 - i, 0, group)),
            back(width, group),
            back(width, group),
            pl.BlockSpec(memory_space=pltpu.SMEM),
        ],
        out_specs=(
            back(width),
            back(STATE),
            back(STATE),
            back(LANES),
            full_block((8, width)),
            full_block((1, width)),
            full_block((8, LANES)),
            full_block((8, width)),
            full_block((STATE, width)),
        ),
        scratch_shapes=[
            pltpu.VMEM((STATE, width), f32),
            pltpu.VMEM((STATE, width), bf16),
            pltpu.VMEM((seg_len, width), bf16),
            pltpu.VMEM((seg_len, width), bf16),
            pltpu.VMEM((seg_len, width), f32),
            pltpu.VMEM((seg_len, width), f32),
            pltpu.VMEM((seg_len, width), f32),
            pltpu.VMEM((8, width), f32),
        ],
        compiler_params=pltpu.CompilerParams(
            dimension_semantics=("arbitrary",), vmem_limit_bytes=VMEM_LIMIT
        ),
        cost_estimate=LIGHT,
    )(
        proj, proj, taps, rim, proj, proj, taps, rim, head, skip, end, prior, values, grad_values,
        core.reshape(1).astype(jnp.int32),
    )


def half_kernel(transposed, count, core_ref, *refs):
    inputs, mine_ref, theirs_ref = refs[: 2 * count], refs[-2], refs[-1]
    total = refs[2 * count][...] if len(refs) > 2 * count + 2 else 0.0
    for left, right in zip(inputs[:count], inputs[count:]):
        total = total + dot(left[...], right[...], ((1,), (1 if transposed else 0,)))
    own = lax.rem(pl.program_id(0), 2) == core_ref[0]

    @pl.when(own)
    def _():
        mine_ref[0] = total

    @pl.when(jnp.logical_not(own))
    def _():
        theirs_ref[0] = total.astype(bf16)


def half_products(core, terms, seg_len, width, transposed, base=()):
    length = terms[0][0].shape[0]
    left = [pl.BlockSpec((seg_len, array.shape[1]), lambda i, core: (i, 0)) for array, _, _ in terms]
    right = []
    for array, matrix, at in terms:
        if transposed:
            right.append(pl.BlockSpec((width, array.shape[1]), lambda i, core, at=at: (0, at(core[0]))))
        else:
            right.append(pl.BlockSpec(matrix.shape, lambda i, core: (0, 0)))
    depth = sum(array.shape[1] for array, _, _ in terms)
    mine, theirs = pl.pallas_call(
        lambda *refs: half_kernel(transposed, len(terms), *refs),
        grid_spec=pltpu.PrefetchScalarGridSpec(
            num_scalar_prefetch=1,
            grid=(length // seg_len,),
            in_specs=left + right + [pl.BlockSpec((seg_len, width), lambda i, core: (i, 0)) for _ in base],
            out_specs=[pl.BlockSpec((1, seg_len, width), lambda i, core: (i // 2, 0, 0))] * 2,
        ),
        out_shape=(
            jax.ShapeDtypeStruct((length // seg_len // 2, seg_len, width), f32),
            jax.ShapeDtypeStruct((length // seg_len // 2, seg_len, width), bf16),
        ),
        compiler_params=pltpu.CompilerParams(dimension_semantics=("arbitrary",), vmem_limit_bytes=VMEM_LIMIT),
        cost_estimate=LIGHT,
    )(core.reshape(1).astype(jnp.int32), *[array for array, _, _ in terms], *[matrix for _, matrix, _ in terms], *base)
    return mine, theirs


def shared_kernel(core_ref, proj_ref, rim_ref, taps_ref, mine_ref, other_ref, grad_ref, taps_grad_ref, edge_ref):
    total, seen = conv_parts(proj_ref[...], rim_ref[...], taps_ref[...])
    sigmoid = jax.nn.sigmoid(total)
    grad_total = mine_ref[...] + other_ref[...]
    grad_total = grad_total * (sigmoid * (1.0 + total * (1.0 - sigmoid)))
    sums = [jnp.sum(grad_total * part, axis=0, keepdims=True) for part in seen]
    sums = sums + [jnp.sum(grad_total, axis=0, keepdims=True), jnp.zeros((8 - CONV - 1, LANES), f32)]
    taps_grad_ref[...] = jnp.concatenate(sums, axis=0)
    edge_ref[...] = grad_total[:8]
    taps = taps_ref[...]
    extended = jnp.concatenate([grad_total, jnp.zeros((8, LANES), f32)], axis=0)
    grad_conv = taps[CONV - 1 : CONV] * grad_total
    for k in range(CONV - 1):
        grad_conv = grad_conv + taps[k : k + 1] * extended[CONV - 1 - k : CONV - 1 - k + grad_total.shape[0]]
    grad_ref[...] = grad_conv.astype(bf16)


def shared_backward(core, proj, rim, taps, mine, other):
    length = proj.shape[0]
    picked = lambda rows: pl.BlockSpec((rows, LANES), lambda i, core: (0, HALF // LANES + core[0]))
    whole = lambda rows: pl.BlockSpec((rows, LANES), lambda i, core: (0, 0))
    return pl.pallas_call(
        shared_kernel,
        grid_spec=pltpu.PrefetchScalarGridSpec(
            num_scalar_prefetch=1,
            grid=(1,),
            in_specs=[picked(length), picked(8), picked(8), whole(length), whole(length)],
            out_specs=(whole(length), whole(8), whole(8)),
        ),
        out_shape=(
            jax.ShapeDtypeStruct((length, LANES), bf16),
            jax.ShapeDtypeStruct((8, LANES), f32),
            jax.ShapeDtypeStruct((8, LANES), f32),
        ),
        compiler_params=pltpu.CompilerParams(vmem_limit_bytes=VMEM_LIMIT),
        cost_estimate=LIGHT,
    )(core.reshape(1).astype(jnp.int32), proj, rim, taps, mine, other)


def per_device(hidden_in, cotangent, in_proj, out_proj, conv_params, pre_gain, gated_gain, head_params):
    chips, line = lax.axis_size("chip"), lax.axis_size("seg")
    core, place = lax.axis_index("core"), lax.axis_index("seg")
    rows, model_width = in_proj.shape[0], hidden_in.shape[2]
    heads = HEADS // 2

    conv_width, gain_width = conv_params.shape[1], gated_gain.shape[0]
    used = HALF + 2 * STATE + heads
    spare = -used % LANES
    small = jnp.zeros((rows, spare), bf16)
    small = small.at[: CONV + 1, :conv_width].set(conv_params)
    small = small.at[CONV + 1, :rows].set(pre_gain)
    small = small.at[CONV + 2, :gain_width].set(gated_gain)

    def conv_side(which):
        return jnp.concatenate(
            [
                own_columns(in_proj[:, INNER : 2 * INNER], which),
                in_proj[:, 2 * INNER : INNER + XBC],
                own_columns(in_proj[:, INNER + XBC :], which),
                small,
            ],
            axis=1,
        )

    def gate_side(which):
        return own_columns(in_proj[:, :INNER], which)

    conv_swap = to_partner(conv_side(1 - core))
    conv_block = in_core_order(conv_side(core), conv_swap, core, 0)
    conv_z = gather_step(conv_block, 2)
    gate_swap = to_partner(gate_side(1 - core))
    gate_block = in_core_order(gate_side(core), gate_swap, core, 0)
    conv_z, hidden_in, gate_block = tie(conv_z, hidden_in, gate_block)
    conv_own = jnp.stack(conv_z)
    conv_near = gather_plane(conv_own, near_steps())
    hidden_half = whole_sequence(hidden_in, core, place)
    conv_own, conv_near, hidden_half, gate_block = tie(conv_own, conv_near, hidden_half, gate_block)
    conv_far = gather_plane(conv_own, far_steps())
    gate_z = gather_step(gate_block, 2)
    hidden_other = to_partner(hidden_half)
    conv_far, gate_z, hidden_other = tie(conv_far, gate_z, hidden_other)
    gate_own = jnp.stack(gate_z)
    gate_near = gather_plane(gate_own, near_steps())
    conv_all = whole_matrix([conv_own, *conv_near, *conv_far], True)

    small_all = conv_all.reshape(chips, 2, line, rows, -1)[..., used:].astype(f32)
    taps_full = small_all[..., : CONV + 1, :conv_width].transpose(3, 0, 1, 2, 4).reshape(CONV + 1, XBC)
    taps = jnp.concatenate([own_columns(taps_full[:, :INNER], core), taps_full[:, INNER:]], axis=1)
    gain_pre = small_all[..., CONV + 1, :rows].reshape(model_width)
    gain_gate = lax.dynamic_index_in_dim(
        small_all[..., CONV + 2, :gain_width], core, axis=1, keepdims=False
    ).reshape(HALF)
    params = own_columns(head_params, core)

    seg_len = hidden_half.shape[1]
    tokens = SEGS * seg_len
    normed, normed_turned = normed_tokens(core, hidden_half, hidden_other, gain_pre, rows)
    projected = dot(normed, conv_all, ((1,), (0,)))
    projected, gate_own, gate_near, out_proj = tie(projected, gate_own, gate_near, out_proj)
    gate_far = gather_plane(gate_own, far_steps())
    out_z = gather_step(out_proj, 2)

    taps = jnp.pad(taps, ((0, 8 - CONV - 1), (0, projected.shape[1] - taps.shape[1])))
    head = jnp.pad(jnp.stack([-jnp.exp(params[0]), params[1]]), ((0, 6), (0, LANES - heads)))
    skip = jnp.repeat(params[2], HEADDIM).reshape(1, HALF)
    wide = HALF + 2 * STATE
    rim = borrowed(projected[tokens - 8 :], 1)
    nothing = jnp.zeros((STATE, HALF), f32)
    values, prior, final, last = scan_forward(projected, taps, head, skip, rim, nothing, seg_len)
    if line > SEGS:
        last = jnp.sum(last.reshape(SEGS, 8, LANES)[:, 0, :heads], axis=0)
        decay = jnp.repeat(jnp.exp2(last), HEADDIM)
        begin = entering(decay, final, 1)
        values, prior, _, _ = scan_forward(projected, taps, head, skip, rim, begin, seg_len)

    values, gate_far, out_z, cotangent = tie(values, gate_far, out_z, cotangent)
    out_own = jnp.stack(out_z)
    out_near = gather_plane(out_own, near_steps())
    cot_half = whole_sequence(cotangent, core, place)
    gate_matrix = whole_matrix([gate_own, *gate_near, *gate_far], True)
    gate_input = dot(normed, gate_matrix, ((1,), (0,)))
    gate_input, out_own, out_near = tie(gate_input, out_own, out_near)
    out_far = gather_plane(out_own, far_steps())

    silu_gate = jax.nn.silu(gate_input)
    gated = values * silu_gate
    squares = jnp.sum(gated * gated, axis=1)
    squares_other = to_partner(squares)
    scale = lax.rsqrt((squares + squares_other) / INNER + epsilon)[:, None]
    mixed, mixed_turned = mixed_tokens(gated, scale, gain_gate, seg_len)
    mixed_turned, cot_half, out_far = tie(mixed_turned, cot_half, out_far)
    cot_other = to_partner(cot_half)
    cot = in_core_order(cot_half, cot_other, core, 1)
    upstream = cot.reshape(tokens, model_width)
    by_owner = lambda grad: grad.astype(bf16).reshape(chip_dims() + (-1, grad.shape[1]))
    out_grad = by_owner(dot(mixed_turned, upstream, ((1,), (0,))))
    out_got_near = reduce_plane([out_grad], near_steps())
    out_matrix = whole_matrix([out_own, *out_near, *out_far], False)
    branch, branch_sent = half_products(core, [(mixed, out_matrix, None)], seg_len, model_width, False)
    branch_sent, upstream = tie(branch_sent, upstream)
    branch_other = to_partner(branch_sent)
    grad_mixed = dot(upstream, out_matrix, ((1,), (1,)))
    grad_mixed, out_got_near, out_grad = tie(grad_mixed, out_got_near, out_grad)
    out_got_far = reduce_plane([out_grad], far_steps())
    unit = gated * scale
    gain_grad = grad_mixed * gain_gate
    along = jnp.sum(gain_grad * unit, axis=1)
    along_other = to_partner(along)
    along_other, branch_other = tie(along_other, branch_other)
    hidden_out = back_to_owner(
        (hidden_half.astype(f32) + branch + branch_other.astype(f32)).astype(bf16), core, place
    )
    along = ((along + along_other) / INNER)[:, None]
    gate_gain_grad = jnp.sum(grad_mixed * unit, axis=0)
    grad_gated = scale * (gain_grad - unit * along)
    grad_values = grad_gated * silu_gate
    sigmoid = jax.nn.sigmoid(gate_input)
    grad_gate = (grad_gated * values * (sigmoid * (1.0 + gate_input * (1.0 - sigmoid)))).astype(bf16)
    gate_grad = by_owner(dot(normed_turned, grad_gate, ((1,), (0,))))
    gate_grad, grad_values, out_got_far, hidden_out = tie(gate_grad, grad_values, out_got_far, hidden_out)
    out_third = reduce_z([([plane_part([out_grad], 0, 0)], [*out_got_near, *out_got_far])])
    gate_got_near = reduce_plane([gate_grad], near_steps())
    scan = lambda later: scan_backward(
        0, core, projected, taps, head, skip, rim, later, prior, values, grad_values, seg_len
    )
    if line > SEGS:
        nothing = entering(decay, scan(nothing)[-1], -1)
    back = scan(nothing)
    back, gate_grad, gate_got_near, out_got, grad_gate = tie(
        back, gate_grad, gate_got_near, arrivals(out_third), grad_gate
    )
    out_third = arrived(out_third, out_got)
    gate_got_far = reduce_plane([gate_grad], far_steps())
    grad_x, mine, theirs, grad_raw, x_taps_grad, skip_grad, head_sums, x_edge, _ = back
    grad_x = spilled(grad_x, x_edge, taps[:, :HALF])
    other = to_partner(theirs)
    x_grad = by_owner(dot(normed_turned, grad_x, ((1,), (0,))))
    other, x_grad = tie(other, x_grad)
    grad_state, state_taps_grad, state_edge = shared_backward(core, projected, rim, taps, mine, other)
    grad_state = spilled(grad_state, state_edge, lax.dynamic_slice_in_dim(taps, HALF + core * STATE, STATE, axis=1))
    grad_raw = grad_raw.astype(bf16)
    rest_grad = by_owner(dot(normed_turned, jnp.concatenate([grad_state, grad_raw], axis=1), ((1,), (0,))))
    rest_grad, x_grad, grad_gate = tie(rest_grad, x_grad, grad_gate)
    conv_near = reduce_plane([x_grad, rest_grad], near_steps())
    base = dot(grad_gate, gate_matrix, ((1,), (1,)))
    base, gate_got_far = tie(base, gate_got_far)
    gate_third = reduce_z([([plane_part([gate_grad], 0, 0)], [*gate_got_near, *gate_got_far])])
    terms = [
        (grad_x, conv_all, lambda core: 0),
        (grad_state, conv_all, lambda core: HALF // LANES + core),
        (grad_raw, conv_all, lambda core: (HALF + 2 * STATE) // LANES),
    ]
    grad_normed, sent_normed = half_products(core, terms, seg_len, model_width, True, (base,))
    row = lax.broadcasted_iota(jnp.int32, (8, 1), 0)
    small = x_taps_grad + jnp.where(row == CONV + 1, gate_gain_grad, 0.0) + jnp.where(row == CONV + 2, skip_grad, 0.0)
    small = jnp.concatenate([small, state_taps_grad + head_sums], axis=1)
    sent_normed, gate_got, conv_near, small, x_grad, rest_grad = tie(
        sent_normed, arrivals(gate_third), conv_near, small, x_grad, rest_grad
    )
    conv_far = reduce_plane([x_grad, rest_grad], far_steps())
    other_normed = to_partner(sent_normed)
    wide_hidden = hidden_half.astype(f32)
    hidden_scale = lax.rsqrt(jnp.mean(wide_hidden * wide_hidden, axis=-1, keepdims=True) + epsilon)
    grad_normed = (grad_normed + other_normed.astype(f32)) * gain_pre
    hidden_unit = wide_hidden * hidden_scale
    along = jnp.mean(grad_normed * hidden_unit, axis=-1, keepdims=True)
    grad_hidden = hidden_scale * (grad_normed - hidden_unit * along)
    grad_in = (cot_half.astype(f32) + grad_hidden).astype(bf16)
    grad_in = back_to_owner(grad_in, core, place)
    grad_in, conv_far = tie(grad_in, conv_far)
    late = reduce_z([([plane_part([x_grad, rest_grad], 0, 0)], [*conv_near, *conv_far])])
    for dim in range(3):
        small = small + sum(moved(small, dim, by) for by in range(1, chip_dims()[dim]))
    small_other = to_partner(small)
    late_got, small_other = tie(arrivals(late), small_other)
    out_share = reduce_end(out_third)
    paired = lambda share: share.astype(bf16).reshape(2, rows, -1)
    gate_share, conv_share = paired(reduce_end(arrived(gate_third, gate_got))), paired(reduce_end(arrived(late, late_got)))

    def mine_and_partner(share):
        keep = lax.dynamic_index_in_dim(share, core, axis=0, keepdims=False)
        give = lax.dynamic_index_in_dim(share, 1 - core, axis=0, keepdims=False)
        return keep, to_partner(give)

    both = in_core_order(small, small_other, core, 0)
    natural = lambda array, width: array.reshape(2, -1, chips, width).transpose(1, 2, 0, 3).reshape(-1, 2 * chips * width)
    device = (lax.axis_index("chip") * 2 + core) * line + place
    columns = natural(both[:, :, :HALF], HALF // chips)
    taps_all = jnp.concatenate([columns, both[0, :, HALF:], both[1, :, HALF:]], axis=1)[: CONV + 1]
    taps_share = lax.dynamic_slice_in_dim(taps_all, device * conv_width, conv_width, axis=1)
    gain_share = lax.dynamic_slice_in_dim(columns[CONV + 1], device * gain_width, gain_width, axis=0)
    head_total = jnp.concatenate(
        [
            natural(both[:, CONV + 1 : CONV + 3, HALF : HALF + heads], heads // chips),
            jnp.sum(columns[CONV + 2].reshape(1, HEADS, HEADDIM), axis=2),
        ]
    )

    def interleave(mine, theirs):
        width = mine.shape[1] // chips
        both = in_core_order(mine.reshape(rows, chips, width), theirs.reshape(rows, chips, width), core, 2)
        return both.reshape(rows, -1)

    keep_gate, got_gate = mine_and_partner(gate_share)
    keep, got = mine_and_partner(conv_share)
    state_end = HALF + STATE
    in_share = jnp.concatenate(
        [
            interleave(keep_gate, got_gate),
            interleave(keep[:, :HALF], got[:, :HALF]),
            in_core_order(keep[:, HALF:state_end], got[:, HALF:state_end], core, 1).reshape(rows, -1),
            interleave(keep[:, state_end : state_end + heads], got[:, state_end : state_end + heads]),
        ],
        axis=1,
    ).astype(f32)
    pre_share = jnp.sum(in_proj.astype(f32) * in_share, axis=1) / pre_gain.astype(f32)
    return (hidden_out, grad_in, in_share, out_share, taps_share, pre_share, gain_share, head_total)


def solution(mesh):
    devices = mesh.devices
    cores = Mesh(devices.reshape(devices.shape[0] // 2, 2, devices.shape[1]), ("chip", "core", "seg"))
    dp, both = ("chip", "core"), ("chip", "core", "seg")
    tokens = P(dp, "seg", None)
    return jax.shard_map(
        per_device,
        mesh=cores,
        in_specs=(tokens, tokens, P(both, None), P(both, None), P(None, both), P(both), P(both), P()),
        out_specs=(tokens, tokens, P(both, None), P(both, None), P(None, both), P(both), P(both), P()),
        check_vma=False,
    )
```

```python
import jax
import jax.numpy as jnp
from jax import lax
from jax.experimental import pallas as pl
from jax.experimental.pallas import tpu as pltpu
from jax.sharding import Mesh
from jax.sharding import PartitionSpec as P

HEADS = 48
HEADDIM = 64
STATE = 128
CONV = 4
INNER = 3072
XBC = 3328
HALF = INNER // 2
LANES = 128
SEGS = 4
LIGHT = pl.CostEstimate(flops=1024, bytes_accessed=1024, transcendentals=0)
VMEM_LIMIT = 48 * 1024 * 1024
LOG2E = 1.4426950408889634

epsilon = 1e-05
f32 = jnp.float32
bf16 = jnp.bfloat16


def own_columns(array, core):
    chips = lax.axis_size("chip")
    width = array.shape[-1] // (2 * chips)
    parted = array.reshape(array.shape[:-1] + (chips, 2, width))
    picked = lax.dynamic_index_in_dim(parted, core, axis=parted.ndim - 2, keepdims=False)
    return picked.reshape(array.shape[:-1] + (chips * width,))


def to_partner(array):
    return lax.ppermute(array, "core", [(0, 1), (1, 0)])


def in_core_order(mine, theirs, core, axis):
    first = jnp.where(core == 0, mine, theirs)
    second = jnp.where(core == 0, theirs, mine)
    return jnp.stack([first, second], axis=axis)


def chip_dims():
    return (lax.axis_size("chip") // 2, 2, lax.axis_size("seg"))


def chip_place():
    chip = lax.axis_index("chip")
    return (chip // 2, chip % 2, lax.axis_index("seg"))


def moved(array, dim, by):
    sizes = chip_dims()
    index = lambda at: (at[0] * sizes[1] + at[1]) * sizes[2] + at[2]
    pairs = []
    for a in range(sizes[0]):
        for b in range(sizes[1]):
            for z in range(sizes[2]):
                to = [a, b, z]
                to[dim] = (to[dim] + by) % sizes[dim]
                pairs.append((index((a, b, z)), index(to)))
    return lax.ppermute(array, ("chip", "seg"), pairs)


def tie(*values):
    return lax.optimization_barrier(values)


def gather_step(data, dim):
    return [data] + [moved(data, dim, by) for by in range(1, chip_dims()[dim])]


def plane_steps():
    a, b, _ = chip_dims()
    steps = [(at // b, at % b) for at in range(1, a * b)]
    return sorted(steps, key=lambda by: bool(by[0] and by[1]))


def near_steps():
    a, b, _ = chip_dims()
    return plane_steps()[: a + b - 2]


def far_steps():
    a, b, _ = chip_dims()
    return plane_steps()[a + b - 2 :]


def moved_plane(array, by_a, by_b):
    a, b, z = chip_dims()
    pairs = [
        ((at_a * b + at_b) * z + at_z, ((at_a + by_a) % a * b + (at_b + by_b) % b) * z + at_z)
        for at_a in range(a)
        for at_b in range(b)
        for at_z in range(z)
    ]
    return lax.ppermute(array, ("chip", "seg"), pairs)


def gather_plane(data, steps):
    return [moved_plane(data, *by) for by in steps]


def placed_kernel(plan, place_ref, *refs):
    sources, target, sems = refs[:-2], refs[-2], refs[-1]
    copies = []
    for source, lead, at, paired in plan:
        spot = [lax.rem(place_ref[dim] + (size - back), size) for dim, (back, size) in enumerate(at)]
        to = target.at[spot[0], spot[1], :, spot[2]] if paired else target.at[spot[0], spot[1], spot[2]]
        copies.append(pltpu.make_async_copy(sources[source].at[lead], to, sems.at[len(copies)]))
    for copy in copies:
        copy.start()
    for copy in copies:
        copy.wait()


def whole_matrix(gathered, paired):
    a, b, z = chip_dims()
    plan = [
        (source, back, ((by[0], a), (by[1], b), (back, z)), paired)
        for source, by in enumerate([(0, 0)] + plane_steps())
        for back in range(z)
    ]
    block = gathered[0].shape[1:]
    shape = (a, b, 2, z) + block[1:] if paired else (a, b, z) + block
    anywhere = pl.BlockSpec(memory_space=pl.ANY)
    whole = pl.pallas_call(
        lambda *refs: placed_kernel(plan, *refs),
        out_shape=jax.ShapeDtypeStruct(shape, bf16),
        in_specs=[pl.BlockSpec(memory_space=pltpu.SMEM)] + [anywhere] * len(gathered),
        out_specs=pl.BlockSpec(memory_space=pltpu.VMEM),
        scratch_shapes=[pltpu.SemaphoreType.DMA((len(plan),))],
        compiler_params=pltpu.CompilerParams(vmem_limit_bytes=VMEM_LIMIT),
        cost_estimate=LIGHT,
    )(jnp.stack(chip_place()).astype(jnp.int32), *gathered)
    return whole.reshape(-1, shape[-1])


def total(terms):
    result = terms[0].astype(f32)
    for term in terms[1:]:
        result = result + term.astype(f32)
    return result


def reduce_send(terms, axis, dim, wire):
    place, size = chip_place()[dim], chip_dims()[dim]
    pick = lambda at: [lax.dynamic_index_in_dim(term, at, axis=axis, keepdims=False) for term in terms]
    received = [moved(total(pick((place + by) % size)).astype(wire), dim, by) for by in range(1, size)]
    return pick(place), received


def plane_part(partials, by_a, by_b):
    (at_a, at_b, _), (a, b, _) = chip_place(), chip_dims()
    chip = (at_a + by_a) % a * b + (at_b + by_b) % b
    flat = [partial.reshape((a * b,) + partial.shape[2:]) for partial in partials]
    return jnp.concatenate([lax.dynamic_index_in_dim(array, chip, axis=0, keepdims=False) for array in flat], axis=-1)


def reduce_plane(partials, steps):
    return [moved_plane(plane_part(partials, *by), *by) for by in steps]


def reduce_z(firsts):
    joined = jnp.concatenate([total(kept + received) for kept, received in firsts], axis=-1)
    return [reduce_send([joined], 0, 2, bf16)]


def reduce_end(third):
    return total(third[0][0] + third[0][1])


def arrivals(parts):
    return [received for _, received in parts]


def arrived(parts, received):
    return [(kept, new) for (kept, _), new in zip(parts, received)]


def line_perm(turn, back):
    line = lax.axis_size("seg")
    parts = line // SEGS
    pairs = []
    for core in range(2):
        for place in range(line):
            half, odd = divmod(place % SEGS, 2)
            source = core * line + place
            target = odd * line + (2 * core + (half ^ turn)) * parts + place // SEGS
            pairs.append((target, source) if back else (source, target))
    return pairs


def swapped(pair, turn):
    return [jnp.where(turn == 0, pair[0], pair[1]), jnp.where(turn == 0, pair[1], pair[0])]


def whole_sequence(array, core, place):
    parts = lax.axis_size("seg") // SEGS
    pieces = swapped([array[0], array[1]], (place % SEGS) // 2)
    got = [lax.ppermute(piece, ("core", "seg"), line_perm(turn, False)) for turn, piece in enumerate(pieces)]
    return jnp.stack(swapped(got, (place // parts) % 2))


def back_to_owner(ordered, core, place):
    parts = lax.axis_size("seg") // SEGS
    pieces = swapped([ordered[0], ordered[1]], (place // parts) % 2)
    got = [lax.ppermute(piece, ("core", "seg"), line_perm(turn, True)) for turn, piece in enumerate(pieces)]
    return jnp.stack(swapped(got, (place % SEGS) // 2))


def part_pairs(step):
    line = lax.axis_size("seg")
    parts = line // SEGS
    return [(i, i + step) for i in range(line) if 0 <= i + step < line and i // parts == (i + step) // parts]


def entering(decay, state, step):
    parts = lax.axis_size("seg") // SEGS
    total = jnp.zeros_like(state)
    for _ in range(parts - 1):
        total = lax.ppermute(decay * total + state, "seg", part_pairs(step))
    return total


def borrowed(array, step):
    parts = lax.axis_size("seg") // SEGS
    if parts == 1:
        return jnp.zeros_like(array)
    return lax.ppermute(array, "seg", part_pairs(step))


def spilled(grad, edge, taps):
    if lax.axis_size("seg") == SEGS:
        return grad
    edge = borrowed(edge, -1)
    spill = jnp.stack(
        [
            sum(taps[k] * edge[CONV - 1 - k - early] for k in range(CONV - early))
            for early in range(CONV - 1, 0, -1)
        ]
    )
    at = grad.shape[0] - CONV + 1
    return grad.at[at:].set((grad[at:].astype(f32) + spill).astype(bf16))


def dot(a, b, contract):
    return lax.dot_general(a, b, (contract, ((), ())), preferred_element_type=f32)


def normed_kernel(slabs, core_ref, mine_ref, other_ref, gain_ref, normed_ref, turned_ref):
    own = lax.rem(pl.program_id(0), 2) == core_ref[0]
    hidden = jnp.where(own, mine_ref[0], other_ref[0]).astype(f32)
    scale = lax.rsqrt(jnp.mean(hidden * hidden, axis=1, keepdims=True) + epsilon)
    normed = hidden * scale * gain_ref[...]
    normed_ref[...] = normed.astype(bf16)
    turned = normed.T.astype(bf16)
    for to, at, size in slabs:
        turned_ref[to : to + size] = turned[at : at + size]


def normed_tokens(core, mine, other, gain, rows):
    segs, seg_len, width = 2 * mine.shape[0], mine.shape[1], mine.shape[2]
    a, b, z = chip_dims()
    group = 2 * z * rows
    inside = rows % 16 == 0
    slabs = [(0, 0, width)]
    if inside:
        slabs = [
            (chip * group + (at * 2 + core_at) * rows, chip * group + (core_at * z + at) * rows, rows)
            for chip in range(a * b)
            for core_at in range(2)
            for at in range(z)
        ]
    normed, turned = pl.pallas_call(
        lambda *refs: normed_kernel(slabs, *refs),
        grid_spec=pltpu.PrefetchScalarGridSpec(
            num_scalar_prefetch=1,
            grid=(segs,),
            in_specs=[
                pl.BlockSpec((1, seg_len, width), lambda i, core: (i // 2, 0, 0)),
                pl.BlockSpec((1, seg_len, width), lambda i, core: (i // 2, 0, 0)),
                pl.BlockSpec((1, width), lambda i, core: (0, 0)),
            ],
            out_specs=(
                pl.BlockSpec((seg_len, width), lambda i, core: (i, 0)),
                pl.BlockSpec((width, seg_len), lambda i, core: (0, i)),
            ),
        ),
        out_shape=(
            jax.ShapeDtypeStruct((segs * seg_len, width), bf16),
            jax.ShapeDtypeStruct((width, segs * seg_len), bf16),
        ),
        compiler_params=pltpu.CompilerParams(dimension_semantics=("arbitrary",), vmem_limit_bytes=VMEM_LIMIT),
        cost_estimate=LIGHT,
    )(core.reshape(1).astype(jnp.int32), mine, other, gain.reshape(1, width))
    if not inside:
        turned = turned.reshape(a, b, 2, z, rows, -1).transpose(0, 1, 3, 2, 4, 5).reshape(turned.shape)
    return normed, turned


def mixed_kernel(gated_ref, scale_ref, gain_ref, mixed_ref, turned_ref):
    mixed = gated_ref[...] * scale_ref[...] * gain_ref[...]
    mixed_ref[...] = mixed.astype(bf16)
    turned_ref[...] = mixed.T.astype(bf16)


def mixed_tokens(gated, scale, gain, seg_len):
    length, width = gated.shape
    return pl.pallas_call(
        mixed_kernel,
        grid=(length // seg_len,),
        in_specs=[
            pl.BlockSpec((seg_len, width), lambda i: (i, 0)),
            pl.BlockSpec((seg_len, 1), lambda i: (i, 0)),
            pl.BlockSpec((1, width), lambda i: (0, 0)),
        ],
        out_specs=(
            pl.BlockSpec((seg_len, width), lambda i: (i, 0)),
            pl.BlockSpec((width, seg_len), lambda i: (0, i)),
        ),
        out_shape=(
            jax.ShapeDtypeStruct((length, width), bf16),
            jax.ShapeDtypeStruct((width, length), bf16),
        ),
        compiler_params=pltpu.CompilerParams(dimension_semantics=("arbitrary",), vmem_limit_bytes=VMEM_LIMIT),
        cost_estimate=LIGHT,
    )(gated, scale, gain.reshape(1, width))


def columns_of(pair):
    return pl.ds(pair * LANES, LANES)


def low_half(shape):
    return lax.broadcasted_iota(jnp.int32, shape, len(shape) - 1) < HEADDIM


def pair_columns(array, pair, low):
    rows = array.shape[0]
    first = jnp.broadcast_to(array[:, 2 * pair : 2 * pair + 1], (rows, LANES))
    second = jnp.broadcast_to(array[:, 2 * pair + 1 : 2 * pair + 2], (rows, LANES))
    return jnp.where(low, first, second)


def conv_parts(current, before, taps):
    rows = current.shape[0]
    padded = jnp.concatenate([before, current], axis=0)
    seen = [padded[8 - CONV + 1 + k : 8 - CONV + 1 + k + rows] for k in range(CONV - 1)] + [current]
    total = taps[CONV : CONV + 1]
    for k in range(CONV):
        total = total + taps[k : k + 1] * seen[k]
    return total, seen


def step_terms(raw, head, seg_len):
    shifted = raw + head[1:2]
    step = jnp.maximum(shifted, 0.0) + jnp.log1p(jnp.exp(-jnp.abs(shifted)))
    log_decay = step * head[0:1]
    at_or_before = lax.broadcasted_iota(jnp.int32, (seg_len, seg_len), 0) >= lax.broadcasted_iota(
        jnp.int32, (seg_len, seg_len), 1
    )
    sums = lax.dot_general(
        jnp.where(at_or_before, 1.0, 0.0), log_decay, (((1,), (0,)), ((), ())),
        precision=lax.Precision.HIGHEST, preferred_element_type=f32,
    )
    return shifted, step, log_decay, sums * LOG2E


def forward_kernel(
    proj_ref, taps_ref, head_ref, skip_ref, rim_ref, init_ref,
    values_ref, prior_ref, final_ref, last_ref, state_ref, tail_ref,
):
    seg_len = proj_ref.shape[0]
    half = seg_len // 2

    @pl.when(pl.program_id(0) == 0)
    def _():
        state_ref[...] = init_ref[...]
        tail_ref[...] = rim_ref[...]

    def activated(begin):
        at = pl.ds(begin, LANES)
        total, _ = conv_parts(proj_ref[:, at], tail_ref[:, at], taps_ref[:, at])
        return total * jax.nn.sigmoid(total)

    b_low = activated(HALF).astype(bf16)
    b_turned = activated(HALF).T.astype(bf16)
    c_low = activated(HALF + STATE).astype(bf16)
    _, step, _, sums = step_terms(proj_ref[:, HALF + 2 * STATE :], head_ref, seg_len)
    sums_turned, step_turned = sums.T, step.T
    scores = dot(c_low, b_low, ((1,), (1,)))
    kept = lax.broadcasted_iota(jnp.int32, (half, half), 0) >= lax.broadcasted_iota(jnp.int32, (half, half), 1)
    first_scores = jnp.where(kept, scores[:half, :half], 0.0)
    later_scores = scores[half:, :half]
    second_scores = jnp.where(kept, scores[half:, half:], 0.0)
    low = low_half((seg_len, LANES))
    last_ref[...] = jnp.broadcast_to(sums[seg_len - 1 :], last_ref.shape)

    for pair in range(HEADS // 4):
        at = columns_of(pair)
        x_values = activated(pair * LANES)
        x_low = x_values.astype(bf16)
        sums_pair = pair_columns(sums, pair, low)
        last_pair = sums_pair[seg_len - 1 :]
        carry = jnp.exp2(last_pair - sums_pair) * pair_columns(step, pair, low)
        scaled_x = (carry * x_low.astype(f32)).astype(bf16)
        prior = state_ref[:, at]
        prior_low = prior.astype(bf16)
        prior_ref[0, :, at] = prior_low
        from_state = jnp.exp2(sums_pair) * dot(c_low, prior_low, ((1,), (0,)))
        state_ref[:, at] = jnp.exp2(last_pair) * prior + dot(b_turned, scaled_x, ((1,), (0,)))
        early, late = 0.0, 0.0
        for side in range(2):
            head = 2 * pair + side
            x_side = jnp.where(low if side == 0 else ~low, x_values, 0.0).astype(bf16)
            at_token = jnp.broadcast_to(sums[:, head : head + 1], (seg_len, half))
            at_source, source_step = sums_turned[head : head + 1], step_turned[head : head + 1]
            first = jnp.exp2(jnp.minimum(at_token[:half] - at_source[:, :half], 0.0)) * first_scores
            first = (first * source_step[:, :half]).astype(bf16)
            later = jnp.exp2(at_token[half:] - at_source[:, :half]) * later_scores
            later = (later * source_step[:, :half]).astype(bf16)
            second = jnp.exp2(jnp.minimum(at_token[half:] - at_source[:, half:], 0.0)) * second_scores
            second = (second * source_step[:, half:]).astype(bf16)
            early = early + dot(first, x_side[:half], ((1,), (0,)))
            late = late + dot(jnp.concatenate([later, second], axis=1), x_side, ((1,), (0,)))
        intra = jnp.concatenate([early, late], axis=0)
        values_ref[:, at] = intra + from_state + skip_ref[:, at] * x_values

    tail_ref[...] = proj_ref[seg_len - 8 :, : HALF + 2 * STATE]
    final_ref[...] = state_ref[...]


def full_block(shape):
    return pl.BlockSpec(shape, lambda *_: (0,) * len(shape))


def scan_forward(proj, taps, head, skip, rim, init, seg_len):
    segs = proj.shape[0] // seg_len
    wide = HALF + 2 * STATE
    return pl.pallas_call(
        forward_kernel,
        grid=(segs,),
        out_shape=(
            jax.ShapeDtypeStruct((proj.shape[0], HALF), f32),
            jax.ShapeDtypeStruct((segs, STATE, HALF), bf16),
            jax.ShapeDtypeStruct((STATE, HALF), f32),
            jax.ShapeDtypeStruct((segs * 8, LANES), f32),
        ),
        in_specs=[
            pl.BlockSpec((seg_len, proj.shape[1]), lambda i: (i, 0)),
            full_block((8, wide)),
            full_block((8, LANES)),
            full_block((1, HALF)),
            full_block((8, wide)),
            full_block((STATE, HALF)),
        ],
        out_specs=(
            pl.BlockSpec((seg_len, HALF), lambda i: (i, 0)),
            pl.BlockSpec((1, STATE, HALF), lambda i: (i, 0, 0)),
            full_block((STATE, HALF)),
            pl.BlockSpec((8, LANES), lambda i: (i, 0)),
        ),
        scratch_shapes=[pltpu.VMEM((STATE, HALF), f32), pltpu.VMEM((8, wide), f32)],
        compiler_params=pltpu.CompilerParams(
            dimension_semantics=("arbitrary",), vmem_limit_bytes=VMEM_LIMIT
        ),
        cost_estimate=LIGHT,
    )(proj, taps, head, skip, rim, init)


def split_dot(array, other):
    high = array.astype(bf16)
    rest = (array - high.astype(f32)).astype(bf16)
    return dot(high, other, ((1,), (0,))) + dot(rest, other, ((1,), (0,)))


def backward_kernel(
    group, proj_ref, before_ref, taps_ref, rim_ref, shared_ref, shared_before_ref, shared_taps_ref, shared_rim_ref,
    head_ref, skip_ref, end_ref, prior_ref, values_ref, grad_ref, core_ref,
    grad_x_ref, mine_ref, theirs_ref, grad_raw_ref, taps_grad_ref, skip_grad_ref, head_grad_ref, edge_ref, start_ref,
    later_ref, local_ref, scaled_ref, grad_state_ref, inner_ref, source_ref, carry_ref, decay_ref,
):
    seg_len = proj_ref.shape[0]
    half = seg_len // 2
    turn = pl.program_id(0)

    @pl.when(turn == 0)
    def _():
        later_ref[...] = end_ref[...]
        edge_ref[...] = jnp.zeros_like(edge_ref)
        taps_grad_ref[...] = jnp.zeros_like(taps_grad_ref)
        skip_grad_ref[...] = jnp.zeros_like(skip_grad_ref)
        head_grad_ref[...] = jnp.zeros_like(head_grad_ref)

    first_segment = turn == pl.num_programs(0) - 1

    def conv_at(at, current, ahead, taps, rim):
        before = jnp.where(first_segment, rim[:, at], ahead[:, at])
        return conv_parts(current[:, at], before, taps[:, at])

    def activated(begin):
        total, _ = conv_at(pl.ds(begin, LANES), shared_ref, shared_before_ref, shared_taps_ref, shared_rim_ref)
        return total * jax.nn.sigmoid(total)

    b_values = activated(0)
    c_values = activated(STATE)
    b_low, c_low, c_turned = b_values.astype(bf16), c_values.astype(bf16), c_values.T.astype(bf16)
    shifted, step, log_decay, sums = step_terms(shared_ref[:, 2 * STATE :], head_ref, seg_len)
    sums_turned = sums.T
    scores = dot(b_low, c_low, ((1,), (1,)))
    kept = lax.broadcasted_iota(jnp.int32, (half, half), 0) <= lax.broadcasted_iota(jnp.int32, (half, half), 1)
    first_scores = jnp.where(kept, scores[:half, :half], 0.0)
    later_scores = scores[:half, half:]
    second_scores = jnp.where(kept, scores[half:, half:], 0.0)
    low = low_half((seg_len, LANES))
    first_grad, later_grad, second_grad = 0.0, 0.0, 0.0

    pairs = grad_ref.shape[1] // LANES
    for pair in range(pairs):
        at = columns_of(pair)
        total, seen = conv_at(at, proj_ref, before_ref, taps_ref, rim_ref)
        sigmoid = jax.nn.sigmoid(total)
        x_values = total * sigmoid
        x_low = x_values.astype(bf16)
        x_wide = x_low.astype(f32)
        sums_pair = pair_columns(sums, group * pairs + pair, low)
        step_pair = pair_columns(step, group * pairs + pair, low)
        last_pair = sums_pair[seg_len - 1 :]
        gap = jnp.exp2(last_pair - sums_pair)
        scaled_ref[:, at] = (gap * step_pair * x_wide).astype(bf16)
        grad_values = grad_ref[:, at]
        grad_state_ref[:, at] = (grad_values * jnp.exp2(sums_pair)).astype(bf16)
        later = later_ref[:, at]
        later_low = later.astype(bf16)
        local_ref[:, at] = later_low
        prior = prior_ref[0, :, at]
        decay_ref[:, at] = jnp.broadcast_to(
            jnp.sum(later * prior.astype(f32), axis=0, keepdims=True), (8, LANES)
        )
        grad_prior = dot(c_turned, grad_state_ref[:, at], ((1,), (0,)))
        later_ref[:, at] = jnp.exp2(last_pair) * later + grad_prior
        grad_scaled = dot(b_low, later_low, ((1,), (0,)))
        stepped = (step_pair * x_wide).astype(bf16)
        early, late = 0.0, 0.0
        for side in range(2):
            head = 2 * (group * pairs + pair) + side
            grad_low = jnp.where(low if side == 0 else ~low, grad_values, 0.0).astype(bf16)
            at_source = jnp.broadcast_to(sums[:, head : head + 1], (seg_len, half))
            at_token = sums_turned[head : head + 1]
            grad_weights = dot(stepped, grad_low, ((1,), (1,)))
            first = jnp.exp2(jnp.minimum(at_token[:, :half] - at_source[:half], 0.0))
            after = jnp.exp2(at_token[:, half:] - at_source[:half])
            second = jnp.exp2(jnp.minimum(at_token[:, half:] - at_source[half:], 0.0))
            first_grad = first_grad + first * grad_weights[:half, :half]
            later_grad = later_grad + after * grad_weights[:half, half:]
            second_grad = second_grad + second * grad_weights[half:, half:]
            upper = jnp.concatenate([first * first_scores, after * later_scores], axis=1).astype(bf16)
            early = early + dot(upper, grad_low, ((1,), (0,)))
            late = late + dot((second * second_scores).astype(bf16), grad_low[half:], ((1,), (0,)))
        inner = jnp.concatenate([early, late], axis=0)
        skip = skip_ref[:, at]
        skip_grad_ref[:, at] += jnp.sum(grad_values * x_values, axis=0, keepdims=True)
        inner_ref[:, at] = grad_values * (values_ref[:, at] - skip * x_values)
        source_ref[:, at] = x_wide * inner
        carry_ref[:, at] = x_wide * grad_scaled
        grad_x = skip * grad_values + step_pair * (inner + gap * grad_scaled)
        grad_total = grad_x * (sigmoid * (1.0 + total * (1.0 - sigmoid)))
        for k in range(CONV):
            taps_grad_ref[k : k + 1, at] += jnp.sum(grad_total * seen[k], axis=0, keepdims=True)
        taps_grad_ref[CONV : CONV + 1, at] += jnp.sum(grad_total, axis=0, keepdims=True)
        extended = jnp.concatenate([grad_total, edge_ref[:, at]], axis=0)
        edge_ref[:, at] = grad_total[:8]
        taps = taps_ref[:, at]
        grad_conv = taps[CONV - 1 : CONV] * grad_total
        for k in range(CONV - 1):
            grad_conv = grad_conv + taps[k : k + 1] * extended[CONV - 1 - k : CONV - 1 - k + seg_len]
        grad_x_ref[:, at] = grad_conv.astype(bf16)

    width = grad_ref.shape[1]
    channel = lax.broadcasted_iota(jnp.int32, (width, LANES), 0) // HEADDIM + group * width // HEADDIM
    heads = jnp.where(channel == lax.broadcasted_iota(jnp.int32, (width, LANES), 1), 1.0, 0.0).astype(bf16)
    tail = jnp.exp2(sums[seg_len - 1 :] - sums)
    source_grad = split_dot(source_ref[...], heads)
    step_grad = source_grad + tail * split_dot(carry_ref[...], heads)
    used = step * step_grad
    sum_grad = split_dot(inner_ref[...], heads) - used
    at_last = jnp.sum(used - step * source_grad, axis=0, keepdims=True)
    at_last = at_last + split_dot(decay_ref[...], heads)[:1] * jnp.exp2(sums[seg_len - 1 :])
    is_last = lax.broadcasted_iota(jnp.int32, (seg_len, LANES), 0) == seg_len - 1
    sum_grad = sum_grad + jnp.where(is_last, at_last, 0.0)
    at_or_after = lax.broadcasted_iota(jnp.int32, (seg_len, seg_len), 0) <= lax.broadcasted_iota(
        jnp.int32, (seg_len, seg_len), 1
    )
    log_grad = lax.dot_general(
        jnp.where(at_or_after, 1.0, 0.0), sum_grad, (((1,), (0,)), ((), ())),
        precision=lax.Precision.HIGHEST, preferred_element_type=f32,
    )
    grad_raw = (step_grad + head_ref[0:1] * log_grad) * jax.nn.sigmoid(shifted)
    grad_raw_ref[...] = grad_raw
    head_grad_ref[CONV + 1 : CONV + 2] += jnp.sum(log_grad * log_decay, axis=0, keepdims=True)
    head_grad_ref[CONV + 2 : CONV + 3] += jnp.sum(grad_raw, axis=0, keepdims=True)

    first_low = jnp.where(kept, first_grad, 0.0)
    second_low = jnp.where(kept, second_grad, 0.0)
    grad_scores = jnp.concatenate(
        [
            jnp.concatenate([first_low, later_grad], axis=1),
            jnp.concatenate([jnp.zeros_like(first_low), second_low], axis=1),
        ],
        axis=0,
    )
    start_ref[...] = later_ref[...]
    grad_b = dot(scaled_ref[...], local_ref[...], ((1,), (1,))) + dot(
        grad_scores.astype(bf16), c_low, ((1,), (0,))
    )
    grad_c = dot(grad_state_ref[...], prior_ref[0], ((1,), (1,))) + dot(
        grad_scores.T.astype(bf16), b_low, ((1,), (0,))
    )
    first = core_ref[0] == 0
    mine_ref[...] = jnp.where(first, grad_b, grad_c)
    theirs_ref[...] = jnp.where(first, grad_c, grad_b)


GROUPS = 1


def scan_backward(group, core, proj, taps, head, skip, rim, end, prior, values, grad_values, seg_len):
    length = proj.shape[0]
    segs = length // seg_len
    width, shared = HALF // GROUPS, proj.shape[1] - HALF
    back = lambda width, at=0: pl.BlockSpec((seg_len, width), lambda i: (segs - 1 - i, at))
    row_ahead = lambda i: jnp.maximum((segs - 1 - i) * (seg_len // 8) - 1, 0)
    ahead = lambda width, at: pl.BlockSpec((8, width), lambda i: (row_ahead(i), at))
    column = lambda rows, width, at: pl.BlockSpec((rows, width), lambda i: (0, at))
    both = HALF // shared
    return pl.pallas_call(
        lambda *refs: backward_kernel(group, *refs),
        grid=(segs,),
        out_shape=(
            jax.ShapeDtypeStruct((length, width), bf16),
            jax.ShapeDtypeStruct((length, STATE), f32),
            jax.ShapeDtypeStruct((length, STATE), f32),
            jax.ShapeDtypeStruct((length, LANES), f32),
            jax.ShapeDtypeStruct((8, width), f32),
            jax.ShapeDtypeStruct((1, width), f32),
            jax.ShapeDtypeStruct((8, LANES), f32),
            jax.ShapeDtypeStruct((8, width), f32),
            jax.ShapeDtypeStruct((STATE, width), f32),
        ),
        in_specs=[
            back(width, group),
            ahead(width, group),
            column(8, width, group),
            column(8, width, group),
            back(shared, both),
            ahead(shared, both),
            column(8, shared, both),
            column(8, shared, both),
            full_block((8, LANES)),
            column(1, width, group),
            column(STATE, width, group),
            pl.BlockSpec((1, STATE, width), lambda i: (segs - 1 - i, 0, group)),
            back(width, group),
            back(width, group),
            pl.BlockSpec(memory_space=pltpu.SMEM),
        ],
        out_specs=(
            back(width),
            back(STATE),
            back(STATE),
            back(LANES),
            full_block((8, width)),
            full_block((1, width)),
            full_block((8, LANES)),
            full_block((8, width)),
            full_block((STATE, width)),
        ),
        scratch_shapes=[
            pltpu.VMEM((STATE, width), f32),
            pltpu.VMEM((STATE, width), bf16),
            pltpu.VMEM((seg_len, width), bf16),
            pltpu.VMEM((seg_len, width), bf16),
            pltpu.VMEM((seg_len, width), f32),
            pltpu.VMEM((seg_len, width), f32),
            pltpu.VMEM((seg_len, width), f32),
            pltpu.VMEM((8, width), f32),
        ],
        compiler_params=pltpu.CompilerParams(
            dimension_semantics=("arbitrary",), vmem_limit_bytes=VMEM_LIMIT
        ),
        cost_estimate=LIGHT,
    )(
        proj, proj, taps, rim, proj, proj, taps, rim, head, skip, end, prior, values, grad_values,
        core.reshape(1).astype(jnp.int32),
    )


def half_kernel(transposed, count, core_ref, *refs):
    inputs, mine_ref, theirs_ref = refs[: 2 * count], refs[-2], refs[-1]
    total = refs[2 * count][...] if len(refs) > 2 * count + 2 else 0.0
    for left, right in zip(inputs[:count], inputs[count:]):
        total = total + dot(left[...], right[...], ((1,), (1 if transposed else 0,)))
    own = lax.rem(pl.program_id(0), 2) == core_ref[0]

    @pl.when(own)
    def _():
        mine_ref[0] = total

    @pl.when(jnp.logical_not(own))
    def _():
        theirs_ref[0] = total.astype(bf16)


def half_products(core, terms, seg_len, width, transposed, base=()):
    length = terms[0][0].shape[0]
    left = [pl.BlockSpec((seg_len, array.shape[1]), lambda i, core: (i, 0)) for array, _, _ in terms]
    right = []
    for array, matrix, at in terms:
        if transposed:
            right.append(pl.BlockSpec((width, array.shape[1]), lambda i, core, at=at: (0, at(core[0]))))
        else:
            right.append(pl.BlockSpec(matrix.shape, lambda i, core: (0, 0)))
    depth = sum(array.shape[1] for array, _, _ in terms)
    mine, theirs = pl.pallas_call(
        lambda *refs: half_kernel(transposed, len(terms), *refs),
        grid_spec=pltpu.PrefetchScalarGridSpec(
            num_scalar_prefetch=1,
            grid=(length // seg_len,),
            in_specs=left + right + [pl.BlockSpec((seg_len, width), lambda i, core: (i, 0)) for _ in base],
            out_specs=[pl.BlockSpec((1, seg_len, width), lambda i, core: (i // 2, 0, 0))] * 2,
        ),
        out_shape=(
            jax.ShapeDtypeStruct((length // seg_len // 2, seg_len, width), f32),
            jax.ShapeDtypeStruct((length // seg_len // 2, seg_len, width), bf16),
        ),
        compiler_params=pltpu.CompilerParams(dimension_semantics=("arbitrary",), vmem_limit_bytes=VMEM_LIMIT),
        cost_estimate=LIGHT,
    )(core.reshape(1).astype(jnp.int32), *[array for array, _, _ in terms], *[matrix for _, matrix, _ in terms], *base)
    return mine, theirs


def shared_kernel(core_ref, proj_ref, rim_ref, taps_ref, mine_ref, other_ref, grad_ref, taps_grad_ref, edge_ref):
    total, seen = conv_parts(proj_ref[...], rim_ref[...], taps_ref[...])
    sigmoid = jax.nn.sigmoid(total)
    grad_total = mine_ref[...] + other_ref[...]
    grad_total = grad_total * (sigmoid * (1.0 + total * (1.0 - sigmoid)))
    sums = [jnp.sum(grad_total * part, axis=0, keepdims=True) for part in seen]
    sums = sums + [jnp.sum(grad_total, axis=0, keepdims=True), jnp.zeros((8 - CONV - 1, LANES), f32)]
    taps_grad_ref[...] = jnp.concatenate(sums, axis=0)
    edge_ref[...] = grad_total[:8]
    taps = taps_ref[...]
    extended = jnp.concatenate([grad_total, jnp.zeros((8, LANES), f32)], axis=0)
    grad_conv = taps[CONV - 1 : CONV] * grad_total
    for k in range(CONV - 1):
        grad_conv = grad_conv + taps[k : k + 1] * extended[CONV - 1 - k : CONV - 1 - k + grad_total.shape[0]]
    grad_ref[...] = grad_conv.astype(bf16)


def shared_backward(core, proj, rim, taps, mine, other):
    length = proj.shape[0]
    picked = lambda rows: pl.BlockSpec((rows, LANES), lambda i, core: (0, HALF // LANES + core[0]))
    whole = lambda rows: pl.BlockSpec((rows, LANES), lambda i, core: (0, 0))
    return pl.pallas_call(
        shared_kernel,
        grid_spec=pltpu.PrefetchScalarGridSpec(
            num_scalar_prefetch=1,
            grid=(1,),
            in_specs=[picked(length), picked(8), picked(8), whole(length), whole(length)],
            out_specs=(whole(length), whole(8), whole(8)),
        ),
        out_shape=(
            jax.ShapeDtypeStruct((length, LANES), bf16),
            jax.ShapeDtypeStruct((8, LANES), f32),
            jax.ShapeDtypeStruct((8, LANES), f32),
        ),
        compiler_params=pltpu.CompilerParams(vmem_limit_bytes=VMEM_LIMIT),
        cost_estimate=LIGHT,
    )(core.reshape(1).astype(jnp.int32), proj, rim, taps, mine, other)


def per_device(hidden_in, cotangent, in_proj, out_proj, conv_params, pre_gain, gated_gain, head_params):
    chips, line = lax.axis_size("chip"), lax.axis_size("seg")
    core, place = lax.axis_index("core"), lax.axis_index("seg")
    rows, model_width = in_proj.shape[0], hidden_in.shape[2]
    heads = HEADS // 2

    conv_width, gain_width = conv_params.shape[1], gated_gain.shape[0]
    used = HALF + 2 * STATE + heads
    spare = -used % LANES
    small = jnp.zeros((rows, spare), bf16)
    small = small.at[: CONV + 1, :conv_width].set(conv_params)
    small = small.at[CONV + 1, :rows].set(pre_gain)
    small = small.at[CONV + 2, :gain_width].set(gated_gain)

    def conv_side(which):
        return jnp.concatenate(
            [
                own_columns(in_proj[:, INNER : 2 * INNER], which),
                in_proj[:, 2 * INNER : INNER + XBC],
                own_columns(in_proj[:, INNER + XBC :], which),
                small,
            ],
            axis=1,
        )

    def gate_side(which):
        return own_columns(in_proj[:, :INNER], which)

    conv_swap = to_partner(conv_side(1 - core))
    conv_block = in_core_order(conv_side(core), conv_swap, core, 0)
    conv_z = gather_step(conv_block, 2)
    gate_swap = to_partner(gate_side(1 - core))
    gate_block = in_core_order(gate_side(core), gate_swap, core, 0)
    conv_z, hidden_in, gate_block = tie(conv_z, hidden_in, gate_block)
    conv_own = jnp.stack(conv_z)
    conv_near = gather_plane(conv_own, near_steps())
    hidden_half = whole_sequence(hidden_in, core, place)
    conv_own, conv_near, hidden_half, gate_block = tie(conv_own, conv_near, hidden_half, gate_block)
    conv_far = gather_plane(conv_own, far_steps())
    gate_z = gather_step(gate_block, 2)
    hidden_other = to_partner(hidden_half)
    conv_far, gate_z, hidden_other, cotangent = tie(conv_far, gate_z, hidden_other, cotangent)
    cot_half = whole_sequence(cotangent, core, place)
    gate_own = jnp.stack(gate_z)
    gate_near = gather_plane(gate_own, near_steps())
    conv_all = whole_matrix([conv_own, *conv_near, *conv_far], True)

    small_all = conv_all.reshape(chips, 2, line, rows, -1)[..., used:].astype(f32)
    taps_full = small_all[..., : CONV + 1, :conv_width].transpose(3, 0, 1, 2, 4).reshape(CONV + 1, XBC)
    taps = jnp.concatenate([own_columns(taps_full[:, :INNER], core), taps_full[:, INNER:]], axis=1)
    gain_pre = small_all[..., CONV + 1, :rows].reshape(model_width)
    gain_gate = lax.dynamic_index_in_dim(
        small_all[..., CONV + 2, :gain_width], core, axis=1, keepdims=False
    ).reshape(HALF)
    params = own_columns(head_params, core)

    seg_len = hidden_half.shape[1]
    tokens = SEGS * seg_len
    normed, normed_turned = normed_tokens(core, hidden_half, hidden_other, gain_pre, rows)
    projected = dot(normed, conv_all, ((1,), (0,)))
    projected, gate_own, gate_near, out_proj = tie(projected, gate_own, gate_near, out_proj)
    gate_far = gather_plane(gate_own, far_steps())
    out_z = gather_step(out_proj, 2)

    taps = jnp.pad(taps, ((0, 8 - CONV - 1), (0, projected.shape[1] - taps.shape[1])))
    head = jnp.pad(jnp.stack([-jnp.exp(params[0]), params[1]]), ((0, 6), (0, LANES - heads)))
    skip = jnp.repeat(params[2], HEADDIM).reshape(1, HALF)
    wide = HALF + 2 * STATE
    rim = borrowed(projected[tokens - 8 :], 1)
    nothing = jnp.zeros((STATE, HALF), f32)
    values, prior, final, last = scan_forward(projected, taps, head, skip, rim, nothing, seg_len)
    if line > SEGS:
        last = jnp.sum(last.reshape(SEGS, 8, LANES)[:, 0, :heads], axis=0)
        decay = jnp.repeat(jnp.exp2(last), HEADDIM)
        begin = entering(decay, final, 1)
        values, prior, _, _ = scan_forward(projected, taps, head, skip, rim, begin, seg_len)

    values, gate_far, out_z, cot_half = tie(values, gate_far, out_z, cot_half)
    out_own = jnp.stack(out_z)
    out_near = gather_plane(out_own, near_steps())
    cot_other = to_partner(cot_half)
    gate_matrix = whole_matrix([gate_own, *gate_near, *gate_far], True)
    gate_input = dot(normed, gate_matrix, ((1,), (0,)))
    gate_input, out_own, out_near = tie(gate_input, out_own, out_near)
    out_far = gather_plane(out_own, far_steps())

    silu_gate = jax.nn.silu(gate_input)
    gated = values * silu_gate
    squares = jnp.sum(gated * gated, axis=1)
    squares_other = to_partner(squares)
    scale = lax.rsqrt((squares + squares_other) / INNER + epsilon)[:, None]
    mixed, mixed_turned = mixed_tokens(gated, scale, gain_gate, seg_len)
    mixed_turned, out_far = tie(mixed_turned, out_far)
    cot = in_core_order(cot_half, cot_other, core, 1)
    upstream = cot.reshape(tokens, model_width)
    by_owner = lambda grad: grad.astype(bf16).reshape(chip_dims() + (-1, grad.shape[1]))
    out_grad = by_owner(dot(mixed_turned, upstream, ((1,), (0,))))
    out_got_near = reduce_plane([out_grad], near_steps())
    out_matrix = whole_matrix([out_own, *out_near, *out_far], False)
    branch, branch_sent = half_products(core, [(mixed, out_matrix, None)], seg_len, model_width, False)
    branch_sent, upstream = tie(branch_sent, upstream)
    branch_other = to_partner(branch_sent)
    grad_mixed = dot(upstream, out_matrix, ((1,), (1,)))
    grad_mixed, out_got_near, out_grad = tie(grad_mixed, out_got_near, out_grad)
    out_got_far = reduce_plane([out_grad], far_steps())
    unit = gated * scale
    gain_grad = grad_mixed * gain_gate
    along = jnp.sum(gain_grad * unit, axis=1)
    along_other = to_partner(along)
    along_other, branch_other = tie(along_other, branch_other)
    hidden_out = back_to_owner(
        (hidden_half.astype(f32) + branch + branch_other.astype(f32)).astype(bf16), core, place
    )
    along = ((along + along_other) / INNER)[:, None]
    gate_gain_grad = jnp.sum(grad_mixed * unit, axis=0)
    grad_gated = scale * (gain_grad - unit * along)
    grad_values = grad_gated * silu_gate
    sigmoid = jax.nn.sigmoid(gate_input)
    grad_gate = (grad_gated * values * (sigmoid * (1.0 + gate_input * (1.0 - sigmoid)))).astype(bf16)
    gate_grad = by_owner(dot(normed_turned, grad_gate, ((1,), (0,))))
    gate_grad, grad_values, out_got_far = tie(gate_grad, grad_values, out_got_far)
    gate_got = reduce_plane([gate_grad], plane_steps())
    scan = lambda later: scan_backward(
        0, core, projected, taps, head, skip, rim, later, prior, values, grad_values, seg_len
    )
    if line > SEGS:
        nothing = entering(decay, scan(nothing)[-1], -1)
    back = scan(nothing)
    back, gate_got, hidden_out, grad_gate = tie(back, gate_got, hidden_out, grad_gate)
    ((early_kept, early_got),) = reduce_z(
        [
            ([plane_part([out_grad], 0, 0)], [*out_got_near, *out_got_far]),
            ([plane_part([gate_grad], 0, 0)], gate_got),
        ]
    )
    grad_x, mine, theirs, grad_raw, x_taps_grad, skip_grad, head_sums, x_edge, _ = back
    grad_x = spilled(grad_x, x_edge, taps[:, :HALF])
    other = to_partner(theirs)
    x_grad = by_owner(dot(normed_turned, grad_x, ((1,), (0,))))
    other, x_grad = tie(other, x_grad)
    grad_state, state_taps_grad, state_edge = shared_backward(core, projected, rim, taps, mine, other)
    grad_state = spilled(grad_state, state_edge, lax.dynamic_slice_in_dim(taps, HALF + core * STATE, STATE, axis=1))
    grad_raw = grad_raw.astype(bf16)
    rest_grad = by_owner(dot(normed_turned, jnp.concatenate([grad_state, grad_raw], axis=1), ((1,), (0,))))
    rest_grad, x_grad, grad_gate, nearest = tie(rest_grad, x_grad, grad_gate, early_got[:1])
    conv_near = reduce_plane([x_grad, rest_grad], near_steps())
    base = dot(grad_gate, gate_matrix, ((1,), (1,)))
    terms = [
        (grad_x, conv_all, lambda core: 0),
        (grad_state, conv_all, lambda core: HALF // LANES + core),
        (grad_raw, conv_all, lambda core: (HALF + 2 * STATE) // LANES),
    ]
    grad_normed, sent_normed = half_products(core, terms, seg_len, model_width, True, (base,))
    row = lax.broadcasted_iota(jnp.int32, (8, 1), 0)
    small = x_taps_grad + jnp.where(row == CONV + 1, gate_gain_grad, 0.0) + jnp.where(row == CONV + 2, skip_grad, 0.0)
    small = jnp.concatenate([small, state_taps_grad + head_sums], axis=1)
    sent_normed, others, conv_near, small, x_grad, rest_grad = tie(
        sent_normed, early_got[1:], conv_near, small, x_grad, rest_grad
    )
    conv_far = reduce_plane([x_grad, rest_grad], far_steps())
    other_normed = to_partner(sent_normed)
    wide_hidden = hidden_half.astype(f32)
    hidden_scale = lax.rsqrt(jnp.mean(wide_hidden * wide_hidden, axis=-1, keepdims=True) + epsilon)
    grad_normed = (grad_normed + other_normed.astype(f32)) * gain_pre
    hidden_unit = wide_hidden * hidden_scale
    along = jnp.mean(grad_normed * hidden_unit, axis=-1, keepdims=True)
    grad_hidden = hidden_scale * (grad_normed - hidden_unit * along)
    grad_in = (cot_half.astype(f32) + grad_hidden).astype(bf16)
    grad_in = back_to_owner(grad_in, core, place)
    grad_in, conv_far = tie(grad_in, conv_far)
    late = reduce_z([([plane_part([x_grad, rest_grad], 0, 0)], [*conv_near, *conv_far])])
    for dim in range(3):
        small = small + sum(moved(small, dim, by) for by in range(1, chip_dims()[dim]))
    small_other = to_partner(small)
    late_got, small_other = tie(arrivals(late), small_other)
    early_share = total([*early_kept, *nearest, *others])
    out_share = early_share[:, :model_width]
    paired = lambda share: share.astype(bf16).reshape(2, rows, -1)
    gate_share, conv_share = paired(early_share[:, model_width:]), paired(reduce_end(arrived(late, late_got)))

    def mine_and_partner(share):
        keep = lax.dynamic_index_in_dim(share, core, axis=0, keepdims=False)
        give = lax.dynamic_index_in_dim(share, 1 - core, axis=0, keepdims=False)
        return keep, to_partner(give)

    both = in_core_order(small, small_other, core, 0)
    natural = lambda array, width: array.reshape(2, -1, chips, width).transpose(1, 2, 0, 3).reshape(-1, 2 * chips * width)
    device = (lax.axis_index("chip") * 2 + core) * line + place
    columns = natural(both[:, :, :HALF], HALF // chips)
    taps_all = jnp.concatenate([columns, both[0, :, HALF:], both[1, :, HALF:]], axis=1)[: CONV + 1]
    taps_share = lax.dynamic_slice_in_dim(taps_all, device * conv_width, conv_width, axis=1)
    gain_share = lax.dynamic_slice_in_dim(columns[CONV + 1], device * gain_width, gain_width, axis=0)
    head_total = jnp.concatenate(
        [
            natural(both[:, CONV + 1 : CONV + 3, HALF : HALF + heads], heads // chips),
            jnp.sum(columns[CONV + 2].reshape(1, HEADS, HEADDIM), axis=2),
        ]
    )

    def interleave(mine, theirs):
        width = mine.shape[1] // chips
        both = in_core_order(mine.reshape(rows, chips, width), theirs.reshape(rows, chips, width), core, 2)
        return both.reshape(rows, -1)

    keep_gate, got_gate = mine_and_partner(gate_share)
    keep, got = mine_and_partner(conv_share)
    state_end = HALF + STATE
    in_share = jnp.concatenate(
        [
            interleave(keep_gate, got_gate),
            interleave(keep[:, :HALF], got[:, :HALF]),
            in_core_order(keep[:, HALF:state_end], got[:, HALF:state_end], core, 1).reshape(rows, -1),
            interleave(keep[:, state_end : state_end + heads], got[:, state_end : state_end + heads]),
        ],
        axis=1,
    ).astype(f32)
    pre_share = jnp.sum(in_proj.astype(f32) * in_share, axis=1) / pre_gain.astype(f32)
    return (hidden_out, grad_in, in_share, out_share, taps_share, pre_share, gain_share, head_total)


def solution(mesh):
    devices = mesh.devices
    cores = Mesh(devices.reshape(devices.shape[0] // 2, 2, devices.shape[1]), ("chip", "core", "seg"))
    dp, both = ("chip", "core"), ("chip", "core", "seg")
    tokens = P(dp, "seg", None)
    return jax.shard_map(
        per_device,
        mesh=cores,
        in_specs=(tokens, tokens, P(both, None), P(both, None), P(None, both), P(both), P(both), P()),
        out_specs=(tokens, tokens, P(both, None), P(both, None), P(None, both), P(both), P(both), P()),
        check_vma=False,
    )
```

```python
import jax
import jax.numpy as jnp
from jax import lax
from jax.experimental import pallas as pl
from jax.experimental.pallas import tpu as pltpu
from jax.sharding import Mesh
from jax.sharding import PartitionSpec as P

HEADS = 48
HEADDIM = 64
STATE = 128
CONV = 4
INNER = 3072
XBC = 3328
HALF = INNER // 2
LANES = 128
SEGS = 4
LIGHT = pl.CostEstimate(flops=1024, bytes_accessed=1024, transcendentals=0)
VMEM_LIMIT = 48 * 1024 * 1024
LOG2E = 1.4426950408889634

epsilon = 1e-05
f32 = jnp.float32
bf16 = jnp.bfloat16


def own_columns(array, core):
    chips = lax.axis_size("chip")
    width = array.shape[-1] // (2 * chips)
    parted = array.reshape(array.shape[:-1] + (chips, 2, width))
    picked = lax.dynamic_index_in_dim(parted, core, axis=parted.ndim - 2, keepdims=False)
    return picked.reshape(array.shape[:-1] + (chips * width,))


def to_partner(array):
    return lax.ppermute(array, "core", [(0, 1), (1, 0)])


def in_core_order(mine, theirs, core, axis):
    first = jnp.where(core == 0, mine, theirs)
    second = jnp.where(core == 0, theirs, mine)
    return jnp.stack([first, second], axis=axis)


def chip_dims():
    return (lax.axis_size("chip") // 2, 2, lax.axis_size("seg"))


def chip_place():
    chip = lax.axis_index("chip")
    return (chip // 2, chip % 2, lax.axis_index("seg"))


def moved(array, dim, by):
    sizes = chip_dims()
    index = lambda at: (at[0] * sizes[1] + at[1]) * sizes[2] + at[2]
    pairs = []
    for a in range(sizes[0]):
        for b in range(sizes[1]):
            for z in range(sizes[2]):
                to = [a, b, z]
                to[dim] = (to[dim] + by) % sizes[dim]
                pairs.append((index((a, b, z)), index(to)))
    return lax.ppermute(array, ("chip", "seg"), pairs)


def tie(*values):
    return lax.optimization_barrier(values)


def gather_step(data, dim):
    return [data] + [moved(data, dim, by) for by in range(1, chip_dims()[dim])]


def exchanged(array, by):
    line = lax.axis_size("seg")
    return lax.ppermute(array, "seg", [(at, at ^ by) for at in range(line)])


def plane_steps():
    a, b, _ = chip_dims()
    steps = [(at // b, at % b) for at in range(1, a * b)]
    return sorted(steps, key=lambda by: bool(by[0] and by[1]))


def near_steps():
    a, b, _ = chip_dims()
    return plane_steps()[: a + b - 2]


def far_steps():
    a, b, _ = chip_dims()
    return plane_steps()[a + b - 2 :]


def moved_plane(array, by_a, by_b):
    a, b, z = chip_dims()
    pairs = [
        ((at_a * b + at_b) * z + at_z, ((at_a + by_a) % a * b + (at_b + by_b) % b) * z + at_z)
        for at_a in range(a)
        for at_b in range(b)
        for at_z in range(z)
    ]
    return lax.ppermute(array, ("chip", "seg"), pairs)


def gather_plane(data, steps):
    return [moved_plane(data, *by) for by in steps]


def placed_kernel(plan, place_ref, *refs):
    sources, target, sems = refs[:-2], refs[-2], refs[-1]
    copies = []
    for source, lead, at, paired in plan:
        spot = [lax.rem(place_ref[dim] + (size - back), size) for dim, (back, size) in enumerate(at)]
        spot.append(place_ref[2 + lead])
        to = target.at[spot[0], spot[1], :, spot[2]] if paired else target.at[spot[0], spot[1], spot[2]]
        copies.append(pltpu.make_async_copy(sources[source].at[lead], to, sems.at[len(copies)]))
    for copy in copies:
        copy.start()
    for copy in copies:
        copy.wait()


def whole_matrix(gathered, paired, by_bits=False):
    a, b, z = chip_dims()
    at_a, at_b, at_z = chip_place()
    spots = [at_z ^ back if by_bits else (at_z + z - back) % z for back in range(z)]
    plan = [
        (source, back, ((by[0], a), (by[1], b)), paired)
        for source, by in enumerate([(0, 0)] + plane_steps())
        for back in range(z)
    ]
    block = gathered[0].shape[1:]
    shape = (a, b, 2, z) + block[1:] if paired else (a, b, z) + block
    anywhere = pl.BlockSpec(memory_space=pl.ANY)
    whole = pl.pallas_call(
        lambda *refs: placed_kernel(plan, *refs),
        out_shape=jax.ShapeDtypeStruct(shape, bf16),
        in_specs=[pl.BlockSpec(memory_space=pltpu.SMEM)] + [anywhere] * len(gathered),
        out_specs=pl.BlockSpec(memory_space=pltpu.VMEM),
        scratch_shapes=[pltpu.SemaphoreType.DMA((len(plan),))],
        compiler_params=pltpu.CompilerParams(vmem_limit_bytes=VMEM_LIMIT),
        cost_estimate=LIGHT,
    )(jnp.stack([at_a, at_b, *spots]).astype(jnp.int32), *gathered)
    return whole.reshape(-1, shape[-1])


def total(terms):
    result = terms[0].astype(f32)
    for term in terms[1:]:
        result = result + term.astype(f32)
    return result


def reduce_send(terms, axis, dim, wire):
    place, size = chip_place()[dim], chip_dims()[dim]
    pick = lambda at: [lax.dynamic_index_in_dim(term, at, axis=axis, keepdims=False) for term in terms]
    received = [moved(total(pick((place + by) % size)).astype(wire), dim, by) for by in range(1, size)]
    return pick(place), received


def plane_part(partials, by_a, by_b):
    (at_a, at_b, _), (a, b, _) = chip_place(), chip_dims()
    chip = (at_a + by_a) % a * b + (at_b + by_b) % b
    flat = [partial.reshape((a * b,) + partial.shape[2:]) for partial in partials]
    return jnp.concatenate([lax.dynamic_index_in_dim(array, chip, axis=0, keepdims=False) for array in flat], axis=-1)


def reduce_plane(partials, steps):
    return [moved_plane(plane_part(partials, *by), *by) for by in steps]


def reduce_z(firsts):
    joined = jnp.concatenate([total(kept + received) for kept, received in firsts], axis=-1)
    return [reduce_send([joined], 0, 2, bf16)]


def reduce_end(third):
    return total(third[0][0] + third[0][1])


def arrivals(parts):
    return [received for _, received in parts]


def arrived(parts, received):
    return [(kept, new) for (kept, _), new in zip(parts, received)]


def line_perm(turn, back):
    line = lax.axis_size("seg")
    parts = line // SEGS
    pairs = []
    for core in range(2):
        for place in range(line):
            half, odd = divmod(place % SEGS, 2)
            source = core * line + place
            target = odd * line + (2 * core + (half ^ turn)) * parts + place // SEGS
            pairs.append((target, source) if back else (source, target))
    return pairs


def swapped(pair, turn):
    return [jnp.where(turn == 0, pair[0], pair[1]), jnp.where(turn == 0, pair[1], pair[0])]


def send_sequence(array, place):
    pieces = swapped([array[0], array[1]], (place % SEGS) // 2)
    return [lax.ppermute(piece, ("core", "seg"), line_perm(turn, False)) for turn, piece in enumerate(pieces)]


def order_sequence(got, place):
    parts = lax.axis_size("seg") // SEGS
    return jnp.stack(swapped(got, (place // parts) % 2))


def send_back(ordered, place):
    parts = lax.axis_size("seg") // SEGS
    pieces = swapped([ordered[0], ordered[1]], (place // parts) % 2)
    return [lax.ppermute(piece, ("core", "seg"), line_perm(turn, True)) for turn, piece in enumerate(pieces)]


def order_back(got, place):
    return jnp.stack(swapped(got, (place % SEGS) // 2))


def part_pairs(step):
    line = lax.axis_size("seg")
    parts = line // SEGS
    return [(i, i + step) for i in range(line) if 0 <= i + step < line and i // parts == (i + step) // parts]


def entering(decay, state, step):
    parts = lax.axis_size("seg") // SEGS
    total = jnp.zeros_like(state)
    for _ in range(parts - 1):
        total = lax.ppermute(decay * total + state, "seg", part_pairs(step))
    return total


def borrowed(array, step):
    parts = lax.axis_size("seg") // SEGS
    if parts == 1:
        return jnp.zeros_like(array)
    return lax.ppermute(array, "seg", part_pairs(step))


def spilled(grad, edge, taps):
    if lax.axis_size("seg") == SEGS:
        return grad
    edge = borrowed(edge, -1)
    spill = jnp.stack(
        [
            sum(taps[k] * edge[CONV - 1 - k - early] for k in range(CONV - early))
            for early in range(CONV - 1, 0, -1)
        ]
    )
    at = grad.shape[0] - CONV + 1
    return grad.at[at:].set((grad[at:].astype(f32) + spill).astype(bf16))


def dot(a, b, contract):
    return lax.dot_general(a, b, (contract, ((), ())), preferred_element_type=f32)


def normed_kernel(slabs, core_ref, mine_ref, other_ref, gain_ref, normed_ref, turned_ref):
    own = lax.rem(pl.program_id(0), 2) == core_ref[0]
    hidden = jnp.where(own, mine_ref[0], other_ref[0]).astype(f32)
    scale = lax.rsqrt(jnp.mean(hidden * hidden, axis=1, keepdims=True) + epsilon)
    normed = hidden * scale * gain_ref[...]
    normed_ref[...] = normed.astype(bf16)
    turned = normed.T.astype(bf16)
    for to, at, size in slabs:
        turned_ref[to : to + size] = turned[at : at + size]


def normed_tokens(core, mine, other, gain, rows):
    segs, seg_len, width = 2 * mine.shape[0], mine.shape[1], mine.shape[2]
    a, b, z = chip_dims()
    group = 2 * z * rows
    inside = rows % 16 == 0
    slabs = [(0, 0, width)]
    if inside:
        slabs = [
            (chip * group + (at * 2 + core_at) * rows, chip * group + (core_at * z + at) * rows, rows)
            for chip in range(a * b)
            for core_at in range(2)
            for at in range(z)
        ]
    normed, turned = pl.pallas_call(
        lambda *refs: normed_kernel(slabs, *refs),
        grid_spec=pltpu.PrefetchScalarGridSpec(
            num_scalar_prefetch=1,
            grid=(segs,),
            in_specs=[
                pl.BlockSpec((1, seg_len, width), lambda i, core: (i // 2, 0, 0)),
                pl.BlockSpec((1, seg_len, width), lambda i, core: (i // 2, 0, 0)),
                pl.BlockSpec((1, width), lambda i, core: (0, 0)),
            ],
            out_specs=(
                pl.BlockSpec((seg_len, width), lambda i, core: (i, 0)),
                pl.BlockSpec((width, seg_len), lambda i, core: (0, i)),
            ),
        ),
        out_shape=(
            jax.ShapeDtypeStruct((segs * seg_len, width), bf16),
            jax.ShapeDtypeStruct((width, segs * seg_len), bf16),
        ),
        compiler_params=pltpu.CompilerParams(dimension_semantics=("arbitrary",), vmem_limit_bytes=VMEM_LIMIT),
        cost_estimate=LIGHT,
    )(core.reshape(1).astype(jnp.int32), mine, other, gain.reshape(1, width))
    if not inside:
        turned = turned.reshape(a, b, 2, z, rows, -1).transpose(0, 1, 3, 2, 4, 5).reshape(turned.shape)
    return normed, turned


def mixed_kernel(gated_ref, scale_ref, gain_ref, mixed_ref, turned_ref):
    mixed = gated_ref[...] * scale_ref[...] * gain_ref[...]
    mixed_ref[...] = mixed.astype(bf16)
    turned_ref[...] = mixed.T.astype(bf16)


def mixed_tokens(gated, scale, gain, seg_len):
    length, width = gated.shape
    return pl.pallas_call(
        mixed_kernel,
        grid=(length // seg_len,),
        in_specs=[
            pl.BlockSpec((seg_len, width), lambda i: (i, 0)),
            pl.BlockSpec((seg_len, 1), lambda i: (i, 0)),
            pl.BlockSpec((1, width), lambda i: (0, 0)),
        ],
        out_specs=(
            pl.BlockSpec((seg_len, width), lambda i: (i, 0)),
            pl.BlockSpec((width, seg_len), lambda i: (0, i)),
        ),
        out_shape=(
            jax.ShapeDtypeStruct((length, width), bf16),
            jax.ShapeDtypeStruct((width, length), bf16),
        ),
        compiler_params=pltpu.CompilerParams(dimension_semantics=("arbitrary",), vmem_limit_bytes=VMEM_LIMIT),
        cost_estimate=LIGHT,
    )(gated, scale, gain.reshape(1, width))


def columns_of(pair):
    return pl.ds(pair * LANES, LANES)


def low_half(shape):
    return lax.broadcasted_iota(jnp.int32, shape, len(shape) - 1) < HEADDIM


def pair_columns(array, pair, low):
    rows = array.shape[0]
    first = jnp.broadcast_to(array[:, 2 * pair : 2 * pair + 1], (rows, LANES))
    second = jnp.broadcast_to(array[:, 2 * pair + 1 : 2 * pair + 2], (rows, LANES))
    return jnp.where(low, first, second)


def conv_parts(current, before, taps):
    rows = current.shape[0]
    padded = jnp.concatenate([before, current], axis=0)
    seen = [padded[8 - CONV + 1 + k : 8 - CONV + 1 + k + rows] for k in range(CONV - 1)] + [current]
    total = taps[CONV : CONV + 1]
    for k in range(CONV):
        total = total + taps[k : k + 1] * seen[k]
    return total, seen


def step_terms(raw, head, seg_len):
    shifted = raw + head[1:2]
    step = jnp.maximum(shifted, 0.0) + jnp.log1p(jnp.exp(-jnp.abs(shifted)))
    log_decay = step * head[0:1]
    at_or_before = lax.broadcasted_iota(jnp.int32, (seg_len, seg_len), 0) >= lax.broadcasted_iota(
        jnp.int32, (seg_len, seg_len), 1
    )
    sums = lax.dot_general(
        jnp.where(at_or_before, 1.0, 0.0), log_decay, (((1,), (0,)), ((), ())),
        precision=lax.Precision.HIGHEST, preferred_element_type=f32,
    )
    return shifted, step, log_decay, sums * LOG2E


def forward_kernel(
    proj_ref, taps_ref, head_ref, skip_ref, rim_ref, init_ref,
    values_ref, prior_ref, final_ref, last_ref, state_ref, tail_ref,
):
    seg_len = proj_ref.shape[0]
    half = seg_len // 2

    @pl.when(pl.program_id(0) == 0)
    def _():
        state_ref[...] = init_ref[...]
        tail_ref[...] = rim_ref[...]

    def activated(begin):
        at = pl.ds(begin, LANES)
        total, _ = conv_parts(proj_ref[:, at], tail_ref[:, at], taps_ref[:, at])
        return total * jax.nn.sigmoid(total)

    b_low = activated(HALF).astype(bf16)
    b_turned = activated(HALF).T.astype(bf16)
    c_low = activated(HALF + STATE).astype(bf16)
    _, step, _, sums = step_terms(proj_ref[:, HALF + 2 * STATE :], head_ref, seg_len)
    sums_turned, step_turned = sums.T, step.T
    scores = dot(c_low, b_low, ((1,), (1,)))
    kept = lax.broadcasted_iota(jnp.int32, (half, half), 0) >= lax.broadcasted_iota(jnp.int32, (half, half), 1)
    first_scores = jnp.where(kept, scores[:half, :half], 0.0)
    later_scores = scores[half:, :half]
    second_scores = jnp.where(kept, scores[half:, half:], 0.0)
    low = low_half((seg_len, LANES))
    last_ref[...] = jnp.broadcast_to(sums[seg_len - 1 :], last_ref.shape)

    for pair in range(HEADS // 4):
        at = columns_of(pair)
        x_values = activated(pair * LANES)
        x_low = x_values.astype(bf16)
        sums_pair = pair_columns(sums, pair, low)
        last_pair = sums_pair[seg_len - 1 :]
        carry = jnp.exp2(last_pair - sums_pair) * pair_columns(step, pair, low)
        scaled_x = (carry * x_low.astype(f32)).astype(bf16)
        prior = state_ref[:, at]
        prior_low = prior.astype(bf16)
        prior_ref[0, :, at] = prior_low
        from_state = jnp.exp2(sums_pair) * dot(c_low, prior_low, ((1,), (0,)))
        state_ref[:, at] = jnp.exp2(last_pair) * prior + dot(b_turned, scaled_x, ((1,), (0,)))
        early, late = 0.0, 0.0
        for side in range(2):
            head = 2 * pair + side
            x_side = jnp.where(low if side == 0 else ~low, x_values, 0.0).astype(bf16)
            at_token = jnp.broadcast_to(sums[:, head : head + 1], (seg_len, half))
            at_source, source_step = sums_turned[head : head + 1], step_turned[head : head + 1]
            first = jnp.exp2(jnp.minimum(at_token[:half] - at_source[:, :half], 0.0)) * first_scores
            first = (first * source_step[:, :half]).astype(bf16)
            later = jnp.exp2(at_token[half:] - at_source[:, :half]) * later_scores
            later = (later * source_step[:, :half]).astype(bf16)
            second = jnp.exp2(jnp.minimum(at_token[half:] - at_source[:, half:], 0.0)) * second_scores
            second = (second * source_step[:, half:]).astype(bf16)
            early = early + dot(first, x_side[:half], ((1,), (0,)))
            late = late + dot(jnp.concatenate([later, second], axis=1), x_side, ((1,), (0,)))
        intra = jnp.concatenate([early, late], axis=0)
        values_ref[:, at] = intra + from_state + skip_ref[:, at] * x_values

    tail_ref[...] = proj_ref[seg_len - 8 :, : HALF + 2 * STATE]
    final_ref[...] = state_ref[...]


def full_block(shape):
    return pl.BlockSpec(shape, lambda *_: (0,) * len(shape))


def scan_forward(proj, taps, head, skip, rim, init, seg_len):
    segs = proj.shape[0] // seg_len
    wide = HALF + 2 * STATE
    return pl.pallas_call(
        forward_kernel,
        grid=(segs,),
        out_shape=(
            jax.ShapeDtypeStruct((proj.shape[0], HALF), f32),
            jax.ShapeDtypeStruct((segs, STATE, HALF), bf16),
            jax.ShapeDtypeStruct((STATE, HALF), f32),
            jax.ShapeDtypeStruct((segs * 8, LANES), f32),
        ),
        in_specs=[
            pl.BlockSpec((seg_len, proj.shape[1]), lambda i: (i, 0)),
            full_block((8, wide)),
            full_block((8, LANES)),
            full_block((1, HALF)),
            full_block((8, wide)),
            full_block((STATE, HALF)),
        ],
        out_specs=(
            pl.BlockSpec((seg_len, HALF), lambda i: (i, 0)),
            pl.BlockSpec((1, STATE, HALF), lambda i: (i, 0, 0)),
            full_block((STATE, HALF)),
            pl.BlockSpec((8, LANES), lambda i: (i, 0)),
        ),
        scratch_shapes=[pltpu.VMEM((STATE, HALF), f32), pltpu.VMEM((8, wide), f32)],
        compiler_params=pltpu.CompilerParams(
            dimension_semantics=("arbitrary",), vmem_limit_bytes=VMEM_LIMIT
        ),
        cost_estimate=LIGHT,
    )(proj, taps, head, skip, rim, init)


def split_dot(array, other):
    high = array.astype(bf16)
    rest = (array - high.astype(f32)).astype(bf16)
    return dot(high, other, ((1,), (0,))) + dot(rest, other, ((1,), (0,)))


def backward_kernel(
    group, proj_ref, before_ref, taps_ref, rim_ref, shared_ref, shared_before_ref, shared_taps_ref, shared_rim_ref,
    head_ref, skip_ref, end_ref, prior_ref, values_ref, grad_ref, core_ref,
    grad_x_ref, mine_ref, theirs_ref, grad_raw_ref, taps_grad_ref, skip_grad_ref, head_grad_ref, edge_ref, start_ref,
    later_ref, local_ref, scaled_ref, grad_state_ref, inner_ref, source_ref, carry_ref, decay_ref,
):
    seg_len = proj_ref.shape[0]
    half = seg_len // 2
    turn = pl.program_id(0)

    @pl.when(turn == 0)
    def _():
        later_ref[...] = end_ref[...]
        edge_ref[...] = jnp.zeros_like(edge_ref)
        taps_grad_ref[...] = jnp.zeros_like(taps_grad_ref)
        skip_grad_ref[...] = jnp.zeros_like(skip_grad_ref)
        head_grad_ref[...] = jnp.zeros_like(head_grad_ref)

    first_segment = turn == pl.num_programs(0) - 1

    def conv_at(at, current, ahead, taps, rim):
        before = jnp.where(first_segment, rim[:, at], ahead[:, at])
        return conv_parts(current[:, at], before, taps[:, at])

    def activated(begin):
        total, _ = conv_at(pl.ds(begin, LANES), shared_ref, shared_before_ref, shared_taps_ref, shared_rim_ref)
        return total * jax.nn.sigmoid(total)

    b_values = activated(0)
    c_values = activated(STATE)
    b_low, c_low, c_turned = b_values.astype(bf16), c_values.astype(bf16), c_values.T.astype(bf16)
    shifted, step, log_decay, sums = step_terms(shared_ref[:, 2 * STATE :], head_ref, seg_len)
    sums_turned = sums.T
    scores = dot(b_low, c_low, ((1,), (1,)))
    kept = lax.broadcasted_iota(jnp.int32, (half, half), 0) <= lax.broadcasted_iota(jnp.int32, (half, half), 1)
    first_scores = jnp.where(kept, scores[:half, :half], 0.0)
    later_scores = scores[:half, half:]
    second_scores = jnp.where(kept, scores[half:, half:], 0.0)
    low = low_half((seg_len, LANES))
    first_grad, later_grad, second_grad = 0.0, 0.0, 0.0

    pairs = grad_ref.shape[1] // LANES
    for pair in range(pairs):
        at = columns_of(pair)
        total, seen = conv_at(at, proj_ref, before_ref, taps_ref, rim_ref)
        sigmoid = jax.nn.sigmoid(total)
        x_values = total * sigmoid
        x_low = x_values.astype(bf16)
        x_wide = x_low.astype(f32)
        sums_pair = pair_columns(sums, group * pairs + pair, low)
        step_pair = pair_columns(step, group * pairs + pair, low)
        last_pair = sums_pair[seg_len - 1 :]
        gap = jnp.exp2(last_pair - sums_pair)
        scaled_ref[:, at] = (gap * step_pair * x_wide).astype(bf16)
        grad_values = grad_ref[:, at]
        grad_state_ref[:, at] = (grad_values * jnp.exp2(sums_pair)).astype(bf16)
        later = later_ref[:, at]
        later_low = later.astype(bf16)
        local_ref[:, at] = later_low
        prior = prior_ref[0, :, at]
        decay_ref[:, at] = jnp.broadcast_to(
            jnp.sum(later * prior.astype(f32), axis=0, keepdims=True), (8, LANES)
        )
        grad_prior = dot(c_turned, grad_state_ref[:, at], ((1,), (0,)))
        later_ref[:, at] = jnp.exp2(last_pair) * later + grad_prior
        grad_scaled = dot(b_low, later_low, ((1,), (0,)))
        stepped = (step_pair * x_wide).astype(bf16)
        early, late = 0.0, 0.0
        for side in range(2):
            head = 2 * (group * pairs + pair) + side
            grad_low = jnp.where(low if side == 0 else ~low, grad_values, 0.0).astype(bf16)
            at_source = jnp.broadcast_to(sums[:, head : head + 1], (seg_len, half))
            at_token = sums_turned[head : head + 1]
            grad_weights = dot(stepped, grad_low, ((1,), (1,)))
            first = jnp.exp2(jnp.minimum(at_token[:, :half] - at_source[:half], 0.0))
            after = jnp.exp2(at_token[:, half:] - at_source[:half])
            second = jnp.exp2(jnp.minimum(at_token[:, half:] - at_source[half:], 0.0))
            first_grad = first_grad + first * grad_weights[:half, :half]
            later_grad = later_grad + after * grad_weights[:half, half:]
            second_grad = second_grad + second * grad_weights[half:, half:]
            upper = jnp.concatenate([first * first_scores, after * later_scores], axis=1).astype(bf16)
            early = early + dot(upper, grad_low, ((1,), (0,)))
            late = late + dot((second * second_scores).astype(bf16), grad_low[half:], ((1,), (0,)))
        inner = jnp.concatenate([early, late], axis=0)
        skip = skip_ref[:, at]
        skip_grad_ref[:, at] += jnp.sum(grad_values * x_values, axis=0, keepdims=True)
        inner_ref[:, at] = grad_values * (values_ref[:, at] - skip * x_values)
        source_ref[:, at] = x_wide * inner
        carry_ref[:, at] = x_wide * grad_scaled
        grad_x = skip * grad_values + step_pair * (inner + gap * grad_scaled)
        grad_total = grad_x * (sigmoid * (1.0 + total * (1.0 - sigmoid)))
        for k in range(CONV):
            taps_grad_ref[k : k + 1, at] += jnp.sum(grad_total * seen[k], axis=0, keepdims=True)
        taps_grad_ref[CONV : CONV + 1, at] += jnp.sum(grad_total, axis=0, keepdims=True)
        extended = jnp.concatenate([grad_total, edge_ref[:, at]], axis=0)
        edge_ref[:, at] = grad_total[:8]
        taps = taps_ref[:, at]
        grad_conv = taps[CONV - 1 : CONV] * grad_total
        for k in range(CONV - 1):
            grad_conv = grad_conv + taps[k : k + 1] * extended[CONV - 1 - k : CONV - 1 - k + seg_len]
        grad_x_ref[:, at] = grad_conv.astype(bf16)

    width = grad_ref.shape[1]
    channel = lax.broadcasted_iota(jnp.int32, (width, LANES), 0) // HEADDIM + group * width // HEADDIM
    heads = jnp.where(channel == lax.broadcasted_iota(jnp.int32, (width, LANES), 1), 1.0, 0.0).astype(bf16)
    tail = jnp.exp2(sums[seg_len - 1 :] - sums)
    source_grad = split_dot(source_ref[...], heads)
    step_grad = source_grad + tail * split_dot(carry_ref[...], heads)
    used = step * step_grad
    sum_grad = split_dot(inner_ref[...], heads) - used
    at_last = jnp.sum(used - step * source_grad, axis=0, keepdims=True)
    at_last = at_last + split_dot(decay_ref[...], heads)[:1] * jnp.exp2(sums[seg_len - 1 :])
    is_last = lax.broadcasted_iota(jnp.int32, (seg_len, LANES), 0) == seg_len - 1
    sum_grad = sum_grad + jnp.where(is_last, at_last, 0.0)
    at_or_after = lax.broadcasted_iota(jnp.int32, (seg_len, seg_len), 0) <= lax.broadcasted_iota(
        jnp.int32, (seg_len, seg_len), 1
    )
    log_grad = lax.dot_general(
        jnp.where(at_or_after, 1.0, 0.0), sum_grad, (((1,), (0,)), ((), ())),
        precision=lax.Precision.HIGHEST, preferred_element_type=f32,
    )
    grad_raw = (step_grad + head_ref[0:1] * log_grad) * jax.nn.sigmoid(shifted)
    grad_raw_ref[...] = grad_raw
    head_grad_ref[CONV + 1 : CONV + 2] += jnp.sum(log_grad * log_decay, axis=0, keepdims=True)
    head_grad_ref[CONV + 2 : CONV + 3] += jnp.sum(grad_raw, axis=0, keepdims=True)

    first_low = jnp.where(kept, first_grad, 0.0)
    second_low = jnp.where(kept, second_grad, 0.0)
    grad_scores = jnp.concatenate(
        [
            jnp.concatenate([first_low, later_grad], axis=1),
            jnp.concatenate([jnp.zeros_like(first_low), second_low], axis=1),
        ],
        axis=0,
    )
    start_ref[...] = later_ref[...]
    grad_b = dot(scaled_ref[...], local_ref[...], ((1,), (1,))) + dot(
        grad_scores.astype(bf16), c_low, ((1,), (0,))
    )
    grad_c = dot(grad_state_ref[...], prior_ref[0], ((1,), (1,))) + dot(
        grad_scores.T.astype(bf16), b_low, ((1,), (0,))
    )
    first = core_ref[0] == 0
    mine_ref[...] = jnp.where(first, grad_b, grad_c)
    theirs_ref[...] = jnp.where(first, grad_c, grad_b)


GROUPS = 1


def scan_backward(group, core, proj, taps, head, skip, rim, end, prior, values, grad_values, seg_len):
    length = proj.shape[0]
    segs = length // seg_len
    width, shared = HALF // GROUPS, proj.shape[1] - HALF
    back = lambda width, at=0: pl.BlockSpec((seg_len, width), lambda i: (segs - 1 - i, at))
    row_ahead = lambda i: jnp.maximum((segs - 1 - i) * (seg_len // 8) - 1, 0)
    ahead = lambda width, at: pl.BlockSpec((8, width), lambda i: (row_ahead(i), at))
    column = lambda rows, width, at: pl.BlockSpec((rows, width), lambda i: (0, at))
    both = HALF // shared
    return pl.pallas_call(
        lambda *refs: backward_kernel(group, *refs),
        grid=(segs,),
        out_shape=(
            jax.ShapeDtypeStruct((length, width), bf16),
            jax.ShapeDtypeStruct((length, STATE), f32),
            jax.ShapeDtypeStruct((length, STATE), f32),
            jax.ShapeDtypeStruct((length, LANES), f32),
            jax.ShapeDtypeStruct((8, width), f32),
            jax.ShapeDtypeStruct((1, width), f32),
            jax.ShapeDtypeStruct((8, LANES), f32),
            jax.ShapeDtypeStruct((8, width), f32),
            jax.ShapeDtypeStruct((STATE, width), f32),
        ),
        in_specs=[
            back(width, group),
            ahead(width, group),
            column(8, width, group),
            column(8, width, group),
            back(shared, both),
            ahead(shared, both),
            column(8, shared, both),
            column(8, shared, both),
            full_block((8, LANES)),
            column(1, width, group),
            column(STATE, width, group),
            pl.BlockSpec((1, STATE, width), lambda i: (segs - 1 - i, 0, group)),
            back(width, group),
            back(width, group),
            pl.BlockSpec(memory_space=pltpu.SMEM),
        ],
        out_specs=(
            back(width),
            back(STATE),
            back(STATE),
            back(LANES),
            full_block((8, width)),
            full_block((1, width)),
            full_block((8, LANES)),
            full_block((8, width)),
            full_block((STATE, width)),
        ),
        scratch_shapes=[
            pltpu.VMEM((STATE, width), f32),
            pltpu.VMEM((STATE, width), bf16),
            pltpu.VMEM((seg_len, width), bf16),
            pltpu.VMEM((seg_len, width), bf16),
            pltpu.VMEM((seg_len, width), f32),
            pltpu.VMEM((seg_len, width), f32),
            pltpu.VMEM((seg_len, width), f32),
            pltpu.VMEM((8, width), f32),
        ],
        compiler_params=pltpu.CompilerParams(
            dimension_semantics=("arbitrary",), vmem_limit_bytes=VMEM_LIMIT
        ),
        cost_estimate=LIGHT,
    )(
        proj, proj, taps, rim, proj, proj, taps, rim, head, skip, end, prior, values, grad_values,
        core.reshape(1).astype(jnp.int32),
    )


def half_kernel(transposed, count, core_ref, *refs):
    inputs, mine_ref, theirs_ref = refs[: 2 * count], refs[-2], refs[-1]
    total = refs[2 * count][...] if len(refs) > 2 * count + 2 else 0.0
    for left, right in zip(inputs[:count], inputs[count:]):
        total = total + dot(left[...], right[...], ((1,), (1 if transposed else 0,)))
    own = lax.rem(pl.program_id(0), 2) == core_ref[0]

    @pl.when(own)
    def _():
        mine_ref[0] = total

    @pl.when(jnp.logical_not(own))
    def _():
        theirs_ref[0] = total.astype(bf16)


def half_products(core, terms, seg_len, width, transposed, base=()):
    length = terms[0][0].shape[0]
    left = [pl.BlockSpec((seg_len, array.shape[1]), lambda i, core: (i, 0)) for array, _, _ in terms]
    right = []
    for array, matrix, at in terms:
        if transposed:
            right.append(pl.BlockSpec((width, array.shape[1]), lambda i, core, at=at: (0, at(core[0]))))
        else:
            right.append(pl.BlockSpec(matrix.shape, lambda i, core: (0, 0)))
    depth = sum(array.shape[1] for array, _, _ in terms)
    mine, theirs = pl.pallas_call(
        lambda *refs: half_kernel(transposed, len(terms), *refs),
        grid_spec=pltpu.PrefetchScalarGridSpec(
            num_scalar_prefetch=1,
            grid=(length // seg_len,),
            in_specs=left + right + [pl.BlockSpec((seg_len, width), lambda i, core: (i, 0)) for _ in base],
            out_specs=[pl.BlockSpec((1, seg_len, width), lambda i, core: (i // 2, 0, 0))] * 2,
        ),
        out_shape=(
            jax.ShapeDtypeStruct((length // seg_len // 2, seg_len, width), f32),
            jax.ShapeDtypeStruct((length // seg_len // 2, seg_len, width), bf16),
        ),
        compiler_params=pltpu.CompilerParams(dimension_semantics=("arbitrary",), vmem_limit_bytes=VMEM_LIMIT),
        cost_estimate=LIGHT,
    )(core.reshape(1).astype(jnp.int32), *[array for array, _, _ in terms], *[matrix for _, matrix, _ in terms], *base)
    return mine, theirs


def shared_kernel(core_ref, proj_ref, rim_ref, taps_ref, mine_ref, other_ref, grad_ref, taps_grad_ref, edge_ref):
    total, seen = conv_parts(proj_ref[...], rim_ref[...], taps_ref[...])
    sigmoid = jax.nn.sigmoid(total)
    grad_total = mine_ref[...] + other_ref[...]
    grad_total = grad_total * (sigmoid * (1.0 + total * (1.0 - sigmoid)))
    sums = [jnp.sum(grad_total * part, axis=0, keepdims=True) for part in seen]
    sums = sums + [jnp.sum(grad_total, axis=0, keepdims=True), jnp.zeros((8 - CONV - 1, LANES), f32)]
    taps_grad_ref[...] = jnp.concatenate(sums, axis=0)
    edge_ref[...] = grad_total[:8]
    taps = taps_ref[...]
    extended = jnp.concatenate([grad_total, jnp.zeros((8, LANES), f32)], axis=0)
    grad_conv = taps[CONV - 1 : CONV] * grad_total
    for k in range(CONV - 1):
        grad_conv = grad_conv + taps[k : k + 1] * extended[CONV - 1 - k : CONV - 1 - k + grad_total.shape[0]]
    grad_ref[...] = grad_conv.astype(bf16)


def shared_backward(core, proj, rim, taps, mine, other):
    length = proj.shape[0]
    picked = lambda rows: pl.BlockSpec((rows, LANES), lambda i, core: (0, HALF // LANES + core[0]))
    whole = lambda rows: pl.BlockSpec((rows, LANES), lambda i, core: (0, 0))
    return pl.pallas_call(
        shared_kernel,
        grid_spec=pltpu.PrefetchScalarGridSpec(
            num_scalar_prefetch=1,
            grid=(1,),
            in_specs=[picked(length), picked(8), picked(8), whole(length), whole(length)],
            out_specs=(whole(length), whole(8), whole(8)),
        ),
        out_shape=(
            jax.ShapeDtypeStruct((length, LANES), bf16),
            jax.ShapeDtypeStruct((8, LANES), f32),
            jax.ShapeDtypeStruct((8, LANES), f32),
        ),
        compiler_params=pltpu.CompilerParams(vmem_limit_bytes=VMEM_LIMIT),
        cost_estimate=LIGHT,
    )(core.reshape(1).astype(jnp.int32), proj, rim, taps, mine, other)


def per_device(hidden_in, cotangent, in_proj, out_proj, conv_params, pre_gain, gated_gain, head_params):
    chips, line = lax.axis_size("chip"), lax.axis_size("seg")
    core, place = lax.axis_index("core"), lax.axis_index("seg")
    rows, model_width = in_proj.shape[0], hidden_in.shape[2]
    heads = HEADS // 2

    conv_width, gain_width = conv_params.shape[1], gated_gain.shape[0]
    used = HALF + 2 * STATE + heads
    spare = -used % LANES
    small = jnp.zeros((rows, spare), bf16)
    small = small.at[: CONV + 1, :conv_width].set(conv_params)
    small = small.at[CONV + 1, :rows].set(pre_gain)
    small = small.at[CONV + 2, :gain_width].set(gated_gain)

    def conv_side(which):
        return jnp.concatenate(
            [
                own_columns(in_proj[:, INNER : 2 * INNER], which),
                in_proj[:, 2 * INNER : INNER + XBC],
                own_columns(in_proj[:, INNER + XBC :], which),
                small,
            ],
            axis=1,
        )

    def gate_side(which):
        return own_columns(in_proj[:, :INNER], which)

    conv_swap = to_partner(conv_side(1 - core))
    conv_block = in_core_order(conv_side(core), conv_swap, core, 0)
    conv_z = gather_step(conv_block, 2)
    gate_swap = to_partner(gate_side(1 - core))
    gate_block = in_core_order(gate_side(core), gate_swap, core, 0)
    conv_z, hidden_in, gate_block = tie(conv_z, hidden_in, gate_block)
    conv_own = jnp.stack(conv_z)
    conv_near = gather_plane(conv_own, near_steps())
    hidden_got = send_sequence(hidden_in, place)
    conv_own, conv_near, hidden_got, gate_block = tie(conv_own, conv_near, hidden_got, gate_block)
    hidden_half = order_sequence(hidden_got, place)
    conv_far = gather_plane(conv_own, far_steps())
    gate_z = gather_step(gate_block, 2)
    hidden_other = to_partner(hidden_half)
    conv_far, gate_z, hidden_other, out_proj = tie(conv_far, gate_z, hidden_other, out_proj)
    out_own = out_proj[None]
    out_other = exchanged(out_own, 1)
    gate_own = jnp.stack(gate_z)
    gate_near = gather_plane(gate_own, near_steps())
    conv_all = whole_matrix([conv_own, *conv_near, *conv_far], True)

    small_all = conv_all.reshape(chips, 2, line, rows, -1)[..., used:].astype(f32)
    taps_full = small_all[..., : CONV + 1, :conv_width].transpose(3, 0, 1, 2, 4).reshape(CONV + 1, XBC)
    taps = jnp.concatenate([own_columns(taps_full[:, :INNER], core), taps_full[:, INNER:]], axis=1)
    gain_pre = small_all[..., CONV + 1, :rows].reshape(model_width)
    gain_gate = lax.dynamic_index_in_dim(
        small_all[..., CONV + 2, :gain_width], core, axis=1, keepdims=False
    ).reshape(HALF)
    params = own_columns(head_params, core)

    seg_len = hidden_half.shape[1]
    tokens = SEGS * seg_len
    normed, normed_turned = normed_tokens(core, hidden_half, hidden_other, gain_pre, rows)
    projected = dot(normed, conv_all, ((1,), (0,)))
    projected, gate_own, gate_near, out_own, out_other = tie(projected, gate_own, gate_near, out_own, out_other)
    gate_far = gather_plane(gate_own, far_steps())
    out_own = jnp.concatenate([out_own, out_other])
    out_others = []
    for bit in range(1, (line - 1).bit_length()):
        out_others.append(exchanged(out_own, 2**bit))
        if 2 ** (bit + 1) < line:
            out_own, out_others = jnp.concatenate([out_own, out_others[-1]]), []

    taps = jnp.pad(taps, ((0, 8 - CONV - 1), (0, projected.shape[1] - taps.shape[1])))
    head = jnp.pad(jnp.stack([-jnp.exp(params[0]), params[1]]), ((0, 6), (0, LANES - heads)))
    skip = jnp.repeat(params[2], HEADDIM).reshape(1, HALF)
    wide = HALF + 2 * STATE
    rim = borrowed(projected[tokens - 8 :], 1)
    nothing = jnp.zeros((STATE, HALF), f32)
    values, prior, final, last = scan_forward(projected, taps, head, skip, rim, nothing, seg_len)
    if line > SEGS:
        last = jnp.sum(last.reshape(SEGS, 8, LANES)[:, 0, :heads], axis=0)
        decay = jnp.repeat(jnp.exp2(last), HEADDIM)
        begin = entering(decay, final, 1)
        values, prior, _, _ = scan_forward(projected, taps, head, skip, rim, begin, seg_len)

    values, gate_far, out_others, cotangent = tie(values, gate_far, out_others, cotangent)
    cot_got = send_sequence(cotangent, place)
    out_own = jnp.concatenate([out_own, *out_others])
    out_all = gather_plane(out_own, plane_steps())
    gate_matrix = whole_matrix([gate_own, *gate_near, *gate_far], True)
    gate_input = dot(normed, gate_matrix, ((1,), (0,)))

    silu_gate = jax.nn.silu(gate_input)
    gated = values * silu_gate
    squares = jnp.sum(gated * gated, axis=1)
    squares_other = to_partner(squares)
    scale = lax.rsqrt((squares + squares_other) / INNER + epsilon)[:, None]
    mixed, mixed_turned = mixed_tokens(gated, scale, gain_gate, seg_len)
    mixed_turned, out_all, cot_got = tie(mixed_turned, out_all, cot_got)
    cot_half = order_sequence(cot_got, place)
    cot_other = to_partner(cot_half)
    cot = in_core_order(cot_half, cot_other, core, 1)
    upstream = cot.reshape(tokens, model_width)
    by_owner = lambda grad: grad.astype(bf16).reshape(chip_dims() + (-1, grad.shape[1]))
    out_grad = by_owner(dot(mixed_turned, upstream, ((1,), (0,))))
    out_got_near = reduce_plane([out_grad], near_steps())
    out_matrix = whole_matrix([out_own, *out_all], False, True)
    branch, branch_sent = half_products(core, [(mixed, out_matrix, None)], seg_len, model_width, False)
    branch_sent, upstream = tie(branch_sent, upstream)
    branch_other = to_partner(branch_sent)
    grad_mixed = dot(upstream, out_matrix, ((1,), (1,)))
    grad_mixed, out_got_near, out_grad = tie(grad_mixed, out_got_near, out_grad)
    out_got_far = reduce_plane([out_grad], far_steps())
    unit = gated * scale
    gain_grad = grad_mixed * gain_gate
    along = jnp.sum(gain_grad * unit, axis=1)
    along_other = to_partner(along)
    along_other, branch_other = tie(along_other, branch_other)
    hidden_out = send_back((hidden_half.astype(f32) + branch + branch_other.astype(f32)).astype(bf16), place)
    along = ((along + along_other) / INNER)[:, None]
    gate_gain_grad = jnp.sum(grad_mixed * unit, axis=0)
    grad_gated = scale * (gain_grad - unit * along)
    grad_values = grad_gated * silu_gate
    sigmoid = jax.nn.sigmoid(gate_input)
    grad_gate = (grad_gated * values * (sigmoid * (1.0 + gate_input * (1.0 - sigmoid)))).astype(bf16)
    gate_grad = by_owner(dot(normed_turned, grad_gate, ((1,), (0,))))
    gate_grad, grad_values, out_got_far = tie(gate_grad, grad_values, out_got_far)
    gate_got = reduce_plane([gate_grad], plane_steps())
    scan = lambda later: scan_backward(
        0, core, projected, taps, head, skip, rim, later, prior, values, grad_values, seg_len
    )
    if line > SEGS:
        nothing = entering(decay, scan(nothing)[-1], -1)
    back = scan(nothing)
    back, gate_got, hidden_out, grad_gate = tie(back, gate_got, hidden_out, grad_gate)
    ((early_kept, early_got),) = reduce_z(
        [
            ([plane_part([out_grad], 0, 0)], [*out_got_near, *out_got_far]),
            ([plane_part([gate_grad], 0, 0)], gate_got),
        ]
    )
    grad_x, mine, theirs, grad_raw, x_taps_grad, skip_grad, head_sums, x_edge, _ = back
    grad_x = spilled(grad_x, x_edge, taps[:, :HALF])
    other = to_partner(theirs)
    x_grad = by_owner(dot(normed_turned, grad_x, ((1,), (0,))))
    other, x_grad = tie(other, x_grad)
    grad_state, state_taps_grad, state_edge = shared_backward(core, projected, rim, taps, mine, other)
    grad_state = spilled(grad_state, state_edge, lax.dynamic_slice_in_dim(taps, HALF + core * STATE, STATE, axis=1))
    grad_raw = grad_raw.astype(bf16)
    rest_grad = by_owner(dot(normed_turned, jnp.concatenate([grad_state, grad_raw], axis=1), ((1,), (0,))))
    rest_grad, x_grad, grad_gate = tie(rest_grad, x_grad, grad_gate)
    conv_near = reduce_plane([x_grad, rest_grad], near_steps())
    base = dot(grad_gate, gate_matrix, ((1,), (1,)))
    terms = [
        (grad_x, conv_all, lambda core: 0),
        (grad_state, conv_all, lambda core: HALF // LANES + core),
        (grad_raw, conv_all, lambda core: (HALF + 2 * STATE) // LANES),
    ]
    grad_normed, sent_normed = half_products(core, terms, seg_len, model_width, True, (base,))
    row = lax.broadcasted_iota(jnp.int32, (8, 1), 0)
    small = x_taps_grad + jnp.where(row == CONV + 1, gate_gain_grad, 0.0) + jnp.where(row == CONV + 2, skip_grad, 0.0)
    small = jnp.concatenate([small, state_taps_grad + head_sums], axis=1)
    sent_normed, early_got, conv_near, small, x_grad, rest_grad = tie(
        sent_normed, early_got, conv_near, small, x_grad, rest_grad
    )
    conv_far = reduce_plane([x_grad, rest_grad], far_steps())
    other_normed = to_partner(sent_normed)
    wide_hidden = hidden_half.astype(f32)
    hidden_scale = lax.rsqrt(jnp.mean(wide_hidden * wide_hidden, axis=-1, keepdims=True) + epsilon)
    grad_normed = (grad_normed + other_normed.astype(f32)) * gain_pre
    hidden_unit = wide_hidden * hidden_scale
    along = jnp.mean(grad_normed * hidden_unit, axis=-1, keepdims=True)
    grad_hidden = hidden_scale * (grad_normed - hidden_unit * along)
    grad_in = (cot_half.astype(f32) + grad_hidden).astype(bf16)
    grad_in, conv_far = tie(send_back(grad_in, place), conv_far)
    late = reduce_z([([plane_part([x_grad, rest_grad], 0, 0)], [*conv_near, *conv_far])])
    for dim in range(3):
        small = small + sum(moved(small, dim, by) for by in range(1, chip_dims()[dim]))
    small_other = to_partner(small)
    late_got, small_other = tie(arrivals(late), small_other)
    early_share = total([*early_kept, *early_got])
    out_share = early_share[:, :model_width]
    paired = lambda share: share.astype(bf16).reshape(2, rows, -1)
    gate_share, conv_share = paired(early_share[:, model_width:]), paired(reduce_end(arrived(late, late_got)))

    def mine_and_partner(share):
        keep = lax.dynamic_index_in_dim(share, core, axis=0, keepdims=False)
        give = lax.dynamic_index_in_dim(share, 1 - core, axis=0, keepdims=False)
        return keep, to_partner(give)

    both = in_core_order(small, small_other, core, 0)
    natural = lambda array, width: array.reshape(2, -1, chips, width).transpose(1, 2, 0, 3).reshape(-1, 2 * chips * width)
    device = (lax.axis_index("chip") * 2 + core) * line + place
    columns = natural(both[:, :, :HALF], HALF // chips)
    taps_all = jnp.concatenate([columns, both[0, :, HALF:], both[1, :, HALF:]], axis=1)[: CONV + 1]
    taps_share = lax.dynamic_slice_in_dim(taps_all, device * conv_width, conv_width, axis=1)
    gain_share = lax.dynamic_slice_in_dim(columns[CONV + 1], device * gain_width, gain_width, axis=0)
    head_total = jnp.concatenate(
        [
            natural(both[:, CONV + 1 : CONV + 3, HALF : HALF + heads], heads // chips),
            jnp.sum(columns[CONV + 2].reshape(1, HEADS, HEADDIM), axis=2),
        ]
    )

    def interleave(mine, theirs):
        width = mine.shape[1] // chips
        both = in_core_order(mine.reshape(rows, chips, width), theirs.reshape(rows, chips, width), core, 2)
        return both.reshape(rows, -1)

    keep_gate, got_gate = mine_and_partner(gate_share)
    keep, got = mine_and_partner(conv_share)
    state_end = HALF + STATE
    in_share = jnp.concatenate(
        [
            interleave(keep_gate, got_gate),
            interleave(keep[:, :HALF], got[:, :HALF]),
            in_core_order(keep[:, HALF:state_end], got[:, HALF:state_end], core, 1).reshape(rows, -1),
            interleave(keep[:, state_end : state_end + heads], got[:, state_end : state_end + heads]),
        ],
        axis=1,
    ).astype(f32)
    pre_share = jnp.sum(in_proj.astype(f32) * in_share, axis=1) / pre_gain.astype(f32)
    hidden_out, grad_in = order_back(hidden_out, place), order_back(grad_in, place)
    return (hidden_out, grad_in, in_share, out_share, taps_share, pre_share, gain_share, head_total)


def solution(mesh):
    devices = mesh.devices
    cores = Mesh(devices.reshape(devices.shape[0] // 2, 2, devices.shape[1]), ("chip", "core", "seg"))
    dp, both = ("chip", "core"), ("chip", "core", "seg")
    tokens = P(dp, "seg", None)
    return jax.shard_map(
        per_device,
        mesh=cores,
        in_specs=(tokens, tokens, P(both, None), P(both, None), P(None, both), P(both), P(both), P()),
        out_specs=(tokens, tokens, P(both, None), P(both, None), P(None, both), P(both), P(both), P()),
        check_vma=False,
    )
```

```python
import jax
import jax.numpy as jnp
from jax import lax
from jax.experimental import pallas as pl
from jax.experimental.pallas import tpu as pltpu
from jax.sharding import Mesh
from jax.sharding import PartitionSpec as P

HEADS = 48
HEADDIM = 64
STATE = 128
CONV = 4
INNER = 3072
XBC = 3328
HALF = INNER // 2
LANES = 128
SEGS = 4
LIGHT = pl.CostEstimate(flops=1024, bytes_accessed=1024, transcendentals=0)
VMEM_LIMIT = 48 * 1024 * 1024
LOG2E = 1.4426950408889634

epsilon = 1e-05
f32 = jnp.float32
bf16 = jnp.bfloat16


def own_columns(array, core):
    chips = lax.axis_size("chip")
    width = array.shape[-1] // (2 * chips)
    parted = array.reshape(array.shape[:-1] + (chips, 2, width))
    picked = lax.dynamic_index_in_dim(parted, core, axis=parted.ndim - 2, keepdims=False)
    return picked.reshape(array.shape[:-1] + (chips * width,))


def to_partner(array):
    return lax.ppermute(array, "core", [(0, 1), (1, 0)])


def in_core_order(mine, theirs, core, axis):
    first = jnp.where(core == 0, mine, theirs)
    second = jnp.where(core == 0, theirs, mine)
    return jnp.stack([first, second], axis=axis)


def chip_dims():
    return (lax.axis_size("chip") // 2, 2, lax.axis_size("seg"))


def chip_place():
    chip = lax.axis_index("chip")
    return (chip // 2, chip % 2, lax.axis_index("seg"))


def moved(array, dim, by):
    sizes = chip_dims()
    index = lambda at: (at[0] * sizes[1] + at[1]) * sizes[2] + at[2]
    pairs = []
    for a in range(sizes[0]):
        for b in range(sizes[1]):
            for z in range(sizes[2]):
                to = [a, b, z]
                to[dim] = (to[dim] + by) % sizes[dim]
                pairs.append((index((a, b, z)), index(to)))
    return lax.ppermute(array, ("chip", "seg"), pairs)


def tie(*values):
    return lax.optimization_barrier(values)


def gather_step(data, dim):
    return [data] + [moved(data, dim, by) for by in range(1, chip_dims()[dim])]


def exchanged(array, by):
    line = lax.axis_size("seg")
    return lax.ppermute(array, "seg", [(at, at ^ by) for at in range(line)])


def plane_steps():
    a, b, _ = chip_dims()
    steps = [(at // b, at % b) for at in range(1, a * b)]
    return sorted(steps, key=lambda by: bool(by[0] and by[1]))


def near_steps():
    a, b, _ = chip_dims()
    return plane_steps()[: a + b - 2]


def far_steps():
    a, b, _ = chip_dims()
    return plane_steps()[a + b - 2 :]


def moved_plane(array, by_a, by_b):
    a, b, z = chip_dims()
    pairs = [
        ((at_a * b + at_b) * z + at_z, ((at_a + by_a) % a * b + (at_b + by_b) % b) * z + at_z)
        for at_a in range(a)
        for at_b in range(b)
        for at_z in range(z)
    ]
    return lax.ppermute(array, ("chip", "seg"), pairs)


def gather_plane(data, steps):
    return [moved_plane(data, *by) for by in steps]


def placed_kernel(plan, place_ref, *refs):
    sources, target, sems = refs[:-2], refs[-2], refs[-1]
    copies = []
    for source, lead, at, paired in plan:
        spot = [lax.rem(place_ref[dim] + (size - back), size) for dim, (back, size) in enumerate(at)]
        spot.append(place_ref[2 + lead])
        to = target.at[spot[0], spot[1], :, spot[2]] if paired else target.at[spot[0], spot[1], spot[2]]
        copies.append(pltpu.make_async_copy(sources[source].at[lead], to, sems.at[len(copies)]))
    for copy in copies:
        copy.start()
    for copy in copies:
        copy.wait()


def whole_matrix(gathered, paired, by_bits=False):
    a, b, z = chip_dims()
    at_a, at_b, at_z = chip_place()
    spots = [at_z ^ back if by_bits else (at_z + z - back) % z for back in range(z)]
    plan = [
        (source, back, ((by[0], a), (by[1], b)), paired)
        for source, by in enumerate([(0, 0)] + plane_steps())
        for back in range(z)
    ]
    block = gathered[0].shape[1:]
    shape = (a, b, 2, z) + block[1:] if paired else (a, b, z) + block
    anywhere = pl.BlockSpec(memory_space=pl.ANY)
    whole = pl.pallas_call(
        lambda *refs: placed_kernel(plan, *refs),
        out_shape=jax.ShapeDtypeStruct(shape, bf16),
        in_specs=[pl.BlockSpec(memory_space=pltpu.SMEM)] + [anywhere] * len(gathered),
        out_specs=pl.BlockSpec(memory_space=pltpu.VMEM),
        scratch_shapes=[pltpu.SemaphoreType.DMA((len(plan),))],
        compiler_params=pltpu.CompilerParams(vmem_limit_bytes=VMEM_LIMIT),
        cost_estimate=LIGHT,
    )(jnp.stack([at_a, at_b, *spots]).astype(jnp.int32), *gathered)
    return whole.reshape(-1, shape[-1])


def total(terms):
    result = terms[0].astype(f32)
    for term in terms[1:]:
        result = result + term.astype(f32)
    return result


def reduce_send(terms, axis, dim, wire):
    place, size = chip_place()[dim], chip_dims()[dim]
    pick = lambda at: [lax.dynamic_index_in_dim(term, at, axis=axis, keepdims=False) for term in terms]
    received = [moved(total(pick((place + by) % size)).astype(wire), dim, by) for by in range(1, size)]
    return pick(place), received


def plane_part(partials, by_a, by_b):
    (at_a, at_b, _), (a, b, _) = chip_place(), chip_dims()
    chip = (at_a + by_a) % a * b + (at_b + by_b) % b
    flat = [partial.reshape((a * b,) + partial.shape[2:]) for partial in partials]
    return jnp.concatenate([lax.dynamic_index_in_dim(array, chip, axis=0, keepdims=False) for array in flat], axis=-1)


def reduce_plane(partials, steps):
    return [moved_plane(plane_part(partials, *by), *by) for by in steps]


def reduce_z(firsts):
    joined = jnp.concatenate([total(kept + received) for kept, received in firsts], axis=-1)
    return [reduce_send([joined], 0, 2, bf16)]


def reduce_end(third):
    return total(third[0][0] + third[0][1])


def arrivals(parts):
    return [received for _, received in parts]


def arrived(parts, received):
    return [(kept, new) for (kept, _), new in zip(parts, received)]


def line_perm(turn, back):
    line = lax.axis_size("seg")
    parts = line // SEGS
    pairs = []
    for core in range(2):
        for place in range(line):
            half, odd = divmod(place % SEGS, 2)
            source = core * line + place
            target = odd * line + (2 * core + (half ^ turn)) * parts + place // SEGS
            pairs.append((target, source) if back else (source, target))
    return pairs


def swapped(pair, turn):
    return [jnp.where(turn == 0, pair[0], pair[1]), jnp.where(turn == 0, pair[1], pair[0])]


def send_sequence(array, place):
    pieces = swapped([array[0], array[1]], (place % SEGS) // 2)
    return [lax.ppermute(piece, ("core", "seg"), line_perm(turn, False)) for turn, piece in enumerate(pieces)]


def order_sequence(got, place):
    parts = lax.axis_size("seg") // SEGS
    return jnp.stack(swapped(got, (place // parts) % 2))


def send_back(ordered, place):
    parts = lax.axis_size("seg") // SEGS
    pieces = swapped([ordered[0], ordered[1]], (place // parts) % 2)
    return [lax.ppermute(piece, ("core", "seg"), line_perm(turn, True)) for turn, piece in enumerate(pieces)]


def order_back(got, place):
    return jnp.stack(swapped(got, (place % SEGS) // 2))


def part_pairs(step):
    line = lax.axis_size("seg")
    parts = line // SEGS
    return [(i, i + step) for i in range(line) if 0 <= i + step < line and i // parts == (i + step) // parts]


def entering(decay, state, step):
    parts = lax.axis_size("seg") // SEGS
    total = jnp.zeros_like(state)
    for _ in range(parts - 1):
        total = lax.ppermute(decay * total + state, "seg", part_pairs(step))
    return total


def borrowed(array, step):
    parts = lax.axis_size("seg") // SEGS
    if parts == 1:
        return jnp.zeros_like(array)
    return lax.ppermute(array, "seg", part_pairs(step))


def spilled(grad, edge, taps):
    if lax.axis_size("seg") == SEGS:
        return grad
    edge = borrowed(edge, -1)
    spill = jnp.stack(
        [
            sum(taps[k] * edge[CONV - 1 - k - early] for k in range(CONV - early))
            for early in range(CONV - 1, 0, -1)
        ]
    )
    at = grad.shape[0] - CONV + 1
    return grad.at[at:].set((grad[at:].astype(f32) + spill).astype(bf16))


def dot(a, b, contract):
    return lax.dot_general(a, b, (contract, ((), ())), preferred_element_type=f32)


def normed_kernel(slabs, core_ref, mine_ref, other_ref, gain_ref, normed_ref, turned_ref):
    own = lax.rem(pl.program_id(0), 2) == core_ref[0]
    hidden = jnp.where(own, mine_ref[0], other_ref[0]).astype(f32)
    scale = lax.rsqrt(jnp.mean(hidden * hidden, axis=1, keepdims=True) + epsilon)
    normed = hidden * scale * gain_ref[...]
    normed_ref[...] = normed.astype(bf16)
    turned = normed.T.astype(bf16)
    for to, at, size in slabs:
        turned_ref[to : to + size] = turned[at : at + size]


def normed_tokens(core, mine, other, gain, rows):
    segs, seg_len, width = 2 * mine.shape[0], mine.shape[1], mine.shape[2]
    a, b, z = chip_dims()
    group = 2 * z * rows
    inside = rows % 16 == 0
    slabs = [(0, 0, width)]
    if inside:
        slabs = [
            (chip * group + (at * 2 + core_at) * rows, chip * group + (core_at * z + at) * rows, rows)
            for chip in range(a * b)
            for core_at in range(2)
            for at in range(z)
        ]
    normed, turned = pl.pallas_call(
        lambda *refs: normed_kernel(slabs, *refs),
        grid_spec=pltpu.PrefetchScalarGridSpec(
            num_scalar_prefetch=1,
            grid=(segs,),
            in_specs=[
                pl.BlockSpec((1, seg_len, width), lambda i, core: (i // 2, 0, 0)),
                pl.BlockSpec((1, seg_len, width), lambda i, core: (i // 2, 0, 0)),
                pl.BlockSpec((1, width), lambda i, core: (0, 0)),
            ],
            out_specs=(
                pl.BlockSpec((seg_len, width), lambda i, core: (i, 0)),
                pl.BlockSpec((width, seg_len), lambda i, core: (0, i)),
            ),
        ),
        out_shape=(
            jax.ShapeDtypeStruct((segs * seg_len, width), bf16),
            jax.ShapeDtypeStruct((width, segs * seg_len), bf16),
        ),
        compiler_params=pltpu.CompilerParams(dimension_semantics=("arbitrary",), vmem_limit_bytes=VMEM_LIMIT),
        cost_estimate=LIGHT,
    )(core.reshape(1).astype(jnp.int32), mine, other, gain.reshape(1, width))
    if not inside:
        turned = turned.reshape(a, b, 2, z, rows, -1).transpose(0, 1, 3, 2, 4, 5).reshape(turned.shape)
    return normed, turned


def mixed_kernel(gated_ref, scale_ref, gain_ref, mixed_ref, turned_ref):
    mixed = gated_ref[...] * scale_ref[...] * gain_ref[...]
    mixed_ref[...] = mixed.astype(bf16)
    turned_ref[...] = mixed.T.astype(bf16)


def mixed_tokens(gated, scale, gain, seg_len):
    length, width = gated.shape
    return pl.pallas_call(
        mixed_kernel,
        grid=(length // seg_len,),
        in_specs=[
            pl.BlockSpec((seg_len, width), lambda i: (i, 0)),
            pl.BlockSpec((seg_len, 1), lambda i: (i, 0)),
            pl.BlockSpec((1, width), lambda i: (0, 0)),
        ],
        out_specs=(
            pl.BlockSpec((seg_len, width), lambda i: (i, 0)),
            pl.BlockSpec((width, seg_len), lambda i: (0, i)),
        ),
        out_shape=(
            jax.ShapeDtypeStruct((length, width), bf16),
            jax.ShapeDtypeStruct((width, length), bf16),
        ),
        compiler_params=pltpu.CompilerParams(dimension_semantics=("arbitrary",), vmem_limit_bytes=VMEM_LIMIT),
        cost_estimate=LIGHT,
    )(gated, scale, gain.reshape(1, width))


def columns_of(pair):
    return pl.ds(pair * LANES, LANES)


def low_half(shape):
    return lax.broadcasted_iota(jnp.int32, shape, len(shape) - 1) < HEADDIM


def pair_columns(array, pair, low):
    rows = array.shape[0]
    first = jnp.broadcast_to(array[:, 2 * pair : 2 * pair + 1], (rows, LANES))
    second = jnp.broadcast_to(array[:, 2 * pair + 1 : 2 * pair + 2], (rows, LANES))
    return jnp.where(low, first, second)


def conv_parts(current, before, taps):
    rows = current.shape[0]
    padded = jnp.concatenate([before, current], axis=0)
    seen = [padded[8 - CONV + 1 + k : 8 - CONV + 1 + k + rows] for k in range(CONV - 1)] + [current]
    total = taps[CONV : CONV + 1]
    for k in range(CONV):
        total = total + taps[k : k + 1] * seen[k]
    return total, seen


def exact_sums(chosen, array):
    chosen = jnp.where(chosen, 1.0, 0.0).astype(bf16)
    result = 0.0
    for _ in range(3):
        part = array.astype(bf16)
        array = array - part.astype(f32)
        result = result + dot(chosen, part, ((1,), (0,)))
    return result


def step_terms(raw, head, seg_len):
    shifted = raw + head[1:2]
    step = jnp.maximum(shifted, 0.0) + jnp.log1p(jnp.exp(-jnp.abs(shifted)))
    log_decay = step * head[0:1]
    at_or_before = lax.broadcasted_iota(jnp.int32, (seg_len, seg_len), 0) >= lax.broadcasted_iota(
        jnp.int32, (seg_len, seg_len), 1
    )
    sums = exact_sums(at_or_before, log_decay)
    return shifted, step, log_decay, sums * LOG2E


def forward_kernel(
    proj_ref, taps_ref, head_ref, skip_ref, rim_ref, init_ref,
    values_ref, prior_ref, final_ref, last_ref, state_ref, tail_ref,
):
    seg_len = proj_ref.shape[0]
    half = seg_len // 2

    @pl.when(pl.program_id(0) == 0)
    def _():
        state_ref[...] = init_ref[...]
        tail_ref[...] = rim_ref[...]

    def activated(begin):
        at = pl.ds(begin, LANES)
        total, _ = conv_parts(proj_ref[:, at], tail_ref[:, at], taps_ref[:, at])
        return total * jax.nn.sigmoid(total)

    b_low = activated(HALF).astype(bf16)
    b_turned = activated(HALF).T.astype(bf16)
    c_low = activated(HALF + STATE).astype(bf16)
    _, step, _, sums = step_terms(proj_ref[:, HALF + 2 * STATE :], head_ref, seg_len)
    sums_turned, step_turned = sums.T, step.T
    scores = dot(c_low, b_low, ((1,), (1,)))
    kept = lax.broadcasted_iota(jnp.int32, (half, half), 0) >= lax.broadcasted_iota(jnp.int32, (half, half), 1)
    first_scores = jnp.where(kept, scores[:half, :half], 0.0)
    later_scores = scores[half:, :half]
    second_scores = jnp.where(kept, scores[half:, half:], 0.0)
    low = low_half((seg_len, LANES))
    last_ref[...] = jnp.broadcast_to(sums[seg_len - 1 :], last_ref.shape)

    for pair in range(HEADS // 4):
        at = columns_of(pair)
        x_values = activated(pair * LANES)
        x_low = x_values.astype(bf16)
        sums_pair = pair_columns(sums, pair, low)
        last_pair = sums_pair[seg_len - 1 :]
        carry = jnp.exp2(last_pair - sums_pair) * pair_columns(step, pair, low)
        scaled_x = (carry * x_low.astype(f32)).astype(bf16)
        prior = state_ref[:, at]
        prior_low = prior.astype(bf16)
        prior_ref[0, :, at] = prior_low
        from_state = jnp.exp2(sums_pair) * dot(c_low, prior_low, ((1,), (0,)))
        state_ref[:, at] = jnp.exp2(last_pair) * prior + dot(b_turned, scaled_x, ((1,), (0,)))
        early, late = 0.0, 0.0
        for side in range(2):
            head = 2 * pair + side
            x_side = jnp.where(low if side == 0 else ~low, x_values, 0.0).astype(bf16)
            at_token = jnp.broadcast_to(sums[:, head : head + 1], (seg_len, half))
            at_source, source_step = sums_turned[head : head + 1], step_turned[head : head + 1]
            first = jnp.exp2(jnp.minimum(at_token[:half] - at_source[:, :half], 0.0)) * first_scores
            first = (first * source_step[:, :half]).astype(bf16)
            later = jnp.exp2(at_token[half:] - at_source[:, :half]) * later_scores
            later = (later * source_step[:, :half]).astype(bf16)
            second = jnp.exp2(jnp.minimum(at_token[half:] - at_source[:, half:], 0.0)) * second_scores
            second = (second * source_step[:, half:]).astype(bf16)
            early = early + dot(first, x_side[:half], ((1,), (0,)))
            late = late + dot(jnp.concatenate([later, second], axis=1), x_side, ((1,), (0,)))
        intra = jnp.concatenate([early, late], axis=0)
        values_ref[:, at] = intra + from_state + skip_ref[:, at] * x_values

    tail_ref[...] = proj_ref[seg_len - 8 :, : HALF + 2 * STATE]
    final_ref[...] = state_ref[...]


def full_block(shape):
    return pl.BlockSpec(shape, lambda *_: (0,) * len(shape))


def scan_forward(proj, taps, head, skip, rim, init, seg_len):
    segs = proj.shape[0] // seg_len
    wide = HALF + 2 * STATE
    return pl.pallas_call(
        forward_kernel,
        grid=(segs,),
        out_shape=(
            jax.ShapeDtypeStruct((proj.shape[0], HALF), f32),
            jax.ShapeDtypeStruct((segs, STATE, HALF), bf16),
            jax.ShapeDtypeStruct((STATE, HALF), f32),
            jax.ShapeDtypeStruct((segs * 8, LANES), f32),
        ),
        in_specs=[
            pl.BlockSpec((seg_len, proj.shape[1]), lambda i: (i, 0)),
            full_block((8, wide)),
            full_block((8, LANES)),
            full_block((1, HALF)),
            full_block((8, wide)),
            full_block((STATE, HALF)),
        ],
        out_specs=(
            pl.BlockSpec((seg_len, HALF), lambda i: (i, 0)),
            pl.BlockSpec((1, STATE, HALF), lambda i: (i, 0, 0)),
            full_block((STATE, HALF)),
            pl.BlockSpec((8, LANES), lambda i: (i, 0)),
        ),
        scratch_shapes=[pltpu.VMEM((STATE, HALF), f32), pltpu.VMEM((8, wide), f32)],
        compiler_params=pltpu.CompilerParams(
            dimension_semantics=("arbitrary",), vmem_limit_bytes=VMEM_LIMIT
        ),
        cost_estimate=LIGHT,
    )(proj, taps, head, skip, rim, init)


def split_dot(array, other):
    high = array.astype(bf16)
    rest = (array - high.astype(f32)).astype(bf16)
    return dot(high, other, ((1,), (0,))) + dot(rest, other, ((1,), (0,)))


def backward_kernel(
    group, proj_ref, before_ref, taps_ref, rim_ref, shared_ref, shared_before_ref, shared_taps_ref, shared_rim_ref,
    head_ref, skip_ref, end_ref, prior_ref, values_ref, grad_ref, core_ref,
    grad_x_ref, mine_ref, theirs_ref, grad_raw_ref, taps_grad_ref, skip_grad_ref, head_grad_ref, edge_ref, start_ref,
    later_ref, local_ref, scaled_ref, grad_state_ref, inner_ref, source_ref, carry_ref, decay_ref,
):
    seg_len = proj_ref.shape[0]
    half = seg_len // 2
    turn = pl.program_id(0)

    @pl.when(turn == 0)
    def _():
        later_ref[...] = end_ref[...]
        edge_ref[...] = jnp.zeros_like(edge_ref)
        taps_grad_ref[...] = jnp.zeros_like(taps_grad_ref)
        skip_grad_ref[...] = jnp.zeros_like(skip_grad_ref)
        head_grad_ref[...] = jnp.zeros_like(head_grad_ref)

    first_segment = turn == pl.num_programs(0) - 1

    def conv_at(at, current, ahead, taps, rim):
        before = jnp.where(first_segment, rim[:, at], ahead[:, at])
        return conv_parts(current[:, at], before, taps[:, at])

    def activated(begin):
        total, _ = conv_at(pl.ds(begin, LANES), shared_ref, shared_before_ref, shared_taps_ref, shared_rim_ref)
        return total * jax.nn.sigmoid(total)

    b_values = activated(0)
    c_values = activated(STATE)
    b_low, c_low, c_turned = b_values.astype(bf16), c_values.astype(bf16), c_values.T.astype(bf16)
    shifted, step, log_decay, sums = step_terms(shared_ref[:, 2 * STATE :], head_ref, seg_len)
    sums_turned = sums.T
    scores = dot(b_low, c_low, ((1,), (1,)))
    kept = lax.broadcasted_iota(jnp.int32, (half, half), 0) <= lax.broadcasted_iota(jnp.int32, (half, half), 1)
    first_scores = jnp.where(kept, scores[:half, :half], 0.0)
    later_scores = scores[:half, half:]
    second_scores = jnp.where(kept, scores[half:, half:], 0.0)
    low = low_half((seg_len, LANES))
    first_grad, later_grad, second_grad = 0.0, 0.0, 0.0

    pairs = grad_ref.shape[1] // LANES
    for pair in range(pairs):
        at = columns_of(pair)
        total, seen = conv_at(at, proj_ref, before_ref, taps_ref, rim_ref)
        sigmoid = jax.nn.sigmoid(total)
        x_values = total * sigmoid
        x_low = x_values.astype(bf16)
        x_wide = x_low.astype(f32)
        sums_pair = pair_columns(sums, group * pairs + pair, low)
        step_pair = pair_columns(step, group * pairs + pair, low)
        last_pair = sums_pair[seg_len - 1 :]
        gap = jnp.exp2(last_pair - sums_pair)
        scaled_ref[:, at] = (gap * step_pair * x_wide).astype(bf16)
        grad_values = grad_ref[:, at]
        grad_state_ref[:, at] = (grad_values * jnp.exp2(sums_pair)).astype(bf16)
        later = later_ref[:, at]
        later_low = later.astype(bf16)
        local_ref[:, at] = later_low
        prior = prior_ref[0, :, at]
        decay_ref[:, at] = jnp.broadcast_to(
            jnp.sum(later * prior.astype(f32), axis=0, keepdims=True), (8, LANES)
        )
        grad_prior = dot(c_turned, grad_state_ref[:, at], ((1,), (0,)))
        later_ref[:, at] = jnp.exp2(last_pair) * later + grad_prior
        grad_scaled = dot(b_low, later_low, ((1,), (0,)))
        stepped = (step_pair * x_wide).astype(bf16)
        early, late = 0.0, 0.0
        for side in range(2):
            head = 2 * (group * pairs + pair) + side
            grad_low = jnp.where(low if side == 0 else ~low, grad_values, 0.0).astype(bf16)
            at_source = jnp.broadcast_to(sums[:, head : head + 1], (seg_len, half))
            at_token = sums_turned[head : head + 1]
            grad_weights = dot(stepped, grad_low, ((1,), (1,)))
            first = jnp.exp2(jnp.minimum(at_token[:, :half] - at_source[:half], 0.0))
            after = jnp.exp2(at_token[:, half:] - at_source[:half])
            second = jnp.exp2(jnp.minimum(at_token[:, half:] - at_source[half:], 0.0))
            first_grad = first_grad + first * grad_weights[:half, :half]
            later_grad = later_grad + after * grad_weights[:half, half:]
            second_grad = second_grad + second * grad_weights[half:, half:]
            upper = jnp.concatenate([first * first_scores, after * later_scores], axis=1).astype(bf16)
            early = early + dot(upper, grad_low, ((1,), (0,)))
            late = late + dot((second * second_scores).astype(bf16), grad_low[half:], ((1,), (0,)))
        inner = jnp.concatenate([early, late], axis=0)
        skip = skip_ref[:, at]
        skip_grad_ref[:, at] += jnp.sum(grad_values * x_values, axis=0, keepdims=True)
        inner_ref[:, at] = grad_values * (values_ref[:, at] - skip * x_values)
        source_ref[:, at] = x_wide * inner
        carry_ref[:, at] = x_wide * grad_scaled
        grad_x = skip * grad_values + step_pair * (inner + gap * grad_scaled)
        grad_total = grad_x * (sigmoid * (1.0 + total * (1.0 - sigmoid)))
        for k in range(CONV):
            taps_grad_ref[k : k + 1, at] += jnp.sum(grad_total * seen[k], axis=0, keepdims=True)
        taps_grad_ref[CONV : CONV + 1, at] += jnp.sum(grad_total, axis=0, keepdims=True)
        extended = jnp.concatenate([grad_total, edge_ref[:, at]], axis=0)
        edge_ref[:, at] = grad_total[:8]
        taps = taps_ref[:, at]
        grad_conv = taps[CONV - 1 : CONV] * grad_total
        for k in range(CONV - 1):
            grad_conv = grad_conv + taps[k : k + 1] * extended[CONV - 1 - k : CONV - 1 - k + seg_len]
        grad_x_ref[:, at] = grad_conv.astype(bf16)

    width = grad_ref.shape[1]
    channel = lax.broadcasted_iota(jnp.int32, (width, LANES), 0) // HEADDIM + group * width // HEADDIM
    heads = jnp.where(channel == lax.broadcasted_iota(jnp.int32, (width, LANES), 1), 1.0, 0.0).astype(bf16)
    tail = jnp.exp2(sums[seg_len - 1 :] - sums)
    source_grad = split_dot(source_ref[...], heads)
    step_grad = source_grad + tail * split_dot(carry_ref[...], heads)
    used = step * step_grad
    sum_grad = split_dot(inner_ref[...], heads) - used
    at_last = jnp.sum(used - step * source_grad, axis=0, keepdims=True)
    at_last = at_last + split_dot(decay_ref[...], heads)[:1] * jnp.exp2(sums[seg_len - 1 :])
    is_last = lax.broadcasted_iota(jnp.int32, (seg_len, LANES), 0) == seg_len - 1
    sum_grad = sum_grad + jnp.where(is_last, at_last, 0.0)
    at_or_after = lax.broadcasted_iota(jnp.int32, (seg_len, seg_len), 0) <= lax.broadcasted_iota(
        jnp.int32, (seg_len, seg_len), 1
    )
    log_grad = exact_sums(at_or_after, sum_grad)
    grad_raw = (step_grad + head_ref[0:1] * log_grad) * jax.nn.sigmoid(shifted)
    grad_raw_ref[...] = grad_raw
    head_grad_ref[CONV + 1 : CONV + 2] += jnp.sum(log_grad * log_decay, axis=0, keepdims=True)
    head_grad_ref[CONV + 2 : CONV + 3] += jnp.sum(grad_raw, axis=0, keepdims=True)

    first_low = jnp.where(kept, first_grad, 0.0)
    second_low = jnp.where(kept, second_grad, 0.0)
    grad_scores = jnp.concatenate(
        [
            jnp.concatenate([first_low, later_grad], axis=1),
            jnp.concatenate([jnp.zeros_like(first_low), second_low], axis=1),
        ],
        axis=0,
    )
    start_ref[...] = later_ref[...]
    grad_b = dot(scaled_ref[...], local_ref[...], ((1,), (1,))) + dot(
        grad_scores.astype(bf16), c_low, ((1,), (0,))
    )
    grad_c = dot(grad_state_ref[...], prior_ref[0], ((1,), (1,))) + dot(
        grad_scores.T.astype(bf16), b_low, ((1,), (0,))
    )
    first = core_ref[0] == 0
    mine_ref[...] = jnp.where(first, grad_b, grad_c)
    theirs_ref[...] = jnp.where(first, grad_c, grad_b)


GROUPS = 1


def scan_backward(group, core, proj, taps, head, skip, rim, end, prior, values, grad_values, seg_len):
    length = proj.shape[0]
    segs = length // seg_len
    width, shared = HALF // GROUPS, proj.shape[1] - HALF
    back = lambda width, at=0: pl.BlockSpec((seg_len, width), lambda i: (segs - 1 - i, at))
    row_ahead = lambda i: jnp.maximum((segs - 1 - i) * (seg_len // 8) - 1, 0)
    ahead = lambda width, at: pl.BlockSpec((8, width), lambda i: (row_ahead(i), at))
    column = lambda rows, width, at: pl.BlockSpec((rows, width), lambda i: (0, at))
    both = HALF // shared
    return pl.pallas_call(
        lambda *refs: backward_kernel(group, *refs),
        grid=(segs,),
        out_shape=(
            jax.ShapeDtypeStruct((length, width), bf16),
            jax.ShapeDtypeStruct((length, STATE), f32),
            jax.ShapeDtypeStruct((length, STATE), f32),
            jax.ShapeDtypeStruct((length, LANES), f32),
            jax.ShapeDtypeStruct((8, width), f32),
            jax.ShapeDtypeStruct((1, width), f32),
            jax.ShapeDtypeStruct((8, LANES), f32),
            jax.ShapeDtypeStruct((8, width), f32),
            jax.ShapeDtypeStruct((STATE, width), f32),
        ),
        in_specs=[
            back(width, group),
            ahead(width, group),
            column(8, width, group),
            column(8, width, group),
            back(shared, both),
            ahead(shared, both),
            column(8, shared, both),
            column(8, shared, both),
            full_block((8, LANES)),
            column(1, width, group),
            column(STATE, width, group),
            pl.BlockSpec((1, STATE, width), lambda i: (segs - 1 - i, 0, group)),
            back(width, group),
            back(width, group),
            pl.BlockSpec(memory_space=pltpu.SMEM),
        ],
        out_specs=(
            back(width),
            back(STATE),
            back(STATE),
            back(LANES),
            full_block((8, width)),
            full_block((1, width)),
            full_block((8, LANES)),
            full_block((8, width)),
            full_block((STATE, width)),
        ),
        scratch_shapes=[
            pltpu.VMEM((STATE, width), f32),
            pltpu.VMEM((STATE, width), bf16),
            pltpu.VMEM((seg_len, width), bf16),
            pltpu.VMEM((seg_len, width), bf16),
            pltpu.VMEM((seg_len, width), f32),
            pltpu.VMEM((seg_len, width), f32),
            pltpu.VMEM((seg_len, width), f32),
            pltpu.VMEM((8, width), f32),
        ],
        compiler_params=pltpu.CompilerParams(
            dimension_semantics=("arbitrary",), vmem_limit_bytes=VMEM_LIMIT
        ),
        cost_estimate=LIGHT,
    )(
        proj, proj, taps, rim, proj, proj, taps, rim, head, skip, end, prior, values, grad_values,
        core.reshape(1).astype(jnp.int32),
    )


def half_kernel(transposed, count, core_ref, *refs):
    inputs, mine_ref, theirs_ref = refs[: 2 * count], refs[-2], refs[-1]
    total = refs[2 * count][...] if len(refs) > 2 * count + 2 else 0.0
    for left, right in zip(inputs[:count], inputs[count:]):
        total = total + dot(left[...], right[...], ((1,), (1 if transposed else 0,)))
    own = lax.rem(pl.program_id(0), 2) == core_ref[0]

    @pl.when(own)
    def _():
        mine_ref[0] = total

    @pl.when(jnp.logical_not(own))
    def _():
        theirs_ref[0] = total.astype(bf16)


def half_products(core, terms, seg_len, width, transposed, base=()):
    length = terms[0][0].shape[0]
    left = [pl.BlockSpec((seg_len, array.shape[1]), lambda i, core: (i, 0)) for array, _, _ in terms]
    right = []
    for array, matrix, at in terms:
        if transposed:
            right.append(pl.BlockSpec((width, array.shape[1]), lambda i, core, at=at: (0, at(core[0]))))
        else:
            right.append(pl.BlockSpec(matrix.shape, lambda i, core: (0, 0)))
    depth = sum(array.shape[1] for array, _, _ in terms)
    mine, theirs = pl.pallas_call(
        lambda *refs: half_kernel(transposed, len(terms), *refs),
        grid_spec=pltpu.PrefetchScalarGridSpec(
            num_scalar_prefetch=1,
            grid=(length // seg_len,),
            in_specs=left + right + [pl.BlockSpec((seg_len, width), lambda i, core: (i, 0)) for _ in base],
            out_specs=[pl.BlockSpec((1, seg_len, width), lambda i, core: (i // 2, 0, 0))] * 2,
        ),
        out_shape=(
            jax.ShapeDtypeStruct((length // seg_len // 2, seg_len, width), f32),
            jax.ShapeDtypeStruct((length // seg_len // 2, seg_len, width), bf16),
        ),
        compiler_params=pltpu.CompilerParams(dimension_semantics=("arbitrary",), vmem_limit_bytes=VMEM_LIMIT),
        cost_estimate=LIGHT,
    )(core.reshape(1).astype(jnp.int32), *[array for array, _, _ in terms], *[matrix for _, matrix, _ in terms], *base)
    return mine, theirs


def shared_kernel(core_ref, proj_ref, rim_ref, taps_ref, mine_ref, other_ref, grad_ref, taps_grad_ref, edge_ref):
    total, seen = conv_parts(proj_ref[...], rim_ref[...], taps_ref[...])
    sigmoid = jax.nn.sigmoid(total)
    grad_total = mine_ref[...] + other_ref[...]
    grad_total = grad_total * (sigmoid * (1.0 + total * (1.0 - sigmoid)))
    sums = [jnp.sum(grad_total * part, axis=0, keepdims=True) for part in seen]
    sums = sums + [jnp.sum(grad_total, axis=0, keepdims=True), jnp.zeros((8 - CONV - 1, LANES), f32)]
    taps_grad_ref[...] = jnp.concatenate(sums, axis=0)
    edge_ref[...] = grad_total[:8]
    taps = taps_ref[...]
    extended = jnp.concatenate([grad_total, jnp.zeros((8, LANES), f32)], axis=0)
    grad_conv = taps[CONV - 1 : CONV] * grad_total
    for k in range(CONV - 1):
        grad_conv = grad_conv + taps[k : k + 1] * extended[CONV - 1 - k : CONV - 1 - k + grad_total.shape[0]]
    grad_ref[...] = grad_conv.astype(bf16)


def shared_backward(core, proj, rim, taps, mine, other):
    length = proj.shape[0]
    picked = lambda rows: pl.BlockSpec((rows, LANES), lambda i, core: (0, HALF // LANES + core[0]))
    whole = lambda rows: pl.BlockSpec((rows, LANES), lambda i, core: (0, 0))
    return pl.pallas_call(
        shared_kernel,
        grid_spec=pltpu.PrefetchScalarGridSpec(
            num_scalar_prefetch=1,
            grid=(1,),
            in_specs=[picked(length), picked(8), picked(8), whole(length), whole(length)],
            out_specs=(whole(length), whole(8), whole(8)),
        ),
        out_shape=(
            jax.ShapeDtypeStruct((length, LANES), bf16),
            jax.ShapeDtypeStruct((8, LANES), f32),
            jax.ShapeDtypeStruct((8, LANES), f32),
        ),
        compiler_params=pltpu.CompilerParams(vmem_limit_bytes=VMEM_LIMIT),
        cost_estimate=LIGHT,
    )(core.reshape(1).astype(jnp.int32), proj, rim, taps, mine, other)


def per_device(hidden_in, cotangent, in_proj, out_proj, conv_params, pre_gain, gated_gain, head_params):
    chips, line = lax.axis_size("chip"), lax.axis_size("seg")
    core, place = lax.axis_index("core"), lax.axis_index("seg")
    rows, model_width = in_proj.shape[0], hidden_in.shape[2]
    heads = HEADS // 2

    conv_width, gain_width = conv_params.shape[1], gated_gain.shape[0]
    used = HALF + 2 * STATE + heads
    spare = -used % LANES
    small = jnp.zeros((rows, spare), bf16)
    small = small.at[: CONV + 1, :conv_width].set(conv_params)
    small = small.at[CONV + 1, :rows].set(pre_gain)
    small = small.at[CONV + 2, :gain_width].set(gated_gain)

    def conv_side(which):
        return jnp.concatenate(
            [
                own_columns(in_proj[:, INNER : 2 * INNER], which),
                in_proj[:, 2 * INNER : INNER + XBC],
                own_columns(in_proj[:, INNER + XBC :], which),
                small,
            ],
            axis=1,
        )

    def gate_side(which):
        return own_columns(in_proj[:, :INNER], which)

    conv_swap = to_partner(conv_side(1 - core))
    conv_block = in_core_order(conv_side(core), conv_swap, core, 0)
    conv_z = gather_step(conv_block, 2)
    gate_swap = to_partner(gate_side(1 - core))
    gate_block = in_core_order(gate_side(core), gate_swap, core, 0)
    conv_z, hidden_in, gate_block = tie(conv_z, hidden_in, gate_block)
    conv_own = jnp.stack(conv_z)
    conv_near = gather_plane(conv_own, near_steps())
    hidden_got = send_sequence(hidden_in, place)
    conv_own, conv_near, hidden_got, gate_block = tie(conv_own, conv_near, hidden_got, gate_block)
    hidden_half = order_sequence(hidden_got, place)
    conv_far = gather_plane(conv_own, far_steps())
    gate_z = gather_step(gate_block, 2)
    hidden_other = to_partner(hidden_half)
    conv_far, gate_z, hidden_other, out_proj = tie(conv_far, gate_z, hidden_other, out_proj)
    out_own = out_proj[None]
    out_other = exchanged(out_own, 1)
    gate_own = jnp.stack(gate_z)
    gate_near = gather_plane(gate_own, near_steps())
    conv_all = whole_matrix([conv_own, *conv_near, *conv_far], True)

    small_all = conv_all.reshape(chips, 2, line, rows, -1)[..., used:].astype(f32)
    taps_full = small_all[..., : CONV + 1, :conv_width].transpose(3, 0, 1, 2, 4).reshape(CONV + 1, XBC)
    taps = jnp.concatenate([own_columns(taps_full[:, :INNER], core), taps_full[:, INNER:]], axis=1)
    gain_pre = small_all[..., CONV + 1, :rows].reshape(model_width)
    gain_gate = lax.dynamic_index_in_dim(
        small_all[..., CONV + 2, :gain_width], core, axis=1, keepdims=False
    ).reshape(HALF)
    params = own_columns(head_params, core)

    seg_len = hidden_half.shape[1]
    tokens = SEGS * seg_len
    normed, normed_turned = normed_tokens(core, hidden_half, hidden_other, gain_pre, rows)
    projected = dot(normed, conv_all, ((1,), (0,)))
    projected, gate_own, gate_near, out_own, out_other = tie(projected, gate_own, gate_near, out_own, out_other)
    gate_far = gather_plane(gate_own, far_steps())
    out_own = jnp.concatenate([out_own, out_other])
    out_others = []
    for bit in range(1, (line - 1).bit_length()):
        out_others.append(exchanged(out_own, 2**bit))
        if 2 ** (bit + 1) < line:
            out_own, out_others = jnp.concatenate([out_own, out_others[-1]]), []

    taps = jnp.pad(taps, ((0, 8 - CONV - 1), (0, projected.shape[1] - taps.shape[1])))
    head = jnp.pad(jnp.stack([-jnp.exp(params[0]), params[1]]), ((0, 6), (0, LANES - heads)))
    skip = jnp.repeat(params[2], HEADDIM).reshape(1, HALF)
    wide = HALF + 2 * STATE
    rim = borrowed(projected[tokens - 8 :], 1)
    nothing = jnp.zeros((STATE, HALF), f32)
    values, prior, final, last = scan_forward(projected, taps, head, skip, rim, nothing, seg_len)
    if line > SEGS:
        last = jnp.sum(last.reshape(SEGS, 8, LANES)[:, 0, :heads], axis=0)
        decay = jnp.repeat(jnp.exp2(last), HEADDIM)
        begin = entering(decay, final, 1)
        values, prior, _, _ = scan_forward(projected, taps, head, skip, rim, begin, seg_len)

    values, gate_far, out_others, cotangent = tie(values, gate_far, out_others, cotangent)
    cot_got = send_sequence(cotangent, place)
    out_own = jnp.concatenate([out_own, *out_others])
    out_all = gather_plane(out_own, plane_steps())
    gate_matrix = whole_matrix([gate_own, *gate_near, *gate_far], True)
    gate_input = dot(normed, gate_matrix, ((1,), (0,)))
    gate_input, cot_first = tie(gate_input, cot_got[0])

    silu_gate = jax.nn.silu(gate_input)
    gated = values * silu_gate
    squares = jnp.sum(gated * gated, axis=1)
    squares_other = to_partner(squares)
    scale = lax.rsqrt((squares + squares_other) / INNER + epsilon)[:, None]
    mixed, mixed_turned = mixed_tokens(gated, scale, gain_gate, seg_len)
    mixed_turned, out_all, cot_second = tie(mixed_turned, out_all, cot_got[1])
    cot_half = order_sequence([cot_first, cot_second], place)
    cot_other = to_partner(cot_half)
    cot = in_core_order(cot_half, cot_other, core, 1)
    upstream = cot.reshape(tokens, model_width)
    by_owner = lambda grad: grad.astype(bf16).reshape(chip_dims() + (-1, grad.shape[1]))
    out_grad = by_owner(dot(mixed_turned, upstream, ((1,), (0,))))
    out_got_near = reduce_plane([out_grad], near_steps())
    out_matrix = whole_matrix([out_own, *out_all], False, True)
    branch, branch_sent = half_products(core, [(mixed, out_matrix, None)], seg_len, model_width, False)
    branch_sent, upstream = tie(branch_sent, upstream)
    branch_other = to_partner(branch_sent)
    grad_mixed = dot(upstream, out_matrix, ((1,), (1,)))
    grad_mixed, out_got_near, out_grad = tie(grad_mixed, out_got_near, out_grad)
    out_got_far = reduce_plane([out_grad], far_steps())
    unit = gated * scale
    gain_grad = grad_mixed * gain_gate
    along = jnp.sum(gain_grad * unit, axis=1)
    along_other = to_partner(along)
    along_other, branch_other = tie(along_other, branch_other)
    hidden_out = send_back((hidden_half.astype(f32) + branch + branch_other.astype(f32)).astype(bf16), place)
    along = ((along + along_other) / INNER)[:, None]
    gate_gain_grad = jnp.sum(grad_mixed * unit, axis=0)
    grad_gated = scale * (gain_grad - unit * along)
    grad_values = grad_gated * silu_gate
    sigmoid = jax.nn.sigmoid(gate_input)
    grad_gate = (grad_gated * values * (sigmoid * (1.0 + gate_input * (1.0 - sigmoid)))).astype(bf16)
    gate_grad = by_owner(dot(normed_turned, grad_gate, ((1,), (0,))))
    gate_grad, grad_values, out_got_far = tie(gate_grad, grad_values, out_got_far)
    gate_got = reduce_plane([gate_grad], plane_steps())
    scan = lambda later: scan_backward(
        0, core, projected, taps, head, skip, rim, later, prior, values, grad_values, seg_len
    )
    if line > SEGS:
        nothing = entering(decay, scan(nothing)[-1], -1)
    back = scan(nothing)
    back, gate_got, hidden_out, grad_gate = tie(back, gate_got, hidden_out, grad_gate)
    ((early_kept, early_got),) = reduce_z(
        [
            ([plane_part([out_grad], 0, 0)], [*out_got_near, *out_got_far]),
            ([plane_part([gate_grad], 0, 0)], gate_got),
        ]
    )
    grad_x, mine, theirs, grad_raw, x_taps_grad, skip_grad, head_sums, x_edge, _ = back
    grad_x = spilled(grad_x, x_edge, taps[:, :HALF])
    other = to_partner(theirs)
    x_grad = by_owner(dot(normed_turned, grad_x, ((1,), (0,))))
    other, x_grad = tie(other, x_grad)
    grad_state, state_taps_grad, state_edge = shared_backward(core, projected, rim, taps, mine, other)
    grad_state = spilled(grad_state, state_edge, lax.dynamic_slice_in_dim(taps, HALF + core * STATE, STATE, axis=1))
    grad_raw = grad_raw.astype(bf16)
    rest_grad = by_owner(dot(normed_turned, jnp.concatenate([grad_state, grad_raw], axis=1), ((1,), (0,))))
    rest_grad, x_grad, grad_gate = tie(rest_grad, x_grad, grad_gate)
    conv_near = reduce_plane([x_grad, rest_grad], near_steps())
    base = dot(grad_gate, gate_matrix, ((1,), (1,)))
    terms = [
        (grad_x, conv_all, lambda core: 0),
        (grad_state, conv_all, lambda core: HALF // LANES + core),
        (grad_raw, conv_all, lambda core: (HALF + 2 * STATE) // LANES),
    ]
    grad_normed, sent_normed = half_products(core, terms, seg_len, model_width, True, (base,))
    row = lax.broadcasted_iota(jnp.int32, (8, 1), 0)
    small = x_taps_grad + jnp.where(row == CONV + 1, gate_gain_grad, 0.0) + jnp.where(row == CONV + 2, skip_grad, 0.0)
    small = jnp.concatenate([small, state_taps_grad + head_sums], axis=1)
    sent_normed, early_got, conv_near, small, x_grad, rest_grad = tie(
        sent_normed, early_got, conv_near, small, x_grad, rest_grad
    )
    other_normed = to_partner(sent_normed)
    wide_hidden = hidden_half.astype(f32)
    hidden_scale = lax.rsqrt(jnp.mean(wide_hidden * wide_hidden, axis=-1, keepdims=True) + epsilon)
    grad_normed = (grad_normed + other_normed.astype(f32)) * gain_pre
    hidden_unit = wide_hidden * hidden_scale
    along = jnp.mean(grad_normed * hidden_unit, axis=-1, keepdims=True)
    grad_hidden = hidden_scale * (grad_normed - hidden_unit * along)
    grad_in = (cot_half.astype(f32) + grad_hidden).astype(bf16)
    grad_in, x_grad, rest_grad = tie(grad_in, x_grad, rest_grad)
    grad_in = send_back(grad_in, place)
    conv_far = reduce_plane([x_grad, rest_grad], far_steps())
    grad_in, conv_far = tie(grad_in, conv_far)
    late = reduce_z([([plane_part([x_grad, rest_grad], 0, 0)], [*conv_near, *conv_far])])
    for dim in range(2):
        small = small + sum(moved(small, dim, by) for by in range(1, chip_dims()[dim]))
    for bit in range((line - 1).bit_length()):
        small = small + exchanged(small, 2**bit)
    small_other = to_partner(small)
    late_got, small_other = tie(arrivals(late), small_other)
    early_share = total([*early_kept, *early_got])
    out_share = early_share[:, :model_width]
    paired = lambda share: share.astype(bf16).reshape(2, rows, -1)
    gate_share, conv_share = paired(early_share[:, model_width:]), paired(reduce_end(arrived(late, late_got)))

    def mine_and_partner(share):
        keep = lax.dynamic_index_in_dim(share, core, axis=0, keepdims=False)
        give = lax.dynamic_index_in_dim(share, 1 - core, axis=0, keepdims=False)
        return keep, to_partner(give)

    both = in_core_order(small, small_other, core, 0)
    natural = lambda array, width: array.reshape(2, -1, chips, width).transpose(1, 2, 0, 3).reshape(-1, 2 * chips * width)
    device = (lax.axis_index("chip") * 2 + core) * line + place
    columns = natural(both[:, :, :HALF], HALF // chips)
    taps_all = jnp.concatenate([columns, both[0, :, HALF:], both[1, :, HALF:]], axis=1)[: CONV + 1]
    taps_share = lax.dynamic_slice_in_dim(taps_all, device * conv_width, conv_width, axis=1)
    gain_share = lax.dynamic_slice_in_dim(columns[CONV + 1], device * gain_width, gain_width, axis=0)
    head_total = jnp.concatenate(
        [
            natural(both[:, CONV + 1 : CONV + 3, HALF : HALF + heads], heads // chips),
            jnp.sum(columns[CONV + 2].reshape(1, HEADS, HEADDIM), axis=2),
        ]
    )

    def interleave(mine, theirs):
        width = mine.shape[1] // chips
        both = in_core_order(mine.reshape(rows, chips, width), theirs.reshape(rows, chips, width), core, 2)
        return both.reshape(rows, -1)

    keep_gate, got_gate = mine_and_partner(gate_share)
    keep, got = mine_and_partner(conv_share)
    state_end = HALF + STATE
    in_share = jnp.concatenate(
        [
            interleave(keep_gate, got_gate),
            interleave(keep[:, :HALF], got[:, :HALF]),
            in_core_order(keep[:, HALF:state_end], got[:, HALF:state_end], core, 1).reshape(rows, -1),
            interleave(keep[:, state_end : state_end + heads], got[:, state_end : state_end + heads]),
        ],
        axis=1,
    ).astype(f32)
    pre_share = jnp.sum(in_proj.astype(f32) * in_share, axis=1) / pre_gain.astype(f32)
    hidden_out, grad_in = order_back(hidden_out, place), order_back(grad_in, place)
    return (hidden_out, grad_in, in_share, out_share, taps_share, pre_share, gain_share, head_total)


def solution(mesh):
    devices = mesh.devices
    cores = Mesh(devices.reshape(devices.shape[0] // 2, 2, devices.shape[1]), ("chip", "core", "seg"))
    dp, both = ("chip", "core"), ("chip", "core", "seg")
    tokens = P(dp, "seg", None)
    return jax.shard_map(
        per_device,
        mesh=cores,
        in_specs=(tokens, tokens, P(both, None), P(both, None), P(None, both), P(both), P(both), P()),
        out_specs=(tokens, tokens, P(both, None), P(both, None), P(None, both), P(both), P(both), P()),
        check_vma=False,
    )
```

```python
import jax
import jax.numpy as jnp
from jax import lax
from jax.experimental import pallas as pl
from jax.experimental.pallas import tpu as pltpu
from jax.sharding import Mesh
from jax.sharding import PartitionSpec as P

HEADS = 48
HEADDIM = 64
STATE = 128
CONV = 4
INNER = 3072
XBC = 3328
HALF = INNER // 2
LANES = 128
SEGS = 4
LIGHT = pl.CostEstimate(flops=1024, bytes_accessed=1024, transcendentals=0)
VMEM_LIMIT = 48 * 1024 * 1024
LOG2E = 1.4426950408889634

epsilon = 1e-05
f32 = jnp.float32
bf16 = jnp.bfloat16


def own_columns(array, core):
    chips = lax.axis_size("chip")
    width = array.shape[-1] // (2 * chips)
    parted = array.reshape(array.shape[:-1] + (chips, 2, width))
    picked = lax.dynamic_index_in_dim(parted, core, axis=parted.ndim - 2, keepdims=False)
    return picked.reshape(array.shape[:-1] + (chips * width,))


def to_partner(array):
    return lax.ppermute(array, "core", [(0, 1), (1, 0)])


def in_core_order(mine, theirs, core, axis):
    first = jnp.where(core == 0, mine, theirs)
    second = jnp.where(core == 0, theirs, mine)
    return jnp.stack([first, second], axis=axis)


def chip_dims():
    return (lax.axis_size("chip") // 2, 2, lax.axis_size("seg"))


def chip_place():
    chip = lax.axis_index("chip")
    return (chip // 2, chip % 2, lax.axis_index("seg"))


def moved(array, dim, by):
    sizes = chip_dims()
    index = lambda at: (at[0] * sizes[1] + at[1]) * sizes[2] + at[2]
    pairs = []
    for a in range(sizes[0]):
        for b in range(sizes[1]):
            for z in range(sizes[2]):
                to = [a, b, z]
                to[dim] = (to[dim] + by) % sizes[dim]
                pairs.append((index((a, b, z)), index(to)))
    return lax.ppermute(array, ("chip", "seg"), pairs)


def tie(*values):
    return lax.optimization_barrier(values)


def gather_step(data, dim):
    return [data] + [moved(data, dim, by) for by in range(1, chip_dims()[dim])]


def exchanged(array, by):
    line = lax.axis_size("seg")
    return lax.ppermute(array, "seg", [(at, at ^ by) for at in range(line)])


def plane_steps():
    a, b, _ = chip_dims()
    steps = [(at // b, at % b) for at in range(1, a * b)]
    return sorted(steps, key=lambda by: bool(by[0] and by[1]))


def near_steps():
    a, b, _ = chip_dims()
    return plane_steps()[: a + b - 2]


def far_steps():
    a, b, _ = chip_dims()
    return plane_steps()[a + b - 2 :]


def moved_plane(array, by_a, by_b):
    a, b, z = chip_dims()
    pairs = [
        ((at_a * b + at_b) * z + at_z, ((at_a + by_a) % a * b + (at_b + by_b) % b) * z + at_z)
        for at_a in range(a)
        for at_b in range(b)
        for at_z in range(z)
    ]
    return lax.ppermute(array, ("chip", "seg"), pairs)


def gather_plane(data, steps):
    return [moved_plane(data, *by) for by in steps]


ORDERS = ((0, 1), (1, 0))


def halves_step(parts, step):
    return [gather_step(jnp.stack(part), order[step]) for order, part in zip(ORDERS, parts)]


def placed_halves_kernel(plan, place_ref, *refs):
    sources, target, sems = refs[:-2], refs[-2], refs[-1]
    copies = []
    for source, lead, at, half in plan:
        spot = [lax.rem(place_ref[dim] + (size - back), size) for dim, (back, size) in enumerate(at)]
        to = target.at[spot[0], spot[1], half, spot[2]]
        copies.append(pltpu.make_async_copy(sources[source].at[lead], to, sems.at[len(copies)]))
    for copy in copies:
        copy.start()
    for copy in copies:
        copy.wait()


def matrix_of_halves(halves):
    sizes = chip_dims()
    plan, sources = [], []
    for half, (order, part) in enumerate(zip(ORDERS, halves)):
        for back_last, piece in enumerate(part):
            for back_mid in range(sizes[order[0]]):
                for back_z in range(sizes[2]):
                    at = [None, None, (back_z, sizes[2])]
                    at[order[1]] = (back_last, sizes[order[1]])
                    at[order[0]] = (back_mid, sizes[order[0]])
                    plan.append((len(sources), (back_mid, back_z), at, half))
            sources.append(piece)
    shape = sizes[:2] + (2, sizes[2]) + sources[0].shape[2:]
    anywhere = pl.BlockSpec(memory_space=pl.ANY)
    whole = pl.pallas_call(
        lambda *refs: placed_halves_kernel(plan, *refs),
        out_shape=jax.ShapeDtypeStruct(shape, bf16),
        in_specs=[pl.BlockSpec(memory_space=pltpu.SMEM)] + [anywhere] * len(sources),
        out_specs=pl.BlockSpec(memory_space=pltpu.VMEM),
        scratch_shapes=[pltpu.SemaphoreType.DMA((len(plan),))],
        compiler_params=pltpu.CompilerParams(vmem_limit_bytes=VMEM_LIMIT),
        cost_estimate=LIGHT,
    )(jnp.stack(chip_place()).astype(jnp.int32), *sources)
    return whole.reshape(-1, shape[-1])


def placed_kernel(plan, place_ref, *refs):
    sources, target, sems = refs[:-2], refs[-2], refs[-1]
    copies = []
    for source, lead, at, paired in plan:
        spot = [lax.rem(place_ref[dim] + (size - back), size) for dim, (back, size) in enumerate(at)]
        spot.append(place_ref[2 + lead])
        to = target.at[spot[0], spot[1], :, spot[2]] if paired else target.at[spot[0], spot[1], spot[2]]
        copies.append(pltpu.make_async_copy(sources[source].at[lead], to, sems.at[len(copies)]))
    for copy in copies:
        copy.start()
    for copy in copies:
        copy.wait()


def whole_matrix(gathered, paired, by_bits=False):
    a, b, z = chip_dims()
    at_a, at_b, at_z = chip_place()
    spots = [at_z ^ back if by_bits else (at_z + z - back) % z for back in range(z)]
    plan = [
        (source, back, ((by[0], a), (by[1], b)), paired)
        for source, by in enumerate([(0, 0)] + plane_steps())
        for back in range(z)
    ]
    block = gathered[0].shape[1:]
    shape = (a, b, 2, z) + block[1:] if paired else (a, b, z) + block
    anywhere = pl.BlockSpec(memory_space=pl.ANY)
    whole = pl.pallas_call(
        lambda *refs: placed_kernel(plan, *refs),
        out_shape=jax.ShapeDtypeStruct(shape, bf16),
        in_specs=[pl.BlockSpec(memory_space=pltpu.SMEM)] + [anywhere] * len(gathered),
        out_specs=pl.BlockSpec(memory_space=pltpu.VMEM),
        scratch_shapes=[pltpu.SemaphoreType.DMA((len(plan),))],
        compiler_params=pltpu.CompilerParams(vmem_limit_bytes=VMEM_LIMIT),
        cost_estimate=LIGHT,
    )(jnp.stack([at_a, at_b, *spots]).astype(jnp.int32), *gathered)
    return whole.reshape(-1, shape[-1])


def total(terms):
    result = terms[0].astype(f32)
    for term in terms[1:]:
        result = result + term.astype(f32)
    return result


def reduce_send(terms, axis, dim, wire):
    place, size = chip_place()[dim], chip_dims()[dim]
    pick = lambda at: [lax.dynamic_index_in_dim(term, at, axis=axis, keepdims=False) for term in terms]
    received = [moved(total(pick((place + by) % size)).astype(wire), dim, by) for by in range(1, size)]
    return pick(place), received


def plane_part(partials, by_a, by_b):
    (at_a, at_b, _), (a, b, _) = chip_place(), chip_dims()
    chip = (at_a + by_a) % a * b + (at_b + by_b) % b
    flat = [partial.reshape((a * b,) + partial.shape[2:]) for partial in partials]
    return jnp.concatenate([lax.dynamic_index_in_dim(array, chip, axis=0, keepdims=False) for array in flat], axis=-1)


def reduce_plane(partials, steps):
    return [moved_plane(plane_part(partials, *by), *by) for by in steps]


def reduce_z(firsts):
    joined = jnp.concatenate([total(kept + received) for kept, received in firsts], axis=-1)
    return [reduce_send([joined], 0, 2, bf16)]


def reduce_end(third):
    return total(third[0][0] + third[0][1])


def arrivals(parts):
    return [received for _, received in parts]


def arrived(parts, received):
    return [(kept, new) for (kept, _), new in zip(parts, received)]


def line_perm(turn, back):
    line = lax.axis_size("seg")
    parts = line // SEGS
    pairs = []
    for core in range(2):
        for place in range(line):
            half, odd = divmod(place % SEGS, 2)
            source = core * line + place
            target = odd * line + (2 * core + (half ^ turn)) * parts + place // SEGS
            pairs.append((target, source) if back else (source, target))
    return pairs


def swapped(pair, turn):
    return [jnp.where(turn == 0, pair[0], pair[1]), jnp.where(turn == 0, pair[1], pair[0])]


def send_sequence(array, place):
    pieces = swapped([array[0], array[1]], (place % SEGS) // 2)
    return [lax.ppermute(piece, ("core", "seg"), line_perm(turn, False)) for turn, piece in enumerate(pieces)]


def order_sequence(got, place):
    parts = lax.axis_size("seg") // SEGS
    return jnp.stack(swapped(got, (place // parts) % 2))


def send_back(ordered, place):
    parts = lax.axis_size("seg") // SEGS
    pieces = swapped([ordered[0], ordered[1]], (place // parts) % 2)
    return [lax.ppermute(piece, ("core", "seg"), line_perm(turn, True)) for turn, piece in enumerate(pieces)]


def order_back(got, place):
    return jnp.stack(swapped(got, (place % SEGS) // 2))


def part_pairs(step):
    line = lax.axis_size("seg")
    parts = line // SEGS
    return [(i, i + step) for i in range(line) if 0 <= i + step < line and i // parts == (i + step) // parts]


def entering(decay, state, step):
    parts = lax.axis_size("seg") // SEGS
    total = jnp.zeros_like(state)
    for _ in range(parts - 1):
        total = lax.ppermute(decay * total + state, "seg", part_pairs(step))
    return total


def borrowed(array, step):
    parts = lax.axis_size("seg") // SEGS
    if parts == 1:
        return jnp.zeros_like(array)
    return lax.ppermute(array, "seg", part_pairs(step))


def spilled(grad, edge, taps):
    if lax.axis_size("seg") == SEGS:
        return grad
    edge = borrowed(edge, -1)
    spill = jnp.stack(
        [
            sum(taps[k] * edge[CONV - 1 - k - early] for k in range(CONV - early))
            for early in range(CONV - 1, 0, -1)
        ]
    )
    at = grad.shape[0] - CONV + 1
    return grad.at[at:].set((grad[at:].astype(f32) + spill).astype(bf16))


def dot(a, b, contract):
    return lax.dot_general(a, b, (contract, ((), ())), preferred_element_type=f32)


def normed_kernel(slabs, core_ref, mine_ref, other_ref, gain_ref, normed_ref, turned_ref):
    own = lax.rem(pl.program_id(0), 2) == core_ref[0]
    hidden = jnp.where(own, mine_ref[0], other_ref[0]).astype(f32)
    scale = lax.rsqrt(jnp.mean(hidden * hidden, axis=1, keepdims=True) + epsilon)
    normed = hidden * scale * gain_ref[...]
    normed_ref[...] = normed.astype(bf16)
    turned = normed.T.astype(bf16)
    for to, at, size in slabs:
        turned_ref[to : to + size] = turned[at : at + size]


def normed_tokens(core, mine, other, gain, rows):
    segs, seg_len, width = 2 * mine.shape[0], mine.shape[1], mine.shape[2]
    a, b, z = chip_dims()
    group = 2 * z * rows
    inside = rows % 16 == 0
    slabs = [(0, 0, width)]
    if inside:
        slabs = [
            (chip * group + (at * 2 + core_at) * rows, chip * group + (core_at * z + at) * rows, rows)
            for chip in range(a * b)
            for core_at in range(2)
            for at in range(z)
        ]
    normed, turned = pl.pallas_call(
        lambda *refs: normed_kernel(slabs, *refs),
        grid_spec=pltpu.PrefetchScalarGridSpec(
            num_scalar_prefetch=1,
            grid=(segs,),
            in_specs=[
                pl.BlockSpec((1, seg_len, width), lambda i, core: (i // 2, 0, 0)),
                pl.BlockSpec((1, seg_len, width), lambda i, core: (i // 2, 0, 0)),
                pl.BlockSpec((1, width), lambda i, core: (0, 0)),
            ],
            out_specs=(
                pl.BlockSpec((seg_len, width), lambda i, core: (i, 0)),
                pl.BlockSpec((width, seg_len), lambda i, core: (0, i)),
            ),
        ),
        out_shape=(
            jax.ShapeDtypeStruct((segs * seg_len, width), bf16),
            jax.ShapeDtypeStruct((width, segs * seg_len), bf16),
        ),
        compiler_params=pltpu.CompilerParams(dimension_semantics=("arbitrary",), vmem_limit_bytes=VMEM_LIMIT),
        cost_estimate=LIGHT,
    )(core.reshape(1).astype(jnp.int32), mine, other, gain.reshape(1, width))
    if not inside:
        turned = turned.reshape(a, b, 2, z, rows, -1).transpose(0, 1, 3, 2, 4, 5).reshape(turned.shape)
    return normed, turned


def mixed_kernel(gated_ref, scale_ref, gain_ref, mixed_ref, turned_ref):
    mixed = gated_ref[...] * scale_ref[...] * gain_ref[...]
    mixed_ref[...] = mixed.astype(bf16)
    turned_ref[...] = mixed.T.astype(bf16)


def mixed_tokens(gated, scale, gain, seg_len):
    length, width = gated.shape
    return pl.pallas_call(
        mixed_kernel,
        grid=(length // seg_len,),
        in_specs=[
            pl.BlockSpec((seg_len, width), lambda i: (i, 0)),
            pl.BlockSpec((seg_len, 1), lambda i: (i, 0)),
            pl.BlockSpec((1, width), lambda i: (0, 0)),
        ],
        out_specs=(
            pl.BlockSpec((seg_len, width), lambda i: (i, 0)),
            pl.BlockSpec((width, seg_len), lambda i: (0, i)),
        ),
        out_shape=(
            jax.ShapeDtypeStruct((length, width), bf16),
            jax.ShapeDtypeStruct((width, length), bf16),
        ),
        compiler_params=pltpu.CompilerParams(dimension_semantics=("arbitrary",), vmem_limit_bytes=VMEM_LIMIT),
        cost_estimate=LIGHT,
    )(gated, scale, gain.reshape(1, width))


def columns_of(pair):
    return pl.ds(pair * LANES, LANES)


def low_half(shape):
    return lax.broadcasted_iota(jnp.int32, shape, len(shape) - 1) < HEADDIM


def pair_columns(array, pair, low):
    rows = array.shape[0]
    first = jnp.broadcast_to(array[:, 2 * pair : 2 * pair + 1], (rows, LANES))
    second = jnp.broadcast_to(array[:, 2 * pair + 1 : 2 * pair + 2], (rows, LANES))
    return jnp.where(low, first, second)


def conv_parts(current, before, taps):
    rows = current.shape[0]
    padded = jnp.concatenate([before, current], axis=0)
    seen = [padded[8 - CONV + 1 + k : 8 - CONV + 1 + k + rows] for k in range(CONV - 1)] + [current]
    total = taps[CONV : CONV + 1]
    for k in range(CONV):
        total = total + taps[k : k + 1] * seen[k]
    return total, seen


def exact_sums(chosen, array):
    chosen = jnp.where(chosen, 1.0, 0.0).astype(bf16)
    result = 0.0
    for _ in range(3):
        part = array.astype(bf16)
        array = array - part.astype(f32)
        result = result + dot(chosen, part, ((1,), (0,)))
    return result


def step_terms(raw, head, seg_len):
    shifted = raw + head[1:2]
    step = jnp.maximum(shifted, 0.0) + jnp.log1p(jnp.exp(-jnp.abs(shifted)))
    log_decay = step * head[0:1]
    at_or_before = lax.broadcasted_iota(jnp.int32, (seg_len, seg_len), 0) >= lax.broadcasted_iota(
        jnp.int32, (seg_len, seg_len), 1
    )
    sums = exact_sums(at_or_before, log_decay)
    return shifted, step, log_decay, sums * LOG2E


def forward_kernel(
    proj_ref, taps_ref, head_ref, skip_ref, rim_ref, init_ref,
    values_ref, prior_ref, final_ref, last_ref, state_ref, tail_ref,
):
    seg_len = proj_ref.shape[0]
    half = seg_len // 2

    @pl.when(pl.program_id(0) == 0)
    def _():
        state_ref[...] = init_ref[...]
        tail_ref[...] = rim_ref[...]

    def activated(begin):
        at = pl.ds(begin, LANES)
        total, _ = conv_parts(proj_ref[:, at], tail_ref[:, at], taps_ref[:, at])
        return total * jax.nn.sigmoid(total)

    b_low = activated(HALF).astype(bf16)
    b_turned = activated(HALF).T.astype(bf16)
    c_low = activated(HALF + STATE).astype(bf16)
    _, step, _, sums = step_terms(proj_ref[:, HALF + 2 * STATE :], head_ref, seg_len)
    sums_turned, step_turned = sums.T, step.T
    scores = dot(c_low, b_low, ((1,), (1,)))
    kept = lax.broadcasted_iota(jnp.int32, (half, half), 0) >= lax.broadcasted_iota(jnp.int32, (half, half), 1)
    first_scores = jnp.where(kept, scores[:half, :half], 0.0)
    later_scores = scores[half:, :half]
    second_scores = jnp.where(kept, scores[half:, half:], 0.0)
    low = low_half((seg_len, LANES))
    last_ref[...] = jnp.broadcast_to(sums[seg_len - 1 :], last_ref.shape)

    for pair in range(HEADS // 4):
        at = columns_of(pair)
        x_values = activated(pair * LANES)
        x_low = x_values.astype(bf16)
        sums_pair = pair_columns(sums, pair, low)
        last_pair = sums_pair[seg_len - 1 :]
        carry = jnp.exp2(last_pair - sums_pair) * pair_columns(step, pair, low)
        scaled_x = (carry * x_low.astype(f32)).astype(bf16)
        prior = state_ref[:, at]
        prior_low = prior.astype(bf16)
        prior_ref[0, :, at] = prior_low
        from_state = jnp.exp2(sums_pair) * dot(c_low, prior_low, ((1,), (0,)))
        state_ref[:, at] = jnp.exp2(last_pair) * prior + dot(b_turned, scaled_x, ((1,), (0,)))
        early, late = 0.0, 0.0
        for side in range(2):
            head = 2 * pair + side
            x_side = jnp.where(low if side == 0 else ~low, x_values, 0.0).astype(bf16)
            at_token = jnp.broadcast_to(sums[:, head : head + 1], (seg_len, half))
            at_source, source_step = sums_turned[head : head + 1], step_turned[head : head + 1]
            first = jnp.exp2(jnp.minimum(at_token[:half] - at_source[:, :half], 0.0)) * first_scores
            first = (first * source_step[:, :half]).astype(bf16)
            later = jnp.exp2(at_token[half:] - at_source[:, :half]) * later_scores
            later = (later * source_step[:, :half]).astype(bf16)
            second = jnp.exp2(jnp.minimum(at_token[half:] - at_source[:, half:], 0.0)) * second_scores
            second = (second * source_step[:, half:]).astype(bf16)
            early = early + dot(first, x_side[:half], ((1,), (0,)))
            late = late + dot(jnp.concatenate([later, second], axis=1), x_side, ((1,), (0,)))
        intra = jnp.concatenate([early, late], axis=0)
        values_ref[:, at] = intra + from_state + skip_ref[:, at] * x_values

    tail_ref[...] = proj_ref[seg_len - 8 :, : HALF + 2 * STATE]
    final_ref[...] = state_ref[...]


def full_block(shape):
    return pl.BlockSpec(shape, lambda *_: (0,) * len(shape))


def scan_forward(proj, taps, head, skip, rim, init, seg_len):
    segs = proj.shape[0] // seg_len
    wide = HALF + 2 * STATE
    return pl.pallas_call(
        forward_kernel,
        grid=(segs,),
        out_shape=(
            jax.ShapeDtypeStruct((proj.shape[0], HALF), f32),
            jax.ShapeDtypeStruct((segs, STATE, HALF), bf16),
            jax.ShapeDtypeStruct((STATE, HALF), f32),
            jax.ShapeDtypeStruct((segs * 8, LANES), f32),
        ),
        in_specs=[
            pl.BlockSpec((seg_len, proj.shape[1]), lambda i: (i, 0)),
            full_block((8, wide)),
            full_block((8, LANES)),
            full_block((1, HALF)),
            full_block((8, wide)),
            full_block((STATE, HALF)),
        ],
        out_specs=(
            pl.BlockSpec((seg_len, HALF), lambda i: (i, 0)),
            pl.BlockSpec((1, STATE, HALF), lambda i: (i, 0, 0)),
            full_block((STATE, HALF)),
            pl.BlockSpec((8, LANES), lambda i: (i, 0)),
        ),
        scratch_shapes=[pltpu.VMEM((STATE, HALF), f32), pltpu.VMEM((8, wide), f32)],
        compiler_params=pltpu.CompilerParams(
            dimension_semantics=("arbitrary",), vmem_limit_bytes=VMEM_LIMIT
        ),
        cost_estimate=LIGHT,
    )(proj, taps, head, skip, rim, init)


def split_dot(array, other):
    high = array.astype(bf16)
    rest = (array - high.astype(f32)).astype(bf16)
    return dot(high, other, ((1,), (0,))) + dot(rest, other, ((1,), (0,)))


def backward_kernel(
    group, proj_ref, before_ref, taps_ref, rim_ref, shared_ref, shared_before_ref, shared_taps_ref, shared_rim_ref,
    head_ref, skip_ref, end_ref, prior_ref, values_ref, grad_ref, core_ref,
    grad_x_ref, mine_ref, theirs_ref, grad_raw_ref, taps_grad_ref, skip_grad_ref, head_grad_ref, edge_ref, start_ref,
    later_ref, local_ref, scaled_ref, grad_state_ref, inner_ref, source_ref, carry_ref, decay_ref,
):
    seg_len = proj_ref.shape[0]
    half = seg_len // 2
    turn = pl.program_id(0)

    @pl.when(turn == 0)
    def _():
        later_ref[...] = end_ref[...]
        edge_ref[...] = jnp.zeros_like(edge_ref)
        taps_grad_ref[...] = jnp.zeros_like(taps_grad_ref)
        skip_grad_ref[...] = jnp.zeros_like(skip_grad_ref)
        head_grad_ref[...] = jnp.zeros_like(head_grad_ref)

    first_segment = turn == pl.num_programs(0) - 1

    def conv_at(at, current, ahead, taps, rim):
        before = jnp.where(first_segment, rim[:, at], ahead[:, at])
        return conv_parts(current[:, at], before, taps[:, at])

    def activated(begin):
        total, _ = conv_at(pl.ds(begin, LANES), shared_ref, shared_before_ref, shared_taps_ref, shared_rim_ref)
        return total * jax.nn.sigmoid(total)

    b_values = activated(0)
    c_values = activated(STATE)
    b_low, c_low, c_turned = b_values.astype(bf16), c_values.astype(bf16), c_values.T.astype(bf16)
    shifted, step, log_decay, sums = step_terms(shared_ref[:, 2 * STATE :], head_ref, seg_len)
    sums_turned = sums.T
    scores = dot(b_low, c_low, ((1,), (1,)))
    kept = lax.broadcasted_iota(jnp.int32, (half, half), 0) <= lax.broadcasted_iota(jnp.int32, (half, half), 1)
    first_scores = jnp.where(kept, scores[:half, :half], 0.0)
    later_scores = scores[:half, half:]
    second_scores = jnp.where(kept, scores[half:, half:], 0.0)
    low = low_half((seg_len, LANES))
    first_grad, later_grad, second_grad = 0.0, 0.0, 0.0

    pairs = grad_ref.shape[1] // LANES
    for pair in range(pairs):
        at = columns_of(pair)
        total, seen = conv_at(at, proj_ref, before_ref, taps_ref, rim_ref)
        sigmoid = jax.nn.sigmoid(total)
        x_values = total * sigmoid
        x_low = x_values.astype(bf16)
        x_wide = x_low.astype(f32)
        sums_pair = pair_columns(sums, group * pairs + pair, low)
        step_pair = pair_columns(step, group * pairs + pair, low)
        last_pair = sums_pair[seg_len - 1 :]
        gap = jnp.exp2(last_pair - sums_pair)
        scaled_ref[:, at] = (gap * step_pair * x_wide).astype(bf16)
        grad_values = grad_ref[:, at]
        grad_state_ref[:, at] = (grad_values * jnp.exp2(sums_pair)).astype(bf16)
        later = later_ref[:, at]
        later_low = later.astype(bf16)
        local_ref[:, at] = later_low
        prior = prior_ref[0, :, at]
        decay_ref[:, at] = jnp.broadcast_to(
            jnp.sum(later * prior.astype(f32), axis=0, keepdims=True), (8, LANES)
        )
        grad_prior = dot(c_turned, grad_state_ref[:, at], ((1,), (0,)))
        later_ref[:, at] = jnp.exp2(last_pair) * later + grad_prior
        grad_scaled = dot(b_low, later_low, ((1,), (0,)))
        stepped = (step_pair * x_wide).astype(bf16)
        early, late = 0.0, 0.0
        for side in range(2):
            head = 2 * (group * pairs + pair) + side
            grad_low = jnp.where(low if side == 0 else ~low, grad_values, 0.0).astype(bf16)
            at_source = jnp.broadcast_to(sums[:, head : head + 1], (seg_len, half))
            at_token = sums_turned[head : head + 1]
            grad_weights = dot(stepped, grad_low, ((1,), (1,)))
            first = jnp.exp2(jnp.minimum(at_token[:, :half] - at_source[:half], 0.0))
            after = jnp.exp2(at_token[:, half:] - at_source[:half])
            second = jnp.exp2(jnp.minimum(at_token[:, half:] - at_source[half:], 0.0))
            first_grad = first_grad + first * grad_weights[:half, :half]
            later_grad = later_grad + after * grad_weights[:half, half:]
            second_grad = second_grad + second * grad_weights[half:, half:]
            upper = jnp.concatenate([first * first_scores, after * later_scores], axis=1).astype(bf16)
            early = early + dot(upper, grad_low, ((1,), (0,)))
            late = late + dot((second * second_scores).astype(bf16), grad_low[half:], ((1,), (0,)))
        inner = jnp.concatenate([early, late], axis=0)
        skip = skip_ref[:, at]
        skip_grad_ref[:, at] += jnp.sum(grad_values * x_values, axis=0, keepdims=True)
        inner_ref[:, at] = grad_values * (values_ref[:, at] - skip * x_values)
        source_ref[:, at] = x_wide * inner
        carry_ref[:, at] = x_wide * grad_scaled
        grad_x = skip * grad_values + step_pair * (inner + gap * grad_scaled)
        grad_total = grad_x * (sigmoid * (1.0 + total * (1.0 - sigmoid)))
        for k in range(CONV):
            taps_grad_ref[k : k + 1, at] += jnp.sum(grad_total * seen[k], axis=0, keepdims=True)
        taps_grad_ref[CONV : CONV + 1, at] += jnp.sum(grad_total, axis=0, keepdims=True)
        extended = jnp.concatenate([grad_total, edge_ref[:, at]], axis=0)
        edge_ref[:, at] = grad_total[:8]
        taps = taps_ref[:, at]
        grad_conv = taps[CONV - 1 : CONV] * grad_total
        for k in range(CONV - 1):
            grad_conv = grad_conv + taps[k : k + 1] * extended[CONV - 1 - k : CONV - 1 - k + seg_len]
        grad_x_ref[:, at] = grad_conv.astype(bf16)

    width = grad_ref.shape[1]
    channel = lax.broadcasted_iota(jnp.int32, (width, LANES), 0) // HEADDIM + group * width // HEADDIM
    heads = jnp.where(channel == lax.broadcasted_iota(jnp.int32, (width, LANES), 1), 1.0, 0.0).astype(bf16)
    tail = jnp.exp2(sums[seg_len - 1 :] - sums)
    source_grad = split_dot(source_ref[...], heads)
    step_grad = source_grad + tail * split_dot(carry_ref[...], heads)
    used = step * step_grad
    sum_grad = split_dot(inner_ref[...], heads) - used
    at_last = jnp.sum(used - step * source_grad, axis=0, keepdims=True)
    at_last = at_last + split_dot(decay_ref[...], heads)[:1] * jnp.exp2(sums[seg_len - 1 :])
    is_last = lax.broadcasted_iota(jnp.int32, (seg_len, LANES), 0) == seg_len - 1
    sum_grad = sum_grad + jnp.where(is_last, at_last, 0.0)
    at_or_after = lax.broadcasted_iota(jnp.int32, (seg_len, seg_len), 0) <= lax.broadcasted_iota(
        jnp.int32, (seg_len, seg_len), 1
    )
    log_grad = exact_sums(at_or_after, sum_grad)
    grad_raw = (step_grad + head_ref[0:1] * log_grad) * jax.nn.sigmoid(shifted)
    grad_raw_ref[...] = grad_raw
    head_grad_ref[CONV + 1 : CONV + 2] += jnp.sum(log_grad * log_decay, axis=0, keepdims=True)
    head_grad_ref[CONV + 2 : CONV + 3] += jnp.sum(grad_raw, axis=0, keepdims=True)

    first_low = jnp.where(kept, first_grad, 0.0)
    second_low = jnp.where(kept, second_grad, 0.0)
    grad_scores = jnp.concatenate(
        [
            jnp.concatenate([first_low, later_grad], axis=1),
            jnp.concatenate([jnp.zeros_like(first_low), second_low], axis=1),
        ],
        axis=0,
    )
    start_ref[...] = later_ref[...]
    grad_b = dot(scaled_ref[...], local_ref[...], ((1,), (1,))) + dot(
        grad_scores.astype(bf16), c_low, ((1,), (0,))
    )
    grad_c = dot(grad_state_ref[...], prior_ref[0], ((1,), (1,))) + dot(
        grad_scores.T.astype(bf16), b_low, ((1,), (0,))
    )
    first = core_ref[0] == 0
    mine_ref[...] = jnp.where(first, grad_b, grad_c)
    theirs_ref[...] = jnp.where(first, grad_c, grad_b)


GROUPS = 1


def scan_backward(group, core, proj, taps, head, skip, rim, end, prior, values, grad_values, seg_len):
    length = proj.shape[0]
    segs = length // seg_len
    width, shared = HALF // GROUPS, proj.shape[1] - HALF
    back = lambda width, at=0: pl.BlockSpec((seg_len, width), lambda i: (segs - 1 - i, at))
    row_ahead = lambda i: jnp.maximum((segs - 1 - i) * (seg_len // 8) - 1, 0)
    ahead = lambda width, at: pl.BlockSpec((8, width), lambda i: (row_ahead(i), at))
    column = lambda rows, width, at: pl.BlockSpec((rows, width), lambda i: (0, at))
    both = HALF // shared
    return pl.pallas_call(
        lambda *refs: backward_kernel(group, *refs),
        grid=(segs,),
        out_shape=(
            jax.ShapeDtypeStruct((length, width), bf16),
            jax.ShapeDtypeStruct((length, STATE), f32),
            jax.ShapeDtypeStruct((length, STATE), f32),
            jax.ShapeDtypeStruct((length, LANES), f32),
            jax.ShapeDtypeStruct((8, width), f32),
            jax.ShapeDtypeStruct((1, width), f32),
            jax.ShapeDtypeStruct((8, LANES), f32),
            jax.ShapeDtypeStruct((8, width), f32),
            jax.ShapeDtypeStruct((STATE, width), f32),
        ),
        in_specs=[
            back(width, group),
            ahead(width, group),
            column(8, width, group),
            column(8, width, group),
            back(shared, both),
            ahead(shared, both),
            column(8, shared, both),
            column(8, shared, both),
            full_block((8, LANES)),
            column(1, width, group),
            column(STATE, width, group),
            pl.BlockSpec((1, STATE, width), lambda i: (segs - 1 - i, 0, group)),
            back(width, group),
            back(width, group),
            pl.BlockSpec(memory_space=pltpu.SMEM),
        ],
        out_specs=(
            back(width),
            back(STATE),
            back(STATE),
            back(LANES),
            full_block((8, width)),
            full_block((1, width)),
            full_block((8, LANES)),
            full_block((8, width)),
            full_block((STATE, width)),
        ),
        scratch_shapes=[
            pltpu.VMEM((STATE, width), f32),
            pltpu.VMEM((STATE, width), bf16),
            pltpu.VMEM((seg_len, width), bf16),
            pltpu.VMEM((seg_len, width), bf16),
            pltpu.VMEM((seg_len, width), f32),
            pltpu.VMEM((seg_len, width), f32),
            pltpu.VMEM((seg_len, width), f32),
            pltpu.VMEM((8, width), f32),
        ],
        compiler_params=pltpu.CompilerParams(
            dimension_semantics=("arbitrary",), vmem_limit_bytes=VMEM_LIMIT
        ),
        cost_estimate=LIGHT,
    )(
        proj, proj, taps, rim, proj, proj, taps, rim, head, skip, end, prior, values, grad_values,
        core.reshape(1).astype(jnp.int32),
    )


def half_kernel(transposed, count, core_ref, *refs):
    inputs, mine_ref, theirs_ref = refs[: 2 * count], refs[-2], refs[-1]
    total = refs[2 * count][...] if len(refs) > 2 * count + 2 else 0.0
    for left, right in zip(inputs[:count], inputs[count:]):
        total = total + dot(left[...], right[...], ((1,), (1 if transposed else 0,)))
    own = lax.rem(pl.program_id(0), 2) == core_ref[0]

    @pl.when(own)
    def _():
        mine_ref[0] = total

    @pl.when(jnp.logical_not(own))
    def _():
        theirs_ref[0] = total.astype(bf16)


def half_products(core, terms, seg_len, width, transposed, base=()):
    length = terms[0][0].shape[0]
    left = [pl.BlockSpec((seg_len, array.shape[1]), lambda i, core: (i, 0)) for array, _, _ in terms]
    right = []
    for array, matrix, at in terms:
        if transposed:
            right.append(pl.BlockSpec((width, array.shape[1]), lambda i, core, at=at: (0, at(core[0]))))
        else:
            right.append(pl.BlockSpec(matrix.shape, lambda i, core: (0, 0)))
    depth = sum(array.shape[1] for array, _, _ in terms)
    mine, theirs = pl.pallas_call(
        lambda *refs: half_kernel(transposed, len(terms), *refs),
        grid_spec=pltpu.PrefetchScalarGridSpec(
            num_scalar_prefetch=1,
            grid=(length // seg_len,),
            in_specs=left + right + [pl.BlockSpec((seg_len, width), lambda i, core: (i, 0)) for _ in base],
            out_specs=[pl.BlockSpec((1, seg_len, width), lambda i, core: (i // 2, 0, 0))] * 2,
        ),
        out_shape=(
            jax.ShapeDtypeStruct((length // seg_len // 2, seg_len, width), f32),
            jax.ShapeDtypeStruct((length // seg_len // 2, seg_len, width), bf16),
        ),
        compiler_params=pltpu.CompilerParams(dimension_semantics=("arbitrary",), vmem_limit_bytes=VMEM_LIMIT),
        cost_estimate=LIGHT,
    )(core.reshape(1).astype(jnp.int32), *[array for array, _, _ in terms], *[matrix for _, matrix, _ in terms], *base)
    return mine, theirs


def shared_kernel(core_ref, proj_ref, rim_ref, taps_ref, mine_ref, other_ref, grad_ref, taps_grad_ref, edge_ref):
    total, seen = conv_parts(proj_ref[...], rim_ref[...], taps_ref[...])
    sigmoid = jax.nn.sigmoid(total)
    grad_total = mine_ref[...] + other_ref[...]
    grad_total = grad_total * (sigmoid * (1.0 + total * (1.0 - sigmoid)))
    sums = [jnp.sum(grad_total * part, axis=0, keepdims=True) for part in seen]
    sums = sums + [jnp.sum(grad_total, axis=0, keepdims=True), jnp.zeros((8 - CONV - 1, LANES), f32)]
    taps_grad_ref[...] = jnp.concatenate(sums, axis=0)
    edge_ref[...] = grad_total[:8]
    taps = taps_ref[...]
    extended = jnp.concatenate([grad_total, jnp.zeros((8, LANES), f32)], axis=0)
    grad_conv = taps[CONV - 1 : CONV] * grad_total
    for k in range(CONV - 1):
        grad_conv = grad_conv + taps[k : k + 1] * extended[CONV - 1 - k : CONV - 1 - k + grad_total.shape[0]]
    grad_ref[...] = grad_conv.astype(bf16)


def shared_backward(core, proj, rim, taps, mine, other):
    length = proj.shape[0]
    picked = lambda rows: pl.BlockSpec((rows, LANES), lambda i, core: (0, HALF // LANES + core[0]))
    whole = lambda rows: pl.BlockSpec((rows, LANES), lambda i, core: (0, 0))
    return pl.pallas_call(
        shared_kernel,
        grid_spec=pltpu.PrefetchScalarGridSpec(
            num_scalar_prefetch=1,
            grid=(1,),
            in_specs=[picked(length), picked(8), picked(8), whole(length), whole(length)],
            out_specs=(whole(length), whole(8), whole(8)),
        ),
        out_shape=(
            jax.ShapeDtypeStruct((length, LANES), bf16),
            jax.ShapeDtypeStruct((8, LANES), f32),
            jax.ShapeDtypeStruct((8, LANES), f32),
        ),
        compiler_params=pltpu.CompilerParams(vmem_limit_bytes=VMEM_LIMIT),
        cost_estimate=LIGHT,
    )(core.reshape(1).astype(jnp.int32), proj, rim, taps, mine, other)


def per_device(hidden_in, cotangent, in_proj, out_proj, conv_params, pre_gain, gated_gain, head_params):
    chips, line = lax.axis_size("chip"), lax.axis_size("seg")
    core, place = lax.axis_index("core"), lax.axis_index("seg")
    rows, model_width = in_proj.shape[0], hidden_in.shape[2]
    heads = HEADS // 2

    conv_width, gain_width = conv_params.shape[1], gated_gain.shape[0]
    used = HALF + 2 * STATE + heads
    spare = -used % LANES
    small = jnp.zeros((rows, spare), bf16)
    small = small.at[: CONV + 1, :conv_width].set(conv_params)
    small = small.at[CONV + 1, :rows].set(pre_gain)
    small = small.at[CONV + 2, :gain_width].set(gated_gain)

    def conv_side(which):
        return jnp.concatenate(
            [
                own_columns(in_proj[:, INNER : 2 * INNER], which),
                in_proj[:, 2 * INNER : INNER + XBC],
                own_columns(in_proj[:, INNER + XBC :], which),
                small,
            ],
            axis=1,
        )

    def gate_side(which):
        return own_columns(in_proj[:, :INNER], which)

    conv_swap = to_partner(conv_side(1 - core))
    conv_block = in_core_order(conv_side(core), conv_swap, core, 0)
    conv_z = gather_step(conv_block, 2)
    gate_swap = to_partner(gate_side(1 - core))
    gate_block = in_core_order(gate_side(core), gate_swap, core, 0)
    conv_z, hidden_in, gate_block = tie(conv_z, hidden_in, gate_block)
    conv_2 = halves_step([[piece[half] for piece in conv_z] for half in range(2)], 0)
    hidden_got = send_sequence(hidden_in, place)
    conv_2, hidden_first = tie(conv_2, hidden_got[0])
    (first_own, *first_got), (second_own, *second_got) = halves_step(conv_2, 1)
    first_got, second_got, hidden_second, gate_block, out_proj = tie(
        first_got, second_got, hidden_got[1], gate_block, out_proj
    )
    hidden_half = order_sequence([hidden_first, hidden_second], place)
    hidden_other = to_partner(hidden_half)
    conv_last = [[first_own, *first_got], [second_own, *second_got]]
    gate_z = gather_step(gate_block, 2)
    out_own = out_proj[None]
    out_other = exchanged(out_own, 1)
    conv_all = matrix_of_halves(conv_last)

    small_all = conv_all.reshape(chips, 2, line, rows, -1)[..., used:].astype(f32)
    taps_full = small_all[..., : CONV + 1, :conv_width].transpose(3, 0, 1, 2, 4).reshape(CONV + 1, XBC)
    taps = jnp.concatenate([own_columns(taps_full[:, :INNER], core), taps_full[:, INNER:]], axis=1)
    gain_pre = small_all[..., CONV + 1, :rows].reshape(model_width)
    gain_gate = lax.dynamic_index_in_dim(
        small_all[..., CONV + 2, :gain_width], core, axis=1, keepdims=False
    ).reshape(HALF)
    params = own_columns(head_params, core)

    seg_len = hidden_half.shape[1]
    tokens = SEGS * seg_len
    normed, normed_turned = normed_tokens(core, hidden_half, hidden_other, gain_pre, rows)
    projected = dot(normed, conv_all, ((1,), (0,)))
    projected, gate_z, out_own, out_other = tie(projected, gate_z, out_own, out_other)
    gate_own = jnp.stack(gate_z)
    gate_all = gather_plane(gate_own, plane_steps())
    out_own = jnp.concatenate([out_own, out_other])
    out_others = []
    for bit in range(1, (line - 1).bit_length()):
        out_others.append(exchanged(out_own, 2**bit))
        if 2 ** (bit + 1) < line:
            out_own, out_others = jnp.concatenate([out_own, out_others[-1]]), []

    taps = jnp.pad(taps, ((0, 8 - CONV - 1), (0, projected.shape[1] - taps.shape[1])))
    head = jnp.pad(jnp.stack([-jnp.exp(params[0]), params[1]]), ((0, 6), (0, LANES - heads)))
    skip = jnp.repeat(params[2], HEADDIM).reshape(1, HALF)
    wide = HALF + 2 * STATE
    rim = borrowed(projected[tokens - 8 :], 1)
    nothing = jnp.zeros((STATE, HALF), f32)
    values, prior, final, last = scan_forward(projected, taps, head, skip, rim, nothing, seg_len)
    if line > SEGS:
        last = jnp.sum(last.reshape(SEGS, 8, LANES)[:, 0, :heads], axis=0)
        decay = jnp.repeat(jnp.exp2(last), HEADDIM)
        begin = entering(decay, final, 1)
        values, prior, _, _ = scan_forward(projected, taps, head, skip, rim, begin, seg_len)

    values, gate_all, out_others, cotangent = tie(values, gate_all, out_others, cotangent)
    cot_got = send_sequence(cotangent, place)
    out_own = jnp.concatenate([out_own, *out_others])
    out_all = gather_plane(out_own, plane_steps())
    gate_matrix = whole_matrix([gate_own, *gate_all], True)
    gate_input = dot(normed, gate_matrix, ((1,), (0,)))
    gate_input, cot_first = tie(gate_input, cot_got[0])

    silu_gate = jax.nn.silu(gate_input)
    gated = values * silu_gate
    squares = jnp.sum(gated * gated, axis=1)
    squares_other = to_partner(squares)
    scale = lax.rsqrt((squares + squares_other) / INNER + epsilon)[:, None]
    mixed, mixed_turned = mixed_tokens(gated, scale, gain_gate, seg_len)
    mixed_turned, out_all, cot_second = tie(mixed_turned, out_all, cot_got[1])
    cot_half = order_sequence([cot_first, cot_second], place)
    cot_other = to_partner(cot_half)
    cot = in_core_order(cot_half, cot_other, core, 1)
    upstream = cot.reshape(tokens, model_width)
    by_owner = lambda grad: grad.astype(bf16).reshape(chip_dims() + (-1, grad.shape[1]))
    out_grad = by_owner(dot(mixed_turned, upstream, ((1,), (0,))))
    out_got_near = reduce_plane([out_grad], near_steps())
    out_matrix = whole_matrix([out_own, *out_all], False, True)
    branch, branch_sent = half_products(core, [(mixed, out_matrix, None)], seg_len, model_width, False)
    branch_sent, upstream = tie(branch_sent, upstream)
    branch_other = to_partner(branch_sent)
    grad_mixed = dot(upstream, out_matrix, ((1,), (1,)))
    grad_mixed, out_got_near, out_grad = tie(grad_mixed, out_got_near, out_grad)
    out_got_far = reduce_plane([out_grad], far_steps())
    unit = gated * scale
    gain_grad = grad_mixed * gain_gate
    along = jnp.sum(gain_grad * unit, axis=1)
    along_other = to_partner(along)
    along_other, branch_other = tie(along_other, branch_other)
    hidden_out = send_back((hidden_half.astype(f32) + branch + branch_other.astype(f32)).astype(bf16), place)
    along = ((along + along_other) / INNER)[:, None]
    gate_gain_grad = jnp.sum(grad_mixed * unit, axis=0)
    grad_gated = scale * (gain_grad - unit * along)
    grad_values = grad_gated * silu_gate
    sigmoid = jax.nn.sigmoid(gate_input)
    grad_gate = (grad_gated * values * (sigmoid * (1.0 + gate_input * (1.0 - sigmoid)))).astype(bf16)
    gate_grad = by_owner(dot(normed_turned, grad_gate, ((1,), (0,))))
    gate_grad, grad_values, out_got_far = tie(gate_grad, grad_values, out_got_far)
    gate_got = reduce_plane([gate_grad], plane_steps())
    scan = lambda later: scan_backward(
        0, core, projected, taps, head, skip, rim, later, prior, values, grad_values, seg_len
    )
    if line > SEGS:
        nothing = entering(decay, scan(nothing)[-1], -1)
    back = scan(nothing)
    back, gate_got, hidden_out, grad_gate = tie(back, gate_got, hidden_out, grad_gate)
    ((early_kept, early_got),) = reduce_z(
        [
            ([plane_part([out_grad], 0, 0)], [*out_got_near, *out_got_far]),
            ([plane_part([gate_grad], 0, 0)], gate_got),
        ]
    )
    grad_x, mine, theirs, grad_raw, x_taps_grad, skip_grad, head_sums, x_edge, _ = back
    grad_x = spilled(grad_x, x_edge, taps[:, :HALF])
    other = to_partner(theirs)
    x_grad = by_owner(dot(normed_turned, grad_x, ((1,), (0,))))
    other, x_grad = tie(other, x_grad)
    grad_state, state_taps_grad, state_edge = shared_backward(core, projected, rim, taps, mine, other)
    grad_state = spilled(grad_state, state_edge, lax.dynamic_slice_in_dim(taps, HALF + core * STATE, STATE, axis=1))
    grad_raw = grad_raw.astype(bf16)
    rest_grad = by_owner(dot(normed_turned, jnp.concatenate([grad_state, grad_raw], axis=1), ((1,), (0,))))
    rest_grad, x_grad, grad_gate = tie(rest_grad, x_grad, grad_gate)
    conv_near = reduce_plane([x_grad, rest_grad], near_steps())
    base = dot(grad_gate, gate_matrix, ((1,), (1,)))
    terms = [
        (grad_x, conv_all, lambda core: 0),
        (grad_state, conv_all, lambda core: HALF // LANES + core),
        (grad_raw, conv_all, lambda core: (HALF + 2 * STATE) // LANES),
    ]
    grad_normed, sent_normed = half_products(core, terms, seg_len, model_width, True, (base,))
    row = lax.broadcasted_iota(jnp.int32, (8, 1), 0)
    small = x_taps_grad + jnp.where(row == CONV + 1, gate_gain_grad, 0.0) + jnp.where(row == CONV + 2, skip_grad, 0.0)
    small = jnp.concatenate([small, state_taps_grad + head_sums], axis=1)
    sent_normed, early_got, conv_near, small, x_grad, rest_grad = tie(
        sent_normed, early_got, conv_near, small, x_grad, rest_grad
    )
    other_normed = to_partner(sent_normed)
    wide_hidden = hidden_half.astype(f32)
    hidden_scale = lax.rsqrt(jnp.mean(wide_hidden * wide_hidden, axis=-1, keepdims=True) + epsilon)
    grad_normed = (grad_normed + other_normed.astype(f32)) * gain_pre
    hidden_unit = wide_hidden * hidden_scale
    along = jnp.mean(grad_normed * hidden_unit, axis=-1, keepdims=True)
    grad_hidden = hidden_scale * (grad_normed - hidden_unit * along)
    grad_in = (cot_half.astype(f32) + grad_hidden).astype(bf16)
    grad_in, x_grad, rest_grad = tie(grad_in, x_grad, rest_grad)
    grad_in = send_back(grad_in, place)
    conv_far = reduce_plane([x_grad, rest_grad], far_steps())
    grad_in, conv_far = tie(grad_in, conv_far)
    late = reduce_z([([plane_part([x_grad, rest_grad], 0, 0)], [*conv_near, *conv_far])])
    for dim in range(2):
        small = small + sum(moved(small, dim, by) for by in range(1, chip_dims()[dim]))
    for bit in range((line - 1).bit_length()):
        small = small + exchanged(small, 2**bit)
    small_other = to_partner(small)
    late_got, small_other = tie(arrivals(late), small_other)
    early_share = total([*early_kept, *early_got])
    out_share = early_share[:, :model_width]
    paired = lambda share: share.astype(bf16).reshape(2, rows, -1)
    gate_share, conv_share = paired(early_share[:, model_width:]), paired(reduce_end(arrived(late, late_got)))

    def mine_and_partner(share):
        keep = lax.dynamic_index_in_dim(share, core, axis=0, keepdims=False)
        give = lax.dynamic_index_in_dim(share, 1 - core, axis=0, keepdims=False)
        return keep, to_partner(give)

    both = in_core_order(small, small_other, core, 0)
    natural = lambda array, width: array.reshape(2, -1, chips, width).transpose(1, 2, 0, 3).reshape(-1, 2 * chips * width)
    device = (lax.axis_index("chip") * 2 + core) * line + place
    columns = natural(both[:, :, :HALF], HALF // chips)
    taps_all = jnp.concatenate([columns, both[0, :, HALF:], both[1, :, HALF:]], axis=1)[: CONV + 1]
    taps_share = lax.dynamic_slice_in_dim(taps_all, device * conv_width, conv_width, axis=1)
    gain_share = lax.dynamic_slice_in_dim(columns[CONV + 1], device * gain_width, gain_width, axis=0)
    head_total = jnp.concatenate(
        [
            natural(both[:, CONV + 1 : CONV + 3, HALF : HALF + heads], heads // chips),
            jnp.sum(columns[CONV + 2].reshape(1, HEADS, HEADDIM), axis=2),
        ]
    )

    def interleave(mine, theirs):
        width = mine.shape[1] // chips
        both = in_core_order(mine.reshape(rows, chips, width), theirs.reshape(rows, chips, width), core, 2)
        return both.reshape(rows, -1)

    keep_gate, got_gate = mine_and_partner(gate_share)
    keep, got = mine_and_partner(conv_share)
    state_end = HALF + STATE
    in_share = jnp.concatenate(
        [
            interleave(keep_gate, got_gate),
            interleave(keep[:, :HALF], got[:, :HALF]),
            in_core_order(keep[:, HALF:state_end], got[:, HALF:state_end], core, 1).reshape(rows, -1),
            interleave(keep[:, state_end : state_end + heads], got[:, state_end : state_end + heads]),
        ],
        axis=1,
    ).astype(f32)
    pre_share = jnp.sum(in_proj.astype(f32) * in_share, axis=1) / pre_gain.astype(f32)
    hidden_out, grad_in = order_back(hidden_out, place), order_back(grad_in, place)
    return (hidden_out, grad_in, in_share, out_share, taps_share, pre_share, gain_share, head_total)


def solution(mesh):
    devices = mesh.devices
    cores = Mesh(devices.reshape(devices.shape[0] // 2, 2, devices.shape[1]), ("chip", "core", "seg"))
    dp, both = ("chip", "core"), ("chip", "core", "seg")
    tokens = P(dp, "seg", None)
    return jax.shard_map(
        per_device,
        mesh=cores,
        in_specs=(tokens, tokens, P(both, None), P(both, None), P(None, both), P(both), P(both), P()),
        out_specs=(tokens, tokens, P(both, None), P(both, None), P(None, both), P(both), P(both), P()),
        check_vma=False,
    )
```

```python
import jax
import jax.numpy as jnp
from jax import lax
from jax.experimental import pallas as pl
from jax.experimental.pallas import tpu as pltpu
from jax.sharding import Mesh
from jax.sharding import PartitionSpec as P

HEADS = 48
HEADDIM = 64
STATE = 128
CONV = 4
INNER = 3072
XBC = 3328
HALF = INNER // 2
LANES = 128
SEGS = 4
LIGHT = pl.CostEstimate(flops=1024, bytes_accessed=1024, transcendentals=0)
VMEM_LIMIT = 48 * 1024 * 1024
LOG2E = 1.4426950408889634

epsilon = 1e-05
f32 = jnp.float32
bf16 = jnp.bfloat16


def own_columns(array, core):
    chips = lax.axis_size("chip")
    width = array.shape[-1] // (2 * chips)
    parted = array.reshape(array.shape[:-1] + (chips, 2, width))
    picked = lax.dynamic_index_in_dim(parted, core, axis=parted.ndim - 2, keepdims=False)
    return picked.reshape(array.shape[:-1] + (chips * width,))


def to_partner(array):
    return lax.ppermute(array, "core", [(0, 1), (1, 0)])


def in_core_order(mine, theirs, core, axis):
    first = jnp.where(core == 0, mine, theirs)
    second = jnp.where(core == 0, theirs, mine)
    return jnp.stack([first, second], axis=axis)


def chip_dims():
    return (lax.axis_size("chip") // 2, 2, lax.axis_size("seg"))


def chip_place():
    chip = lax.axis_index("chip")
    return (chip // 2, chip % 2, lax.axis_index("seg"))


def moved(array, dim, by):
    sizes = chip_dims()
    index = lambda at: (at[0] * sizes[1] + at[1]) * sizes[2] + at[2]
    pairs = []
    for a in range(sizes[0]):
        for b in range(sizes[1]):
            for z in range(sizes[2]):
                to = [a, b, z]
                to[dim] = (to[dim] + by) % sizes[dim]
                pairs.append((index((a, b, z)), index(to)))
    return lax.ppermute(array, ("chip", "seg"), pairs)


def tie(*values):
    return lax.optimization_barrier(values)


def gather_step(data, dim):
    return [data] + [moved(data, dim, by) for by in range(1, chip_dims()[dim])]


def exchanged(array, by):
    line = lax.axis_size("seg")
    return lax.ppermute(array, "seg", [(at, at ^ by) for at in range(line)])


def plane_steps():
    a, b, _ = chip_dims()
    steps = [(at // b, at % b) for at in range(1, a * b)]
    return sorted(steps, key=lambda by: bool(by[0] and by[1]))


def near_steps():
    a, b, _ = chip_dims()
    return plane_steps()[: a + b - 2]


def far_steps():
    a, b, _ = chip_dims()
    return plane_steps()[a + b - 2 :]


def moved_plane(array, by_a, by_b):
    a, b, z = chip_dims()
    pairs = [
        ((at_a * b + at_b) * z + at_z, ((at_a + by_a) % a * b + (at_b + by_b) % b) * z + at_z)
        for at_a in range(a)
        for at_b in range(b)
        for at_z in range(z)
    ]
    return lax.ppermute(array, ("chip", "seg"), pairs)


def gather_plane(data, steps):
    return [moved_plane(data, *by) for by in steps]


def placed_kernel(plan, place_ref, *refs):
    sources, target, sems = refs[:-2], refs[-2], refs[-1]
    copies = []
    for source, lead, at, paired in plan:
        spot = [lax.rem(place_ref[dim] + (size - back), size) for dim, (back, size) in enumerate(at)]
        spot.append(place_ref[2 + lead])
        to = target.at[spot[0], spot[1], :, spot[2]] if paired else target.at[spot[0], spot[1], spot[2]]
        copies.append(pltpu.make_async_copy(sources[source].at[lead], to, sems.at[len(copies)]))
    for copy in copies:
        copy.start()
    for copy in copies:
        copy.wait()


def whole_matrix(gathered, paired, by_bits=False):
    a, b, z = chip_dims()
    at_a, at_b, at_z = chip_place()
    spots = [at_z ^ back if by_bits else (at_z + z - back) % z for back in range(z)]
    plan = [
        (source, back, ((by[0], a), (by[1], b)), paired)
        for source, by in enumerate([(0, 0)] + plane_steps())
        for back in range(z)
    ]
    block = gathered[0].shape[1:]
    shape = (a, b, 2, z) + block[1:] if paired else (a, b, z) + block
    anywhere = pl.BlockSpec(memory_space=pl.ANY)
    whole = pl.pallas_call(
        lambda *refs: placed_kernel(plan, *refs),
        out_shape=jax.ShapeDtypeStruct(shape, bf16),
        in_specs=[pl.BlockSpec(memory_space=pltpu.SMEM)] + [anywhere] * len(gathered),
        out_specs=pl.BlockSpec(memory_space=pltpu.VMEM),
        scratch_shapes=[pltpu.SemaphoreType.DMA((len(plan),))],
        compiler_params=pltpu.CompilerParams(vmem_limit_bytes=VMEM_LIMIT),
        cost_estimate=LIGHT,
    )(jnp.stack([at_a, at_b, *spots]).astype(jnp.int32), *gathered)
    return whole.reshape(-1, shape[-1])


def total(terms):
    result = terms[0].astype(f32)
    for term in terms[1:]:
        result = result + term.astype(f32)
    return result


def reduce_send(terms, axis, dim, wire):
    place, size = chip_place()[dim], chip_dims()[dim]
    pick = lambda at: [lax.dynamic_index_in_dim(term, at, axis=axis, keepdims=False) for term in terms]
    received = [moved(total(pick((place + by) % size)).astype(wire), dim, by) for by in range(1, size)]
    return pick(place), received


def plane_part(partials, by_a, by_b):
    (at_a, at_b, _), (a, b, _) = chip_place(), chip_dims()
    chip = (at_a + by_a) % a * b + (at_b + by_b) % b
    flat = [partial.reshape((a * b,) + partial.shape[2:]) for partial in partials]
    return jnp.concatenate([lax.dynamic_index_in_dim(array, chip, axis=0, keepdims=False) for array in flat], axis=-1)


def reduce_plane(partials, steps):
    return [moved_plane(plane_part(partials, *by), *by) for by in steps]


def reduce_z(firsts):
    joined = jnp.concatenate([total(kept + received) for kept, received in firsts], axis=-1)
    return [reduce_send([joined], 0, 2, bf16)]


def reduce_end(third):
    return total(third[0][0] + third[0][1])


def arrivals(parts):
    return [received for _, received in parts]


def arrived(parts, received):
    return [(kept, new) for (kept, _), new in zip(parts, received)]


def line_perm(turn, back):
    line = lax.axis_size("seg")
    parts = line // SEGS
    pairs = []
    for core in range(2):
        for place in range(line):
            half, odd = divmod(place % SEGS, 2)
            source = core * line + place
            target = odd * line + (2 * core + (half ^ turn)) * parts + place // SEGS
            pairs.append((target, source) if back else (source, target))
    return pairs


def swapped(pair, turn):
    return [jnp.where(turn == 0, pair[0], pair[1]), jnp.where(turn == 0, pair[1], pair[0])]


def send_sequence(array, place):
    pieces = swapped([array[0], array[1]], (place % SEGS) // 2)
    return [lax.ppermute(piece, ("core", "seg"), line_perm(turn, False)) for turn, piece in enumerate(pieces)]


def order_sequence(got, place):
    parts = lax.axis_size("seg") // SEGS
    return jnp.stack(swapped(got, (place // parts) % 2))


def send_back(ordered, place):
    parts = lax.axis_size("seg") // SEGS
    pieces = swapped([ordered[0], ordered[1]], (place // parts) % 2)
    return [lax.ppermute(piece, ("core", "seg"), line_perm(turn, True)) for turn, piece in enumerate(pieces)]


def order_back(got, place):
    return jnp.stack(swapped(got, (place % SEGS) // 2))


def part_pairs(step):
    line = lax.axis_size("seg")
    parts = line // SEGS
    return [(i, i + step) for i in range(line) if 0 <= i + step < line and i // parts == (i + step) // parts]


def entering(decay, state, step):
    parts = lax.axis_size("seg") // SEGS
    total = jnp.zeros_like(state)
    for _ in range(parts - 1):
        total = lax.ppermute(decay * total + state, "seg", part_pairs(step))
    return total


def borrowed(array, step):
    parts = lax.axis_size("seg") // SEGS
    if parts == 1:
        return jnp.zeros_like(array)
    return lax.ppermute(array, "seg", part_pairs(step))


def spilled(grad, edge, taps):
    if lax.axis_size("seg") == SEGS:
        return grad
    edge = borrowed(edge, -1)
    spill = jnp.stack(
        [
            sum(taps[k] * edge[CONV - 1 - k - early] for k in range(CONV - early))
            for early in range(CONV - 1, 0, -1)
        ]
    )
    at = grad.shape[0] - CONV + 1
    return grad.at[at:].set((grad[at:].astype(f32) + spill).astype(bf16))


def dot(a, b, contract):
    return lax.dot_general(a, b, (contract, ((), ())), preferred_element_type=f32)


def normed_kernel(slabs, core_ref, mine_ref, other_ref, gain_ref, normed_ref, turned_ref):
    own = lax.rem(pl.program_id(0), 2) == core_ref[0]
    hidden = jnp.where(own, mine_ref[0], other_ref[0]).astype(f32)
    scale = lax.rsqrt(jnp.mean(hidden * hidden, axis=1, keepdims=True) + epsilon)
    normed = hidden * scale * gain_ref[...]
    normed_ref[...] = normed.astype(bf16)
    turned = normed.T.astype(bf16)
    for to, at, size in slabs:
        turned_ref[to : to + size] = turned[at : at + size]


def normed_tokens(core, mine, other, gain, rows):
    segs, seg_len, width = 2 * mine.shape[0], mine.shape[1], mine.shape[2]
    a, b, z = chip_dims()
    group = 2 * z * rows
    inside = rows % 16 == 0
    slabs = [(0, 0, width)]
    if inside:
        slabs = [
            (chip * group + (at * 2 + core_at) * rows, chip * group + (core_at * z + at) * rows, rows)
            for chip in range(a * b)
            for core_at in range(2)
            for at in range(z)
        ]
    normed, turned = pl.pallas_call(
        lambda *refs: normed_kernel(slabs, *refs),
        grid_spec=pltpu.PrefetchScalarGridSpec(
            num_scalar_prefetch=1,
            grid=(segs,),
            in_specs=[
                pl.BlockSpec((1, seg_len, width), lambda i, core: (i // 2, 0, 0)),
                pl.BlockSpec((1, seg_len, width), lambda i, core: (i // 2, 0, 0)),
                pl.BlockSpec((1, width), lambda i, core: (0, 0)),
            ],
            out_specs=(
                pl.BlockSpec((seg_len, width), lambda i, core: (i, 0)),
                pl.BlockSpec((width, seg_len), lambda i, core: (0, i)),
            ),
        ),
        out_shape=(
            jax.ShapeDtypeStruct((segs * seg_len, width), bf16),
            jax.ShapeDtypeStruct((width, segs * seg_len), bf16),
        ),
        compiler_params=pltpu.CompilerParams(dimension_semantics=("arbitrary",), vmem_limit_bytes=VMEM_LIMIT),
        cost_estimate=LIGHT,
    )(core.reshape(1).astype(jnp.int32), mine, other, gain.reshape(1, width))
    if not inside:
        turned = turned.reshape(a, b, 2, z, rows, -1).transpose(0, 1, 3, 2, 4, 5).reshape(turned.shape)
    return normed, turned


def mixed_kernel(gated_ref, scale_ref, gain_ref, mixed_ref, turned_ref):
    mixed = gated_ref[...] * scale_ref[...] * gain_ref[...]
    mixed_ref[...] = mixed.astype(bf16)
    turned_ref[...] = mixed.T.astype(bf16)


def mixed_tokens(gated, scale, gain, seg_len):
    length, width = gated.shape
    return pl.pallas_call(
        mixed_kernel,
        grid=(length // seg_len,),
        in_specs=[
            pl.BlockSpec((seg_len, width), lambda i: (i, 0)),
            pl.BlockSpec((seg_len, 1), lambda i: (i, 0)),
            pl.BlockSpec((1, width), lambda i: (0, 0)),
        ],
        out_specs=(
            pl.BlockSpec((seg_len, width), lambda i: (i, 0)),
            pl.BlockSpec((width, seg_len), lambda i: (0, i)),
        ),
        out_shape=(
            jax.ShapeDtypeStruct((length, width), bf16),
            jax.ShapeDtypeStruct((width, length), bf16),
        ),
        compiler_params=pltpu.CompilerParams(dimension_semantics=("arbitrary",), vmem_limit_bytes=VMEM_LIMIT),
        cost_estimate=LIGHT,
    )(gated, scale, gain.reshape(1, width))


def columns_of(pair):
    return pl.ds(pair * LANES, LANES)


def low_half(shape):
    return lax.broadcasted_iota(jnp.int32, shape, len(shape) - 1) < HEADDIM


def pair_columns(array, pair, low):
    rows = array.shape[0]
    first = jnp.broadcast_to(array[:, 2 * pair : 2 * pair + 1], (rows, LANES))
    second = jnp.broadcast_to(array[:, 2 * pair + 1 : 2 * pair + 2], (rows, LANES))
    return jnp.where(low, first, second)


def conv_parts(current, before, taps):
    rows = current.shape[0]
    padded = jnp.concatenate([before, current], axis=0)
    seen = [padded[8 - CONV + 1 + k : 8 - CONV + 1 + k + rows] for k in range(CONV - 1)] + [current]
    total = taps[CONV : CONV + 1]
    for k in range(CONV):
        total = total + taps[k : k + 1] * seen[k]
    return total, seen


def exact_sums(chosen, array):
    chosen = jnp.where(chosen, 1.0, 0.0).astype(bf16)
    result = 0.0
    for _ in range(3):
        part = array.astype(bf16)
        array = array - part.astype(f32)
        result = result + dot(chosen, part, ((1,), (0,)))
    return result


def step_terms(raw, head, seg_len):
    shifted = raw + head[1:2]
    step = jnp.maximum(shifted, 0.0) + jnp.log1p(jnp.exp(-jnp.abs(shifted)))
    log_decay = step * head[0:1]
    at_or_before = lax.broadcasted_iota(jnp.int32, (seg_len, seg_len), 0) >= lax.broadcasted_iota(
        jnp.int32, (seg_len, seg_len), 1
    )
    sums = exact_sums(at_or_before, log_decay)
    return shifted, step, log_decay, sums * LOG2E


def forward_kernel(
    proj_ref, taps_ref, head_ref, skip_ref, rim_ref, init_ref,
    values_ref, prior_ref, final_ref, last_ref, state_ref, tail_ref,
):
    seg_len = proj_ref.shape[0]
    half = seg_len // 2

    @pl.when(pl.program_id(0) == 0)
    def _():
        state_ref[...] = init_ref[...]
        tail_ref[...] = rim_ref[...]

    def activated(begin):
        at = pl.ds(begin, LANES)
        total, _ = conv_parts(proj_ref[:, at], tail_ref[:, at], taps_ref[:, at])
        return total * jax.nn.sigmoid(total)

    b_low = activated(HALF).astype(bf16)
    b_turned = activated(HALF).T.astype(bf16)
    c_low = activated(HALF + STATE).astype(bf16)
    _, step, _, sums = step_terms(proj_ref[:, HALF + 2 * STATE :], head_ref, seg_len)
    sums_turned, step_turned = sums.T, step.T
    scores = dot(c_low, b_low, ((1,), (1,)))
    kept = lax.broadcasted_iota(jnp.int32, (half, half), 0) >= lax.broadcasted_iota(jnp.int32, (half, half), 1)
    first_scores = jnp.where(kept, scores[:half, :half], 0.0)
    later_scores = scores[half:, :half]
    second_scores = jnp.where(kept, scores[half:, half:], 0.0)
    low = low_half((seg_len, LANES))
    last_ref[...] = jnp.broadcast_to(sums[seg_len - 1 :], last_ref.shape)

    for pair in range(HEADS // 4):
        at = columns_of(pair)
        x_values = activated(pair * LANES)
        x_low = x_values.astype(bf16)
        sums_pair = pair_columns(sums, pair, low)
        last_pair = sums_pair[seg_len - 1 :]
        carry = jnp.exp2(last_pair - sums_pair) * pair_columns(step, pair, low)
        scaled_x = (carry * x_low.astype(f32)).astype(bf16)
        prior = state_ref[:, at]
        prior_low = prior.astype(bf16)
        prior_ref[0, :, at] = prior_low
        from_state = jnp.exp2(sums_pair) * dot(c_low, prior_low, ((1,), (0,)))
        state_ref[:, at] = jnp.exp2(last_pair) * prior + dot(b_turned, scaled_x, ((1,), (0,)))
        early, late = 0.0, 0.0
        for side in range(2):
            head = 2 * pair + side
            x_side = jnp.where(low if side == 0 else ~low, x_values, 0.0).astype(bf16)
            at_token = jnp.broadcast_to(sums[:, head : head + 1], (seg_len, half))
            at_source, source_step = sums_turned[head : head + 1], step_turned[head : head + 1]
            first = jnp.exp2(jnp.minimum(at_token[:half] - at_source[:, :half], 0.0)) * first_scores
            first = (first * source_step[:, :half]).astype(bf16)
            later = jnp.exp2(at_token[half:] - at_source[:, :half]) * later_scores
            later = (later * source_step[:, :half]).astype(bf16)
            second = jnp.exp2(jnp.minimum(at_token[half:] - at_source[:, half:], 0.0)) * second_scores
            second = (second * source_step[:, half:]).astype(bf16)
            early = early + dot(first, x_side[:half], ((1,), (0,)))
            late = late + dot(jnp.concatenate([later, second], axis=1), x_side, ((1,), (0,)))
        intra = jnp.concatenate([early, late], axis=0)
        values_ref[:, at] = intra + from_state + skip_ref[:, at] * x_values

    tail_ref[...] = proj_ref[seg_len - 8 :, : HALF + 2 * STATE]
    final_ref[...] = state_ref[...]


def full_block(shape):
    return pl.BlockSpec(shape, lambda *_: (0,) * len(shape))


def scan_forward(proj, taps, head, skip, rim, init, seg_len):
    segs = proj.shape[0] // seg_len
    wide = HALF + 2 * STATE
    return pl.pallas_call(
        forward_kernel,
        grid=(segs,),
        out_shape=(
            jax.ShapeDtypeStruct((proj.shape[0], HALF), f32),
            jax.ShapeDtypeStruct((segs, STATE, HALF), bf16),
            jax.ShapeDtypeStruct((STATE, HALF), f32),
            jax.ShapeDtypeStruct((segs * 8, LANES), f32),
        ),
        in_specs=[
            pl.BlockSpec((seg_len, proj.shape[1]), lambda i: (i, 0)),
            full_block((8, wide)),
            full_block((8, LANES)),
            full_block((1, HALF)),
            full_block((8, wide)),
            full_block((STATE, HALF)),
        ],
        out_specs=(
            pl.BlockSpec((seg_len, HALF), lambda i: (i, 0)),
            pl.BlockSpec((1, STATE, HALF), lambda i: (i, 0, 0)),
            full_block((STATE, HALF)),
            pl.BlockSpec((8, LANES), lambda i: (i, 0)),
        ),
        scratch_shapes=[pltpu.VMEM((STATE, HALF), f32), pltpu.VMEM((8, wide), f32)],
        compiler_params=pltpu.CompilerParams(
            dimension_semantics=("arbitrary",), vmem_limit_bytes=VMEM_LIMIT
        ),
        cost_estimate=LIGHT,
    )(proj, taps, head, skip, rim, init)


def split_dot(array, other):
    high = array.astype(bf16)
    rest = (array - high.astype(f32)).astype(bf16)
    return dot(high, other, ((1,), (0,))) + dot(rest, other, ((1,), (0,)))


def backward_kernel(
    group, proj_ref, before_ref, taps_ref, rim_ref, shared_ref, shared_before_ref, shared_taps_ref, shared_rim_ref,
    head_ref, skip_ref, end_ref, prior_ref, values_ref, grad_ref, core_ref,
    grad_x_ref, mine_ref, theirs_ref, grad_raw_ref, taps_grad_ref, skip_grad_ref, head_grad_ref, edge_ref, start_ref,
    later_ref, local_ref, scaled_ref, grad_state_ref, inner_ref, source_ref, carry_ref, decay_ref,
):
    seg_len = proj_ref.shape[0]
    half = seg_len // 2
    turn = pl.program_id(0)

    @pl.when(turn == 0)
    def _():
        later_ref[...] = end_ref[...]
        edge_ref[...] = jnp.zeros_like(edge_ref)
        taps_grad_ref[...] = jnp.zeros_like(taps_grad_ref)
        skip_grad_ref[...] = jnp.zeros_like(skip_grad_ref)
        head_grad_ref[...] = jnp.zeros_like(head_grad_ref)

    first_segment = turn == pl.num_programs(0) - 1

    def conv_at(at, current, ahead, taps, rim):
        before = jnp.where(first_segment, rim[:, at], ahead[:, at])
        return conv_parts(current[:, at], before, taps[:, at])

    def activated(begin):
        total, _ = conv_at(pl.ds(begin, LANES), shared_ref, shared_before_ref, shared_taps_ref, shared_rim_ref)
        return total * jax.nn.sigmoid(total)

    b_values = activated(0)
    c_values = activated(STATE)
    b_low, c_low, c_turned = b_values.astype(bf16), c_values.astype(bf16), c_values.T.astype(bf16)
    shifted, step, log_decay, sums = step_terms(shared_ref[:, 2 * STATE :], head_ref, seg_len)
    sums_turned = sums.T
    scores = dot(b_low, c_low, ((1,), (1,)))
    kept = lax.broadcasted_iota(jnp.int32, (half, half), 0) <= lax.broadcasted_iota(jnp.int32, (half, half), 1)
    first_scores = jnp.where(kept, scores[:half, :half], 0.0)
    later_scores = scores[:half, half:]
    second_scores = jnp.where(kept, scores[half:, half:], 0.0)
    low = low_half((seg_len, LANES))
    first_grad, later_grad, second_grad = 0.0, 0.0, 0.0

    pairs = grad_ref.shape[1] // LANES
    for pair in range(pairs):
        at = columns_of(pair)
        total, seen = conv_at(at, proj_ref, before_ref, taps_ref, rim_ref)
        sigmoid = jax.nn.sigmoid(total)
        x_values = total * sigmoid
        x_low = x_values.astype(bf16)
        x_wide = x_low.astype(f32)
        sums_pair = pair_columns(sums, group * pairs + pair, low)
        step_pair = pair_columns(step, group * pairs + pair, low)
        last_pair = sums_pair[seg_len - 1 :]
        gap = jnp.exp2(last_pair - sums_pair)
        scaled_ref[:, at] = (gap * step_pair * x_wide).astype(bf16)
        grad_values = grad_ref[:, at]
        grad_state_ref[:, at] = (grad_values * jnp.exp2(sums_pair)).astype(bf16)
        later = later_ref[:, at]
        later_low = later.astype(bf16)
        local_ref[:, at] = later_low
        prior = prior_ref[0, :, at]
        decay_ref[:, at] = jnp.broadcast_to(
            jnp.sum(later * prior.astype(f32), axis=0, keepdims=True), (8, LANES)
        )
        grad_prior = dot(c_turned, grad_state_ref[:, at], ((1,), (0,)))
        later_ref[:, at] = jnp.exp2(last_pair) * later + grad_prior
        grad_scaled = dot(b_low, later_low, ((1,), (0,)))
        stepped = (step_pair * x_wide).astype(bf16)
        early, late = 0.0, 0.0
        for side in range(2):
            head = 2 * (group * pairs + pair) + side
            grad_low = jnp.where(low if side == 0 else ~low, grad_values, 0.0).astype(bf16)
            at_source = jnp.broadcast_to(sums[:, head : head + 1], (seg_len, half))
            at_token = sums_turned[head : head + 1]
            grad_weights = dot(stepped, grad_low, ((1,), (1,)))
            first = jnp.exp2(jnp.minimum(at_token[:, :half] - at_source[:half], 0.0))
            after = jnp.exp2(at_token[:, half:] - at_source[:half])
            second = jnp.exp2(jnp.minimum(at_token[:, half:] - at_source[half:], 0.0))
            first_grad = first_grad + first * grad_weights[:half, :half]
            later_grad = later_grad + after * grad_weights[:half, half:]
            second_grad = second_grad + second * grad_weights[half:, half:]
            upper = jnp.concatenate([first * first_scores, after * later_scores], axis=1).astype(bf16)
            early = early + dot(upper, grad_low, ((1,), (0,)))
            late = late + dot((second * second_scores).astype(bf16), grad_low[half:], ((1,), (0,)))
        inner = jnp.concatenate([early, late], axis=0)
        skip = skip_ref[:, at]
        skip_grad_ref[:, at] += jnp.sum(grad_values * x_values, axis=0, keepdims=True)
        inner_ref[:, at] = grad_values * (values_ref[:, at] - skip * x_values)
        source_ref[:, at] = x_wide * inner
        carry_ref[:, at] = x_wide * grad_scaled
        grad_x = skip * grad_values + step_pair * (inner + gap * grad_scaled)
        grad_total = grad_x * (sigmoid * (1.0 + total * (1.0 - sigmoid)))
        for k in range(CONV):
            taps_grad_ref[k : k + 1, at] += jnp.sum(grad_total * seen[k], axis=0, keepdims=True)
        taps_grad_ref[CONV : CONV + 1, at] += jnp.sum(grad_total, axis=0, keepdims=True)
        extended = jnp.concatenate([grad_total, edge_ref[:, at]], axis=0)
        edge_ref[:, at] = grad_total[:8]
        taps = taps_ref[:, at]
        grad_conv = taps[CONV - 1 : CONV] * grad_total
        for k in range(CONV - 1):
            grad_conv = grad_conv + taps[k : k + 1] * extended[CONV - 1 - k : CONV - 1 - k + seg_len]
        grad_x_ref[:, at] = grad_conv.astype(bf16)

    width = grad_ref.shape[1]
    channel = lax.broadcasted_iota(jnp.int32, (width, LANES), 0) // HEADDIM + group * width // HEADDIM
    heads = jnp.where(channel == lax.broadcasted_iota(jnp.int32, (width, LANES), 1), 1.0, 0.0).astype(bf16)
    tail = jnp.exp2(sums[seg_len - 1 :] - sums)
    source_grad = split_dot(source_ref[...], heads)
    step_grad = source_grad + tail * split_dot(carry_ref[...], heads)
    used = step * step_grad
    sum_grad = split_dot(inner_ref[...], heads) - used
    at_last = jnp.sum(used - step * source_grad, axis=0, keepdims=True)
    at_last = at_last + split_dot(decay_ref[...], heads)[:1] * jnp.exp2(sums[seg_len - 1 :])
    is_last = lax.broadcasted_iota(jnp.int32, (seg_len, LANES), 0) == seg_len - 1
    sum_grad = sum_grad + jnp.where(is_last, at_last, 0.0)
    at_or_after = lax.broadcasted_iota(jnp.int32, (seg_len, seg_len), 0) <= lax.broadcasted_iota(
        jnp.int32, (seg_len, seg_len), 1
    )
    log_grad = exact_sums(at_or_after, sum_grad)
    grad_raw = (step_grad + head_ref[0:1] * log_grad) * jax.nn.sigmoid(shifted)
    grad_raw_ref[...] = grad_raw
    head_grad_ref[CONV + 1 : CONV + 2] += jnp.sum(log_grad * log_decay, axis=0, keepdims=True)
    head_grad_ref[CONV + 2 : CONV + 3] += jnp.sum(grad_raw, axis=0, keepdims=True)

    first_low = jnp.where(kept, first_grad, 0.0)
    second_low = jnp.where(kept, second_grad, 0.0)
    grad_scores = jnp.concatenate(
        [
            jnp.concatenate([first_low, later_grad], axis=1),
            jnp.concatenate([jnp.zeros_like(first_low), second_low], axis=1),
        ],
        axis=0,
    )
    start_ref[...] = later_ref[...]
    grad_b = dot(scaled_ref[...], local_ref[...], ((1,), (1,))) + dot(
        grad_scores.astype(bf16), c_low, ((1,), (0,))
    )
    grad_c = dot(grad_state_ref[...], prior_ref[0], ((1,), (1,))) + dot(
        grad_scores.T.astype(bf16), b_low, ((1,), (0,))
    )
    first = core_ref[0] == 0
    mine_ref[...] = jnp.where(first, grad_b, grad_c)
    theirs_ref[...] = jnp.where(first, grad_c, grad_b)


GROUPS = 1


def scan_backward(group, core, proj, taps, head, skip, rim, end, prior, values, grad_values, seg_len):
    length = proj.shape[0]
    segs = length // seg_len
    width, shared = HALF // GROUPS, proj.shape[1] - HALF
    back = lambda width, at=0: pl.BlockSpec((seg_len, width), lambda i: (segs - 1 - i, at))
    row_ahead = lambda i: jnp.maximum((segs - 1 - i) * (seg_len // 8) - 1, 0)
    ahead = lambda width, at: pl.BlockSpec((8, width), lambda i: (row_ahead(i), at))
    column = lambda rows, width, at: pl.BlockSpec((rows, width), lambda i: (0, at))
    both = HALF // shared
    return pl.pallas_call(
        lambda *refs: backward_kernel(group, *refs),
        grid=(segs,),
        out_shape=(
            jax.ShapeDtypeStruct((length, width), bf16),
            jax.ShapeDtypeStruct((length, STATE), f32),
            jax.ShapeDtypeStruct((length, STATE), f32),
            jax.ShapeDtypeStruct((length, LANES), f32),
            jax.ShapeDtypeStruct((8, width), f32),
            jax.ShapeDtypeStruct((1, width), f32),
            jax.ShapeDtypeStruct((8, LANES), f32),
            jax.ShapeDtypeStruct((8, width), f32),
            jax.ShapeDtypeStruct((STATE, width), f32),
        ),
        in_specs=[
            back(width, group),
            ahead(width, group),
            column(8, width, group),
            column(8, width, group),
            back(shared, both),
            ahead(shared, both),
            column(8, shared, both),
            column(8, shared, both),
            full_block((8, LANES)),
            column(1, width, group),
            column(STATE, width, group),
            pl.BlockSpec((1, STATE, width), lambda i: (segs - 1 - i, 0, group)),
            back(width, group),
            back(width, group),
            pl.BlockSpec(memory_space=pltpu.SMEM),
        ],
        out_specs=(
            back(width),
            back(STATE),
            back(STATE),
            back(LANES),
            full_block((8, width)),
            full_block((1, width)),
            full_block((8, LANES)),
            full_block((8, width)),
            full_block((STATE, width)),
        ),
        scratch_shapes=[
            pltpu.VMEM((STATE, width), f32),
            pltpu.VMEM((STATE, width), bf16),
            pltpu.VMEM((seg_len, width), bf16),
            pltpu.VMEM((seg_len, width), bf16),
            pltpu.VMEM((seg_len, width), f32),
            pltpu.VMEM((seg_len, width), f32),
            pltpu.VMEM((seg_len, width), f32),
            pltpu.VMEM((8, width), f32),
        ],
        compiler_params=pltpu.CompilerParams(
            dimension_semantics=("arbitrary",), vmem_limit_bytes=VMEM_LIMIT
        ),
        cost_estimate=LIGHT,
    )(
        proj, proj, taps, rim, proj, proj, taps, rim, head, skip, end, prior, values, grad_values,
        core.reshape(1).astype(jnp.int32),
    )


def half_kernel(transposed, count, core_ref, *refs):
    inputs, mine_ref, theirs_ref = refs[: 2 * count], refs[-2], refs[-1]
    total = refs[2 * count][...] if len(refs) > 2 * count + 2 else 0.0
    for left, right in zip(inputs[:count], inputs[count:]):
        total = total + dot(left[...], right[...], ((1,), (1 if transposed else 0,)))
    own = lax.rem(pl.program_id(0), 2) == core_ref[0]

    @pl.when(own)
    def _():
        mine_ref[0] = total

    @pl.when(jnp.logical_not(own))
    def _():
        theirs_ref[0] = total.astype(bf16)


def half_products(core, terms, seg_len, width, transposed, base=()):
    length = terms[0][0].shape[0]
    left = [pl.BlockSpec((seg_len, array.shape[1]), lambda i, core: (i, 0)) for array, _, _ in terms]
    right = []
    for array, matrix, at in terms:
        if transposed:
            right.append(pl.BlockSpec((width, array.shape[1]), lambda i, core, at=at: (0, at(core[0]))))
        else:
            right.append(pl.BlockSpec(matrix.shape, lambda i, core: (0, 0)))
    depth = sum(array.shape[1] for array, _, _ in terms)
    mine, theirs = pl.pallas_call(
        lambda *refs: half_kernel(transposed, len(terms), *refs),
        grid_spec=pltpu.PrefetchScalarGridSpec(
            num_scalar_prefetch=1,
            grid=(length // seg_len,),
            in_specs=left + right + [pl.BlockSpec((seg_len, width), lambda i, core: (i, 0)) for _ in base],
            out_specs=[pl.BlockSpec((1, seg_len, width), lambda i, core: (i // 2, 0, 0))] * 2,
        ),
        out_shape=(
            jax.ShapeDtypeStruct((length // seg_len // 2, seg_len, width), f32),
            jax.ShapeDtypeStruct((length // seg_len // 2, seg_len, width), bf16),
        ),
        compiler_params=pltpu.CompilerParams(dimension_semantics=("arbitrary",), vmem_limit_bytes=VMEM_LIMIT),
        cost_estimate=LIGHT,
    )(core.reshape(1).astype(jnp.int32), *[array for array, _, _ in terms], *[matrix for _, matrix, _ in terms], *base)
    return mine, theirs


def shared_kernel(core_ref, proj_ref, rim_ref, taps_ref, mine_ref, other_ref, grad_ref, taps_grad_ref, edge_ref):
    total, seen = conv_parts(proj_ref[...], rim_ref[...], taps_ref[...])
    sigmoid = jax.nn.sigmoid(total)
    grad_total = mine_ref[...] + other_ref[...]
    grad_total = grad_total * (sigmoid * (1.0 + total * (1.0 - sigmoid)))
    sums = [jnp.sum(grad_total * part, axis=0, keepdims=True) for part in seen]
    sums = sums + [jnp.sum(grad_total, axis=0, keepdims=True), jnp.zeros((8 - CONV - 1, LANES), f32)]
    taps_grad_ref[...] = jnp.concatenate(sums, axis=0)
    edge_ref[...] = grad_total[:8]
    taps = taps_ref[...]
    extended = jnp.concatenate([grad_total, jnp.zeros((8, LANES), f32)], axis=0)
    grad_conv = taps[CONV - 1 : CONV] * grad_total
    for k in range(CONV - 1):
        grad_conv = grad_conv + taps[k : k + 1] * extended[CONV - 1 - k : CONV - 1 - k + grad_total.shape[0]]
    grad_ref[...] = grad_conv.astype(bf16)


def shared_backward(core, proj, rim, taps, mine, other):
    length = proj.shape[0]
    picked = lambda rows: pl.BlockSpec((rows, LANES), lambda i, core: (0, HALF // LANES + core[0]))
    whole = lambda rows: pl.BlockSpec((rows, LANES), lambda i, core: (0, 0))
    return pl.pallas_call(
        shared_kernel,
        grid_spec=pltpu.PrefetchScalarGridSpec(
            num_scalar_prefetch=1,
            grid=(1,),
            in_specs=[picked(length), picked(8), picked(8), whole(length), whole(length)],
            out_specs=(whole(length), whole(8), whole(8)),
        ),
        out_shape=(
            jax.ShapeDtypeStruct((length, LANES), bf16),
            jax.ShapeDtypeStruct((8, LANES), f32),
            jax.ShapeDtypeStruct((8, LANES), f32),
        ),
        compiler_params=pltpu.CompilerParams(vmem_limit_bytes=VMEM_LIMIT),
        cost_estimate=LIGHT,
    )(core.reshape(1).astype(jnp.int32), proj, rim, taps, mine, other)


def per_device(hidden_in, cotangent, in_proj, out_proj, conv_params, pre_gain, gated_gain, head_params):
    chips, line = lax.axis_size("chip"), lax.axis_size("seg")
    core, place = lax.axis_index("core"), lax.axis_index("seg")
    rows, model_width = in_proj.shape[0], hidden_in.shape[2]
    heads = HEADS // 2

    conv_width, gain_width = conv_params.shape[1], gated_gain.shape[0]
    used = HALF + 2 * STATE + heads
    spare = -used % LANES
    small = jnp.zeros((rows, spare), bf16)
    small = small.at[: CONV + 1, :conv_width].set(conv_params)
    small = small.at[CONV + 1, :rows].set(pre_gain)
    small = small.at[CONV + 2, :gain_width].set(gated_gain)

    def conv_side(which):
        return jnp.concatenate(
            [
                own_columns(in_proj[:, INNER : 2 * INNER], which),
                in_proj[:, 2 * INNER : INNER + XBC],
                own_columns(in_proj[:, INNER + XBC :], which),
                small,
            ],
            axis=1,
        )

    def gate_side(which):
        return own_columns(in_proj[:, :INNER], which)

    conv_swap = to_partner(conv_side(1 - core))
    conv_block = in_core_order(conv_side(core), conv_swap, core, 0)
    conv_z = gather_step(conv_block, 2)
    gate_swap = to_partner(gate_side(1 - core))
    gate_block = in_core_order(gate_side(core), gate_swap, core, 0)
    conv_z, hidden_in, gate_block = tie(conv_z, hidden_in, gate_block)
    conv_own = jnp.stack(conv_z)
    conv_near = gather_plane(conv_own, near_steps())
    hidden_got = send_sequence(hidden_in, place)
    conv_own, conv_near, hidden_got, gate_block = tie(conv_own, conv_near, hidden_got, gate_block)
    hidden_half = order_sequence(hidden_got, place)
    conv_far = gather_plane(conv_own, far_steps())
    gate_z = gather_step(gate_block, 2)
    hidden_other = to_partner(hidden_half)
    conv_far, gate_z, hidden_other, out_proj = tie(conv_far, gate_z, hidden_other, out_proj)
    gate_own = jnp.stack(gate_z)
    gate_near = gather_plane(gate_own, near_steps())
    conv_all = whole_matrix([conv_own, *conv_near, *conv_far], True)

    small_all = conv_all.reshape(chips, 2, line, rows, -1)[..., used:].astype(f32)
    taps_full = small_all[..., : CONV + 1, :conv_width].transpose(3, 0, 1, 2, 4).reshape(CONV + 1, XBC)
    taps = jnp.concatenate([own_columns(taps_full[:, :INNER], core), taps_full[:, INNER:]], axis=1)
    gain_pre = small_all[..., CONV + 1, :rows].reshape(model_width)
    gain_gate = lax.dynamic_index_in_dim(
        small_all[..., CONV + 2, :gain_width], core, axis=1, keepdims=False
    ).reshape(HALF)
    params = own_columns(head_params, core)

    seg_len = hidden_half.shape[1]
    tokens = SEGS * seg_len
    normed, normed_turned = normed_tokens(core, hidden_half, hidden_other, gain_pre, rows)
    normed, out_proj = tie(normed, out_proj)
    out_own = out_proj[None]
    out_other = exchanged(out_own, 1)
    projected = dot(normed, conv_all, ((1,), (0,)))
    projected, gate_own, gate_near, out_own, out_other = tie(projected, gate_own, gate_near, out_own, out_other)
    gate_far = gather_plane(gate_own, far_steps())
    out_own = jnp.concatenate([out_own, out_other])
    out_others = []
    for bit in range(1, (line - 1).bit_length()):
        out_others.append(exchanged(out_own, 2**bit))
        if 2 ** (bit + 1) < line:
            out_own, out_others = jnp.concatenate([out_own, out_others[-1]]), []

    taps = jnp.pad(taps, ((0, 8 - CONV - 1), (0, projected.shape[1] - taps.shape[1])))
    head = jnp.pad(jnp.stack([-jnp.exp(params[0]), params[1]]), ((0, 6), (0, LANES - heads)))
    skip = jnp.repeat(params[2], HEADDIM).reshape(1, HALF)
    wide = HALF + 2 * STATE
    rim = borrowed(projected[tokens - 8 :], 1)
    nothing = jnp.zeros((STATE, HALF), f32)
    values, prior, final, last = scan_forward(projected, taps, head, skip, rim, nothing, seg_len)
    if line > SEGS:
        last = jnp.sum(last.reshape(SEGS, 8, LANES)[:, 0, :heads], axis=0)
        decay = jnp.repeat(jnp.exp2(last), HEADDIM)
        begin = entering(decay, final, 1)
        values, prior, _, _ = scan_forward(projected, taps, head, skip, rim, begin, seg_len)

    values, gate_far, out_others, cotangent = tie(values, gate_far, out_others, cotangent)
    cot_got = send_sequence(cotangent, place)
    out_own = jnp.concatenate([out_own, *out_others])
    out_all = gather_plane(out_own, plane_steps())
    gate_matrix = whole_matrix([gate_own, *gate_near, *gate_far], True)
    gate_input = dot(normed, gate_matrix, ((1,), (0,)))
    gate_input, cot_first = tie(gate_input, cot_got[0])

    silu_gate = jax.nn.silu(gate_input)
    gated = values * silu_gate
    squares = jnp.sum(gated * gated, axis=1)
    squares_other = to_partner(squares)
    scale = lax.rsqrt((squares + squares_other) / INNER + epsilon)[:, None]
    mixed, mixed_turned = mixed_tokens(gated, scale, gain_gate, seg_len)
    mixed_turned, out_all, cot_second = tie(mixed_turned, out_all, cot_got[1])
    cot_half = order_sequence([cot_first, cot_second], place)
    cot_other = to_partner(cot_half)
    cot = in_core_order(cot_half, cot_other, core, 1)
    upstream = cot.reshape(tokens, model_width)
    by_owner = lambda grad: grad.astype(bf16).reshape(chip_dims() + (-1, grad.shape[1]))
    out_grad = by_owner(dot(mixed_turned, upstream, ((1,), (0,))))
    out_got_near = reduce_plane([out_grad], near_steps())
    out_matrix = whole_matrix([out_own, *out_all], False, True)
    branch, branch_sent = half_products(core, [(mixed, out_matrix, None)], seg_len, model_width, False)
    branch_sent, upstream = tie(branch_sent, upstream)
    branch_other = to_partner(branch_sent)
    grad_mixed = dot(upstream, out_matrix, ((1,), (1,)))
    grad_mixed, out_got_near, out_grad = tie(grad_mixed, out_got_near, out_grad)
    out_got_far = reduce_plane([out_grad], far_steps())
    unit = gated * scale
    gain_grad = grad_mixed * gain_gate
    along = jnp.sum(gain_grad * unit, axis=1)
    along_other = to_partner(along)
    along_other, branch_other = tie(along_other, branch_other)
    hidden_out = send_back((hidden_half.astype(f32) + branch + branch_other.astype(f32)).astype(bf16), place)
    along = ((along + along_other) / INNER)[:, None]
    gate_gain_grad = jnp.sum(grad_mixed * unit, axis=0)
    grad_gated = scale * (gain_grad - unit * along)
    grad_values = grad_gated * silu_gate
    sigmoid = jax.nn.sigmoid(gate_input)
    grad_gate = (grad_gated * values * (sigmoid * (1.0 + gate_input * (1.0 - sigmoid)))).astype(bf16)
    gate_grad = by_owner(dot(normed_turned, grad_gate, ((1,), (0,))))
    gate_grad, grad_values, out_got_far = tie(gate_grad, grad_values, out_got_far)
    gate_got = reduce_plane([gate_grad], plane_steps())
    scan = lambda later: scan_backward(
        0, core, projected, taps, head, skip, rim, later, prior, values, grad_values, seg_len
    )
    if line > SEGS:
        nothing = entering(decay, scan(nothing)[-1], -1)
    back = scan(nothing)
    back, gate_got, hidden_out, grad_gate = tie(back, gate_got, hidden_out, grad_gate)
    ((early_kept, early_got),) = reduce_z(
        [
            ([plane_part([out_grad], 0, 0)], [*out_got_near, *out_got_far]),
            ([plane_part([gate_grad], 0, 0)], gate_got),
        ]
    )
    grad_x, mine, theirs, grad_raw, x_taps_grad, skip_grad, head_sums, x_edge, _ = back
    grad_x = spilled(grad_x, x_edge, taps[:, :HALF])
    other = to_partner(theirs)
    x_grad = by_owner(dot(normed_turned, grad_x, ((1,), (0,))))
    other, x_grad = tie(other, x_grad)
    grad_state, state_taps_grad, state_edge = shared_backward(core, projected, rim, taps, mine, other)
    grad_state = spilled(grad_state, state_edge, lax.dynamic_slice_in_dim(taps, HALF + core * STATE, STATE, axis=1))
    grad_raw = grad_raw.astype(bf16)
    rest_grad = by_owner(dot(normed_turned, jnp.concatenate([grad_state, grad_raw], axis=1), ((1,), (0,))))
    rest_grad, x_grad, grad_gate = tie(rest_grad, x_grad, grad_gate)
    conv_near = reduce_plane([x_grad, rest_grad], near_steps())
    base = dot(grad_gate, gate_matrix, ((1,), (1,)))
    terms = [
        (grad_x, conv_all, lambda core: 0),
        (grad_state, conv_all, lambda core: HALF // LANES + core),
        (grad_raw, conv_all, lambda core: (HALF + 2 * STATE) // LANES),
    ]
    grad_normed, sent_normed = half_products(core, terms, seg_len, model_width, True, (base,))
    row = lax.broadcasted_iota(jnp.int32, (8, 1), 0)
    small = x_taps_grad + jnp.where(row == CONV + 1, gate_gain_grad, 0.0) + jnp.where(row == CONV + 2, skip_grad, 0.0)
    small = jnp.concatenate([small, state_taps_grad + head_sums], axis=1)
    sent_normed, early_got, conv_near, small, x_grad, rest_grad = tie(
        sent_normed, early_got, conv_near, small, x_grad, rest_grad
    )
    other_normed = to_partner(sent_normed)
    wide_hidden = hidden_half.astype(f32)
    hidden_scale = lax.rsqrt(jnp.mean(wide_hidden * wide_hidden, axis=-1, keepdims=True) + epsilon)
    grad_normed = (grad_normed + other_normed.astype(f32)) * gain_pre
    hidden_unit = wide_hidden * hidden_scale
    along = jnp.mean(grad_normed * hidden_unit, axis=-1, keepdims=True)
    grad_hidden = hidden_scale * (grad_normed - hidden_unit * along)
    grad_in = (cot_half.astype(f32) + grad_hidden).astype(bf16)
    grad_in, x_grad, rest_grad = tie(grad_in, x_grad, rest_grad)
    grad_in = send_back(grad_in, place)
    conv_far = reduce_plane([x_grad, rest_grad], far_steps())
    grad_in, conv_far = tie(grad_in, conv_far)
    late = reduce_z([([plane_part([x_grad, rest_grad], 0, 0)], [*conv_near, *conv_far])])
    for dim in range(2):
        small = small + sum(moved(small, dim, by) for by in range(1, chip_dims()[dim]))
    for bit in range((line - 1).bit_length()):
        small = small + exchanged(small, 2**bit)
    small_other = to_partner(small)
    late_got, small_other = tie(arrivals(late), small_other)
    early_share = total([*early_kept, *early_got])
    out_share = early_share[:, :model_width]
    paired = lambda share: share.astype(bf16).reshape(2, rows, -1)
    gate_share, conv_share = paired(early_share[:, model_width:]), paired(reduce_end(arrived(late, late_got)))

    def mine_and_partner(share):
        keep = lax.dynamic_index_in_dim(share, core, axis=0, keepdims=False)
        give = lax.dynamic_index_in_dim(share, 1 - core, axis=0, keepdims=False)
        return keep, to_partner(give)

    both = in_core_order(small, small_other, core, 0)
    natural = lambda array, width: array.reshape(2, -1, chips, width).transpose(1, 2, 0, 3).reshape(-1, 2 * chips * width)
    device = (lax.axis_index("chip") * 2 + core) * line + place
    columns = natural(both[:, :, :HALF], HALF // chips)
    taps_all = jnp.concatenate([columns, both[0, :, HALF:], both[1, :, HALF:]], axis=1)[: CONV + 1]
    taps_share = lax.dynamic_slice_in_dim(taps_all, device * conv_width, conv_width, axis=1)
    gain_share = lax.dynamic_slice_in_dim(columns[CONV + 1], device * gain_width, gain_width, axis=0)
    head_total = jnp.concatenate(
        [
            natural(both[:, CONV + 1 : CONV + 3, HALF : HALF + heads], heads // chips),
            jnp.sum(columns[CONV + 2].reshape(1, HEADS, HEADDIM), axis=2),
        ]
    )

    def interleave(mine, theirs):
        width = mine.shape[1] // chips
        both = in_core_order(mine.reshape(rows, chips, width), theirs.reshape(rows, chips, width), core, 2)
        return both.reshape(rows, -1)

    keep_gate, got_gate = mine_and_partner(gate_share)
    keep, got = mine_and_partner(conv_share)
    state_end = HALF + STATE
    in_share = jnp.concatenate(
        [
            interleave(keep_gate, got_gate),
            interleave(keep[:, :HALF], got[:, :HALF]),
            in_core_order(keep[:, HALF:state_end], got[:, HALF:state_end], core, 1).reshape(rows, -1),
            interleave(keep[:, state_end : state_end + heads], got[:, state_end : state_end + heads]),
        ],
        axis=1,
    ).astype(f32)
    pre_share = jnp.sum(in_proj.astype(f32) * in_share, axis=1) / pre_gain.astype(f32)
    hidden_out, grad_in = order_back(hidden_out, place), order_back(grad_in, place)
    return (hidden_out, grad_in, in_share, out_share, taps_share, pre_share, gain_share, head_total)


def solution(mesh):
    devices = mesh.devices
    cores = Mesh(devices.reshape(devices.shape[0] // 2, 2, devices.shape[1]), ("chip", "core", "seg"))
    dp, both = ("chip", "core"), ("chip", "core", "seg")
    tokens = P(dp, "seg", None)
    return jax.shard_map(
        per_device,
        mesh=cores,
        in_specs=(tokens, tokens, P(both, None), P(both, None), P(None, both), P(both), P(both), P()),
        out_specs=(tokens, tokens, P(both, None), P(both, None), P(None, both), P(both), P(both), P()),
        check_vma=False,
    )
```

```python
import jax
import jax.numpy as jnp
from jax import lax
from jax.experimental import pallas as pl
from jax.experimental.pallas import tpu as pltpu
from jax.sharding import Mesh
from jax.sharding import PartitionSpec as P

HEADS = 48
HEADDIM = 64
STATE = 128
CONV = 4
INNER = 3072
XBC = 3328
HALF = INNER // 2
LANES = 128
SEGS = 4
LIGHT = pl.CostEstimate(flops=1024, bytes_accessed=1024, transcendentals=0)
VMEM_LIMIT = 48 * 1024 * 1024
LOG2E = 1.4426950408889634

epsilon = 1e-05
f32 = jnp.float32
bf16 = jnp.bfloat16


def own_columns(array, core):
    chips = lax.axis_size("chip")
    width = array.shape[-1] // (2 * chips)
    parted = array.reshape(array.shape[:-1] + (chips, 2, width))
    picked = lax.dynamic_index_in_dim(parted, core, axis=parted.ndim - 2, keepdims=False)
    return picked.reshape(array.shape[:-1] + (chips * width,))


def to_partner(array):
    return lax.ppermute(array, "core", [(0, 1), (1, 0)])


def in_core_order(mine, theirs, core, axis):
    first = jnp.where(core == 0, mine, theirs)
    second = jnp.where(core == 0, theirs, mine)
    return jnp.stack([first, second], axis=axis)


def chip_dims():
    return (lax.axis_size("chip") // 2, 2, lax.axis_size("seg"))


def chip_place():
    chip = lax.axis_index("chip")
    return (chip // 2, chip % 2, lax.axis_index("seg"))


def moved(array, dim, by):
    sizes = chip_dims()
    index = lambda at: (at[0] * sizes[1] + at[1]) * sizes[2] + at[2]
    pairs = []
    for a in range(sizes[0]):
        for b in range(sizes[1]):
            for z in range(sizes[2]):
                to = [a, b, z]
                to[dim] = (to[dim] + by) % sizes[dim]
                pairs.append((index((a, b, z)), index(to)))
    return lax.ppermute(array, ("chip", "seg"), pairs)


def tie(*values):
    return lax.optimization_barrier(values)


def gather_step(data, dim):
    return [data] + [moved(data, dim, by) for by in range(1, chip_dims()[dim])]


def exchanged(array, by):
    line = lax.axis_size("seg")
    return lax.ppermute(array, "seg", [(at, at ^ by) for at in range(line)])


def plane_steps():
    a, b, _ = chip_dims()
    steps = [(at // b, at % b) for at in range(1, a * b)]
    return sorted(steps, key=lambda by: bool(by[0] and by[1]))


def near_steps():
    a, b, _ = chip_dims()
    return plane_steps()[: a + b - 2]


def far_steps():
    a, b, _ = chip_dims()
    return plane_steps()[a + b - 2 :]


def moved_plane(array, by_a, by_b):
    a, b, z = chip_dims()
    pairs = [
        ((at_a * b + at_b) * z + at_z, ((at_a + by_a) % a * b + (at_b + by_b) % b) * z + at_z)
        for at_a in range(a)
        for at_b in range(b)
        for at_z in range(z)
    ]
    return lax.ppermute(array, ("chip", "seg"), pairs)


def gather_plane(data, steps):
    return [moved_plane(data, *by) for by in steps]


def placed_kernel(plan, place_ref, *refs):
    sources, target, sems = refs[:-2], refs[-2], refs[-1]
    copies = []
    for source, lead, at, paired in plan:
        spot = [lax.rem(place_ref[dim] + (size - back), size) for dim, (back, size) in enumerate(at)]
        spot.append(place_ref[2 + lead])
        to = target.at[spot[0], spot[1], :, spot[2]] if paired else target.at[spot[0], spot[1], spot[2]]
        copies.append(pltpu.make_async_copy(sources[source].at[lead], to, sems.at[len(copies)]))
    for copy in copies:
        copy.start()
    for copy in copies:
        copy.wait()


def whole_matrix(gathered, paired, by_bits=False):
    a, b, z = chip_dims()
    at_a, at_b, at_z = chip_place()
    spots = [at_z ^ back if by_bits else (at_z + z - back) % z for back in range(z)]
    plan = [
        (source, back, ((by[0], a), (by[1], b)), paired)
        for source, by in enumerate([(0, 0)] + plane_steps())
        for back in range(z)
    ]
    block = gathered[0].shape[1:]
    shape = (a, b, 2, z) + block[1:] if paired else (a, b, z) + block
    anywhere = pl.BlockSpec(memory_space=pl.ANY)
    whole = pl.pallas_call(
        lambda *refs: placed_kernel(plan, *refs),
        out_shape=jax.ShapeDtypeStruct(shape, bf16),
        in_specs=[pl.BlockSpec(memory_space=pltpu.SMEM)] + [anywhere] * len(gathered),
        out_specs=pl.BlockSpec(memory_space=pltpu.VMEM),
        scratch_shapes=[pltpu.SemaphoreType.DMA((len(plan),))],
        compiler_params=pltpu.CompilerParams(vmem_limit_bytes=VMEM_LIMIT),
        cost_estimate=LIGHT,
    )(jnp.stack([at_a, at_b, *spots]).astype(jnp.int32), *gathered)
    return whole.reshape(-1, shape[-1])


def total(terms):
    result = terms[0].astype(f32)
    for term in terms[1:]:
        result = result + term.astype(f32)
    return result


def reduce_send(terms, axis, dim, wire):
    place, size = chip_place()[dim], chip_dims()[dim]
    pick = lambda at: [lax.dynamic_index_in_dim(term, at, axis=axis, keepdims=False) for term in terms]
    received = [moved(total(pick((place + by) % size)).astype(wire), dim, by) for by in range(1, size)]
    return pick(place), received


def plane_part(partials, by_a, by_b):
    (at_a, at_b, _), (a, b, _) = chip_place(), chip_dims()
    chip = (at_a + by_a) % a * b + (at_b + by_b) % b
    flat = [partial.reshape((a * b,) + partial.shape[2:]) for partial in partials]
    return jnp.concatenate([lax.dynamic_index_in_dim(array, chip, axis=0, keepdims=False) for array in flat], axis=-1)


def reduce_plane(partials, steps):
    return [moved_plane(plane_part(partials, *by), *by) for by in steps]


def reduce_z(firsts):
    joined = jnp.concatenate([total(kept + received) for kept, received in firsts], axis=-1)
    return [reduce_send([joined], 0, 2, bf16)]


def reduce_end(third):
    return total(third[0][0] + third[0][1])


def arrivals(parts):
    return [received for _, received in parts]


def arrived(parts, received):
    return [(kept, new) for (kept, _), new in zip(parts, received)]


def line_perm(turn, back):
    line = lax.axis_size("seg")
    parts = line // SEGS
    pairs = []
    for core in range(2):
        for place in range(line):
            half, odd = divmod(place % SEGS, 2)
            source = core * line + place
            target = odd * line + (2 * core + (half ^ turn)) * parts + place // SEGS
            pairs.append((target, source) if back else (source, target))
    return pairs


def swapped(pair, turn):
    return [jnp.where(turn == 0, pair[0], pair[1]), jnp.where(turn == 0, pair[1], pair[0])]


def send_sequence(array, place):
    pieces = swapped([array[0], array[1]], (place % SEGS) // 2)
    return [lax.ppermute(piece, ("core", "seg"), line_perm(turn, False)) for turn, piece in enumerate(pieces)]


def order_sequence(got, place):
    parts = lax.axis_size("seg") // SEGS
    return jnp.stack(swapped(got, (place // parts) % 2))


def send_back(ordered, place):
    parts = lax.axis_size("seg") // SEGS
    pieces = swapped([ordered[0], ordered[1]], (place // parts) % 2)
    return [lax.ppermute(piece, ("core", "seg"), line_perm(turn, True)) for turn, piece in enumerate(pieces)]


def order_back(got, place):
    return jnp.stack(swapped(got, (place % SEGS) // 2))


def part_pairs(step):
    line = lax.axis_size("seg")
    parts = line // SEGS
    return [(i, i + step) for i in range(line) if 0 <= i + step < line and i // parts == (i + step) // parts]


def entering(decay, state, step):
    parts = lax.axis_size("seg") // SEGS
    total = jnp.zeros_like(state)
    for _ in range(parts - 1):
        total = lax.ppermute(decay * total + state, "seg", part_pairs(step))
    return total


def borrowed(array, step):
    parts = lax.axis_size("seg") // SEGS
    if parts == 1:
        return jnp.zeros_like(array)
    return lax.ppermute(array, "seg", part_pairs(step))


def spilled(grad, edge, taps):
    if lax.axis_size("seg") == SEGS:
        return grad
    edge = borrowed(edge, -1)
    spill = jnp.stack(
        [
            sum(taps[k] * edge[CONV - 1 - k - early] for k in range(CONV - early))
            for early in range(CONV - 1, 0, -1)
        ]
    )
    at = grad.shape[0] - CONV + 1
    return grad.at[at:].set((grad[at:].astype(f32) + spill).astype(bf16))


def dot(a, b, contract):
    return lax.dot_general(a, b, (contract, ((), ())), preferred_element_type=f32)


def normed_kernel(slabs, core_ref, mine_ref, other_ref, gain_ref, normed_ref, turned_ref):
    own = lax.rem(pl.program_id(0), 2) == core_ref[0]
    hidden = jnp.where(own, mine_ref[0], other_ref[0]).astype(f32)
    scale = lax.rsqrt(jnp.mean(hidden * hidden, axis=1, keepdims=True) + epsilon)
    normed = hidden * scale * gain_ref[...]
    normed_ref[...] = normed.astype(bf16)
    turned = normed.T.astype(bf16)
    for to, at, size in slabs:
        turned_ref[to : to + size] = turned[at : at + size]


def normed_tokens(core, mine, other, gain, rows):
    segs, seg_len, width = 2 * mine.shape[0], mine.shape[1], mine.shape[2]
    a, b, z = chip_dims()
    group = 2 * z * rows
    inside = rows % 16 == 0
    slabs = [(0, 0, width)]
    if inside:
        slabs = [
            (chip * group + (at * 2 + core_at) * rows, chip * group + (core_at * z + at) * rows, rows)
            for chip in range(a * b)
            for core_at in range(2)
            for at in range(z)
        ]
    normed, turned = pl.pallas_call(
        lambda *refs: normed_kernel(slabs, *refs),
        grid_spec=pltpu.PrefetchScalarGridSpec(
            num_scalar_prefetch=1,
            grid=(segs,),
            in_specs=[
                pl.BlockSpec((1, seg_len, width), lambda i, core: (i // 2, 0, 0)),
                pl.BlockSpec((1, seg_len, width), lambda i, core: (i // 2, 0, 0)),
                pl.BlockSpec((1, width), lambda i, core: (0, 0)),
            ],
            out_specs=(
                pl.BlockSpec((seg_len, width), lambda i, core: (i, 0)),
                pl.BlockSpec((width, seg_len), lambda i, core: (0, i)),
            ),
        ),
        out_shape=(
            jax.ShapeDtypeStruct((segs * seg_len, width), bf16),
            jax.ShapeDtypeStruct((width, segs * seg_len), bf16),
        ),
        compiler_params=pltpu.CompilerParams(dimension_semantics=("arbitrary",), vmem_limit_bytes=VMEM_LIMIT),
        cost_estimate=LIGHT,
    )(core.reshape(1).astype(jnp.int32), mine, other, gain.reshape(1, width))
    if not inside:
        turned = turned.reshape(a, b, 2, z, rows, -1).transpose(0, 1, 3, 2, 4, 5).reshape(turned.shape)
    return normed, turned


def mixed_kernel(gated_ref, scale_ref, gain_ref, mixed_ref, turned_ref):
    mixed = gated_ref[...] * scale_ref[...] * gain_ref[...]
    mixed_ref[...] = mixed.astype(bf16)
    turned_ref[...] = mixed.T.astype(bf16)


def mixed_tokens(gated, scale, gain, seg_len):
    length, width = gated.shape
    return pl.pallas_call(
        mixed_kernel,
        grid=(length // seg_len,),
        in_specs=[
            pl.BlockSpec((seg_len, width), lambda i: (i, 0)),
            pl.BlockSpec((seg_len, 1), lambda i: (i, 0)),
            pl.BlockSpec((1, width), lambda i: (0, 0)),
        ],
        out_specs=(
            pl.BlockSpec((seg_len, width), lambda i: (i, 0)),
            pl.BlockSpec((width, seg_len), lambda i: (0, i)),
        ),
        out_shape=(
            jax.ShapeDtypeStruct((length, width), bf16),
            jax.ShapeDtypeStruct((width, length), bf16),
        ),
        compiler_params=pltpu.CompilerParams(dimension_semantics=("arbitrary",), vmem_limit_bytes=VMEM_LIMIT),
        cost_estimate=LIGHT,
    )(gated, scale, gain.reshape(1, width))


def columns_of(pair):
    return pl.ds(pair * LANES, LANES)


def low_half(shape):
    return lax.broadcasted_iota(jnp.int32, shape, len(shape) - 1) < HEADDIM


def pair_columns(array, pair, low):
    rows = array.shape[0]
    first = jnp.broadcast_to(array[:, 2 * pair : 2 * pair + 1], (rows, LANES))
    second = jnp.broadcast_to(array[:, 2 * pair + 1 : 2 * pair + 2], (rows, LANES))
    return jnp.where(low, first, second)


def conv_parts(current, before, taps):
    rows = current.shape[0]
    padded = jnp.concatenate([before, current], axis=0)
    seen = [padded[8 - CONV + 1 + k : 8 - CONV + 1 + k + rows] for k in range(CONV - 1)] + [current]
    total = taps[CONV : CONV + 1]
    for k in range(CONV):
        total = total + taps[k : k + 1] * seen[k]
    return total, seen


def exact_sums(chosen, array):
    chosen = jnp.where(chosen, 1.0, 0.0).astype(bf16)
    result = 0.0
    for _ in range(3):
        part = array.astype(bf16)
        array = array - part.astype(f32)
        result = result + dot(chosen, part, ((1,), (0,)))
    return result


def step_terms(raw, head, seg_len):
    shifted = raw + head[1:2]
    step = jnp.maximum(shifted, 0.0) + jnp.log1p(jnp.exp(-jnp.abs(shifted)))
    log_decay = step * head[0:1]
    at_or_before = lax.broadcasted_iota(jnp.int32, (seg_len, seg_len), 0) >= lax.broadcasted_iota(
        jnp.int32, (seg_len, seg_len), 1
    )
    sums = exact_sums(at_or_before, log_decay)
    return shifted, step, log_decay, sums * LOG2E


def forward_kernel(
    proj_ref, taps_ref, head_ref, skip_ref, rim_ref, init_ref,
    values_ref, prior_ref, final_ref, last_ref, state_ref, tail_ref,
):
    seg_len = proj_ref.shape[0]
    half = seg_len // 2

    @pl.when(pl.program_id(0) == 0)
    def _():
        state_ref[...] = init_ref[...]
        tail_ref[...] = rim_ref[...]

    def activated(begin):
        at = pl.ds(begin, LANES)
        total, _ = conv_parts(proj_ref[:, at], tail_ref[:, at], taps_ref[:, at])
        return total * jax.nn.sigmoid(total)

    b_low = activated(HALF).astype(bf16)
    b_turned = activated(HALF).T.astype(bf16)
    c_low = activated(HALF + STATE).astype(bf16)
    _, step, _, sums = step_terms(proj_ref[:, HALF + 2 * STATE :], head_ref, seg_len)
    sums_turned, step_turned = sums.T, step.T
    scores = dot(c_low, b_low, ((1,), (1,)))
    kept = lax.broadcasted_iota(jnp.int32, (half, half), 0) >= lax.broadcasted_iota(jnp.int32, (half, half), 1)
    first_scores = jnp.where(kept, scores[:half, :half], 0.0)
    later_scores = scores[half:, :half]
    second_scores = jnp.where(kept, scores[half:, half:], 0.0)
    low = low_half((seg_len, LANES))
    last_ref[...] = jnp.broadcast_to(sums[seg_len - 1 :], last_ref.shape)

    for pair in range(HEADS // 4):
        at = columns_of(pair)
        x_values = activated(pair * LANES)
        x_low = x_values.astype(bf16)
        sums_pair = pair_columns(sums, pair, low)
        last_pair = sums_pair[seg_len - 1 :]
        carry = jnp.exp2(last_pair - sums_pair) * pair_columns(step, pair, low)
        scaled_x = (carry * x_low.astype(f32)).astype(bf16)
        prior = state_ref[:, at]
        prior_low = prior.astype(bf16)
        prior_ref[0, :, at] = prior_low
        from_state = jnp.exp2(sums_pair) * dot(c_low, prior_low, ((1,), (0,)))
        state_ref[:, at] = jnp.exp2(last_pair) * prior + dot(b_turned, scaled_x, ((1,), (0,)))
        early, late = 0.0, 0.0
        for side in range(2):
            head = 2 * pair + side
            x_side = jnp.where(low if side == 0 else ~low, x_values, 0.0).astype(bf16)
            at_token = jnp.broadcast_to(sums[:, head : head + 1], (seg_len, half))
            at_source, source_step = sums_turned[head : head + 1], step_turned[head : head + 1]
            first = jnp.exp2(jnp.minimum(at_token[:half] - at_source[:, :half], 0.0)) * first_scores
            first = (first * source_step[:, :half]).astype(bf16)
            later = jnp.exp2(at_token[half:] - at_source[:, :half]) * later_scores
            later = (later * source_step[:, :half]).astype(bf16)
            second = jnp.exp2(jnp.minimum(at_token[half:] - at_source[:, half:], 0.0)) * second_scores
            second = (second * source_step[:, half:]).astype(bf16)
            early = early + dot(first, x_side[:half], ((1,), (0,)))
            late = late + dot(jnp.concatenate([later, second], axis=1), x_side, ((1,), (0,)))
        intra = jnp.concatenate([early, late], axis=0)
        values_ref[:, at] = intra + from_state + skip_ref[:, at] * x_values

    tail_ref[...] = proj_ref[seg_len - 8 :, : HALF + 2 * STATE]
    final_ref[...] = state_ref[...]


def full_block(shape):
    return pl.BlockSpec(shape, lambda *_: (0,) * len(shape))


def scan_forward(proj, taps, head, skip, rim, init, seg_len):
    segs = proj.shape[0] // seg_len
    wide = HALF + 2 * STATE
    return pl.pallas_call(
        forward_kernel,
        grid=(segs,),
        out_shape=(
            jax.ShapeDtypeStruct((proj.shape[0], HALF), f32),
            jax.ShapeDtypeStruct((segs, STATE, HALF), bf16),
            jax.ShapeDtypeStruct((STATE, HALF), f32),
            jax.ShapeDtypeStruct((segs * 8, LANES), f32),
        ),
        in_specs=[
            pl.BlockSpec((seg_len, proj.shape[1]), lambda i: (i, 0)),
            full_block((8, wide)),
            full_block((8, LANES)),
            full_block((1, HALF)),
            full_block((8, wide)),
            full_block((STATE, HALF)),
        ],
        out_specs=(
            pl.BlockSpec((seg_len, HALF), lambda i: (i, 0)),
            pl.BlockSpec((1, STATE, HALF), lambda i: (i, 0, 0)),
            full_block((STATE, HALF)),
            pl.BlockSpec((8, LANES), lambda i: (i, 0)),
        ),
        scratch_shapes=[pltpu.VMEM((STATE, HALF), f32), pltpu.VMEM((8, wide), f32)],
        compiler_params=pltpu.CompilerParams(
            dimension_semantics=("arbitrary",), vmem_limit_bytes=VMEM_LIMIT
        ),
        cost_estimate=LIGHT,
    )(proj, taps, head, skip, rim, init)


def split_dot(array, other):
    high = array.astype(bf16)
    rest = (array - high.astype(f32)).astype(bf16)
    return dot(high, other, ((1,), (0,))) + dot(rest, other, ((1,), (0,)))


def backward_kernel(
    group, proj_ref, before_ref, taps_ref, rim_ref, shared_ref, shared_before_ref, shared_taps_ref, shared_rim_ref,
    head_ref, skip_ref, end_ref, prior_ref, values_ref, grad_ref, core_ref,
    grad_x_ref, mine_ref, theirs_ref, grad_raw_ref, taps_grad_ref, skip_grad_ref, head_grad_ref, edge_ref, start_ref,
    later_ref, local_ref, scaled_ref, grad_state_ref, inner_ref, source_ref, carry_ref, decay_ref,
):
    seg_len = proj_ref.shape[0]
    half = seg_len // 2
    turn = pl.program_id(0)

    @pl.when(turn == 0)
    def _():
        later_ref[...] = end_ref[...]
        edge_ref[...] = jnp.zeros_like(edge_ref)
        taps_grad_ref[...] = jnp.zeros_like(taps_grad_ref)
        skip_grad_ref[...] = jnp.zeros_like(skip_grad_ref)
        head_grad_ref[...] = jnp.zeros_like(head_grad_ref)

    first_segment = turn == pl.num_programs(0) - 1

    def conv_at(at, current, ahead, taps, rim):
        before = jnp.where(first_segment, rim[:, at], ahead[:, at])
        return conv_parts(current[:, at], before, taps[:, at])

    def activated(begin):
        total, _ = conv_at(pl.ds(begin, LANES), shared_ref, shared_before_ref, shared_taps_ref, shared_rim_ref)
        return total * jax.nn.sigmoid(total)

    b_values = activated(0)
    c_values = activated(STATE)
    b_low, c_low, c_turned = b_values.astype(bf16), c_values.astype(bf16), c_values.T.astype(bf16)
    shifted, step, log_decay, sums = step_terms(shared_ref[:, 2 * STATE :], head_ref, seg_len)
    sums_turned = sums.T
    scores = dot(b_low, c_low, ((1,), (1,)))
    kept = lax.broadcasted_iota(jnp.int32, (half, half), 0) <= lax.broadcasted_iota(jnp.int32, (half, half), 1)
    first_scores = jnp.where(kept, scores[:half, :half], 0.0)
    later_scores = scores[:half, half:]
    second_scores = jnp.where(kept, scores[half:, half:], 0.0)
    low = low_half((seg_len, LANES))
    first_grad, later_grad, second_grad = 0.0, 0.0, 0.0

    pairs = grad_ref.shape[1] // LANES
    for pair in range(pairs):
        at = columns_of(pair)
        total, seen = conv_at(at, proj_ref, before_ref, taps_ref, rim_ref)
        sigmoid = jax.nn.sigmoid(total)
        x_values = total * sigmoid
        x_low = x_values.astype(bf16)
        x_wide = x_low.astype(f32)
        sums_pair = pair_columns(sums, group * pairs + pair, low)
        step_pair = pair_columns(step, group * pairs + pair, low)
        last_pair = sums_pair[seg_len - 1 :]
        gap = jnp.exp2(last_pair - sums_pair)
        scaled_ref[:, at] = (gap * step_pair * x_wide).astype(bf16)
        grad_values = grad_ref[:, at]
        grad_state_ref[:, at] = (grad_values * jnp.exp2(sums_pair)).astype(bf16)
        later = later_ref[:, at]
        later_low = later.astype(bf16)
        local_ref[:, at] = later_low
        prior = prior_ref[0, :, at]
        decay_ref[:, at] = jnp.broadcast_to(
            jnp.sum(later * prior.astype(f32), axis=0, keepdims=True), (8, LANES)
        )
        grad_prior = dot(c_turned, grad_state_ref[:, at], ((1,), (0,)))
        later_ref[:, at] = jnp.exp2(last_pair) * later + grad_prior
        grad_scaled = dot(b_low, later_low, ((1,), (0,)))
        stepped = (step_pair * x_wide).astype(bf16)
        early, late = 0.0, 0.0
        for side in range(2):
            head = 2 * (group * pairs + pair) + side
            grad_low = jnp.where(low if side == 0 else ~low, grad_values, 0.0).astype(bf16)
            at_source = jnp.broadcast_to(sums[:, head : head + 1], (seg_len, half))
            at_token = sums_turned[head : head + 1]
            grad_weights = dot(stepped, grad_low, ((1,), (1,)))
            first = jnp.exp2(jnp.minimum(at_token[:, :half] - at_source[:half], 0.0))
            after = jnp.exp2(at_token[:, half:] - at_source[:half])
            second = jnp.exp2(jnp.minimum(at_token[:, half:] - at_source[half:], 0.0))
            first_grad = first_grad + first * grad_weights[:half, :half]
            later_grad = later_grad + after * grad_weights[:half, half:]
            second_grad = second_grad + second * grad_weights[half:, half:]
            upper = jnp.concatenate([first * first_scores, after * later_scores], axis=1).astype(bf16)
            early = early + dot(upper, grad_low, ((1,), (0,)))
            late = late + dot((second * second_scores).astype(bf16), grad_low[half:], ((1,), (0,)))
        inner = jnp.concatenate([early, late], axis=0)
        skip = skip_ref[:, at]
        skip_grad_ref[:, at] += jnp.sum(grad_values * x_values, axis=0, keepdims=True)
        inner_ref[:, at] = grad_values * (values_ref[:, at] - skip * x_values)
        source_ref[:, at] = x_wide * inner
        carry_ref[:, at] = x_wide * grad_scaled
        grad_x = skip * grad_values + step_pair * (inner + gap * grad_scaled)
        grad_total = grad_x * (sigmoid * (1.0 + total * (1.0 - sigmoid)))
        for k in range(CONV):
            taps_grad_ref[k : k + 1, at] += jnp.sum(grad_total * seen[k], axis=0, keepdims=True)
        taps_grad_ref[CONV : CONV + 1, at] += jnp.sum(grad_total, axis=0, keepdims=True)
        extended = jnp.concatenate([grad_total, edge_ref[:, at]], axis=0)
        edge_ref[:, at] = grad_total[:8]
        taps = taps_ref[:, at]
        grad_conv = taps[CONV - 1 : CONV] * grad_total
        for k in range(CONV - 1):
            grad_conv = grad_conv + taps[k : k + 1] * extended[CONV - 1 - k : CONV - 1 - k + seg_len]
        grad_x_ref[:, at] = grad_conv.astype(bf16)

    width = grad_ref.shape[1]
    channel = lax.broadcasted_iota(jnp.int32, (width, LANES), 0) // HEADDIM + group * width // HEADDIM
    heads = jnp.where(channel == lax.broadcasted_iota(jnp.int32, (width, LANES), 1), 1.0, 0.0).astype(bf16)
    tail = jnp.exp2(sums[seg_len - 1 :] - sums)
    source_grad = split_dot(source_ref[...], heads)
    step_grad = source_grad + tail * split_dot(carry_ref[...], heads)
    used = step * step_grad
    sum_grad = split_dot(inner_ref[...], heads) - used
    at_last = jnp.sum(used - step * source_grad, axis=0, keepdims=True)
    at_last = at_last + split_dot(decay_ref[...], heads)[:1] * jnp.exp2(sums[seg_len - 1 :])
    is_last = lax.broadcasted_iota(jnp.int32, (seg_len, LANES), 0) == seg_len - 1
    sum_grad = sum_grad + jnp.where(is_last, at_last, 0.0)
    at_or_after = lax.broadcasted_iota(jnp.int32, (seg_len, seg_len), 0) <= lax.broadcasted_iota(
        jnp.int32, (seg_len, seg_len), 1
    )
    log_grad = exact_sums(at_or_after, sum_grad)
    grad_raw = (step_grad + head_ref[0:1] * log_grad) * jax.nn.sigmoid(shifted)
    grad_raw_ref[...] = grad_raw
    head_grad_ref[CONV + 1 : CONV + 2] += jnp.sum(log_grad * log_decay, axis=0, keepdims=True)
    head_grad_ref[CONV + 2 : CONV + 3] += jnp.sum(grad_raw, axis=0, keepdims=True)

    first_low = jnp.where(kept, first_grad, 0.0)
    second_low = jnp.where(kept, second_grad, 0.0)
    grad_scores = jnp.concatenate(
        [
            jnp.concatenate([first_low, later_grad], axis=1),
            jnp.concatenate([jnp.zeros_like(first_low), second_low], axis=1),
        ],
        axis=0,
    )
    start_ref[...] = later_ref[...]
    grad_b = dot(scaled_ref[...], local_ref[...], ((1,), (1,))) + dot(
        grad_scores.astype(bf16), c_low, ((1,), (0,))
    )
    grad_c = dot(grad_state_ref[...], prior_ref[0], ((1,), (1,))) + dot(
        grad_scores.T.astype(bf16), b_low, ((1,), (0,))
    )
    first = core_ref[0] == 0
    mine_ref[...] = jnp.where(first, grad_b, grad_c)
    theirs_ref[...] = jnp.where(first, grad_c, grad_b)


GROUPS = 1


def scan_backward(group, core, proj, taps, head, skip, rim, end, prior, values, grad_values, seg_len):
    length = proj.shape[0]
    segs = length // seg_len
    width, shared = HALF // GROUPS, proj.shape[1] - HALF
    back = lambda width, at=0: pl.BlockSpec((seg_len, width), lambda i: (segs - 1 - i, at))
    row_ahead = lambda i: jnp.maximum((segs - 1 - i) * (seg_len // 8) - 1, 0)
    ahead = lambda width, at: pl.BlockSpec((8, width), lambda i: (row_ahead(i), at))
    column = lambda rows, width, at: pl.BlockSpec((rows, width), lambda i: (0, at))
    both = HALF // shared
    return pl.pallas_call(
        lambda *refs: backward_kernel(group, *refs),
        grid=(segs,),
        out_shape=(
            jax.ShapeDtypeStruct((length, width), bf16),
            jax.ShapeDtypeStruct((length, STATE), f32),
            jax.ShapeDtypeStruct((length, STATE), f32),
            jax.ShapeDtypeStruct((length, LANES), f32),
            jax.ShapeDtypeStruct((8, width), f32),
            jax.ShapeDtypeStruct((1, width), f32),
            jax.ShapeDtypeStruct((8, LANES), f32),
            jax.ShapeDtypeStruct((8, width), f32),
            jax.ShapeDtypeStruct((STATE, width), f32),
        ),
        in_specs=[
            back(width, group),
            ahead(width, group),
            column(8, width, group),
            column(8, width, group),
            back(shared, both),
            ahead(shared, both),
            column(8, shared, both),
            column(8, shared, both),
            full_block((8, LANES)),
            column(1, width, group),
            column(STATE, width, group),
            pl.BlockSpec((1, STATE, width), lambda i: (segs - 1 - i, 0, group)),
            back(width, group),
            back(width, group),
            pl.BlockSpec(memory_space=pltpu.SMEM),
        ],
        out_specs=(
            back(width),
            back(STATE),
            back(STATE),
            back(LANES),
            full_block((8, width)),
            full_block((1, width)),
            full_block((8, LANES)),
            full_block((8, width)),
            full_block((STATE, width)),
        ),
        scratch_shapes=[
            pltpu.VMEM((STATE, width), f32),
            pltpu.VMEM((STATE, width), bf16),
            pltpu.VMEM((seg_len, width), bf16),
            pltpu.VMEM((seg_len, width), bf16),
            pltpu.VMEM((seg_len, width), f32),
            pltpu.VMEM((seg_len, width), f32),
            pltpu.VMEM((seg_len, width), f32),
            pltpu.VMEM((8, width), f32),
        ],
        compiler_params=pltpu.CompilerParams(
            dimension_semantics=("arbitrary",), vmem_limit_bytes=VMEM_LIMIT
        ),
        cost_estimate=LIGHT,
    )(
        proj, proj, taps, rim, proj, proj, taps, rim, head, skip, end, prior, values, grad_values,
        core.reshape(1).astype(jnp.int32),
    )


def half_kernel(transposed, count, core_ref, *refs):
    inputs, mine_ref, theirs_ref = refs[: 2 * count], refs[-2], refs[-1]
    total = refs[2 * count][...] if len(refs) > 2 * count + 2 else 0.0
    for left, right in zip(inputs[:count], inputs[count:]):
        total = total + dot(left[...], right[...], ((1,), (1 if transposed else 0,)))
    own = lax.rem(pl.program_id(0), 2) == core_ref[0]

    @pl.when(own)
    def _():
        mine_ref[0] = total

    @pl.when(jnp.logical_not(own))
    def _():
        theirs_ref[0] = total.astype(bf16)


def half_products(core, terms, seg_len, width, transposed, base=()):
    length = terms[0][0].shape[0]
    left = [pl.BlockSpec((seg_len, array.shape[1]), lambda i, core: (i, 0)) for array, _, _ in terms]
    right = []
    for array, matrix, at in terms:
        if transposed:
            right.append(pl.BlockSpec((width, array.shape[1]), lambda i, core, at=at: (0, at(core[0]))))
        else:
            right.append(pl.BlockSpec(matrix.shape, lambda i, core: (0, 0)))
    depth = sum(array.shape[1] for array, _, _ in terms)
    mine, theirs = pl.pallas_call(
        lambda *refs: half_kernel(transposed, len(terms), *refs),
        grid_spec=pltpu.PrefetchScalarGridSpec(
            num_scalar_prefetch=1,
            grid=(length // seg_len,),
            in_specs=left + right + [pl.BlockSpec((seg_len, width), lambda i, core: (i, 0)) for _ in base],
            out_specs=[pl.BlockSpec((1, seg_len, width), lambda i, core: (i // 2, 0, 0))] * 2,
        ),
        out_shape=(
            jax.ShapeDtypeStruct((length // seg_len // 2, seg_len, width), f32),
            jax.ShapeDtypeStruct((length // seg_len // 2, seg_len, width), bf16),
        ),
        compiler_params=pltpu.CompilerParams(dimension_semantics=("arbitrary",), vmem_limit_bytes=VMEM_LIMIT),
        cost_estimate=LIGHT,
    )(core.reshape(1).astype(jnp.int32), *[array for array, _, _ in terms], *[matrix for _, matrix, _ in terms], *base)
    return mine, theirs


def shared_kernel(core_ref, proj_ref, rim_ref, taps_ref, mine_ref, other_ref, grad_ref, taps_grad_ref, edge_ref):
    total, seen = conv_parts(proj_ref[...], rim_ref[...], taps_ref[...])
    sigmoid = jax.nn.sigmoid(total)
    grad_total = mine_ref[...] + other_ref[...]
    grad_total = grad_total * (sigmoid * (1.0 + total * (1.0 - sigmoid)))
    sums = [jnp.sum(grad_total * part, axis=0, keepdims=True) for part in seen]
    sums = sums + [jnp.sum(grad_total, axis=0, keepdims=True), jnp.zeros((8 - CONV - 1, LANES), f32)]
    taps_grad_ref[...] = jnp.concatenate(sums, axis=0)
    edge_ref[...] = grad_total[:8]
    taps = taps_ref[...]
    extended = jnp.concatenate([grad_total, jnp.zeros((8, LANES), f32)], axis=0)
    grad_conv = taps[CONV - 1 : CONV] * grad_total
    for k in range(CONV - 1):
        grad_conv = grad_conv + taps[k : k + 1] * extended[CONV - 1 - k : CONV - 1 - k + grad_total.shape[0]]
    grad_ref[...] = grad_conv.astype(bf16)


def shared_backward(core, proj, rim, taps, mine, other):
    length = proj.shape[0]
    picked = lambda rows: pl.BlockSpec((rows, LANES), lambda i, core: (0, HALF // LANES + core[0]))
    whole = lambda rows: pl.BlockSpec((rows, LANES), lambda i, core: (0, 0))
    return pl.pallas_call(
        shared_kernel,
        grid_spec=pltpu.PrefetchScalarGridSpec(
            num_scalar_prefetch=1,
            grid=(1,),
            in_specs=[picked(length), picked(8), picked(8), whole(length), whole(length)],
            out_specs=(whole(length), whole(8), whole(8)),
        ),
        out_shape=(
            jax.ShapeDtypeStruct((length, LANES), bf16),
            jax.ShapeDtypeStruct((8, LANES), f32),
            jax.ShapeDtypeStruct((8, LANES), f32),
        ),
        compiler_params=pltpu.CompilerParams(vmem_limit_bytes=VMEM_LIMIT),
        cost_estimate=LIGHT,
    )(core.reshape(1).astype(jnp.int32), proj, rim, taps, mine, other)


def per_device(hidden_in, cotangent, in_proj, out_proj, conv_params, pre_gain, gated_gain, head_params):
    chips, line = lax.axis_size("chip"), lax.axis_size("seg")
    core, place = lax.axis_index("core"), lax.axis_index("seg")
    rows, model_width = in_proj.shape[0], hidden_in.shape[2]
    heads = HEADS // 2

    conv_width, gain_width = conv_params.shape[1], gated_gain.shape[0]
    used = HALF + 2 * STATE + heads
    spare = -used % LANES
    small = jnp.zeros((rows, spare), bf16)
    small = small.at[: CONV + 1, :conv_width].set(conv_params)
    small = small.at[CONV + 1, :rows].set(pre_gain)
    small = small.at[CONV + 2, :gain_width].set(gated_gain)

    def conv_side(which):
        return jnp.concatenate(
            [
                own_columns(in_proj[:, INNER : 2 * INNER], which),
                in_proj[:, 2 * INNER : INNER + XBC],
                own_columns(in_proj[:, INNER + XBC :], which),
                small,
            ],
            axis=1,
        )

    def gate_side(which):
        return own_columns(in_proj[:, :INNER], which)

    conv_swap = to_partner(conv_side(1 - core))
    conv_block = in_core_order(conv_side(core), conv_swap, core, 0)
    conv_z = gather_step(conv_block, 2)
    gate_swap = to_partner(gate_side(1 - core))
    gate_block = in_core_order(gate_side(core), gate_swap, core, 0)
    conv_z, hidden_in, gate_block = tie(conv_z, hidden_in, gate_block)
    conv_own = jnp.stack(conv_z)
    conv_near = gather_plane(conv_own, near_steps())
    hidden_got = send_sequence(hidden_in, place)
    conv_own, conv_near, hidden_got, gate_block = tie(conv_own, conv_near, hidden_got, gate_block)
    hidden_half = order_sequence(hidden_got, place)
    conv_far = gather_plane(conv_own, far_steps())
    gate_z = gather_step(gate_block, 2)
    hidden_other = to_partner(hidden_half)
    conv_far, gate_z, hidden_other, out_proj = tie(conv_far, gate_z, hidden_other, out_proj)
    out_own = out_proj[None]
    out_other = exchanged(out_own, 1)
    gate_own = jnp.stack(gate_z)
    gate_near = gather_plane(gate_own, near_steps())
    conv_all = whole_matrix([conv_own, *conv_near, *conv_far], True)

    small_all = conv_all.reshape(chips, 2, line, rows, -1)[..., used:].astype(f32)
    taps_full = small_all[..., : CONV + 1, :conv_width].transpose(3, 0, 1, 2, 4).reshape(CONV + 1, XBC)
    taps = jnp.concatenate([own_columns(taps_full[:, :INNER], core), taps_full[:, INNER:]], axis=1)
    gain_pre = small_all[..., CONV + 1, :rows].reshape(model_width)
    gain_gate = lax.dynamic_index_in_dim(
        small_all[..., CONV + 2, :gain_width], core, axis=1, keepdims=False
    ).reshape(HALF)
    params = own_columns(head_params, core)

    seg_len = hidden_half.shape[1]
    tokens = SEGS * seg_len
    normed, normed_turned = normed_tokens(core, hidden_half, hidden_other, gain_pre, rows)
    projected = dot(normed, conv_all, ((1,), (0,)))
    projected, gate_own, gate_near, out_own, out_other = tie(projected, gate_own, gate_near, out_own, out_other)
    gate_far = gather_plane(gate_own, far_steps())
    out_own = jnp.concatenate([out_own, out_other])
    out_others = []
    for bit in range(1, (line - 1).bit_length()):
        out_others.append(exchanged(out_own, 2**bit))
        if 2 ** (bit + 1) < line:
            out_own, out_others = jnp.concatenate([out_own, out_others[-1]]), []

    taps = jnp.pad(taps, ((0, 8 - CONV - 1), (0, projected.shape[1] - taps.shape[1])))
    head = jnp.pad(jnp.stack([-jnp.exp(params[0]), params[1]]), ((0, 6), (0, LANES - heads)))
    skip = jnp.repeat(params[2], HEADDIM).reshape(1, HALF)
    wide = HALF + 2 * STATE
    rim = borrowed(projected[tokens - 8 :], 1)
    nothing = jnp.zeros((STATE, HALF), f32)
    values, prior, final, last = scan_forward(projected, taps, head, skip, rim, nothing, seg_len)
    if line > SEGS:
        last = jnp.sum(last.reshape(SEGS, 8, LANES)[:, 0, :heads], axis=0)
        decay = jnp.repeat(jnp.exp2(last), HEADDIM)
        begin = entering(decay, final, 1)
        values, prior, _, _ = scan_forward(projected, taps, head, skip, rim, begin, seg_len)

    values, gate_far, out_others, cotangent = tie(values, gate_far, out_others, cotangent)
    cot_got = send_sequence(cotangent, place)
    out_own = jnp.concatenate([out_own, *out_others])
    out_all = gather_plane(out_own, plane_steps())
    gate_matrix = whole_matrix([gate_own, *gate_near, *gate_far], True)
    gate_input = dot(normed, gate_matrix, ((1,), (0,)))
    gate_input, cot_first = tie(gate_input, cot_got[0])

    silu_gate = jax.nn.silu(gate_input)
    gated = values * silu_gate
    squares = jnp.sum(gated * gated, axis=1)
    squares_other = to_partner(squares)
    scale = lax.rsqrt((squares + squares_other) / INNER + epsilon)[:, None]
    mixed, mixed_turned = mixed_tokens(gated, scale, gain_gate, seg_len)
    mixed_turned, out_all, cot_second = tie(mixed_turned, out_all, cot_got[1])
    cot_half = order_sequence([cot_first, cot_second], place)
    cot_other = to_partner(cot_half)
    cot = in_core_order(cot_half, cot_other, core, 1)
    upstream = cot.reshape(tokens, model_width)
    by_owner = lambda grad: grad.astype(bf16).reshape(chip_dims() + (-1, grad.shape[1]))
    out_grad = by_owner(dot(mixed_turned, upstream, ((1,), (0,))))
    cut = model_width // 2
    out_first = [reduce_send([out_grad[..., :cut]], 1, 1, bf16), reduce_send([out_grad[..., cut:]], 0, 0, bf16)]
    out_matrix = whole_matrix([out_own, *out_all], False, True)
    branch, branch_sent = half_products(core, [(mixed, out_matrix, None)], seg_len, model_width, False)
    branch_sent, upstream = tie(branch_sent, upstream)
    branch_other = to_partner(branch_sent)
    grad_mixed = dot(upstream, out_matrix, ((1,), (1,)))
    grad_mixed, out_got = tie(grad_mixed, arrivals(out_first))
    out_second = [
        reduce_send(kept + received, 0, dim, bf16) for (kept, received), dim in zip(arrived(out_first, out_got), (0, 1))
    ]
    unit = gated * scale
    gain_grad = grad_mixed * gain_gate
    along = jnp.sum(gain_grad * unit, axis=1)
    along_other = to_partner(along)
    along_other, branch_other = tie(along_other, branch_other)
    hidden_out = send_back((hidden_half.astype(f32) + branch + branch_other.astype(f32)).astype(bf16), place)
    along = ((along + along_other) / INNER)[:, None]
    gate_gain_grad = jnp.sum(grad_mixed * unit, axis=0)
    grad_gated = scale * (gain_grad - unit * along)
    grad_values = grad_gated * silu_gate
    sigmoid = jax.nn.sigmoid(gate_input)
    grad_gate = (grad_gated * values * (sigmoid * (1.0 + gate_input * (1.0 - sigmoid)))).astype(bf16)
    gate_grad = by_owner(dot(normed_turned, grad_gate, ((1,), (0,))))
    gate_grad, grad_values, out_got = tie(gate_grad, grad_values, arrivals(out_second))
    gate_got = reduce_plane([gate_grad], plane_steps())
    scan = lambda later: scan_backward(
        0, core, projected, taps, head, skip, rim, later, prior, values, grad_values, seg_len
    )
    if line > SEGS:
        nothing = entering(decay, scan(nothing)[-1], -1)
    back = scan(nothing)
    back, gate_got, hidden_out, grad_gate = tie(back, gate_got, hidden_out, grad_gate)
    ((early_kept, early_got),) = reduce_z(
        [
            *arrived(out_second, out_got),
            ([plane_part([gate_grad], 0, 0)], gate_got),
        ]
    )
    grad_x, mine, theirs, grad_raw, x_taps_grad, skip_grad, head_sums, x_edge, _ = back
    grad_x = spilled(grad_x, x_edge, taps[:, :HALF])
    other = to_partner(theirs)
    x_grad = by_owner(dot(normed_turned, grad_x, ((1,), (0,))))
    other, x_grad = tie(other, x_grad)
    grad_state, state_taps_grad, state_edge = shared_backward(core, projected, rim, taps, mine, other)
    grad_state = spilled(grad_state, state_edge, lax.dynamic_slice_in_dim(taps, HALF + core * STATE, STATE, axis=1))
    grad_raw = grad_raw.astype(bf16)
    rest_grad = by_owner(dot(normed_turned, jnp.concatenate([grad_state, grad_raw], axis=1), ((1,), (0,))))
    rest_grad, x_grad, grad_gate = tie(rest_grad, x_grad, grad_gate)
    conv_near = reduce_plane([x_grad, rest_grad], near_steps())
    base = dot(grad_gate, gate_matrix, ((1,), (1,)))
    terms = [
        (grad_x, conv_all, lambda core: 0),
        (grad_state, conv_all, lambda core: HALF // LANES + core),
        (grad_raw, conv_all, lambda core: (HALF + 2 * STATE) // LANES),
    ]
    grad_normed, sent_normed = half_products(core, terms, seg_len, model_width, True, (base,))
    row = lax.broadcasted_iota(jnp.int32, (8, 1), 0)
    small = x_taps_grad + jnp.where(row == CONV + 1, gate_gain_grad, 0.0) + jnp.where(row == CONV + 2, skip_grad, 0.0)
    small = jnp.concatenate([small, state_taps_grad + head_sums], axis=1)
    sent_normed, early_got, conv_near, small, x_grad, rest_grad = tie(
        sent_normed, early_got, conv_near, small, x_grad, rest_grad
    )
    other_normed = to_partner(sent_normed)
    wide_hidden = hidden_half.astype(f32)
    hidden_scale = lax.rsqrt(jnp.mean(wide_hidden * wide_hidden, axis=-1, keepdims=True) + epsilon)
    grad_normed = (grad_normed + other_normed.astype(f32)) * gain_pre
    hidden_unit = wide_hidden * hidden_scale
    along = jnp.mean(grad_normed * hidden_unit, axis=-1, keepdims=True)
    grad_hidden = hidden_scale * (grad_normed - hidden_unit * along)
    grad_in = (cot_half.astype(f32) + grad_hidden).astype(bf16)
    grad_in, x_grad, rest_grad = tie(grad_in, x_grad, rest_grad)
    grad_in = send_back(grad_in, place)
    conv_far = reduce_plane([x_grad, rest_grad], far_steps())
    grad_in, conv_far = tie(grad_in, conv_far)
    late = reduce_z([([plane_part([x_grad, rest_grad], 0, 0)], [*conv_near, *conv_far])])
    for dim in range(2):
        small = small + sum(moved(small, dim, by) for by in range(1, chip_dims()[dim]))
    for bit in range((line - 1).bit_length()):
        small = small + exchanged(small, 2**bit)
    small_other = to_partner(small)
    late_got, small_other = tie(arrivals(late), small_other)
    early_share = total([*early_kept, *early_got])
    out_share = early_share[:, :model_width]
    paired = lambda share: share.astype(bf16).reshape(2, rows, -1)
    gate_share, conv_share = paired(early_share[:, model_width:]), paired(reduce_end(arrived(late, late_got)))

    def mine_and_partner(share):
        keep = lax.dynamic_index_in_dim(share, core, axis=0, keepdims=False)
        give = lax.dynamic_index_in_dim(share, 1 - core, axis=0, keepdims=False)
        return keep, to_partner(give)

    both = in_core_order(small, small_other, core, 0)
    natural = lambda array, width: array.reshape(2, -1, chips, width).transpose(1, 2, 0, 3).reshape(-1, 2 * chips * width)
    device = (lax.axis_index("chip") * 2 + core) * line + place
    columns = natural(both[:, :, :HALF], HALF // chips)
    taps_all = jnp.concatenate([columns, both[0, :, HALF:], both[1, :, HALF:]], axis=1)[: CONV + 1]
    taps_share = lax.dynamic_slice_in_dim(taps_all, device * conv_width, conv_width, axis=1)
    gain_share = lax.dynamic_slice_in_dim(columns[CONV + 1], device * gain_width, gain_width, axis=0)
    head_total = jnp.concatenate(
        [
            natural(both[:, CONV + 1 : CONV + 3, HALF : HALF + heads], heads // chips),
            jnp.sum(columns[CONV + 2].reshape(1, HEADS, HEADDIM), axis=2),
        ]
    )

    def interleave(mine, theirs):
        width = mine.shape[1] // chips
        both = in_core_order(mine.reshape(rows, chips, width), theirs.reshape(rows, chips, width), core, 2)
        return both.reshape(rows, -1)

    keep_gate, got_gate = mine_and_partner(gate_share)
    keep, got = mine_and_partner(conv_share)
    state_end = HALF + STATE
    in_share = jnp.concatenate(
        [
            interleave(keep_gate, got_gate),
            interleave(keep[:, :HALF], got[:, :HALF]),
            in_core_order(keep[:, HALF:state_end], got[:, HALF:state_end], core, 1).reshape(rows, -1),
            interleave(keep[:, state_end : state_end + heads], got[:, state_end : state_end + heads]),
        ],
        axis=1,
    ).astype(f32)
    pre_share = jnp.sum(in_proj.astype(f32) * in_share, axis=1) / pre_gain.astype(f32)
    hidden_out, grad_in = order_back(hidden_out, place), order_back(grad_in, place)
    return (hidden_out, grad_in, in_share, out_share, taps_share, pre_share, gain_share, head_total)


def solution(mesh):
    devices = mesh.devices
    cores = Mesh(devices.reshape(devices.shape[0] // 2, 2, devices.shape[1]), ("chip", "core", "seg"))
    dp, both = ("chip", "core"), ("chip", "core", "seg")
    tokens = P(dp, "seg", None)
    return jax.shard_map(
        per_device,
        mesh=cores,
        in_specs=(tokens, tokens, P(both, None), P(both, None), P(None, both), P(both), P(both), P()),
        out_specs=(tokens, tokens, P(both, None), P(both, None), P(None, both), P(both), P(both), P()),
        check_vma=False,
    )
```

```python
import jax
import jax.numpy as jnp
from jax import lax
from jax.experimental import pallas as pl
from jax.experimental.pallas import tpu as pltpu
from jax.sharding import Mesh
from jax.sharding import PartitionSpec as P

HEADS = 48
HEADDIM = 64
STATE = 128
CONV = 4
INNER = 3072
XBC = 3328
HALF = INNER // 2
LANES = 128
SEGS = 4
LIGHT = pl.CostEstimate(flops=1024, bytes_accessed=1024, transcendentals=0)
VMEM_LIMIT = 48 * 1024 * 1024
LOG2E = 1.4426950408889634

epsilon = 1e-05
f32 = jnp.float32
bf16 = jnp.bfloat16


def own_columns(array, core):
    chips = lax.axis_size("chip")
    width = array.shape[-1] // (2 * chips)
    parted = array.reshape(array.shape[:-1] + (chips, 2, width))
    picked = lax.dynamic_index_in_dim(parted, core, axis=parted.ndim - 2, keepdims=False)
    return picked.reshape(array.shape[:-1] + (chips * width,))


def to_partner(array):
    return lax.ppermute(array, "core", [(0, 1), (1, 0)])


def in_core_order(mine, theirs, core, axis):
    first = jnp.where(core == 0, mine, theirs)
    second = jnp.where(core == 0, theirs, mine)
    return jnp.stack([first, second], axis=axis)


def chip_dims():
    return (lax.axis_size("chip") // 2, 2, lax.axis_size("seg"))


def chip_place():
    chip = lax.axis_index("chip")
    return (chip // 2, chip % 2, lax.axis_index("seg"))


def moved(array, dim, by):
    sizes = chip_dims()
    index = lambda at: (at[0] * sizes[1] + at[1]) * sizes[2] + at[2]
    pairs = []
    for a in range(sizes[0]):
        for b in range(sizes[1]):
            for z in range(sizes[2]):
                to = [a, b, z]
                to[dim] = (to[dim] + by) % sizes[dim]
                pairs.append((index((a, b, z)), index(to)))
    return lax.ppermute(array, ("chip", "seg"), pairs)


def tie(*values):
    return lax.optimization_barrier(values)


def gather_step(data, dim):
    return [data] + [moved(data, dim, by) for by in range(1, chip_dims()[dim])]


def exchanged(array, by):
    line = lax.axis_size("seg")
    return lax.ppermute(array, "seg", [(at, at ^ by) for at in range(line)])


def plane_steps():
    a, b, _ = chip_dims()
    steps = [(at // b, at % b) for at in range(1, a * b)]
    return sorted(steps, key=lambda by: bool(by[0] and by[1]))


def near_steps():
    a, b, _ = chip_dims()
    return plane_steps()[: a + b - 2]


def far_steps():
    a, b, _ = chip_dims()
    return plane_steps()[a + b - 2 :]


def moved_plane(array, by_a, by_b):
    a, b, z = chip_dims()
    pairs = [
        ((at_a * b + at_b) * z + at_z, ((at_a + by_a) % a * b + (at_b + by_b) % b) * z + at_z)
        for at_a in range(a)
        for at_b in range(b)
        for at_z in range(z)
    ]
    return lax.ppermute(array, ("chip", "seg"), pairs)


def gather_plane(data, steps):
    return [moved_plane(data, *by) for by in steps]


def placed_kernel(plan, place_ref, *refs):
    sources, target, sems = refs[:-2], refs[-2], refs[-1]
    copies = []
    for source, lead, at, paired in plan:
        spot = [lax.rem(place_ref[dim] + (size - back), size) for dim, (back, size) in enumerate(at)]
        spot.append(place_ref[2 + lead])
        to = target.at[spot[0], spot[1], :, spot[2]] if paired else target.at[spot[0], spot[1], spot[2]]
        copies.append(pltpu.make_async_copy(sources[source].at[lead], to, sems.at[len(copies)]))
    for copy in copies:
        copy.start()
    for copy in copies:
        copy.wait()


def whole_matrix(gathered, paired, by_bits=False):
    a, b, z = chip_dims()
    at_a, at_b, at_z = chip_place()
    spots = [at_z ^ back if by_bits else (at_z + z - back) % z for back in range(z)]
    plan = [
        (source, back, ((by[0], a), (by[1], b)), paired)
        for source, by in enumerate([(0, 0)] + plane_steps())
        for back in range(z)
    ]
    block = gathered[0].shape[1:]
    shape = (a, b, 2, z) + block[1:] if paired else (a, b, z) + block
    anywhere = pl.BlockSpec(memory_space=pl.ANY)
    whole = pl.pallas_call(
        lambda *refs: placed_kernel(plan, *refs),
        out_shape=jax.ShapeDtypeStruct(shape, bf16),
        in_specs=[pl.BlockSpec(memory_space=pltpu.SMEM)] + [anywhere] * len(gathered),
        out_specs=pl.BlockSpec(memory_space=pltpu.VMEM),
        scratch_shapes=[pltpu.SemaphoreType.DMA((len(plan),))],
        compiler_params=pltpu.CompilerParams(vmem_limit_bytes=VMEM_LIMIT),
        cost_estimate=LIGHT,
    )(jnp.stack([at_a, at_b, *spots]).astype(jnp.int32), *gathered)
    return whole.reshape(-1, shape[-1])


def total(terms):
    result = terms[0].astype(f32)
    for term in terms[1:]:
        result = result + term.astype(f32)
    return result


def reduce_send(terms, axis, dim, wire):
    place, size = chip_place()[dim], chip_dims()[dim]
    pick = lambda at: [lax.dynamic_index_in_dim(term, at, axis=axis, keepdims=False) for term in terms]
    received = [moved(total(pick((place + by) % size)).astype(wire), dim, by) for by in range(1, size)]
    return pick(place), received


def plane_part(partials, by_a, by_b):
    (at_a, at_b, _), (a, b, _) = chip_place(), chip_dims()
    chip = (at_a + by_a) % a * b + (at_b + by_b) % b
    flat = [partial.reshape((a * b,) + partial.shape[2:]) for partial in partials]
    return jnp.concatenate([lax.dynamic_index_in_dim(array, chip, axis=0, keepdims=False) for array in flat], axis=-1)


def reduce_plane(partials, steps):
    return [moved_plane(plane_part(partials, *by), *by) for by in steps]


def reduce_z(firsts):
    joined = jnp.concatenate([total(kept + received) for kept, received in firsts], axis=-1)
    return [reduce_send([joined], 0, 2, bf16)]


def reduce_end(third):
    return total(third[0][0] + third[0][1])


def arrivals(parts):
    return [received for _, received in parts]


def arrived(parts, received):
    return [(kept, new) for (kept, _), new in zip(parts, received)]


def line_perm(turn, back):
    line = lax.axis_size("seg")
    parts = line // SEGS
    pairs = []
    for core in range(2):
        for place in range(line):
            half, odd = divmod(place % SEGS, 2)
            source = core * line + place
            target = odd * line + (2 * core + (half ^ turn)) * parts + place // SEGS
            pairs.append((target, source) if back else (source, target))
    return pairs


def swapped(pair, turn):
    return [jnp.where(turn == 0, pair[0], pair[1]), jnp.where(turn == 0, pair[1], pair[0])]


def send_sequence(array, place):
    pieces = swapped([array[0], array[1]], (place % SEGS) // 2)
    return [lax.ppermute(piece, ("core", "seg"), line_perm(turn, False)) for turn, piece in enumerate(pieces)]


def order_sequence(got, place):
    parts = lax.axis_size("seg") // SEGS
    return jnp.stack(swapped(got, (place // parts) % 2))


def send_back(ordered, place):
    parts = lax.axis_size("seg") // SEGS
    pieces = swapped([ordered[0], ordered[1]], (place // parts) % 2)
    return [lax.ppermute(piece, ("core", "seg"), line_perm(turn, True)) for turn, piece in enumerate(pieces)]


def order_back(got, place):
    return jnp.stack(swapped(got, (place % SEGS) // 2))


def part_pairs(step):
    line = lax.axis_size("seg")
    parts = line // SEGS
    return [(i, i + step) for i in range(line) if 0 <= i + step < line and i // parts == (i + step) // parts]


def entering(decay, state, step):
    parts = lax.axis_size("seg") // SEGS
    total = jnp.zeros_like(state)
    for _ in range(parts - 1):
        total = lax.ppermute(decay * total + state, "seg", part_pairs(step))
    return total


def borrowed(array, step):
    parts = lax.axis_size("seg") // SEGS
    if parts == 1:
        return jnp.zeros_like(array)
    return lax.ppermute(array, "seg", part_pairs(step))


def spilled(grad, edge, taps):
    if lax.axis_size("seg") == SEGS:
        return grad
    edge = borrowed(edge, -1)
    spill = jnp.stack(
        [
            sum(taps[k] * edge[CONV - 1 - k - early] for k in range(CONV - early))
            for early in range(CONV - 1, 0, -1)
        ]
    )
    at = grad.shape[0] - CONV + 1
    return grad.at[at:].set((grad[at:].astype(f32) + spill).astype(bf16))


def dot(a, b, contract):
    return lax.dot_general(a, b, (contract, ((), ())), preferred_element_type=f32)


def normed_kernel(slabs, core_ref, mine_ref, other_ref, gain_ref, normed_ref, turned_ref):
    own = lax.rem(pl.program_id(0), 2) == core_ref[0]
    hidden = jnp.where(own, mine_ref[0], other_ref[0]).astype(f32)
    scale = lax.rsqrt(jnp.mean(hidden * hidden, axis=1, keepdims=True) + epsilon)
    normed = hidden * scale * gain_ref[...]
    normed_ref[...] = normed.astype(bf16)
    turned = normed.T.astype(bf16)
    for to, at, size in slabs:
        turned_ref[to : to + size] = turned[at : at + size]


def normed_tokens(core, mine, other, gain, rows):
    segs, seg_len, width = 2 * mine.shape[0], mine.shape[1], mine.shape[2]
    a, b, z = chip_dims()
    group = 2 * z * rows
    inside = rows % 16 == 0
    slabs = [(0, 0, width)]
    if inside:
        slabs = [
            (chip * group + (at * 2 + core_at) * rows, chip * group + (core_at * z + at) * rows, rows)
            for chip in range(a * b)
            for core_at in range(2)
            for at in range(z)
        ]
    normed, turned = pl.pallas_call(
        lambda *refs: normed_kernel(slabs, *refs),
        grid_spec=pltpu.PrefetchScalarGridSpec(
            num_scalar_prefetch=1,
            grid=(segs,),
            in_specs=[
                pl.BlockSpec((1, seg_len, width), lambda i, core: (i // 2, 0, 0)),
                pl.BlockSpec((1, seg_len, width), lambda i, core: (i // 2, 0, 0)),
                pl.BlockSpec((1, width), lambda i, core: (0, 0)),
            ],
            out_specs=(
                pl.BlockSpec((seg_len, width), lambda i, core: (i, 0)),
                pl.BlockSpec((width, seg_len), lambda i, core: (0, i)),
            ),
        ),
        out_shape=(
            jax.ShapeDtypeStruct((segs * seg_len, width), bf16),
            jax.ShapeDtypeStruct((width, segs * seg_len), bf16),
        ),
        compiler_params=pltpu.CompilerParams(dimension_semantics=("arbitrary",), vmem_limit_bytes=VMEM_LIMIT),
        cost_estimate=LIGHT,
    )(core.reshape(1).astype(jnp.int32), mine, other, gain.reshape(1, width))
    if not inside:
        turned = turned.reshape(a, b, 2, z, rows, -1).transpose(0, 1, 3, 2, 4, 5).reshape(turned.shape)
    return normed, turned


def mixed_kernel(gated_ref, scale_ref, gain_ref, mixed_ref, turned_ref):
    mixed = gated_ref[...] * scale_ref[...] * gain_ref[...]
    mixed_ref[...] = mixed.astype(bf16)
    turned_ref[...] = mixed.T.astype(bf16)


def mixed_tokens(gated, scale, gain, seg_len):
    length, width = gated.shape
    return pl.pallas_call(
        mixed_kernel,
        grid=(length // seg_len,),
        in_specs=[
            pl.BlockSpec((seg_len, width), lambda i: (i, 0)),
            pl.BlockSpec((seg_len, 1), lambda i: (i, 0)),
            pl.BlockSpec((1, width), lambda i: (0, 0)),
        ],
        out_specs=(
            pl.BlockSpec((seg_len, width), lambda i: (i, 0)),
            pl.BlockSpec((width, seg_len), lambda i: (0, i)),
        ),
        out_shape=(
            jax.ShapeDtypeStruct((length, width), bf16),
            jax.ShapeDtypeStruct((width, length), bf16),
        ),
        compiler_params=pltpu.CompilerParams(dimension_semantics=("arbitrary",), vmem_limit_bytes=VMEM_LIMIT),
        cost_estimate=LIGHT,
    )(gated, scale, gain.reshape(1, width))


def columns_of(pair):
    return pl.ds(pair * LANES, LANES)


def low_half(shape):
    return lax.broadcasted_iota(jnp.int32, shape, len(shape) - 1) < HEADDIM


def pair_columns(array, pair, low):
    rows = array.shape[0]
    first = jnp.broadcast_to(array[:, 2 * pair : 2 * pair + 1], (rows, LANES))
    second = jnp.broadcast_to(array[:, 2 * pair + 1 : 2 * pair + 2], (rows, LANES))
    return jnp.where(low, first, second)


def conv_parts(current, before, taps):
    rows = current.shape[0]
    padded = jnp.concatenate([before, current], axis=0)
    seen = [padded[8 - CONV + 1 + k : 8 - CONV + 1 + k + rows] for k in range(CONV - 1)] + [current]
    total = taps[CONV : CONV + 1]
    for k in range(CONV):
        total = total + taps[k : k + 1] * seen[k]
    return total, seen


def exact_sums(chosen, array):
    chosen = jnp.where(chosen, 1.0, 0.0).astype(bf16)
    result = 0.0
    for _ in range(3):
        part = array.astype(bf16)
        array = array - part.astype(f32)
        result = result + dot(chosen, part, ((1,), (0,)))
    return result


def step_terms(raw, head, seg_len):
    shifted = raw + head[1:2]
    step = jnp.maximum(shifted, 0.0) + jnp.log1p(jnp.exp(-jnp.abs(shifted)))
    log_decay = step * head[0:1]
    at_or_before = lax.broadcasted_iota(jnp.int32, (seg_len, seg_len), 0) >= lax.broadcasted_iota(
        jnp.int32, (seg_len, seg_len), 1
    )
    sums = exact_sums(at_or_before, log_decay)
    return shifted, step, log_decay, sums * LOG2E


def forward_kernel(
    proj_ref, taps_ref, head_ref, skip_ref, rim_ref, init_ref,
    values_ref, prior_ref, final_ref, last_ref, state_ref, tail_ref,
):
    seg_len = proj_ref.shape[0]
    half = seg_len // 2

    @pl.when(pl.program_id(0) == 0)
    def _():
        state_ref[...] = init_ref[...]
        tail_ref[...] = rim_ref[...]

    def activated(begin):
        at = pl.ds(begin, LANES)
        total, _ = conv_parts(proj_ref[:, at], tail_ref[:, at], taps_ref[:, at])
        return total * jax.nn.sigmoid(total)

    b_values = activated(HALF)
    b_low, b_turned = b_values.astype(bf16), b_values.T.astype(bf16)
    c_low = activated(HALF + STATE).astype(bf16)
    _, step, _, sums = step_terms(proj_ref[:, HALF + 2 * STATE :], head_ref, seg_len)
    sums_turned, step_turned = sums.T, step.T
    scores = dot(c_low, b_low, ((1,), (1,)))
    kept = lax.broadcasted_iota(jnp.int32, (half, half), 0) >= lax.broadcasted_iota(jnp.int32, (half, half), 1)
    first_scores = jnp.where(kept, scores[:half, :half], 0.0)
    later_scores = scores[half:, :half]
    second_scores = jnp.where(kept, scores[half:, half:], 0.0)
    low = low_half((seg_len, LANES))
    last_ref[...] = jnp.broadcast_to(sums[seg_len - 1 :], last_ref.shape)

    for pair in range(HEADS // 4):
        at = columns_of(pair)
        x_values = activated(pair * LANES)
        x_low = x_values.astype(bf16)
        sums_pair = pair_columns(sums, pair, low)
        last_pair = sums_pair[seg_len - 1 :]
        carry = jnp.exp2(last_pair - sums_pair) * pair_columns(step, pair, low)
        scaled_x = (carry * x_low.astype(f32)).astype(bf16)
        prior = state_ref[:, at]
        prior_low = prior.astype(bf16)
        prior_ref[0, :, at] = prior_low
        from_state = jnp.exp2(sums_pair) * dot(c_low, prior_low, ((1,), (0,)))
        state_ref[:, at] = jnp.exp2(last_pair) * prior + dot(b_turned, scaled_x, ((1,), (0,)))
        early, late = 0.0, 0.0
        for side in range(2):
            head = 2 * pair + side
            x_side = jnp.where(low if side == 0 else ~low, x_values, 0.0).astype(bf16)
            at_token = jnp.broadcast_to(sums[:, head : head + 1], (seg_len, half))
            at_source, source_step = sums_turned[head : head + 1], step_turned[head : head + 1]
            first = jnp.exp2(jnp.minimum(at_token[:half] - at_source[:, :half], 0.0)) * first_scores
            first = (first * source_step[:, :half]).astype(bf16)
            later = jnp.exp2(at_token[half:] - at_source[:, :half]) * later_scores
            later = (later * source_step[:, :half]).astype(bf16)
            second = jnp.exp2(jnp.minimum(at_token[half:] - at_source[:, half:], 0.0)) * second_scores
            second = (second * source_step[:, half:]).astype(bf16)
            early = early + dot(first, x_side[:half], ((1,), (0,)))
            late = late + dot(jnp.concatenate([later, second], axis=1), x_side, ((1,), (0,)))
        intra = jnp.concatenate([early, late], axis=0)
        values_ref[:, at] = intra + from_state + skip_ref[:, at] * x_values

    tail_ref[...] = proj_ref[seg_len - 8 :, : HALF + 2 * STATE]
    final_ref[...] = state_ref[...]


def full_block(shape):
    return pl.BlockSpec(shape, lambda *_: (0,) * len(shape))


def scan_forward(proj, taps, head, skip, rim, init, seg_len):
    segs = proj.shape[0] // seg_len
    wide = HALF + 2 * STATE
    return pl.pallas_call(
        forward_kernel,
        grid=(segs,),
        out_shape=(
            jax.ShapeDtypeStruct((proj.shape[0], HALF), f32),
            jax.ShapeDtypeStruct((segs, STATE, HALF), bf16),
            jax.ShapeDtypeStruct((STATE, HALF), f32),
            jax.ShapeDtypeStruct((segs * 8, LANES), f32),
        ),
        in_specs=[
            pl.BlockSpec((seg_len, proj.shape[1]), lambda i: (i, 0)),
            full_block((8, wide)),
            full_block((8, LANES)),
            full_block((1, HALF)),
            full_block((8, wide)),
            full_block((STATE, HALF)),
        ],
        out_specs=(
            pl.BlockSpec((seg_len, HALF), lambda i: (i, 0)),
            pl.BlockSpec((1, STATE, HALF), lambda i: (i, 0, 0)),
            full_block((STATE, HALF)),
            pl.BlockSpec((8, LANES), lambda i: (i, 0)),
        ),
        scratch_shapes=[pltpu.VMEM((STATE, HALF), f32), pltpu.VMEM((8, wide), f32)],
        compiler_params=pltpu.CompilerParams(
            dimension_semantics=("arbitrary",), vmem_limit_bytes=VMEM_LIMIT
        ),
        cost_estimate=LIGHT,
    )(proj, taps, head, skip, rim, init)


def split_dot(array, other):
    high = array.astype(bf16)
    rest = (array - high.astype(f32)).astype(bf16)
    return dot(high, other, ((1,), (0,))) + dot(rest, other, ((1,), (0,)))


def backward_kernel(
    group, proj_ref, before_ref, taps_ref, rim_ref, shared_ref, shared_before_ref, shared_taps_ref, shared_rim_ref,
    head_ref, skip_ref, end_ref, prior_ref, values_ref, grad_ref, core_ref,
    grad_x_ref, mine_ref, theirs_ref, grad_raw_ref, taps_grad_ref, skip_grad_ref, head_grad_ref, edge_ref, start_ref,
    later_ref, local_ref, scaled_ref, grad_state_ref, inner_ref, source_ref, carry_ref, decay_ref,
):
    seg_len = proj_ref.shape[0]
    half = seg_len // 2
    turn = pl.program_id(0)

    @pl.when(turn == 0)
    def _():
        later_ref[...] = end_ref[...]
        edge_ref[...] = jnp.zeros_like(edge_ref)
        taps_grad_ref[...] = jnp.zeros_like(taps_grad_ref)
        skip_grad_ref[...] = jnp.zeros_like(skip_grad_ref)
        head_grad_ref[...] = jnp.zeros_like(head_grad_ref)

    first_segment = turn == pl.num_programs(0) - 1

    def conv_at(at, current, ahead, taps, rim):
        before = jnp.where(first_segment, rim[:, at], ahead[:, at])
        return conv_parts(current[:, at], before, taps[:, at])

    def activated(begin):
        total, _ = conv_at(pl.ds(begin, LANES), shared_ref, shared_before_ref, shared_taps_ref, shared_rim_ref)
        return total * jax.nn.sigmoid(total)

    b_values = activated(0)
    c_values = activated(STATE)
    b_low, c_low, c_turned = b_values.astype(bf16), c_values.astype(bf16), c_values.T.astype(bf16)
    shifted, step, log_decay, sums = step_terms(shared_ref[:, 2 * STATE :], head_ref, seg_len)
    sums_turned = sums.T
    scores = dot(b_low, c_low, ((1,), (1,)))
    kept = lax.broadcasted_iota(jnp.int32, (half, half), 0) <= lax.broadcasted_iota(jnp.int32, (half, half), 1)
    first_scores = jnp.where(kept, scores[:half, :half], 0.0)
    later_scores = scores[:half, half:]
    second_scores = jnp.where(kept, scores[half:, half:], 0.0)
    low = low_half((seg_len, LANES))
    first_grad, later_grad, second_grad = 0.0, 0.0, 0.0

    pairs = grad_ref.shape[1] // LANES
    for pair in range(pairs):
        at = columns_of(pair)
        total, seen = conv_at(at, proj_ref, before_ref, taps_ref, rim_ref)
        sigmoid = jax.nn.sigmoid(total)
        x_values = total * sigmoid
        x_low = x_values.astype(bf16)
        x_wide = x_low.astype(f32)
        sums_pair = pair_columns(sums, group * pairs + pair, low)
        step_pair = pair_columns(step, group * pairs + pair, low)
        last_pair = sums_pair[seg_len - 1 :]
        gap = jnp.exp2(last_pair - sums_pair)
        scaled_ref[:, at] = (gap * step_pair * x_wide).astype(bf16)
        grad_values = grad_ref[:, at]
        grad_state_ref[:, at] = (grad_values * jnp.exp2(sums_pair)).astype(bf16)
        later = later_ref[:, at]
        later_low = later.astype(bf16)
        local_ref[:, at] = later_low
        prior = prior_ref[0, :, at]
        decay_ref[:, at] = jnp.broadcast_to(
            jnp.sum(later * prior.astype(f32), axis=0, keepdims=True), (8, LANES)
        )
        grad_prior = dot(c_turned, grad_state_ref[:, at], ((1,), (0,)))
        later_ref[:, at] = jnp.exp2(last_pair) * later + grad_prior
        grad_scaled = dot(b_low, later_low, ((1,), (0,)))
        stepped = (step_pair * x_wide).astype(bf16)
        early, late = 0.0, 0.0
        for side in range(2):
            head = 2 * (group * pairs + pair) + side
            grad_low = jnp.where(low if side == 0 else ~low, grad_values, 0.0).astype(bf16)
            at_source = jnp.broadcast_to(sums[:, head : head + 1], (seg_len, half))
            at_token = sums_turned[head : head + 1]
            upper_weights = dot(stepped[:half], grad_low, ((1,), (1,)))
            lower_weights = dot(stepped[half:], grad_low[half:], ((1,), (1,)))
            first = jnp.exp2(jnp.minimum(at_token[:, :half] - at_source[:half], 0.0))
            after = jnp.exp2(at_token[:, half:] - at_source[:half])
            second = jnp.exp2(jnp.minimum(at_token[:, half:] - at_source[half:], 0.0))
            first_grad = first_grad + first * upper_weights[:, :half]
            later_grad = later_grad + after * upper_weights[:, half:]
            second_grad = second_grad + second * lower_weights
            upper = jnp.concatenate([first * first_scores, after * later_scores], axis=1).astype(bf16)
            early = early + dot(upper, grad_low, ((1,), (0,)))
            late = late + dot((second * second_scores).astype(bf16), grad_low[half:], ((1,), (0,)))
        inner = jnp.concatenate([early, late], axis=0)
        skip = skip_ref[:, at]
        skip_grad_ref[:, at] += jnp.sum(grad_values * x_values, axis=0, keepdims=True)
        inner_ref[:, at] = grad_values * (values_ref[:, at] - skip * x_values)
        source_ref[:, at] = x_wide * inner
        carry_ref[:, at] = x_wide * grad_scaled
        grad_x = skip * grad_values + step_pair * (inner + gap * grad_scaled)
        grad_total = grad_x * (sigmoid * (1.0 + total * (1.0 - sigmoid)))
        for k in range(CONV):
            taps_grad_ref[k : k + 1, at] += jnp.sum(grad_total * seen[k], axis=0, keepdims=True)
        taps_grad_ref[CONV : CONV + 1, at] += jnp.sum(grad_total, axis=0, keepdims=True)
        extended = jnp.concatenate([grad_total, edge_ref[:, at]], axis=0)
        edge_ref[:, at] = grad_total[:8]
        taps = taps_ref[:, at]
        grad_conv = taps[CONV - 1 : CONV] * grad_total
        for k in range(CONV - 1):
            grad_conv = grad_conv + taps[k : k + 1] * extended[CONV - 1 - k : CONV - 1 - k + seg_len]
        grad_x_ref[:, at] = grad_conv.astype(bf16)

    width = grad_ref.shape[1]
    channel = lax.broadcasted_iota(jnp.int32, (width, LANES), 0) // HEADDIM + group * width // HEADDIM
    heads = jnp.where(channel == lax.broadcasted_iota(jnp.int32, (width, LANES), 1), 1.0, 0.0).astype(bf16)
    tail = jnp.exp2(sums[seg_len - 1 :] - sums)
    source_grad = split_dot(source_ref[...], heads)
    step_grad = source_grad + tail * split_dot(carry_ref[...], heads)
    used = step * step_grad
    sum_grad = split_dot(inner_ref[...], heads) - used
    at_last = jnp.sum(used - step * source_grad, axis=0, keepdims=True)
    at_last = at_last + split_dot(decay_ref[...], heads)[:1] * jnp.exp2(sums[seg_len - 1 :])
    is_last = lax.broadcasted_iota(jnp.int32, (seg_len, LANES), 0) == seg_len - 1
    sum_grad = sum_grad + jnp.where(is_last, at_last, 0.0)
    at_or_after = lax.broadcasted_iota(jnp.int32, (seg_len, seg_len), 0) <= lax.broadcasted_iota(
        jnp.int32, (seg_len, seg_len), 1
    )
    log_grad = exact_sums(at_or_after, sum_grad)
    grad_raw = (step_grad + head_ref[0:1] * log_grad) * jax.nn.sigmoid(shifted)
    grad_raw_ref[...] = grad_raw
    head_grad_ref[CONV + 1 : CONV + 2] += jnp.sum(log_grad * log_decay, axis=0, keepdims=True)
    head_grad_ref[CONV + 2 : CONV + 3] += jnp.sum(grad_raw, axis=0, keepdims=True)

    first_low = jnp.where(kept, first_grad, 0.0)
    second_low = jnp.where(kept, second_grad, 0.0)
    grad_scores = jnp.concatenate(
        [
            jnp.concatenate([first_low, later_grad], axis=1),
            jnp.concatenate([jnp.zeros_like(first_low), second_low], axis=1),
        ],
        axis=0,
    )
    start_ref[...] = later_ref[...]
    grad_b = dot(scaled_ref[...], local_ref[...], ((1,), (1,))) + dot(
        grad_scores.astype(bf16), c_low, ((1,), (0,))
    )
    grad_c = dot(grad_state_ref[...], prior_ref[0], ((1,), (1,))) + dot(
        grad_scores.T.astype(bf16), b_low, ((1,), (0,))
    )
    first = core_ref[0] == 0
    mine_ref[...] = jnp.where(first, grad_b, grad_c)
    theirs_ref[...] = jnp.where(first, grad_c, grad_b)


GROUPS = 1


def scan_backward(group, core, proj, taps, head, skip, rim, end, prior, values, grad_values, seg_len):
    length = proj.shape[0]
    segs = length // seg_len
    width, shared = HALF // GROUPS, proj.shape[1] - HALF
    back = lambda width, at=0: pl.BlockSpec((seg_len, width), lambda i: (segs - 1 - i, at))
    row_ahead = lambda i: jnp.maximum((segs - 1 - i) * (seg_len // 8) - 1, 0)
    ahead = lambda width, at: pl.BlockSpec((8, width), lambda i: (row_ahead(i), at))
    column = lambda rows, width, at: pl.BlockSpec((rows, width), lambda i: (0, at))
    both = HALF // shared
    return pl.pallas_call(
        lambda *refs: backward_kernel(group, *refs),
        grid=(segs,),
        out_shape=(
            jax.ShapeDtypeStruct((length, width), bf16),
            jax.ShapeDtypeStruct((length, STATE), f32),
            jax.ShapeDtypeStruct((length, STATE), f32),
            jax.ShapeDtypeStruct((length, LANES), f32),
            jax.ShapeDtypeStruct((8, width), f32),
            jax.ShapeDtypeStruct((1, width), f32),
            jax.ShapeDtypeStruct((8, LANES), f32),
            jax.ShapeDtypeStruct((8, width), f32),
            jax.ShapeDtypeStruct((STATE, width), f32),
        ),
        in_specs=[
            back(width, group),
            ahead(width, group),
            column(8, width, group),
            column(8, width, group),
            back(shared, both),
            ahead(shared, both),
            column(8, shared, both),
            column(8, shared, both),
            full_block((8, LANES)),
            column(1, width, group),
            column(STATE, width, group),
            pl.BlockSpec((1, STATE, width), lambda i: (segs - 1 - i, 0, group)),
            back(width, group),
            back(width, group),
            pl.BlockSpec(memory_space=pltpu.SMEM),
        ],
        out_specs=(
            back(width),
            back(STATE),
            back(STATE),
            back(LANES),
            full_block((8, width)),
            full_block((1, width)),
            full_block((8, LANES)),
            full_block((8, width)),
            full_block((STATE, width)),
        ),
        scratch_shapes=[
            pltpu.VMEM((STATE, width), f32),
            pltpu.VMEM((STATE, width), bf16),
            pltpu.VMEM((seg_len, width), bf16),
            pltpu.VMEM((seg_len, width), bf16),
            pltpu.VMEM((seg_len, width), f32),
            pltpu.VMEM((seg_len, width), f32),
            pltpu.VMEM((seg_len, width), f32),
            pltpu.VMEM((8, width), f32),
        ],
        compiler_params=pltpu.CompilerParams(
            dimension_semantics=("arbitrary",), vmem_limit_bytes=VMEM_LIMIT
        ),
        cost_estimate=LIGHT,
    )(
        proj, proj, taps, rim, proj, proj, taps, rim, head, skip, end, prior, values, grad_values,
        core.reshape(1).astype(jnp.int32),
    )


def half_kernel(transposed, count, core_ref, *refs):
    inputs, mine_ref, theirs_ref = refs[: 2 * count], refs[-2], refs[-1]
    total = refs[2 * count][...] if len(refs) > 2 * count + 2 else 0.0
    for left, right in zip(inputs[:count], inputs[count:]):
        total = total + dot(left[...], right[...], ((1,), (1 if transposed else 0,)))
    own = lax.rem(pl.program_id(0), 2) == core_ref[0]

    @pl.when(own)
    def _():
        mine_ref[0] = total

    @pl.when(jnp.logical_not(own))
    def _():
        theirs_ref[0] = total.astype(bf16)


def half_products(core, terms, seg_len, width, transposed, base=()):
    length = terms[0][0].shape[0]
    left = [pl.BlockSpec((seg_len, array.shape[1]), lambda i, core: (i, 0)) for array, _, _ in terms]
    right = []
    for array, matrix, at in terms:
        if transposed:
            right.append(pl.BlockSpec((width, array.shape[1]), lambda i, core, at=at: (0, at(core[0]))))
        else:
            right.append(pl.BlockSpec(matrix.shape, lambda i, core: (0, 0)))
    depth = sum(array.shape[1] for array, _, _ in terms)
    mine, theirs = pl.pallas_call(
        lambda *refs: half_kernel(transposed, len(terms), *refs),
        grid_spec=pltpu.PrefetchScalarGridSpec(
            num_scalar_prefetch=1,
            grid=(length // seg_len,),
            in_specs=left + right + [pl.BlockSpec((seg_len, width), lambda i, core: (i, 0)) for _ in base],
            out_specs=[pl.BlockSpec((1, seg_len, width), lambda i, core: (i // 2, 0, 0))] * 2,
        ),
        out_shape=(
            jax.ShapeDtypeStruct((length // seg_len // 2, seg_len, width), f32),
            jax.ShapeDtypeStruct((length // seg_len // 2, seg_len, width), bf16),
        ),
        compiler_params=pltpu.CompilerParams(dimension_semantics=("arbitrary",), vmem_limit_bytes=VMEM_LIMIT),
        cost_estimate=LIGHT,
    )(core.reshape(1).astype(jnp.int32), *[array for array, _, _ in terms], *[matrix for _, matrix, _ in terms], *base)
    return mine, theirs


def shared_kernel(core_ref, proj_ref, rim_ref, taps_ref, mine_ref, other_ref, grad_ref, taps_grad_ref, edge_ref):
    total, seen = conv_parts(proj_ref[...], rim_ref[...], taps_ref[...])
    sigmoid = jax.nn.sigmoid(total)
    grad_total = mine_ref[...] + other_ref[...]
    grad_total = grad_total * (sigmoid * (1.0 + total * (1.0 - sigmoid)))
    sums = [jnp.sum(grad_total * part, axis=0, keepdims=True) for part in seen]
    sums = sums + [jnp.sum(grad_total, axis=0, keepdims=True), jnp.zeros((8 - CONV - 1, LANES), f32)]
    taps_grad_ref[...] = jnp.concatenate(sums, axis=0)
    edge_ref[...] = grad_total[:8]
    taps = taps_ref[...]
    extended = jnp.concatenate([grad_total, jnp.zeros((8, LANES), f32)], axis=0)
    grad_conv = taps[CONV - 1 : CONV] * grad_total
    for k in range(CONV - 1):
        grad_conv = grad_conv + taps[k : k + 1] * extended[CONV - 1 - k : CONV - 1 - k + grad_total.shape[0]]
    grad_ref[...] = grad_conv.astype(bf16)


def shared_backward(core, proj, rim, taps, mine, other):
    length = proj.shape[0]
    picked = lambda rows: pl.BlockSpec((rows, LANES), lambda i, core: (0, HALF // LANES + core[0]))
    whole = lambda rows: pl.BlockSpec((rows, LANES), lambda i, core: (0, 0))
    return pl.pallas_call(
        shared_kernel,
        grid_spec=pltpu.PrefetchScalarGridSpec(
            num_scalar_prefetch=1,
            grid=(1,),
            in_specs=[picked(length), picked(8), picked(8), whole(length), whole(length)],
            out_specs=(whole(length), whole(8), whole(8)),
        ),
        out_shape=(
            jax.ShapeDtypeStruct((length, LANES), bf16),
            jax.ShapeDtypeStruct((8, LANES), f32),
            jax.ShapeDtypeStruct((8, LANES), f32),
        ),
        compiler_params=pltpu.CompilerParams(vmem_limit_bytes=VMEM_LIMIT),
        cost_estimate=LIGHT,
    )(core.reshape(1).astype(jnp.int32), proj, rim, taps, mine, other)


def per_device(hidden_in, cotangent, in_proj, out_proj, conv_params, pre_gain, gated_gain, head_params):
    chips, line = lax.axis_size("chip"), lax.axis_size("seg")
    core, place = lax.axis_index("core"), lax.axis_index("seg")
    rows, model_width = in_proj.shape[0], hidden_in.shape[2]
    heads = HEADS // 2

    conv_width, gain_width = conv_params.shape[1], gated_gain.shape[0]
    used = HALF + 2 * STATE + heads
    spare = -used % LANES
    small = jnp.zeros((rows, spare), bf16)
    small = small.at[: CONV + 1, :conv_width].set(conv_params)
    small = small.at[CONV + 1, :rows].set(pre_gain)
    small = small.at[CONV + 2, :gain_width].set(gated_gain)

    def conv_side(which):
        return jnp.concatenate(
            [
                own_columns(in_proj[:, INNER : 2 * INNER], which),
                in_proj[:, 2 * INNER : INNER + XBC],
                own_columns(in_proj[:, INNER + XBC :], which),
                small,
            ],
            axis=1,
        )

    def gate_side(which):
        return own_columns(in_proj[:, :INNER], which)

    conv_swap = to_partner(conv_side(1 - core))
    conv_block = in_core_order(conv_side(core), conv_swap, core, 0)
    conv_z = gather_step(conv_block, 2)
    gate_swap = to_partner(gate_side(1 - core))
    gate_block = in_core_order(gate_side(core), gate_swap, core, 0)
    conv_z, hidden_in, gate_block = tie(conv_z, hidden_in, gate_block)
    conv_own = jnp.stack(conv_z)
    conv_near = gather_plane(conv_own, near_steps())
    hidden_got = send_sequence(hidden_in, place)
    conv_own, conv_near, hidden_got, gate_block = tie(conv_own, conv_near, hidden_got, gate_block)
    hidden_half = order_sequence(hidden_got, place)
    conv_far = gather_plane(conv_own, far_steps())
    gate_z = gather_step(gate_block, 2)
    hidden_other = to_partner(hidden_half)
    conv_far, gate_z, hidden_other, out_proj = tie(conv_far, gate_z, hidden_other, out_proj)
    out_own = out_proj[None]
    out_other = exchanged(out_own, 1)
    gate_own = jnp.stack(gate_z)
    gate_near = gather_plane(gate_own, near_steps())
    conv_all = whole_matrix([conv_own, *conv_near, *conv_far], True)

    small_all = conv_all.reshape(chips, 2, line, rows, -1)[..., used:].astype(f32)
    taps_full = small_all[..., : CONV + 1, :conv_width].transpose(3, 0, 1, 2, 4).reshape(CONV + 1, XBC)
    taps = jnp.concatenate([own_columns(taps_full[:, :INNER], core), taps_full[:, INNER:]], axis=1)
    gain_pre = small_all[..., CONV + 1, :rows].reshape(model_width)
    gain_gate = lax.dynamic_index_in_dim(
        small_all[..., CONV + 2, :gain_width], core, axis=1, keepdims=False
    ).reshape(HALF)
    params = own_columns(head_params, core)

    seg_len = hidden_half.shape[1]
    tokens = SEGS * seg_len
    normed, normed_turned = normed_tokens(core, hidden_half, hidden_other, gain_pre, rows)
    projected = dot(normed, conv_all, ((1,), (0,)))
    projected, gate_own, gate_near, out_own, out_other = tie(projected, gate_own, gate_near, out_own, out_other)
    gate_far = gather_plane(gate_own, far_steps())
    out_own = jnp.concatenate([out_own, out_other])
    out_others = []
    for bit in range(1, (line - 1).bit_length()):
        out_others.append(exchanged(out_own, 2**bit))
        if 2 ** (bit + 1) < line:
            out_own, out_others = jnp.concatenate([out_own, out_others[-1]]), []

    taps = jnp.pad(taps, ((0, 8 - CONV - 1), (0, projected.shape[1] - taps.shape[1])))
    head = jnp.pad(jnp.stack([-jnp.exp(params[0]), params[1]]), ((0, 6), (0, LANES - heads)))
    skip = jnp.repeat(params[2], HEADDIM).reshape(1, HALF)
    wide = HALF + 2 * STATE
    rim = borrowed(projected[tokens - 8 :], 1)
    nothing = jnp.zeros((STATE, HALF), f32)
    values, prior, final, last = scan_forward(projected, taps, head, skip, rim, nothing, seg_len)
    if line > SEGS:
        last = jnp.sum(last.reshape(SEGS, 8, LANES)[:, 0, :heads], axis=0)
        decay = jnp.repeat(jnp.exp2(last), HEADDIM)
        begin = entering(decay, final, 1)
        values, prior, _, _ = scan_forward(projected, taps, head, skip, rim, begin, seg_len)

    values, gate_far, out_others, cotangent = tie(values, gate_far, out_others, cotangent)
    cot_got = send_sequence(cotangent, place)
    out_own = jnp.concatenate([out_own, *out_others])
    out_all = gather_plane(out_own, plane_steps())
    gate_matrix = whole_matrix([gate_own, *gate_near, *gate_far], True)
    gate_input = dot(normed, gate_matrix, ((1,), (0,)))
    gate_input, cot_first = tie(gate_input, cot_got[0])

    silu_gate = jax.nn.silu(gate_input)
    gated = values * silu_gate
    squares = jnp.sum(gated * gated, axis=1)
    squares_other = to_partner(squares)
    scale = lax.rsqrt((squares + squares_other) / INNER + epsilon)[:, None]
    mixed, mixed_turned = mixed_tokens(gated, scale, gain_gate, seg_len)
    mixed_turned, out_all, cot_second = tie(mixed_turned, out_all, cot_got[1])
    cot_half = order_sequence([cot_first, cot_second], place)
    cot_other = to_partner(cot_half)
    cot = in_core_order(cot_half, cot_other, core, 1)
    upstream = cot.reshape(tokens, model_width)
    by_owner = lambda grad: grad.astype(bf16).reshape(chip_dims() + (-1, grad.shape[1]))
    out_grad = by_owner(dot(mixed_turned, upstream, ((1,), (0,))))
    cut = model_width // 2
    out_first = [reduce_send([out_grad[..., :cut]], 1, 1, bf16), reduce_send([out_grad[..., cut:]], 0, 0, bf16)]
    out_matrix = whole_matrix([out_own, *out_all], False, True)
    branch, branch_sent = half_products(core, [(mixed, out_matrix, None)], seg_len, model_width, False)
    branch_sent, upstream = tie(branch_sent, upstream)
    branch_other = to_partner(branch_sent)
    grad_mixed = dot(upstream, out_matrix, ((1,), (1,)))
    grad_mixed, out_got = tie(grad_mixed, arrivals(out_first))
    out_second = [
        reduce_send(kept + received, 0, dim, bf16) for (kept, received), dim in zip(arrived(out_first, out_got), (0, 1))
    ]
    unit = gated * scale
    gain_grad = grad_mixed * gain_gate
    along = jnp.sum(gain_grad * unit, axis=1)
    along_other = to_partner(along)
    along_other, branch_other = tie(along_other, branch_other)
    hidden_out = send_back((hidden_half.astype(f32) + branch + branch_other.astype(f32)).astype(bf16), place)
    along = ((along + along_other) / INNER)[:, None]
    gate_gain_grad = jnp.sum(grad_mixed * unit, axis=0)
    grad_gated = scale * (gain_grad - unit * along)
    grad_values = grad_gated * silu_gate
    sigmoid = jax.nn.sigmoid(gate_input)
    grad_gate = (grad_gated * values * (sigmoid * (1.0 + gate_input * (1.0 - sigmoid)))).astype(bf16)
    gate_grad = by_owner(dot(normed_turned, grad_gate, ((1,), (0,))))
    gate_grad, grad_values, out_got = tie(gate_grad, grad_values, arrivals(out_second))
    gate_got = reduce_plane([gate_grad], plane_steps())
    scan = lambda later: scan_backward(
        0, core, projected, taps, head, skip, rim, later, prior, values, grad_values, seg_len
    )
    if line > SEGS:
        nothing = entering(decay, scan(nothing)[-1], -1)
    back = scan(nothing)
    back, gate_got, hidden_out, grad_gate = tie(back, gate_got, hidden_out, grad_gate)
    ((early_kept, early_got),) = reduce_z(
        [
            *arrived(out_second, out_got),
            ([plane_part([gate_grad], 0, 0)], gate_got),
        ]
    )
    grad_x, mine, theirs, grad_raw, x_taps_grad, skip_grad, head_sums, x_edge, _ = back
    grad_x = spilled(grad_x, x_edge, taps[:, :HALF])
    other = to_partner(theirs)
    x_grad = by_owner(dot(normed_turned, grad_x, ((1,), (0,))))
    other, x_grad = tie(other, x_grad)
    grad_state, state_taps_grad, state_edge = shared_backward(core, projected, rim, taps, mine, other)
    grad_state = spilled(grad_state, state_edge, lax.dynamic_slice_in_dim(taps, HALF + core * STATE, STATE, axis=1))
    grad_raw = grad_raw.astype(bf16)
    rest_grad = by_owner(dot(normed_turned, jnp.concatenate([grad_state, grad_raw], axis=1), ((1,), (0,))))
    rest_grad, x_grad, grad_gate = tie(rest_grad, x_grad, grad_gate)
    conv_near = reduce_plane([x_grad, rest_grad], near_steps())
    base = dot(grad_gate, gate_matrix, ((1,), (1,)))
    terms = [
        (grad_x, conv_all, lambda core: 0),
        (grad_state, conv_all, lambda core: HALF // LANES + core),
        (grad_raw, conv_all, lambda core: (HALF + 2 * STATE) // LANES),
    ]
    grad_normed, sent_normed = half_products(core, terms, seg_len, model_width, True, (base,))
    row = lax.broadcasted_iota(jnp.int32, (8, 1), 0)
    small = x_taps_grad + jnp.where(row == CONV + 1, gate_gain_grad, 0.0) + jnp.where(row == CONV + 2, skip_grad, 0.0)
    small = jnp.concatenate([small, state_taps_grad + head_sums], axis=1)
    sent_normed, early_got, conv_near, small, x_grad, rest_grad = tie(
        sent_normed, early_got, conv_near, small, x_grad, rest_grad
    )
    other_normed = to_partner(sent_normed)
    wide_hidden = hidden_half.astype(f32)
    hidden_scale = lax.rsqrt(jnp.mean(wide_hidden * wide_hidden, axis=-1, keepdims=True) + epsilon)
    grad_normed = (grad_normed + other_normed.astype(f32)) * gain_pre
    hidden_unit = wide_hidden * hidden_scale
    along = jnp.mean(grad_normed * hidden_unit, axis=-1, keepdims=True)
    grad_hidden = hidden_scale * (grad_normed - hidden_unit * along)
    grad_in = (cot_half.astype(f32) + grad_hidden).astype(bf16)
    grad_in, x_grad, rest_grad = tie(grad_in, x_grad, rest_grad)
    grad_in = send_back(grad_in, place)
    conv_far = reduce_plane([x_grad, rest_grad], far_steps())
    grad_in, conv_far = tie(grad_in, conv_far)
    late = reduce_z([([plane_part([x_grad, rest_grad], 0, 0)], [*conv_near, *conv_far])])
    for dim in range(2):
        small = small + sum(moved(small, dim, by) for by in range(1, chip_dims()[dim]))
    for bit in range((line - 1).bit_length()):
        small = small + exchanged(small, 2**bit)
    small_other = to_partner(small)
    late_got, small_other = tie(arrivals(late), small_other)
    early_share = total([*early_kept, *early_got])
    out_share = early_share[:, :model_width]
    paired = lambda share: share.astype(bf16).reshape(2, rows, -1)
    gate_share, conv_share = paired(early_share[:, model_width:]), paired(reduce_end(arrived(late, late_got)))

    def mine_and_partner(share):
        keep = lax.dynamic_index_in_dim(share, core, axis=0, keepdims=False)
        give = lax.dynamic_index_in_dim(share, 1 - core, axis=0, keepdims=False)
        return keep, to_partner(give)

    both = in_core_order(small, small_other, core, 0)
    natural = lambda array, width: array.reshape(2, -1, chips, width).transpose(1, 2, 0, 3).reshape(-1, 2 * chips * width)
    device = (lax.axis_index("chip") * 2 + core) * line + place
    columns = natural(both[:, :, :HALF], HALF // chips)
    taps_all = jnp.concatenate([columns, both[0, :, HALF:], both[1, :, HALF:]], axis=1)[: CONV + 1]
    taps_share = lax.dynamic_slice_in_dim(taps_all, device * conv_width, conv_width, axis=1)
    gain_share = lax.dynamic_slice_in_dim(columns[CONV + 1], device * gain_width, gain_width, axis=0)
    head_total = jnp.concatenate(
        [
            natural(both[:, CONV + 1 : CONV + 3, HALF : HALF + heads], heads // chips),
            jnp.sum(columns[CONV + 2].reshape(1, HEADS, HEADDIM), axis=2),
        ]
    )

    def interleave(mine, theirs):
        width = mine.shape[1] // chips
        both = in_core_order(mine.reshape(rows, chips, width), theirs.reshape(rows, chips, width), core, 2)
        return both.reshape(rows, -1)

    keep_gate, got_gate = mine_and_partner(gate_share)
    keep, got = mine_and_partner(conv_share)
    state_end = HALF + STATE
    in_share = jnp.concatenate(
        [
            interleave(keep_gate, got_gate),
            interleave(keep[:, :HALF], got[:, :HALF]),
            in_core_order(keep[:, HALF:state_end], got[:, HALF:state_end], core, 1).reshape(rows, -1),
            interleave(keep[:, state_end : state_end + heads], got[:, state_end : state_end + heads]),
        ],
        axis=1,
    ).astype(f32)
    pre_share = jnp.sum(in_proj.astype(f32) * in_share, axis=1) / pre_gain.astype(f32)
    hidden_out, grad_in = order_back(hidden_out, place), order_back(grad_in, place)
    return (hidden_out, grad_in, in_share, out_share, taps_share, pre_share, gain_share, head_total)


def solution(mesh):
    devices = mesh.devices
    cores = Mesh(devices.reshape(devices.shape[0] // 2, 2, devices.shape[1]), ("chip", "core", "seg"))
    dp, both = ("chip", "core"), ("chip", "core", "seg")
    tokens = P(dp, "seg", None)
    return jax.shard_map(
        per_device,
        mesh=cores,
        in_specs=(tokens, tokens, P(both, None), P(both, None), P(None, both), P(both), P(both), P()),
        out_specs=(tokens, tokens, P(both, None), P(both, None), P(None, both), P(both), P(both), P()),
        check_vma=False,
    )
```
